32 devices in a mesh: dp: 8 (over z, y), seq: 4 (over x, core).
Axes of the slice: x: 2, y: 2, z: 4, core: 2. Of those that a mesh axis runs over, the one named last changes fastest.
Arguments:
- long_ids: int32 [24, 512], P('dp', 'seq'), may hold values from 0 to 4100
- long_targets: int32 [24, 512], P('dp', 'seq'), may hold values from 0 to 4100
- long_mask: int32 [24, 512], P('dp', 'seq'), may hold values from 0 to 1
- long_lengths: int32 [24], P('dp'), may hold values from 256 to 512, as said below
- short_ids: int32 [64, 128], P(('dp', 'seq')), may hold values from 0 to 4100
- short_targets: int32 [64, 128], P(('dp', 'seq')), may hold values from 0 to 4100
- short_mask: int32 [64, 128], P(('dp', 'seq')), may hold values from 0 to 1
- short_lengths: int32 [64], P(('dp', 'seq')), may hold values from 64 to 128, as said below
- table: float32 [4101, 768], P(None, ('dp', 'seq')), may hold values from -0.21875 to 0.21875
- position: float32 [512, 768], P(None, ('dp', 'seq')), may hold values from -0.21875 to 0.21875
- qkv_weight: float32 [768, 2304], P(('dp', 'seq')), may hold values from -0.21875 to 0.21875
- out_weight: float32 [768, 768], P(('dp', 'seq')), may hold values from -1.75 to 1.75
- in_weight: float32 [768, 3072], P(('dp', 'seq')), may hold values from -0.21875 to 0.21875
- down_weight: float32 [3072, 768], P(('dp', 'seq')), may hold values from -0.109375 to 0.109375
- norms: float32 [768, 6], P(('dp', 'seq')), may hold values from -1 to 3, as said below
- table_rows: float32 [4101], replicated, may hold values from 1.5875193e-08 to 6.350077e-08
- table_cols: float32 [768], P(('dp', 'seq')), may hold values from 1.5875193e-08 to 6.350077e-08
- position_rows: float32 [512], replicated, may hold values from 2.4283373e-09 to 9.713349e-09
- position_cols: float32 [768], P(('dp', 'seq')), may hold values from 2.4283373e-09 to 9.713349e-09
- qkv_rows: float32 [768], P(('dp', 'seq')), may hold values from 8.477105e-08 to 3.390842e-07
- qkv_cols: float32 [2304], replicated, may hold values from 8.477105e-08 to 3.390842e-07
- out_rows: float32 [768], P(('dp', 'seq')), may hold values from 8.477105e-08 to 3.390842e-07
- out_cols: float32 [768], replicated, may hold values from 8.477105e-08 to 3.390842e-07
- in_rows: float32 [768], P(('dp', 'seq')), may hold values from 8.477105e-08 to 3.390842e-07
- in_cols: float32 [3072], replicated, may hold values from 8.477105e-08 to 3.390842e-07
- down_rows: float32 [3072], P(('dp', 'seq')), may hold values from 8.477105e-08 to 3.390842e-07
- down_cols: float32 [768], replicated, may hold values from 8.477105e-08 to 3.390842e-07
- norm_moment: float32 [768, 6], P(('dp', 'seq')), may hold values from 8.477105e-08 to 3.390842e-07
Outputs:
- loss_sum: float32 [], replicated
- mask_count: float32 [], replicated
- table_grad: float32 [4101, 768], P(None, ('dp', 'seq'))
- position_grad: float32 [512, 768], P(None, ('dp', 'seq'))
- qkv_grad: float32 [768, 2304], P(('dp', 'seq'))
- out_grad: float32 [768, 768], P(('dp', 'seq'))
- in_grad: float32 [768, 3072], P(('dp', 'seq'))
- down_grad: float32 [3072, 768], P(('dp', 'seq'))
- norm_grad: float32 [768, 6], P(('dp', 'seq'))
- table_rows_new: float32 [4101], replicated
- table_cols_new: float32 [768], P(('dp', 'seq'))
- position_rows_new: float32 [512], replicated
- position_cols_new: float32 [768], P(('dp', 'seq'))
- qkv_rows_new: float32 [768], P(('dp', 'seq'))
- qkv_cols_new: float32 [2304], replicated
- out_rows_new: float32 [768], P(('dp', 'seq'))
- out_cols_new: float32 [768], replicated
- in_rows_new: float32 [768], P(('dp', 'seq'))
- in_cols_new: float32 [3072], replicated
- down_rows_new: float32 [3072], P(('dp', 'seq'))
- down_cols_new: float32 [768], replicated
- norm_moment_new: float32 [768, 6], P(('dp', 'seq'))
- table_new: float32 [4101, 768], P(None, ('dp', 'seq'))
- position_new: float32 [512, 768], P(None, ('dp', 'seq'))
- qkv_new: float32 [768, 2304], P(('dp', 'seq'))
- out_new: float32 [768, 768], P(('dp', 'seq'))
- in_new: float32 [768, 3072], P(('dp', 'seq'))
- down_new: float32 [3072, 768], P(('dp', 'seq'))
- norm_new: float32 [768, 6], P(('dp', 'seq'))
The draws below stay inside these ranges and needn't reach their ends.
Inputs may be any that keep to these rules, and one draw needn't show every extreme that they name: `long_lengths`: in every aligned block of 3 rows one row has length 512. `short_lengths`: in every aligned block of 2 rows one row has length 128. `norms`: columns 0, 2 and 4 are positive gains, columns 1, 3 and 5 shifts.
All inputs are finite; a program needn't handle non-finite values.
Results may differ from the reference program's by a relative error of at most 0.0085.
The reference program's roundings to bfloat16 on the way count: a program that leaves them out, or rounds other values in their place, can miss the bound.
Values may be sent and summed in bfloat16 or wider, within the bound.
A program may use at most 192 MiB of HBM per device.

```python
import math
import jax
import jax.numpy as jnp
from jax import lax

D = 768
HEADS = 12
HEAD_DIM = 64
FF = 3072
V = 4101
LLEN = 512
SLEN = 128
B_LONG = 3
B_SHORT = 2
STEP = 10
LROWS = 24
SROWS = 64
N_DP = 8
N_SEQ = 4


def full_rows(key, count, group, shortest, longest):
    first, second = jax.random.split(key)
    lengths = jax.random.randint(first, (count,), shortest, longest + 1)
    chosen = jax.random.randint(second, (count // group,), 0, group)
    index = lax.iota(jnp.int32, count)
    marked = index % group == jnp.repeat(chosen, group, total_repeat_length=count)
    return jnp.where(marked, longest, lengths).astype(jnp.int32)


def draw_long_lengths(key, part):
    key = jax.random.fold_in(key, 13)
    return full_rows(key, LROWS, B_LONG, LLEN // 2, LLEN)


def draw_short_lengths(key, part):
    key = jax.random.fold_in(key, 19)
    return full_rows(key, SROWS, B_SHORT, SLEN // 2, SLEN)


def draw_long_mask(key, part):
    key = jax.random.fold_in(key, 11)
    row = lax.broadcasted_iota(jnp.int32, (LROWS, LLEN), 0)
    column = lax.broadcasted_iota(jnp.int32, (LROWS, LLEN), 1)
    limit = 50 * (LROWS + 2 * row) * (LLEN + 2 * column) // (LROWS * LLEN)
    return (jax.random.randint(key, (LROWS, LLEN), 0, 1000) < limit).astype(jnp.int32)


def draw_short_mask(key, part):
    key = jax.random.fold_in(key, 23)
    device = lax.broadcasted_iota(jnp.int32, (SROWS, SLEN), 0) // B_SHORT
    data_index = device // N_SEQ
    seq_index = device % N_SEQ
    limit = 50 * (N_DP + 2 * data_index) * (N_SEQ + 2 * seq_index) // (N_DP * N_SEQ)
    return (jax.random.randint(key, (SROWS, SLEN), 0, 1000) < limit).astype(jnp.int32)


def draw_norms(key, part):
    key = jax.random.fold_in(key, 17)
    first, second = jax.random.split(key)
    place = lax.broadcasted_iota(jnp.float32, (D, 3), 0) / D
    gains = (0.5 + place) * jax.random.uniform(first, (D, 3), jnp.float32, 0.8, 1.2)
    shifts = jnp.clip(0.25 * jax.random.normal(second, (D, 3), jnp.float32), -0.9, 0.9)
    return jnp.stack((gains, shifts), 2).reshape(D, 6)


def plant(array, own_key, smallest, largest):
    shape = array.shape
    spot = [jax.random.randint(jax.random.fold_in(own_key, axis), (), 0, shape[axis]) for axis in range(len(shape))]
    array = array.at[tuple(spot)].set(smallest)
    longest = shape.index(max(shape))
    spot[longest] = (spot[longest] + 1) % shape[longest]
    return array.at[tuple(spot)].set(largest)


def steps_of(key, extent, cuts, low, largest):
    factor_of = 1.0
    for axis_at, parts in cuts:
        steps = jax.random.uniform(jax.random.fold_in(jax.random.fold_in(key, 6), axis_at), (parts,), jnp.float32, low / len(cuts), largest / len(cuts))
        factor_of = factor_of * jnp.repeat(jnp.exp(steps), extent[axis_at] // parts).reshape((-1,) + (1,) * (len(extent) - 1 - axis_at))
    return factor_of


def scatter_about(rng, extent, scale, most, shards=(), kind=jnp.bfloat16):
    drawn = jax.random.normal(rng, extent, jnp.float32) * scale
    if len(shards) > 0:
        drawn = steps_of(rng, extent, shards, -0.22, 0.18) * drawn
    return jnp.clip(drawn, min=-most, max=most).astype(kind)


def setup_inputs(seed: int = 0) -> dict:
    seeds = jax.random.split(jax.random.key(seed), 29)
    long_ids = plant(jax.random.randint(seeds[0], (LROWS, LLEN), 0, V), jax.random.fold_in(seeds[0], 1), 0, V - 1).astype(jnp.int32)
    long_targets = plant(jax.random.randint(seeds[1], (LROWS, LLEN), 0, V), jax.random.fold_in(seeds[1], 1), 0, V - 1).astype(jnp.int32)
    long_mask = draw_long_mask(jax.random.fold_in(seeds[28], 71), 0)
    long_lengths = draw_long_lengths(jax.random.fold_in(seeds[28], 71), 0)
    short_ids = plant(jax.random.randint(seeds[4], (SROWS, SLEN), 0, V), jax.random.fold_in(seeds[4], 1), 0, V - 1).astype(jnp.int32)
    short_targets = plant(jax.random.randint(seeds[5], (SROWS, SLEN), 0, V), jax.random.fold_in(seeds[5], 1), 0, V - 1).astype(jnp.int32)
    short_mask = draw_short_mask(jax.random.fold_in(seeds[28], 71), 0)
    short_lengths = draw_short_lengths(jax.random.fold_in(seeds[28], 71), 0)
    table = scatter_about(seeds[8], (V, D), D ** -0.5, 0.21875, ((1, 32),), jnp.float32)
    position = scatter_about(seeds[9], (LLEN, D), D ** -0.5, 0.21875, ((1, 32),), jnp.float32)
    qkv_weight = scatter_about(seeds[10], (D, 3 * D), D ** -0.5, 0.21875, ((0, 32),), jnp.float32)
    out_weight = scatter_about(seeds[11], (D, D), (D // 64) ** -0.5, 1.75, ((0, 32),), jnp.float32)
    in_weight = scatter_about(seeds[12], (D, FF), D ** -0.5, 0.21875, ((0, 32),), jnp.float32)
    down_weight = scatter_about(seeds[13], (FF, D), FF ** -0.5, 0.109375, ((0, 32),), jnp.float32)
    norms = draw_norms(jax.random.fold_in(seeds[28], 71), 0)
    table_rows = jnp.clip(jnp.exp(jax.random.uniform(seeds[15], (V,), jnp.float32, math.log(1.5875192715952835e-08), math.log(6.350077086381134e-08))), 1.5875192715952835e-08, 6.350077086381134e-08)
    table_cols = jnp.clip(jnp.exp(math.log(6.350077086381134e-08) - 1.3862944 * jax.random.uniform(seeds[16], (D,), jnp.float32) ** steps_of(seeds[16], (D,), ((0, 32),), -0.2, 0.2)), 1.5875192715952835e-08, 6.350077086381134e-08)
    position_rows = jnp.clip(jnp.exp(jax.random.uniform(seeds[17], (LLEN,), jnp.float32, math.log(2.428337309012818e-09), math.log(9.713349236051272e-09))), 2.428337309012818e-09, 9.713349236051272e-09)
    position_cols = jnp.clip(jnp.exp(math.log(9.713349236051272e-09) - 1.3862944 * jax.random.uniform(seeds[18], (D,), jnp.float32) ** steps_of(seeds[18], (D,), ((0, 32),), -0.2, 0.2)), 2.428337309012818e-09, 9.713349236051272e-09)
    qkv_rows = jnp.clip(jnp.exp(math.log(3.3908420959960495e-07) - 1.3862944 * jax.random.uniform(seeds[19], (D,), jnp.float32) ** steps_of(seeds[19], (D,), ((0, 32),), -0.2, 0.2)), 8.477105239990124e-08, 3.3908420959960495e-07)
    qkv_cols = jnp.clip(jnp.exp(jax.random.uniform(seeds[20], (3 * D,), jnp.float32, math.log(8.477105239990124e-08), math.log(3.3908420959960495e-07))), 8.477105239990124e-08, 3.3908420959960495e-07)
    out_rows = jnp.clip(jnp.exp(math.log(3.3908420959960495e-07) - 1.3862944 * jax.random.uniform(seeds[21], (D,), jnp.float32) ** steps_of(seeds[21], (D,), ((0, 32),), -0.2, 0.2)), 8.477105239990124e-08, 3.3908420959960495e-07)
    out_cols = jnp.clip(jnp.exp(jax.random.uniform(seeds[22], (D,), jnp.float32, math.log(8.477105239990124e-08), math.log(3.3908420959960495e-07))), 8.477105239990124e-08, 3.3908420959960495e-07)
    in_rows = jnp.clip(jnp.exp(math.log(3.3908420959960495e-07) - 1.3862944 * jax.random.uniform(seeds[23], (D,), jnp.float32) ** steps_of(seeds[23], (D,), ((0, 32),), -0.2, 0.2)), 8.477105239990124e-08, 3.3908420959960495e-07)
    in_cols = jnp.clip(jnp.exp(jax.random.uniform(seeds[24], (FF,), jnp.float32, math.log(8.477105239990124e-08), math.log(3.3908420959960495e-07))), 8.477105239990124e-08, 3.3908420959960495e-07)
    down_rows = jnp.clip(jnp.exp(math.log(3.3908420959960495e-07) - 1.3862944 * jax.random.uniform(seeds[25], (FF,), jnp.float32) ** steps_of(seeds[25], (FF,), ((0, 32),), -0.2, 0.2)), 8.477105239990124e-08, 3.3908420959960495e-07)
    down_cols = jnp.clip(jnp.exp(jax.random.uniform(seeds[26], (D,), jnp.float32, math.log(8.477105239990124e-08), math.log(3.3908420959960495e-07))), 8.477105239990124e-08, 3.3908420959960495e-07)
    norm_moment = jnp.clip(jnp.exp(math.log(3.3908420959960495e-07) - 1.3862944 * jax.random.uniform(seeds[27], (D, 6), jnp.float32) ** steps_of(seeds[27], (D, 6), ((0, 32),), -0.2, 0.2)), 8.477105239990124e-08, 3.3908420959960495e-07)
    return {"long_ids": long_ids, "long_targets": long_targets, "long_mask": long_mask, "long_lengths": long_lengths, "short_ids": short_ids, "short_targets": short_targets, "short_mask": short_mask, "short_lengths": short_lengths, "table": table, "position": position, "qkv_weight": qkv_weight, "out_weight": out_weight, "in_weight": in_weight, "down_weight": down_weight, "norms": norms, "table_rows": table_rows, "table_cols": table_cols, "position_rows": position_rows, "position_cols": position_cols, "qkv_rows": qkv_rows, "qkv_cols": qkv_cols, "out_rows": out_rows, "out_cols": out_cols, "in_rows": in_rows, "in_cols": in_cols, "down_rows": down_rows, "down_cols": down_cols, "norm_moment": norm_moment}


@jax.custom_vjp
def low(v):
    return lax.optimization_barrier(v.astype(jnp.bfloat16)).astype(jnp.float32)

@jax.custom_vjp
def low_back(v):
    return v

def low_keep(v):
    return (low(v), None)

def low_pass(kept, grad):
    return (grad,)

def back_keep(v):
    return (v, None)

def back_low(kept, grad):
    return (low(grad),)
low.defvjp(low_keep, low_pass)
low_back.defvjp(back_keep, back_low)
EPSILON = 1e-12
SQUARE_FLOOR = 1e-30
learn_rate = 0.3
HIGHEST = lax.Precision.HIGHEST

def layer_norm(value, gain, shift):
    centred = value - lax.optimization_barrier(jnp.mean(value, -1, keepdims=True))
    return centred * lax.rsqrt(lax.optimization_barrier(jnp.mean(centred * centred, -1, keepdims=True)) + EPSILON) * gain + shift

def product(form, left, right):
    return jnp.einsum(form, left, right, precision=HIGHEST)

def bucket_loss(params, ids, targets, weight, keep_row):
    table, place, qkv_w, out_w, in_w, down_w, norms = params
    row_count, tok_count = ids.shape
    embedded = table[ids] + place[:tok_count][None]
    first = layer_norm(embedded, norms[:, 0], norms[:, 1])
    qkv = low(low_back(product('btd,de->bte', low(first), qkv_w)))
    qkv = qkv.reshape(row_count, tok_count, 3, HEADS, HEAD_DIM)
    scores = low_back(0.125 * product('bqhe,bkhe->bhqk', qkv[:, :, 0], qkv[:, :, 1]))
    scores = jnp.where(keep_row[:, None, None, :], scores, -1e+30)
    raised = jnp.exp(scores - lax.optimization_barrier(jnp.max(scores, -1, keepdims=True)))
    shares = raised / lax.optimization_barrier(jnp.sum(raised, -1, keepdims=True))
    mixture = low(low_back(product('bhqk,bkhe->bqhe', low(shares), qkv[:, :, 2])))
    mixture = mixture.reshape(row_count, tok_count, D)
    second = layer_norm(first + low_back(product('btd,de->bte', mixture, out_w)), norms[:, 2], norms[:, 3])
    hidden = low_back(product('btd,df->btf', low(second), in_w))
    active = low(jax.nn.gelu(hidden, approximate=False))
    third = layer_norm(second + low_back(product('btf,fd->btd', active, down_w)), norms[:, 4], norms[:, 5])
    logits = low_back(product('btd,vd->btv', low(third), table))
    picked = jnp.take_along_axis(logits, targets[..., None], -1)[..., 0]
    return jnp.sum(weight * (jax.nn.logsumexp(logits, -1) - picked))

def bucket_total(params, ids, targets, weight, keep_row, block):
    shaped = tuple((source.reshape((-1, block) + source.shape[1:]) for source in (ids, targets, weight, keep_row)))

    def advance(carry, pieces):
        return (carry + jax.checkpoint(bucket_loss)(params, *pieces), None)
    return lax.scan(advance, jnp.zeros((), jnp.float32), shaped)[0]

def factored(weight, grad, rows_old, cols_old, decay):
    square = grad * grad + SQUARE_FLOOR
    rows_new = decay * rows_old + (1.0 - decay) * lax.optimization_barrier(jnp.mean(square, 1))
    cols_new = decay * cols_old + (1.0 - decay) * lax.optimization_barrier(jnp.mean(square, 0))
    update = grad * lax.rsqrt(rows_new[:, None] * cols_new[None, :] / jnp.mean(rows_new))
    update = update / jnp.maximum(1.0, jnp.sqrt(jnp.mean(update * update)))
    return (rows_new, cols_new, weight - learn_rate * jnp.sqrt(jnp.mean(weight * weight)) * update)

def reference(long_ids, long_targets, long_mask, long_lengths, short_ids, short_targets, short_mask, short_lengths, table, position, qkv_weight, out_weight, in_weight, down_weight, norms, table_rows, table_cols, position_rows, position_cols, qkv_rows, qkv_cols, out_rows, out_cols, in_rows, in_cols, down_rows, down_cols, norm_moment):
    long_keep = jnp.arange(LLEN, dtype=jnp.int32)[None, :] < long_lengths[:, None]
    short_keep = jnp.arange(SLEN, dtype=jnp.int32)[None, :] < short_lengths[:, None]
    long_weight = long_mask.astype(jnp.float32) * long_keep.astype(jnp.float32)
    short_weight = short_mask.astype(jnp.float32) * short_keep.astype(jnp.float32)
    mask_count = jnp.sum(long_weight) + jnp.sum(short_weight)
    params = (table, position, qkv_weight, out_weight, in_weight, down_weight, norms)

    def objective(weights):
        rounded = tuple((low(member) for member in weights))
        total = bucket_total(rounded, long_ids, long_targets, long_weight, long_keep, 8)
        total = total + bucket_total(rounded, short_ids, short_targets, short_weight, short_keep, 32)
        return (total / mask_count, total)
    value, pullback, loss_sum = jax.vjp(objective, params, has_aux=True)
    grads = pullback(jnp.ones((), jnp.float32))[0]
    decay = 1.0 - STEP ** (-0.8)
    olds = ((table_rows, table_cols), (position_rows, position_cols), (qkv_rows, qkv_cols), (out_rows, out_cols), (in_rows, in_cols), (down_rows, down_cols))
    stats = []
    news = []
    for index in range(6):
        rows_new, cols_new, updated = factored(params[index], grads[index], olds[index][0], olds[index][1], decay)
        stats = stats + [rows_new, cols_new]
        news.append(updated)
    norm_g = grads[6]
    moment_new = decay * norm_moment + (1.0 - decay) * (norm_g * norm_g + SQUARE_FLOOR)
    update = norm_g * lax.rsqrt(moment_new)
    update = update / jnp.maximum(1.0, jnp.sqrt(lax.optimization_barrier(jnp.mean(update * update, 0))))
    norm_new = norms - learn_rate * jnp.sqrt(lax.optimization_barrier(jnp.mean(norms * norms, 0))) * update
    return (loss_sum, mask_count, grads[0], grads[1], grads[2], grads[3], grads[4], grads[5], grads[6], stats[0], stats[1], stats[2], stats[3], stats[4], stats[5], stats[6], stats[7], stats[8], stats[9], stats[10], stats[11], moment_new, news[0], news[1], news[2], news[3], news[4], news[5], norm_new)
```

```python
import functools

import jax
import jax.numpy as jnp
from jax import lax
from jax.experimental import pallas as pl
from jax.experimental.pallas import tpu as pltpu
from jax.sharding import PartitionSpec as P

D = 768
HEADS = 12
HEAD_DIM = 64
VOCAB = 4101
STEP = 10
SPAN = 128

EPSILON = 1e-12
SQUARE_FLOOR = 1e-30
learn_rate = 0.3

MESH = pl.DeviceIdType.MESH
F32 = jnp.float32
BF16 = jnp.bfloat16

NORM_AT = VOCAB
COUNT_AT = VOCAB + 6
PLACE_AT = 4352
WIDE = PLACE_AT + 512

SHAPES = ((24, WIDE), (24, 3 * D), (24, D), (24, 4 * D), (96, D))
E_, Q_, O_, I_, D_ = range(5)
CLASS_A, CLASS_B, CLASS_C = (E_, O_), (Q_, D_), (I_,)
UP, DOWN, XWAY, YWAY, SIDE = range(5)


def here():
    dp, seq = lax.axis_index("dp"), lax.axis_index("seq")
    return dp // 2, dp % 2, seq // 2, seq % 2


def device(z, y, x, c):
    return {"dp": z * 2 + y, "seq": x * 2 + c}


def chip(z, y, x):
    return z * 4 + y * 2 + x


def near_first(z, s):
    inner = (z * (3 - z)) // 2
    found = s + inner * (1, 1, -2, 0)[s]
    return found + (z // 2) * (3 - 2 * found)


def greet(peers):
    barrier = pltpu.get_barrier_semaphore()
    z, y, x, c = here()

    @pl.when(z < 3)
    def _():
        pl.semaphore_signal(barrier, inc=1, device_id=peers[UP], device_id_type=MESH)

    @pl.when(z > 0)
    def _():
        pl.semaphore_signal(barrier, inc=1, device_id=peers[DOWN], device_id_type=MESH)

    for way in (XWAY, YWAY, SIDE):
        pl.semaphore_signal(barrier, inc=1, device_id=peers[way], device_id_type=MESH)

    @pl.when((z == 0) | (z == 3))
    def _():
        pl.semaphore_wait(barrier, 4)

    @pl.when((z > 0) & (z < 3))
    def _():
        pl.semaphore_wait(barrier, 5)


def all_peers():
    z, y, x, c = here()
    return (
        device(z + 1, y, x, c),
        device(z - 1, y, x, c),
        device(z, y, 1 - x, c),
        device(z, 1 - y, x, c),
        device(z, y, x, 1 - c),
    )


def gather_kernel(*refs):
    shards, outs, merge, mine = refs[0:5], refs[5:10], refs[10:15], refs[15:20]
    swap_send, swap_recv, local_sem, send_sem, link_recv, side_recv = refs[20:]
    z, y, x, c = here()
    peers = all_peers()
    me = chip(z, y, x)

    def part(m, k, half):
        size, wide = 2 * SHAPES[m][0], SHAPES[m][1] // 2
        return outs[m].at[
            pl.ds(pl.multiple_of(k * size, size), size), pl.ds(pl.multiple_of(half * wide, 128), wide)
        ]

    def copy_of(m, k, way, own):
        return pltpu.make_async_remote_copy(
            src_ref=mine[m] if own else part(m, k, c),
            dst_ref=part(m, k, c),
            send_sem=send_sem.at[m, k, way],
            recv_sem=(side_recv if way == SIDE else link_recv).at[m, k],
            device_id=peers[way],
            device_id_type=MESH,
        )

    sent = []

    def push(m, k, way, own=False, only=None):
        sent.append((m, k, way, own, only))
        if only is None:
            copy_of(m, k, way, own).start()
        else:

            @pl.when(only)
            def _():
                copy_of(m, k, way, own).start()

    def arrived(m, k):
        copy_of(m, k, XWAY, False).wait_recv()

    greet(peers)
    swaps = []
    for m, (size, wide) in enumerate(SHAPES):
        half = wide // 2
        swaps.append(
            pltpu.make_async_remote_copy(
                src_ref=shards[m].at[:, pl.ds(pl.multiple_of((1 - c) * half, 128), half)],
                dst_ref=merge[m].at[pl.ds(pl.multiple_of(c * size, 8), size), :],
                send_sem=swap_send.at[m],
                recv_sem=swap_recv.at[m],
                device_id=peers[SIDE],
                device_id_type=MESH,
            )
        )
        swaps[m].start()
    for m, (size, wide) in enumerate(SHAPES):
        half = wide // 2
        merge[m][pl.ds(pl.multiple_of(c * size, 8), size), :] = shards[m][
            :, pl.ds(pl.multiple_of(c * half, 128), half)
        ]

    keeps = []
    for m in (I_, E_, Q_, D_, O_):
        swaps[m].wait_recv()
        mine[m][...] = merge[m][...].astype(BF16)
        for way, only in ((UP, z < 3), (DOWN, z > 0), (XWAY, None), (YWAY, None), (SIDE, None)):
            push(m, me, way, True, only)
        keeps.append(pltpu.make_async_copy(mine[m], part(m, me, c), local_sem.at[m]))
        keeps[-1].start()

    def onward(m, k, far):
        push(m, k, UP, only=(far < z) & (z < 3))
        push(m, k, DOWN, only=(far > z) & (z > 0))

    def line(ms, s, ways):
        far = near_first(z, s)
        k = chip(far, y, x)
        for m in ms:
            arrived(m, k)
            onward(m, k, far)
            for way in ways:
                push(m, k, way)

    def second(ms, s, axis):
        far = near_first(z, s)
        k = chip(far, y, 1 - x) if axis == XWAY else chip(far, 1 - y, x)
        for m in ms:
            arrived(m, k)
            push(m, k, YWAY if axis == XWAY else XWAY)
            push(m, k, SIDE)

    def third(ms, s, axis):
        far = near_first(z, s)
        for other in range(2):
            k = chip(far, 1 - y, other) if axis == YWAY else chip(far, other, 1 - x)
            for m in ms:
                arrived(m, k)
                push(m, k, SIDE)

    def c_first():
        k = chip(z, 1 - y, x)
        for m in CLASS_C:
            arrived(m, k)
            push(m, k, XWAY)
            push(m, k, UP, only=z < 3)
            push(m, k, DOWN, only=z > 0)
            push(m, k, SIDE)

    def c_second():
        for other in (y, 1 - y):
            k = chip(z, other, 1 - x)
            for m in CLASS_C:
                arrived(m, k)
                push(m, k, UP, only=z < 3)
                push(m, k, DOWN, only=z > 0)
                push(m, k, SIDE)

    def c_line(s):
        far = near_first(z, s)
        for k in (chip(far, y, x), chip(far, 1 - y, x), chip(far, y, 1 - x), chip(far, 1 - y, 1 - x)):
            for m in CLASS_C:
                arrived(m, k)
                onward(m, k, far)
                push(m, k, SIDE)

    both = (XWAY, YWAY, SIDE)
    c_first()
    line(CLASS_A, 1, both)
    line(CLASS_B, 1, both)
    c_second()
    second(CLASS_A, 0, XWAY)
    second(CLASS_B, 0, YWAY)
    c_line(1)
    line(CLASS_A, 2, both)
    line(CLASS_B, 2, both)
    second(CLASS_A, 1, XWAY)
    second(CLASS_B, 1, YWAY)
    c_line(2)
    line(CLASS_A, 3, both)
    line(CLASS_B, 3, both)
    second(CLASS_A, 2, XWAY)
    second(CLASS_B, 2, YWAY)
    c_line(3)
    second(CLASS_A, 3, XWAY)
    second(CLASS_B, 3, YWAY)
    for s in range(4):
        third(CLASS_A, s, YWAY)
        third(CLASS_B, s, XWAY)
    for m in range(5):
        for k in range(16):
            pltpu.make_async_remote_copy(
                src_ref=part(m, k, 1 - c),
                dst_ref=part(m, k, 1 - c),
                send_sem=send_sem.at[m, k, SIDE],
                recv_sem=side_recv.at[m, k],
                device_id=peers[SIDE],
                device_id_type=MESH,
            ).wait_recv()
    for swap in swaps:
        swap.wait_send()
    for keep in keeps:
        keep.wait()
    for m, k, way, own, only in sent:
        if only is None:
            copy_of(m, k, way, own).wait_send()
        else:

            @pl.when(only)
            def _(m=m, k=k, way=way, own=own):
                copy_of(m, k, way, own).wait_send()


def gather_weights(shards):
    return pl.pallas_call(
        gather_kernel,
        out_shape=[jax.ShapeDtypeStruct((32 * size, wide), BF16) for size, wide in SHAPES],
        in_specs=[pl.BlockSpec(memory_space=pltpu.VMEM)] * 5,
        out_specs=[pl.BlockSpec(memory_space=pl.ANY)] * 5,
        scratch_shapes=[pltpu.VMEM((2 * size, wide // 2), F32) for size, wide in SHAPES]
        + [pltpu.VMEM((2 * size, wide // 2), BF16) for size, wide in SHAPES]
        + [
            pltpu.SemaphoreType.DMA((5,)),
            pltpu.SemaphoreType.DMA((5,)),
            pltpu.SemaphoreType.DMA((5,)),
            pltpu.SemaphoreType.DMA((5, 16, 5)),
            pltpu.SemaphoreType.DMA((5, 16)),
            pltpu.SemaphoreType.DMA((5, 16)),
        ],
        compiler_params=pltpu.CompilerParams(
            collective_id=0, has_side_effects=True, vmem_limit_bytes=48 * 1024 * 1024
        ),
    )(*shards)


def reduce_kernel(*refs):
    grads, outs = refs[0:5], refs[5:10]
    own, side, first, second, low, high, fin = (refs[10 + 5 * i : 15 + 5 * i] for i in range(7))
    own_sem, side_send, side_recv, first_send, first_recv, second_send, second_recv = refs[45:52]
    up_send, low_recv, down_send, high_recv, swap_send, swap_recv = refs[52:]
    z, y, x, c = here()
    peers = all_peers()
    me = chip(z, y, x)

    def slot(ref, m, index):
        size = 2 * SHAPES[m][0]
        return ref[m].at[pl.ds(pl.multiple_of(index * size, size), size), :]

    def cols(m, half):
        wide = SHAPES[m][1] // 2
        return pl.ds(pl.multiple_of(half * wide, 128), wide)

    def combine(m, target, parts):
        def step(j, carry):
            at = pl.ds(pl.multiple_of(j * 128, 128), 128)
            total = parts[0][:, at].astype(F32)
            for member in parts[1:]:
                total = total + member[:, at].astype(F32)
            target[:, at] = total.astype(target.dtype)
            return carry

        lax.fori_loop(0, SHAPES[m][1] // 256, step, 0)

    def side_copy(m, k):
        size = 2 * SHAPES[m][0]
        return pltpu.make_async_remote_copy(
            src_ref=grads[m].at[pl.ds(pl.multiple_of(k * size, size), size), cols(m, 1 - c)],
            dst_ref=slot(side, m, k),
            send_sem=side_send.at[m, k],
            recv_sem=side_recv.at[m, k],
            device_id=peers[SIDE],
            device_id_type=MESH,
        )

    def own_copy(m):
        return pltpu.make_async_copy(grads[m].at[:, cols(m, c)], own[m], own_sem.at[m])

    def hop(m, k, land, index, sems, way):
        return pltpu.make_async_remote_copy(
            src_ref=slot(own, m, k),
            dst_ref=slot(land, m, index),
            send_sem=sems[0].at[m, index],
            recv_sem=sems[1].at[m, index],
            device_id=peers[way],
            device_id_type=MESH,
        )

    FIRST, SECOND = (first_send, first_recv), (second_send, second_recv)
    RISE, FALL = (up_send, low_recv), (down_send, high_recv)
    sent = []

    def send(m, k, land, index, sems, way, only=None):
        sent.append((m, k, land, index, sems, way, only))
        hop(m, k, land, index, sems, way).start()

    def landed(m, land, index, sems):
        hop(m, me, land, index, sems, XWAY).wait_recv()

    def block(m, a, b, far):
        return chip(far, a, b) if m in CLASS_A else chip(far, b, a)

    def split(m):
        return (y, x, YWAY, XWAY) if m in CLASS_A else (x, y, XWAY, YWAY)

    greet(peers)
    for m in (E_, Q_, I_, D_, O_):
        own_copy(m).start()

    def side_order():
        for i in range(8):
            for m in CLASS_A + CLASS_B:
                a, b, _, _ = split(m)
                yield m, block(m, 1 - a, i % 2, i // 2)
            for m in CLASS_C:
                for n in range(2):
                    yield m, (z * 4 + 4 + 2 * i + n) % 16
        for i in range(8):
            for m in CLASS_A + CLASS_B:
                a, b, _, _ = split(m)
                other = 1 - b if i < 4 else b
                yield m, block(m, a, other, i % 4)

    order = list(side_order())
    for m, k in order:
        side_copy(m, k).start()

    loaded = set()

    def ready(m, k):
        if m not in loaded:
            loaded.add(m)
            own_copy(m).wait()
        side_copy(m, k).wait_recv()

    def c_rise(t, yx):
        k = t * 4 + yx
        below = z < t
        for m in CLASS_C:

            @pl.when(below)
            def _():
                side_copy(m, k).wait_recv()

                @pl.when(z == 0)
                def _():
                    combine(m, slot(own, m, k), (slot(own, m, k), slot(side, m, k)))

                @pl.when(z > 0)
                def _():
                    landed(m, low, k, RISE)
                    combine(m, slot(own, m, k), (slot(own, m, k), slot(side, m, k), slot(low, m, k)))

                send(m, k, low, k, RISE, UP, below)

    def c_fall(t, yx):
        k = t * 4 + yx
        above = z > t
        for m in CLASS_C:

            @pl.when(above)
            def _():
                side_copy(m, k).wait_recv()

                @pl.when(z == 3)
                def _():
                    combine(m, slot(own, m, k), (slot(own, m, k), slot(side, m, k)))

                @pl.when(z < 3)
                def _():
                    landed(m, high, k, FALL)
                    combine(m, slot(own, m, k), (slot(own, m, k), slot(side, m, k), slot(high, m, k)))

                send(m, k, high, k, FALL, DOWN, above)

    c_steps = []
    for t in range(3):
        for yx in range(4):
            c_steps.append((c_rise, 3 - t, yx))
            c_steps.append((c_fall, t, yx))

    for m in CLASS_C:
        loaded.add(m)
        own_copy(m).wait()
    for i in range(8):
        for m in CLASS_A + CLASS_B:
            a, b, way, _ = split(m)
            k = block(m, 1 - a, i % 2, i // 2)
            ready(m, k)
            combine(m, slot(own, m, k), (slot(own, m, k), slot(side, m, k)))
            send(m, k, first, i, FIRST, way)
        for call, t, yx in c_steps[3 * i : 3 * i + 3]:
            call(t, yx)

    for i in range(4):
        for m in CLASS_A + CLASS_B:
            a, b, _, way = split(m)
            k = block(m, a, 1 - b, i)
            ready(m, k)
            at = 2 * i + (1 - b)
            landed(m, first, at, FIRST)
            combine(m, slot(own, m, k), (slot(own, m, k), slot(side, m, k), slot(first, m, at)))
            send(m, k, second, i, SECOND, way)
        if i == 0:
            for m in CLASS_C:
                for other in range(2):
                    k = chip(z, other, 1 - x)
                    ready(m, k)

                    @pl.when(z > 0)
                    def _():
                        landed(m, low, k, RISE)

                    @pl.when(z < 3)
                    def _():
                        landed(m, high, k, FALL)

                    with_ends(z, m, k, slot, own, side, low, high, combine, slot(own, m, k), ())
                    send(m, k, first, other, FIRST, XWAY)
        if i == 2:
            for m in CLASS_C:
                k = chip(z, 1 - y, x)
                ready(m, k)

                @pl.when(z > 0)
                def _():
                    landed(m, low, k, RISE)

                @pl.when(z < 3)
                def _():
                    landed(m, high, k, FALL)

                landed(m, first, 1 - y, FIRST)
                with_ends(
                    z, m, k, slot, own, side, low, high, combine, slot(own, m, k), (slot(first, m, 1 - y),)
                )
                send(m, k, second, 0, SECOND, YWAY)

    def z_parts(m, t):
        a, b, _, _ = split(m)
        k = block(m, a, b, t)
        return k, (slot(own, m, k), slot(side, m, k), slot(first, m, 2 * t + b), slot(second, m, t))

    def z_ready(m, k, t):
        a, b, _, _ = split(m)
        side_copy(m, k).wait_recv()
        landed(m, first, 2 * t + b, FIRST)
        landed(m, second, t, SECOND)

    for step in range(3):
        t = 3 - step
        below = z < t
        for m in CLASS_A + CLASS_B:
            k, parts = z_parts(m, t)

            @pl.when(below)
            def _():
                z_ready(m, k, t)

                @pl.when(z == 0)
                def _():
                    combine(m, slot(own, m, k), parts)

                @pl.when(z > 0)
                def _():
                    landed(m, low, t, RISE)
                    combine(m, slot(own, m, k), parts + (slot(low, m, t),))

                send(m, k, low, t, RISE, UP, below)

        t = step
        above = z > t
        for m in CLASS_A + CLASS_B:
            k, parts = z_parts(m, t)

            @pl.when(above)
            def _():
                z_ready(m, k, t)

                @pl.when(z == 3)
                def _():
                    combine(m, slot(own, m, k), parts)

                @pl.when(z < 3)
                def _():
                    landed(m, high, t, FALL)
                    combine(m, slot(own, m, k), parts + (slot(high, m, t),))

                send(m, k, high, t, FALL, DOWN, above)

    swaps = []
    for m in CLASS_C + CLASS_A + CLASS_B:
        if m in CLASS_C:
            ready(m, me)
            landed(m, first, y, FIRST)
            landed(m, second, 0, SECOND)
            at, more = me, (slot(first, m, y), slot(second, m, 0))
        else:
            z_ready(m, me, z)
            at, more = z, z_parts(m, z)[1][2:]

        @pl.when(z > 0)
        def _():
            landed(m, low, at, RISE)

        @pl.when(z < 3)
        def _():
            landed(m, high, at, FALL)

        with_ends(z, m, me, slot, own, side, low, high, combine, fin[m], more, at)
        size = SHAPES[m][0]
        swaps.append(
            pltpu.make_async_remote_copy(
                src_ref=fin[m].at[pl.ds(pl.multiple_of((1 - c) * size, 8), size), :],
                dst_ref=outs[m].at[:, cols(m, c)],
                send_sem=swap_send.at[m],
                recv_sem=swap_recv.at[m],
                device_id=peers[SIDE],
                device_id_type=MESH,
            )
        )
        swaps[-1].start()
        outs[m][:, cols(m, c)] = fin[m][pl.ds(pl.multiple_of(c * size, 8), size), :]
    for swap in swaps:
        swap.wait()
    for m, k in order:
        side_copy(m, k).wait_send()
    for m, k, land, index, sems, way, only in sent:
        if only is None:
            hop(m, k, land, index, sems, way).wait_send()
        else:

            @pl.when(only)
            def _(m=m, k=k, land=land, index=index, sems=sems, way=way):
                hop(m, k, land, index, sems, way).wait_send()


def with_ends(z, m, k, slot, own, side, low, high, combine, target, more, at=None):
    at = k if at is None else at
    base = (slot(own, m, k), slot(side, m, k)) + more

    @pl.when(z == 0)
    def _():
        combine(m, target, base + (slot(high, m, at),))

    @pl.when(z == 3)
    def _():
        combine(m, target, base + (slot(low, m, at),))

    @pl.when((z > 0) & (z < 3))
    def _():
        combine(m, target, base + (slot(low, m, at), slot(high, m, at)))


def reduce_grads(grads):
    def rows(count, m):
        size, wide = SHAPES[m]
        return pltpu.VMEM((count * 2 * size, wide // 2), BF16)

    every = range(5)
    scratch = (
        [rows(16, m) for m in every]
        + [rows(16, m) for m in every]
        + [rows(2 if m in CLASS_C else 8, m) for m in every]
        + [rows(1 if m in CLASS_C else 4, m) for m in every]
        + [rows(16 if m in CLASS_C else 4, m) for m in every]
        + [rows(16 if m in CLASS_C else 4, m) for m in every]
        + [pltpu.VMEM((2 * size, wide // 2), F32) for size, wide in SHAPES]
        + [pltpu.SemaphoreType.DMA((5,))]
        + [pltpu.SemaphoreType.DMA((5, 16))] * 2
        + [pltpu.SemaphoreType.DMA((5, 8))] * 2
        + [pltpu.SemaphoreType.DMA((5, 4))] * 2
        + [pltpu.SemaphoreType.DMA((5, 16))] * 4
        + [pltpu.SemaphoreType.DMA((5,))] * 2
    )
    return pl.pallas_call(
        reduce_kernel,
        out_shape=[jax.ShapeDtypeStruct(shape, F32) for shape in SHAPES],
        in_specs=[pl.BlockSpec(memory_space=pl.ANY)] * 5,
        out_specs=[pl.BlockSpec(memory_space=pltpu.VMEM)] * 5,
        scratch_shapes=scratch,
        compiler_params=pltpu.CompilerParams(
            collective_id=1, has_side_effects=True, vmem_limit_bytes=56 * 1024 * 1024
        ),
    )(*grads)


def total_kernel(in_ref, out_ref, land, held, send_sem, recv_sem):
    z, y, x, c = here()
    near = z + 1 - 2 * (z % 2)
    far = (z + 2) % 4
    partners = (
        device(z, y, x, 1 - c),
        device(z, y, 1 - x, c),
        device(z, 1 - y, x, c),
        device(near, y, x, c),
        device(far, y, x, c),
    )
    barrier = pltpu.get_barrier_semaphore()
    for partner in partners:
        pl.semaphore_signal(barrier, inc=1, device_id=partner, device_id_type=MESH)
    pl.semaphore_wait(barrier, 5)
    held[0] = in_ref[...]
    copies = []
    for i, partner in enumerate(partners):
        copies.append(
            pltpu.make_async_remote_copy(
                src_ref=held.at[i],
                dst_ref=land.at[i],
                send_sem=send_sem.at[i],
                recv_sem=recv_sem.at[i],
                device_id=partner,
                device_id_type=MESH,
            )
        )
        copies[i].start()
        copies[i].wait_recv()
        held[i + 1] = held[i] + land[i]
    out_ref[...] = held[5]
    for copy in copies:
        copy.wait_send()


def total_of(array, collective_id):
    return pl.pallas_call(
        total_kernel,
        out_shape=jax.ShapeDtypeStruct(array.shape, F32),
        in_specs=[pl.BlockSpec(memory_space=pltpu.VMEM)],
        out_specs=pl.BlockSpec(memory_space=pltpu.VMEM),
        scratch_shapes=[
            pltpu.VMEM((5,) + array.shape, F32),
            pltpu.VMEM((6,) + array.shape, F32),
            pltpu.SemaphoreType.DMA((5,)),
            pltpu.SemaphoreType.DMA((5,)),
        ],
        compiler_params=pltpu.CompilerParams(collective_id=collective_id, has_side_effects=True),
    )(array)


def gelu_pair(hidden):
    normal_cdf = 0.5 * (1.0 + lax.erf(hidden * 0.7071067811865476))
    return (
        hidden * normal_cdf,
        normal_cdf + hidden * jnp.exp(-0.5 * hidden * hidden) * 0.3989422804014327,
    )


def norm_forward(value, gain, shift):
    centred = value - jnp.mean(value, -1, keepdims=True)
    inverse = lax.rsqrt(jnp.mean(centred * centred, -1, keepdims=True) + EPSILON)
    normed = centred * inverse
    return (normed * gain + shift, normed, inverse)


def norm_backward(grad_out, normed, inverse, gain):
    scaled = grad_out * gain
    back = inverse * (
        scaled
        - jnp.mean(scaled, -1, keepdims=True)
        - normed * jnp.mean(scaled * normed, -1, keepdims=True)
    )
    return (back, jnp.sum(grad_out * normed, 0), jnp.sum(grad_out, 0))


def mm(left, right, sides):
    return lax.dot_general(left, right, ((sides[:1], sides[1:]), ((), ())), preferred_element_type=F32)


def attend(qkv, allowed):
    by_head = qkv.reshape(qkv.shape[0], 3, HEADS, HEAD_DIM)
    query, key, value = by_head[:, 0], by_head[:, 1], by_head[:, 2]
    scores = jnp.einsum("qhe,khe->hqk", query, key, preferred_element_type=F32) * 0.125
    scores = jnp.where(allowed[None], scores, -1e30)
    highest = jnp.max(scores, -1, keepdims=True)
    raised = jnp.exp(scores - highest)
    summed = jnp.sum(raised, -1, keepdims=True)
    shares = (raised / summed).astype(BF16)
    mixture = jnp.einsum("hqk,khe->qhe", shares, value, preferred_element_type=F32)
    return mixture.astype(BF16).reshape(qkv.shape[0], D), highest + jnp.log(summed)


def attend_back(qkv, allowed, log_total, grad_mix):
    by_head = qkv.reshape(qkv.shape[0], 3, HEADS, HEAD_DIM)
    query, key, value = by_head[:, 0], by_head[:, 1], by_head[:, 2]
    grad_mix = grad_mix.reshape(qkv.shape[0], HEADS, HEAD_DIM)
    scores = jnp.einsum("qhe,khe->hqk", query, key, preferred_element_type=F32) * 0.125
    scores = jnp.where(allowed[None], scores, -1e30)
    shares = jnp.exp(scores - log_total)
    grad_share = jnp.einsum("qhe,khe->hqk", grad_mix, value, preferred_element_type=F32)
    grad_score = (shares * (grad_share - jnp.sum(shares * grad_share, -1, keepdims=True))).astype(BF16)
    grad_query = jnp.einsum("hqk,khe->qhe", grad_score, key, preferred_element_type=F32) * 0.125
    grad_key = jnp.einsum("hqk,qhe->khe", grad_score, query, preferred_element_type=F32) * 0.125
    grad_value = jnp.einsum("hqk,qhe->khe", shares.astype(BF16), grad_mix, preferred_element_type=F32)
    return jnp.stack((grad_query, grad_key, grad_value), 1).astype(BF16).reshape(qkv.shape)


def on_device(
    whole_mesh,
    long_ids,
    long_targets,
    long_mask,
    long_lengths,
    short_ids,
    short_targets,
    short_mask,
    short_lengths,
    table,
    position,
    qkv_weight,
    out_weight,
    in_weight,
    down_weight,
    norms,
    table_rows,
    table_cols,
    position_rows,
    position_cols,
    qkv_rows,
    qkv_cols,
    out_rows,
    out_cols,
    in_rows,
    in_cols,
    down_rows,
    down_cols,
    norm_moment,
):
    devices = lax.axis_size(("dp", "seq"))
    fast = whole_mesh == (8, 4)
    seq_index = lax.axis_index("seq")
    held = norms.shape[0]

    span = long_ids.shape[1]
    long_place = seq_index * span + lax.iota(jnp.int32, span)
    long_keep = (long_place[None, :] < long_lengths[:, None]).astype(jnp.int32)
    short_keep = (lax.iota(jnp.int32, SPAN)[None, :] < short_lengths[:, None]).astype(jnp.int32)
    long_pack = jnp.stack((long_ids, long_targets, long_mask * long_keep, long_keep), 1)
    short_pack = jnp.stack((short_ids, short_targets, short_mask * short_keep, short_keep), 1)
    moved = lax.all_to_all(
        jnp.concatenate((long_pack, short_pack[1:]), 0), "seq", split_axis=0, concat_axis=0, tiled=True
    )
    tokens = jnp.concatenate((moved, short_pack[:1]), 0)
    ids, targets, weight, keep = (tokens[:, i].reshape(-1) for i in range(4))
    weight = weight.astype(F32)
    count = tokens.shape[0] * span
    last = count - span
    alone = seq_index == lax.axis_size("seq") - 1
    token = lax.iota(jnp.int32, count)
    place = jnp.where(alone | (token >= last), token % span, token)
    row = jnp.where(alone | (token >= last), token // span, 0)
    allowed_long = (row[:last, None] == row[None, :last]) & (keep[None, :last] > 0)
    allowed_short = jnp.broadcast_to(keep[None, last:] > 0, (span, span))

    here_count = jnp.sum(long_pack[:, 2]) + jnp.sum(short_pack[:, 2])
    tall = table.T
    counts = jnp.broadcast_to(jnp.stack((here_count // 256, here_count % 256)).astype(F32)[None], (held, 2))
    wide_shard = jnp.concatenate(
        (tall, norms, counts, jnp.zeros((held, PLACE_AT - COUNT_AT - 2), F32), position.T), 1
    )
    shards = (wide_shard, qkv_weight, out_weight, in_weight, down_weight)
    if fast:
        wide_w, qkv_w, out_w, in_w, down_w = gather_weights(shards)
    else:
        wide_w, qkv_w, out_w, in_w, down_w = (
            lax.all_gather(shard.astype(BF16), ("dp", "seq"), axis=0, tiled=True) for shard in shards
        )
    gains = wide_w[:, NORM_AT : NORM_AT + 6].astype(F32)
    sums = jnp.sum(wide_w[:, COUNT_AT : COUNT_AT + 2].astype(F32), 0)
    mask_count = (sums[0] * 256.0 + sums[1]) / held
    inverse_count = 1.0 / mask_count

    column = lax.broadcasted_iota(jnp.int32, (1, WIDE), 1)
    chosen = ((ids[:, None] == column) | ((place[:, None] + PLACE_AT) == column)).astype(BF16)
    embedded = mm(chosen, wide_w, (1, 1))
    first, normed_a, inverse_a = norm_forward(embedded, gains[:, 0], gains[:, 1])
    first_b = first.astype(BF16)
    qkv_b = mm(first_b, qkv_w, (1, 0)).astype(BF16)
    mix_long, total_long = attend(qkv_b[:last], allowed_long)
    mix_short, total_short = attend(qkv_b[last:], allowed_short)
    mixture = jnp.concatenate((mix_long, mix_short), 0)
    second, normed_b, inverse_b = norm_forward(first + mm(mixture, out_w, (1, 0)), gains[:, 2], gains[:, 3])
    second_b = second.astype(BF16)
    hidden = mm(second_b, in_w, (1, 0))
    active, slope = gelu_pair(hidden)
    active_b = active.astype(BF16)
    third, normed_c, inverse_c = norm_forward(second + mm(active_b, down_w, (1, 0)), gains[:, 4], gains[:, 5])
    third_b = third.astype(BF16)
    logits = jnp.where(column < VOCAB, mm(third_b, wide_w, (1, 0)), -1e30)
    highest = jnp.max(logits, -1, keepdims=True)
    log_sum = highest + jnp.log(jnp.sum(jnp.exp(logits - highest), -1, keepdims=True))
    onehot = targets[:, None] == column
    picked = jnp.sum(jnp.where(onehot, logits, 0.0), -1)
    loss_part = jnp.sum(weight * (log_sum[:, 0] - picked))
    grad_logit = (
        (jnp.exp(logits - log_sum) - onehot.astype(F32)) * (weight * inverse_count)[:, None]
    ).astype(BF16)
    grad_third = mm(grad_logit, wide_w, (1, 1))
    grad_second, gain_c, shift_c = norm_backward(grad_third, normed_c, inverse_c, gains[:, 4])
    grad_ffn = grad_second.astype(BF16)
    down_grad = mm(active_b, grad_ffn, (0, 0)).astype(BF16)
    grad_hidden = (mm(grad_ffn, down_w, (1, 1)) * slope).astype(BF16)
    in_grad = mm(second_b, grad_hidden, (0, 0)).astype(BF16)
    grad_second = grad_second + mm(grad_hidden, in_w, (1, 1))
    grad_first, gain_b, shift_b = norm_backward(grad_second, normed_b, inverse_b, gains[:, 2])
    grad_attn = grad_first.astype(BF16)
    out_grad = mm(mixture, grad_attn, (0, 0)).astype(BF16)
    grad_mix = mm(grad_attn, out_w, (1, 1)).astype(BF16)
    grad_qkv = jnp.concatenate(
        (
            attend_back(qkv_b[:last], allowed_long, total_long, grad_mix[:last]),
            attend_back(qkv_b[last:], allowed_short, total_short, grad_mix[last:]),
        ),
        0,
    )
    qkv_grad = mm(first_b, grad_qkv, (0, 0)).astype(BF16)
    grad_first = grad_first + mm(grad_qkv, qkv_w, (1, 1))
    grad_embed, gain_a, shift_a = norm_backward(grad_first, normed_a, inverse_a, gains[:, 0])
    wide_grad = mm(
        jnp.concatenate((third_b, grad_embed.astype(BF16)), 0),
        jnp.concatenate((grad_logit, chosen), 0),
        (0, 0),
    )
    norm_part = jnp.stack((gain_a, shift_a, gain_b, shift_b, gain_c, shift_c), 1)
    wide_grad = lax.dynamic_update_slice(wide_grad.astype(BF16), norm_part.astype(BF16), (0, NORM_AT))
    grads = (wide_grad, qkv_grad, out_grad, in_grad, down_grad)
    if fast:
        wide_g, qkv_g, out_g, in_g, down_g = reduce_grads(grads)
    else:
        wide_g, qkv_g, out_g, in_g, down_g = (
            lax.psum_scatter(grad.astype(F32), ("dp", "seq"), scatter_dimension=0, tiled=True) for grad in grads
        )
    table_g, place_g = wide_g[:, :VOCAB], wide_g[:, PLACE_AT:]
    norm_g = wide_g[:, NORM_AT : NORM_AT + 6]

    def summed_over_all(parts, collective_id):
        if not fast:
            return lax.psum(parts, ("dp", "seq"))
        flat = jnp.concatenate([member.reshape(-1) for member in parts])
        room = -flat.shape[0] % 1024
        flat = jnp.concatenate((flat, jnp.zeros((room,), F32))).reshape(-1, 128)
        flat = total_of(flat, collective_id).reshape(-1)
        found, start = [], 0
        for member in parts:
            found.append(flat[start : start + member.size].reshape(member.shape))
            start += member.size
        return found

    decay = 1.0 - STEP ** (-0.8)
    matrices = (
        (qkv_weight, qkv_g, qkv_rows, qkv_cols),
        (out_weight, out_g, out_rows, out_cols),
        (in_weight, in_g, in_rows, in_cols),
        (down_weight, down_g, down_rows, down_cols),
    )
    wide = (
        (tall, table_g, table_cols, table_rows),
        (position.T, place_g, position_cols, position_rows),
    )
    row_news = [
        decay * member[2] + (1.0 - decay) * jnp.mean(member[1] * member[1] + SQUARE_FLOOR, 1)
        for member in matrices + wide
    ]
    col_parts = [jnp.sum(member[1] * member[1] + SQUARE_FLOOR, 0) for member in matrices + wide]
    row_totals = jnp.stack([jnp.sum(rows_new) for rows_new in row_news])
    weight_sq = jnp.stack([jnp.sum(member[0] * member[0]) for member in matrices + wide])
    stats = summed_over_all(
        col_parts + [row_totals, weight_sq, jnp.sum(norms * norms, 0), loss_part.reshape(1)], 2
    )
    updates = []
    cols_out = []
    for index, member in enumerate(matrices + wide):
        full_rows = member[0].shape[0] * devices
        cols_new = decay * member[3] + (1.0 - decay) * stats[index] / full_rows
        if index < 4:
            mean = stats[6][index] / full_rows
        else:
            mean = jnp.mean(cols_new)
        updates.append(member[1] * lax.rsqrt(row_news[index][:, None] * cols_new[None, :] / mean))
        cols_out.append(cols_new)
    moment_new = decay * norm_moment + (1.0 - decay) * (norm_g * norm_g + SQUARE_FLOOR)
    norm_update = norm_g * lax.rsqrt(moment_new)
    update_sq = jnp.stack([jnp.sum(update * update) for update in updates])
    totals = summed_over_all([update_sq, jnp.sum(norm_update * norm_update, 0)], 3)
    news = []
    for index, member in enumerate(matrices + wide):
        entries = member[0].shape[0] * member[0].shape[1] * devices
        clip = jnp.maximum(1.0, jnp.sqrt(totals[0][index] / entries))
        news.append(
            member[0] - learn_rate * jnp.sqrt(stats[7][index] / entries) * updates[index] / clip
        )
    norm_rows = norms.shape[0] * devices
    norm_clip = jnp.maximum(1.0, jnp.sqrt(totals[1] / norm_rows))
    norm_new = norms - learn_rate * jnp.sqrt(stats[8] / norm_rows) * norm_update / norm_clip
    return (
        stats[9][0],
        mask_count,
        table_g.T,
        place_g.T,
        qkv_g,
        out_g,
        in_g,
        down_g,
        norm_g,
        cols_out[4],
        row_news[4],
        cols_out[5],
        row_news[5],
        row_news[0],
        cols_out[0],
        row_news[1],
        cols_out[1],
        row_news[2],
        cols_out[2],
        row_news[3],
        cols_out[3],
        moment_new,
        news[4].T,
        news[5].T,
        news[0],
        news[1],
        news[2],
        news[3],
        norm_new,
    )


def solution(mesh):
    split, wide = P(("dp", "seq"), None), P(None, ("dp", "seq"))
    shard, same = P(("dp", "seq")), P()
    return jax.shard_map(
        functools.partial(on_device, (mesh.shape["dp"], mesh.shape["seq"])),
        mesh=mesh,
        in_specs=(P("dp", "seq"),) * 3
        + (P("dp"),)
        + (split,) * 3
        + (shard,)
        + (wide,) * 2
        + (split,) * 5
        + (same, shard) * 2
        + (shard, same) * 4
        + (split,),
        out_specs=(same, same)
        + (wide,) * 2
        + (split,) * 5
        + (same, shard) * 2
        + (shard, same) * 4
        + (split,)
        + (wide,) * 2
        + (split,) * 5,
        check_vma=False,
    )
```

```python
import functools

import jax
import jax.numpy as jnp
from jax import lax
from jax.experimental import pallas as pl
from jax.experimental.pallas import tpu as pltpu
from jax.sharding import PartitionSpec as P

D = 768
HEADS = 12
HEAD_DIM = 64
VOCAB = 4101
STEP = 10
SPAN = 128

EPSILON = 1e-12
SQUARE_FLOOR = 1e-30
learn_rate = 0.3

MESH = pl.DeviceIdType.MESH
F32 = jnp.float32
BF16 = jnp.bfloat16

NORM_AT = VOCAB
COUNT_AT = VOCAB + 6
PLACE_AT = 4352
WIDE = PLACE_AT + 512

SHAPES = ((24, WIDE), (24, 3 * D), (24, D), (24, 4 * D), (96, D))
E_, Q_, O_, I_, D_ = range(5)
CLASS_A, CLASS_B, CLASS_C = (E_, O_), (Q_, D_), (I_,)
UP, DOWN, XWAY, YWAY, SIDE = range(5)


def here():
    dp, seq = lax.axis_index("dp"), lax.axis_index("seq")
    return dp // 2, dp % 2, seq // 2, seq % 2


def device(z, y, x, c):
    return {"dp": z * 2 + y, "seq": x * 2 + c}


def chip(z, y, x):
    return z * 4 + y * 2 + x


def near_first(z, s):
    inner = (z * (3 - z)) // 2
    found = s + inner * (1, 1, -2, 0)[s]
    return found + (z // 2) * (3 - 2 * found)


def greet(peers):
    barrier = pltpu.get_barrier_semaphore()
    z, y, x, c = here()

    @pl.when(z < 3)
    def _():
        pl.semaphore_signal(barrier, inc=1, device_id=peers[UP], device_id_type=MESH)

    @pl.when(z > 0)
    def _():
        pl.semaphore_signal(barrier, inc=1, device_id=peers[DOWN], device_id_type=MESH)

    for way in (XWAY, YWAY, SIDE):
        pl.semaphore_signal(barrier, inc=1, device_id=peers[way], device_id_type=MESH)

    @pl.when((z == 0) | (z == 3))
    def _():
        pl.semaphore_wait(barrier, 4)

    @pl.when((z > 0) & (z < 3))
    def _():
        pl.semaphore_wait(barrier, 5)


def all_peers():
    z, y, x, c = here()
    return (
        device(z + 1, y, x, c),
        device(z - 1, y, x, c),
        device(z, y, 1 - x, c),
        device(z, 1 - y, x, c),
        device(z, y, x, 1 - c),
    )


def gather_kernel(*refs):
    shards, outs, merge, mine = refs[0:5], refs[5:10], refs[10:15], refs[15:20]
    swap_send, swap_recv, local_sem, send_sem, link_recv, side_recv = refs[20:]
    z, y, x, c = here()
    peers = all_peers()
    me = chip(z, y, x)

    def part(m, k, half):
        size, wide = 2 * SHAPES[m][0], SHAPES[m][1] // 2
        return outs[m].at[
            pl.ds(pl.multiple_of(k * size, size), size), pl.ds(pl.multiple_of(half * wide, 128), wide)
        ]

    def copy_of(m, k, way, own):
        return pltpu.make_async_remote_copy(
            src_ref=mine[m] if own else part(m, k, c),
            dst_ref=part(m, k, c),
            send_sem=send_sem.at[m, k, way],
            recv_sem=(side_recv if way == SIDE else link_recv).at[m, k],
            device_id=peers[way],
            device_id_type=MESH,
        )

    sent = []

    def push(m, k, way, own=False, only=None):
        sent.append((m, k, way, own, only))
        if only is None:
            copy_of(m, k, way, own).start()
        else:

            @pl.when(only)
            def _():
                copy_of(m, k, way, own).start()

    def arrived(m, k):
        copy_of(m, k, XWAY, False).wait_recv()

    greet(peers)
    swaps = []
    for m, (size, wide) in enumerate(SHAPES):
        half = wide // 2
        swaps.append(
            pltpu.make_async_remote_copy(
                src_ref=shards[m].at[:, pl.ds(pl.multiple_of((1 - c) * half, 128), half)],
                dst_ref=merge[m].at[pl.ds(pl.multiple_of(c * size, 8), size), :],
                send_sem=swap_send.at[m],
                recv_sem=swap_recv.at[m],
                device_id=peers[SIDE],
                device_id_type=MESH,
            )
        )
        swaps[m].start()
    for m, (size, wide) in enumerate(SHAPES):
        half = wide // 2
        merge[m][pl.ds(pl.multiple_of(c * size, 8), size), :] = shards[m][
            :, pl.ds(pl.multiple_of(c * half, 128), half)
        ]

    keeps = []
    for m in (I_, E_, Q_, D_, O_):
        swaps[m].wait_recv()
        mine[m][...] = merge[m][...].astype(BF16)
        for way, only in ((UP, z < 3), (DOWN, z > 0), (XWAY, None), (YWAY, None), (SIDE, None)):
            push(m, me, way, True, only)
        keeps.append(pltpu.make_async_copy(mine[m], part(m, me, c), local_sem.at[m]))
        keeps[-1].start()

    def onward(m, k, far):
        push(m, k, UP, only=(far < z) & (z < 3))
        push(m, k, DOWN, only=(far > z) & (z > 0))

    def line(ms, s, ways):
        far = near_first(z, s)
        k = chip(far, y, x)
        for m in ms:
            arrived(m, k)
            onward(m, k, far)
            for way in ways:
                push(m, k, way)

    def second(ms, s, axis):
        far = near_first(z, s)
        k = chip(far, y, 1 - x) if axis == XWAY else chip(far, 1 - y, x)
        for m in ms:
            arrived(m, k)
            push(m, k, YWAY if axis == XWAY else XWAY)
            push(m, k, SIDE)

    def third(ms, s, axis):
        far = near_first(z, s)
        for other in range(2):
            k = chip(far, 1 - y, other) if axis == YWAY else chip(far, other, 1 - x)
            for m in ms:
                arrived(m, k)
                push(m, k, SIDE)

    def c_first():
        k = chip(z, 1 - y, x)
        for m in CLASS_C:
            arrived(m, k)
            push(m, k, XWAY)
            push(m, k, UP, only=z < 3)
            push(m, k, DOWN, only=z > 0)
            push(m, k, SIDE)

    def c_second():
        for other in (y, 1 - y):
            k = chip(z, other, 1 - x)
            for m in CLASS_C:
                arrived(m, k)
                push(m, k, UP, only=z < 3)
                push(m, k, DOWN, only=z > 0)
                push(m, k, SIDE)

    def c_line(s):
        far = near_first(z, s)
        for k in (chip(far, y, x), chip(far, 1 - y, x), chip(far, y, 1 - x), chip(far, 1 - y, 1 - x)):
            for m in CLASS_C:
                arrived(m, k)
                onward(m, k, far)
                push(m, k, SIDE)

    both = (XWAY, YWAY, SIDE)
    c_first()
    line(CLASS_A, 1, both)
    line(CLASS_B, 1, both)
    c_second()
    second(CLASS_A, 0, XWAY)
    second(CLASS_B, 0, YWAY)
    c_line(1)
    line(CLASS_A, 2, both)
    line(CLASS_B, 2, both)
    second(CLASS_A, 1, XWAY)
    second(CLASS_B, 1, YWAY)
    c_line(2)
    line(CLASS_A, 3, both)
    line(CLASS_B, 3, both)
    second(CLASS_A, 2, XWAY)
    second(CLASS_B, 2, YWAY)
    c_line(3)
    second(CLASS_A, 3, XWAY)
    second(CLASS_B, 3, YWAY)
    for s in range(4):
        third(CLASS_A, s, YWAY)
        third(CLASS_B, s, XWAY)
    for m in range(5):
        for k in range(16):
            pltpu.make_async_remote_copy(
                src_ref=part(m, k, 1 - c),
                dst_ref=part(m, k, 1 - c),
                send_sem=send_sem.at[m, k, SIDE],
                recv_sem=side_recv.at[m, k],
                device_id=peers[SIDE],
                device_id_type=MESH,
            ).wait_recv()
    for swap in swaps:
        swap.wait_send()
    for keep in keeps:
        keep.wait()
    for m, k, way, own, only in sent:
        if only is None:
            copy_of(m, k, way, own).wait_send()
        else:

            @pl.when(only)
            def _(m=m, k=k, way=way, own=own):
                copy_of(m, k, way, own).wait_send()


def gather_weights(shards):
    return pl.pallas_call(
        gather_kernel,
        out_shape=[jax.ShapeDtypeStruct((32 * size, wide), BF16) for size, wide in SHAPES],
        in_specs=[pl.BlockSpec(memory_space=pltpu.VMEM)] * 5,
        out_specs=[pl.BlockSpec(memory_space=pl.ANY)] * 5,
        scratch_shapes=[pltpu.VMEM((2 * size, wide // 2), F32) for size, wide in SHAPES]
        + [pltpu.VMEM((2 * size, wide // 2), BF16) for size, wide in SHAPES]
        + [
            pltpu.SemaphoreType.DMA((5,)),
            pltpu.SemaphoreType.DMA((5,)),
            pltpu.SemaphoreType.DMA((5,)),
            pltpu.SemaphoreType.DMA((5, 16, 5)),
            pltpu.SemaphoreType.DMA((5, 16)),
            pltpu.SemaphoreType.DMA((5, 16)),
        ],
        compiler_params=pltpu.CompilerParams(
            collective_id=0, has_side_effects=True, vmem_limit_bytes=48 * 1024 * 1024
        ),
    )(*shards)


def reduce_kernel(*refs):
    grads, outs = refs[0:5], refs[5:10]
    own, side, first, second, low, high, fin = (refs[10 + 5 * i : 15 + 5 * i] for i in range(7))
    own_sem, side_send, side_recv, first_send, first_recv, second_send, second_recv = refs[45:52]
    up_send, low_recv, down_send, high_recv, swap_send, swap_recv = refs[52:]
    z, y, x, c = here()
    peers = all_peers()
    me = chip(z, y, x)

    def slot(ref, m, index):
        size = 2 * SHAPES[m][0]
        return ref[m].at[pl.ds(pl.multiple_of(index * size, size), size), :]

    def cols(m, half):
        wide = SHAPES[m][1] // 2
        return pl.ds(pl.multiple_of(half * wide, 128), wide)

    def combine(m, target, parts):
        def step(j, carry):
            at = pl.ds(pl.multiple_of(j * 128, 128), 128)
            total = parts[0][:, at].astype(F32)
            for member in parts[1:]:
                total = total + member[:, at].astype(F32)
            target[:, at] = total.astype(target.dtype)
            return carry

        lax.fori_loop(0, SHAPES[m][1] // 256, step, 0)

    def side_copy(m, k):
        size = 2 * SHAPES[m][0]
        return pltpu.make_async_remote_copy(
            src_ref=grads[m].at[pl.ds(pl.multiple_of(k * size, size), size), cols(m, 1 - c)],
            dst_ref=slot(side, m, k),
            send_sem=side_send.at[m, k],
            recv_sem=side_recv.at[m, k],
            device_id=peers[SIDE],
            device_id_type=MESH,
        )

    def own_copy(m):
        return pltpu.make_async_copy(grads[m].at[:, cols(m, c)], own[m], own_sem.at[m])

    def hop(m, k, land, index, sems, way):
        return pltpu.make_async_remote_copy(
            src_ref=slot(own, m, k),
            dst_ref=slot(land, m, index),
            send_sem=sems[0].at[m, index],
            recv_sem=sems[1].at[m, index],
            device_id=peers[way],
            device_id_type=MESH,
        )

    FIRST, SECOND = (first_send, first_recv), (second_send, second_recv)
    RISE, FALL = (up_send, low_recv), (down_send, high_recv)
    sent = []

    def send(m, k, land, index, sems, way, only=None):
        sent.append((m, k, land, index, sems, way, only))
        hop(m, k, land, index, sems, way).start()

    def landed(m, land, index, sems):
        hop(m, me, land, index, sems, XWAY).wait_recv()

    def block(m, a, b, far):
        return chip(far, a, b) if m in CLASS_A else chip(far, b, a)

    def split(m):
        return (y, x, YWAY, XWAY) if m in CLASS_A else (x, y, XWAY, YWAY)

    greet(peers)
    for m in (E_, Q_, I_, D_, O_):
        own_copy(m).start()

    def side_order():
        for i in range(8):
            for m in CLASS_A + CLASS_B:
                a, b, _, _ = split(m)
                yield m, block(m, 1 - a, i % 2, i // 2)
            for m in CLASS_C:
                for n in range(2):
                    yield m, (z * 4 + 4 + 2 * i + n) % 16
        for i in range(8):
            for m in CLASS_A + CLASS_B:
                a, b, _, _ = split(m)
                other = 1 - b if i < 4 else b
                yield m, block(m, a, other, i % 4)

    order = list(side_order())
    for m, k in order:
        side_copy(m, k).start()

    loaded = set()

    def ready(m, k):
        if m not in loaded:
            loaded.add(m)
            own_copy(m).wait()
        side_copy(m, k).wait_recv()

    def c_rise(t, yx):
        k = t * 4 + yx
        below = z < t
        for m in CLASS_C:

            @pl.when(below)
            def _():
                side_copy(m, k).wait_recv()

                @pl.when(z == 0)
                def _():
                    combine(m, slot(own, m, k), (slot(own, m, k), slot(side, m, k)))

                @pl.when(z > 0)
                def _():
                    landed(m, low, k, RISE)
                    combine(m, slot(own, m, k), (slot(own, m, k), slot(side, m, k), slot(low, m, k)))

                send(m, k, low, k, RISE, UP, below)

    def c_fall(t, yx):
        k = t * 4 + yx
        above = z > t
        for m in CLASS_C:

            @pl.when(above)
            def _():
                side_copy(m, k).wait_recv()

                @pl.when(z == 3)
                def _():
                    combine(m, slot(own, m, k), (slot(own, m, k), slot(side, m, k)))

                @pl.when(z < 3)
                def _():
                    landed(m, high, k, FALL)
                    combine(m, slot(own, m, k), (slot(own, m, k), slot(side, m, k), slot(high, m, k)))

                send(m, k, high, k, FALL, DOWN, above)

    c_steps = []
    for t in range(3):
        for yx in range(4):
            c_steps.append((c_rise, 3 - t, yx))
            c_steps.append((c_fall, t, yx))

    for m in CLASS_C:
        loaded.add(m)
        own_copy(m).wait()
    for i in range(8):
        for m in CLASS_A + CLASS_B:
            a, b, way, _ = split(m)
            k = block(m, 1 - a, i % 2, i // 2)
            ready(m, k)
            combine(m, slot(own, m, k), (slot(own, m, k), slot(side, m, k)))
            send(m, k, first, i, FIRST, way)
        for call, t, yx in c_steps[3 * i : 3 * i + 3]:
            call(t, yx)

    for i in range(4):
        for m in CLASS_A + CLASS_B:
            a, b, _, way = split(m)
            k = block(m, a, 1 - b, i)
            ready(m, k)
            at = 2 * i + (1 - b)
            landed(m, first, at, FIRST)
            combine(m, slot(own, m, k), (slot(own, m, k), slot(side, m, k), slot(first, m, at)))
            send(m, k, second, i, SECOND, way)
        if i == 0:
            for m in CLASS_C:
                for other in range(2):
                    k = chip(z, other, 1 - x)
                    ready(m, k)

                    @pl.when(z > 0)
                    def _():
                        landed(m, low, k, RISE)

                    @pl.when(z < 3)
                    def _():
                        landed(m, high, k, FALL)

                    with_ends(z, m, k, slot, own, side, low, high, combine, slot(own, m, k), ())
                    send(m, k, first, other, FIRST, XWAY)
        if i == 2:
            for m in CLASS_C:
                k = chip(z, 1 - y, x)
                ready(m, k)

                @pl.when(z > 0)
                def _():
                    landed(m, low, k, RISE)

                @pl.when(z < 3)
                def _():
                    landed(m, high, k, FALL)

                landed(m, first, 1 - y, FIRST)
                with_ends(
                    z, m, k, slot, own, side, low, high, combine, slot(own, m, k), (slot(first, m, 1 - y),)
                )
                send(m, k, second, 0, SECOND, YWAY)

    def z_parts(m, t):
        a, b, _, _ = split(m)
        k = block(m, a, b, t)
        return k, (slot(own, m, k), slot(side, m, k), slot(first, m, 2 * t + b), slot(second, m, t))

    def z_ready(m, k, t):
        a, b, _, _ = split(m)
        side_copy(m, k).wait_recv()
        landed(m, first, 2 * t + b, FIRST)
        landed(m, second, t, SECOND)

    for step in range(3):
        t = 3 - step
        below = z < t
        for m in CLASS_A + CLASS_B:
            k, parts = z_parts(m, t)

            @pl.when(below)
            def _():
                z_ready(m, k, t)

                @pl.when(z == 0)
                def _():
                    combine(m, slot(own, m, k), parts)

                @pl.when(z > 0)
                def _():
                    landed(m, low, t, RISE)
                    combine(m, slot(own, m, k), parts + (slot(low, m, t),))

                send(m, k, low, t, RISE, UP, below)

        t = step
        above = z > t
        for m in CLASS_A + CLASS_B:
            k, parts = z_parts(m, t)

            @pl.when(above)
            def _():
                z_ready(m, k, t)

                @pl.when(z == 3)
                def _():
                    combine(m, slot(own, m, k), parts)

                @pl.when(z < 3)
                def _():
                    landed(m, high, t, FALL)
                    combine(m, slot(own, m, k), parts + (slot(high, m, t),))

                send(m, k, high, t, FALL, DOWN, above)

    swaps = []
    for m in CLASS_C + CLASS_A + CLASS_B:
        if m in CLASS_C:
            ready(m, me)
            landed(m, first, y, FIRST)
            landed(m, second, 0, SECOND)
            at, more = me, (slot(first, m, y), slot(second, m, 0))
        else:
            z_ready(m, me, z)
            at, more = z, z_parts(m, z)[1][2:]

        @pl.when(z > 0)
        def _():
            landed(m, low, at, RISE)

        @pl.when(z < 3)
        def _():
            landed(m, high, at, FALL)

        with_ends(z, m, me, slot, own, side, low, high, combine, fin[m], more, at)
        size = SHAPES[m][0]
        swaps.append(
            pltpu.make_async_remote_copy(
                src_ref=fin[m].at[pl.ds(pl.multiple_of((1 - c) * size, 8), size), :],
                dst_ref=outs[m].at[:, cols(m, c)],
                send_sem=swap_send.at[m],
                recv_sem=swap_recv.at[m],
                device_id=peers[SIDE],
                device_id_type=MESH,
            )
        )
        swaps[-1].start()
        outs[m][:, cols(m, c)] = fin[m][pl.ds(pl.multiple_of(c * size, 8), size), :]
    for swap in swaps:
        swap.wait()
    for m, k in order:
        side_copy(m, k).wait_send()
    for m, k, land, index, sems, way, only in sent:
        if only is None:
            hop(m, k, land, index, sems, way).wait_send()
        else:

            @pl.when(only)
            def _(m=m, k=k, land=land, index=index, sems=sems, way=way):
                hop(m, k, land, index, sems, way).wait_send()


def with_ends(z, m, k, slot, own, side, low, high, combine, target, more, at=None):
    at = k if at is None else at
    base = (slot(own, m, k), slot(side, m, k)) + more

    @pl.when(z == 0)
    def _():
        combine(m, target, base + (slot(high, m, at),))

    @pl.when(z == 3)
    def _():
        combine(m, target, base + (slot(low, m, at),))

    @pl.when((z > 0) & (z < 3))
    def _():
        combine(m, target, base + (slot(low, m, at), slot(high, m, at)))


def reduce_grads(grads):
    def rows(count, m):
        size, wide = SHAPES[m]
        return pltpu.VMEM((count * 2 * size, wide // 2), BF16)

    every = range(5)
    scratch = (
        [rows(16, m) for m in every]
        + [rows(16, m) for m in every]
        + [rows(2 if m in CLASS_C else 8, m) for m in every]
        + [rows(1 if m in CLASS_C else 4, m) for m in every]
        + [rows(16 if m in CLASS_C else 4, m) for m in every]
        + [rows(16 if m in CLASS_C else 4, m) for m in every]
        + [pltpu.VMEM((2 * size, wide // 2), F32) for size, wide in SHAPES]
        + [pltpu.SemaphoreType.DMA((5,))]
        + [pltpu.SemaphoreType.DMA((5, 16))] * 2
        + [pltpu.SemaphoreType.DMA((5, 8))] * 2
        + [pltpu.SemaphoreType.DMA((5, 4))] * 2
        + [pltpu.SemaphoreType.DMA((5, 16))] * 4
        + [pltpu.SemaphoreType.DMA((5,))] * 2
    )
    return pl.pallas_call(
        reduce_kernel,
        out_shape=[jax.ShapeDtypeStruct(shape, F32) for shape in SHAPES],
        in_specs=[pl.BlockSpec(memory_space=pl.ANY)] * 5,
        out_specs=[pl.BlockSpec(memory_space=pltpu.VMEM)] * 5,
        scratch_shapes=scratch,
        compiler_params=pltpu.CompilerParams(
            collective_id=1, has_side_effects=True, vmem_limit_bytes=56 * 1024 * 1024
        ),
    )(*grads)


SUM_AT = (0, WIDE, WIDE + 3 * D, WIDE + 4 * D, WIDE + 8 * D, WIDE + 9 * D)
SUMS = WIDE + 9 * D + 128


def lanes_of(members):
    lane = lax.broadcasted_iota(jnp.int32, (1, 128), 1)
    row = jnp.zeros((1, 128), F32)
    for index, member in enumerate(members):
        row = jnp.where(lane == index, member, row)
    return row


def lane_at(row, index):
    lane = lax.broadcasted_iota(jnp.int32, row.shape, 1)
    return jnp.sum(jnp.where(lane == index, row, 0.0), 1, keepdims=True)


def column_of(row):
    size = row.shape[1]
    diagonal = lax.broadcasted_iota(jnp.int32, (size, size), 0) == lax.broadcasted_iota(
        jnp.int32, (size, size), 1
    )
    return jnp.sum(jnp.where(diagonal, row, 0.0), 1, keepdims=True)


def row_of(column):
    size = column.shape[0]
    diagonal = lax.broadcasted_iota(jnp.int32, (size, size), 0) == lax.broadcasted_iota(
        jnp.int32, (size, size), 1
    )
    return jnp.sum(jnp.where(diagonal, column, 0.0), 0, keepdims=True)


def total_sum(array):
    return jnp.sum(jnp.sum(array, 1, keepdims=True), 0, keepdims=True)


def sum_everywhere(value, first, second, third, sems):
    z, y, x, c = here()
    spot = y * 2 + x
    side_send, side_recv, plane_send, plane_recv, z_send, z_recv = sems

    def copy(src, dst, send, recv, peer):
        return pltpu.make_async_remote_copy(
            src_ref=src, dst_ref=dst, send_sem=send, recv_sem=recv, device_id=peer, device_id_type=MESH
        )

    first[0] = value
    swap = copy(first.at[0], first.at[1], side_send, side_recv, device(z, y, x, 1 - c))
    swap.start()
    swap.wait_recv()
    second[spot] = first[0] + first[1]
    plane = []
    for i, (to_y, to_x) in enumerate(((y, 1 - x), (1 - y, x), (1 - y, 1 - x))):
        plane.append(
            copy(second.at[spot], second.at[spot], plane_send.at[i], plane_recv.at[i], device(z, to_y, to_x, c))
        )
        plane[i].start()
    for member in plane:
        member.wait_recv()
    third[z] = (second[0] + second[1]) + (second[2] + second[3])
    column = []
    for i in range(3):
        to_z = (z + 1 + i) % 4
        column.append(copy(third.at[z], third.at[z], z_send.at[i], z_recv.at[i], device(to_z, y, x, c)))
        column[i].start()
    for member in column:
        member.wait_recv()
    for member in [swap] + plane + column:
        member.wait_send()
    return (third[0] + third[1]) + (third[2] + third[3])


def update_kernel(*refs):
    grads = refs[0:5]
    table, place, qkv_w, out_w, in_w, down_w, norms = refs[5:12]
    table_rows, table_cols, place_rows, place_cols, qkv_rows, qkv_cols = refs[12:18]
    out_rows, out_cols, in_rows, in_cols, down_rows, down_cols, moment, loss = refs[18:26]
    (loss_out, table_g, place_g, norm_g_out) = refs[26:30]
    lane_outs, side_outs, moment_out, news, norm_new = refs[30:36], refs[36:42], refs[42], refs[43:49], refs[49]
    first, second, third, first_small, second_small, third_small = refs[50:56]
    sems, small_sems = refs[56:62], refs[62:68]
    z, y, x, c = here()
    barrier = pltpu.get_barrier_semaphore()
    peers = [device(z, y, x, 1 - c), device(z, y, 1 - x, c), device(z, 1 - y, x, c), device(z, 1 - y, 1 - x, c)]
    peers += [device((z + 1 + i) % 4, y, x, c) for i in range(3)]
    for peer in peers:
        pl.semaphore_signal(barrier, inc=1, device_id=peer, device_id_type=MESH)

    decay = 1.0 - STEP ** (-0.8)
    fresh = 1.0 - decay
    devices = 32
    wide_g = grads[0][...]
    table_g[...] = wide_g[:, :VOCAB]
    place_g[...] = wide_g[:, PLACE_AT:]
    gs = (wide_g[:, :VOCAB], wide_g[:, PLACE_AT:], grads[1][...], grads[2][...], grads[3][...], grads[4][...])
    ws = (table, place, qkv_w, out_w, in_w, down_w)
    lane_olds = (table_rows, place_rows, qkv_cols, out_cols, in_cols, down_cols)
    side_olds = (table_cols, place_cols, qkv_rows, out_rows, in_rows, down_rows)

    wide_square = wide_g * wide_g + SQUARE_FLOOR
    squares = [wide_square[:, :VOCAB], wide_square[:, PLACE_AT:]] + [g * g + SQUARE_FLOOR for g in gs[2:]]
    side_news, side_totals = [], []
    for index in range(6):
        mean = jnp.sum(squares[index], 1, keepdims=True) / squares[index].shape[1]
        side_news.append(decay * column_of(side_olds[index][...]) + fresh * mean)
        side_outs[index][...] = row_of(side_news[index])
        side_totals.append(jnp.sum(side_news[index], 0, keepdims=True))
    weight_sq = [total_sum(w[...] * w[...]) for w in ws]
    norms_now = norms[...]
    norm_sq = jnp.sum(norms_now * norms_now, 1, keepdims=True)
    norm_sq = [norm_sq[i : i + 1] for i in range(6)]
    scalars = lanes_of(side_totals + weight_sq + norm_sq + [loss[...]])
    sums = jnp.concatenate(
        [jnp.sum(wide_square, 0, keepdims=True)]
        + [jnp.sum(square, 0, keepdims=True) for square in squares[2:]]
        + [scalars],
        1,
    )
    pl.semaphore_wait(barrier, 7)
    sums = sum_everywhere(sums, first, second, third, sems)
    parts = [sums[:, :VOCAB], sums[:, PLACE_AT:WIDE]]
    parts += [sums[:, SUM_AT[i] : SUM_AT[i + 1]] for i in range(1, 5)]
    scalars = sums[:, SUM_AT[5] :]
    loss_out[...] = lane_at(scalars, 18)
    updates, update_sq = [], []
    for index in range(6):
        height = gs[index].shape[0] * devices
        lane_new = decay * lane_olds[index][...] + fresh * (parts[index] / height)
        lane_outs[index][...] = lane_new
        if index < 2:
            mean = jnp.sum(lane_new, 1, keepdims=True) / lane_new.shape[1]
        else:
            mean = lane_at(scalars, index) / height
        update = gs[index] * lax.rsqrt(side_news[index] * lane_new / mean)
        updates.append(update)
        update_sq.append(total_sum(update * update))
    norm_tile = wide_g[:, 4096:4224]
    norm_g = jnp.concatenate([row_of(lane_at(norm_tile, NORM_AT - 4096 + i)) for i in range(6)], 0)
    norm_g_out[...] = norm_g
    moment_new = decay * moment[...] + fresh * (norm_g * norm_g + SQUARE_FLOOR)
    moment_out[...] = moment_new
    norm_update = norm_g * lax.rsqrt(moment_new)
    norm_update_sq = jnp.sum(norm_update * norm_update, 1, keepdims=True)
    totals = lanes_of(update_sq + [norm_update_sq[i : i + 1] for i in range(6)])
    totals = sum_everywhere(totals, first_small, second_small, third_small, small_sems)
    for index in range(6):
        entries = gs[index].shape[0] * gs[index].shape[1] * devices
        clip = jnp.maximum(1.0, jnp.sqrt(lane_at(totals, index) / entries))
        scale = learn_rate * jnp.sqrt(lane_at(scalars, 6 + index) / entries) / clip
        news[index][...] = ws[index][...] - scale * updates[index]
    for i in range(6):
        clip = jnp.maximum(1.0, jnp.sqrt(lane_at(totals, 6 + i) / D))
        scale = learn_rate * jnp.sqrt(lane_at(scalars, 12 + i) / D) / clip
        norm_new[i : i + 1, :] = norms_now[i : i + 1, :] - scale * norm_update[i : i + 1, :]


def update_weights(operands):
    lanes = (VOCAB, 512, 3 * D, D, 4 * D, D)
    held = (24, 24, 24, 24, 24, 96)
    shapes = [(1, 1), (24, VOCAB), (24, 512), (6, 24)]
    shapes += [(1, lane) for lane in lanes] + [(1, size) for size in held] + [(6, 24)]
    shapes += list(zip(held, lanes)) + [(6, 24)]
    exchange = [pltpu.SemaphoreType.DMA] * 2 + [pltpu.SemaphoreType.DMA((3,))] * 4
    return pl.pallas_call(
        update_kernel,
        out_shape=[jax.ShapeDtypeStruct(shape, F32) for shape in shapes],
        in_specs=[pl.BlockSpec(memory_space=pltpu.VMEM)] * len(operands),
        out_specs=[pl.BlockSpec(memory_space=pltpu.VMEM)] * len(shapes),
        scratch_shapes=[pltpu.VMEM((count, 1, SUMS), F32) for count in (2, 4, 4)]
        + [pltpu.VMEM((count, 1, 128), F32) for count in (2, 4, 4)]
        + exchange * 2,
        compiler_params=pltpu.CompilerParams(
            collective_id=2, has_side_effects=True, vmem_limit_bytes=48 * 1024 * 1024
        ),
    )(*operands)


def gelu_pair(hidden):
    normal_cdf = 0.5 * (1.0 + lax.erf(hidden * 0.7071067811865476))
    return (
        hidden * normal_cdf,
        normal_cdf + hidden * jnp.exp(-0.5 * hidden * hidden) * 0.3989422804014327,
    )


def norm_forward(value, gain, shift):
    centred = value - jnp.mean(value, -1, keepdims=True)
    inverse = lax.rsqrt(jnp.mean(centred * centred, -1, keepdims=True) + EPSILON)
    normed = centred * inverse
    return (normed * gain + shift, normed, inverse)


def norm_backward(grad_out, normed, inverse, gain):
    scaled = grad_out * gain
    back = inverse * (
        scaled
        - jnp.mean(scaled, -1, keepdims=True)
        - normed * jnp.mean(scaled * normed, -1, keepdims=True)
    )
    return (back, jnp.sum(grad_out * normed, 0), jnp.sum(grad_out, 0))


def mm(left, right, sides):
    return lax.dot_general(left, right, ((sides[:1], sides[1:]), ((), ())), preferred_element_type=F32)


def attend(qkv, allowed):
    by_head = qkv.reshape(qkv.shape[0], 3, HEADS, HEAD_DIM)
    query, key, value = by_head[:, 0], by_head[:, 1], by_head[:, 2]
    scores = jnp.einsum("qhe,khe->hqk", query, key, preferred_element_type=F32) * 0.125
    scores = jnp.where(allowed[None], scores, -1e30)
    highest = jnp.max(scores, -1, keepdims=True)
    raised = jnp.exp(scores - highest)
    summed = jnp.sum(raised, -1, keepdims=True)
    shares = (raised / summed).astype(BF16)
    mixture = jnp.einsum("hqk,khe->qhe", shares, value, preferred_element_type=F32)
    return mixture.astype(BF16).reshape(qkv.shape[0], D), highest + jnp.log(summed)


def attend_back(qkv, allowed, log_total, grad_mix):
    by_head = qkv.reshape(qkv.shape[0], 3, HEADS, HEAD_DIM)
    query, key, value = by_head[:, 0], by_head[:, 1], by_head[:, 2]
    grad_mix = grad_mix.reshape(qkv.shape[0], HEADS, HEAD_DIM)
    scores = jnp.einsum("qhe,khe->hqk", query, key, preferred_element_type=F32) * 0.125
    scores = jnp.where(allowed[None], scores, -1e30)
    shares = jnp.exp(scores - log_total)
    grad_share = jnp.einsum("qhe,khe->hqk", grad_mix, value, preferred_element_type=F32)
    grad_score = (shares * (grad_share - jnp.sum(shares * grad_share, -1, keepdims=True))).astype(BF16)
    grad_query = jnp.einsum("hqk,khe->qhe", grad_score, key, preferred_element_type=F32) * 0.125
    grad_key = jnp.einsum("hqk,qhe->khe", grad_score, query, preferred_element_type=F32) * 0.125
    grad_value = jnp.einsum("hqk,qhe->khe", shares.astype(BF16), grad_mix, preferred_element_type=F32)
    return jnp.stack((grad_query, grad_key, grad_value), 1).astype(BF16).reshape(qkv.shape)


def on_device(
    whole_mesh,
    long_ids,
    long_targets,
    long_mask,
    long_lengths,
    short_ids,
    short_targets,
    short_mask,
    short_lengths,
    table,
    position,
    qkv_weight,
    out_weight,
    in_weight,
    down_weight,
    norms,
    table_rows,
    table_cols,
    position_rows,
    position_cols,
    qkv_rows,
    qkv_cols,
    out_rows,
    out_cols,
    in_rows,
    in_cols,
    down_rows,
    down_cols,
    norm_moment,
):
    devices = lax.axis_size(("dp", "seq"))
    fast = whole_mesh == (8, 4)
    seq_index = lax.axis_index("seq")
    held = norms.shape[0]

    span = long_ids.shape[1]
    long_place = seq_index * span + lax.iota(jnp.int32, span)
    long_keep = (long_place[None, :] < long_lengths[:, None]).astype(jnp.int32)
    short_keep = (lax.iota(jnp.int32, SPAN)[None, :] < short_lengths[:, None]).astype(jnp.int32)
    long_pack = jnp.stack((long_ids, long_targets, long_mask * long_keep, long_keep), 1)
    short_pack = jnp.stack((short_ids, short_targets, short_mask * short_keep, short_keep), 1)
    moved = lax.all_to_all(
        jnp.concatenate((long_pack, short_pack[1:]), 0), "seq", split_axis=0, concat_axis=0, tiled=True
    )
    tokens = jnp.concatenate((moved, short_pack[:1]), 0)
    ids, targets, weight, keep = (tokens[:, i].reshape(-1) for i in range(4))
    weight = weight.astype(F32)
    count = tokens.shape[0] * span
    last = count - span
    alone = seq_index == lax.axis_size("seq") - 1
    token = lax.iota(jnp.int32, count)
    place = jnp.where(alone | (token >= last), token % span, token)
    row = jnp.where(alone | (token >= last), token // span, 0)
    allowed_long = (row[:last, None] == row[None, :last]) & (keep[None, :last] > 0)
    allowed_short = jnp.broadcast_to(keep[None, last:] > 0, (span, span))

    here_count = jnp.sum(long_pack[:, 2]) + jnp.sum(short_pack[:, 2])
    tall = table.T
    counts = jnp.broadcast_to(jnp.stack((here_count // 256, here_count % 256)).astype(F32)[None], (held, 2))
    wide_shard = jnp.concatenate(
        (tall, norms, counts, jnp.zeros((held, PLACE_AT - COUNT_AT - 2), F32), position.T), 1
    )
    shards = (wide_shard, qkv_weight, out_weight, in_weight, down_weight)
    if fast:
        wide_w, qkv_w, out_w, in_w, down_w = gather_weights(shards)
    else:
        wide_w, qkv_w, out_w, in_w, down_w = (
            lax.all_gather(shard.astype(BF16), ("dp", "seq"), axis=0, tiled=True) for shard in shards
        )
    gains = wide_w[:, NORM_AT : NORM_AT + 6].astype(F32)
    sums = jnp.sum(wide_w[:, COUNT_AT : COUNT_AT + 2].astype(F32), 0)
    mask_count = (sums[0] * 256.0 + sums[1]) / held
    inverse_count = 1.0 / mask_count

    column = lax.broadcasted_iota(jnp.int32, (1, WIDE), 1)
    chosen = ((ids[:, None] == column) | ((place[:, None] + PLACE_AT) == column)).astype(BF16)
    embedded = mm(chosen, wide_w, (1, 1))
    first, normed_a, inverse_a = norm_forward(embedded, gains[:, 0], gains[:, 1])
    first_b = first.astype(BF16)
    qkv_b = mm(first_b, qkv_w, (1, 0)).astype(BF16)
    mix_long, total_long = attend(qkv_b[:last], allowed_long)
    mix_short, total_short = attend(qkv_b[last:], allowed_short)
    mixture = jnp.concatenate((mix_long, mix_short), 0)
    second, normed_b, inverse_b = norm_forward(first + mm(mixture, out_w, (1, 0)), gains[:, 2], gains[:, 3])
    second_b = second.astype(BF16)
    hidden = mm(second_b, in_w, (1, 0))
    active, slope = gelu_pair(hidden)
    active_b = active.astype(BF16)
    third, normed_c, inverse_c = norm_forward(second + mm(active_b, down_w, (1, 0)), gains[:, 4], gains[:, 5])
    third_b = third.astype(BF16)
    logits = jnp.where(column < VOCAB, mm(third_b, wide_w, (1, 0)), -1e30)
    highest = jnp.max(logits, -1, keepdims=True)
    log_sum = highest + jnp.log(jnp.sum(jnp.exp(logits - highest), -1, keepdims=True))
    onehot = targets[:, None] == column
    picked = jnp.sum(jnp.where(onehot, logits, 0.0), -1)
    loss_part = jnp.sum(weight * (log_sum[:, 0] - picked))
    grad_logit = (
        (jnp.exp(logits - log_sum) - onehot.astype(F32)) * (weight * inverse_count)[:, None]
    ).astype(BF16)
    grad_third = mm(grad_logit, wide_w, (1, 1))
    grad_second, gain_c, shift_c = norm_backward(grad_third, normed_c, inverse_c, gains[:, 4])
    grad_ffn = grad_second.astype(BF16)
    down_grad = mm(active_b, grad_ffn, (0, 0)).astype(BF16)
    grad_hidden = (mm(grad_ffn, down_w, (1, 1)) * slope).astype(BF16)
    in_grad = mm(second_b, grad_hidden, (0, 0)).astype(BF16)
    grad_second = grad_second + mm(grad_hidden, in_w, (1, 1))
    grad_first, gain_b, shift_b = norm_backward(grad_second, normed_b, inverse_b, gains[:, 2])
    grad_attn = grad_first.astype(BF16)
    out_grad = mm(mixture, grad_attn, (0, 0)).astype(BF16)
    grad_mix = mm(grad_attn, out_w, (1, 1)).astype(BF16)
    grad_qkv = jnp.concatenate(
        (
            attend_back(qkv_b[:last], allowed_long, total_long, grad_mix[:last]),
            attend_back(qkv_b[last:], allowed_short, total_short, grad_mix[last:]),
        ),
        0,
    )
    qkv_grad = mm(first_b, grad_qkv, (0, 0)).astype(BF16)
    grad_first = grad_first + mm(grad_qkv, qkv_w, (1, 1))
    grad_embed, gain_a, shift_a = norm_backward(grad_first, normed_a, inverse_a, gains[:, 0])
    wide_grad = mm(
        jnp.concatenate((third_b, grad_embed.astype(BF16)), 0),
        jnp.concatenate((grad_logit, chosen), 0),
        (0, 0),
    )
    norm_part = jnp.stack((gain_a, shift_a, gain_b, shift_b, gain_c, shift_c), 1)
    wide_grad = lax.dynamic_update_slice(wide_grad.astype(BF16), norm_part.astype(BF16), (0, NORM_AT))
    grads = (wide_grad, qkv_grad, out_grad, in_grad, down_grad)
    if fast:
        grads = reduce_grads(grads)
        row = lambda vector: vector.reshape(1, -1)
        found = update_weights(
            tuple(grads)
            + (tall, position.T, qkv_weight, out_weight, in_weight, down_weight, norms.T)
            + (row(table_rows), row(table_cols), row(position_rows), row(position_cols))
            + (row(qkv_rows), row(qkv_cols), row(out_rows), row(out_cols))
            + (row(in_rows), row(in_cols), row(down_rows), row(down_cols))
            + (norm_moment.T, loss_part.reshape(1, 1))
        )
        loss_sum, table_g, place_g, norm_g = found[0:4]
        lane_news = [member.reshape(-1) for member in found[4:10]]
        side_news = [member.reshape(-1) for member in found[10:16]]
        moment_new, norm_new = found[16], found[23]
        news = found[17:23]
        return (
            loss_sum.reshape(()),
            mask_count,
            table_g.T,
            place_g.T,
            grads[1],
            grads[2],
            grads[3],
            grads[4],
            norm_g.T,
            lane_news[0],
            side_news[0],
            lane_news[1],
            side_news[1],
            side_news[2],
            lane_news[2],
            side_news[3],
            lane_news[3],
            side_news[4],
            lane_news[4],
            side_news[5],
            lane_news[5],
            moment_new.T,
            news[0].T,
            news[1].T,
            news[2],
            news[3],
            news[4],
            news[5],
            norm_new.T,
        )
    wide_g, qkv_g, out_g, in_g, down_g = (
        lax.psum_scatter(grad.astype(F32), ("dp", "seq"), scatter_dimension=0, tiled=True) for grad in grads
    )
    table_g, place_g = wide_g[:, :VOCAB], wide_g[:, PLACE_AT:]
    norm_g = wide_g[:, NORM_AT : NORM_AT + 6]

    decay = 1.0 - STEP ** (-0.8)
    matrices = (
        (qkv_weight, qkv_g, qkv_rows, qkv_cols),
        (out_weight, out_g, out_rows, out_cols),
        (in_weight, in_g, in_rows, in_cols),
        (down_weight, down_g, down_rows, down_cols),
    )
    wide = (
        (tall, table_g, table_cols, table_rows),
        (position.T, place_g, position_cols, position_rows),
    )
    row_news = [
        decay * member[2] + (1.0 - decay) * jnp.mean(member[1] * member[1] + SQUARE_FLOOR, 1)
        for member in matrices + wide
    ]
    col_parts = [jnp.sum(member[1] * member[1] + SQUARE_FLOOR, 0) for member in matrices + wide]
    row_totals = jnp.stack([jnp.sum(rows_new) for rows_new in row_news])
    weight_sq = jnp.stack([jnp.sum(member[0] * member[0]) for member in matrices + wide])
    stats = lax.psum(
        col_parts + [row_totals, weight_sq, jnp.sum(norms * norms, 0), loss_part.reshape(1)], ("dp", "seq")
    )
    updates = []
    cols_out = []
    for index, member in enumerate(matrices + wide):
        full_rows = member[0].shape[0] * devices
        cols_new = decay * member[3] + (1.0 - decay) * stats[index] / full_rows
        if index < 4:
            mean = stats[6][index] / full_rows
        else:
            mean = jnp.mean(cols_new)
        updates.append(member[1] * lax.rsqrt(row_news[index][:, None] * cols_new[None, :] / mean))
        cols_out.append(cols_new)
    moment_new = decay * norm_moment + (1.0 - decay) * (norm_g * norm_g + SQUARE_FLOOR)
    norm_update = norm_g * lax.rsqrt(moment_new)
    update_sq = jnp.stack([jnp.sum(update * update) for update in updates])
    totals = lax.psum((update_sq, jnp.sum(norm_update * norm_update, 0)), ("dp", "seq"))
    news = []
    for index, member in enumerate(matrices + wide):
        entries = member[0].shape[0] * member[0].shape[1] * devices
        clip = jnp.maximum(1.0, jnp.sqrt(totals[0][index] / entries))
        news.append(
            member[0] - learn_rate * jnp.sqrt(stats[7][index] / entries) * updates[index] / clip
        )
    norm_rows = norms.shape[0] * devices
    norm_clip = jnp.maximum(1.0, jnp.sqrt(totals[1] / norm_rows))
    norm_new = norms - learn_rate * jnp.sqrt(stats[8] / norm_rows) * norm_update / norm_clip
    return (
        stats[9][0],
        mask_count,
        table_g.T,
        place_g.T,
        qkv_g,
        out_g,
        in_g,
        down_g,
        norm_g,
        cols_out[4],
        row_news[4],
        cols_out[5],
        row_news[5],
        row_news[0],
        cols_out[0],
        row_news[1],
        cols_out[1],
        row_news[2],
        cols_out[2],
        row_news[3],
        cols_out[3],
        moment_new,
        news[4].T,
        news[5].T,
        news[0],
        news[1],
        news[2],
        news[3],
        norm_new,
    )


def solution(mesh):
    split, wide = P(("dp", "seq"), None), P(None, ("dp", "seq"))
    shard, same = P(("dp", "seq")), P()
    return jax.shard_map(
        functools.partial(on_device, (mesh.shape["dp"], mesh.shape["seq"])),
        mesh=mesh,
        in_specs=(P("dp", "seq"),) * 3
        + (P("dp"),)
        + (split,) * 3
        + (shard,)
        + (wide,) * 2
        + (split,) * 5
        + (same, shard) * 2
        + (shard, same) * 4
        + (split,),
        out_specs=(same, same)
        + (wide,) * 2
        + (split,) * 5
        + (same, shard) * 2
        + (shard, same) * 4
        + (split,)
        + (wide,) * 2
        + (split,) * 5,
        check_vma=False,
    )
```

```python
import functools

import jax
import jax.numpy as jnp
from jax import lax
from jax.experimental import pallas as pl
from jax.experimental.pallas import tpu as pltpu
from jax.sharding import PartitionSpec as P

D = 768
HEADS = 12
HEAD_DIM = 64
VOCAB = 4101
STEP = 10
SPAN = 128

EPSILON = 1e-12
SQUARE_FLOOR = 1e-30
learn_rate = 0.3

MESH = pl.DeviceIdType.MESH
F32 = jnp.float32
BF16 = jnp.bfloat16

NORM_AT = VOCAB
COUNT_AT = VOCAB + 6
PLACE_AT = 4352
WIDE = PLACE_AT + 512

SHAPES = ((24, WIDE), (24, 3 * D), (24, D), (24, 4 * D), (96, D))
E_, Q_, O_, I_, D_ = range(5)
CLASS_A, CLASS_B, CLASS_C = (E_, O_), (Q_, D_), (I_,)
UP, DOWN, XWAY, YWAY, SIDE = range(5)


def here():
    dp, seq = lax.axis_index("dp"), lax.axis_index("seq")
    return dp // 2, dp % 2, seq // 2, seq % 2


def device(z, y, x, c):
    return {"dp": z * 2 + y, "seq": x * 2 + c}


def chip(z, y, x):
    return z * 4 + y * 2 + x


def near_first(z, s):
    inner = (z * (3 - z)) // 2
    found = s + inner * (1, 1, -2, 0)[s]
    return found + (z // 2) * (3 - 2 * found)


def greet(peers):
    barrier = pltpu.get_barrier_semaphore()
    z, y, x, c = here()

    @pl.when(z < 3)
    def _():
        pl.semaphore_signal(barrier, inc=1, device_id=peers[UP], device_id_type=MESH)

    @pl.when(z > 0)
    def _():
        pl.semaphore_signal(barrier, inc=1, device_id=peers[DOWN], device_id_type=MESH)

    for way in (XWAY, YWAY, SIDE):
        pl.semaphore_signal(barrier, inc=1, device_id=peers[way], device_id_type=MESH)

    @pl.when((z == 0) | (z == 3))
    def _():
        pl.semaphore_wait(barrier, 4)

    @pl.when((z > 0) & (z < 3))
    def _():
        pl.semaphore_wait(barrier, 5)


def all_peers():
    z, y, x, c = here()
    return (
        device(z + 1, y, x, c),
        device(z - 1, y, x, c),
        device(z, y, 1 - x, c),
        device(z, 1 - y, x, c),
        device(z, y, x, 1 - c),
    )


def gather_kernel(*refs):
    shards, outs, merge, mine = refs[0:5], refs[5:10], refs[10:15], refs[15:20]
    swap_send, swap_recv, local_sem, send_sem, link_recv, side_recv = refs[20:]
    z, y, x, c = here()
    peers = all_peers()
    me = chip(z, y, x)

    def part(m, k, half):
        size, wide = 2 * SHAPES[m][0], SHAPES[m][1] // 2
        return outs[m].at[
            pl.ds(pl.multiple_of(k * size, size), size), pl.ds(pl.multiple_of(half * wide, 128), wide)
        ]

    def copy_of(m, k, way, own):
        return pltpu.make_async_remote_copy(
            src_ref=mine[m] if own else part(m, k, c),
            dst_ref=part(m, k, c),
            send_sem=send_sem.at[m, k, way],
            recv_sem=(side_recv if way == SIDE else link_recv).at[m, k],
            device_id=peers[way],
            device_id_type=MESH,
        )

    sent = []

    def push(m, k, way, own=False, only=None):
        sent.append((m, k, way, own, only))
        if only is None:
            copy_of(m, k, way, own).start()
        else:

            @pl.when(only)
            def _():
                copy_of(m, k, way, own).start()

    def arrived(m, k):
        copy_of(m, k, XWAY, False).wait_recv()

    greet(peers)
    swaps = []
    for m, (size, wide) in enumerate(SHAPES):
        half = wide // 2
        swaps.append(
            pltpu.make_async_remote_copy(
                src_ref=shards[m].at[:, pl.ds(pl.multiple_of((1 - c) * half, 128), half)],
                dst_ref=merge[m].at[pl.ds(pl.multiple_of(c * size, 8), size), :],
                send_sem=swap_send.at[m],
                recv_sem=swap_recv.at[m],
                device_id=peers[SIDE],
                device_id_type=MESH,
            )
        )
        swaps[m].start()
    for m, (size, wide) in enumerate(SHAPES):
        half = wide // 2
        merge[m][pl.ds(pl.multiple_of(c * size, 8), size), :] = shards[m][
            :, pl.ds(pl.multiple_of(c * half, 128), half)
        ]

    keeps = []
    for m in (I_, E_, Q_, D_, O_):
        swaps[m].wait_recv()
        mine[m][...] = merge[m][...].astype(BF16)
        for way, only in ((UP, z < 3), (DOWN, z > 0), (XWAY, None), (YWAY, None), (SIDE, None)):
            push(m, me, way, True, only)
        keeps.append(pltpu.make_async_copy(mine[m], part(m, me, c), local_sem.at[m]))
        keeps[-1].start()

    def onward(m, k, far):
        push(m, k, UP, only=(far < z) & (z < 3))
        push(m, k, DOWN, only=(far > z) & (z > 0))

    def line(ms, s, ways):
        far = near_first(z, s)
        k = chip(far, y, x)
        for m in ms:
            arrived(m, k)
            onward(m, k, far)
            for way in ways:
                push(m, k, way)

    def second(ms, s, axis):
        far = near_first(z, s)
        k = chip(far, y, 1 - x) if axis == XWAY else chip(far, 1 - y, x)
        for m in ms:
            arrived(m, k)
            push(m, k, YWAY if axis == XWAY else XWAY)
            push(m, k, SIDE)

    def third(ms, s, axis):
        far = near_first(z, s)
        for other in range(2):
            k = chip(far, 1 - y, other) if axis == YWAY else chip(far, other, 1 - x)
            for m in ms:
                arrived(m, k)
                push(m, k, SIDE)

    def c_first():
        k = chip(z, 1 - y, x)
        for m in CLASS_C:
            arrived(m, k)
            push(m, k, XWAY)
            push(m, k, UP, only=z < 3)
            push(m, k, DOWN, only=z > 0)
            push(m, k, SIDE)

    def c_second():
        for other in (y, 1 - y):
            k = chip(z, other, 1 - x)
            for m in CLASS_C:
                arrived(m, k)
                push(m, k, UP, only=z < 3)
                push(m, k, DOWN, only=z > 0)
                push(m, k, SIDE)

    def c_line(s):
        far = near_first(z, s)
        for k in (chip(far, y, x), chip(far, 1 - y, x), chip(far, y, 1 - x), chip(far, 1 - y, 1 - x)):
            for m in CLASS_C:
                arrived(m, k)
                onward(m, k, far)
                push(m, k, SIDE)

    both = (XWAY, YWAY, SIDE)
    c_first()
    line(CLASS_A, 1, both)
    line(CLASS_B, 1, both)
    c_second()
    second(CLASS_A, 0, XWAY)
    second(CLASS_B, 0, YWAY)
    c_line(1)
    line(CLASS_A, 2, both)
    line(CLASS_B, 2, both)
    second(CLASS_A, 1, XWAY)
    second(CLASS_B, 1, YWAY)
    c_line(2)
    line(CLASS_A, 3, both)
    line(CLASS_B, 3, both)
    second(CLASS_A, 2, XWAY)
    second(CLASS_B, 2, YWAY)
    c_line(3)
    second(CLASS_A, 3, XWAY)
    second(CLASS_B, 3, YWAY)
    for s in range(4):
        third(CLASS_A, s, YWAY)
        third(CLASS_B, s, XWAY)
    for m in range(5):
        for k in range(16):
            pltpu.make_async_remote_copy(
                src_ref=part(m, k, 1 - c),
                dst_ref=part(m, k, 1 - c),
                send_sem=send_sem.at[m, k, SIDE],
                recv_sem=side_recv.at[m, k],
                device_id=peers[SIDE],
                device_id_type=MESH,
            ).wait_recv()
    for swap in swaps:
        swap.wait_send()
    for keep in keeps:
        keep.wait()
    for m, k, way, own, only in sent:
        if only is None:
            copy_of(m, k, way, own).wait_send()
        else:

            @pl.when(only)
            def _(m=m, k=k, way=way, own=own):
                copy_of(m, k, way, own).wait_send()


def gather_weights(shards):
    return pl.pallas_call(
        gather_kernel,
        out_shape=[jax.ShapeDtypeStruct((32 * size, wide), BF16) for size, wide in SHAPES],
        in_specs=[pl.BlockSpec(memory_space=pltpu.VMEM)] * 5,
        out_specs=[pl.BlockSpec(memory_space=pl.ANY)] * 5,
        scratch_shapes=[pltpu.VMEM((2 * size, wide // 2), F32) for size, wide in SHAPES]
        + [pltpu.VMEM((2 * size, wide // 2), BF16) for size, wide in SHAPES]
        + [
            pltpu.SemaphoreType.DMA((5,)),
            pltpu.SemaphoreType.DMA((5,)),
            pltpu.SemaphoreType.DMA((5,)),
            pltpu.SemaphoreType.DMA((5, 16, 5)),
            pltpu.SemaphoreType.DMA((5, 16)),
            pltpu.SemaphoreType.DMA((5, 16)),
        ],
        compiler_params=pltpu.CompilerParams(
            collective_id=0, has_side_effects=True, vmem_limit_bytes=48 * 1024 * 1024
        ),
    )(*shards)


def reduce_kernel(*refs):
    grads, outs = refs[0:5], refs[5:10]
    own, side, first, second, low, high, fin = (refs[10 + 5 * i : 15 + 5 * i] for i in range(7))
    own_sem, side_send, side_recv, first_send, first_recv, second_send, second_recv = refs[45:52]
    up_send, low_recv, down_send, high_recv, swap_send, swap_recv = refs[52:]
    z, y, x, c = here()
    peers = all_peers()
    me = chip(z, y, x)

    def slot(ref, m, index):
        size = 2 * SHAPES[m][0]
        return ref[m].at[pl.ds(pl.multiple_of(index * size, size), size), :]

    def cols(m, half):
        wide = SHAPES[m][1] // 2
        return pl.ds(pl.multiple_of(half * wide, 128), wide)

    def combine(m, target, parts):
        def step(j, carry):
            at = pl.ds(pl.multiple_of(j * 128, 128), 128)
            total = parts[0][:, at].astype(F32)
            for member in parts[1:]:
                total = total + member[:, at].astype(F32)
            target[:, at] = total.astype(target.dtype)
            return carry

        lax.fori_loop(0, SHAPES[m][1] // 256, step, 0)

    def side_copy(m, k):
        size = 2 * SHAPES[m][0]
        return pltpu.make_async_remote_copy(
            src_ref=grads[m].at[pl.ds(pl.multiple_of(k * size, size), size), cols(m, 1 - c)],
            dst_ref=slot(side, m, k),
            send_sem=side_send.at[m, k],
            recv_sem=side_recv.at[m, k],
            device_id=peers[SIDE],
            device_id_type=MESH,
        )

    def own_copy(m):
        return pltpu.make_async_copy(grads[m].at[:, cols(m, c)], own[m], own_sem.at[m])

    def hop(m, k, land, index, sems, way):
        return pltpu.make_async_remote_copy(
            src_ref=slot(own, m, k),
            dst_ref=slot(land, m, index),
            send_sem=sems[0].at[m, index],
            recv_sem=sems[1].at[m, index],
            device_id=peers[way],
            device_id_type=MESH,
        )

    FIRST, SECOND = (first_send, first_recv), (second_send, second_recv)
    RISE, FALL = (up_send, low_recv), (down_send, high_recv)
    sent = []

    def send(m, k, land, index, sems, way, only=None):
        sent.append((m, k, land, index, sems, way, only))
        hop(m, k, land, index, sems, way).start()

    def landed(m, land, index, sems):
        hop(m, me, land, index, sems, XWAY).wait_recv()

    def block(m, a, b, far):
        return chip(far, a, b) if m in CLASS_A else chip(far, b, a)

    def split(m):
        return (y, x, YWAY, XWAY) if m in CLASS_A else (x, y, XWAY, YWAY)

    greet(peers)
    for m in (E_, Q_, I_, D_, O_):
        own_copy(m).start()

    def side_order():
        for i in range(8):
            for m in CLASS_A + CLASS_B:
                a, b, _, _ = split(m)
                yield m, block(m, 1 - a, i % 2, i // 2)
            for m in CLASS_C:
                for n in range(2):
                    yield m, (z * 4 + 4 + 2 * i + n) % 16
        for i in range(8):
            for m in CLASS_A + CLASS_B:
                a, b, _, _ = split(m)
                other = 1 - b if i < 4 else b
                yield m, block(m, a, other, i % 4)

    order = list(side_order())
    for m, k in order:
        side_copy(m, k).start()

    loaded = set()

    def ready(m, k):
        if m not in loaded:
            loaded.add(m)
            own_copy(m).wait()
        side_copy(m, k).wait_recv()

    def c_rise(t, yx):
        k = t * 4 + yx
        below = z < t
        for m in CLASS_C:

            @pl.when(below)
            def _():
                side_copy(m, k).wait_recv()

                @pl.when(z == 0)
                def _():
                    combine(m, slot(own, m, k), (slot(own, m, k), slot(side, m, k)))

                @pl.when(z > 0)
                def _():
                    landed(m, low, k, RISE)
                    combine(m, slot(own, m, k), (slot(own, m, k), slot(side, m, k), slot(low, m, k)))

                send(m, k, low, k, RISE, UP, below)

    def c_fall(t, yx):
        k = t * 4 + yx
        above = z > t
        for m in CLASS_C:

            @pl.when(above)
            def _():
                side_copy(m, k).wait_recv()

                @pl.when(z == 3)
                def _():
                    combine(m, slot(own, m, k), (slot(own, m, k), slot(side, m, k)))

                @pl.when(z < 3)
                def _():
                    landed(m, high, k, FALL)
                    combine(m, slot(own, m, k), (slot(own, m, k), slot(side, m, k), slot(high, m, k)))

                send(m, k, high, k, FALL, DOWN, above)

    c_steps = []
    for t in range(3):
        for yx in range(4):
            c_steps.append((c_rise, 3 - t, yx))
            c_steps.append((c_fall, t, yx))

    for m in CLASS_C:
        loaded.add(m)
        own_copy(m).wait()
    for i in range(8):
        for m in CLASS_A + CLASS_B:
            a, b, way, _ = split(m)
            k = block(m, 1 - a, i % 2, i // 2)
            ready(m, k)
            combine(m, slot(own, m, k), (slot(own, m, k), slot(side, m, k)))
            send(m, k, first, i, FIRST, way)
        for call, t, yx in c_steps[3 * i : 3 * i + 3]:
            call(t, yx)

    for i in range(4):
        for m in CLASS_A + CLASS_B:
            a, b, _, way = split(m)
            k = block(m, a, 1 - b, i)
            ready(m, k)
            at = 2 * i + (1 - b)
            landed(m, first, at, FIRST)
            combine(m, slot(own, m, k), (slot(own, m, k), slot(side, m, k), slot(first, m, at)))
            send(m, k, second, i, SECOND, way)
        if i == 0:
            for m in CLASS_C:
                for other in range(2):
                    k = chip(z, other, 1 - x)
                    ready(m, k)

                    @pl.when(z > 0)
                    def _():
                        landed(m, low, k, RISE)

                    @pl.when(z < 3)
                    def _():
                        landed(m, high, k, FALL)

                    with_ends(z, m, k, slot, own, side, low, high, combine, slot(own, m, k), ())
                    send(m, k, first, other, FIRST, XWAY)
        if i == 2:
            for m in CLASS_C:
                k = chip(z, 1 - y, x)
                ready(m, k)

                @pl.when(z > 0)
                def _():
                    landed(m, low, k, RISE)

                @pl.when(z < 3)
                def _():
                    landed(m, high, k, FALL)

                landed(m, first, 1 - y, FIRST)
                with_ends(
                    z, m, k, slot, own, side, low, high, combine, slot(own, m, k), (slot(first, m, 1 - y),)
                )
                send(m, k, second, 0, SECOND, YWAY)

    def z_parts(m, t):
        a, b, _, _ = split(m)
        k = block(m, a, b, t)
        return k, (slot(own, m, k), slot(side, m, k), slot(first, m, 2 * t + b), slot(second, m, t))

    def z_ready(m, k, t):
        a, b, _, _ = split(m)
        side_copy(m, k).wait_recv()
        landed(m, first, 2 * t + b, FIRST)
        landed(m, second, t, SECOND)

    for step in range(3):
        t = 3 - step
        below = z < t
        for m in CLASS_A + CLASS_B:
            k, parts = z_parts(m, t)

            @pl.when(below)
            def _():
                z_ready(m, k, t)

                @pl.when(z == 0)
                def _():
                    combine(m, slot(own, m, k), parts)

                @pl.when(z > 0)
                def _():
                    landed(m, low, t, RISE)
                    combine(m, slot(own, m, k), parts + (slot(low, m, t),))

                send(m, k, low, t, RISE, UP, below)

        t = step
        above = z > t
        for m in CLASS_A + CLASS_B:
            k, parts = z_parts(m, t)

            @pl.when(above)
            def _():
                z_ready(m, k, t)

                @pl.when(z == 3)
                def _():
                    combine(m, slot(own, m, k), parts)

                @pl.when(z < 3)
                def _():
                    landed(m, high, t, FALL)
                    combine(m, slot(own, m, k), parts + (slot(high, m, t),))

                send(m, k, high, t, FALL, DOWN, above)

    swaps = []
    for m in CLASS_C + CLASS_A + CLASS_B:
        if m in CLASS_C:
            ready(m, me)
            landed(m, first, y, FIRST)
            landed(m, second, 0, SECOND)
            at, more = me, (slot(first, m, y), slot(second, m, 0))
        else:
            z_ready(m, me, z)
            at, more = z, z_parts(m, z)[1][2:]

        @pl.when(z > 0)
        def _():
            landed(m, low, at, RISE)

        @pl.when(z < 3)
        def _():
            landed(m, high, at, FALL)

        with_ends(z, m, me, slot, own, side, low, high, combine, fin[m], more, at)
        size = SHAPES[m][0]
        swaps.append(
            pltpu.make_async_remote_copy(
                src_ref=fin[m].at[pl.ds(pl.multiple_of((1 - c) * size, 8), size), :],
                dst_ref=outs[m].at[:, cols(m, c)],
                send_sem=swap_send.at[m],
                recv_sem=swap_recv.at[m],
                device_id=peers[SIDE],
                device_id_type=MESH,
            )
        )
        swaps[-1].start()
        outs[m][:, cols(m, c)] = fin[m][pl.ds(pl.multiple_of(c * size, 8), size), :]
    for swap in swaps:
        swap.wait()
    for m, k in order:
        side_copy(m, k).wait_send()
    for m, k, land, index, sems, way, only in sent:
        if only is None:
            hop(m, k, land, index, sems, way).wait_send()
        else:

            @pl.when(only)
            def _(m=m, k=k, land=land, index=index, sems=sems, way=way):
                hop(m, k, land, index, sems, way).wait_send()


def with_ends(z, m, k, slot, own, side, low, high, combine, target, more, at=None):
    at = k if at is None else at
    base = (slot(own, m, k), slot(side, m, k)) + more

    @pl.when(z == 0)
    def _():
        combine(m, target, base + (slot(high, m, at),))

    @pl.when(z == 3)
    def _():
        combine(m, target, base + (slot(low, m, at),))

    @pl.when((z > 0) & (z < 3))
    def _():
        combine(m, target, base + (slot(low, m, at), slot(high, m, at)))


def reduce_grads(grads):
    def rows(count, m):
        size, wide = SHAPES[m]
        return pltpu.VMEM((count * 2 * size, wide // 2), BF16)

    every = range(5)
    scratch = (
        [rows(16, m) for m in every]
        + [rows(16, m) for m in every]
        + [rows(2 if m in CLASS_C else 8, m) for m in every]
        + [rows(1 if m in CLASS_C else 4, m) for m in every]
        + [rows(16 if m in CLASS_C else 4, m) for m in every]
        + [rows(16 if m in CLASS_C else 4, m) for m in every]
        + [pltpu.VMEM((2 * size, wide // 2), F32) for size, wide in SHAPES]
        + [pltpu.SemaphoreType.DMA((5,))]
        + [pltpu.SemaphoreType.DMA((5, 16))] * 2
        + [pltpu.SemaphoreType.DMA((5, 8))] * 2
        + [pltpu.SemaphoreType.DMA((5, 4))] * 2
        + [pltpu.SemaphoreType.DMA((5, 16))] * 4
        + [pltpu.SemaphoreType.DMA((5,))] * 2
    )
    return pl.pallas_call(
        reduce_kernel,
        out_shape=[jax.ShapeDtypeStruct(shape, F32) for shape in SHAPES],
        in_specs=[pl.BlockSpec(memory_space=pl.ANY)] * 5,
        out_specs=[pl.BlockSpec(memory_space=pltpu.VMEM)] * 5,
        scratch_shapes=scratch,
        compiler_params=pltpu.CompilerParams(
            collective_id=1, has_side_effects=True, vmem_limit_bytes=56 * 1024 * 1024
        ),
    )(*grads)


SUM_AT = (0, WIDE, WIDE + 3 * D, WIDE + 4 * D, WIDE + 8 * D, WIDE + 9 * D)
SUMS = WIDE + 9 * D + 128


def lanes_of(members):
    lane = lax.broadcasted_iota(jnp.int32, (1, 128), 1)
    row = jnp.zeros((1, 128), F32)
    for index, member in enumerate(members):
        row = jnp.where(lane == index, member, row)
    return row


def lane_at(row, index):
    lane = lax.broadcasted_iota(jnp.int32, row.shape, 1)
    return jnp.sum(jnp.where(lane == index, row, 0.0), 1, keepdims=True)


def column_of(row):
    size = row.shape[1]
    diagonal = lax.broadcasted_iota(jnp.int32, (size, size), 0) == lax.broadcasted_iota(
        jnp.int32, (size, size), 1
    )
    return jnp.sum(jnp.where(diagonal, row, 0.0), 1, keepdims=True)


def row_of(column):
    size = column.shape[0]
    diagonal = lax.broadcasted_iota(jnp.int32, (size, size), 0) == lax.broadcasted_iota(
        jnp.int32, (size, size), 1
    )
    return jnp.sum(jnp.where(diagonal, column, 0.0), 0, keepdims=True)


def total_sum(array):
    return jnp.sum(jnp.sum(array, 1, keepdims=True), 0, keepdims=True)


def sum_everywhere(value, first, second, third, sems):
    z, y, x, c = here()
    spot = y * 2 + x
    side_send, side_recv, plane_send, plane_recv, z_send, z_recv = sems

    def copy(src, dst, send, recv, peer):
        return pltpu.make_async_remote_copy(
            src_ref=src, dst_ref=dst, send_sem=send, recv_sem=recv, device_id=peer, device_id_type=MESH
        )

    first[0] = value
    swap = copy(first.at[0], first.at[1], side_send, side_recv, device(z, y, x, 1 - c))
    swap.start()
    swap.wait_recv()
    second[spot] = first[0] + first[1]
    plane = []
    for i, (to_y, to_x) in enumerate(((y, 1 - x), (1 - y, x), (1 - y, 1 - x))):
        plane.append(
            copy(second.at[spot], second.at[spot], plane_send.at[i], plane_recv.at[i], device(z, to_y, to_x, c))
        )
        plane[i].start()
    for member in plane:
        member.wait_recv()
    third[z] = (second[0] + second[1]) + (second[2] + second[3])
    column = []
    for i in range(3):
        to_z = (z + 1 + i) % 4
        column.append(copy(third.at[z], third.at[z], z_send.at[i], z_recv.at[i], device(to_z, y, x, c)))
        column[i].start()
    for member in column:
        member.wait_recv()
    for member in [swap] + plane + column:
        member.wait_send()
    return (third[0] + third[1]) + (third[2] + third[3])


def update_kernel(*refs):
    grads = refs[0:5]
    table, place, qkv_w, out_w, in_w, down_w, norms = refs[5:12]
    table_rows, table_cols, place_rows, place_cols, qkv_rows, qkv_cols = refs[12:18]
    out_rows, out_cols, in_rows, in_cols, down_rows, down_cols, moment, loss = refs[18:26]
    (loss_out, table_g, place_g, norm_g_out) = refs[26:30]
    lane_outs, side_outs, moment_out, news, norm_new = refs[30:36], refs[36:42], refs[42], refs[43:49], refs[49]
    first, second, third, first_small, second_small, third_small = refs[50:56]
    sems, small_sems = refs[56:62], refs[62:68]
    z, y, x, c = here()
    barrier = pltpu.get_barrier_semaphore()
    peers = [device(z, y, x, 1 - c), device(z, y, 1 - x, c), device(z, 1 - y, x, c), device(z, 1 - y, 1 - x, c)]
    peers += [device((z + 1 + i) % 4, y, x, c) for i in range(3)]
    for peer in peers:
        pl.semaphore_signal(barrier, inc=1, device_id=peer, device_id_type=MESH)

    decay = 1.0 - STEP ** (-0.8)
    fresh = 1.0 - decay
    devices = 32
    wide_g = grads[0][...]
    table_g[...] = wide_g[:, :VOCAB]
    place_g[...] = wide_g[:, PLACE_AT:]
    gs = (wide_g[:, :VOCAB], wide_g[:, PLACE_AT:], grads[1][...], grads[2][...], grads[3][...], grads[4][...])
    ws = (table, place, qkv_w, out_w, in_w, down_w)
    lane_olds = (table_rows, place_rows, qkv_cols, out_cols, in_cols, down_cols)
    side_olds = (table_cols, place_cols, qkv_rows, out_rows, in_rows, down_rows)

    wide_square = wide_g * wide_g + SQUARE_FLOOR
    squares = [wide_square[:, :VOCAB], wide_square[:, PLACE_AT:]] + [g * g + SQUARE_FLOOR for g in gs[2:]]
    side_news, side_totals = [], []
    for index in range(6):
        mean = jnp.sum(squares[index], 1, keepdims=True) / squares[index].shape[1]
        side_news.append(decay * column_of(side_olds[index][...]) + fresh * mean)
        side_outs[index][...] = row_of(side_news[index])
        side_totals.append(jnp.sum(side_news[index], 0, keepdims=True))
    weight_sq = [total_sum(w[...] * w[...]) for w in ws]
    norms_now = norms[...]
    norm_sq = jnp.sum(norms_now * norms_now, 1, keepdims=True)
    norm_sq = [norm_sq[i : i + 1] for i in range(6)]
    scalars = lanes_of(side_totals + weight_sq + norm_sq + [loss[...]])
    sums = jnp.concatenate(
        [jnp.sum(wide_square, 0, keepdims=True)]
        + [jnp.sum(square, 0, keepdims=True) for square in squares[2:]]
        + [scalars],
        1,
    )
    pl.semaphore_wait(barrier, 7)
    sums = sum_everywhere(sums, first, second, third, sems)
    parts = [sums[:, :VOCAB], sums[:, PLACE_AT:WIDE]]
    parts += [sums[:, SUM_AT[i] : SUM_AT[i + 1]] for i in range(1, 5)]
    scalars = sums[:, SUM_AT[5] :]
    loss_out[...] = lane_at(scalars, 18)
    updates, update_sq = [], []
    for index in range(6):
        height = gs[index].shape[0] * devices
        lane_new = decay * lane_olds[index][...] + fresh * (parts[index] / height)
        lane_outs[index][...] = lane_new
        if index < 2:
            mean = jnp.sum(lane_new, 1, keepdims=True) / lane_new.shape[1]
        else:
            mean = lane_at(scalars, index) / height
        update = gs[index] * lax.rsqrt(side_news[index] * lane_new / mean)
        updates.append(update)
        update_sq.append(total_sum(update * update))
    norm_tile = wide_g[:, 4096:4224]
    norm_g = jnp.concatenate([row_of(lane_at(norm_tile, NORM_AT - 4096 + i)) for i in range(6)], 0)
    norm_g_out[...] = norm_g
    moment_new = decay * moment[...] + fresh * (norm_g * norm_g + SQUARE_FLOOR)
    moment_out[...] = moment_new
    norm_update = norm_g * lax.rsqrt(moment_new)
    norm_update_sq = jnp.sum(norm_update * norm_update, 1, keepdims=True)
    totals = lanes_of(update_sq + [norm_update_sq[i : i + 1] for i in range(6)])
    totals = sum_everywhere(totals, first_small, second_small, third_small, small_sems)
    for index in range(6):
        entries = gs[index].shape[0] * gs[index].shape[1] * devices
        clip = jnp.maximum(1.0, jnp.sqrt(lane_at(totals, index) / entries))
        scale = learn_rate * jnp.sqrt(lane_at(scalars, 6 + index) / entries) / clip
        news[index][...] = ws[index][...] - scale * updates[index]
    for i in range(6):
        clip = jnp.maximum(1.0, jnp.sqrt(lane_at(totals, 6 + i) / D))
        scale = learn_rate * jnp.sqrt(lane_at(scalars, 12 + i) / D) / clip
        norm_new[i : i + 1, :] = norms_now[i : i + 1, :] - scale * norm_update[i : i + 1, :]


def update_weights(operands):
    lanes = (VOCAB, 512, 3 * D, D, 4 * D, D)
    held = (24, 24, 24, 24, 24, 96)
    shapes = [(1, 1), (24, VOCAB), (24, 512), (6, 24)]
    shapes += [(1, lane) for lane in lanes] + [(1, size) for size in held] + [(6, 24)]
    shapes += list(zip(held, lanes)) + [(6, 24)]
    exchange = [pltpu.SemaphoreType.DMA] * 2 + [pltpu.SemaphoreType.DMA((3,))] * 4
    return pl.pallas_call(
        update_kernel,
        out_shape=[jax.ShapeDtypeStruct(shape, F32) for shape in shapes],
        in_specs=[pl.BlockSpec(memory_space=pltpu.VMEM)] * len(operands),
        out_specs=[pl.BlockSpec(memory_space=pltpu.VMEM)] * len(shapes),
        scratch_shapes=[pltpu.VMEM((count, 1, SUMS), F32) for count in (2, 4, 4)]
        + [pltpu.VMEM((count, 1, 128), F32) for count in (2, 4, 4)]
        + exchange * 2,
        compiler_params=pltpu.CompilerParams(
            collective_id=2, has_side_effects=True, vmem_limit_bytes=48 * 1024 * 1024
        ),
    )(*operands)


def gelu_pair(hidden):
    normal_cdf = 0.5 * (1.0 + lax.erf(hidden * 0.7071067811865476))
    return (
        hidden * normal_cdf,
        normal_cdf + hidden * jnp.exp(-0.5 * hidden * hidden) * 0.3989422804014327,
    )


def dot_nn(left, right):
    return jnp.dot(left, right, preferred_element_type=F32)


def dot_nt(left, right):
    return lax.dot_general(left, right, (((1,), (1,)), ((), ())), preferred_element_type=F32)


def dot_tn(left, right):
    return lax.dot_general(left, right, (((0,), (0,)), ((), ())), preferred_element_type=F32)


def at(index, size):
    return pl.ds(pl.multiple_of(index * size, size), size)


def each(count, body):
    def step(index, carry):
        body(index)
        return carry

    lax.fori_loop(0, count, step, 0)


ROWS = 128
TILE = 256
HALF = 320
TABLE_TILES = PLACE_AT // TILE


def head_lanes(first):
    lane = lax.broadcasted_iota(jnp.int32, (1, 128), 1)
    return (lane < HEAD_DIM) if first else (lane >= HEAD_DIM)


def layer_norm(value, gain, shift):
    centred = value - jnp.sum(value, 1, keepdims=True) / D
    inverse = lax.rsqrt(jnp.sum(centred * centred, 1, keepdims=True) / D + EPSILON)
    normed = centred * inverse
    return normed * gain + shift, normed, inverse


def layer_norm_back(grad, normed, inverse, gain):
    scaled = grad * gain
    return inverse * (
        scaled - jnp.sum(scaled, 1, keepdims=True) / D - normed * (jnp.sum(scaled * normed, 1, keepdims=True) / D)
    )


def put_lane(ref, rows, index, value):
    lane = lax.broadcasted_iota(jnp.int32, (1, 128), 1)
    ref[rows, :] = jnp.where(lane == index, value, ref[rows, :])


def set_bias(bias, cols, keys, last):
    same = cols[0:last, 4:5] == keys[1:2, 0:last]
    bias[...] = jnp.where(same & (keys[0:1, 0:last] > 0), 0.0, -1e30)


def forward_kernel(*refs):
    weights, (cols, keys) = refs[0:5], refs[5:7]
    loss_out, count_out, gains_out, norm_out, side = refs[7:12]
    x_t, mix_t, a_t, act_t, y_t, glog_out, slope_out, qkv_out, na_out, nb_out, grad_out = refs[12:23]
    wide, qkv_w, out_w, in_w, down_w = refs[23:28]
    value, na, nb, nc, grad, low_a, mix, qkv, act, slope, logits, pick, bias, turned, act_turned = refs[28:43]
    weight_sem, out_sem, turn_sem, act_sem = refs[43:47]
    tokens = value.shape[0]
    last = tokens - SPAN
    loads = [
        pltpu.make_async_copy(weights[m], (wide, qkv_w, out_w, in_w, down_w)[m], weight_sem.at[m]) for m in range(5)
    ]
    for load in loads:
        load.start()
    set_bias(bias, cols, keys, last)
    side[...] = jnp.zeros(side.shape, F32)
    turns = []

    def turn_out(source, target, slot):
        for copy in turns:
            if copy[1] == slot:
                copy[0].wait()
        turns[:] = [copy for copy in turns if copy[1] != slot]

        def part(index):
            turned[slot, :, at(index, ROWS)] = source[at(index, ROWS), :].T

        each(tokens // ROWS, part)
        copy = pltpu.make_async_copy(turned.at[slot], target, turn_sem.at[slot])
        copy.start()
        turns.append((copy, slot))

    outs = []

    def put_out(source, target):
        copy = pltpu.make_async_copy(source, target, out_sem.at[len(outs)])
        copy.start()
        outs.append(copy)

    loads[0].wait()
    for half in range(tokens // HALF):
        rows = pl.ds(half * HALF, HALF)

        def choose(index):
            column = lax.broadcasted_iota(jnp.int32, (1, TILE), 1) + index * TILE
            hit = (cols[rows, 0:1] == column) | (cols[rows, 1:2] == column)
            pick[:, at(index, TILE)] = jnp.where(hit, 1.0, 0.0).astype(BF16)

        each(WIDE // TILE, choose)

        def embed(index):
            value[rows, at(index, TILE)] = dot_nt(pick[...], wide[at(index, TILE), :])

        each(D // TILE, embed)

    gains = wide[:, 4096:4224].astype(F32).T
    gains_out[...] = gains[0:16]
    counts = jnp.sum(gains[11:13], 1, keepdims=True) / 24.0
    mask_count = counts[0:1] * 256.0 + counts[1:2]
    count_out[...] = mask_count
    inverse_count = 1.0 / mask_count
    norm_rows = [gains_out[5 + i : 6 + i, :] for i in range(6)]

    def norm_a(index):
        rows = at(index, ROWS)
        found, normed, inverse = layer_norm(value[rows, :], norm_rows[0], norm_rows[1])
        value[rows, :] = found
        low_a[rows, :] = found.astype(BF16)
        na[rows, :] = normed
        put_lane(side, rows, 12, inverse)

    each(tokens // ROWS, norm_a)
    put_out(na, na_out)
    loads[1].wait()

    def project(index):
        qkv[:, at(index, TILE)] = dot_nn(low_a[...], qkv_w[:, at(index, TILE)]).astype(BF16)

    each(3 * D // TILE, project)
    put_out(qkv, qkv_out)
    turn_out(low_a, x_t, 0)

    def attend_pair(pair):
        for start, size in ((0, last), (last, SPAN)):
            rows = pl.ds(start, size)
            query = qkv[rows, at(pair, 128)]
            key = qkv[rows, pl.ds(pl.multiple_of(D + pair * 128, 128), 128)]
            val = qkv[rows, pl.ds(pl.multiple_of(2 * D + pair * 128, 128), 128)]
            mask = bias[...] if start == 0 else jnp.where(keys[0:1, last:tokens] > 0, 0.0, -1e30)
            mixed = []
            for first in (True, False):
                chosen = jnp.where(head_lanes(first), query, jnp.zeros_like(query))
                scores = dot_nt(chosen, key) * 0.125 + mask
                highest = jnp.max(scores, 1, keepdims=True)
                raised = jnp.exp(scores - highest)
                summed = jnp.sum(raised, 1, keepdims=True)
                shares = (raised * (1.0 / summed)).astype(BF16)
                mixed.append(dot_nn(shares, val))
                put_lane(side, rows, 2 * pair + (0 if first else 1), highest + jnp.log(summed))
            mix[rows, at(pair, 128)] = jnp.where(head_lanes(True), mixed[0], mixed[1]).astype(BF16)

    each(HEADS // 2, attend_pair)
    loads[2].wait()

    def out_project(index):
        value[:, at(index, TILE)] = value[:, at(index, TILE)] + dot_nn(mix[...], out_w[:, at(index, TILE)])

    each(D // TILE, out_project)
    turn_out(mix, mix_t, 1)

    def norm_b(index):
        rows = at(index, ROWS)
        found, normed, inverse = layer_norm(value[rows, :], norm_rows[2], norm_rows[3])
        value[rows, :] = found
        low_a[rows, :] = found.astype(BF16)
        nb[rows, :] = normed
        put_lane(side, rows, 13, inverse)

    each(tokens // ROWS, norm_b)
    put_out(nb, nb_out)
    loads[3].wait()

    def feed_in(index):
        hidden = dot_nn(low_a[...], in_w[:, at(index, TILE)])
        active, slant = gelu_pair(hidden)
        active = active.astype(BF16)
        act[:, at(index, TILE)] = active
        slope[:, at(index, TILE)] = slant.astype(BF16)
        slot = lax.rem(index, 2)

        def copy():
            return pltpu.make_async_copy(act_turned.at[slot], act_t.at[at(index, TILE), :], act_sem.at[slot])

        @pl.when(index >= 2)
        def _():
            copy().wait()

        act_turned[slot] = active.T
        copy().start()

    each(4 * D // TILE, feed_in)
    for slot in range(2):
        pltpu.make_async_copy(act_turned.at[slot], act_t.at[0:TILE, :], act_sem.at[slot]).wait()
    put_out(slope, slope_out)
    turn_out(low_a, a_t, 0)
    loads[4].wait()

    def feed_out(index):
        value[:, at(index, TILE)] = value[:, at(index, TILE)] + dot_nn(act[...], down_w[:, at(index, TILE)])

    each(D // TILE, feed_out)

    def norm_c(index):
        rows = at(index, ROWS)
        found, normed, inverse = layer_norm(value[rows, :], norm_rows[4], norm_rows[5])
        low_a[rows, :] = found.astype(BF16)
        nc[rows, :] = normed
        put_lane(side, rows, 14, inverse)

    each(tokens // ROWS, norm_c)
    turn_out(low_a, y_t, 1)
    loss = jnp.zeros((1, 1), F32)
    for half in range(tokens // HALF):
        rows = pl.ds(half * HALF, HALF)
        target = cols[rows, 2:3]
        weight = cols[rows, 3:4].astype(F32)

        def lanes(index):
            return lax.broadcasted_iota(jnp.int32, (1, TILE), 1) + index * TILE

        def multiply(index, highest):
            found = dot_nn(low_a[rows, :], wide[:, at(index, TILE)])
            found = jnp.where(lanes(index) < VOCAB, found, -1e30)
            logits[:, at(index, TILE)] = found
            return jnp.maximum(highest, jnp.maximum(found[:, 0:128], found[:, 128:256]))

        highest = lax.fori_loop(0, TABLE_TILES, multiply, jnp.full((HALF, 128), -1e30, F32))
        highest = jnp.max(highest, 1, keepdims=True)

        def raise_to(index, carry):
            summed, picked = carry
            found = logits[:, at(index, TILE)]
            raised = jnp.exp(found - highest)
            logits[:, at(index, TILE)] = raised
            hit = jnp.where(lanes(index) == target, found, 0.0)
            return summed + raised[:, 0:128] + raised[:, 128:256], picked + hit[:, 0:128] + hit[:, 128:256]

        zero = jnp.zeros((HALF, 128), F32)
        summed, picked = lax.fori_loop(0, TABLE_TILES, raise_to, (zero, zero))
        summed = jnp.sum(summed, 1, keepdims=True)
        picked = jnp.sum(picked, 1, keepdims=True)
        loss = loss + jnp.sum(weight * (highest + jnp.log(summed) - picked), 0, keepdims=True)
        scale = weight * inverse_count
        share = scale / summed
        if half > 0:
            outs[-1].wait()

        def differ(index):
            found = logits[:, at(index, TILE)] * share - jnp.where(lanes(index) == target, scale, 0.0)
            pick[:, at(index, TILE)] = found.astype(BF16)

        each(TABLE_TILES, differ)
        put_out(pick.at[:, 0:PLACE_AT], glog_out.at[rows, :])

        def back(index):
            grad[rows, at(index, TILE)] = dot_nt(pick[:, 0:PLACE_AT], wide[at(index, TILE), 0:PLACE_AT])

        each(D // TILE, back)
    loss_out[...] = loss

    def norm_c_back(index, carry):
        gain, shift = carry
        rows = at(index, ROWS)
        inverse = lane_at(side[rows, :], 14)
        found, normed = grad[rows, :], nc[rows, :]
        grad[rows, :] = layer_norm_back(found, normed, inverse, norm_rows[4])
        return gain + jnp.sum(found * normed, 0, keepdims=True), shift + jnp.sum(found, 0, keepdims=True)

    zero = jnp.zeros((1, D), F32)
    gain, shift = lax.fori_loop(0, tokens // ROWS, norm_c_back, (zero, zero))
    norm_out[0:1, :] = gain
    norm_out[1:2, :] = shift
    put_out(grad, grad_out)
    for index, copy in enumerate(outs):
        if index != 4:
            copy.wait()
    for copy, _ in turns:
        copy.wait()


def forward(weights, cols, keys):
    tokens = cols.shape[0]
    vmem, hbm = pl.BlockSpec(memory_space=pltpu.VMEM), pl.BlockSpec(memory_space=pl.ANY)
    shape = jax.ShapeDtypeStruct
    small = [shape((1, 1), F32), shape((1, 1), F32), shape((16, D), F32), shape((2, D), F32), shape((tokens, 128), F32)]
    large = [shape((D, tokens), BF16)] * 3 + [shape((4 * D, tokens), BF16), shape((D, tokens), BF16)]
    large += [shape((tokens, PLACE_AT), BF16), shape((tokens, 4 * D), BF16), shape((tokens, 3 * D), BF16)]
    large += [shape((tokens, D), F32)] * 3
    return pl.pallas_call(
        forward_kernel,
        out_shape=small + large,
        in_specs=[hbm] * 5 + [vmem] * 2,
        out_specs=[vmem] * len(small) + [hbm] * len(large),
        scratch_shapes=[pltpu.VMEM((32 * size, wide), BF16) for size, wide in SHAPES]
        + [pltpu.VMEM((tokens, D), F32)] * 5
        + [pltpu.VMEM((tokens, D), BF16)] * 2
        + [
            pltpu.VMEM((tokens, 3 * D), BF16),
            pltpu.VMEM((tokens, 4 * D), BF16),
            pltpu.VMEM((tokens, 4 * D), BF16),
            pltpu.VMEM((HALF, PLACE_AT), F32),
            pltpu.VMEM((HALF, WIDE), BF16),
            pltpu.VMEM((tokens - SPAN, tokens - SPAN), F32),
            pltpu.VMEM((2, D, tokens), BF16),
            pltpu.VMEM((2, TILE, tokens), BF16),
            pltpu.SemaphoreType.DMA((5,)),
            pltpu.SemaphoreType.DMA((8,)),
            pltpu.SemaphoreType.DMA((2,)),
            pltpu.SemaphoreType.DMA((2,)),
        ],
        compiler_params=pltpu.CompilerParams(vmem_limit_bytes=62 * 1024 * 1024),
    )(*weights, cols, keys)


def backward_kernel(*refs):
    loaded, (cols, keys, side, gains) = refs[0:9], refs[9:13]
    norm_out, ge_t, gffn_out, gh_out, gattn_out, gqkv_out = refs[13:19]
    qkv_w, out_w, in_w, down_w, slope, qkv, na, nb, grad = refs[19:28]
    low, attn, gh, bias, turned, load_sem, out_sem = refs[28:35]
    tokens = grad.shape[0]
    last = tokens - SPAN
    held = (qkv_w, out_w, in_w, down_w, slope, qkv, na, nb, grad)
    loads = [pltpu.make_async_copy(loaded[i], held[i], load_sem.at[i]) for i in range(9)]
    order = (8, 3, 4, 2, 7, 1, 5, 0, 6)
    for i in order:
        loads[i].start()
    outs = []

    def put_out(source, target):
        copy = pltpu.make_async_copy(source, target, out_sem.at[len(outs)])
        copy.start()
        outs.append(copy)

    set_bias(bias, cols, keys, last)
    loads[8].wait()

    def round_grad(index):
        rows = at(index, ROWS)
        low[rows, :] = grad[rows, :].astype(BF16)

    each(tokens // ROWS, round_grad)
    put_out(low, gffn_out)
    loads[3].wait()
    loads[4].wait()

    def feed_out_back(index):
        found = dot_nt(low[...], down_w[at(index, TILE), :]) * slope[:, at(index, TILE)].astype(F32)
        gh[:, at(index, TILE)] = found.astype(BF16)

    each(4 * D // TILE, feed_out_back)
    put_out(gh, gh_out)
    loads[2].wait()

    def feed_in_back(index):
        grad[:, at(index, TILE)] = grad[:, at(index, TILE)] + dot_nt(gh[...], in_w[at(index, TILE), :])

    each(D // TILE, feed_in_back)
    loads[7].wait()
    outs[0].wait()
    zero = jnp.zeros((1, D), F32)

    def norm_b_back(index, carry):
        gain, shift = carry
        rows = at(index, ROWS)
        inverse = lane_at(side[rows, :], 13)
        found, normed = grad[rows, :], nb[rows, :]
        back = layer_norm_back(found, normed, inverse, gains[7:8, :])
        grad[rows, :] = back
        low[rows, :] = back.astype(BF16)
        return gain + jnp.sum(found * normed, 0, keepdims=True), shift + jnp.sum(found, 0, keepdims=True)

    gain, shift = lax.fori_loop(0, tokens // ROWS, norm_b_back, (zero, zero))
    norm_out[2:3, :] = gain
    norm_out[3:4, :] = shift
    put_out(low, gattn_out)
    loads[1].wait()

    def out_back(index):
        attn[:, at(index, TILE)] = dot_nt(low[...], out_w[at(index, TILE), :]).astype(BF16)

    each(D // TILE, out_back)
    loads[5].wait()

    def attend_pair_back(pair):
        for start, size in ((0, last), (last, SPAN)):
            rows = pl.ds(start, size)
            spots = [pl.ds(pl.multiple_of(i * D + pair * 128, 128), 128) for i in range(3)]
            query, key, val = (qkv[rows, spot] for spot in spots)
            given = attn[rows, at(pair, 128)]
            mask = bias[...] if start == 0 else jnp.where(keys[0:1, last:tokens] > 0, 0.0, -1e30)
            found = []
            for first in (True, False):
                lanes = head_lanes(first)
                chosen = jnp.where(lanes, query, jnp.zeros_like(query))
                mine = jnp.where(lanes, given, jnp.zeros_like(given))
                total = lane_at(side[rows, :], 2 * pair + (0 if first else 1))
                shares = jnp.exp(dot_nt(chosen, key) * 0.125 + mask - total)
                grad_share = dot_nt(mine, val)
                middle = jnp.sum(shares * grad_share, 1, keepdims=True)
                grad_score = (shares * (grad_share - middle)).astype(BF16)
                found.append(
                    (
                        dot_nn(grad_score, key) * 0.125,
                        dot_tn(grad_score, query) * 0.125,
                        dot_tn(shares.astype(BF16), given),
                    )
                )
            for i in range(3):
                qkv[rows, spots[i]] = jnp.where(head_lanes(True), found[0][i], found[1][i]).astype(BF16)

    each(HEADS // 2, attend_pair_back)
    put_out(qkv, gqkv_out)
    loads[0].wait()

    def project_back(index):
        grad[:, at(index, TILE)] = grad[:, at(index, TILE)] + dot_nt(qkv[...], qkv_w[at(index, TILE), :])

    each(D // TILE, project_back)
    loads[6].wait()

    def norm_a_back(index, carry):
        gain, shift = carry
        rows = at(index, ROWS)
        inverse = lane_at(side[rows, :], 12)
        found, normed = grad[rows, :], na[rows, :]
        turned[:, rows] = layer_norm_back(found, normed, inverse, gains[5:6, :]).astype(BF16).T
        return gain + jnp.sum(found * normed, 0, keepdims=True), shift + jnp.sum(found, 0, keepdims=True)

    gain, shift = lax.fori_loop(0, tokens // ROWS, norm_a_back, (zero, zero))
    norm_out[0:1, :] = gain
    norm_out[1:2, :] = shift
    put_out(turned, ge_t)
    for copy in outs[1:]:
        copy.wait()


def backward(weights, slope, qkv, na, nb, grad, cols, keys, side, gains):
    tokens = grad.shape[0]
    vmem, hbm = pl.BlockSpec(memory_space=pltpu.VMEM), pl.BlockSpec(memory_space=pl.ANY)
    shape = jax.ShapeDtypeStruct
    loaded = tuple(weights) + (slope, qkv, na, nb, grad)
    widths = (D, D, 4 * D, D, 3 * D)
    return pl.pallas_call(
        backward_kernel,
        out_shape=[shape((4, D), F32), shape((D, tokens), BF16)]
        + [shape((tokens, width), BF16) for width in (D, 4 * D, D, 3 * D)],
        in_specs=[hbm] * 9 + [vmem] * 4,
        out_specs=[vmem] + [hbm] * 5,
        scratch_shapes=[pltpu.VMEM(member.shape, member.dtype) for member in loaded]
        + [
            pltpu.VMEM((tokens, D), BF16),
            pltpu.VMEM((tokens, D), BF16),
            pltpu.VMEM((tokens, 4 * D), BF16),
            pltpu.VMEM((tokens - SPAN, tokens - SPAN), F32),
            pltpu.VMEM((D, tokens), BF16),
            pltpu.SemaphoreType.DMA((9,)),
            pltpu.SemaphoreType.DMA((5,)),
        ],
        compiler_params=pltpu.CompilerParams(vmem_limit_bytes=60 * 1024 * 1024),
    )(*loaded, cols, keys, side, gains)


def norm_forward(value, gain, shift):
    centred = value - jnp.mean(value, -1, keepdims=True)
    inverse = lax.rsqrt(jnp.mean(centred * centred, -1, keepdims=True) + EPSILON)
    normed = centred * inverse
    return (normed * gain + shift, normed, inverse)


def norm_backward(grad_out, normed, inverse, gain):
    scaled = grad_out * gain
    back = inverse * (
        scaled
        - jnp.mean(scaled, -1, keepdims=True)
        - normed * jnp.mean(scaled * normed, -1, keepdims=True)
    )
    return (back, jnp.sum(grad_out * normed, 0), jnp.sum(grad_out, 0))


def mm(left, right, sides):
    return lax.dot_general(left, right, ((sides[:1], sides[1:]), ((), ())), preferred_element_type=F32)


def attend(qkv, allowed):
    by_head = qkv.reshape(qkv.shape[0], 3, HEADS, HEAD_DIM)
    query, key, value = by_head[:, 0], by_head[:, 1], by_head[:, 2]
    scores = jnp.einsum("qhe,khe->hqk", query, key, preferred_element_type=F32) * 0.125
    scores = jnp.where(allowed[None], scores, -1e30)
    highest = jnp.max(scores, -1, keepdims=True)
    raised = jnp.exp(scores - highest)
    summed = jnp.sum(raised, -1, keepdims=True)
    shares = (raised / summed).astype(BF16)
    mixture = jnp.einsum("hqk,khe->qhe", shares, value, preferred_element_type=F32)
    return mixture.astype(BF16).reshape(qkv.shape[0], D), highest + jnp.log(summed)


def attend_back(qkv, allowed, log_total, grad_mix):
    by_head = qkv.reshape(qkv.shape[0], 3, HEADS, HEAD_DIM)
    query, key, value = by_head[:, 0], by_head[:, 1], by_head[:, 2]
    grad_mix = grad_mix.reshape(qkv.shape[0], HEADS, HEAD_DIM)
    scores = jnp.einsum("qhe,khe->hqk", query, key, preferred_element_type=F32) * 0.125
    scores = jnp.where(allowed[None], scores, -1e30)
    shares = jnp.exp(scores - log_total)
    grad_share = jnp.einsum("qhe,khe->hqk", grad_mix, value, preferred_element_type=F32)
    grad_score = (shares * (grad_share - jnp.sum(shares * grad_share, -1, keepdims=True))).astype(BF16)
    grad_query = jnp.einsum("hqk,khe->qhe", grad_score, key, preferred_element_type=F32) * 0.125
    grad_key = jnp.einsum("hqk,qhe->khe", grad_score, query, preferred_element_type=F32) * 0.125
    grad_value = jnp.einsum("hqk,qhe->khe", shares.astype(BF16), grad_mix, preferred_element_type=F32)
    return jnp.stack((grad_query, grad_key, grad_value), 1).astype(BF16).reshape(qkv.shape)


def on_device(
    whole_mesh,
    long_ids,
    long_targets,
    long_mask,
    long_lengths,
    short_ids,
    short_targets,
    short_mask,
    short_lengths,
    table,
    position,
    qkv_weight,
    out_weight,
    in_weight,
    down_weight,
    norms,
    table_rows,
    table_cols,
    position_rows,
    position_cols,
    qkv_rows,
    qkv_cols,
    out_rows,
    out_cols,
    in_rows,
    in_cols,
    down_rows,
    down_cols,
    norm_moment,
):
    devices = lax.axis_size(("dp", "seq"))
    fast = whole_mesh == (8, 4)
    seq_index = lax.axis_index("seq")
    held = norms.shape[0]

    span = long_ids.shape[1]
    long_place = seq_index * span + lax.iota(jnp.int32, span)
    long_keep = (long_place[None, :] < long_lengths[:, None]).astype(jnp.int32)
    short_keep = (lax.iota(jnp.int32, SPAN)[None, :] < short_lengths[:, None]).astype(jnp.int32)
    long_pack = jnp.stack((long_ids, long_targets, long_mask * long_keep, long_keep), 1)
    short_pack = jnp.stack((short_ids, short_targets, short_mask * short_keep, short_keep), 1)
    moved = lax.all_to_all(
        jnp.concatenate((long_pack, short_pack[1:]), 0), "seq", split_axis=0, concat_axis=0, tiled=True
    )
    tokens = jnp.concatenate((moved, short_pack[:1]), 0)
    ids, targets, weight, keep = (tokens[:, i].reshape(-1) for i in range(4))
    weight = weight.astype(F32)
    count = tokens.shape[0] * span
    last = count - span
    alone = seq_index == lax.axis_size("seq") - 1
    token = lax.iota(jnp.int32, count)
    place = jnp.where(alone | (token >= last), token % span, token)
    row = jnp.where(alone | (token >= last), token // span, 0)
    allowed_long = (row[:last, None] == row[None, :last]) & (keep[None, :last] > 0)
    allowed_short = jnp.broadcast_to(keep[None, last:] > 0, (span, span))

    here_count = jnp.sum(long_pack[:, 2]) + jnp.sum(short_pack[:, 2])
    tall = table.T
    counts = jnp.broadcast_to(jnp.stack((here_count // 256, here_count % 256)).astype(F32)[None], (held, 2))
    wide_shard = jnp.concatenate(
        (tall, norms, counts, jnp.zeros((held, PLACE_AT - COUNT_AT - 2), F32), position.T), 1
    )
    shards = (wide_shard, qkv_weight, out_weight, in_weight, down_weight)
    if fast:
        wide_w, qkv_w, out_w, in_w, down_w = gather_weights(shards)
    else:
        wide_w, qkv_w, out_w, in_w, down_w = (
            lax.all_gather(shard.astype(BF16), ("dp", "seq"), axis=0, tiled=True) for shard in shards
        )
    column = lax.broadcasted_iota(jnp.int32, (1, WIDE), 1)
    chosen = ((ids[:, None] == column) | ((place[:, None] + PLACE_AT) == column)).astype(BF16)
    if fast:
        zero = jnp.zeros_like(ids)
        cols = jnp.stack((ids, place + PLACE_AT, targets, weight.astype(jnp.int32), row) + (zero,) * 3, 1)
        keys = jnp.stack((keep, row) + (zero,) * 6, 0)
        found = forward((wide_w, qkv_w, out_w, in_w, down_w), cols, keys)
        loss_part, mask_count, gains, norm_c, side = found[0:5]
        loss_part, mask_count = loss_part[0, 0], mask_count[0, 0]
        x_t, mix_t, a_t, act_t, y_t, grad_logit, slope, qkv_b, normed_a, normed_b, grad_second = found[5:]
        norm_ab, ge_t, grad_ffn, grad_hidden, grad_attn, grad_qkv = backward(
            (qkv_w, out_w, in_w, down_w), slope, qkv_b, normed_a, normed_b, grad_second, cols, keys, side, gains
        )
        down_grad = mm(act_t, grad_ffn, (1, 0)).astype(BF16)
        in_grad = mm(a_t, grad_hidden, (1, 0)).astype(BF16)
        out_grad = mm(mix_t, grad_attn, (1, 0)).astype(BF16)
        qkv_grad = mm(x_t, grad_qkv, (1, 0)).astype(BF16)
        padded = jnp.concatenate((grad_logit, jnp.zeros((ids.shape[0], WIDE - PLACE_AT), BF16)), 1)
        wide_grad = mm(
            jnp.concatenate((y_t, ge_t), 1), jnp.concatenate((padded, chosen), 0), (1, 0)
        )
        norm_part = jnp.concatenate((norm_ab, norm_c), 0).T
        wide_grad = lax.dynamic_update_slice(wide_grad.astype(BF16), norm_part.astype(BF16), (0, NORM_AT))
        grads = (wide_grad, qkv_grad, out_grad, in_grad, down_grad)
        grads = reduce_grads(grads)
        row = lambda vector: vector.reshape(1, -1)
        found = update_weights(
            tuple(grads)
            + (tall, position.T, qkv_weight, out_weight, in_weight, down_weight, norms.T)
            + (row(table_rows), row(table_cols), row(position_rows), row(position_cols))
            + (row(qkv_rows), row(qkv_cols), row(out_rows), row(out_cols))
            + (row(in_rows), row(in_cols), row(down_rows), row(down_cols))
            + (norm_moment.T, loss_part.reshape(1, 1))
        )
        loss_sum, table_g, place_g, norm_g = found[0:4]
        lane_news = [member.reshape(-1) for member in found[4:10]]
        side_news = [member.reshape(-1) for member in found[10:16]]
        moment_new, norm_new = found[16], found[23]
        news = found[17:23]
        return (
            loss_sum.reshape(()),
            mask_count,
            table_g.T,
            place_g.T,
            grads[1],
            grads[2],
            grads[3],
            grads[4],
            norm_g.T,
            lane_news[0],
            side_news[0],
            lane_news[1],
            side_news[1],
            side_news[2],
            lane_news[2],
            side_news[3],
            lane_news[3],
            side_news[4],
            lane_news[4],
            side_news[5],
            lane_news[5],
            moment_new.T,
            news[0].T,
            news[1].T,
            news[2],
            news[3],
            news[4],
            news[5],
            norm_new.T,
        )
    gains = wide_w[:, NORM_AT : NORM_AT + 6].astype(F32)
    sums = jnp.sum(wide_w[:, COUNT_AT : COUNT_AT + 2].astype(F32), 0)
    mask_count = (sums[0] * 256.0 + sums[1]) / held
    inverse_count = 1.0 / mask_count

    embedded = mm(chosen, wide_w, (1, 1))
    first, normed_a, inverse_a = norm_forward(embedded, gains[:, 0], gains[:, 1])
    first_b = first.astype(BF16)
    qkv_b = mm(first_b, qkv_w, (1, 0)).astype(BF16)
    mix_long, total_long = attend(qkv_b[:last], allowed_long)
    mix_short, total_short = attend(qkv_b[last:], allowed_short)
    mixture = jnp.concatenate((mix_long, mix_short), 0)
    second, normed_b, inverse_b = norm_forward(first + mm(mixture, out_w, (1, 0)), gains[:, 2], gains[:, 3])
    second_b = second.astype(BF16)
    hidden = mm(second_b, in_w, (1, 0))
    active, slope = gelu_pair(hidden)
    active_b = active.astype(BF16)
    third, normed_c, inverse_c = norm_forward(second + mm(active_b, down_w, (1, 0)), gains[:, 4], gains[:, 5])
    third_b = third.astype(BF16)
    logits = jnp.where(column < VOCAB, mm(third_b, wide_w, (1, 0)), -1e30)
    highest = jnp.max(logits, -1, keepdims=True)
    log_sum = highest + jnp.log(jnp.sum(jnp.exp(logits - highest), -1, keepdims=True))
    onehot = targets[:, None] == column
    picked = jnp.sum(jnp.where(onehot, logits, 0.0), -1)
    loss_part = jnp.sum(weight * (log_sum[:, 0] - picked))
    grad_logit = (
        (jnp.exp(logits - log_sum) - onehot.astype(F32)) * (weight * inverse_count)[:, None]
    ).astype(BF16)
    grad_third = mm(grad_logit, wide_w, (1, 1))
    grad_second, gain_c, shift_c = norm_backward(grad_third, normed_c, inverse_c, gains[:, 4])
    grad_ffn = grad_second.astype(BF16)
    down_grad = mm(active_b, grad_ffn, (0, 0)).astype(BF16)
    grad_hidden = (mm(grad_ffn, down_w, (1, 1)) * slope).astype(BF16)
    in_grad = mm(second_b, grad_hidden, (0, 0)).astype(BF16)
    grad_second = grad_second + mm(grad_hidden, in_w, (1, 1))
    grad_first, gain_b, shift_b = norm_backward(grad_second, normed_b, inverse_b, gains[:, 2])
    grad_attn = grad_first.astype(BF16)
    out_grad = mm(mixture, grad_attn, (0, 0)).astype(BF16)
    grad_mix = mm(grad_attn, out_w, (1, 1)).astype(BF16)
    grad_qkv = jnp.concatenate(
        (
            attend_back(qkv_b[:last], allowed_long, total_long, grad_mix[:last]),
            attend_back(qkv_b[last:], allowed_short, total_short, grad_mix[last:]),
        ),
        0,
    )
    qkv_grad = mm(first_b, grad_qkv, (0, 0)).astype(BF16)
    grad_first = grad_first + mm(grad_qkv, qkv_w, (1, 1))
    grad_embed, gain_a, shift_a = norm_backward(grad_first, normed_a, inverse_a, gains[:, 0])
    wide_grad = mm(
        jnp.concatenate((third_b, grad_embed.astype(BF16)), 0),
        jnp.concatenate((grad_logit, chosen), 0),
        (0, 0),
    )
    norm_part = jnp.stack((gain_a, shift_a, gain_b, shift_b, gain_c, shift_c), 1)
    wide_grad = lax.dynamic_update_slice(wide_grad.astype(BF16), norm_part.astype(BF16), (0, NORM_AT))
    grads = (wide_grad, qkv_grad, out_grad, in_grad, down_grad)
    wide_g, qkv_g, out_g, in_g, down_g = (
        lax.psum_scatter(grad.astype(F32), ("dp", "seq"), scatter_dimension=0, tiled=True) for grad in grads
    )
    table_g, place_g = wide_g[:, :VOCAB], wide_g[:, PLACE_AT:]
    norm_g = wide_g[:, NORM_AT : NORM_AT + 6]

    decay = 1.0 - STEP ** (-0.8)
    matrices = (
        (qkv_weight, qkv_g, qkv_rows, qkv_cols),
        (out_weight, out_g, out_rows, out_cols),
        (in_weight, in_g, in_rows, in_cols),
        (down_weight, down_g, down_rows, down_cols),
    )
    wide = (
        (tall, table_g, table_cols, table_rows),
        (position.T, place_g, position_cols, position_rows),
    )
    row_news = [
        decay * member[2] + (1.0 - decay) * jnp.mean(member[1] * member[1] + SQUARE_FLOOR, 1)
        for member in matrices + wide
    ]
    col_parts = [jnp.sum(member[1] * member[1] + SQUARE_FLOOR, 0) for member in matrices + wide]
    row_totals = jnp.stack([jnp.sum(rows_new) for rows_new in row_news])
    weight_sq = jnp.stack([jnp.sum(member[0] * member[0]) for member in matrices + wide])
    stats = lax.psum(
        col_parts + [row_totals, weight_sq, jnp.sum(norms * norms, 0), loss_part.reshape(1)], ("dp", "seq")
    )
    updates = []
    cols_out = []
    for index, member in enumerate(matrices + wide):
        full_rows = member[0].shape[0] * devices
        cols_new = decay * member[3] + (1.0 - decay) * stats[index] / full_rows
        if index < 4:
            mean = stats[6][index] / full_rows
        else:
            mean = jnp.mean(cols_new)
        updates.append(member[1] * lax.rsqrt(row_news[index][:, None] * cols_new[None, :] / mean))
        cols_out.append(cols_new)
    moment_new = decay * norm_moment + (1.0 - decay) * (norm_g * norm_g + SQUARE_FLOOR)
    norm_update = norm_g * lax.rsqrt(moment_new)
    update_sq = jnp.stack([jnp.sum(update * update) for update in updates])
    totals = lax.psum((update_sq, jnp.sum(norm_update * norm_update, 0)), ("dp", "seq"))
    news = []
    for index, member in enumerate(matrices + wide):
        entries = member[0].shape[0] * member[0].shape[1] * devices
        clip = jnp.maximum(1.0, jnp.sqrt(totals[0][index] / entries))
        news.append(
            member[0] - learn_rate * jnp.sqrt(stats[7][index] / entries) * updates[index] / clip
        )
    norm_rows = norms.shape[0] * devices
    norm_clip = jnp.maximum(1.0, jnp.sqrt(totals[1] / norm_rows))
    norm_new = norms - learn_rate * jnp.sqrt(stats[8] / norm_rows) * norm_update / norm_clip
    return (
        stats[9][0],
        mask_count,
        table_g.T,
        place_g.T,
        qkv_g,
        out_g,
        in_g,
        down_g,
        norm_g,
        cols_out[4],
        row_news[4],
        cols_out[5],
        row_news[5],
        row_news[0],
        cols_out[0],
        row_news[1],
        cols_out[1],
        row_news[2],
        cols_out[2],
        row_news[3],
        cols_out[3],
        moment_new,
        news[4].T,
        news[5].T,
        news[0],
        news[1],
        news[2],
        news[3],
        norm_new,
    )


def solution(mesh):
    split, wide = P(("dp", "seq"), None), P(None, ("dp", "seq"))
    shard, same = P(("dp", "seq")), P()
    return jax.shard_map(
        functools.partial(on_device, (mesh.shape["dp"], mesh.shape["seq"])),
        mesh=mesh,
        in_specs=(P("dp", "seq"),) * 3
        + (P("dp"),)
        + (split,) * 3
        + (shard,)
        + (wide,) * 2
        + (split,) * 5
        + (same, shard) * 2
        + (shard, same) * 4
        + (split,),
        out_specs=(same, same)
        + (wide,) * 2
        + (split,) * 5
        + (same, shard) * 2
        + (shard, same) * 4
        + (split,)
        + (wide,) * 2
        + (split,) * 5,
        check_vma=False,
    )
```

```python
import functools

import jax
import jax.numpy as jnp
from jax import lax
from jax.experimental import pallas as pl
from jax.experimental.pallas import tpu as pltpu
from jax.sharding import PartitionSpec as P

D = 768
HEADS = 12
HEAD_DIM = 64
VOCAB = 4101
STEP = 10
SPAN = 128

EPSILON = 1e-12
SQUARE_FLOOR = 1e-30
learn_rate = 0.3

MESH = pl.DeviceIdType.MESH
F32 = jnp.float32
BF16 = jnp.bfloat16

NORM_AT = VOCAB
COUNT_AT = VOCAB + 6
TABLE_END = 4352
PLACE_AT = 4608
WIDE = PLACE_AT + 512

SHAPES = ((24, WIDE), (24, 3 * D), (24, D), (24, 4 * D), (96, D))
E_, Q_, O_, I_, D_ = range(5)
CLASS_A, CLASS_B, CLASS_C = (E_, O_), (Q_, D_), (I_,)
UP, DOWN, XWAY, YWAY, SIDE = range(5)


def here():
    dp, seq = lax.axis_index("dp"), lax.axis_index("seq")
    return dp // 2, dp % 2, seq // 2, seq % 2


def device(z, y, x, c):
    return {"dp": z * 2 + y, "seq": x * 2 + c}


def chip(z, y, x):
    return z * 4 + y * 2 + x


def near_first(z, s):
    inner = (z * (3 - z)) // 2
    found = s + inner * (1, 1, -2, 0)[s]
    return found + (z // 2) * (3 - 2 * found)


def greet(peers):
    barrier = pltpu.get_barrier_semaphore()
    z, y, x, c = here()

    @pl.when(z < 3)
    def _():
        pl.semaphore_signal(barrier, inc=1, device_id=peers[UP], device_id_type=MESH)

    @pl.when(z > 0)
    def _():
        pl.semaphore_signal(barrier, inc=1, device_id=peers[DOWN], device_id_type=MESH)

    for way in (XWAY, YWAY, SIDE):
        pl.semaphore_signal(barrier, inc=1, device_id=peers[way], device_id_type=MESH)

    @pl.when((z == 0) | (z == 3))
    def _():
        pl.semaphore_wait(barrier, 4)

    @pl.when((z > 0) & (z < 3))
    def _():
        pl.semaphore_wait(barrier, 5)


def all_peers():
    z, y, x, c = here()
    return (
        device(z + 1, y, x, c),
        device(z - 1, y, x, c),
        device(z, y, 1 - x, c),
        device(z, 1 - y, x, c),
        device(z, y, x, 1 - c),
    )


def gather_kernel(*refs):
    shards, outs, squares, merge, mine = refs[0:5], refs[5:10], refs[10], refs[11:16], refs[16:21]
    swap_send, swap_recv, local_sem, send_sem, link_recv, side_recv = refs[21:]
    z, y, x, c = here()
    peers = all_peers()
    me = chip(z, y, x)

    def part(m, k, half):
        size, wide = 2 * SHAPES[m][0], SHAPES[m][1] // 2
        return outs[m].at[
            pl.ds(pl.multiple_of(k * size, size), size), pl.ds(pl.multiple_of(half * wide, 128), wide)
        ]

    def copy_of(m, k, way, own):
        return pltpu.make_async_remote_copy(
            src_ref=mine[m] if own else part(m, k, c),
            dst_ref=part(m, k, c),
            send_sem=send_sem.at[m, k, way],
            recv_sem=(side_recv if way == SIDE else link_recv).at[m, k],
            device_id=peers[way],
            device_id_type=MESH,
        )

    sent = []

    def push(m, k, way, own=False, only=None):
        sent.append((m, k, way, own, only))
        if only is None:
            copy_of(m, k, way, own).start()
        else:

            @pl.when(only)
            def _():
                copy_of(m, k, way, own).start()

    def arrived(m, k):
        copy_of(m, k, XWAY, False).wait_recv()

    greet(peers)
    swaps = []
    for m, (size, wide) in enumerate(SHAPES):
        half = wide // 2
        swaps.append(
            pltpu.make_async_remote_copy(
                src_ref=shards[m].at[:, pl.ds(pl.multiple_of((1 - c) * half, 128), half)],
                dst_ref=merge[m].at[pl.ds(pl.multiple_of(c * size, 8), size), :],
                send_sem=swap_send.at[m],
                recv_sem=swap_recv.at[m],
                device_id=peers[SIDE],
                device_id_type=MESH,
            )
        )
        swaps[m].start()
    for m, (size, wide) in enumerate(SHAPES):
        half = wide // 2
        merge[m][pl.ds(pl.multiple_of(c * size, 8), size), :] = shards[m][
            :, pl.ds(pl.multiple_of(c * half, 128), half)
        ]

    keeps = []
    for m in (I_, E_, Q_, D_, O_):
        swaps[m].wait_recv()
        mine[m][...] = merge[m][...].astype(BF16)
        for way, only in ((UP, z < 3), (DOWN, z > 0), (XWAY, None), (YWAY, None), (SIDE, None)):
            push(m, me, way, True, only)
        keeps.append(pltpu.make_async_copy(mine[m], part(m, me, c), local_sem.at[m]))
        keeps[-1].start()

    wide_sq = shards[E_][...] * shards[E_][...]
    found = [total_sum(wide_sq[:, :VOCAB]), total_sum(wide_sq[:, PLACE_AT:])]
    found += [total_sum(shards[m][...] * shards[m][...]) for m in (Q_, O_, I_, D_)]
    norm_tile = jnp.sum(wide_sq[:, 4096:4224], 0, keepdims=True)
    found += [lane_at(norm_tile, NORM_AT - 4096 + i) for i in range(6)]
    squares[...] = lanes_of(found)

    def onward(m, k, far):
        push(m, k, UP, only=(far < z) & (z < 3))
        push(m, k, DOWN, only=(far > z) & (z > 0))

    def line(ms, s, ways):
        far = near_first(z, s)
        k = chip(far, y, x)
        for m in ms:
            arrived(m, k)
            onward(m, k, far)
            for way in ways:
                push(m, k, way)

    def second(ms, s, axis):
        far = near_first(z, s)
        k = chip(far, y, 1 - x) if axis == XWAY else chip(far, 1 - y, x)
        for m in ms:
            arrived(m, k)
            push(m, k, YWAY if axis == XWAY else XWAY)
            push(m, k, SIDE)

    def third(ms, s, axis):
        far = near_first(z, s)
        for other in range(2):
            k = chip(far, 1 - y, other) if axis == YWAY else chip(far, other, 1 - x)
            for m in ms:
                arrived(m, k)
                push(m, k, SIDE)

    def c_first():
        k = chip(z, 1 - y, x)
        for m in CLASS_C:
            arrived(m, k)
            push(m, k, XWAY)
            push(m, k, UP, only=z < 3)
            push(m, k, DOWN, only=z > 0)
            push(m, k, SIDE)

    def c_second():
        for other in (y, 1 - y):
            k = chip(z, other, 1 - x)
            for m in CLASS_C:
                arrived(m, k)
                push(m, k, UP, only=z < 3)
                push(m, k, DOWN, only=z > 0)
                push(m, k, SIDE)

    def c_line(s):
        far = near_first(z, s)
        for k in (chip(far, y, x), chip(far, 1 - y, x), chip(far, y, 1 - x), chip(far, 1 - y, 1 - x)):
            for m in CLASS_C:
                arrived(m, k)
                onward(m, k, far)
                push(m, k, SIDE)

    both = (XWAY, YWAY, SIDE)
    c_first()
    line(CLASS_A, 1, both)
    line(CLASS_B, 1, both)
    c_second()
    second(CLASS_A, 0, XWAY)
    second(CLASS_B, 0, YWAY)
    c_line(1)
    line(CLASS_A, 2, both)
    line(CLASS_B, 2, both)
    second(CLASS_A, 1, XWAY)
    second(CLASS_B, 1, YWAY)
    c_line(2)
    line(CLASS_A, 3, both)
    line(CLASS_B, 3, both)
    second(CLASS_A, 2, XWAY)
    second(CLASS_B, 2, YWAY)
    c_line(3)
    second(CLASS_A, 3, XWAY)
    second(CLASS_B, 3, YWAY)
    for s in range(4):
        third(CLASS_A, s, YWAY)
        third(CLASS_B, s, XWAY)
    for m in range(5):
        for k in range(16):
            pltpu.make_async_remote_copy(
                src_ref=part(m, k, 1 - c),
                dst_ref=part(m, k, 1 - c),
                send_sem=send_sem.at[m, k, SIDE],
                recv_sem=side_recv.at[m, k],
                device_id=peers[SIDE],
                device_id_type=MESH,
            ).wait_recv()
    for swap in swaps:
        swap.wait_send()
    for keep in keeps:
        keep.wait()
    for m, k, way, own, only in sent:
        if only is None:
            copy_of(m, k, way, own).wait_send()
        else:

            @pl.when(only)
            def _(m=m, k=k, way=way, own=own):
                copy_of(m, k, way, own).wait_send()


def gather_weights(shards):
    return pl.pallas_call(
        gather_kernel,
        out_shape=[jax.ShapeDtypeStruct((32 * size, wide), BF16) for size, wide in SHAPES]
        + [jax.ShapeDtypeStruct((1, 128), F32)],
        in_specs=[pl.BlockSpec(memory_space=pltpu.VMEM)] * 5,
        out_specs=[pl.BlockSpec(memory_space=pl.ANY)] * 5 + [pl.BlockSpec(memory_space=pltpu.VMEM)],
        scratch_shapes=[pltpu.VMEM((2 * size, wide // 2), F32) for size, wide in SHAPES]
        + [pltpu.VMEM((2 * size, wide // 2), BF16) for size, wide in SHAPES]
        + [
            pltpu.SemaphoreType.DMA((5,)),
            pltpu.SemaphoreType.DMA((5,)),
            pltpu.SemaphoreType.DMA((5,)),
            pltpu.SemaphoreType.DMA((5, 16, 5)),
            pltpu.SemaphoreType.DMA((5, 16)),
            pltpu.SemaphoreType.DMA((5, 16)),
        ],
        compiler_params=pltpu.CompilerParams(
            collective_id=0, has_side_effects=True, vmem_limit_bytes=48 * 1024 * 1024
        ),
    )(*shards)


SUM_AT = (0, WIDE, WIDE + 3 * D, WIDE + 4 * D, WIDE + 8 * D, WIDE + 9 * D)
SUMS = WIDE + 9 * D + 256


def lanes_of(members):
    lane = lax.broadcasted_iota(jnp.int32, (1, 128), 1)
    row = jnp.zeros((1, 128), F32)
    for index, member in enumerate(members):
        row = jnp.where(lane == index, member, row)
    return row


def lane_at(row, index):
    lane = lax.broadcasted_iota(jnp.int32, row.shape, 1)
    return jnp.sum(jnp.where(lane == index, row, 0.0), 1, keepdims=True)


def column_of(row):
    size = row.shape[1]
    diagonal = lax.broadcasted_iota(jnp.int32, (size, size), 0) == lax.broadcasted_iota(
        jnp.int32, (size, size), 1
    )
    return jnp.sum(jnp.where(diagonal, row, 0.0), 1, keepdims=True)


def row_of(column):
    size = column.shape[0]
    diagonal = lax.broadcasted_iota(jnp.int32, (size, size), 0) == lax.broadcasted_iota(
        jnp.int32, (size, size), 1
    )
    return jnp.sum(jnp.where(diagonal, column, 0.0), 0, keepdims=True)


def total_sum(array):
    return jnp.sum(jnp.sum(array, 1, keepdims=True), 0, keepdims=True)


def sum_everywhere(value, first, second, third, sems):
    z, y, x, c = here()
    spot = y * 2 + x
    side_send, side_recv, plane_send, plane_recv, z_send, z_recv = sems

    def copy(src, dst, send, recv, peer):
        return pltpu.make_async_remote_copy(
            src_ref=src, dst_ref=dst, send_sem=send, recv_sem=recv, device_id=peer, device_id_type=MESH
        )

    first[0] = value
    swap = copy(first.at[0], first.at[1], side_send, side_recv, device(z, y, x, 1 - c))
    swap.start()
    swap.wait_recv()
    second[spot] = first[0] + first[1]
    plane = []
    for i, (to_y, to_x) in enumerate(((y, 1 - x), (1 - y, x), (1 - y, 1 - x))):
        plane.append(
            copy(second.at[spot], second.at[spot], plane_send.at[i], plane_recv.at[i], device(z, to_y, to_x, c))
        )
        plane[i].start()
    for member in plane:
        member.wait_recv()
    third[z] = (second[0] + second[1]) + (second[2] + second[3])
    column = []
    for i in range(3):
        to_z = (z + 1 + i) % 4
        column.append(copy(third.at[z], third.at[z], z_send.at[i], z_recv.at[i], device(to_z, y, x, c)))
        column[i].start()
    for member in column:
        member.wait_recv()
    for member in [swap] + plane + column:
        member.wait_send()
    return (third[0] + third[1]) + (third[2] + third[3])


def gelu_pair(hidden):
    normal_cdf = 0.5 * (1.0 + lax.erf(hidden * 0.7071067811865476))
    return (
        hidden * normal_cdf,
        normal_cdf + hidden * jnp.exp(-0.5 * hidden * hidden) * 0.3989422804014327,
    )


def dot_nn(left, right):
    return jnp.dot(left, right, preferred_element_type=F32)


def dot_nt(left, right):
    return lax.dot_general(left, right, (((1,), (1,)), ((), ())), preferred_element_type=F32)


def dot_tn(left, right):
    return lax.dot_general(left, right, (((0,), (0,)), ((), ())), preferred_element_type=F32)


def at(index, size):
    return pl.ds(pl.multiple_of(index * size, size), size)


def each(count, body):
    def step(index, carry):
        body(index)
        return carry

    lax.fori_loop(0, count, step, 0)


ROWS = 128
TILE = 256
HALF = 320
TABLE_TILES = TABLE_END // TILE


def head_lanes(first):
    lane = lax.broadcasted_iota(jnp.int32, (1, 128), 1)
    return (lane < HEAD_DIM) if first else (lane >= HEAD_DIM)


def layer_norm(value, gain, shift):
    centred = value - jnp.sum(value, 1, keepdims=True) / D
    inverse = lax.rsqrt(jnp.sum(centred * centred, 1, keepdims=True) / D + EPSILON)
    normed = centred * inverse
    return normed * gain + shift, normed, inverse


def layer_norm_back(grad, normed, inverse, gain):
    scaled = grad * gain
    return inverse * (
        scaled - jnp.sum(scaled, 1, keepdims=True) / D - normed * (jnp.sum(scaled * normed, 1, keepdims=True) / D)
    )


def put_lane(ref, rows, index, value):
    lane = lax.broadcasted_iota(jnp.int32, (1, 128), 1)
    ref[rows, :] = jnp.where(lane == index, value, ref[rows, :])


def set_bias(bias, cols, keys, last):
    same = cols[0:last, 4:5] == keys[1:2, 0:last]
    bias[...] = jnp.where(same & (keys[0:1, 0:last] > 0), 0.0, -1e30)


def forward_kernel(*refs):
    weights, (cols, keys) = refs[0:5], refs[5:7]
    loss_out, count_out, gains_out, norm_out, side = refs[7:12]
    x_t, mix_t, a_t, act_t, y_t, glog_out, slope_out, qkv_out, na_out, nb_out, grad_out = refs[12:23]
    wide, qkv_w, out_w, in_w, down_w = refs[23:28]
    value, na, nb, nc, grad, low_a, mix, qkv, act, slope, logits, pick, bias, turned, act_turned = refs[28:43]
    weight_sem, out_sem, turn_sem, act_sem = refs[43:47]
    tokens = value.shape[0]
    last = tokens - SPAN
    loads = [
        pltpu.make_async_copy(weights[m], (wide, qkv_w, out_w, in_w, down_w)[m], weight_sem.at[m]) for m in range(5)
    ]
    for load in loads:
        load.start()
    set_bias(bias, cols, keys, last)
    side[...] = jnp.zeros(side.shape, F32)
    turns = []

    def turn_out(source, target, slot):
        for copy in turns:
            if copy[1] == slot:
                copy[0].wait()
        turns[:] = [copy for copy in turns if copy[1] != slot]

        def part(index):
            turned[slot, :, at(index, ROWS)] = source[at(index, ROWS), :].T

        each(tokens // ROWS, part)
        copy = pltpu.make_async_copy(turned.at[slot], target, turn_sem.at[slot])
        copy.start()
        turns.append((copy, slot))

    outs = []

    def put_out(source, target):
        copy = pltpu.make_async_copy(source, target, out_sem.at[len(outs)])
        copy.start()
        outs.append(copy)

    loads[0].wait()
    for half in range(tokens // HALF):
        rows = pl.ds(half * HALF, HALF)

        def choose(index):
            column = lax.broadcasted_iota(jnp.int32, (1, TILE), 1) + index * TILE
            hit = (cols[rows, 0:1] == column) | (cols[rows, 1:2] == column)
            pick[:, at(index, TILE)] = jnp.where(hit, 1.0, 0.0).astype(BF16)

        each(WIDE // TILE, choose)

        def embed(index):
            value[rows, at(index, TILE)] = dot_nt(pick[...], wide[at(index, TILE), :])

        each(D // TILE, embed)

    gains = wide[:, 4096:4224].astype(F32).T
    gains_out[...] = gains[0:16]
    counts = jnp.sum(gains[11:13], 1, keepdims=True) / 24.0
    mask_count = counts[0:1] * 256.0 + counts[1:2]
    count_out[...] = mask_count
    inverse_count = 1.0 / mask_count
    norm_rows = [gains_out[5 + i : 6 + i, :] for i in range(6)]

    def norm_a(index):
        rows = at(index, ROWS)
        found, normed, inverse = layer_norm(value[rows, :], norm_rows[0], norm_rows[1])
        value[rows, :] = found
        low_a[rows, :] = found.astype(BF16)
        na[rows, :] = normed
        put_lane(side, rows, 12, inverse)

    each(tokens // ROWS, norm_a)
    put_out(na, na_out)
    loads[1].wait()

    def project(index):
        qkv[:, at(index, TILE)] = dot_nn(low_a[...], qkv_w[:, at(index, TILE)]).astype(BF16)

    each(3 * D // TILE, project)
    put_out(qkv, qkv_out)
    turn_out(low_a, x_t, 0)

    def attend_pair(pair):
        for start, size in ((0, last), (last, SPAN)):
            rows = pl.ds(start, size)
            query = qkv[rows, at(pair, 128)]
            key = qkv[rows, pl.ds(pl.multiple_of(D + pair * 128, 128), 128)]
            val = qkv[rows, pl.ds(pl.multiple_of(2 * D + pair * 128, 128), 128)]
            mask = bias[...] if start == 0 else jnp.where(keys[0:1, last:tokens] > 0, 0.0, -1e30)
            mixed = []
            for first in (True, False):
                chosen = jnp.where(head_lanes(first), query, jnp.zeros_like(query))
                scores = dot_nt(chosen, key) * 0.125 + mask
                highest = jnp.max(scores, 1, keepdims=True)
                raised = jnp.exp(scores - highest)
                summed = jnp.sum(raised, 1, keepdims=True)
                shares = (raised * (1.0 / summed)).astype(BF16)
                mixed.append(dot_nn(shares, val))
                put_lane(side, rows, 2 * pair + (0 if first else 1), highest + jnp.log(summed))
            mix[rows, at(pair, 128)] = jnp.where(head_lanes(True), mixed[0], mixed[1]).astype(BF16)

    each(HEADS // 2, attend_pair)
    loads[2].wait()

    def out_project(index):
        value[:, at(index, TILE)] = value[:, at(index, TILE)] + dot_nn(mix[...], out_w[:, at(index, TILE)])

    each(D // TILE, out_project)
    turn_out(mix, mix_t, 1)

    def norm_b(index):
        rows = at(index, ROWS)
        found, normed, inverse = layer_norm(value[rows, :], norm_rows[2], norm_rows[3])
        value[rows, :] = found
        low_a[rows, :] = found.astype(BF16)
        nb[rows, :] = normed
        put_lane(side, rows, 13, inverse)

    each(tokens // ROWS, norm_b)
    put_out(nb, nb_out)
    loads[3].wait()

    def feed_in(index):
        hidden = dot_nn(low_a[...], in_w[:, at(index, TILE)])
        active, slant = gelu_pair(hidden)
        active = active.astype(BF16)
        act[:, at(index, TILE)] = active
        slope[:, at(index, TILE)] = slant.astype(BF16)
        slot = lax.rem(index, 2)

        def copy():
            return pltpu.make_async_copy(act_turned.at[slot], act_t.at[at(index, TILE), :], act_sem.at[slot])

        @pl.when(index >= 2)
        def _():
            copy().wait()

        act_turned[slot] = active.T
        copy().start()

    each(4 * D // TILE, feed_in)
    for slot in range(2):
        pltpu.make_async_copy(act_turned.at[slot], act_t.at[0:TILE, :], act_sem.at[slot]).wait()
    put_out(slope, slope_out)
    turn_out(low_a, a_t, 0)
    loads[4].wait()

    def feed_out(index):
        value[:, at(index, TILE)] = value[:, at(index, TILE)] + dot_nn(act[...], down_w[:, at(index, TILE)])

    each(D // TILE, feed_out)

    def norm_c(index):
        rows = at(index, ROWS)
        found, normed, inverse = layer_norm(value[rows, :], norm_rows[4], norm_rows[5])
        low_a[rows, :] = found.astype(BF16)
        nc[rows, :] = normed
        put_lane(side, rows, 14, inverse)

    each(tokens // ROWS, norm_c)
    turn_out(low_a, y_t, 1)
    loss = jnp.zeros((1, 1), F32)
    for half in range(tokens // HALF):
        rows = pl.ds(half * HALF, HALF)
        target = cols[rows, 2:3]
        weight = cols[rows, 3:4].astype(F32)

        def lanes(index):
            return lax.broadcasted_iota(jnp.int32, (1, TILE), 1) + index * TILE

        def multiply(index, highest):
            found = dot_nn(low_a[rows, :], wide[:, at(index, TILE)])
            found = jnp.where(lanes(index) < VOCAB, found, -1e30)
            logits[:, at(index, TILE)] = found
            return jnp.maximum(highest, jnp.maximum(found[:, 0:128], found[:, 128:256]))

        highest = lax.fori_loop(0, TABLE_TILES, multiply, jnp.full((HALF, 128), -1e30, F32))
        highest = jnp.max(highest, 1, keepdims=True)

        def raise_to(index, carry):
            summed, picked = carry
            found = logits[:, at(index, TILE)]
            raised = jnp.exp(found - highest)
            logits[:, at(index, TILE)] = raised
            hit = jnp.where(lanes(index) == target, found, 0.0)
            return summed + raised[:, 0:128] + raised[:, 128:256], picked + hit[:, 0:128] + hit[:, 128:256]

        zero = jnp.zeros((HALF, 128), F32)
        summed, picked = lax.fori_loop(0, TABLE_TILES, raise_to, (zero, zero))
        summed = jnp.sum(summed, 1, keepdims=True)
        picked = jnp.sum(picked, 1, keepdims=True)
        loss = loss + jnp.sum(weight * (highest + jnp.log(summed) - picked), 0, keepdims=True)
        scale = weight * inverse_count
        share = scale / summed
        if half > 0:
            outs[-1].wait()

        def differ(index):
            found = logits[:, at(index, TILE)] * share - jnp.where(lanes(index) == target, scale, 0.0)
            pick[:, at(index, TILE)] = found.astype(BF16)

        each(TABLE_TILES, differ)
        put_out(pick.at[:, 0:TABLE_END], glog_out.at[rows, :])

        def back(index):
            grad[rows, at(index, TILE)] = dot_nt(pick[:, 0:TABLE_END], wide[at(index, TILE), 0:TABLE_END])

        each(D // TILE, back)
    loss_out[...] = loss

    def norm_c_back(index, carry):
        gain, shift = carry
        rows = at(index, ROWS)
        inverse = lane_at(side[rows, :], 14)
        found, normed = grad[rows, :], nc[rows, :]
        grad[rows, :] = layer_norm_back(found, normed, inverse, norm_rows[4])
        return gain + jnp.sum(found * normed, 0, keepdims=True), shift + jnp.sum(found, 0, keepdims=True)

    zero = jnp.zeros((1, D), F32)
    gain, shift = lax.fori_loop(0, tokens // ROWS, norm_c_back, (zero, zero))
    norm_out[0:1, :] = gain
    norm_out[1:2, :] = shift
    put_out(grad, grad_out)
    for index, copy in enumerate(outs):
        if index != 4:
            copy.wait()
    for copy, _ in turns:
        copy.wait()


def forward(weights, cols, keys):
    tokens = cols.shape[0]
    vmem, hbm = pl.BlockSpec(memory_space=pltpu.VMEM), pl.BlockSpec(memory_space=pl.ANY)
    shape = jax.ShapeDtypeStruct
    small = [shape((1, 1), F32), shape((1, 1), F32), shape((16, D), F32), shape((2, D), F32), shape((tokens, 128), F32)]
    large = [shape((D, tokens), BF16)] * 3 + [shape((4 * D, tokens), BF16), shape((D, tokens), BF16)]
    large += [shape((tokens, TABLE_END), BF16), shape((tokens, 4 * D), BF16), shape((tokens, 3 * D), BF16)]
    large += [shape((tokens, D), F32)] * 3
    return pl.pallas_call(
        forward_kernel,
        out_shape=small + large,
        in_specs=[hbm] * 5 + [vmem] * 2,
        out_specs=[vmem] * len(small) + [hbm] * len(large),
        scratch_shapes=[pltpu.VMEM((32 * size, wide), BF16) for size, wide in SHAPES]
        + [pltpu.VMEM((tokens, D), F32)] * 5
        + [pltpu.VMEM((tokens, D), BF16)] * 2
        + [
            pltpu.VMEM((tokens, 3 * D), BF16),
            pltpu.VMEM((tokens, 4 * D), BF16),
            pltpu.VMEM((tokens, 4 * D), BF16),
            pltpu.VMEM((HALF, TABLE_END), F32),
            pltpu.VMEM((HALF, WIDE), BF16),
            pltpu.VMEM((tokens - SPAN, tokens - SPAN), F32),
            pltpu.VMEM((2, D, tokens), BF16),
            pltpu.VMEM((2, TILE, tokens), BF16),
            pltpu.SemaphoreType.DMA((5,)),
            pltpu.SemaphoreType.DMA((8,)),
            pltpu.SemaphoreType.DMA((2,)),
            pltpu.SemaphoreType.DMA((2,)),
        ],
        compiler_params=pltpu.CompilerParams(vmem_limit_bytes=62 * 1024 * 1024),
    )(*weights, cols, keys)


def backward_kernel(*refs):
    loaded, (cols, keys, side, gains) = refs[0:9], refs[9:13]
    norm_out, ge_t, gffn_out, gh_out, gattn_out, gqkv_out = refs[13:19]
    qkv_w, out_w, in_w, down_w, slope, qkv, na, nb, grad = refs[19:28]
    low, attn, gh, bias, turned, load_sem, out_sem = refs[28:35]
    tokens = grad.shape[0]
    last = tokens - SPAN
    held = (qkv_w, out_w, in_w, down_w, slope, qkv, na, nb, grad)
    loads = [pltpu.make_async_copy(loaded[i], held[i], load_sem.at[i]) for i in range(9)]
    order = (8, 3, 4, 2, 7, 1, 5, 0, 6)
    for i in order:
        loads[i].start()
    outs = []

    def put_out(source, target):
        copy = pltpu.make_async_copy(source, target, out_sem.at[len(outs)])
        copy.start()
        outs.append(copy)

    set_bias(bias, cols, keys, last)
    loads[8].wait()

    def round_grad(index):
        rows = at(index, ROWS)
        low[rows, :] = grad[rows, :].astype(BF16)

    each(tokens // ROWS, round_grad)
    put_out(low, gffn_out)
    loads[3].wait()
    loads[4].wait()

    def feed_out_back(index):
        found = dot_nt(low[...], down_w[at(index, TILE), :]) * slope[:, at(index, TILE)].astype(F32)
        gh[:, at(index, TILE)] = found.astype(BF16)

    each(4 * D // TILE, feed_out_back)
    put_out(gh, gh_out)
    loads[2].wait()

    def feed_in_back(index):
        grad[:, at(index, TILE)] = grad[:, at(index, TILE)] + dot_nt(gh[...], in_w[at(index, TILE), :])

    each(D // TILE, feed_in_back)
    loads[7].wait()
    outs[0].wait()
    zero = jnp.zeros((1, D), F32)

    def norm_b_back(index, carry):
        gain, shift = carry
        rows = at(index, ROWS)
        inverse = lane_at(side[rows, :], 13)
        found, normed = grad[rows, :], nb[rows, :]
        back = layer_norm_back(found, normed, inverse, gains[7:8, :])
        grad[rows, :] = back
        low[rows, :] = back.astype(BF16)
        return gain + jnp.sum(found * normed, 0, keepdims=True), shift + jnp.sum(found, 0, keepdims=True)

    gain, shift = lax.fori_loop(0, tokens // ROWS, norm_b_back, (zero, zero))
    norm_out[2:3, :] = gain
    norm_out[3:4, :] = shift
    put_out(low, gattn_out)
    loads[1].wait()

    def out_back(index):
        attn[:, at(index, TILE)] = dot_nt(low[...], out_w[at(index, TILE), :]).astype(BF16)

    each(D // TILE, out_back)
    loads[5].wait()

    def attend_pair_back(pair):
        for start, size in ((0, last), (last, SPAN)):
            rows = pl.ds(start, size)
            spots = [pl.ds(pl.multiple_of(i * D + pair * 128, 128), 128) for i in range(3)]
            query, key, val = (qkv[rows, spot] for spot in spots)
            given = attn[rows, at(pair, 128)]
            mask = bias[...] if start == 0 else jnp.where(keys[0:1, last:tokens] > 0, 0.0, -1e30)
            found = []
            for first in (True, False):
                lanes = head_lanes(first)
                chosen = jnp.where(lanes, query, jnp.zeros_like(query))
                mine = jnp.where(lanes, given, jnp.zeros_like(given))
                total = lane_at(side[rows, :], 2 * pair + (0 if first else 1))
                shares = jnp.exp(dot_nt(chosen, key) * 0.125 + mask - total)
                grad_share = dot_nt(mine, val)
                middle = jnp.sum(shares * grad_share, 1, keepdims=True)
                grad_score = (shares * (grad_share - middle)).astype(BF16)
                found.append(
                    (
                        dot_nn(grad_score, key) * 0.125,
                        dot_tn(grad_score, query) * 0.125,
                        dot_tn(shares.astype(BF16), given),
                    )
                )
            for i in range(3):
                qkv[rows, spots[i]] = jnp.where(head_lanes(True), found[0][i], found[1][i]).astype(BF16)

    each(HEADS // 2, attend_pair_back)
    put_out(qkv, gqkv_out)
    loads[0].wait()

    def project_back(index):
        grad[:, at(index, TILE)] = grad[:, at(index, TILE)] + dot_nt(qkv[...], qkv_w[at(index, TILE), :])

    each(D // TILE, project_back)
    loads[6].wait()

    def norm_a_back(index, carry):
        gain, shift = carry
        rows = at(index, ROWS)
        inverse = lane_at(side[rows, :], 12)
        found, normed = grad[rows, :], na[rows, :]
        turned[:, rows] = layer_norm_back(found, normed, inverse, gains[5:6, :]).astype(BF16).T
        return gain + jnp.sum(found * normed, 0, keepdims=True), shift + jnp.sum(found, 0, keepdims=True)

    gain, shift = lax.fori_loop(0, tokens // ROWS, norm_a_back, (zero, zero))
    norm_out[0:1, :] = gain
    norm_out[1:2, :] = shift
    put_out(turned, ge_t)
    for copy in outs[1:]:
        copy.wait()


def backward(weights, slope, qkv, na, nb, grad, cols, keys, side, gains):
    tokens = grad.shape[0]
    vmem, hbm = pl.BlockSpec(memory_space=pltpu.VMEM), pl.BlockSpec(memory_space=pl.ANY)
    shape = jax.ShapeDtypeStruct
    loaded = tuple(weights) + (slope, qkv, na, nb, grad)
    widths = (D, D, 4 * D, D, 3 * D)
    return pl.pallas_call(
        backward_kernel,
        out_shape=[shape((4, D), F32), shape((D, tokens), BF16)]
        + [shape((tokens, width), BF16) for width in (D, 4 * D, D, 3 * D)],
        in_specs=[hbm] * 9 + [vmem] * 4,
        out_specs=[vmem] + [hbm] * 5,
        scratch_shapes=[pltpu.VMEM(member.shape, member.dtype) for member in loaded]
        + [
            pltpu.VMEM((tokens, D), BF16),
            pltpu.VMEM((tokens, D), BF16),
            pltpu.VMEM((tokens, 4 * D), BF16),
            pltpu.VMEM((tokens - SPAN, tokens - SPAN), F32),
            pltpu.VMEM((D, tokens), BF16),
            pltpu.SemaphoreType.DMA((9,)),
            pltpu.SemaphoreType.DMA((5,)),
        ],
        compiler_params=pltpu.CompilerParams(vmem_limit_bytes=60 * 1024 * 1024),
    )(*loaded, cols, keys, side, gains)


LEFT = 768


def reduce_kernel(*refs):
    given, (cols, norm_ab, norm_c, loss, squares) = refs[0:11], refs[11:16]
    y_t, ge_t, glog, x_t, gqkv, mix_t, gattn, a_t, gh, act_t, gffn = given
    lane_olds, side_olds, moment = refs[16:22], refs[22:28], refs[28]
    outs, sums_out, totals_out = refs[29:34], refs[34], refs[35]
    own, side, first, second, column, fin = (refs[36 + 5 * i : 41 + 5 * i] for i in range(6))
    left, (glog_v, gqkv_v, gattn_v, gh_v, gffn_v), stage, tails, norm_t = refs[66:71], refs[71:76], refs[76], refs[77], refs[78]
    spread, spread_small = refs[79:82], refs[82:85]
    load_sem, ring_sem, tail_sem, side_recv, first_send, first_recv, second_send, second_recv = refs[85:93]
    z_send, z_recv, swap_send, swap_recv = refs[93:97]
    sems, small_sems = refs[97:103], refs[103:109]
    z, y, x, c = here()
    peers = all_peers()
    me = chip(z, y, x)
    FIRST, SECOND = (first_send, first_recv), (second_send, second_recv)

    barrier = pltpu.get_barrier_semaphore()
    greeted = [peers[XWAY], peers[YWAY], peers[SIDE], device(z, 1 - y, 1 - x, c)]
    greeted += [device((z + 1 + i) % 4, y, x, c) for i in range(3)]
    for peer in greeted:
        pl.semaphore_signal(barrier, inc=1, device_id=peer, device_id_type=MESH)

    def load(index, source, target):
        return pltpu.make_async_copy(source, target, load_sem.at[index])

    loads = [
        load(0, a_t, left[0]),
        load(1, gh, gh_v),
        load(2, x_t, left[1]),
        load(3, gqkv, gqkv_v),
        load(4, y_t, left[2]),
        load(5, ge_t, left[3]),
        load(6, glog, glog_v),
        load(7, gffn, gffn_v),
        load(8, mix_t, left[4]),
        load(9, gattn, gattn_v),
    ] + [load(10 + i, act_t.at[pl.ds(LEFT * i, LEFT), :], left[i]) for i in range(4)]
    for member in loads[0:10]:
        member.start()
    norm_t[...] = jnp.zeros(norm_t.shape, F32)
    norm_t[5:9, :] = norm_ab[...]
    norm_t[9:11, :] = norm_c[...]
    pl.semaphore_wait(barrier, 7)

    def slot(ref, m, index):
        size = 2 * SHAPES[m][0]
        return ref[m].at[pl.ds(pl.multiple_of(index * size, size), size), :]

    def half_of(m):
        return SHAPES[m][1] // 2

    def chosen(start):
        lane = lax.broadcasted_iota(jnp.int32, (1, TILE), 1) + start
        hit = (cols[:, 0:1] == lane) | (cols[:, 1:2] == lane)
        return jnp.where(hit, 1.0, 0.0).astype(BF16)

    def ring_copy(m, rows, lanes, number, index):
        place = lax.rem(number, 3)
        return pltpu.make_async_remote_copy(
            src_ref=stage.at[place],
            dst_ref=side[m].at[rows, lanes],
            send_sem=ring_sem.at[place],
            recv_sem=side_recv.at[m, index],
            device_id=peers[SIDE],
            device_id_type=MESH,
        )

    def tail_copy(m, rows, lanes, number, index):
        return pltpu.make_async_remote_copy(
            src_ref=tails.at[number],
            dst_ref=side[m].at[rows, lanes],
            send_sem=tail_sem.at[number],
            recv_sem=side_recv.at[m, index],
            device_id=peers[SIDE],
            device_id_type=MESH,
        )

    whole = pl.ds(0, LEFT)

    def give(m, rows, lanes, number, index):
        def write(value):
            stage[lax.rem(number, 3)] = value.astype(BF16)

        def before():
            @pl.when(number >= 3)
            def _():
                ring_copy(m, rows, lanes, number, index).wait_send()

        return before, write, lambda: ring_copy(m, rows, lanes, number, index).start()

    def keep(m, rows, lanes):
        def write(value):
            own[m][rows, lanes] = value.astype(BF16)

        return lambda: None, write, lambda: None

    def plain(m, half, right, left_of, base, tail_base):
        wide = half_of(m)
        groups = SHAPES[m][0] // 24
        for group in range(groups):
            rows = pl.ds(LEFT * group, LEFT)
            source = left[left_of + group]

            def step(j, base=base, rows=rows, source=source, group=group):
                lanes = at(j, TILE)
                if base is None:
                    before, write, after = keep(m, rows, lanes)
                else:
                    before, write, after = give(m, rows, lanes, base + group * (wide // TILE) + j, group + j)
                before()
                write(dot_nn(source[...], right[:, pl.ds(pl.multiple_of(half * wide + j * TILE, 128), TILE)]))
                after()

            each(wide // TILE, step)
            if wide % TILE:
                start = wide - 128
                value = dot_nn(source[...], right[:, pl.ds(pl.multiple_of(half * wide + start, 128), 128)])
                if base is None:
                    own[m][rows, start:wide] = value.astype(BF16)
                else:
                    tails[tail_base + group] = value.astype(BF16)
                    tail_copy(m, rows, pl.ds(start, 128), tail_base + group, groups * (wide // TILE) + group).start()

    def wide_product(half, base):
        wide = half_of(E_)

        def both(j):
            start = pl.multiple_of(half * wide + j * TILE, TILE)
            return dot_nn(left[2][...], glog_v[:, pl.ds(start, TILE)]) + dot_nn(left[3][...], chosen(start))

        def target(j):
            lanes = at(j, TILE)
            return keep(E_, whole, lanes) if base is None else give(E_, whole, lanes, base + j, j)

        def step(j):
            before, write, after = target(j)
            before()
            write(both(j))
            after()

        each(6, step)
        before, write, after = target(6)
        before()
        norm_part = jnp.where(half == 1, norm_t[...], 0.0).T
        write(both(6) + jnp.concatenate((norm_part, jnp.zeros((LEFT, TILE - 128), F32)), 1))
        after()
        for j in range(7, 10):
            before, write, after = target(j)
            before()

            @pl.when(half == 0)
            def _():
                write(both(j))

            @pl.when(half == 1)
            def _():
                if j == 7:
                    write(jnp.zeros((LEFT, TILE), F32))
                else:
                    write(dot_nn(left[3][...], chosen(half_of(E_) + j * TILE)))

            after()

    def combine(m, target, parts):
        def piece(rows, lanes):
            total = parts[0][rows, lanes].astype(F32)
            for member in parts[1:]:
                total = total + member[rows, lanes].astype(F32)
            target[rows, lanes] = total.astype(target.dtype)

        wide = half_of(m)
        if m == D_:
            each(4, lambda group: piece(at(group, 48), slice(0, wide)))
            return
        if wide >= 512:
            each(wide // 512, lambda j: piece(slice(0, 48), at(j, 512)))
        if wide % 512:
            piece(slice(0, 48), slice(wide // 512 * 512, wide))

    def hop(m, k, land, index, sems, way):
        return pltpu.make_async_remote_copy(
            src_ref=slot(own, m, k),
            dst_ref=slot(land, m, index),
            send_sem=sems[0].at[m, index],
            recv_sem=sems[1].at[m, index],
            device_id=peers[way],
            device_id_type=MESH,
        )

    def landed(m, land, index, sems):
        hop(m, me, land, index, sems, XWAY).wait_recv()

    def block(m, a, b, far):
        return chip(far, a, b) if m in CLASS_A else chip(far, b, a)

    def split(m):
        return (y, x, YWAY, XWAY) if m in CLASS_A else (x, y, XWAY, YWAY)

    def ready(m):
        wide, groups = half_of(m), SHAPES[m][0] // 24
        for group in range(groups):
            for j in range(wide // TILE):
                ring_copy(m, pl.ds(LEFT * group, LEFT), at(j, TILE), 0, group + j).wait_recv()
            if wide % TILE:
                index = groups * (wide // TILE) + group
                tail_copy(m, pl.ds(LEFT * group, LEFT), pl.ds(wide - 128, 128), 0, index).wait_recv()

    def both_cores(m, k):
        return (slot(own, m, k), slot(side, m, k))

    def first_block(m, i):
        a, b, way, _ = split(m)
        return block(m, 1 - a, lax.rem(i, 2), i // 2), way

    def first_phase(m):
        def step(i):
            k, way = first_block(m, i)
            combine(m, slot(own, m, k), both_cores(m, k))
            hop(m, k, first, i, FIRST, way).start()

        each(8, step)

    def second_block(m, t):
        a, b, _, way = split(m)
        return block(m, a, 1 - b, t), way

    def second_phase(m):
        def step(t):
            k, way = second_block(m, t)
            spot = 2 * t + 1 - split(m)[1]
            landed(m, first, spot, FIRST)
            combine(m, slot(own, m, k), both_cores(m, k) + (slot(first, m, spot),))
            hop(m, k, second, t, SECOND, way).start()

        each(4, step)

    def count_of(m):
        return 4 if m in CLASS_C else 1

    def z_block(m, t, q):
        return t * 4 + q if m in CLASS_C else chip(t, y, x)

    def z_copy(m, t, q, rise):
        n = count_of(m)
        index = (t - z - 1 if rise else 5 - z + t) * n + q
        k = z_block(m, t, q)
        return pltpu.make_async_remote_copy(
            src_ref=slot(own, m, k),
            dst_ref=slot(column, m, index),
            send_sem=z_send.at[m, t * n + q],
            recv_sem=z_recv.at[m, index],
            device_id=peers[UP if rise else DOWN],
            device_id_type=MESH,
        )

    def z_landed(m, index):
        pltpu.make_async_remote_copy(
            src_ref=slot(own, m, me),
            dst_ref=slot(column, m, index),
            send_sem=z_send.at[m, 0],
            recv_sem=z_recv.at[m, index],
            device_id=peers[UP],
            device_id_type=MESH,
        ).wait_recv()

    def gathered(m, k, t):
        if m in CLASS_C:
            return both_cores(m, k)
        spot = 2 * t + split(m)[1]
        landed(m, first, spot, FIRST)
        landed(m, second, t, SECOND)
        return both_cores(m, k) + (slot(first, m, spot), slot(second, m, t))

    def z_push(m, t, q, rise, follows):
        k = z_block(m, t, q)
        parts = gathered(m, k, t)
        if follows:
            index = (t - z if rise else 4 - z + t) * count_of(m) + q
            z_landed(m, index)
            parts = parts + (slot(column, m, index),)
        combine(m, slot(own, m, k), parts)
        z_copy(m, t, q, rise).start()

    stages = (
        ((0, 3, lambda i: 3 - i, True, False), (3, 3, lambda i: i, False, False)),
        ((1, 2, lambda i: 3 - i, True, True), (2, 2, lambda i: i, False, True)),
        ((1, 1, lambda i: i, False, True), (2, 1, lambda i: 3 - i, True, True)),
    )

    def z_stage(m, number):
        n = count_of(m)
        for level, length, which, rise, follows in stages[number]:

            @pl.when(z == level)
            def _():
                each(length * n, lambda i: z_push(m, which(i // n), lax.rem(i, n), rise, follows))

    def z_sent(m):
        n = count_of(m)
        for stage_members in stages:
            for level, length, which, rise, _ in stage_members:

                @pl.when(z == level)
                def _():
                    each(length * n, lambda i: z_copy(m, which(i // n), lax.rem(i, n), rise).wait_send())

    def with_ends(m, target, base, q):
        n = count_of(m)
        low, high = q, 4 * n + q

        @pl.when(z == 0)
        def _():
            z_landed(m, high)
            combine(m, target, base + (slot(column, m, high),))

        @pl.when(z == 3)
        def _():
            z_landed(m, low)
            combine(m, target, base + (slot(column, m, low),))

        @pl.when((z > 0) & (z < 3))
        def _():
            z_landed(m, low)
            z_landed(m, high)
            combine(m, target, base + (slot(column, m, low), slot(column, m, high)))

    def c_across():
        for m in CLASS_C:
            for other in range(2):
                k = chip(z, other, 1 - x)
                with_ends(m, slot(own, m, k), both_cores(m, k), other * 2 + 1 - x)
                hop(m, k, first, other, FIRST, XWAY).start()

    def c_along():
        for m in CLASS_C:
            k = chip(z, 1 - y, x)
            landed(m, first, 1 - y, FIRST)
            with_ends(m, slot(own, m, k), both_cores(m, k) + (slot(first, m, 1 - y),), (1 - y) * 2 + x)
            hop(m, k, second, 0, SECOND, YWAY).start()

    swaps = []

    def finish(m):
        if m in CLASS_C:
            landed(m, first, y, FIRST)
            landed(m, second, 0, SECOND)
            with_ends(m, fin[m], both_cores(m, me) + (slot(first, m, y), slot(second, m, 0)), y * 2 + x)
        else:
            with_ends(m, fin[m], gathered(m, me, z), 0)
        size, wide = SHAPES[m][0], half_of(m)
        lanes = pl.ds(pl.multiple_of(c * wide, 128), wide)
        swaps.append(
            pltpu.make_async_remote_copy(
                src_ref=fin[m].at[pl.ds(pl.multiple_of((1 - c) * size, 8), size), :],
                dst_ref=outs[m].at[:, lanes],
                send_sem=swap_send.at[m],
                recv_sem=swap_recv.at[m],
                device_id=peers[SIDE],
                device_id_type=MESH,
            )
        )
        swaps[-1].start()
        outs[m][:, lanes] = fin[m][pl.ds(pl.multiple_of(c * size, 8), size), :]

    loads[0].wait()
    loads[1].wait()
    plain(I_, 1 - c, gh_v, 0, 0, 0)
    plain(I_, c, gh_v, 0, None, 0)
    loads[10].start()
    loads[2].wait()
    loads[3].wait()
    plain(Q_, 1 - c, gqkv_v, 1, 6, 0)
    plain(Q_, c, gqkv_v, 1, None, 0)
    loads[11].start()
    ready(I_)
    z_stage(I_, 0)
    loads[4].wait()
    loads[5].wait()
    loads[6].wait()
    wide_product(1 - c, 10)
    z_stage(I_, 1)
    ready(Q_)
    first_phase(Q_)
    wide_product(c, None)
    loads[12].start()
    loads[13].start()
    z_stage(I_, 2)
    ready(E_)
    first_phase(E_)
    for i in (7, 10, 11, 12, 13):
        loads[i].wait()
    plain(D_, 1 - c, gffn_v, 0, 20, 1)
    plain(D_, c, gffn_v, 0, None, 1)
    c_across()
    ready(D_)
    first_phase(D_)
    loads[8].wait()
    loads[9].wait()
    plain(O_, 1 - c, gattn_v, 4, 24, 5)
    plain(O_, c, gattn_v, 4, None, 5)
    second_phase(Q_)
    ready(O_)
    first_phase(O_)
    c_along()
    second_phase(E_)
    second_phase(D_)
    second_phase(O_)
    for number in range(3):
        for m in (Q_, E_, D_, O_):
            z_stage(m, number)
    for m in (I_, Q_, E_, D_, O_):
        finish(m)
    for m in range(5):
        z_sent(m)
        if m in CLASS_C:
            for other in range(2):
                hop(m, chip(z, other, 1 - x), first, other, FIRST, XWAY).wait_send()
            hop(m, chip(z, 1 - y, x), second, 0, SECOND, YWAY).wait_send()
        else:
            each(8, lambda i: hop(m, first_block(m, i)[0], first, i, FIRST, first_block(m, i)[1]).wait_send())
            each(4, lambda t: hop(m, second_block(m, t)[0], second, t, SECOND, second_block(m, t)[1]).wait_send())
    for number in (22, 23, 24):
        ring_copy(O_, whole, pl.ds(0, TILE), number, 0).wait_send()
    for number in range(6):
        tail_copy(O_, whole, pl.ds(TILE, 128), number, 1).wait_send()
    for swap in swaps:
        swap.wait()

    sides, lanes, squared, gs = statistics(outs, lane_olds, side_olds)
    scalars = jnp.concatenate((lanes_of([jnp.sum(member, 0, keepdims=True) for member in sides] + [loss[...]]),), 1)
    sums = jnp.concatenate(lanes + [scalars, squares[...]], 1)
    sums = sum_everywhere(sums, *spread, sems)
    sums_out[...] = sums
    updates = updates_of(sums, gs, sides, lane_olds, moment)[0]
    totals = lanes_of(
        [total_sum(update * update) for update in updates[:6]]
        + [jnp.sum(updates[6][i : i + 1] * updates[6][i : i + 1], 1, keepdims=True) for i in range(6)]
    )
    totals_out[...] = sum_everywhere(totals, *spread_small, small_sems)


def statistics(grads, lane_olds, side_olds):
    wide_g = grads[E_][...]
    gs = (wide_g[:, :VOCAB], wide_g[:, PLACE_AT:]) + tuple(grads[m][...] for m in (Q_, O_, I_, D_))
    gs = gs + (wide_g[:, 4096:4224],)
    decay = 1.0 - STEP ** (-0.8)
    sides, lanes = [], []
    wide_square = wide_g * wide_g + SQUARE_FLOOR
    squares = [wide_square[:, :VOCAB], wide_square[:, PLACE_AT:]] + [g * g + SQUARE_FLOOR for g in gs[2:6]]
    for index in range(6):
        mean = jnp.sum(squares[index], 1, keepdims=True) / squares[index].shape[1]
        sides.append(decay * column_of(side_olds[index][...]) + (1.0 - decay) * mean)
    lanes = [jnp.sum(square, 0, keepdims=True) for square in [wide_square] + squares[2:]]
    return sides, lanes, squares, gs


def updates_of(sums, gs, sides, lane_olds, moment):
    decay = 1.0 - STEP ** (-0.8)
    fresh = 1.0 - decay
    parts = [sums[:, :VOCAB], sums[:, PLACE_AT:WIDE]]
    parts += [sums[:, SUM_AT[i] : SUM_AT[i + 1]] for i in range(1, 5)]
    scalars = sums[:, SUM_AT[5] : SUM_AT[5] + 128]
    updates, lane_news = [], []
    for index in range(6):
        height = gs[index].shape[0] * 32
        lane_news.append(decay * lane_olds[index][...] + fresh * (parts[index] / height))
        if index < 2:
            mean = jnp.sum(lane_news[index], 1, keepdims=True) / lane_news[index].shape[1]
        else:
            mean = lane_at(scalars, index) / height
        updates.append(gs[index] * lax.rsqrt(sides[index] * lane_news[index] / mean))
    norm_g = jnp.concatenate([row_of(lane_at(gs[6], NORM_AT - 4096 + i)) for i in range(6)], 0)
    moment_new = decay * moment[...] + fresh * (norm_g * norm_g + SQUARE_FLOOR)
    updates.append(norm_g * lax.rsqrt(moment_new))
    return updates, lane_news, norm_g, moment_new


def reduce_grads(large, small):
    def rows(count, m):
        size, wide = SHAPES[m]
        return pltpu.VMEM((count * 2 * size, wide // 2), BF16)

    every = range(5)
    tokens = large[2].shape[0]
    vmem, hbm = pl.BlockSpec(memory_space=pltpu.VMEM), pl.BlockSpec(memory_space=pl.ANY)
    dma = pltpu.SemaphoreType.DMA
    scratch = (
        [rows(16, m) for m in every]
        + [rows(16, m) for m in every]
        + [rows(2 if m in CLASS_C else 8, m) for m in every]
        + [rows(1 if m in CLASS_C else 4, m) for m in every]
        + [rows(20 if m in CLASS_C else 5, m) for m in every]
        + [pltpu.VMEM((2 * size, wide // 2), F32) for size, wide in SHAPES]
        + [pltpu.VMEM((LEFT, tokens), BF16)] * 5
        + [pltpu.VMEM((tokens, width), BF16) for width in (TABLE_END, 3 * D, D, 4 * D, D)]
        + [pltpu.VMEM((3, LEFT, TILE), BF16), pltpu.VMEM((6, LEFT, 128), BF16), pltpu.VMEM((128, D), F32)]
        + [pltpu.VMEM((count, 1, SUMS), F32) for count in (2, 4, 4)]
        + [pltpu.VMEM((count, 1, 128), F32) for count in (2, 4, 4)]
        + [dma((14,)), dma((3,)), dma((6,)), dma((5, 10))]
        + [dma((5, 8))] * 2
        + [dma((5, 4))] * 2
        + [dma((5, 16)), dma((5, 20)), dma((5,)), dma((5,))]
        + ([dma] * 2 + [dma((3,))] * 4) * 2
    )
    return pl.pallas_call(
        reduce_kernel,
        out_shape=[jax.ShapeDtypeStruct(shape, F32) for shape in SHAPES + ((1, SUMS), (1, 128))],
        in_specs=[hbm] * 11 + [vmem] * len(small),
        out_specs=[vmem] * 7,
        scratch_shapes=scratch,
        compiler_params=pltpu.CompilerParams(
            collective_id=1, has_side_effects=True, vmem_limit_bytes=63 * 1024 * 1024
        ),
    )(*large, *small)


def update_kernel(*refs):
    grads, sums, totals, ws, norms = refs[0:5], refs[5], refs[6], refs[7:13], refs[13]
    lane_olds, side_olds, moment = refs[14:20], refs[20:26], refs[26]
    loss_out, table_g, place_g, norm_g_out = refs[27:31]
    lane_outs, side_outs, moment_out, news, norm_new = refs[31:37], refs[37:43], refs[43], refs[44:50], refs[50]
    grad_outs = refs[51:55]
    sides, _, _, gs = statistics(grads, lane_olds, side_olds)
    updates, lane_news, norm_g, moment_new = updates_of(sums[...], gs, sides, lane_olds, moment)
    scalars = sums[:, SUM_AT[5] : SUM_AT[5] + 128]
    squares = sums[:, SUM_AT[5] + 128 :]
    loss_out[...] = lane_at(scalars, 6)
    table_g[...] = gs[0]
    place_g[...] = gs[1]
    norm_g_out[...] = norm_g
    moment_out[...] = moment_new
    for index in range(6):
        lane_outs[index][...] = lane_news[index]
        side_outs[index][...] = row_of(sides[index])
        if index >= 2:
            grad_outs[index - 2][...] = gs[index]
        entries = gs[index].shape[0] * gs[index].shape[1] * 32
        clip = jnp.maximum(1.0, jnp.sqrt(lane_at(totals[...], index) / entries))
        scale = learn_rate * jnp.sqrt(lane_at(squares, index) / entries) / clip
        news[index][...] = ws[index][...] - scale * updates[index]
    for i in range(6):
        clip = jnp.maximum(1.0, jnp.sqrt(lane_at(totals[...], 6 + i) / D))
        scale = learn_rate * jnp.sqrt(lane_at(squares, 6 + i) / D) / clip
        norm_new[i : i + 1, :] = norms[i : i + 1, :] - scale * updates[6][i : i + 1, :]


def update_weights(operands):
    lanes = (VOCAB, 512, 3 * D, D, 4 * D, D)
    held = (24, 24, 24, 24, 24, 96)
    shapes = [(1, 1), (24, VOCAB), (24, 512), (6, 24)]
    shapes += [(1, lane) for lane in lanes] + [(1, size) for size in held] + [(6, 24)]
    shapes += list(zip(held, lanes)) + [(6, 24)] + list(zip(held, lanes))[2:]
    return pl.pallas_call(
        update_kernel,
        out_shape=[jax.ShapeDtypeStruct(shape, F32) for shape in shapes],
        in_specs=[pl.BlockSpec(memory_space=pltpu.VMEM)] * len(operands),
        out_specs=[pl.BlockSpec(memory_space=pltpu.VMEM)] * len(shapes),
        compiler_params=pltpu.CompilerParams(vmem_limit_bytes=32 * 1024 * 1024),
    )(*operands)


def norm_forward(value, gain, shift):
    centred = value - jnp.mean(value, -1, keepdims=True)
    inverse = lax.rsqrt(jnp.mean(centred * centred, -1, keepdims=True) + EPSILON)
    normed = centred * inverse
    return (normed * gain + shift, normed, inverse)


def norm_backward(grad_out, normed, inverse, gain):
    scaled = grad_out * gain
    back = inverse * (
        scaled
        - jnp.mean(scaled, -1, keepdims=True)
        - normed * jnp.mean(scaled * normed, -1, keepdims=True)
    )
    return (back, jnp.sum(grad_out * normed, 0), jnp.sum(grad_out, 0))


def mm(left, right, sides):
    return lax.dot_general(left, right, ((sides[:1], sides[1:]), ((), ())), preferred_element_type=F32)


def attend(qkv, allowed):
    by_head = qkv.reshape(qkv.shape[0], 3, HEADS, HEAD_DIM)
    query, key, value = by_head[:, 0], by_head[:, 1], by_head[:, 2]
    scores = jnp.einsum("qhe,khe->hqk", query, key, preferred_element_type=F32) * 0.125
    scores = jnp.where(allowed[None], scores, -1e30)
    highest = jnp.max(scores, -1, keepdims=True)
    raised = jnp.exp(scores - highest)
    summed = jnp.sum(raised, -1, keepdims=True)
    shares = (raised / summed).astype(BF16)
    mixture = jnp.einsum("hqk,khe->qhe", shares, value, preferred_element_type=F32)
    return mixture.astype(BF16).reshape(qkv.shape[0], D), highest + jnp.log(summed)


def attend_back(qkv, allowed, log_total, grad_mix):
    by_head = qkv.reshape(qkv.shape[0], 3, HEADS, HEAD_DIM)
    query, key, value = by_head[:, 0], by_head[:, 1], by_head[:, 2]
    grad_mix = grad_mix.reshape(qkv.shape[0], HEADS, HEAD_DIM)
    scores = jnp.einsum("qhe,khe->hqk", query, key, preferred_element_type=F32) * 0.125
    scores = jnp.where(allowed[None], scores, -1e30)
    shares = jnp.exp(scores - log_total)
    grad_share = jnp.einsum("qhe,khe->hqk", grad_mix, value, preferred_element_type=F32)
    grad_score = (shares * (grad_share - jnp.sum(shares * grad_share, -1, keepdims=True))).astype(BF16)
    grad_query = jnp.einsum("hqk,khe->qhe", grad_score, key, preferred_element_type=F32) * 0.125
    grad_key = jnp.einsum("hqk,qhe->khe", grad_score, query, preferred_element_type=F32) * 0.125
    grad_value = jnp.einsum("hqk,qhe->khe", shares.astype(BF16), grad_mix, preferred_element_type=F32)
    return jnp.stack((grad_query, grad_key, grad_value), 1).astype(BF16).reshape(qkv.shape)


def on_device(
    whole_mesh,
    long_ids,
    long_targets,
    long_mask,
    long_lengths,
    short_ids,
    short_targets,
    short_mask,
    short_lengths,
    table,
    position,
    qkv_weight,
    out_weight,
    in_weight,
    down_weight,
    norms,
    table_rows,
    table_cols,
    position_rows,
    position_cols,
    qkv_rows,
    qkv_cols,
    out_rows,
    out_cols,
    in_rows,
    in_cols,
    down_rows,
    down_cols,
    norm_moment,
):
    devices = lax.axis_size(("dp", "seq"))
    fast = whole_mesh == (8, 4)
    seq_index = lax.axis_index("seq")
    held = norms.shape[0]

    span = long_ids.shape[1]
    long_place = seq_index * span + lax.iota(jnp.int32, span)
    long_keep = (long_place[None, :] < long_lengths[:, None]).astype(jnp.int32)
    short_keep = (lax.iota(jnp.int32, SPAN)[None, :] < short_lengths[:, None]).astype(jnp.int32)
    long_pack = jnp.stack((long_ids, long_targets, long_mask * long_keep, long_keep), 1)
    short_pack = jnp.stack((short_ids, short_targets, short_mask * short_keep, short_keep), 1)
    moved = lax.all_to_all(
        jnp.concatenate((long_pack, short_pack[1:]), 0), "seq", split_axis=0, concat_axis=0, tiled=True
    )
    tokens = jnp.concatenate((moved, short_pack[:1]), 0)
    ids, targets, weight, keep = (tokens[:, i].reshape(-1) for i in range(4))
    weight = weight.astype(F32)
    count = tokens.shape[0] * span
    last = count - span
    alone = seq_index == lax.axis_size("seq") - 1
    token = lax.iota(jnp.int32, count)
    place = jnp.where(alone | (token >= last), token % span, token)
    row = jnp.where(alone | (token >= last), token // span, 0)
    allowed_long = (row[:last, None] == row[None, :last]) & (keep[None, :last] > 0)
    allowed_short = jnp.broadcast_to(keep[None, last:] > 0, (span, span))

    here_count = jnp.sum(long_pack[:, 2]) + jnp.sum(short_pack[:, 2])
    tall = table.T
    counts = jnp.broadcast_to(jnp.stack((here_count // 256, here_count % 256)).astype(F32)[None], (held, 2))
    wide_shard = jnp.concatenate(
        (tall, norms, counts, jnp.zeros((held, PLACE_AT - COUNT_AT - 2), F32), position.T), 1
    )
    shards = (wide_shard, qkv_weight, out_weight, in_weight, down_weight)
    if fast:
        wide_w, qkv_w, out_w, in_w, down_w, weight_sq = gather_weights(shards)
    else:
        wide_w, qkv_w, out_w, in_w, down_w = (
            lax.all_gather(shard.astype(BF16), ("dp", "seq"), axis=0, tiled=True) for shard in shards
        )
    if fast:
        zero = jnp.zeros_like(ids)
        cols = jnp.stack((ids, place + PLACE_AT, targets, weight.astype(jnp.int32), row) + (zero,) * 3, 1)
        keys = jnp.stack((keep, row) + (zero,) * 6, 0)
        found = forward((wide_w, qkv_w, out_w, in_w, down_w), cols, keys)
        loss_part, mask_count, gains, norm_c, side = found[0:5]
        loss_part, mask_count = loss_part[0, 0], mask_count[0, 0]
        x_t, mix_t, a_t, act_t, y_t, grad_logit, slope, qkv_b, normed_a, normed_b, grad_second = found[5:]
        norm_ab, ge_t, grad_ffn, grad_hidden, grad_attn, grad_qkv = backward(
            (qkv_w, out_w, in_w, down_w), slope, qkv_b, normed_a, normed_b, grad_second, cols, keys, side, gains
        )
        row = lambda vector: vector.reshape(1, -1)
        lane_olds = (table_rows, position_rows, qkv_cols, out_cols, in_cols, down_cols)
        side_olds = (table_cols, position_cols, qkv_rows, out_rows, in_rows, down_rows)
        olds = tuple(row(member) for member in lane_olds + side_olds) + (norm_moment.T,)
        reduced = reduce_grads(
            (y_t, ge_t, grad_logit, x_t, grad_qkv, mix_t, grad_attn, a_t, grad_hidden, act_t, grad_ffn),
            (cols, norm_ab, norm_c, loss_part.reshape(1, 1), weight_sq) + olds,
        )
        found = update_weights(
            tuple(reduced)
            + (tall, position.T, qkv_weight, out_weight, in_weight, down_weight, norms.T)
            + olds
        )
        grads = (None,) + tuple(found[24:28])
        loss_sum, table_g, place_g, norm_g = found[0:4]
        lane_news = [member.reshape(-1) for member in found[4:10]]
        side_news = [member.reshape(-1) for member in found[10:16]]
        moment_new, norm_new = found[16], found[23]
        news = found[17:23]
        return (
            loss_sum.reshape(()),
            mask_count,
            table_g.T,
            place_g.T,
            grads[1],
            grads[2],
            grads[3],
            grads[4],
            norm_g.T,
            lane_news[0],
            side_news[0],
            lane_news[1],
            side_news[1],
            side_news[2],
            lane_news[2],
            side_news[3],
            lane_news[3],
            side_news[4],
            lane_news[4],
            side_news[5],
            lane_news[5],
            moment_new.T,
            news[0].T,
            news[1].T,
            news[2],
            news[3],
            news[4],
            news[5],
            norm_new.T,
        )
    column = lax.broadcasted_iota(jnp.int32, (1, WIDE), 1)
    chosen = ((ids[:, None] == column) | ((place[:, None] + PLACE_AT) == column)).astype(BF16)
    gains = wide_w[:, NORM_AT : NORM_AT + 6].astype(F32)
    sums = jnp.sum(wide_w[:, COUNT_AT : COUNT_AT + 2].astype(F32), 0)
    mask_count = (sums[0] * 256.0 + sums[1]) / held
    inverse_count = 1.0 / mask_count

    embedded = mm(chosen, wide_w, (1, 1))
    first, normed_a, inverse_a = norm_forward(embedded, gains[:, 0], gains[:, 1])
    first_b = first.astype(BF16)
    qkv_b = mm(first_b, qkv_w, (1, 0)).astype(BF16)
    mix_long, total_long = attend(qkv_b[:last], allowed_long)
    mix_short, total_short = attend(qkv_b[last:], allowed_short)
    mixture = jnp.concatenate((mix_long, mix_short), 0)
    second, normed_b, inverse_b = norm_forward(first + mm(mixture, out_w, (1, 0)), gains[:, 2], gains[:, 3])
    second_b = second.astype(BF16)
    hidden = mm(second_b, in_w, (1, 0))
    active, slope = gelu_pair(hidden)
    active_b = active.astype(BF16)
    third, normed_c, inverse_c = norm_forward(second + mm(active_b, down_w, (1, 0)), gains[:, 4], gains[:, 5])
    third_b = third.astype(BF16)
    logits = jnp.where(column < VOCAB, mm(third_b, wide_w, (1, 0)), -1e30)
    highest = jnp.max(logits, -1, keepdims=True)
    log_sum = highest + jnp.log(jnp.sum(jnp.exp(logits - highest), -1, keepdims=True))
    onehot = targets[:, None] == column
    picked = jnp.sum(jnp.where(onehot, logits, 0.0), -1)
    loss_part = jnp.sum(weight * (log_sum[:, 0] - picked))
    grad_logit = (
        (jnp.exp(logits - log_sum) - onehot.astype(F32)) * (weight * inverse_count)[:, None]
    ).astype(BF16)
    grad_third = mm(grad_logit, wide_w, (1, 1))
    grad_second, gain_c, shift_c = norm_backward(grad_third, normed_c, inverse_c, gains[:, 4])
    grad_ffn = grad_second.astype(BF16)
    down_grad = mm(active_b, grad_ffn, (0, 0)).astype(BF16)
    grad_hidden = (mm(grad_ffn, down_w, (1, 1)) * slope).astype(BF16)
    in_grad = mm(second_b, grad_hidden, (0, 0)).astype(BF16)
    grad_second = grad_second + mm(grad_hidden, in_w, (1, 1))
    grad_first, gain_b, shift_b = norm_backward(grad_second, normed_b, inverse_b, gains[:, 2])
    grad_attn = grad_first.astype(BF16)
    out_grad = mm(mixture, grad_attn, (0, 0)).astype(BF16)
    grad_mix = mm(grad_attn, out_w, (1, 1)).astype(BF16)
    grad_qkv = jnp.concatenate(
        (
            attend_back(qkv_b[:last], allowed_long, total_long, grad_mix[:last]),
            attend_back(qkv_b[last:], allowed_short, total_short, grad_mix[last:]),
        ),
        0,
    )
    qkv_grad = mm(first_b, grad_qkv, (0, 0)).astype(BF16)
    grad_first = grad_first + mm(grad_qkv, qkv_w, (1, 1))
    grad_embed, gain_a, shift_a = norm_backward(grad_first, normed_a, inverse_a, gains[:, 0])
    wide_grad = mm(
        jnp.concatenate((third_b, grad_embed.astype(BF16)), 0),
        jnp.concatenate((grad_logit, chosen), 0),
        (0, 0),
    )
    norm_part = jnp.stack((gain_a, shift_a, gain_b, shift_b, gain_c, shift_c), 1)
    wide_grad = lax.dynamic_update_slice(wide_grad.astype(BF16), norm_part.astype(BF16), (0, NORM_AT))
    grads = (wide_grad, qkv_grad, out_grad, in_grad, down_grad)
    wide_g, qkv_g, out_g, in_g, down_g = (
        lax.psum_scatter(grad.astype(F32), ("dp", "seq"), scatter_dimension=0, tiled=True) for grad in grads
    )
    table_g, place_g = wide_g[:, :VOCAB], wide_g[:, PLACE_AT:]
    norm_g = wide_g[:, NORM_AT : NORM_AT + 6]

    decay = 1.0 - STEP ** (-0.8)
    matrices = (
        (qkv_weight, qkv_g, qkv_rows, qkv_cols),
        (out_weight, out_g, out_rows, out_cols),
        (in_weight, in_g, in_rows, in_cols),
        (down_weight, down_g, down_rows, down_cols),
    )
    wide = (
        (tall, table_g, table_cols, table_rows),
        (position.T, place_g, position_cols, position_rows),
    )
    row_news = [
        decay * member[2] + (1.0 - decay) * jnp.mean(member[1] * member[1] + SQUARE_FLOOR, 1)
        for member in matrices + wide
    ]
    col_parts = [jnp.sum(member[1] * member[1] + SQUARE_FLOOR, 0) for member in matrices + wide]
    row_totals = jnp.stack([jnp.sum(rows_new) for rows_new in row_news])
    weight_sq = jnp.stack([jnp.sum(member[0] * member[0]) for member in matrices + wide])
    stats = lax.psum(
        col_parts + [row_totals, weight_sq, jnp.sum(norms * norms, 0), loss_part.reshape(1)], ("dp", "seq")
    )
    updates = []
    cols_out = []
    for index, member in enumerate(matrices + wide):
        full_rows = member[0].shape[0] * devices
        cols_new = decay * member[3] + (1.0 - decay) * stats[index] / full_rows
        if index < 4:
            mean = stats[6][index] / full_rows
        else:
            mean = jnp.mean(cols_new)
        updates.append(member[1] * lax.rsqrt(row_news[index][:, None] * cols_new[None, :] / mean))
        cols_out.append(cols_new)
    moment_new = decay * norm_moment + (1.0 - decay) * (norm_g * norm_g + SQUARE_FLOOR)
    norm_update = norm_g * lax.rsqrt(moment_new)
    update_sq = jnp.stack([jnp.sum(update * update) for update in updates])
    totals = lax.psum((update_sq, jnp.sum(norm_update * norm_update, 0)), ("dp", "seq"))
    news = []
    for index, member in enumerate(matrices + wide):
        entries = member[0].shape[0] * member[0].shape[1] * devices
        clip = jnp.maximum(1.0, jnp.sqrt(totals[0][index] / entries))
        news.append(
            member[0] - learn_rate * jnp.sqrt(stats[7][index] / entries) * updates[index] / clip
        )
    norm_rows = norms.shape[0] * devices
    norm_clip = jnp.maximum(1.0, jnp.sqrt(totals[1] / norm_rows))
    norm_new = norms - learn_rate * jnp.sqrt(stats[8] / norm_rows) * norm_update / norm_clip
    return (
        stats[9][0],
        mask_count,
        table_g.T,
        place_g.T,
        qkv_g,
        out_g,
        in_g,
        down_g,
        norm_g,
        cols_out[4],
        row_news[4],
        cols_out[5],
        row_news[5],
        row_news[0],
        cols_out[0],
        row_news[1],
        cols_out[1],
        row_news[2],
        cols_out[2],
        row_news[3],
        cols_out[3],
        moment_new,
        news[4].T,
        news[5].T,
        news[0],
        news[1],
        news[2],
        news[3],
        norm_new,
    )


def solution(mesh):
    split, wide = P(("dp", "seq"), None), P(None, ("dp", "seq"))
    shard, same = P(("dp", "seq")), P()
    return jax.shard_map(
        functools.partial(on_device, (mesh.shape["dp"], mesh.shape["seq"])),
        mesh=mesh,
        in_specs=(P("dp", "seq"),) * 3
        + (P("dp"),)
        + (split,) * 3
        + (shard,)
        + (wide,) * 2
        + (split,) * 5
        + (same, shard) * 2
        + (shard, same) * 4
        + (split,),
        out_specs=(same, same)
        + (wide,) * 2
        + (split,) * 5
        + (same, shard) * 2
        + (shard, same) * 4
        + (split,)
        + (wide,) * 2
        + (split,) * 5,
        check_vma=False,
    )
```

```python
import functools

import jax
import jax.numpy as jnp
from jax import lax
from jax.experimental import pallas as pl
from jax.experimental.pallas import tpu as pltpu
from jax.sharding import PartitionSpec as P

D = 768
HEADS = 12
HEAD_DIM = 64
VOCAB = 4101
STEP = 10
SPAN = 128

EPSILON = 1e-12
SQUARE_FLOOR = 1e-30
learn_rate = 0.3

MESH = pl.DeviceIdType.MESH
F32 = jnp.float32
BF16 = jnp.bfloat16

NORM_AT = VOCAB
COUNT_AT = VOCAB + 6
TABLE_END = 4352
PLACE_AT = 4608
WIDE = PLACE_AT + 512

SHAPES = ((24, WIDE), (24, 3 * D), (24, D), (24, 4 * D), (96, D))
E_, Q_, O_, I_, D_ = range(5)
CLASS_A, CLASS_B, CLASS_C = (E_, O_), (Q_, D_), (I_,)
UP, DOWN, XWAY, YWAY, SIDE = range(5)


def here():
    dp, seq = lax.axis_index("dp"), lax.axis_index("seq")
    return dp // 2, dp % 2, seq // 2, seq % 2


def device(z, y, x, c):
    return {"dp": z * 2 + y, "seq": x * 2 + c}


def chip(z, y, x):
    return z * 4 + y * 2 + x


def near_first(z, s):
    inner = (z * (3 - z)) // 2
    found = s + inner * (1, 1, -2, 0)[s]
    return found + (z // 2) * (3 - 2 * found)


def greet(peers):
    barrier = pltpu.get_barrier_semaphore()
    z, y, x, c = here()

    @pl.when(z < 3)
    def _():
        pl.semaphore_signal(barrier, inc=1, device_id=peers[UP], device_id_type=MESH)

    @pl.when(z > 0)
    def _():
        pl.semaphore_signal(barrier, inc=1, device_id=peers[DOWN], device_id_type=MESH)

    for way in (XWAY, YWAY, SIDE):
        pl.semaphore_signal(barrier, inc=1, device_id=peers[way], device_id_type=MESH)

    @pl.when((z == 0) | (z == 3))
    def _():
        pl.semaphore_wait(barrier, 4)

    @pl.when((z > 0) & (z < 3))
    def _():
        pl.semaphore_wait(barrier, 5)


def all_peers():
    z, y, x, c = here()
    return (
        device(z + 1, y, x, c),
        device(z - 1, y, x, c),
        device(z, y, 1 - x, c),
        device(z, 1 - y, x, c),
        device(z, y, x, 1 - c),
    )


def gather_kernel(*refs):
    shards, outs, squares, merge, mine = refs[0:5], refs[5:10], refs[10], refs[11:16], refs[16:21]
    swap_send, swap_recv, local_sem, send_sem, link_recv, side_recv = refs[21:]
    z, y, x, c = here()
    peers = all_peers()
    me = chip(z, y, x)

    def part(m, k, half):
        size, wide = 2 * SHAPES[m][0], SHAPES[m][1] // 2
        return outs[m].at[
            pl.ds(pl.multiple_of(k * size, size), size), pl.ds(pl.multiple_of(half * wide, 128), wide)
        ]

    def copy_of(m, k, way, own):
        return pltpu.make_async_remote_copy(
            src_ref=mine[m] if own else part(m, k, c),
            dst_ref=part(m, k, c),
            send_sem=send_sem.at[m, k, way],
            recv_sem=(side_recv if way == SIDE else link_recv).at[m, k],
            device_id=peers[way],
            device_id_type=MESH,
        )

    sent = []

    def push(m, k, way, own=False, only=None):
        sent.append((m, k, way, own, only))
        if only is None:
            copy_of(m, k, way, own).start()
        else:

            @pl.when(only)
            def _():
                copy_of(m, k, way, own).start()

    def arrived(m, k):
        copy_of(m, k, XWAY, False).wait_recv()

    greet(peers)
    swaps = []
    for m, (size, wide) in enumerate(SHAPES):
        half = wide // 2
        swaps.append(
            pltpu.make_async_remote_copy(
                src_ref=shards[m].at[:, pl.ds(pl.multiple_of((1 - c) * half, 128), half)],
                dst_ref=merge[m].at[pl.ds(pl.multiple_of(c * size, 8), size), :],
                send_sem=swap_send.at[m],
                recv_sem=swap_recv.at[m],
                device_id=peers[SIDE],
                device_id_type=MESH,
            )
        )
        swaps[m].start()
    for m, (size, wide) in enumerate(SHAPES):
        half = wide // 2
        merge[m][pl.ds(pl.multiple_of(c * size, 8), size), :] = shards[m][
            :, pl.ds(pl.multiple_of(c * half, 128), half)
        ]

    keeps = []
    for m in (I_, E_, Q_, D_, O_):
        swaps[m].wait_recv()
        mine[m][...] = merge[m][...].astype(BF16)
        for way, only in ((UP, z < 3), (DOWN, z > 0), (XWAY, None), (YWAY, None), (SIDE, None)):
            push(m, me, way, True, only)
        keeps.append(pltpu.make_async_copy(mine[m], part(m, me, c), local_sem.at[m]))
        keeps[-1].start()

    wide_sq = shards[E_][...] * shards[E_][...]
    found = [total_sum(wide_sq[:, :VOCAB]), total_sum(wide_sq[:, PLACE_AT:])]
    found += [total_sum(shards[m][...] * shards[m][...]) for m in (Q_, O_, I_, D_)]
    norm_tile = jnp.sum(wide_sq[:, 4096:4224], 0, keepdims=True)
    found += [lane_at(norm_tile, NORM_AT - 4096 + i) for i in range(6)]
    squares[...] = lanes_of(found)

    def onward(m, k, far):
        push(m, k, UP, only=(far < z) & (z < 3))
        push(m, k, DOWN, only=(far > z) & (z > 0))

    def line(ms, s, ways):
        far = near_first(z, s)
        k = chip(far, y, x)
        for m in ms:
            arrived(m, k)
            onward(m, k, far)
            for way in ways:
                push(m, k, way)

    def second(ms, s, axis):
        far = near_first(z, s)
        k = chip(far, y, 1 - x) if axis == XWAY else chip(far, 1 - y, x)
        for m in ms:
            arrived(m, k)
            push(m, k, YWAY if axis == XWAY else XWAY)
            push(m, k, SIDE)

    def third(ms, s, axis):
        far = near_first(z, s)
        for other in range(2):
            k = chip(far, 1 - y, other) if axis == YWAY else chip(far, other, 1 - x)
            for m in ms:
                arrived(m, k)
                push(m, k, SIDE)

    def c_first():
        k = chip(z, 1 - y, x)
        for m in CLASS_C:
            arrived(m, k)
            push(m, k, XWAY)
            push(m, k, UP, only=z < 3)
            push(m, k, DOWN, only=z > 0)
            push(m, k, SIDE)

    def c_second():
        for other in (y, 1 - y):
            k = chip(z, other, 1 - x)
            for m in CLASS_C:
                arrived(m, k)
                push(m, k, UP, only=z < 3)
                push(m, k, DOWN, only=z > 0)
                push(m, k, SIDE)

    def c_line(s):
        far = near_first(z, s)
        for k in (chip(far, y, x), chip(far, 1 - y, x), chip(far, y, 1 - x), chip(far, 1 - y, 1 - x)):
            for m in CLASS_C:
                arrived(m, k)
                onward(m, k, far)
                push(m, k, SIDE)

    both = (XWAY, YWAY, SIDE)
    c_first()
    line(CLASS_A, 1, both)
    line(CLASS_B, 1, both)
    c_second()
    second(CLASS_A, 0, XWAY)
    second(CLASS_B, 0, YWAY)
    c_line(1)
    line(CLASS_A, 2, both)
    line(CLASS_B, 2, both)
    second(CLASS_A, 1, XWAY)
    second(CLASS_B, 1, YWAY)
    c_line(2)
    line(CLASS_A, 3, both)
    line(CLASS_B, 3, both)
    second(CLASS_A, 2, XWAY)
    second(CLASS_B, 2, YWAY)
    c_line(3)
    second(CLASS_A, 3, XWAY)
    second(CLASS_B, 3, YWAY)
    for s in range(4):
        third(CLASS_A, s, YWAY)
        third(CLASS_B, s, XWAY)
    for m in range(5):
        for k in range(16):
            pltpu.make_async_remote_copy(
                src_ref=part(m, k, 1 - c),
                dst_ref=part(m, k, 1 - c),
                send_sem=send_sem.at[m, k, SIDE],
                recv_sem=side_recv.at[m, k],
                device_id=peers[SIDE],
                device_id_type=MESH,
            ).wait_recv()
    for swap in swaps:
        swap.wait_send()
    for keep in keeps:
        keep.wait()
    for m, k, way, own, only in sent:
        if only is None:
            copy_of(m, k, way, own).wait_send()
        else:

            @pl.when(only)
            def _(m=m, k=k, way=way, own=own):
                copy_of(m, k, way, own).wait_send()


def gather_weights(shards):
    return pl.pallas_call(
        gather_kernel,
        out_shape=[jax.ShapeDtypeStruct((32 * size, wide), BF16) for size, wide in SHAPES]
        + [jax.ShapeDtypeStruct((1, 128), F32)],
        in_specs=[pl.BlockSpec(memory_space=pltpu.VMEM)] * 5,
        out_specs=[pl.BlockSpec(memory_space=pl.ANY)] * 5 + [pl.BlockSpec(memory_space=pltpu.VMEM)],
        scratch_shapes=[pltpu.VMEM((2 * size, wide // 2), F32) for size, wide in SHAPES]
        + [pltpu.VMEM((2 * size, wide // 2), BF16) for size, wide in SHAPES]
        + [
            pltpu.SemaphoreType.DMA((5,)),
            pltpu.SemaphoreType.DMA((5,)),
            pltpu.SemaphoreType.DMA((5,)),
            pltpu.SemaphoreType.DMA((5, 16, 5)),
            pltpu.SemaphoreType.DMA((5, 16)),
            pltpu.SemaphoreType.DMA((5, 16)),
        ],
        compiler_params=pltpu.CompilerParams(
            collective_id=0, has_side_effects=True, vmem_limit_bytes=48 * 1024 * 1024
        ),
    )(*shards)


SUM_AT = (0, WIDE, WIDE + 3 * D, WIDE + 4 * D, WIDE + 8 * D, WIDE + 9 * D)
SUMS = WIDE + 9 * D + 256


def lanes_of(members):
    lane = lax.broadcasted_iota(jnp.int32, (1, 128), 1)
    row = jnp.zeros((1, 128), F32)
    for index, member in enumerate(members):
        row = jnp.where(lane == index, member, row)
    return row


def lane_at(row, index):
    lane = lax.broadcasted_iota(jnp.int32, row.shape, 1)
    return jnp.sum(jnp.where(lane == index, row, 0.0), 1, keepdims=True)


def column_of(row):
    size = row.shape[1]
    diagonal = lax.broadcasted_iota(jnp.int32, (size, size), 0) == lax.broadcasted_iota(
        jnp.int32, (size, size), 1
    )
    return jnp.sum(jnp.where(diagonal, row, 0.0), 1, keepdims=True)


def row_of(column):
    size = column.shape[0]
    diagonal = lax.broadcasted_iota(jnp.int32, (size, size), 0) == lax.broadcasted_iota(
        jnp.int32, (size, size), 1
    )
    return jnp.sum(jnp.where(diagonal, column, 0.0), 0, keepdims=True)


def total_sum(array):
    return jnp.sum(jnp.sum(array, 1, keepdims=True), 0, keepdims=True)


def sum_everywhere(value, first, second, third, sems):
    z, y, x, c = here()
    spot = y * 2 + x
    side_send, side_recv, plane_send, plane_recv, z_send, z_recv = sems

    def copy(src, dst, send, recv, peer):
        return pltpu.make_async_remote_copy(
            src_ref=src, dst_ref=dst, send_sem=send, recv_sem=recv, device_id=peer, device_id_type=MESH
        )

    first[0] = value
    swap = copy(first.at[0], first.at[1], side_send, side_recv, device(z, y, x, 1 - c))
    swap.start()
    swap.wait_recv()
    second[spot] = first[0] + first[1]
    plane = []
    for i, (to_y, to_x) in enumerate(((y, 1 - x), (1 - y, x), (1 - y, 1 - x))):
        plane.append(
            copy(second.at[spot], second.at[spot], plane_send.at[i], plane_recv.at[i], device(z, to_y, to_x, c))
        )
        plane[i].start()
    for member in plane:
        member.wait_recv()
    third[z] = (second[0] + second[1]) + (second[2] + second[3])
    column = []
    for i in range(3):
        to_z = (z + 1 + i) % 4
        column.append(copy(third.at[z], third.at[z], z_send.at[i], z_recv.at[i], device(to_z, y, x, c)))
        column[i].start()
    for member in column:
        member.wait_recv()
    for member in [swap] + plane + column:
        member.wait_send()
    return (third[0] + third[1]) + (third[2] + third[3])


def gelu_pair(hidden):
    normal_cdf = 0.5 * (1.0 + lax.erf(hidden * 0.7071067811865476))
    return (
        hidden * normal_cdf,
        normal_cdf + hidden * jnp.exp(-0.5 * hidden * hidden) * 0.3989422804014327,
    )


def dot_nn(left, right):
    return jnp.dot(left, right, preferred_element_type=F32)


def dot_nt(left, right):
    return lax.dot_general(left, right, (((1,), (1,)), ((), ())), preferred_element_type=F32)


def dot_tn(left, right):
    return lax.dot_general(left, right, (((0,), (0,)), ((), ())), preferred_element_type=F32)


def at(index, size):
    return pl.ds(pl.multiple_of(index * size, size), size)


def each(count, body):
    def step(index, carry):
        body(index)
        return carry

    lax.fori_loop(0, count, step, 0)


ROWS = 128
TILE = 256
HALF = 320
TABLE_TILES = TABLE_END // TILE


def head_lanes(first):
    lane = lax.broadcasted_iota(jnp.int32, (1, 128), 1)
    return (lane < HEAD_DIM) if first else (lane >= HEAD_DIM)


def layer_norm(value, gain, shift):
    centred = value - jnp.sum(value, 1, keepdims=True) / D
    inverse = lax.rsqrt(jnp.sum(centred * centred, 1, keepdims=True) / D + EPSILON)
    normed = centred * inverse
    return normed * gain + shift, normed, inverse


def layer_norm_back(grad, normed, inverse, gain):
    scaled = grad * gain
    return inverse * (
        scaled - jnp.sum(scaled, 1, keepdims=True) / D - normed * (jnp.sum(scaled * normed, 1, keepdims=True) / D)
    )


def put_lane(ref, rows, index, value):
    lane = lax.broadcasted_iota(jnp.int32, (1, 128), 1)
    ref[rows, :] = jnp.where(lane == index, value, ref[rows, :])


def set_bias(bias, cols, keys, last):
    same = cols[0:last, 4:5] == keys[1:2, 0:last]
    bias[...] = jnp.where(same & (keys[0:1, 0:last] > 0), 0.0, -1e30)


def forward_kernel(*refs):
    weights, (cols, keys) = refs[0:5], refs[5:7]
    loss_out, count_out, gains_out, norm_out, side = refs[7:12]
    x_t, mix_t, a_t, act_t, y_t, glog_out, slope_out, qkv_out, na_out, nb_out, grad_out = refs[12:23]
    wide, qkv_w, out_w, in_w, down_w = refs[23:28]
    value, na, nb, nc, grad, low_a, mix, qkv, act, slope, logits, pick, bias, turned, act_turned = refs[28:43]
    weight_sem, out_sem, turn_sem, act_sem = refs[43:47]
    tokens = value.shape[0]
    last = tokens - SPAN
    loads = [
        pltpu.make_async_copy(weights[m], (wide, qkv_w, out_w, in_w, down_w)[m], weight_sem.at[m]) for m in range(5)
    ]
    for load in loads:
        load.start()
    set_bias(bias, cols, keys, last)
    side[...] = jnp.zeros(side.shape, F32)
    turns = []

    def turn_out(source, target, slot):
        for copy in turns:
            if copy[1] == slot:
                copy[0].wait()
        turns[:] = [copy for copy in turns if copy[1] != slot]

        def part(index):
            turned[slot, :, at(index, ROWS)] = source[at(index, ROWS), :].T

        each(tokens // ROWS, part)
        copy = pltpu.make_async_copy(turned.at[slot], target, turn_sem.at[slot])
        copy.start()
        turns.append((copy, slot))

    outs = []

    def put_out(source, target):
        copy = pltpu.make_async_copy(source, target, out_sem.at[len(outs)])
        copy.start()
        outs.append(copy)

    loads[0].wait()
    for half in range(tokens // HALF):
        rows = pl.ds(half * HALF, HALF)

        def choose(index):
            column = lax.broadcasted_iota(jnp.int32, (1, TILE), 1) + index * TILE
            hit = (cols[rows, 0:1] == column) | (cols[rows, 1:2] == column)
            pick[:, at(index, TILE)] = jnp.where(hit, 1.0, 0.0).astype(BF16)

        each(WIDE // TILE, choose)

        def embed(index):
            value[rows, at(index, TILE)] = dot_nt(pick[...], wide[at(index, TILE), :])

        each(D // TILE, embed)

    gains = wide[:, 4096:4224].astype(F32).T
    gains_out[...] = gains[0:16]
    counts = jnp.sum(gains[11:13], 1, keepdims=True) / 24.0
    mask_count = counts[0:1] * 256.0 + counts[1:2]
    count_out[...] = mask_count
    inverse_count = 1.0 / mask_count
    norm_rows = [gains_out[5 + i : 6 + i, :] for i in range(6)]

    def norm_a(index):
        rows = at(index, ROWS)
        found, normed, inverse = layer_norm(value[rows, :], norm_rows[0], norm_rows[1])
        value[rows, :] = found
        low_a[rows, :] = found.astype(BF16)
        na[rows, :] = normed
        put_lane(side, rows, 12, inverse)

    each(tokens // ROWS, norm_a)
    put_out(na, na_out)
    loads[1].wait()

    def project(index):
        qkv[:, at(index, TILE)] = dot_nn(low_a[...], qkv_w[:, at(index, TILE)]).astype(BF16)

    each(3 * D // TILE, project)
    put_out(qkv, qkv_out)
    turn_out(low_a, x_t, 0)

    def attend_pair(pair):
        for start, size in ((0, last), (last, SPAN)):
            rows = pl.ds(start, size)
            query = qkv[rows, at(pair, 128)]
            key = qkv[rows, pl.ds(pl.multiple_of(D + pair * 128, 128), 128)]
            val = qkv[rows, pl.ds(pl.multiple_of(2 * D + pair * 128, 128), 128)]
            mask = bias[...] if start == 0 else jnp.where(keys[0:1, last:tokens] > 0, 0.0, -1e30)
            mixed = []
            for first in (True, False):
                chosen = jnp.where(head_lanes(first), query, jnp.zeros_like(query))
                scores = dot_nt(chosen, key) * 0.125 + mask
                highest = jnp.max(scores, 1, keepdims=True)
                raised = jnp.exp(scores - highest)
                summed = jnp.sum(raised, 1, keepdims=True)
                shares = (raised * (1.0 / summed)).astype(BF16)
                mixed.append(dot_nn(shares, val))
                put_lane(side, rows, 2 * pair + (0 if first else 1), highest + jnp.log(summed))
            mix[rows, at(pair, 128)] = jnp.where(head_lanes(True), mixed[0], mixed[1]).astype(BF16)

    each(HEADS // 2, attend_pair)
    loads[2].wait()

    def out_project(index):
        value[:, at(index, TILE)] = value[:, at(index, TILE)] + dot_nn(mix[...], out_w[:, at(index, TILE)])

    each(D // TILE, out_project)
    turn_out(mix, mix_t, 1)

    def norm_b(index):
        rows = at(index, ROWS)
        found, normed, inverse = layer_norm(value[rows, :], norm_rows[2], norm_rows[3])
        value[rows, :] = found
        low_a[rows, :] = found.astype(BF16)
        nb[rows, :] = normed
        put_lane(side, rows, 13, inverse)

    each(tokens // ROWS, norm_b)
    put_out(nb, nb_out)
    loads[3].wait()

    def feed_in(index):
        hidden = dot_nn(low_a[...], in_w[:, at(index, TILE)])
        active, slant = gelu_pair(hidden)
        active = active.astype(BF16)
        act[:, at(index, TILE)] = active
        slope[:, at(index, TILE)] = slant.astype(BF16)
        slot = lax.rem(index, 2)

        def copy():
            return pltpu.make_async_copy(act_turned.at[slot], act_t.at[at(index, TILE), :], act_sem.at[slot])

        @pl.when(index >= 2)
        def _():
            copy().wait()

        act_turned[slot] = active.T
        copy().start()

    each(4 * D // TILE, feed_in)
    for slot in range(2):
        pltpu.make_async_copy(act_turned.at[slot], act_t.at[0:TILE, :], act_sem.at[slot]).wait()
    put_out(slope, slope_out)
    turn_out(low_a, a_t, 0)
    loads[4].wait()

    def feed_out(index):
        value[:, at(index, TILE)] = value[:, at(index, TILE)] + dot_nn(act[...], down_w[:, at(index, TILE)])

    each(D // TILE, feed_out)

    def norm_c(index):
        rows = at(index, ROWS)
        found, normed, inverse = layer_norm(value[rows, :], norm_rows[4], norm_rows[5])
        low_a[rows, :] = found.astype(BF16)
        nc[rows, :] = normed
        put_lane(side, rows, 14, inverse)

    each(tokens // ROWS, norm_c)
    turn_out(low_a, y_t, 1)
    loss = jnp.zeros((1, 1), F32)
    for half in range(tokens // HALF):
        rows = pl.ds(half * HALF, HALF)
        target = cols[rows, 2:3]
        weight = cols[rows, 3:4].astype(F32)

        def lanes(index):
            return lax.broadcasted_iota(jnp.int32, (1, TILE), 1) + index * TILE

        def multiply(index, highest):
            found = dot_nn(low_a[rows, :], wide[:, at(index, TILE)])
            found = jnp.where(lanes(index) < VOCAB, found, -1e30)
            logits[:, at(index, TILE)] = found
            return jnp.maximum(highest, jnp.maximum(found[:, 0:128], found[:, 128:256]))

        highest = lax.fori_loop(0, TABLE_TILES, multiply, jnp.full((HALF, 128), -1e30, F32))
        highest = jnp.max(highest, 1, keepdims=True)

        def raise_to(index, carry):
            summed, picked = carry
            found = logits[:, at(index, TILE)]
            raised = jnp.exp(found - highest)
            logits[:, at(index, TILE)] = raised
            hit = jnp.where(lanes(index) == target, found, 0.0)
            return summed + raised[:, 0:128] + raised[:, 128:256], picked + hit[:, 0:128] + hit[:, 128:256]

        zero = jnp.zeros((HALF, 128), F32)
        summed, picked = lax.fori_loop(0, TABLE_TILES, raise_to, (zero, zero))
        summed = jnp.sum(summed, 1, keepdims=True)
        picked = jnp.sum(picked, 1, keepdims=True)
        loss = loss + jnp.sum(weight * (highest + jnp.log(summed) - picked), 0, keepdims=True)
        scale = weight * inverse_count
        share = scale / summed
        if half > 0:
            outs[-1].wait()

        def differ(index):
            found = logits[:, at(index, TILE)] * share - jnp.where(lanes(index) == target, scale, 0.0)
            pick[:, at(index, TILE)] = found.astype(BF16)

        each(TABLE_TILES, differ)
        put_out(pick.at[:, 0:TABLE_END], glog_out.at[rows, :])

        def back(index):
            grad[rows, at(index, TILE)] = dot_nt(pick[:, 0:TABLE_END], wide[at(index, TILE), 0:TABLE_END])

        each(D // TILE, back)
    loss_out[...] = loss

    def norm_c_back(index, carry):
        gain, shift = carry
        rows = at(index, ROWS)
        inverse = lane_at(side[rows, :], 14)
        found, normed = grad[rows, :], nc[rows, :]
        grad[rows, :] = layer_norm_back(found, normed, inverse, norm_rows[4])
        return gain + jnp.sum(found * normed, 0, keepdims=True), shift + jnp.sum(found, 0, keepdims=True)

    zero = jnp.zeros((1, D), F32)
    gain, shift = lax.fori_loop(0, tokens // ROWS, norm_c_back, (zero, zero))
    norm_out[0:1, :] = gain
    norm_out[1:2, :] = shift
    put_out(grad, grad_out)
    for index, copy in enumerate(outs):
        if index != 4:
            copy.wait()
    for copy, _ in turns:
        copy.wait()


def forward(weights, cols, keys):
    tokens = cols.shape[0]
    vmem, hbm = pl.BlockSpec(memory_space=pltpu.VMEM), pl.BlockSpec(memory_space=pl.ANY)
    shape = jax.ShapeDtypeStruct
    small = [shape((1, 1), F32), shape((1, 1), F32), shape((16, D), F32), shape((2, D), F32), shape((tokens, 128), F32)]
    large = [shape((D, tokens), BF16)] * 3 + [shape((4 * D, tokens), BF16), shape((D, tokens), BF16)]
    large += [shape((tokens, TABLE_END), BF16), shape((tokens, 4 * D), BF16), shape((tokens, 3 * D), BF16)]
    large += [shape((tokens, D), F32)] * 3
    return pl.pallas_call(
        forward_kernel,
        out_shape=small + large,
        in_specs=[hbm] * 5 + [vmem] * 2,
        out_specs=[vmem] * len(small) + [hbm] * len(large),
        scratch_shapes=[pltpu.VMEM((32 * size, wide), BF16) for size, wide in SHAPES]
        + [pltpu.VMEM((tokens, D), F32)] * 5
        + [pltpu.VMEM((tokens, D), BF16)] * 2
        + [
            pltpu.VMEM((tokens, 3 * D), BF16),
            pltpu.VMEM((tokens, 4 * D), BF16),
            pltpu.VMEM((tokens, 4 * D), BF16),
            pltpu.VMEM((HALF, TABLE_END), F32),
            pltpu.VMEM((HALF, WIDE), BF16),
            pltpu.VMEM((tokens - SPAN, tokens - SPAN), F32),
            pltpu.VMEM((2, D, tokens), BF16),
            pltpu.VMEM((2, TILE, tokens), BF16),
            pltpu.SemaphoreType.DMA((5,)),
            pltpu.SemaphoreType.DMA((8,)),
            pltpu.SemaphoreType.DMA((2,)),
            pltpu.SemaphoreType.DMA((2,)),
        ],
        compiler_params=pltpu.CompilerParams(vmem_limit_bytes=62 * 1024 * 1024),
    )(*weights, cols, keys)


def backward_kernel(*refs):
    loaded, (cols, keys, side, gains) = refs[0:9], refs[9:13]
    norm_out, ge_t, gffn_out, gh_out, gattn_out, gqkv_out = refs[13:19]
    qkv_w, out_w, in_w, down_w, slope, qkv, na, nb, grad = refs[19:28]
    low, attn, gh, bias, turned, load_sem, out_sem = refs[28:35]
    tokens = grad.shape[0]
    last = tokens - SPAN
    held = (qkv_w, out_w, in_w, down_w, slope, qkv, na, nb, grad)
    loads = [pltpu.make_async_copy(loaded[i], held[i], load_sem.at[i]) for i in range(9)]
    order = (8, 3, 4, 2, 7, 1, 5, 0, 6)
    for i in order:
        loads[i].start()
    outs = []

    def put_out(source, target):
        copy = pltpu.make_async_copy(source, target, out_sem.at[len(outs)])
        copy.start()
        outs.append(copy)

    set_bias(bias, cols, keys, last)
    loads[8].wait()

    def round_grad(index):
        rows = at(index, ROWS)
        low[rows, :] = grad[rows, :].astype(BF16)

    each(tokens // ROWS, round_grad)
    put_out(low, gffn_out)
    loads[3].wait()
    loads[4].wait()

    def feed_out_back(index):
        found = dot_nt(low[...], down_w[at(index, TILE), :]) * slope[:, at(index, TILE)].astype(F32)
        gh[:, at(index, TILE)] = found.astype(BF16)

    each(4 * D // TILE, feed_out_back)
    put_out(gh, gh_out)
    loads[2].wait()

    def feed_in_back(index):
        grad[:, at(index, TILE)] = grad[:, at(index, TILE)] + dot_nt(gh[...], in_w[at(index, TILE), :])

    each(D // TILE, feed_in_back)
    loads[7].wait()
    outs[0].wait()
    zero = jnp.zeros((1, D), F32)

    def norm_b_back(index, carry):
        gain, shift = carry
        rows = at(index, ROWS)
        inverse = lane_at(side[rows, :], 13)
        found, normed = grad[rows, :], nb[rows, :]
        back = layer_norm_back(found, normed, inverse, gains[7:8, :])
        grad[rows, :] = back
        low[rows, :] = back.astype(BF16)
        return gain + jnp.sum(found * normed, 0, keepdims=True), shift + jnp.sum(found, 0, keepdims=True)

    gain, shift = lax.fori_loop(0, tokens // ROWS, norm_b_back, (zero, zero))
    norm_out[2:3, :] = gain
    norm_out[3:4, :] = shift
    put_out(low, gattn_out)
    loads[1].wait()

    def out_back(index):
        attn[:, at(index, TILE)] = dot_nt(low[...], out_w[at(index, TILE), :]).astype(BF16)

    each(D // TILE, out_back)
    loads[5].wait()

    def attend_pair_back(pair):
        for start, size in ((0, last), (last, SPAN)):
            rows = pl.ds(start, size)
            spots = [pl.ds(pl.multiple_of(i * D + pair * 128, 128), 128) for i in range(3)]
            query, key, val = (qkv[rows, spot] for spot in spots)
            given = attn[rows, at(pair, 128)]
            mask = bias[...] if start == 0 else jnp.where(keys[0:1, last:tokens] > 0, 0.0, -1e30)
            found = []
            for first in (True, False):
                lanes = head_lanes(first)
                chosen = jnp.where(lanes, query, jnp.zeros_like(query))
                mine = jnp.where(lanes, given, jnp.zeros_like(given))
                total = lane_at(side[rows, :], 2 * pair + (0 if first else 1))
                shares = jnp.exp(dot_nt(chosen, key) * 0.125 + mask - total)
                grad_share = dot_nt(mine, val)
                middle = jnp.sum(shares * grad_share, 1, keepdims=True)
                grad_score = (shares * (grad_share - middle)).astype(BF16)
                found.append(
                    (
                        dot_nn(grad_score, key) * 0.125,
                        dot_tn(grad_score, query) * 0.125,
                        dot_tn(shares.astype(BF16), given),
                    )
                )
            for i in range(3):
                qkv[rows, spots[i]] = jnp.where(head_lanes(True), found[0][i], found[1][i]).astype(BF16)

    each(HEADS // 2, attend_pair_back)
    put_out(qkv, gqkv_out)
    loads[0].wait()

    def project_back(index):
        grad[:, at(index, TILE)] = grad[:, at(index, TILE)] + dot_nt(qkv[...], qkv_w[at(index, TILE), :])

    each(D // TILE, project_back)
    loads[6].wait()

    def norm_a_back(index, carry):
        gain, shift = carry
        rows = at(index, ROWS)
        inverse = lane_at(side[rows, :], 12)
        found, normed = grad[rows, :], na[rows, :]
        turned[:, rows] = layer_norm_back(found, normed, inverse, gains[5:6, :]).astype(BF16).T
        return gain + jnp.sum(found * normed, 0, keepdims=True), shift + jnp.sum(found, 0, keepdims=True)

    gain, shift = lax.fori_loop(0, tokens // ROWS, norm_a_back, (zero, zero))
    norm_out[0:1, :] = gain
    norm_out[1:2, :] = shift
    put_out(turned, ge_t)
    for copy in outs[1:]:
        copy.wait()


def backward(weights, slope, qkv, na, nb, grad, cols, keys, side, gains):
    tokens = grad.shape[0]
    vmem, hbm = pl.BlockSpec(memory_space=pltpu.VMEM), pl.BlockSpec(memory_space=pl.ANY)
    shape = jax.ShapeDtypeStruct
    loaded = tuple(weights) + (slope, qkv, na, nb, grad)
    widths = (D, D, 4 * D, D, 3 * D)
    return pl.pallas_call(
        backward_kernel,
        out_shape=[shape((4, D), F32), shape((D, tokens), BF16)]
        + [shape((tokens, width), BF16) for width in (D, 4 * D, D, 3 * D)],
        in_specs=[hbm] * 9 + [vmem] * 4,
        out_specs=[vmem] + [hbm] * 5,
        scratch_shapes=[pltpu.VMEM(member.shape, member.dtype) for member in loaded]
        + [
            pltpu.VMEM((tokens, D), BF16),
            pltpu.VMEM((tokens, D), BF16),
            pltpu.VMEM((tokens, 4 * D), BF16),
            pltpu.VMEM((tokens - SPAN, tokens - SPAN), F32),
            pltpu.VMEM((D, tokens), BF16),
            pltpu.SemaphoreType.DMA((9,)),
            pltpu.SemaphoreType.DMA((5,)),
        ],
        compiler_params=pltpu.CompilerParams(vmem_limit_bytes=60 * 1024 * 1024),
    )(*loaded, cols, keys, side, gains)


LEFT = 768
PIECES = ((Q_, 0, 1152), (E_, 0, 1280), (E_, 1280, 1280), (I_, 0, 1536), (D_, 0, 384), (O_, 0, 384))
Y_FIRST = (0, 1, 4)
TASKS = (
    0, 1, 96, 9, 4, 129, 97, 2, 103, 5, 99, 7, 8, 6, 101, 128, 102, 105,
    100, 132, 133, 64, 108, 12, 104, 136, 139, 134, 65, 15, 107, 111, 109, 137, 161, 13,
    160, 3, 131, 11, 141, 142, 70, 32, 68, 112, 110, 76, 140, 16, 168, 67, 144, 72,
    169, 75, 135, 71, 33, 36, 69, 143, 166, 173, 38, 98, 39, 43, 78, 130, 167, 73,
    37, 40, 79, 44, 34, 164, 46, 66, 77, 14, 47, 165, 45, 162, 171, 41, 172, 176,
    80, 138, 174, 74, 48, 10, 106, 42, 175, 35, 81, 145, 163, 170, 113, 17, 49, 177,
)


def reduce_kernel(*refs):
    given, (cols, norm_ab, norm_c, loss, squares) = refs[0:11], refs[11:16]
    y_t, ge_t, glog, x_t, gqkv, mix_t, gattn, a_t, gh, act_t, gffn = given
    lane_olds, side_olds, moment = refs[16:22], refs[22:28], refs[28]
    outs, sums_out, totals_out = refs[29:34], refs[34], refs[35]
    own, side, first, second, column, fin = (refs[36 + 6 * i : 42 + 6 * i] for i in range(6))
    left, (glog_v, gqkv_v, gattn_v, gh_v, gffn_v), stage, tails, norm_t = refs[72:79], refs[79:84], refs[84], refs[85], refs[86]
    spread, spread_small = refs[87:90], refs[90:93]
    load_sem, ring_sem, tail_sem, side_recv, first_send, first_recv, second_send, second_recv = refs[93:101]
    z_send, z_recv, swap_send, swap_recv = refs[101:105]
    sems, small_sems = refs[105:111], refs[111:117]
    z, y, x, c = here()
    peers = all_peers()
    me = chip(z, y, x)

    barrier = pltpu.get_barrier_semaphore()
    greeted = [peers[XWAY], peers[YWAY], peers[SIDE], device(z, 1 - y, 1 - x, c)]
    greeted += [device((z + 1 + i) % 4, y, x, c) for i in range(3)]
    for peer in greeted:
        pl.semaphore_signal(barrier, inc=1, device_id=peer, device_id_type=MESH)

    def act_part(group):
        return act_t.at[pl.ds(LEFT * group, LEFT), :]

    operands = (
        ((x_t, left[1]), (gqkv, gqkv_v)),
        ((y_t, left[2]), (ge_t, left[3]), (glog, glog_v)),
        (),
        ((a_t, left[0]), (gh, gh_v)),
        ((gffn, gffn_v), (act_part(0), left[5]), (act_part(1), left[6])),
        ((mix_t, left[4]), (gattn, gattn_v)),
    )
    loads = {}
    waited = set()
    for task in TASKS:
        piece = task // 32 if task // 32 != 2 else 1
        if piece not in loads:
            loads[piece] = []
            for source, target in operands[piece]:
                number = sum(len(member) for member in loads.values())
                loads[piece].append(pltpu.make_async_copy(source, target, load_sem.at[number]))
                loads[piece][-1].start()

    def loaded(piece):
        piece = 1 if piece == 2 else piece
        if piece not in waited:
            waited.add(piece)
            for member in loads[piece]:
                member.wait()

    norm_t[...] = jnp.zeros(norm_t.shape, F32)
    norm_t[5:9, :] = norm_ab[...]
    norm_t[9:11, :] = norm_c[...]
    pl.semaphore_wait(barrier, 7)

    def size_of(piece):
        return 2 * SHAPES[PIECES[piece][0]][0]

    def slot(ref, piece, index):
        size = size_of(piece)
        return ref[piece].at[pl.ds(pl.multiple_of(index * size, size), size), :]

    def half_of(piece):
        return SHAPES[PIECES[piece][0]][1] // 2

    def chosen(start):
        lane = lax.broadcasted_iota(jnp.int32, (1, TILE), 1) + start
        hit = (cols[:, 0:1] == lane) | (cols[:, 1:2] == lane)
        return jnp.where(hit, 1.0, 0.0).astype(BF16)

    def ring_copy(piece, rows, lanes, number, index):
        place = lax.rem(number, 3)
        return pltpu.make_async_remote_copy(
            src_ref=stage.at[place],
            dst_ref=side[piece].at[rows, lanes],
            send_sem=ring_sem.at[place],
            recv_sem=side_recv.at[piece, index],
            device_id=peers[SIDE],
            device_id_type=MESH,
        )

    def tail_copy(piece, rows, lanes, number, index):
        return pltpu.make_async_remote_copy(
            src_ref=tails.at[number],
            dst_ref=side[piece].at[rows, lanes],
            send_sem=tail_sem.at[number],
            recv_sem=side_recv.at[piece, index],
            device_id=peers[SIDE],
            device_id_type=MESH,
        )

    whole = pl.ds(0, LEFT)
    ring_count, tail_count = [0], [0]

    def give(piece, rows, lanes, number, index):
        def before():
            @pl.when(number >= 3)
            def _():
                ring_copy(piece, rows, lanes, number, index).wait_send()

        def write(value):
            stage[lax.rem(number, 3)] = value.astype(BF16)

        return before, write, lambda: ring_copy(piece, rows, lanes, number, index).start()

    def keep(piece, rows, lanes):
        def write(value):
            own[piece][rows, lanes] = value.astype(BF16)

        return lambda: None, write, lambda: None

    def plain(piece, mine, source, right, group):
        wide = PIECES[piece][2]
        half = c if mine else 1 - c
        rows = pl.ds(LEFT * group, LEFT)
        base = ring_count[0]

        def step(j):
            lanes = at(j, TILE)
            before, write, after = keep(piece, rows, lanes) if mine else give(
                piece, rows, lanes, base + j, group * (wide // TILE) + j
            )
            before()
            write(dot_nn(source[...], right[:, pl.ds(pl.multiple_of(half * wide + j * TILE, 128), TILE)]))
            after()

        each(wide // TILE, step)
        if not mine:
            ring_count[0] += wide // TILE
        if wide % TILE:
            start = wide - 128
            value = dot_nn(source[...], right[:, pl.ds(pl.multiple_of(half * wide + start, 128), 128)])
            if mine:
                own[piece][rows, start:wide] = value.astype(BF16)
            else:
                number = tail_count[0]
                tail_count[0] += 1
                groups = SHAPES[PIECES[piece][0]][0] // 24
                tails[number] = value.astype(BF16)
                tail_copy(piece, rows, pl.ds(start, 128), number, groups * (wide // TILE) + group).start()

    def wide_product(piece, mine):
        half = c if mine else 1 - c
        wide = half_of(piece)
        skip = PIECES[piece][1] // TILE
        base = ring_count[0]

        def both(j):
            start = pl.multiple_of(half * wide + (skip + j) * TILE, TILE)
            return dot_nn(left[2][...], glog_v[:, pl.ds(start, TILE)]) + dot_nn(left[3][...], chosen(start))

        def target(j):
            lanes = at(j, TILE)
            return keep(piece, whole, lanes) if mine else give(piece, whole, lanes, base + j, j)

        def step(j):
            before, write, after = target(j)
            before()
            write(both(j))
            after()

        if not mine:
            ring_count[0] += 5
        if skip == 0:
            each(5, step)
            return
        each(1, step)
        before, write, after = target(1)
        before()
        norm_part = jnp.where(half == 1, norm_t[...], 0.0).T
        write(both(1) + jnp.concatenate((norm_part, jnp.zeros((LEFT, TILE - 128), F32)), 1))
        after()
        for j in range(2, 5):
            before, write, after = target(j)
            before()

            @pl.when(half == 0)
            def _():
                write(both(j))

            @pl.when(half == 1)
            def _():
                if j == 2:
                    write(jnp.zeros((LEFT, TILE), F32))
                else:
                    write(dot_nn(left[3][...], chosen(half_of(piece) + (skip + j) * TILE)))

            after()

    def products(piece, mine):
        loaded(piece)
        if piece in (1, 2):
            wide_product(piece, mine)
        elif piece == 4:
            if not mine:
                for group in range(4):
                    source = left[5 + group % 2]
                    if group >= 2:
                        loads[piece][1 + group % 2].wait()
                    plain(piece, False, source, gffn_v, group)
                    plain(piece, True, source, gffn_v, group)
                    if group < 2:
                        again = pltpu.make_async_copy(act_part(group + 2), source, load_sem.at[12 + group])
                        again.start()
                        loads[piece][1 + group] = again
        else:
            source, right = {0: (left[1], gqkv_v), 3: (left[0], gh_v), 5: (left[4], gattn_v)}[piece]
            plain(piece, mine, source, right, 0)

    def combine(piece, target, parts):
        def some(rows, lanes):
            total = parts[0][rows, lanes].astype(F32)
            for member in parts[1:]:
                total = total + member[rows, lanes].astype(F32)
            target[rows, lanes] = total.astype(target.dtype)

        wide = PIECES[piece][2]
        if piece == 4:
            each(4, lambda group: some(at(group, 48), slice(0, wide)))
            return
        if wide >= 512:
            each(wide // 512, lambda j: some(slice(0, 48), at(j, 512)))
        if wide % 512:
            some(slice(0, 48), slice(wide // 512 * 512, wide))

    def hop(piece, k, land, index, sems, way):
        return pltpu.make_async_remote_copy(
            src_ref=slot(own, piece, k),
            dst_ref=slot(land, piece, index),
            send_sem=sems[0].at[piece, index],
            recv_sem=sems[1].at[piece, index],
            device_id=peers[way],
            device_id_type=MESH,
        )

    FIRST, SECOND = (first_send, first_recv), (second_send, second_recv)

    def landed(piece, land, index, sems):
        hop(piece, me, land, index, sems, XWAY).wait_recv()

    def block(piece, a, b, far):
        return chip(far, a, b) if piece in Y_FIRST else chip(far, b, a)

    def split(piece):
        return (y, x, YWAY, XWAY) if piece in Y_FIRST else (x, y, XWAY, YWAY)

    readied = set()

    def ready(piece):
        if piece in readied:
            return
        readied.add(piece)
        wide, groups = PIECES[piece][2], SHAPES[PIECES[piece][0]][0] // 24
        for group in range(groups):
            for j in range(wide // TILE):
                ring_copy(piece, pl.ds(LEFT * group, LEFT), at(j, TILE), 0, group * (wide // TILE) + j).wait_recv()
            if wide % TILE:
                index = groups * (wide // TILE) + group
                tail_copy(piece, pl.ds(LEFT * group, LEFT), pl.ds(wide - 128, 128), 0, index).wait_recv()

    def both_cores(piece, k):
        return (slot(own, piece, k), slot(side, piece, k))

    def first_block(piece, i):
        a, b, way, _ = split(piece)
        t, v = (z + i // 2) % 4, (1 - b) if i % 2 == 0 else b
        return block(piece, 1 - a, v, t), 2 * t + v, way

    def first_send_of(piece, i):
        ready(piece)
        k, index, way = first_block(piece, i)
        combine(piece, slot(own, piece, k), both_cores(piece, k))
        hop(piece, k, first, index, FIRST, way).start()

    def second_block(piece, i):
        a, b, _, way = split(piece)
        t = (z + i) % 4
        return block(piece, a, 1 - b, t), t, way

    def second_send_of(piece, i):
        k, t, way = second_block(piece, i)
        spot = 2 * t + 1 - split(piece)[1]
        landed(piece, first, spot, FIRST)
        combine(piece, slot(own, piece, k), both_cores(piece, k) + (slot(first, piece, spot),))
        hop(piece, k, second, t, SECOND, way).start()

    def z_copy(piece, i):
        t = (z + i) % 4
        return pltpu.make_async_remote_copy(
            src_ref=slot(own, piece, chip(t, y, x)),
            dst_ref=slot(column, piece, z),
            send_sem=z_send.at[piece, t],
            recv_sem=z_recv.at[piece, z],
            device_id=device(t, y, x, c),
            device_id_type=MESH,
        )

    def z_landed(piece, i):
        t = (z + i) % 4
        pltpu.make_async_remote_copy(
            src_ref=slot(own, piece, me),
            dst_ref=slot(column, piece, t),
            send_sem=z_send.at[piece, t],
            recv_sem=z_recv.at[piece, t],
            device_id=device(t, y, x, c),
            device_id_type=MESH,
        ).wait_recv()
        return slot(column, piece, t)

    def gathered(piece, t):
        spot = 2 * t + split(piece)[1]
        landed(piece, first, spot, FIRST)
        landed(piece, second, t, SECOND)
        return both_cores(piece, chip(t, y, x)) + (slot(first, piece, spot), slot(second, piece, t))

    def z_send_of(piece, i):
        t = (z + i) % 4
        combine(piece, slot(own, piece, chip(t, y, x)), gathered(piece, t))
        z_copy(piece, i).start()

    swaps = []

    def finish(piece):
        parts = gathered(piece, z)
        parts = parts + tuple(z_landed(piece, i) for i in (1, 2, 3))
        combine(piece, fin[piece], parts)
        m, skip, wide = PIECES[piece]
        size = SHAPES[m][0]
        lanes = pl.ds(pl.multiple_of(c * half_of(piece) + skip, 128), wide)
        swaps.append(
            pltpu.make_async_remote_copy(
                src_ref=fin[piece].at[pl.ds(pl.multiple_of((1 - c) * size, 8), size), :],
                dst_ref=outs[m].at[:, lanes],
                send_sem=swap_send.at[piece],
                recv_sem=swap_recv.at[piece],
                device_id=peers[SIDE],
                device_id_type=MESH,
            )
        )
        swaps[-1].start()
        outs[m][:, lanes] = fin[piece][pl.ds(pl.multiple_of(c * size, 8), size), :]

    for task in TASKS:
        piece, number = task // 32, task % 32
        if number < 2:
            products(piece, number == 1)
        elif number < 10:
            first_send_of(piece, number - 2)
        elif number < 14:
            second_send_of(piece, number - 10)
        elif number < 17:
            z_send_of(piece, number - 13)
        else:
            finish(piece)
    for piece in range(6):
        for i in range(8):
            k, index, way = first_block(piece, i)
            hop(piece, k, first, index, FIRST, way).wait_send()
        for i in range(4):
            k, t, way = second_block(piece, i)
            hop(piece, k, second, t, SECOND, way).wait_send()
        for i in (1, 2, 3):
            z_copy(piece, i).wait_send()
    for number in range(ring_count[0] - 3, ring_count[0]):
        ring_copy(1, whole, pl.ds(0, TILE), number, 0).wait_send()
    for number in range(tail_count[0]):
        tail_copy(1, whole, pl.ds(0, 128), number, 0).wait_send()
    for swap in swaps:
        swap.wait()

    sides, lanes, _, gs = statistics(outs, lane_olds, side_olds)
    scalars = lanes_of([jnp.sum(member, 0, keepdims=True) for member in sides] + [loss[...]])
    sums = jnp.concatenate(lanes + [scalars, squares[...]], 1)
    sums = sum_everywhere(sums, *spread, sems)
    sums_out[...] = sums
    updates = updates_of(sums, gs, sides, lane_olds, moment)[0]
    totals = lanes_of(
        [total_sum(update * update) for update in updates[:6]]
        + [jnp.sum(updates[6][i : i + 1] * updates[6][i : i + 1], 1, keepdims=True) for i in range(6)]
    )
    totals_out[...] = sum_everywhere(totals, *spread_small, small_sems)


def statistics(grads, lane_olds, side_olds):
    wide_g = grads[E_][...]
    gs = (wide_g[:, :VOCAB], wide_g[:, PLACE_AT:]) + tuple(grads[m][...] for m in (Q_, O_, I_, D_))
    gs = gs + (wide_g[:, 4096:4224],)
    decay = 1.0 - STEP ** (-0.8)
    sides, lanes = [], []
    wide_square = wide_g * wide_g + SQUARE_FLOOR
    squares = [wide_square[:, :VOCAB], wide_square[:, PLACE_AT:]] + [g * g + SQUARE_FLOOR for g in gs[2:6]]
    for index in range(6):
        mean = jnp.sum(squares[index], 1, keepdims=True) / squares[index].shape[1]
        sides.append(decay * column_of(side_olds[index][...]) + (1.0 - decay) * mean)
    lanes = [jnp.sum(square, 0, keepdims=True) for square in [wide_square] + squares[2:]]
    return sides, lanes, squares, gs


def updates_of(sums, gs, sides, lane_olds, moment):
    decay = 1.0 - STEP ** (-0.8)
    fresh = 1.0 - decay
    parts = [sums[:, :VOCAB], sums[:, PLACE_AT:WIDE]]
    parts += [sums[:, SUM_AT[i] : SUM_AT[i + 1]] for i in range(1, 5)]
    scalars = sums[:, SUM_AT[5] : SUM_AT[5] + 128]
    updates, lane_news = [], []
    for index in range(6):
        height = gs[index].shape[0] * 32
        lane_news.append(decay * lane_olds[index][...] + fresh * (parts[index] / height))
        if index < 2:
            mean = jnp.sum(lane_news[index], 1, keepdims=True) / lane_news[index].shape[1]
        else:
            mean = lane_at(scalars, index) / height
        updates.append(gs[index] * lax.rsqrt(sides[index] * lane_news[index] / mean))
    norm_g = jnp.concatenate([row_of(lane_at(gs[6], NORM_AT - 4096 + i)) for i in range(6)], 0)
    moment_new = decay * moment[...] + fresh * (norm_g * norm_g + SQUARE_FLOOR)
    updates.append(norm_g * lax.rsqrt(moment_new))
    return updates, lane_news, norm_g, moment_new


def reduce_grads(large, small):
    tokens = large[2].shape[0]
    vmem, hbm = pl.BlockSpec(memory_space=pltpu.VMEM), pl.BlockSpec(memory_space=pl.ANY)
    dma = pltpu.SemaphoreType.DMA
    scratch = []
    for count in (16, 16, 8, 4, 4):
        scratch += [pltpu.VMEM((count * 2 * SHAPES[m][0], wide), BF16) for m, _, wide in PIECES]
    scratch += [pltpu.VMEM((2 * SHAPES[m][0], wide), F32) for m, _, wide in PIECES]
    scratch += [pltpu.VMEM((LEFT, tokens), BF16)] * 7
    scratch += [pltpu.VMEM((tokens, width), BF16) for width in (TABLE_END, 3 * D, D, 4 * D, D)]
    scratch += [pltpu.VMEM((3, LEFT, TILE), BF16), pltpu.VMEM((6, LEFT, 128), BF16), pltpu.VMEM((128, D), F32)]
    scratch += [pltpu.VMEM((count, 1, SUMS), F32) for count in (2, 4, 4)]
    scratch += [pltpu.VMEM((count, 1, 128), F32) for count in (2, 4, 4)]
    scratch += [dma((14,)), dma((3,)), dma((6,)), dma((6, 10)), dma((6, 8)), dma((6, 8)), dma((6, 4)), dma((6, 4))]
    scratch += [dma((6, 4)), dma((6, 4)), dma((6,)), dma((6,))]
    scratch += ([dma] * 2 + [dma((3,))] * 4) * 2
    return pl.pallas_call(
        reduce_kernel,
        out_shape=[jax.ShapeDtypeStruct(shape, F32) for shape in SHAPES + ((1, SUMS), (1, 128))],
        in_specs=[hbm] * 11 + [vmem] * len(small),
        out_specs=[vmem] * 7,
        scratch_shapes=scratch,
        compiler_params=pltpu.CompilerParams(
            collective_id=1, has_side_effects=True, vmem_limit_bytes=63 * 1024 * 1024
        ),
    )(*large, *small)


def update_kernel(*refs):
    copies = [pltpu.make_async_copy(refs[i], refs[55 + i], refs[82].at[i]) for i in range(27)]
    for copy in copies:
        copy.start()
    for copy in copies:
        copy.wait()
    refs = refs[55:82] + refs[27:55]
    grads, sums, totals, ws, norms = refs[0:5], refs[5], refs[6], refs[7:13], refs[13]
    lane_olds, side_olds, moment = refs[14:20], refs[20:26], refs[26]
    loss_out, table_g, place_g, norm_g_out = refs[27:31]
    lane_outs, side_outs, moment_out, news, norm_new = refs[31:37], refs[37:43], refs[43], refs[44:50], refs[50]
    grad_outs = refs[51:55]
    sides, _, _, gs = statistics(grads, lane_olds, side_olds)
    updates, lane_news, norm_g, moment_new = updates_of(sums[...], gs, sides, lane_olds, moment)
    scalars = sums[:, SUM_AT[5] : SUM_AT[5] + 128]
    squares = sums[:, SUM_AT[5] + 128 :]
    loss_out[...] = lane_at(scalars, 6)
    table_g[...] = gs[0]
    place_g[...] = gs[1]
    norm_g_out[...] = norm_g
    moment_out[...] = moment_new
    for index in range(6):
        lane_outs[index][...] = lane_news[index]
        side_outs[index][...] = row_of(sides[index])
        if index >= 2:
            grad_outs[index - 2][...] = gs[index]
        entries = gs[index].shape[0] * gs[index].shape[1] * 32
        clip = jnp.maximum(1.0, jnp.sqrt(lane_at(totals[...], index) / entries))
        scale = learn_rate * jnp.sqrt(lane_at(squares, index) / entries) / clip
        news[index][...] = ws[index][...] - scale * updates[index]
    for i in range(6):
        clip = jnp.maximum(1.0, jnp.sqrt(lane_at(totals[...], 6 + i) / D))
        scale = learn_rate * jnp.sqrt(lane_at(squares, 6 + i) / D) / clip
        norm_new[i : i + 1, :] = norms[i : i + 1, :] - scale * updates[6][i : i + 1, :]


def update_weights(operands):
    lanes = (VOCAB, 512, 3 * D, D, 4 * D, D)
    held = (24, 24, 24, 24, 24, 96)
    shapes = [(1, 1), (24, VOCAB), (24, 512), (6, 24)]
    shapes += [(1, lane) for lane in lanes] + [(1, size) for size in held] + [(6, 24)]
    shapes += list(zip(held, lanes)) + [(6, 24)] + list(zip(held, lanes))[2:]
    return pl.pallas_call(
        update_kernel,
        out_shape=[jax.ShapeDtypeStruct(shape, F32) for shape in shapes],
        in_specs=[pl.BlockSpec(memory_space=pl.ANY)] * len(operands),
        out_specs=[pl.BlockSpec(memory_space=pltpu.VMEM)] * len(shapes),
        scratch_shapes=[pltpu.VMEM(member.shape, member.dtype) for member in operands]
        + [pltpu.SemaphoreType.DMA((len(operands),))],
        compiler_params=pltpu.CompilerParams(vmem_limit_bytes=32 * 1024 * 1024),
    )(*operands)


def norm_forward(value, gain, shift):
    centred = value - jnp.mean(value, -1, keepdims=True)
    inverse = lax.rsqrt(jnp.mean(centred * centred, -1, keepdims=True) + EPSILON)
    normed = centred * inverse
    return (normed * gain + shift, normed, inverse)


def norm_backward(grad_out, normed, inverse, gain):
    scaled = grad_out * gain
    back = inverse * (
        scaled
        - jnp.mean(scaled, -1, keepdims=True)
        - normed * jnp.mean(scaled * normed, -1, keepdims=True)
    )
    return (back, jnp.sum(grad_out * normed, 0), jnp.sum(grad_out, 0))


def mm(left, right, sides):
    return lax.dot_general(left, right, ((sides[:1], sides[1:]), ((), ())), preferred_element_type=F32)


def attend(qkv, allowed):
    by_head = qkv.reshape(qkv.shape[0], 3, HEADS, HEAD_DIM)
    query, key, value = by_head[:, 0], by_head[:, 1], by_head[:, 2]
    scores = jnp.einsum("qhe,khe->hqk", query, key, preferred_element_type=F32) * 0.125
    scores = jnp.where(allowed[None], scores, -1e30)
    highest = jnp.max(scores, -1, keepdims=True)
    raised = jnp.exp(scores - highest)
    summed = jnp.sum(raised, -1, keepdims=True)
    shares = (raised / summed).astype(BF16)
    mixture = jnp.einsum("hqk,khe->qhe", shares, value, preferred_element_type=F32)
    return mixture.astype(BF16).reshape(qkv.shape[0], D), highest + jnp.log(summed)


def attend_back(qkv, allowed, log_total, grad_mix):
    by_head = qkv.reshape(qkv.shape[0], 3, HEADS, HEAD_DIM)
    query, key, value = by_head[:, 0], by_head[:, 1], by_head[:, 2]
    grad_mix = grad_mix.reshape(qkv.shape[0], HEADS, HEAD_DIM)
    scores = jnp.einsum("qhe,khe->hqk", query, key, preferred_element_type=F32) * 0.125
    scores = jnp.where(allowed[None], scores, -1e30)
    shares = jnp.exp(scores - log_total)
    grad_share = jnp.einsum("qhe,khe->hqk", grad_mix, value, preferred_element_type=F32)
    grad_score = (shares * (grad_share - jnp.sum(shares * grad_share, -1, keepdims=True))).astype(BF16)
    grad_query = jnp.einsum("hqk,khe->qhe", grad_score, key, preferred_element_type=F32) * 0.125
    grad_key = jnp.einsum("hqk,qhe->khe", grad_score, query, preferred_element_type=F32) * 0.125
    grad_value = jnp.einsum("hqk,qhe->khe", shares.astype(BF16), grad_mix, preferred_element_type=F32)
    return jnp.stack((grad_query, grad_key, grad_value), 1).astype(BF16).reshape(qkv.shape)


def on_device(
    whole_mesh,
    long_ids,
    long_targets,
    long_mask,
    long_lengths,
    short_ids,
    short_targets,
    short_mask,
    short_lengths,
    table,
    position,
    qkv_weight,
    out_weight,
    in_weight,
    down_weight,
    norms,
    table_rows,
    table_cols,
    position_rows,
    position_cols,
    qkv_rows,
    qkv_cols,
    out_rows,
    out_cols,
    in_rows,
    in_cols,
    down_rows,
    down_cols,
    norm_moment,
):
    devices = lax.axis_size(("dp", "seq"))
    fast = whole_mesh == (8, 4)
    seq_index = lax.axis_index("seq")
    held = norms.shape[0]

    span = long_ids.shape[1]
    long_place = seq_index * span + lax.iota(jnp.int32, span)
    long_keep = (long_place[None, :] < long_lengths[:, None]).astype(jnp.int32)
    short_keep = (lax.iota(jnp.int32, SPAN)[None, :] < short_lengths[:, None]).astype(jnp.int32)
    long_pack = jnp.stack((long_ids, long_targets, long_mask * long_keep, long_keep), 1)
    short_pack = jnp.stack((short_ids, short_targets, short_mask * short_keep, short_keep), 1)
    moved = lax.all_to_all(
        jnp.concatenate((long_pack, short_pack[1:]), 0), "seq", split_axis=0, concat_axis=0, tiled=True
    )
    tokens = jnp.concatenate((moved, short_pack[:1]), 0)
    ids, targets, weight, keep = (tokens[:, i].reshape(-1) for i in range(4))
    weight = weight.astype(F32)
    count = tokens.shape[0] * span
    last = count - span
    alone = seq_index == lax.axis_size("seq") - 1
    token = lax.iota(jnp.int32, count)
    place = jnp.where(alone | (token >= last), token % span, token)
    row = jnp.where(alone | (token >= last), token // span, 0)
    allowed_long = (row[:last, None] == row[None, :last]) & (keep[None, :last] > 0)
    allowed_short = jnp.broadcast_to(keep[None, last:] > 0, (span, span))

    here_count = jnp.sum(long_pack[:, 2]) + jnp.sum(short_pack[:, 2])
    tall = table.T
    counts = jnp.broadcast_to(jnp.stack((here_count // 256, here_count % 256)).astype(F32)[None], (held, 2))
    wide_shard = jnp.concatenate(
        (tall, norms, counts, jnp.zeros((held, PLACE_AT - COUNT_AT - 2), F32), position.T), 1
    )
    shards = (wide_shard, qkv_weight, out_weight, in_weight, down_weight)
    if fast:
        wide_w, qkv_w, out_w, in_w, down_w, weight_sq = gather_weights(shards)
    else:
        wide_w, qkv_w, out_w, in_w, down_w = (
            lax.all_gather(shard.astype(BF16), ("dp", "seq"), axis=0, tiled=True) for shard in shards
        )
    if fast:
        zero = jnp.zeros_like(ids)
        cols = jnp.stack((ids, place + PLACE_AT, targets, weight.astype(jnp.int32), row) + (zero,) * 3, 1)
        keys = jnp.stack((keep, row) + (zero,) * 6, 0)
        found = forward((wide_w, qkv_w, out_w, in_w, down_w), cols, keys)
        loss_part, mask_count, gains, norm_c, side = found[0:5]
        loss_part, mask_count = loss_part[0, 0], mask_count[0, 0]
        x_t, mix_t, a_t, act_t, y_t, grad_logit, slope, qkv_b, normed_a, normed_b, grad_second = found[5:]
        norm_ab, ge_t, grad_ffn, grad_hidden, grad_attn, grad_qkv = backward(
            (qkv_w, out_w, in_w, down_w), slope, qkv_b, normed_a, normed_b, grad_second, cols, keys, side, gains
        )
        row = lambda vector: vector.reshape(1, -1)
        lane_olds = (table_rows, position_rows, qkv_cols, out_cols, in_cols, down_cols)
        side_olds = (table_cols, position_cols, qkv_rows, out_rows, in_rows, down_rows)
        olds = tuple(row(member) for member in lane_olds + side_olds) + (norm_moment.T,)
        reduced = reduce_grads(
            (y_t, ge_t, grad_logit, x_t, grad_qkv, mix_t, grad_attn, a_t, grad_hidden, act_t, grad_ffn),
            (cols, norm_ab, norm_c, loss_part.reshape(1, 1), weight_sq) + olds,
        )
        found = update_weights(
            tuple(reduced)
            + (tall, position.T, qkv_weight, out_weight, in_weight, down_weight, norms.T)
            + olds
        )
        grads = (None,) + tuple(found[24:28])
        loss_sum, table_g, place_g, norm_g = found[0:4]
        lane_news = [member.reshape(-1) for member in found[4:10]]
        side_news = [member.reshape(-1) for member in found[10:16]]
        moment_new, norm_new = found[16], found[23]
        news = found[17:23]
        return (
            loss_sum.reshape(()),
            mask_count,
            table_g.T,
            place_g.T,
            grads[1],
            grads[2],
            grads[3],
            grads[4],
            norm_g.T,
            lane_news[0],
            side_news[0],
            lane_news[1],
            side_news[1],
            side_news[2],
            lane_news[2],
            side_news[3],
            lane_news[3],
            side_news[4],
            lane_news[4],
            side_news[5],
            lane_news[5],
            moment_new.T,
            news[0].T,
            news[1].T,
            news[2],
            news[3],
            news[4],
            news[5],
            norm_new.T,
        )
    column = lax.broadcasted_iota(jnp.int32, (1, WIDE), 1)
    chosen = ((ids[:, None] == column) | ((place[:, None] + PLACE_AT) == column)).astype(BF16)
    gains = wide_w[:, NORM_AT : NORM_AT + 6].astype(F32)
    sums = jnp.sum(wide_w[:, COUNT_AT : COUNT_AT + 2].astype(F32), 0)
    mask_count = (sums[0] * 256.0 + sums[1]) / held
    inverse_count = 1.0 / mask_count

    embedded = mm(chosen, wide_w, (1, 1))
    first, normed_a, inverse_a = norm_forward(embedded, gains[:, 0], gains[:, 1])
    first_b = first.astype(BF16)
    qkv_b = mm(first_b, qkv_w, (1, 0)).astype(BF16)
    mix_long, total_long = attend(qkv_b[:last], allowed_long)
    mix_short, total_short = attend(qkv_b[last:], allowed_short)
    mixture = jnp.concatenate((mix_long, mix_short), 0)
    second, normed_b, inverse_b = norm_forward(first + mm(mixture, out_w, (1, 0)), gains[:, 2], gains[:, 3])
    second_b = second.astype(BF16)
    hidden = mm(second_b, in_w, (1, 0))
    active, slope = gelu_pair(hidden)
    active_b = active.astype(BF16)
    third, normed_c, inverse_c = norm_forward(second + mm(active_b, down_w, (1, 0)), gains[:, 4], gains[:, 5])
    third_b = third.astype(BF16)
    logits = jnp.where(column < VOCAB, mm(third_b, wide_w, (1, 0)), -1e30)
    highest = jnp.max(logits, -1, keepdims=True)
    log_sum = highest + jnp.log(jnp.sum(jnp.exp(logits - highest), -1, keepdims=True))
    onehot = targets[:, None] == column
    picked = jnp.sum(jnp.where(onehot, logits, 0.0), -1)
    loss_part = jnp.sum(weight * (log_sum[:, 0] - picked))
    grad_logit = (
        (jnp.exp(logits - log_sum) - onehot.astype(F32)) * (weight * inverse_count)[:, None]
    ).astype(BF16)
    grad_third = mm(grad_logit, wide_w, (1, 1))
    grad_second, gain_c, shift_c = norm_backward(grad_third, normed_c, inverse_c, gains[:, 4])
    grad_ffn = grad_second.astype(BF16)
    down_grad = mm(active_b, grad_ffn, (0, 0)).astype(BF16)
    grad_hidden = (mm(grad_ffn, down_w, (1, 1)) * slope).astype(BF16)
    in_grad = mm(second_b, grad_hidden, (0, 0)).astype(BF16)
    grad_second = grad_second + mm(grad_hidden, in_w, (1, 1))
    grad_first, gain_b, shift_b = norm_backward(grad_second, normed_b, inverse_b, gains[:, 2])
    grad_attn = grad_first.astype(BF16)
    out_grad = mm(mixture, grad_attn, (0, 0)).astype(BF16)
    grad_mix = mm(grad_attn, out_w, (1, 1)).astype(BF16)
    grad_qkv = jnp.concatenate(
        (
            attend_back(qkv_b[:last], allowed_long, total_long, grad_mix[:last]),
            attend_back(qkv_b[last:], allowed_short, total_short, grad_mix[last:]),
        ),
        0,
    )
    qkv_grad = mm(first_b, grad_qkv, (0, 0)).astype(BF16)
    grad_first = grad_first + mm(grad_qkv, qkv_w, (1, 1))
    grad_embed, gain_a, shift_a = norm_backward(grad_first, normed_a, inverse_a, gains[:, 0])
    wide_grad = mm(
        jnp.concatenate((third_b, grad_embed.astype(BF16)), 0),
        jnp.concatenate((grad_logit, chosen), 0),
        (0, 0),
    )
    norm_part = jnp.stack((gain_a, shift_a, gain_b, shift_b, gain_c, shift_c), 1)
    wide_grad = lax.dynamic_update_slice(wide_grad.astype(BF16), norm_part.astype(BF16), (0, NORM_AT))
    grads = (wide_grad, qkv_grad, out_grad, in_grad, down_grad)
    wide_g, qkv_g, out_g, in_g, down_g = (
        lax.psum_scatter(grad.astype(F32), ("dp", "seq"), scatter_dimension=0, tiled=True) for grad in grads
    )
    table_g, place_g = wide_g[:, :VOCAB], wide_g[:, PLACE_AT:]
    norm_g = wide_g[:, NORM_AT : NORM_AT + 6]

    decay = 1.0 - STEP ** (-0.8)
    matrices = (
        (qkv_weight, qkv_g, qkv_rows, qkv_cols),
        (out_weight, out_g, out_rows, out_cols),
        (in_weight, in_g, in_rows, in_cols),
        (down_weight, down_g, down_rows, down_cols),
    )
    wide = (
        (tall, table_g, table_cols, table_rows),
        (position.T, place_g, position_cols, position_rows),
    )
    row_news = [
        decay * member[2] + (1.0 - decay) * jnp.mean(member[1] * member[1] + SQUARE_FLOOR, 1)
        for member in matrices + wide
    ]
    col_parts = [jnp.sum(member[1] * member[1] + SQUARE_FLOOR, 0) for member in matrices + wide]
    row_totals = jnp.stack([jnp.sum(rows_new) for rows_new in row_news])
    weight_sq = jnp.stack([jnp.sum(member[0] * member[0]) for member in matrices + wide])
    stats = lax.psum(
        col_parts + [row_totals, weight_sq, jnp.sum(norms * norms, 0), loss_part.reshape(1)], ("dp", "seq")
    )
    updates = []
    cols_out = []
    for index, member in enumerate(matrices + wide):
        full_rows = member[0].shape[0] * devices
        cols_new = decay * member[3] + (1.0 - decay) * stats[index] / full_rows
        if index < 4:
            mean = stats[6][index] / full_rows
        else:
            mean = jnp.mean(cols_new)
        updates.append(member[1] * lax.rsqrt(row_news[index][:, None] * cols_new[None, :] / mean))
        cols_out.append(cols_new)
    moment_new = decay * norm_moment + (1.0 - decay) * (norm_g * norm_g + SQUARE_FLOOR)
    norm_update = norm_g * lax.rsqrt(moment_new)
    update_sq = jnp.stack([jnp.sum(update * update) for update in updates])
    totals = lax.psum((update_sq, jnp.sum(norm_update * norm_update, 0)), ("dp", "seq"))
    news = []
    for index, member in enumerate(matrices + wide):
        entries = member[0].shape[0] * member[0].shape[1] * devices
        clip = jnp.maximum(1.0, jnp.sqrt(totals[0][index] / entries))
        news.append(
            member[0] - learn_rate * jnp.sqrt(stats[7][index] / entries) * updates[index] / clip
        )
    norm_rows = norms.shape[0] * devices
    norm_clip = jnp.maximum(1.0, jnp.sqrt(totals[1] / norm_rows))
    norm_new = norms - learn_rate * jnp.sqrt(stats[8] / norm_rows) * norm_update / norm_clip
    return (
        stats[9][0],
        mask_count,
        table_g.T,
        place_g.T,
        qkv_g,
        out_g,
        in_g,
        down_g,
        norm_g,
        cols_out[4],
        row_news[4],
        cols_out[5],
        row_news[5],
        row_news[0],
        cols_out[0],
        row_news[1],
        cols_out[1],
        row_news[2],
        cols_out[2],
        row_news[3],
        cols_out[3],
        moment_new,
        news[4].T,
        news[5].T,
        news[0],
        news[1],
        news[2],
        news[3],
        norm_new,
    )


def solution(mesh):
    split, wide = P(("dp", "seq"), None), P(None, ("dp", "seq"))
    shard, same = P(("dp", "seq")), P()
    return jax.shard_map(
        functools.partial(on_device, (mesh.shape["dp"], mesh.shape["seq"])),
        mesh=mesh,
        in_specs=(P("dp", "seq"),) * 3
        + (P("dp"),)
        + (split,) * 3
        + (shard,)
        + (wide,) * 2
        + (split,) * 5
        + (same, shard) * 2
        + (shard, same) * 4
        + (split,),
        out_specs=(same, same)
        + (wide,) * 2
        + (split,) * 5
        + (same, shard) * 2
        + (shard, same) * 4
        + (split,)
        + (wide,) * 2
        + (split,) * 5,
        check_vma=False,
    )
```

```python
import functools

import jax
import jax.numpy as jnp
from jax import lax
from jax.experimental import pallas as pl
from jax.experimental.pallas import tpu as pltpu
from jax.sharding import PartitionSpec as P

D = 768
HEADS = 12
HEAD_DIM = 64
VOCAB = 4101
STEP = 10
SPAN = 128

EPSILON = 1e-12
SQUARE_FLOOR = 1e-30
learn_rate = 0.3

MESH = pl.DeviceIdType.MESH
F32 = jnp.float32
BF16 = jnp.bfloat16

NORM_AT = VOCAB
COUNT_AT = VOCAB + 6
TABLE_END = 4352
PLACE_AT = 4608
WIDE = PLACE_AT + 512

SHAPES = ((24, WIDE), (24, 3 * D), (24, D), (24, 4 * D), (96, D))
E_, Q_, O_, I_, D_ = range(5)
CLASS_A, CLASS_B, CLASS_C = (E_, O_), (Q_, D_), (I_,)
UP, DOWN, XWAY, YWAY, SIDE = range(5)


def here():
    dp, seq = lax.axis_index("dp"), lax.axis_index("seq")
    return dp // 2, dp % 2, seq // 2, seq % 2


def device(z, y, x, c):
    return {"dp": z * 2 + y, "seq": x * 2 + c}


def chip(z, y, x):
    return z * 4 + y * 2 + x


def all_peers():
    z, y, x, c = here()
    return (
        device(z + 1, y, x, c),
        device(z - 1, y, x, c),
        device(z, y, 1 - x, c),
        device(z, 1 - y, x, c),
        device(z, y, x, 1 - c),
    )


SUM_AT = (0, WIDE, WIDE + 3 * D, WIDE + 4 * D, WIDE + 8 * D, WIDE + 9 * D)
SUMS = WIDE + 9 * D + 256


def lanes_of(members):
    lane = lax.broadcasted_iota(jnp.int32, (1, 128), 1)
    row = jnp.zeros((1, 128), F32)
    for index, member in enumerate(members):
        row = jnp.where(lane == index, member, row)
    return row


def lane_at(row, index):
    lane = lax.broadcasted_iota(jnp.int32, row.shape, 1)
    return jnp.sum(jnp.where(lane == index, row, 0.0), 1, keepdims=True)


def column_of(row):
    size = row.shape[1]
    diagonal = lax.broadcasted_iota(jnp.int32, (size, size), 0) == lax.broadcasted_iota(
        jnp.int32, (size, size), 1
    )
    return jnp.sum(jnp.where(diagonal, row, 0.0), 1, keepdims=True)


def row_of(column):
    size = column.shape[0]
    diagonal = lax.broadcasted_iota(jnp.int32, (size, size), 0) == lax.broadcasted_iota(
        jnp.int32, (size, size), 1
    )
    return jnp.sum(jnp.where(diagonal, column, 0.0), 0, keepdims=True)


def total_sum(array):
    return jnp.sum(jnp.sum(array, 1, keepdims=True), 0, keepdims=True)


def sum_everywhere(value, first, second, third, sems):
    z, y, x, c = here()
    spot = y * 2 + x
    side_send, side_recv, plane_send, plane_recv, z_send, z_recv = sems

    def copy(src, dst, send, recv, peer):
        return pltpu.make_async_remote_copy(
            src_ref=src, dst_ref=dst, send_sem=send, recv_sem=recv, device_id=peer, device_id_type=MESH
        )

    first[0] = value
    swap = copy(first.at[0], first.at[1], side_send, side_recv, device(z, y, x, 1 - c))
    swap.start()
    swap.wait_recv()
    second[spot] = first[0] + first[1]
    plane = []
    for i, (to_y, to_x) in enumerate(((y, 1 - x), (1 - y, x), (1 - y, 1 - x))):
        plane.append(
            copy(second.at[spot], second.at[spot], plane_send.at[i], plane_recv.at[i], device(z, to_y, to_x, c))
        )
        plane[i].start()
    for member in plane:
        member.wait_recv()
    third[z] = (second[0] + second[1]) + (second[2] + second[3])
    column = []
    for i in range(3):
        to_z = (z + 1 + i) % 4
        column.append(copy(third.at[z], third.at[z], z_send.at[i], z_recv.at[i], device(to_z, y, x, c)))
        column[i].start()
    for member in column:
        member.wait_recv()
    for member in [swap] + plane + column:
        member.wait_send()
    return (third[0] + third[1]) + (third[2] + third[3])


def gelu_pair(hidden):
    normal_cdf = 0.5 * (1.0 + lax.erf(hidden * 0.7071067811865476))
    return (
        hidden * normal_cdf,
        normal_cdf + hidden * jnp.exp(-0.5 * hidden * hidden) * 0.3989422804014327,
    )


def dot_nn(left, right):
    return jnp.dot(left, right, preferred_element_type=F32)


def dot_nt(left, right):
    return lax.dot_general(left, right, (((1,), (1,)), ((), ())), preferred_element_type=F32)


def dot_tn(left, right):
    return lax.dot_general(left, right, (((0,), (0,)), ((), ())), preferred_element_type=F32)


def at(index, size):
    return pl.ds(pl.multiple_of(index * size, size), size)


def each(count, body):
    def step(index, carry):
        body(index)
        return carry

    lax.fori_loop(0, count, step, 0)


ROWS = 128
TILE = 256
HALF = 320
TABLE_TILES = TABLE_END // TILE


def head_lanes(first):
    lane = lax.broadcasted_iota(jnp.int32, (1, 128), 1)
    return (lane < HEAD_DIM) if first else (lane >= HEAD_DIM)


def layer_norm(value, gain, shift):
    centred = value - jnp.sum(value, 1, keepdims=True) / D
    inverse = lax.rsqrt(jnp.sum(centred * centred, 1, keepdims=True) / D + EPSILON)
    normed = centred * inverse
    return normed * gain + shift, normed, inverse


def layer_norm_back(grad, normed, inverse, gain):
    scaled = grad * gain
    return inverse * (
        scaled - jnp.sum(scaled, 1, keepdims=True) / D - normed * (jnp.sum(scaled * normed, 1, keepdims=True) / D)
    )


def put_lane(ref, rows, index, value):
    lane = lax.broadcasted_iota(jnp.int32, (1, 128), 1)
    ref[rows, :] = jnp.where(lane == index, value, ref[rows, :])


def set_bias(bias, cols, keys, last):
    same = cols[0:last, 4:5] == keys[1:2, 0:last]
    bias[...] = jnp.where(same & (keys[0:1, 0:last] > 0), 0.0, -1e30)


CHOOSE, EMBED, NORM_A, PROJECT, TURN_X, ATTEND, OUT, NORM_B, FEED_IN, TURN_A, FEED_OUT, REST = range(12)
FRONT = (
    68, 36, 35, 34, 67, 131, 4, 64, 37, 65, 3, 33, 40, 66, 71, 162, 70, 41, 2, 38,
    72, 165, 96, 75, 8, 5, 69, 32, 39, 1, 160, 0, 46, 169, 13, 14, 74, 73, 44, 42,
    82, 161, 9, 49, 78, 80, 130, 43, 76, 77, 6, 167, 50, 83, 48, 45, 47, 81, 166, 98,
    174, 51, 164, 79, 97, 7, 1000, 178, 170, 128, 129, 172, 101, 1016, 16, 1017, 10, 12, 100, 1018,
    11, 163, 15, 1001, 102, 1019, 17, 1020, 99, 18, 103, 19, 1021, 136, 1032, 105, 1048, 177, 168, 132,
    171, 176, 1049, 110, 1050, 1051, 112, 106, 1052, 104, 1053, 1054, 133, 1055, 1056, 1064, 1080, 107, 179, 135,
    1081, 1082, 173, 114, 134, 175, 1083, 109, 1084, 1085, 1096, 113, 1097, 137, 1098, 108, 111, 146, 115, 1112,
    142, 140, 139, 144, 141, 1128, 1129, 1130, 1131, 138, 1132, 1133, 143, 1134, 1135, 1136, 1137, 1138, 145, 147,
    1139, 1144, 1160, 1161, 1162, 1176,
)


def front_hooks():
    hooks, before = {}, []
    for task in FRONT:
        if task < 1000:
            before.append(task)
        else:
            hooks[((task - 1000) // 16, (task - 1000) % 16)] = before
            before = []
    return hooks


def front_kernel(*refs):
    raw, (long_len, short_len) = refs[0:13], refs[13:15]
    loss_out, count_out, gains_out, norm_out, side, cols, keys, squares = refs[15:23]
    x_t, mix_t, a_t, act_t, y_t, glog_out, slope_out, qkv_out, na_out, nb_out, grad_out = refs[23:34]
    weight_outs = refs[34:38]
    wide, qkv_w, out_w, in_w, down_w = weights = refs[38:43]
    value, na, nb, low_a, mix, qkv, act, slope, logits, pick, bias, turned, act_turned = refs[43:56]
    held, wide_shard, merge, pieces, land = refs[56:69], refs[69], refs[70:75], refs[75], refs[76]
    raw_sem, swap_send, swap_recv, token_send, token_recv, send_sem, link_recv, side_recv = refs[77:85]
    out_sem, turn_sem, act_sem = refs[85:88]
    z, y, x, c = here()
    peers = all_peers()
    me = chip(z, y, x)
    seq = x * 2 + c
    alone = seq // 3
    tokens = value.shape[0]
    last = tokens - SPAN
    hooks = front_hooks()

    barrier = pltpu.get_barrier_semaphore()
    cross = device(z, y, 1 - x, 1 - c)
    column = [device((z + 1 + i) % 4, y, x, c) for i in range(3)]
    for peer in [peers[XWAY], peers[YWAY], peers[SIDE], cross] + column:
        pl.semaphore_signal(barrier, inc=1, device_id=peer, device_id_type=MESH)
    raws = [pltpu.make_async_copy(raw[i], held[i], raw_sem.at[i]) for i in range(13)]
    for member in raws:
        member.start()
    for member in raws:
        member.wait()
    long_ids, long_targets, long_mask, short_ids, short_targets, short_mask, tall, place, qkv_s, out_s, in_s, down_s, norms = held

    pieces[...] = jnp.zeros(pieces.shape, jnp.int32)
    land[4] = jnp.zeros((8, SPAN), jnp.int32)
    lane = lax.broadcasted_iota(jnp.int32, (1, SPAN), 1)
    count = jnp.zeros((1, SPAN), jnp.int32)
    for t in range(5):
        if t < 3:
            ids, targets, mask = long_ids[t : t + 1, :], long_targets[t : t + 1, :], long_mask[t : t + 1, :]
            keep = (lane + seq * SPAN < long_len[t]).astype(jnp.int32)
        else:
            row = (1, 0)[t - 3]
            ids, targets, mask = (member[row : row + 1, :] for member in (short_ids, short_targets, short_mask))
            keep = (lane < short_len[row]).astype(jnp.int32)
        target = pieces.at[t] if t < 4 else land.at[4]
        target[0:1, :] = ids
        target[2:3, :] = targets
        target[3:4, :] = mask * keep
        target[5:6, :] = keep
        count = count + mask * keep
    count = jnp.sum(count.astype(F32), 1, keepdims=True)
    high = jnp.floor(count * (1.0 / 256.0))

    wide_shard[:, 0:4096] = tall[:, 0:4096]
    edge = jnp.zeros((24, 128), F32)
    tile_lane = lax.broadcasted_iota(jnp.int32, (24, 128), 1)
    tall_edge = tall[:, 4096:VOCAB]
    members = [lane_at(tall_edge, i) for i in range(VOCAB - 4096)]
    members += [column_of(norms[i : i + 1, :]) for i in range(6)]
    members += [high, count - high * 256.0]
    for i, member in enumerate(members):
        edge = jnp.where(tile_lane == i, member, edge)
    wide_shard[:, 4096:4224] = edge
    wide_shard[:, 4224:PLACE_AT] = jnp.zeros((24, PLACE_AT - 4224), F32)
    wide_shard[:, PLACE_AT:] = place[...]
    shards = (wide_shard, qkv_s, out_s, in_s, down_s)

    pl.semaphore_wait(barrier, 7)
    swaps = []
    for m in (E_, Q_, I_, D_, O_):
        size, half = SHAPES[m][0], SHAPES[m][1] // 2
        swaps.append(
            pltpu.make_async_remote_copy(
                src_ref=shards[m].at[:, pl.ds(pl.multiple_of((1 - c) * half, 128), half)],
                dst_ref=merge[m].at[pl.ds(pl.multiple_of(c * size, 8), size), :],
                send_sem=swap_send.at[m],
                recv_sem=swap_recv.at[m],
                device_id=peers[SIDE],
                device_id_type=MESH,
            )
        )
        swaps[-1].start()
    token_copies = []
    for i, (to_x, to_c) in enumerate(((x, 1 - c), (1 - x, c), (1 - x, 1 - c))):
        token_copies.append(
            pltpu.make_async_remote_copy(
                src_ref=pieces.at[to_x * 2 + to_c],
                dst_ref=land.at[seq],
                send_sem=token_send.at[i],
                recv_sem=token_recv.at[i],
                device_id=device(z, y, to_x, to_c),
                device_id_type=MESH,
            )
        )
        token_copies[-1].start()
    land[seq] = pieces[seq]

    def part(piece, k, half):
        m, skip, wide_part = PIECES[piece]
        size = 2 * SHAPES[m][0]
        start = pl.multiple_of(half * (SHAPES[m][1] // 2) + skip, 128)
        return weights[m].at[pl.ds(pl.multiple_of(k * size, size), size), pl.ds(start, wide_part)]

    FIRST_WAY, SECOND_WAY, SIDE_WAY = 0, 1, 2

    def copy_of(piece, k, way):
        ways = (XWAY, YWAY) if piece in Y_FIRST else (YWAY, XWAY)
        peer = column[way - 3] if way > 2 else peers[SIDE] if way == SIDE_WAY else peers[ways[way]]
        return pltpu.make_async_remote_copy(
            src_ref=part(piece, k, c),
            dst_ref=part(piece, k, c),
            send_sem=send_sem.at[piece, k, way],
            recv_sem=(side_recv if way == SIDE_WAY else link_recv).at[piece, k],
            device_id=peer,
            device_id_type=MESH,
        )

    def block_of(number):
        piece, task = number // 32, number % 32
        last_y = piece in Y_FIRST
        if task < 5:
            return piece, me, (3 + task if task < 3 else FIRST_WAY if task == 3 else SECOND_WAY,), False
        if task < 8:
            return piece, chip((z + task - 4) % 4, y, x), (FIRST_WAY, SECOND_WAY, SIDE_WAY), True
        if task < 12:
            t = (z + task - 8) % 4
            return piece, chip(t, y, 1 - x) if last_y else chip(t, 1 - y, x), (SECOND_WAY, SIDE_WAY), True
        t, other = (z + (task - 12) // 2) % 4, (task - 12) % 2
        if last_y:
            return piece, chip(t, 1 - y, 1 - x if other else x), (SIDE_WAY,), True
        return piece, chip(t, 1 - y if other else y, 1 - x), (SIDE_WAY,), True

    def transfer(number):
        piece, k, ways, waits = block_of(number)
        if waits:
            copy_of(piece, k, FIRST_WAY).wait_recv()
        for way in ways:
            copy_of(piece, k, way).start()

    def before(step, index, base=0):
        for (name, part_index), tasks in hooks.items():
            part_index = part_index - base
            if name != step or not tasks or (step == EMBED and not 0 <= part_index < 3):
                continue
            if index is None or isinstance(index, int):
                if part_index == (index or 0):
                    for number in tasks:
                        transfer(number)
            else:

                @pl.when(index == part_index)
                def _(tasks=tasks):
                    for number in tasks:
                        transfer(number)

    def need(*wanted):
        for piece in wanted:
            for k in range(16):
                pltpu.make_async_remote_copy(
                    src_ref=part(piece, k, 1 - c),
                    dst_ref=part(piece, k, 1 - c),
                    send_sem=send_sem.at[piece, k, SIDE_WAY],
                    recv_sem=side_recv.at[piece, k],
                    device_id=peers[SIDE],
                    device_id_type=MESH,
                ).wait_recv()

    for number, m in enumerate((E_, Q_, I_, D_, O_)):
        swaps[number].wait_recv()
        size, half = SHAPES[m][0], SHAPES[m][1] // 2
        merge[m][pl.ds(pl.multiple_of(c * size, 8), size), :] = shards[m][:, pl.ds(pl.multiple_of(c * half, 128), half)]
        rows = pl.ds(pl.multiple_of(me * 2 * size, 2 * size), 2 * size)
        weights[m][rows, pl.ds(pl.multiple_of(c * half, 128), half)] = merge[m][...].astype(BF16)
        for piece in range(6):
            if PIECES[piece][0] == m:
                copy_of(piece, me, SIDE_WAY).start()
    for copy in token_copies:
        copy.wait_recv()
    side[...] = jnp.zeros(side.shape, F32)
    keys[...] = jnp.zeros(keys.shape, jnp.int32)
    zeros = jnp.zeros((1, SPAN), F32)
    for b in range(5):
        tile = land[b]
        shift = b * SPAN * (1 - alone) if b < 4 else 0
        row = b * alone if b < 4 else 0
        spot = (lane + shift + PLACE_AT).astype(F32)
        row_lane = (lane * 0 + row).astype(F32)
        ids, targets, weight = (tile[i : i + 1].astype(F32) for i in (0, 2, 3))
        stacked = jnp.concatenate((ids, spot, targets, weight, row_lane, zeros, zeros, zeros), 0)
        stacked = jnp.concatenate((stacked, jnp.zeros((120, SPAN), F32)), 0)
        cols[b * SPAN : (b + 1) * SPAN, :] = stacked.T.astype(jnp.int32)
        keys[0:1, b * SPAN : (b + 1) * SPAN] = tile[5:6]
        keys[1:2, b * SPAN : (b + 1) * SPAN] = lane * 0 + row
    set_bias(bias, cols, keys, last)
    found = [total_sum(member[...] * member[...]) for member in (tall, place, qkv_s, out_s, in_s, down_s)]
    norm_squares = jnp.sum(norms[...] * norms[...], 1, keepdims=True)
    squares[...] = lanes_of(found + [norm_squares[i : i + 1] for i in range(6)])

    turns, outs = {}, {}

    def turn_out(source, target, slot):
        if slot in turns:
            turns[slot].wait()

        def some(index):
            turned[slot, :, at(index, ROWS)] = source[at(index, ROWS), :].T

        each(tokens // ROWS, some)
        turns[slot] = pltpu.make_async_copy(turned.at[slot], target, turn_sem.at[slot])
        turns[slot].start()

    def put_out(name, source, target):
        outs[name] = pltpu.make_async_copy(source, target, out_sem.at[len(outs)])
        outs[name].start()

    for half in range(tokens // HALF):
        rows = pl.ds(half * HALF, HALF)
        before(CHOOSE, half)
        if half == 0:
            need(1, 2)

        def choose(index):
            column_lane = lax.broadcasted_iota(jnp.int32, (1, TILE), 1) + index * TILE
            hit = (cols[rows, 0:1] == column_lane) | (cols[rows, 1:2] == column_lane)
            pick[:, at(index, TILE)] = jnp.where(hit, 1.0, 0.0).astype(BF16)

        each(WIDE // TILE, choose)

        def embed(index):
            before(EMBED, index, half * 3)
            value[rows, at(index, TILE)] = dot_nt(pick[...], wide[at(index, TILE), :])

        each(D // TILE, embed)

    gains = wide[:, 4096:4224].astype(F32).T
    gains_out[...] = gains[0:16]
    counts = jnp.sum(gains[11:13], 1, keepdims=True) / 24.0
    mask_count = counts[0:1] * 256.0 + counts[1:2]
    count_out[...] = mask_count
    inverse_count = 1.0 / mask_count
    norm_rows = [gains_out[5 + i : 6 + i, :] for i in range(6)]
    before(NORM_A, None)

    def norm_a(index):
        rows = at(index, ROWS)
        found, normed, inverse = layer_norm(value[rows, :], norm_rows[0], norm_rows[1])
        value[rows, :] = found
        low_a[rows, :] = found.astype(BF16)
        na[rows, :] = normed
        put_lane(side, rows, 12, inverse)

    each(tokens // ROWS, norm_a)
    put_out("na", na, na_out)
    before(PROJECT, 0)
    need(0)

    def project(index):
        before(PROJECT, index)
        qkv[:, at(index, TILE)] = dot_nn(low_a[...], qkv_w[:, at(index, TILE)]).astype(BF16)

    hooks.pop((PROJECT, 0))
    each(3 * D // TILE, project)
    put_out("qkv", qkv, qkv_out)
    put_out("qkv_w", qkv_w, weight_outs[0])
    before(TURN_X, None)
    turn_out(low_a, x_t, 0)

    def attend_pair(pair):
        before(ATTEND, pair)
        for start, size in ((0, last), (last, SPAN)):
            rows = pl.ds(start, size)
            query = qkv[rows, at(pair, 128)]
            key = qkv[rows, pl.ds(pl.multiple_of(D + pair * 128, 128), 128)]
            val = qkv[rows, pl.ds(pl.multiple_of(2 * D + pair * 128, 128), 128)]
            mask = bias[...] if start == 0 else jnp.where(keys[0:1, last:tokens] > 0, 0.0, -1e30)
            mixed = []
            for first in (True, False):
                chosen = jnp.where(head_lanes(first), query, jnp.zeros_like(query))
                scores = dot_nt(chosen, key) * 0.125 + mask
                highest = jnp.max(scores, 1, keepdims=True)
                raised = jnp.exp(scores - highest)
                summed = jnp.sum(raised, 1, keepdims=True)
                shares = (raised * (1.0 / summed)).astype(BF16)
                mixed.append(dot_nn(shares, val))
                put_lane(side, rows, 2 * pair + (0 if first else 1), highest + jnp.log(summed))
            mix[rows, at(pair, 128)] = jnp.where(head_lanes(True), mixed[0], mixed[1]).astype(BF16)

    each(HEADS // 2, attend_pair)
    before(OUT, 0)
    hooks.pop((OUT, 0))
    need(5)

    def out_project(index):
        before(OUT, index)
        value[:, at(index, TILE)] = value[:, at(index, TILE)] + dot_nn(mix[...], out_w[:, at(index, TILE)])

    each(D // TILE, out_project)
    put_out("out_w", out_w, weight_outs[1])
    turn_out(mix, mix_t, 1)
    before(NORM_B, None)

    def norm_b(index):
        rows = at(index, ROWS)
        found, normed, inverse = layer_norm(value[rows, :], norm_rows[2], norm_rows[3])
        value[rows, :] = found
        low_a[rows, :] = found.astype(BF16)
        nb[rows, :] = normed
        put_lane(side, rows, 13, inverse)

    each(tokens // ROWS, norm_b)
    put_out("nb", nb, nb_out)
    before(FEED_IN, 0)
    hooks.pop((FEED_IN, 0))
    need(3)

    def feed_in(index):
        before(FEED_IN, index)
        hidden = dot_nn(low_a[...], in_w[:, at(index, TILE)])
        active, slant = gelu_pair(hidden)
        active = active.astype(BF16)
        act[:, at(index, TILE)] = active
        slope[:, at(index, TILE)] = slant.astype(BF16)
        slot = lax.rem(index, 2)

        def copy():
            return pltpu.make_async_copy(act_turned.at[slot], act_t.at[at(index, TILE), :], act_sem.at[slot])

        @pl.when(index >= 2)
        def _():
            copy().wait()

        act_turned[slot] = active.T
        copy().start()

    each(4 * D // TILE, feed_in)
    for slot in range(2):
        pltpu.make_async_copy(act_turned.at[slot], act_t.at[0:TILE, :], act_sem.at[slot]).wait()
    put_out("slope", slope, slope_out)
    put_out("in_w", in_w, weight_outs[2])
    before(TURN_A, None)
    turn_out(low_a, a_t, 0)
    before(FEED_OUT, 0)
    hooks.pop((FEED_OUT, 0))
    need(4)

    def feed_out(index):
        before(FEED_OUT, index)
        value[:, at(index, TILE)] = value[:, at(index, TILE)] + dot_nn(act[...], down_w[:, at(index, TILE)])

    each(D // TILE, feed_out)
    put_out("down_w", down_w, weight_outs[3])
    before(REST, None)
    outs["nb"].wait()

    def norm_c(index):
        rows = at(index, ROWS)
        found, normed, inverse = layer_norm(value[rows, :], norm_rows[4], norm_rows[5])
        low_a[rows, :] = found.astype(BF16)
        nb[rows, :] = normed
        put_lane(side, rows, 14, inverse)

    each(tokens // ROWS, norm_c)
    turn_out(low_a, y_t, 1)
    outs["na"].wait()
    loss = jnp.zeros((1, 1), F32)
    for half in range(tokens // HALF):
        rows = pl.ds(half * HALF, HALF)
        target = cols[rows, 2:3]
        weight = cols[rows, 3:4].astype(F32)

        def lanes(index):
            return lax.broadcasted_iota(jnp.int32, (1, TILE), 1) + index * TILE

        def multiply(index, highest):
            found = dot_nn(low_a[rows, :], wide[:, at(index, TILE)])
            found = jnp.where(lanes(index) < VOCAB, found, -1e30)
            logits[:, at(index, TILE)] = found
            return jnp.maximum(highest, jnp.maximum(found[:, 0:128], found[:, 128:256]))

        highest = lax.fori_loop(0, TABLE_TILES, multiply, jnp.full((HALF, 128), -1e30, F32))
        highest = jnp.max(highest, 1, keepdims=True)

        def raise_to(index, carry):
            summed, picked = carry
            found = logits[:, at(index, TILE)]
            raised = jnp.exp(found - highest)
            logits[:, at(index, TILE)] = raised
            hit = jnp.where(lanes(index) == target, found, 0.0)
            return summed + raised[:, 0:128] + raised[:, 128:256], picked + hit[:, 0:128] + hit[:, 128:256]

        zero = jnp.zeros((HALF, 128), F32)
        summed, picked = lax.fori_loop(0, TABLE_TILES, raise_to, (zero, zero))
        summed = jnp.sum(summed, 1, keepdims=True)
        picked = jnp.sum(picked, 1, keepdims=True)
        loss = loss + jnp.sum(weight * (highest + jnp.log(summed) - picked), 0, keepdims=True)
        scale = weight * inverse_count
        share = scale / summed
        if half > 0:
            outs["glog0"].wait()

        def differ(index):
            found = logits[:, at(index, TILE)] * share - jnp.where(lanes(index) == target, scale, 0.0)
            pick[:, at(index, TILE)] = found.astype(BF16)

        each(TABLE_TILES, differ)
        put_out("glog%d" % half, pick.at[:, 0:TABLE_END], glog_out.at[rows, :])

        def back(index):
            na[rows, at(index, TILE)] = dot_nt(pick[:, 0:TABLE_END], wide[at(index, TILE), 0:TABLE_END])

        each(D // TILE, back)
    loss_out[...] = loss

    def norm_c_back(index, carry):
        gain, shift = carry
        rows = at(index, ROWS)
        inverse = lane_at(side[rows, :], 14)
        found, normed = na[rows, :], nb[rows, :]
        na[rows, :] = layer_norm_back(found, normed, inverse, norm_rows[4])
        return gain + jnp.sum(found * normed, 0, keepdims=True), shift + jnp.sum(found, 0, keepdims=True)

    zero = jnp.zeros((1, D), F32)
    gain, shift = lax.fori_loop(0, tokens // ROWS, norm_c_back, (zero, zero))
    norm_out[0:1, :] = gain
    norm_out[1:2, :] = shift
    put_out("grad", na, grad_out)
    for swap in swaps:
        swap.wait_send()
    for copy in token_copies:
        copy.wait_send()
    for piece in range(6):
        copy_of(piece, me, SIDE_WAY).wait_send()
    for number in FRONT:
        if number < 1000:
            piece, k, ways, _ = block_of(number)
            for way in ways:
                copy_of(piece, k, way).wait_send()
    for name, copy in outs.items():
        if name not in ("na", "nb", "glog0"):
            copy.wait()
    for copy in turns.values():
        copy.wait()


def front(large, lengths):
    vmem, hbm = pl.BlockSpec(memory_space=pltpu.VMEM), pl.BlockSpec(memory_space=pl.ANY)
    smem = pl.BlockSpec(memory_space=pltpu.SMEM)
    shape, dma = jax.ShapeDtypeStruct, pltpu.SemaphoreType.DMA
    tokens = 5 * SPAN
    small = [shape((1, 1), F32), shape((1, 1), F32), shape((16, D), F32), shape((2, D), F32), shape((tokens, 128), F32)]
    small += [shape((tokens, 128), jnp.int32), shape((8, tokens), jnp.int32), shape((1, 128), F32)]
    out = [shape((D, tokens), BF16)] * 3 + [shape((4 * D, tokens), BF16), shape((D, tokens), BF16)]
    out += [shape((tokens, TABLE_END), BF16), shape((tokens, 4 * D), BF16), shape((tokens, 3 * D), BF16)]
    out += [shape((tokens, D), F32)] * 3
    out += [shape((32 * SHAPES[m][0], SHAPES[m][1]), BF16) for m in (Q_, O_, I_, D_)]
    return pl.pallas_call(
        front_kernel,
        out_shape=small + out,
        in_specs=[hbm] * 13 + [smem] * 2,
        out_specs=[vmem] * len(small) + [hbm] * len(out),
        scratch_shapes=[pltpu.VMEM((32 * size, wide), BF16) for size, wide in SHAPES]
        + [pltpu.VMEM((tokens, D), F32)] * 3
        + [pltpu.VMEM((tokens, D), BF16)] * 2
        + [
            pltpu.VMEM((tokens, 3 * D), BF16),
            pltpu.VMEM((tokens, 4 * D), BF16),
            pltpu.VMEM((tokens, 4 * D), BF16),
            pltpu.VMEM((HALF, TABLE_END), F32),
            pltpu.VMEM((HALF, WIDE), BF16),
            pltpu.VMEM((tokens - SPAN, tokens - SPAN), F32),
            pltpu.VMEM((2, D, tokens), BF16),
            pltpu.VMEM((2, TILE, tokens), BF16),
        ]
        + [pltpu.VMEM(member.shape, member.dtype) for member in large]
        + [pltpu.VMEM(SHAPES[E_], F32)]
        + [pltpu.VMEM((2 * size, wide // 2), F32) for size, wide in SHAPES]
        + [pltpu.VMEM((4, 8, SPAN), jnp.int32), pltpu.VMEM((5, 8, SPAN), jnp.int32)]
        + [dma((13,)), dma((5,)), dma((5,)), dma((3,)), dma((3,)), dma((6, 16, 6)), dma((6, 16)), dma((6, 16))]
        + [dma((12,)), dma((2,)), dma((2,))],
        compiler_params=pltpu.CompilerParams(
            collective_id=0, has_side_effects=True, vmem_limit_bytes=63 * 1024 * 1024
        ),
    )(*large, *lengths)


def backward_kernel(*refs):
    loaded, (cols, keys, side, gains) = refs[0:9], refs[9:13]
    norm_out, ge_t, gffn_out, gh_out, gattn_out, gqkv_out = refs[13:19]
    qkv_w, out_w, in_w, down_w, slope, qkv, na, nb, grad = refs[19:28]
    low, attn, gh, bias, turned, load_sem, out_sem = refs[28:35]
    tokens = grad.shape[0]
    last = tokens - SPAN
    held = (qkv_w, out_w, in_w, down_w, slope, qkv, na, nb, grad)
    loads = [pltpu.make_async_copy(loaded[i], held[i], load_sem.at[i]) for i in range(9)]
    order = (8, 3, 4, 2, 7, 1, 5, 0, 6)
    for i in order:
        loads[i].start()
    outs = []

    def put_out(source, target):
        copy = pltpu.make_async_copy(source, target, out_sem.at[len(outs)])
        copy.start()
        outs.append(copy)

    set_bias(bias, cols, keys, last)
    loads[8].wait()

    def round_grad(index):
        rows = at(index, ROWS)
        low[rows, :] = grad[rows, :].astype(BF16)

    each(tokens // ROWS, round_grad)
    put_out(low, gffn_out)
    loads[3].wait()
    loads[4].wait()

    def feed_out_back(index):
        found = dot_nt(low[...], down_w[at(index, TILE), :]) * slope[:, at(index, TILE)].astype(F32)
        gh[:, at(index, TILE)] = found.astype(BF16)

    each(4 * D // TILE, feed_out_back)
    put_out(gh, gh_out)
    loads[2].wait()

    def feed_in_back(index):
        grad[:, at(index, TILE)] = grad[:, at(index, TILE)] + dot_nt(gh[...], in_w[at(index, TILE), :])

    each(D // TILE, feed_in_back)
    loads[7].wait()
    outs[0].wait()
    zero = jnp.zeros((1, D), F32)

    def norm_b_back(index, carry):
        gain, shift = carry
        rows = at(index, ROWS)
        inverse = lane_at(side[rows, :], 13)
        found, normed = grad[rows, :], nb[rows, :]
        back = layer_norm_back(found, normed, inverse, gains[7:8, :])
        grad[rows, :] = back
        low[rows, :] = back.astype(BF16)
        return gain + jnp.sum(found * normed, 0, keepdims=True), shift + jnp.sum(found, 0, keepdims=True)

    gain, shift = lax.fori_loop(0, tokens // ROWS, norm_b_back, (zero, zero))
    norm_out[2:3, :] = gain
    norm_out[3:4, :] = shift
    put_out(low, gattn_out)
    loads[1].wait()

    def out_back(index):
        attn[:, at(index, TILE)] = dot_nt(low[...], out_w[at(index, TILE), :]).astype(BF16)

    each(D // TILE, out_back)
    loads[5].wait()

    def attend_pair_back(pair):
        for start, size in ((0, last), (last, SPAN)):
            rows = pl.ds(start, size)
            spots = [pl.ds(pl.multiple_of(i * D + pair * 128, 128), 128) for i in range(3)]
            query, key, val = (qkv[rows, spot] for spot in spots)
            given = attn[rows, at(pair, 128)]
            mask = bias[...] if start == 0 else jnp.where(keys[0:1, last:tokens] > 0, 0.0, -1e30)
            found = []
            for first in (True, False):
                lanes = head_lanes(first)
                chosen = jnp.where(lanes, query, jnp.zeros_like(query))
                mine = jnp.where(lanes, given, jnp.zeros_like(given))
                total = lane_at(side[rows, :], 2 * pair + (0 if first else 1))
                shares = jnp.exp(dot_nt(chosen, key) * 0.125 + mask - total)
                grad_share = dot_nt(mine, val)
                middle = jnp.sum(shares * grad_share, 1, keepdims=True)
                grad_score = (shares * (grad_share - middle)).astype(BF16)
                found.append(
                    (
                        dot_nn(grad_score, key) * 0.125,
                        dot_tn(grad_score, query) * 0.125,
                        dot_tn(shares.astype(BF16), given),
                    )
                )
            for i in range(3):
                qkv[rows, spots[i]] = jnp.where(head_lanes(True), found[0][i], found[1][i]).astype(BF16)

    each(HEADS // 2, attend_pair_back)
    put_out(qkv, gqkv_out)
    loads[0].wait()

    def project_back(index):
        grad[:, at(index, TILE)] = grad[:, at(index, TILE)] + dot_nt(qkv[...], qkv_w[at(index, TILE), :])

    each(D // TILE, project_back)
    loads[6].wait()

    def norm_a_back(index, carry):
        gain, shift = carry
        rows = at(index, ROWS)
        inverse = lane_at(side[rows, :], 12)
        found, normed = grad[rows, :], na[rows, :]
        turned[:, rows] = layer_norm_back(found, normed, inverse, gains[5:6, :]).astype(BF16).T
        return gain + jnp.sum(found * normed, 0, keepdims=True), shift + jnp.sum(found, 0, keepdims=True)

    gain, shift = lax.fori_loop(0, tokens // ROWS, norm_a_back, (zero, zero))
    norm_out[0:1, :] = gain
    norm_out[1:2, :] = shift
    put_out(turned, ge_t)
    for copy in outs[1:]:
        copy.wait()


def backward(weights, slope, qkv, na, nb, grad, cols, keys, side, gains):
    tokens = grad.shape[0]
    vmem, hbm = pl.BlockSpec(memory_space=pltpu.VMEM), pl.BlockSpec(memory_space=pl.ANY)
    shape = jax.ShapeDtypeStruct
    loaded = tuple(weights) + (slope, qkv, na, nb, grad)
    widths = (D, D, 4 * D, D, 3 * D)
    return pl.pallas_call(
        backward_kernel,
        out_shape=[shape((4, D), F32), shape((D, tokens), BF16)]
        + [shape((tokens, width), BF16) for width in (D, 4 * D, D, 3 * D)],
        in_specs=[hbm] * 9 + [vmem] * 4,
        out_specs=[vmem] + [hbm] * 5,
        scratch_shapes=[pltpu.VMEM(member.shape, member.dtype) for member in loaded]
        + [
            pltpu.VMEM((tokens, D), BF16),
            pltpu.VMEM((tokens, D), BF16),
            pltpu.VMEM((tokens, 4 * D), BF16),
            pltpu.VMEM((tokens - SPAN, tokens - SPAN), F32),
            pltpu.VMEM((D, tokens), BF16),
            pltpu.SemaphoreType.DMA((9,)),
            pltpu.SemaphoreType.DMA((5,)),
        ],
        compiler_params=pltpu.CompilerParams(vmem_limit_bytes=60 * 1024 * 1024),
    )(*loaded, cols, keys, side, gains)


LEFT = 768
PIECES = ((Q_, 0, 1152), (E_, 0, 1280), (E_, 1280, 1280), (I_, 0, 1536), (D_, 0, 384), (O_, 0, 384))
Y_FIRST = (0, 1, 4)
TASKS = (
    0, 1, 96, 9, 4, 129, 97, 2, 103, 5, 99, 7, 8, 6, 101, 128, 102, 105,
    100, 132, 133, 64, 108, 12, 104, 136, 139, 134, 65, 15, 107, 111, 109, 137, 161, 13,
    160, 3, 131, 11, 141, 142, 70, 32, 68, 112, 110, 76, 140, 16, 168, 67, 144, 72,
    169, 75, 135, 71, 33, 36, 69, 143, 166, 173, 38, 98, 39, 43, 78, 130, 167, 73,
    37, 40, 79, 44, 34, 164, 46, 66, 77, 14, 47, 165, 45, 162, 171, 41, 172, 176,
    80, 138, 174, 74, 48, 10, 106, 42, 175, 35, 81, 145, 163, 170, 113, 17, 49, 177,
)


def reduce_kernel(*refs):
    given, (cols, norm_ab, norm_c, loss, squares) = refs[0:11], refs[11:16]
    y_t, ge_t, glog, x_t, gqkv, mix_t, gattn, a_t, gh, act_t, gffn = given
    lane_olds, side_olds, moment = refs[16:22], refs[22:28], refs[28]
    outs, sums_out, totals_out = refs[29:34], refs[34], refs[35]
    own, side, first, second, column, fin = (refs[36 + 6 * i : 42 + 6 * i] for i in range(6))
    left, (glog_v, gqkv_v, gattn_v, gh_v, gffn_v), stage, tails, norm_t = refs[72:79], refs[79:84], refs[84], refs[85], refs[86]
    spread, spread_small = refs[87:90], refs[90:93]
    load_sem, ring_sem, tail_sem, side_recv, first_send, first_recv, second_send, second_recv = refs[93:101]
    z_send, z_recv, swap_send, swap_recv = refs[101:105]
    sems, small_sems = refs[105:111], refs[111:117]
    z, y, x, c = here()
    peers = all_peers()
    me = chip(z, y, x)

    barrier = pltpu.get_barrier_semaphore()
    greeted = [peers[XWAY], peers[YWAY], peers[SIDE], device(z, 1 - y, 1 - x, c)]
    greeted += [device((z + 1 + i) % 4, y, x, c) for i in range(3)]
    for peer in greeted:
        pl.semaphore_signal(barrier, inc=1, device_id=peer, device_id_type=MESH)

    def act_part(group):
        return act_t.at[pl.ds(LEFT * group, LEFT), :]

    operands = (
        ((x_t, left[1]), (gqkv, gqkv_v)),
        ((y_t, left[2]), (ge_t, left[3]), (glog, glog_v)),
        (),
        ((a_t, left[0]), (gh, gh_v)),
        ((gffn, gffn_v), (act_part(0), left[5]), (act_part(1), left[6])),
        ((mix_t, left[4]), (gattn, gattn_v)),
    )
    loads = {}
    waited = set()
    for task in TASKS:
        piece = task // 32 if task // 32 != 2 else 1
        if piece not in loads:
            loads[piece] = []
            for source, target in operands[piece]:
                number = sum(len(member) for member in loads.values())
                loads[piece].append(pltpu.make_async_copy(source, target, load_sem.at[number]))
                loads[piece][-1].start()

    def loaded(piece):
        piece = 1 if piece == 2 else piece
        if piece not in waited:
            waited.add(piece)
            for member in loads[piece]:
                member.wait()

    norm_t[...] = jnp.zeros(norm_t.shape, F32)
    norm_t[5:9, :] = norm_ab[...]
    norm_t[9:11, :] = norm_c[...]
    pl.semaphore_wait(barrier, 7)

    def size_of(piece):
        return 2 * SHAPES[PIECES[piece][0]][0]

    def slot(ref, piece, index):
        size = size_of(piece)
        return ref[piece].at[pl.ds(pl.multiple_of(index * size, size), size), :]

    def half_of(piece):
        return SHAPES[PIECES[piece][0]][1] // 2

    def chosen(start):
        lane = lax.broadcasted_iota(jnp.int32, (1, TILE), 1) + start
        hit = (cols[:, 0:1] == lane) | (cols[:, 1:2] == lane)
        return jnp.where(hit, 1.0, 0.0).astype(BF16)

    def ring_copy(piece, rows, lanes, number, index):
        place = lax.rem(number, 3)
        return pltpu.make_async_remote_copy(
            src_ref=stage.at[place],
            dst_ref=side[piece].at[rows, lanes],
            send_sem=ring_sem.at[place],
            recv_sem=side_recv.at[piece, index],
            device_id=peers[SIDE],
            device_id_type=MESH,
        )

    def tail_copy(piece, rows, lanes, number, index):
        return pltpu.make_async_remote_copy(
            src_ref=tails.at[number],
            dst_ref=side[piece].at[rows, lanes],
            send_sem=tail_sem.at[number],
            recv_sem=side_recv.at[piece, index],
            device_id=peers[SIDE],
            device_id_type=MESH,
        )

    whole = pl.ds(0, LEFT)
    ring_count, tail_count = [0], [0]

    def give(piece, rows, lanes, number, index):
        def before():
            @pl.when(number >= 3)
            def _():
                ring_copy(piece, rows, lanes, number, index).wait_send()

        def write(value):
            stage[lax.rem(number, 3)] = value.astype(BF16)

        return before, write, lambda: ring_copy(piece, rows, lanes, number, index).start()

    def keep(piece, rows, lanes):
        def write(value):
            own[piece][rows, lanes] = value.astype(BF16)

        return lambda: None, write, lambda: None

    def plain(piece, mine, source, right, group):
        wide = PIECES[piece][2]
        half = c if mine else 1 - c
        rows = pl.ds(LEFT * group, LEFT)
        base = ring_count[0]

        def step(j):
            lanes = at(j, TILE)
            before, write, after = keep(piece, rows, lanes) if mine else give(
                piece, rows, lanes, base + j, group * (wide // TILE) + j
            )
            before()
            write(dot_nn(source[...], right[:, pl.ds(pl.multiple_of(half * wide + j * TILE, 128), TILE)]))
            after()

        each(wide // TILE, step)
        if not mine:
            ring_count[0] += wide // TILE
        if wide % TILE:
            start = wide - 128
            value = dot_nn(source[...], right[:, pl.ds(pl.multiple_of(half * wide + start, 128), 128)])
            if mine:
                own[piece][rows, start:wide] = value.astype(BF16)
            else:
                number = tail_count[0]
                tail_count[0] += 1
                groups = SHAPES[PIECES[piece][0]][0] // 24
                tails[number] = value.astype(BF16)
                tail_copy(piece, rows, pl.ds(start, 128), number, groups * (wide // TILE) + group).start()

    def wide_product(piece, mine):
        half = c if mine else 1 - c
        wide = half_of(piece)
        skip = PIECES[piece][1] // TILE
        base = ring_count[0]

        def both(j):
            start = pl.multiple_of(half * wide + (skip + j) * TILE, TILE)
            return dot_nn(left[2][...], glog_v[:, pl.ds(start, TILE)]) + dot_nn(left[3][...], chosen(start))

        def target(j):
            lanes = at(j, TILE)
            return keep(piece, whole, lanes) if mine else give(piece, whole, lanes, base + j, j)

        def step(j):
            before, write, after = target(j)
            before()
            write(both(j))
            after()

        if not mine:
            ring_count[0] += 5
        if skip == 0:
            each(5, step)
            return
        each(1, step)
        before, write, after = target(1)
        before()
        norm_part = jnp.where(half == 1, norm_t[...], 0.0).T
        write(both(1) + jnp.concatenate((norm_part, jnp.zeros((LEFT, TILE - 128), F32)), 1))
        after()
        for j in range(2, 5):
            before, write, after = target(j)
            before()

            @pl.when(half == 0)
            def _():
                write(both(j))

            @pl.when(half == 1)
            def _():
                if j == 2:
                    write(jnp.zeros((LEFT, TILE), F32))
                else:
                    write(dot_nn(left[3][...], chosen(half_of(piece) + (skip + j) * TILE)))

            after()

    def products(piece, mine):
        loaded(piece)
        if piece in (1, 2):
            wide_product(piece, mine)
        elif piece == 4:
            if not mine:
                for group in range(4):
                    source = left[5 + group % 2]
                    if group >= 2:
                        loads[piece][1 + group % 2].wait()
                    plain(piece, False, source, gffn_v, group)
                    plain(piece, True, source, gffn_v, group)
                    if group < 2:
                        again = pltpu.make_async_copy(act_part(group + 2), source, load_sem.at[12 + group])
                        again.start()
                        loads[piece][1 + group] = again
        else:
            source, right = {0: (left[1], gqkv_v), 3: (left[0], gh_v), 5: (left[4], gattn_v)}[piece]
            plain(piece, mine, source, right, 0)

    def combine(piece, target, parts):
        def some(rows, lanes):
            total = parts[0][rows, lanes].astype(F32)
            for member in parts[1:]:
                total = total + member[rows, lanes].astype(F32)
            target[rows, lanes] = total.astype(target.dtype)

        wide = PIECES[piece][2]
        if piece == 4:
            each(4, lambda group: some(at(group, 48), slice(0, wide)))
            return
        if wide >= 512:
            each(wide // 512, lambda j: some(slice(0, 48), at(j, 512)))
        if wide % 512:
            some(slice(0, 48), slice(wide // 512 * 512, wide))

    def hop(piece, k, land, index, sems, way):
        return pltpu.make_async_remote_copy(
            src_ref=slot(own, piece, k),
            dst_ref=slot(land, piece, index),
            send_sem=sems[0].at[piece, index],
            recv_sem=sems[1].at[piece, index],
            device_id=peers[way],
            device_id_type=MESH,
        )

    FIRST, SECOND = (first_send, first_recv), (second_send, second_recv)

    def landed(piece, land, index, sems):
        hop(piece, me, land, index, sems, XWAY).wait_recv()

    def block(piece, a, b, far):
        return chip(far, a, b) if piece in Y_FIRST else chip(far, b, a)

    def split(piece):
        return (y, x, YWAY, XWAY) if piece in Y_FIRST else (x, y, XWAY, YWAY)

    readied = set()

    def ready(piece):
        if piece in readied:
            return
        readied.add(piece)
        wide, groups = PIECES[piece][2], SHAPES[PIECES[piece][0]][0] // 24
        for group in range(groups):
            for j in range(wide // TILE):
                ring_copy(piece, pl.ds(LEFT * group, LEFT), at(j, TILE), 0, group * (wide // TILE) + j).wait_recv()
            if wide % TILE:
                index = groups * (wide // TILE) + group
                tail_copy(piece, pl.ds(LEFT * group, LEFT), pl.ds(wide - 128, 128), 0, index).wait_recv()

    def both_cores(piece, k):
        return (slot(own, piece, k), slot(side, piece, k))

    def first_block(piece, i):
        a, b, way, _ = split(piece)
        t, v = (z + i // 2) % 4, (1 - b) if i % 2 == 0 else b
        return block(piece, 1 - a, v, t), 2 * t + v, way

    def first_send_of(piece, i):
        ready(piece)
        k, index, way = first_block(piece, i)
        combine(piece, slot(own, piece, k), both_cores(piece, k))
        hop(piece, k, first, index, FIRST, way).start()

    def second_block(piece, i):
        a, b, _, way = split(piece)
        t = (z + i) % 4
        return block(piece, a, 1 - b, t), t, way

    def second_send_of(piece, i):
        k, t, way = second_block(piece, i)
        spot = 2 * t + 1 - split(piece)[1]
        landed(piece, first, spot, FIRST)
        combine(piece, slot(own, piece, k), both_cores(piece, k) + (slot(first, piece, spot),))
        hop(piece, k, second, t, SECOND, way).start()

    def z_copy(piece, i):
        t = (z + i) % 4
        return pltpu.make_async_remote_copy(
            src_ref=slot(own, piece, chip(t, y, x)),
            dst_ref=slot(column, piece, z),
            send_sem=z_send.at[piece, t],
            recv_sem=z_recv.at[piece, z],
            device_id=device(t, y, x, c),
            device_id_type=MESH,
        )

    def z_landed(piece, i):
        t = (z + i) % 4
        pltpu.make_async_remote_copy(
            src_ref=slot(own, piece, me),
            dst_ref=slot(column, piece, t),
            send_sem=z_send.at[piece, t],
            recv_sem=z_recv.at[piece, t],
            device_id=device(t, y, x, c),
            device_id_type=MESH,
        ).wait_recv()
        return slot(column, piece, t)

    def gathered(piece, t):
        spot = 2 * t + split(piece)[1]
        landed(piece, first, spot, FIRST)
        landed(piece, second, t, SECOND)
        return both_cores(piece, chip(t, y, x)) + (slot(first, piece, spot), slot(second, piece, t))

    def z_send_of(piece, i):
        t = (z + i) % 4
        combine(piece, slot(own, piece, chip(t, y, x)), gathered(piece, t))
        z_copy(piece, i).start()

    swaps = []

    def finish(piece):
        parts = gathered(piece, z)
        parts = parts + tuple(z_landed(piece, i) for i in (1, 2, 3))
        combine(piece, fin[piece], parts)
        m, skip, wide = PIECES[piece]
        size = SHAPES[m][0]
        lanes = pl.ds(pl.multiple_of(c * half_of(piece) + skip, 128), wide)
        swaps.append(
            pltpu.make_async_remote_copy(
                src_ref=fin[piece].at[pl.ds(pl.multiple_of((1 - c) * size, 8), size), :],
                dst_ref=outs[m].at[:, lanes],
                send_sem=swap_send.at[piece],
                recv_sem=swap_recv.at[piece],
                device_id=peers[SIDE],
                device_id_type=MESH,
            )
        )
        swaps[-1].start()
        outs[m][:, lanes] = fin[piece][pl.ds(pl.multiple_of(c * size, 8), size), :]

    for task in TASKS:
        piece, number = task // 32, task % 32
        if number < 2:
            products(piece, number == 1)
        elif number < 10:
            first_send_of(piece, number - 2)
        elif number < 14:
            second_send_of(piece, number - 10)
        elif number < 17:
            z_send_of(piece, number - 13)
        else:
            finish(piece)
    for piece in range(6):
        for i in range(8):
            k, index, way = first_block(piece, i)
            hop(piece, k, first, index, FIRST, way).wait_send()
        for i in range(4):
            k, t, way = second_block(piece, i)
            hop(piece, k, second, t, SECOND, way).wait_send()
        for i in (1, 2, 3):
            z_copy(piece, i).wait_send()
    for number in range(ring_count[0] - 3, ring_count[0]):
        ring_copy(1, whole, pl.ds(0, TILE), number, 0).wait_send()
    for number in range(tail_count[0]):
        tail_copy(1, whole, pl.ds(0, 128), number, 0).wait_send()
    for swap in swaps:
        swap.wait()

    sides, lanes, _, gs = statistics(outs, lane_olds, side_olds)
    scalars = lanes_of([jnp.sum(member, 0, keepdims=True) for member in sides] + [loss[...]])
    sums = jnp.concatenate(lanes + [scalars, squares[...]], 1)
    sums = sum_everywhere(sums, *spread, sems)
    sums_out[...] = sums
    updates = updates_of(sums, gs, sides, lane_olds, moment)[0]
    totals = lanes_of(
        [total_sum(update * update) for update in updates[:6]]
        + [jnp.sum(updates[6][i : i + 1] * updates[6][i : i + 1], 1, keepdims=True) for i in range(6)]
    )
    totals_out[...] = sum_everywhere(totals, *spread_small, small_sems)


def statistics(grads, lane_olds, side_olds):
    wide_g = grads[E_][...]
    gs = (wide_g[:, :VOCAB], wide_g[:, PLACE_AT:]) + tuple(grads[m][...] for m in (Q_, O_, I_, D_))
    gs = gs + (wide_g[:, 4096:4224],)
    decay = 1.0 - STEP ** (-0.8)
    sides, lanes = [], []
    wide_square = wide_g * wide_g + SQUARE_FLOOR
    squares = [wide_square[:, :VOCAB], wide_square[:, PLACE_AT:]] + [g * g + SQUARE_FLOOR for g in gs[2:6]]
    for index in range(6):
        mean = jnp.sum(squares[index], 1, keepdims=True) / squares[index].shape[1]
        sides.append(decay * column_of(side_olds[index][...]) + (1.0 - decay) * mean)
    lanes = [jnp.sum(square, 0, keepdims=True) for square in [wide_square] + squares[2:]]
    return sides, lanes, squares, gs


def updates_of(sums, gs, sides, lane_olds, moment):
    decay = 1.0 - STEP ** (-0.8)
    fresh = 1.0 - decay
    parts = [sums[:, :VOCAB], sums[:, PLACE_AT:WIDE]]
    parts += [sums[:, SUM_AT[i] : SUM_AT[i + 1]] for i in range(1, 5)]
    scalars = sums[:, SUM_AT[5] : SUM_AT[5] + 128]
    updates, lane_news = [], []
    for index in range(6):
        height = gs[index].shape[0] * 32
        lane_news.append(decay * lane_olds[index][...] + fresh * (parts[index] / height))
        if index < 2:
            mean = jnp.sum(lane_news[index], 1, keepdims=True) / lane_news[index].shape[1]
        else:
            mean = lane_at(scalars, index) / height
        updates.append(gs[index] * lax.rsqrt(sides[index] * lane_news[index] / mean))
    norm_g = jnp.concatenate([row_of(lane_at(gs[6], NORM_AT - 4096 + i)) for i in range(6)], 0)
    moment_new = decay * moment[...] + fresh * (norm_g * norm_g + SQUARE_FLOOR)
    updates.append(norm_g * lax.rsqrt(moment_new))
    return updates, lane_news, norm_g, moment_new


def reduce_grads(large, small):
    tokens = large[2].shape[0]
    vmem, hbm = pl.BlockSpec(memory_space=pltpu.VMEM), pl.BlockSpec(memory_space=pl.ANY)
    dma = pltpu.SemaphoreType.DMA
    scratch = []
    for count in (16, 16, 8, 4, 4):
        scratch += [pltpu.VMEM((count * 2 * SHAPES[m][0], wide), BF16) for m, _, wide in PIECES]
    scratch += [pltpu.VMEM((2 * SHAPES[m][0], wide), F32) for m, _, wide in PIECES]
    scratch += [pltpu.VMEM((LEFT, tokens), BF16)] * 7
    scratch += [pltpu.VMEM((tokens, width), BF16) for width in (TABLE_END, 3 * D, D, 4 * D, D)]
    scratch += [pltpu.VMEM((3, LEFT, TILE), BF16), pltpu.VMEM((6, LEFT, 128), BF16), pltpu.VMEM((128, D), F32)]
    scratch += [pltpu.VMEM((count, 1, SUMS), F32) for count in (2, 4, 4)]
    scratch += [pltpu.VMEM((count, 1, 128), F32) for count in (2, 4, 4)]
    scratch += [dma((14,)), dma((3,)), dma((6,)), dma((6, 10)), dma((6, 8)), dma((6, 8)), dma((6, 4)), dma((6, 4))]
    scratch += [dma((6, 4)), dma((6, 4)), dma((6,)), dma((6,))]
    scratch += ([dma] * 2 + [dma((3,))] * 4) * 2
    return pl.pallas_call(
        reduce_kernel,
        out_shape=[jax.ShapeDtypeStruct(shape, F32) for shape in SHAPES + ((1, SUMS), (1, 128))],
        in_specs=[hbm] * 11 + [vmem] * len(small),
        out_specs=[vmem] * 7,
        scratch_shapes=scratch,
        compiler_params=pltpu.CompilerParams(
            collective_id=1, has_side_effects=True, vmem_limit_bytes=63 * 1024 * 1024
        ),
    )(*large, *small)


def update_kernel(*refs):
    copies = [pltpu.make_async_copy(refs[i], refs[55 + i], refs[82].at[i]) for i in range(27)]
    for copy in copies:
        copy.start()
    for copy in copies:
        copy.wait()
    refs = refs[55:82] + refs[27:55]
    grads, sums, totals, ws, norms = refs[0:5], refs[5], refs[6], refs[7:13], refs[13]
    lane_olds, side_olds, moment = refs[14:20], refs[20:26], refs[26]
    loss_out, table_g, place_g, norm_g_out = refs[27:31]
    lane_outs, side_outs, moment_out, news, norm_new = refs[31:37], refs[37:43], refs[43], refs[44:50], refs[50]
    grad_outs = refs[51:55]
    sides, _, _, gs = statistics(grads, lane_olds, side_olds)
    updates, lane_news, norm_g, moment_new = updates_of(sums[...], gs, sides, lane_olds, moment)
    scalars = sums[:, SUM_AT[5] : SUM_AT[5] + 128]
    squares = sums[:, SUM_AT[5] + 128 :]
    loss_out[...] = lane_at(scalars, 6)
    table_g[...] = gs[0]
    place_g[...] = gs[1]
    norm_g_out[...] = norm_g
    moment_out[...] = moment_new
    for index in range(6):
        lane_outs[index][...] = lane_news[index]
        side_outs[index][...] = row_of(sides[index])
        if index >= 2:
            grad_outs[index - 2][...] = gs[index]
        entries = gs[index].shape[0] * gs[index].shape[1] * 32
        clip = jnp.maximum(1.0, jnp.sqrt(lane_at(totals[...], index) / entries))
        scale = learn_rate * jnp.sqrt(lane_at(squares, index) / entries) / clip
        news[index][...] = ws[index][...] - scale * updates[index]
    for i in range(6):
        clip = jnp.maximum(1.0, jnp.sqrt(lane_at(totals[...], 6 + i) / D))
        scale = learn_rate * jnp.sqrt(lane_at(squares, 6 + i) / D) / clip
        norm_new[i : i + 1, :] = norms[i : i + 1, :] - scale * updates[6][i : i + 1, :]


def update_weights(operands):
    lanes = (VOCAB, 512, 3 * D, D, 4 * D, D)
    held = (24, 24, 24, 24, 24, 96)
    shapes = [(1, 1), (24, VOCAB), (24, 512), (6, 24)]
    shapes += [(1, lane) for lane in lanes] + [(1, size) for size in held] + [(6, 24)]
    shapes += list(zip(held, lanes)) + [(6, 24)] + list(zip(held, lanes))[2:]
    return pl.pallas_call(
        update_kernel,
        out_shape=[jax.ShapeDtypeStruct(shape, F32) for shape in shapes],
        in_specs=[pl.BlockSpec(memory_space=pl.ANY)] * len(operands),
        out_specs=[pl.BlockSpec(memory_space=pltpu.VMEM)] * len(shapes),
        scratch_shapes=[pltpu.VMEM(member.shape, member.dtype) for member in operands]
        + [pltpu.SemaphoreType.DMA((len(operands),))],
        compiler_params=pltpu.CompilerParams(vmem_limit_bytes=63 * 1024 * 1024),
    )(*operands)


def norm_forward(value, gain, shift):
    centred = value - jnp.mean(value, -1, keepdims=True)
    inverse = lax.rsqrt(jnp.mean(centred * centred, -1, keepdims=True) + EPSILON)
    normed = centred * inverse
    return (normed * gain + shift, normed, inverse)


def norm_backward(grad_out, normed, inverse, gain):
    scaled = grad_out * gain
    back = inverse * (
        scaled
        - jnp.mean(scaled, -1, keepdims=True)
        - normed * jnp.mean(scaled * normed, -1, keepdims=True)
    )
    return (back, jnp.sum(grad_out * normed, 0), jnp.sum(grad_out, 0))


def mm(left, right, sides):
    return lax.dot_general(left, right, ((sides[:1], sides[1:]), ((), ())), preferred_element_type=F32)


def attend(qkv, allowed):
    by_head = qkv.reshape(qkv.shape[0], 3, HEADS, HEAD_DIM)
    query, key, value = by_head[:, 0], by_head[:, 1], by_head[:, 2]
    scores = jnp.einsum("qhe,khe->hqk", query, key, preferred_element_type=F32) * 0.125
    scores = jnp.where(allowed[None], scores, -1e30)
    highest = jnp.max(scores, -1, keepdims=True)
    raised = jnp.exp(scores - highest)
    summed = jnp.sum(raised, -1, keepdims=True)
    shares = (raised / summed).astype(BF16)
    mixture = jnp.einsum("hqk,khe->qhe", shares, value, preferred_element_type=F32)
    return mixture.astype(BF16).reshape(qkv.shape[0], D), highest + jnp.log(summed)


def attend_back(qkv, allowed, log_total, grad_mix):
    by_head = qkv.reshape(qkv.shape[0], 3, HEADS, HEAD_DIM)
    query, key, value = by_head[:, 0], by_head[:, 1], by_head[:, 2]
    grad_mix = grad_mix.reshape(qkv.shape[0], HEADS, HEAD_DIM)
    scores = jnp.einsum("qhe,khe->hqk", query, key, preferred_element_type=F32) * 0.125
    scores = jnp.where(allowed[None], scores, -1e30)
    shares = jnp.exp(scores - log_total)
    grad_share = jnp.einsum("qhe,khe->hqk", grad_mix, value, preferred_element_type=F32)
    grad_score = (shares * (grad_share - jnp.sum(shares * grad_share, -1, keepdims=True))).astype(BF16)
    grad_query = jnp.einsum("hqk,khe->qhe", grad_score, key, preferred_element_type=F32) * 0.125
    grad_key = jnp.einsum("hqk,qhe->khe", grad_score, query, preferred_element_type=F32) * 0.125
    grad_value = jnp.einsum("hqk,qhe->khe", shares.astype(BF16), grad_mix, preferred_element_type=F32)
    return jnp.stack((grad_query, grad_key, grad_value), 1).astype(BF16).reshape(qkv.shape)


def on_slice(token_arrays, lengths, weights, lane_olds, side_olds, moment):
    row = lambda vector: vector.reshape(1, -1)
    olds = tuple(row(member) for member in lane_olds + side_olds) + (moment,)
    found = front(token_arrays + weights, lengths)
    loss_part, mask_count, gains, norm_c, side, cols, keys, weight_sq = found[0:8]
    x_t, mix_t, a_t, act_t, y_t, grad_logit, slope, qkv_b, normed_a, normed_b, grad_second = found[8:19]
    norm_ab, ge_t, grad_ffn, grad_hidden, grad_attn, grad_qkv = backward(
        found[19:23], slope, qkv_b, normed_a, normed_b, grad_second, cols, keys, side, gains
    )
    reduced = reduce_grads(
        (y_t, ge_t, grad_logit, x_t, grad_qkv, mix_t, grad_attn, a_t, grad_hidden, act_t, grad_ffn),
        (cols, norm_ab, norm_c, loss_part, weight_sq) + olds,
    )
    found = update_weights(tuple(reduced) + weights + olds)
    grads = (None,) + tuple(found[24:28])
    mask_count = mask_count.reshape(())
    loss_sum, table_g, place_g, norm_g = found[0:4]
    lane_news = [member.reshape(-1) for member in found[4:10]]
    side_news = [member.reshape(-1) for member in found[10:16]]
    moment_new, norm_new = found[16], found[23]
    news = found[17:23]
    return (
        loss_sum.reshape(()),
        mask_count,
        table_g.T,
        place_g.T,
        grads[1],
        grads[2],
        grads[3],
        grads[4],
        norm_g.T,
        lane_news[0],
        side_news[0],
        lane_news[1],
        side_news[1],
        side_news[2],
        lane_news[2],
        side_news[3],
        lane_news[3],
        side_news[4],
        lane_news[4],
        side_news[5],
        lane_news[5],
        moment_new.T,
        news[0].T,
        news[1].T,
        news[2],
        news[3],
        news[4],
        news[5],
        norm_new.T,
    )


def on_device(
    whole_mesh,
    long_ids,
    long_targets,
    long_mask,
    long_lengths,
    short_ids,
    short_targets,
    short_mask,
    short_lengths,
    table,
    position,
    qkv_weight,
    out_weight,
    in_weight,
    down_weight,
    norms,
    table_rows,
    table_cols,
    position_rows,
    position_cols,
    qkv_rows,
    qkv_cols,
    out_rows,
    out_cols,
    in_rows,
    in_cols,
    down_rows,
    down_cols,
    norm_moment,
):
    if whole_mesh == (8, 4):
        return on_slice(
            (long_ids, long_targets, long_mask, short_ids, short_targets, short_mask),
            (long_lengths, short_lengths),
            (table.T, position.T, qkv_weight, out_weight, in_weight, down_weight, norms.T),
            (table_rows, position_rows, qkv_cols, out_cols, in_cols, down_cols),
            (table_cols, position_cols, qkv_rows, out_rows, in_rows, down_rows),
            norm_moment.T,
        )
    devices = lax.axis_size(("dp", "seq"))
    seq_index = lax.axis_index("seq")
    held = norms.shape[0]

    span = long_ids.shape[1]
    long_place = seq_index * span + lax.iota(jnp.int32, span)
    long_keep = (long_place[None, :] < long_lengths[:, None]).astype(jnp.int32)
    short_keep = (lax.iota(jnp.int32, SPAN)[None, :] < short_lengths[:, None]).astype(jnp.int32)
    long_pack = jnp.stack((long_ids, long_targets, long_mask * long_keep, long_keep), 1)
    short_pack = jnp.stack((short_ids, short_targets, short_mask * short_keep, short_keep), 1)
    moved = lax.all_to_all(
        jnp.concatenate((long_pack, short_pack[1:]), 0), "seq", split_axis=0, concat_axis=0, tiled=True
    )
    tokens = jnp.concatenate((moved, short_pack[:1]), 0)
    ids, targets, weight, keep = (tokens[:, i].reshape(-1) for i in range(4))
    weight = weight.astype(F32)
    count = tokens.shape[0] * span
    last = count - span
    alone = seq_index == lax.axis_size("seq") - 1
    token = lax.iota(jnp.int32, count)
    place = jnp.where(alone | (token >= last), token % span, token)
    row = jnp.where(alone | (token >= last), token // span, 0)
    allowed_long = (row[:last, None] == row[None, :last]) & (keep[None, :last] > 0)
    allowed_short = jnp.broadcast_to(keep[None, last:] > 0, (span, span))

    here_count = jnp.sum(long_pack[:, 2]) + jnp.sum(short_pack[:, 2])
    tall = table.T
    counts = jnp.broadcast_to(jnp.stack((here_count // 256, here_count % 256)).astype(F32)[None], (held, 2))
    wide_shard = jnp.concatenate(
        (tall, norms, counts, jnp.zeros((held, PLACE_AT - COUNT_AT - 2), F32), position.T), 1
    )
    shards = (wide_shard, qkv_weight, out_weight, in_weight, down_weight)
    wide_w, qkv_w, out_w, in_w, down_w = (
        lax.all_gather(shard.astype(BF16), ("dp", "seq"), axis=0, tiled=True) for shard in shards
    )
    column = lax.broadcasted_iota(jnp.int32, (1, WIDE), 1)
    chosen = ((ids[:, None] == column) | ((place[:, None] + PLACE_AT) == column)).astype(BF16)
    gains = wide_w[:, NORM_AT : NORM_AT + 6].astype(F32)
    sums = jnp.sum(wide_w[:, COUNT_AT : COUNT_AT + 2].astype(F32), 0)
    mask_count = (sums[0] * 256.0 + sums[1]) / held
    inverse_count = 1.0 / mask_count

    embedded = mm(chosen, wide_w, (1, 1))
    first, normed_a, inverse_a = norm_forward(embedded, gains[:, 0], gains[:, 1])
    first_b = first.astype(BF16)
    qkv_b = mm(first_b, qkv_w, (1, 0)).astype(BF16)
    mix_long, total_long = attend(qkv_b[:last], allowed_long)
    mix_short, total_short = attend(qkv_b[last:], allowed_short)
    mixture = jnp.concatenate((mix_long, mix_short), 0)
    second, normed_b, inverse_b = norm_forward(first + mm(mixture, out_w, (1, 0)), gains[:, 2], gains[:, 3])
    second_b = second.astype(BF16)
    hidden = mm(second_b, in_w, (1, 0))
    active, slope = gelu_pair(hidden)
    active_b = active.astype(BF16)
    third, normed_c, inverse_c = norm_forward(second + mm(active_b, down_w, (1, 0)), gains[:, 4], gains[:, 5])
    third_b = third.astype(BF16)
    logits = jnp.where(column < VOCAB, mm(third_b, wide_w, (1, 0)), -1e30)
    highest = jnp.max(logits, -1, keepdims=True)
    log_sum = highest + jnp.log(jnp.sum(jnp.exp(logits - highest), -1, keepdims=True))
    onehot = targets[:, None] == column
    picked = jnp.sum(jnp.where(onehot, logits, 0.0), -1)
    loss_part = jnp.sum(weight * (log_sum[:, 0] - picked))
    grad_logit = (
        (jnp.exp(logits - log_sum) - onehot.astype(F32)) * (weight * inverse_count)[:, None]
    ).astype(BF16)
    grad_third = mm(grad_logit, wide_w, (1, 1))
    grad_second, gain_c, shift_c = norm_backward(grad_third, normed_c, inverse_c, gains[:, 4])
    grad_ffn = grad_second.astype(BF16)
    down_grad = mm(active_b, grad_ffn, (0, 0)).astype(BF16)
    grad_hidden = (mm(grad_ffn, down_w, (1, 1)) * slope).astype(BF16)
    in_grad = mm(second_b, grad_hidden, (0, 0)).astype(BF16)
    grad_second = grad_second + mm(grad_hidden, in_w, (1, 1))
    grad_first, gain_b, shift_b = norm_backward(grad_second, normed_b, inverse_b, gains[:, 2])
    grad_attn = grad_first.astype(BF16)
    out_grad = mm(mixture, grad_attn, (0, 0)).astype(BF16)
    grad_mix = mm(grad_attn, out_w, (1, 1)).astype(BF16)
    grad_qkv = jnp.concatenate(
        (
            attend_back(qkv_b[:last], allowed_long, total_long, grad_mix[:last]),
            attend_back(qkv_b[last:], allowed_short, total_short, grad_mix[last:]),
        ),
        0,
    )
    qkv_grad = mm(first_b, grad_qkv, (0, 0)).astype(BF16)
    grad_first = grad_first + mm(grad_qkv, qkv_w, (1, 1))
    grad_embed, gain_a, shift_a = norm_backward(grad_first, normed_a, inverse_a, gains[:, 0])
    wide_grad = mm(
        jnp.concatenate((third_b, grad_embed.astype(BF16)), 0),
        jnp.concatenate((grad_logit, chosen), 0),
        (0, 0),
    )
    norm_part = jnp.stack((gain_a, shift_a, gain_b, shift_b, gain_c, shift_c), 1)
    wide_grad = lax.dynamic_update_slice(wide_grad.astype(BF16), norm_part.astype(BF16), (0, NORM_AT))
    grads = (wide_grad, qkv_grad, out_grad, in_grad, down_grad)
    wide_g, qkv_g, out_g, in_g, down_g = (
        lax.psum_scatter(grad.astype(F32), ("dp", "seq"), scatter_dimension=0, tiled=True) for grad in grads
    )
    table_g, place_g = wide_g[:, :VOCAB], wide_g[:, PLACE_AT:]
    norm_g = wide_g[:, NORM_AT : NORM_AT + 6]

    decay = 1.0 - STEP ** (-0.8)
    matrices = (
        (qkv_weight, qkv_g, qkv_rows, qkv_cols),
        (out_weight, out_g, out_rows, out_cols),
        (in_weight, in_g, in_rows, in_cols),
        (down_weight, down_g, down_rows, down_cols),
    )
    wide = (
        (tall, table_g, table_cols, table_rows),
        (position.T, place_g, position_cols, position_rows),
    )
    row_news = [
        decay * member[2] + (1.0 - decay) * jnp.mean(member[1] * member[1] + SQUARE_FLOOR, 1)
        for member in matrices + wide
    ]
    col_parts = [jnp.sum(member[1] * member[1] + SQUARE_FLOOR, 0) for member in matrices + wide]
    row_totals = jnp.stack([jnp.sum(rows_new) for rows_new in row_news])
    weight_sq = jnp.stack([jnp.sum(member[0] * member[0]) for member in matrices + wide])
    stats = lax.psum(
        col_parts + [row_totals, weight_sq, jnp.sum(norms * norms, 0), loss_part.reshape(1)], ("dp", "seq")
    )
    updates = []
    cols_out = []
    for index, member in enumerate(matrices + wide):
        full_rows = member[0].shape[0] * devices
        cols_new = decay * member[3] + (1.0 - decay) * stats[index] / full_rows
        if index < 4:
            mean = stats[6][index] / full_rows
        else:
            mean = jnp.mean(cols_new)
        updates.append(member[1] * lax.rsqrt(row_news[index][:, None] * cols_new[None, :] / mean))
        cols_out.append(cols_new)
    moment_new = decay * norm_moment + (1.0 - decay) * (norm_g * norm_g + SQUARE_FLOOR)
    norm_update = norm_g * lax.rsqrt(moment_new)
    update_sq = jnp.stack([jnp.sum(update * update) for update in updates])
    totals = lax.psum((update_sq, jnp.sum(norm_update * norm_update, 0)), ("dp", "seq"))
    news = []
    for index, member in enumerate(matrices + wide):
        entries = member[0].shape[0] * member[0].shape[1] * devices
        clip = jnp.maximum(1.0, jnp.sqrt(totals[0][index] / entries))
        news.append(
            member[0] - learn_rate * jnp.sqrt(stats[7][index] / entries) * updates[index] / clip
        )
    norm_rows = norms.shape[0] * devices
    norm_clip = jnp.maximum(1.0, jnp.sqrt(totals[1] / norm_rows))
    norm_new = norms - learn_rate * jnp.sqrt(stats[8] / norm_rows) * norm_update / norm_clip
    return (
        stats[9][0],
        mask_count,
        table_g.T,
        place_g.T,
        qkv_g,
        out_g,
        in_g,
        down_g,
        norm_g,
        cols_out[4],
        row_news[4],
        cols_out[5],
        row_news[5],
        row_news[0],
        cols_out[0],
        row_news[1],
        cols_out[1],
        row_news[2],
        cols_out[2],
        row_news[3],
        cols_out[3],
        moment_new,
        news[4].T,
        news[5].T,
        news[0],
        news[1],
        news[2],
        news[3],
        norm_new,
    )


def solution(mesh):
    split, wide = P(("dp", "seq"), None), P(None, ("dp", "seq"))
    shard, same = P(("dp", "seq")), P()
    return jax.shard_map(
        functools.partial(on_device, (mesh.shape["dp"], mesh.shape["seq"])),
        mesh=mesh,
        in_specs=(P("dp", "seq"),) * 3
        + (P("dp"),)
        + (split,) * 3
        + (shard,)
        + (wide,) * 2
        + (split,) * 5
        + (same, shard) * 2
        + (shard, same) * 4
        + (split,),
        out_specs=(same, same)
        + (wide,) * 2
        + (split,) * 5
        + (same, shard) * 2
        + (shard, same) * 4
        + (split,)
        + (wide,) * 2
        + (split,) * 5,
        check_vma=False,
    )
```

```python
import functools

import jax
import jax.numpy as jnp
from jax import lax
from jax.experimental import pallas as pl
from jax.experimental.pallas import tpu as pltpu
from jax.sharding import PartitionSpec as P

D = 768
HEADS = 12
HEAD_DIM = 64
VOCAB = 4101
STEP = 10
SPAN = 128

EPSILON = 1e-12
SQUARE_FLOOR = 1e-30
learn_rate = 0.3

MESH = pl.DeviceIdType.MESH
F32 = jnp.float32
BF16 = jnp.bfloat16

NORM_AT = VOCAB
COUNT_AT = VOCAB + 6
TABLE_END = 4352
PLACE_AT = 4608
WIDE = PLACE_AT + 512

SHAPES = ((24, WIDE), (24, 3 * D), (24, D), (24, 4 * D), (96, D))
E_, Q_, O_, I_, D_ = range(5)
CLASS_A, CLASS_B, CLASS_C = (E_, O_), (Q_, D_), (I_,)
UP, DOWN, XWAY, YWAY, SIDE = range(5)


def here():
    dp, seq = lax.axis_index("dp"), lax.axis_index("seq")
    return dp // 2, dp % 2, seq // 2, seq % 2


def device(z, y, x, c):
    return {"dp": z * 2 + y, "seq": x * 2 + c}


def chip(z, y, x):
    return z * 4 + y * 2 + x


def all_peers():
    z, y, x, c = here()
    return (
        device(z + 1, y, x, c),
        device(z - 1, y, x, c),
        device(z, y, 1 - x, c),
        device(z, 1 - y, x, c),
        device(z, y, x, 1 - c),
    )


SUM_AT = (0, WIDE, WIDE + 3 * D, WIDE + 4 * D, WIDE + 8 * D, WIDE + 9 * D)
SUMS = WIDE + 9 * D + 256


def lanes_of(members):
    lane = lax.broadcasted_iota(jnp.int32, (1, 128), 1)
    row = jnp.zeros((1, 128), F32)
    for index, member in enumerate(members):
        row = jnp.where(lane == index, member, row)
    return row


def lane_at(row, index):
    lane = lax.broadcasted_iota(jnp.int32, row.shape, 1)
    return jnp.sum(jnp.where(lane == index, row, 0.0), 1, keepdims=True)


def column_of(row):
    size = row.shape[1]
    diagonal = lax.broadcasted_iota(jnp.int32, (size, size), 0) == lax.broadcasted_iota(
        jnp.int32, (size, size), 1
    )
    return jnp.sum(jnp.where(diagonal, row, 0.0), 1, keepdims=True)


def row_of(column):
    size = column.shape[0]
    diagonal = lax.broadcasted_iota(jnp.int32, (size, size), 0) == lax.broadcasted_iota(
        jnp.int32, (size, size), 1
    )
    return jnp.sum(jnp.where(diagonal, column, 0.0), 0, keepdims=True)


def as_row(ref):
    return ref[...].reshape(1, ref.shape[0])


def total_sum(array):
    return jnp.sum(jnp.sum(array, 1, keepdims=True), 0, keepdims=True)


def sum_everywhere(value, first, second, third, sems):
    z, y, x, c = here()
    spot = y * 2 + x
    side_send, side_recv, plane_send, plane_recv, z_send, z_recv = sems

    def copy(src, dst, send, recv, peer):
        return pltpu.make_async_remote_copy(
            src_ref=src, dst_ref=dst, send_sem=send, recv_sem=recv, device_id=peer, device_id_type=MESH
        )

    first[0] = value
    swap = copy(first.at[0], first.at[1], side_send, side_recv, device(z, y, x, 1 - c))
    swap.start()
    swap.wait_recv()
    second[spot] = first[0] + first[1]
    plane = []
    for i, (to_y, to_x) in enumerate(((y, 1 - x), (1 - y, x), (1 - y, 1 - x))):
        plane.append(
            copy(second.at[spot], second.at[spot], plane_send.at[i], plane_recv.at[i], device(z, to_y, to_x, c))
        )
        plane[i].start()
    for member in plane:
        member.wait_recv()
    third[z] = (second[0] + second[1]) + (second[2] + second[3])
    column = []
    for i in range(3):
        to_z = (z + 1 + i) % 4
        column.append(copy(third.at[z], third.at[z], z_send.at[i], z_recv.at[i], device(to_z, y, x, c)))
        column[i].start()
    for member in column:
        member.wait_recv()
    for member in [swap] + plane + column:
        member.wait_send()
    return (third[0] + third[1]) + (third[2] + third[3])


def gelu_pair(hidden):
    normal_cdf = 0.5 * (1.0 + lax.erf(hidden * 0.7071067811865476))
    return (
        hidden * normal_cdf,
        normal_cdf + hidden * jnp.exp(-0.5 * hidden * hidden) * 0.3989422804014327,
    )


def dot_nn(left, right):
    return jnp.dot(left, right, preferred_element_type=F32)


def dot_nt(left, right):
    return lax.dot_general(left, right, (((1,), (1,)), ((), ())), preferred_element_type=F32)


def dot_tn(left, right):
    return lax.dot_general(left, right, (((0,), (0,)), ((), ())), preferred_element_type=F32)


def at(index, size):
    if isinstance(index, int):
        return pl.ds(index * size, size)
    return pl.ds(pl.multiple_of(index * size, size), size)


def each(count, body):
    def step(index, carry):
        body(index)
        return carry

    lax.fori_loop(0, count, step, 0)


def each_unrolled(count, body):
    for index in range(count):
        body(index)


ROWS = 128
TILE = 256
HALF = 320
TABLE_TILES = TABLE_END // TILE


def head_lanes(first):
    lane = lax.broadcasted_iota(jnp.int32, (1, 128), 1)
    return (lane < HEAD_DIM) if first else (lane >= HEAD_DIM)


def layer_norm(value, gain, shift):
    centred = value - jnp.sum(value, 1, keepdims=True) / D
    inverse = lax.rsqrt(jnp.sum(centred * centred, 1, keepdims=True) / D + EPSILON)
    normed = centred * inverse
    return normed * gain + shift, normed, inverse


def layer_norm_back(grad, normed, inverse, gain):
    scaled = grad * gain
    return inverse * (
        scaled - jnp.sum(scaled, 1, keepdims=True) / D - normed * (jnp.sum(scaled * normed, 1, keepdims=True) / D)
    )


def put_lane(ref, rows, index, value):
    lane = lax.broadcasted_iota(jnp.int32, (1, 128), 1)
    ref[rows, :] = jnp.where(lane == index, value, ref[rows, :])


def set_bias(bias, cols, keys, last):
    same = cols[0:last, 4:5] == keys[1:2, 0:last]
    bias[...] = jnp.where(same & (keys[0:1, 0:last] > 0), 0.0, -1e30)


CHOOSE, EMBED, NORM_A, PROJECT, TURN_X, ATTEND, OUT, NORM_B, FEED_IN, TURN_A, FEED_OUT, REST = range(12)
FRONT = (
    68, 36, 35, 34, 67, 131, 4, 64, 37, 65, 3, 33, 40, 66, 71, 162, 70, 41, 2, 38,
    72, 165, 96, 75, 8, 5, 69, 32, 39, 1, 160, 0, 46, 169, 13, 14, 74, 73, 44, 42,
    82, 161, 9, 49, 78, 80, 130, 43, 76, 77, 6, 167, 50, 83, 48, 45, 47, 81, 166, 98,
    174, 51, 164, 79, 97, 7, 1000, 178, 170, 128, 129, 172, 101, 1016, 16, 1017, 10, 12, 100, 1018,
    11, 163, 15, 1001, 102, 1019, 17, 1020, 99, 18, 103, 19, 1021, 136, 1032, 105, 1048, 177, 168, 132,
    171, 176, 1049, 110, 1050, 1051, 112, 106, 1052, 104, 1053, 1054, 133, 1055, 1056, 1064, 1080, 107, 179, 135,
    1081, 1082, 173, 114, 134, 175, 1083, 109, 1084, 1085, 1096, 113, 1097, 137, 1098, 108, 111, 146, 115, 1112,
    142, 140, 139, 144, 141, 1128, 1129, 1130, 1131, 138, 1132, 1133, 143, 1134, 1135, 1136, 1137, 1138, 145, 147,
    1139, 1144, 1160, 1161, 1162, 1176,
)


def front_hooks():
    hooks, before = {}, []
    for task in FRONT:
        if task < 1000:
            before.append(task)
        else:
            hooks[((task - 1000) // 16, (task - 1000) % 16)] = before
            before = []
    return hooks


def front_kernel(*refs):
    raw, (long_len, short_len) = refs[0:13], refs[13:15]
    loss_out, count_out, gains_out, norm_out, side, cols, keys, squares = refs[15:23]
    x_t, mix_t, a_t, act_t, y_t, glog_out, slope_out, qkv_out, na_out, nb_out, grad_out = refs[23:34]
    weight_outs = refs[34:38]
    wide, qkv_w, out_w, in_w, down_w = weights = refs[38:43]
    value, na, nb, low_a, mix, qkv, act, slope, logits, pick, bias, turned, act_turned = refs[43:56]
    held, wide_shard, merge, pieces, land = refs[56:69], refs[69], refs[70:75], refs[75], refs[76]
    raw_sem, swap_send, swap_recv, token_send, token_recv, send_sem, link_recv, side_recv = refs[77:85]
    out_sem, turn_sem, act_sem = refs[85:88]
    z, y, x, c = here()
    peers = all_peers()
    me = chip(z, y, x)
    seq = x * 2 + c
    alone = seq // 3
    tokens = value.shape[0]
    last = tokens - SPAN
    hooks = front_hooks()

    barrier = pltpu.get_barrier_semaphore()
    cross = device(z, y, 1 - x, 1 - c)
    column = [device((z + 1 + i) % 4, y, x, c) for i in range(3)]
    for peer in [peers[XWAY], peers[YWAY], peers[SIDE], cross] + column:
        pl.semaphore_signal(barrier, inc=1, device_id=peer, device_id_type=MESH)
    raws = [pltpu.make_async_copy(raw[i], held[i], raw_sem.at[i]) for i in range(13)]
    for member in raws:
        member.start()
    for member in raws:
        member.wait()
    long_ids, long_targets, long_mask, short_ids, short_targets, short_mask, tall, place, qkv_s, out_s, in_s, down_s, norms = held

    pieces[...] = jnp.zeros(pieces.shape, jnp.int32)
    land[4] = jnp.zeros((8, SPAN), jnp.int32)
    lane = lax.broadcasted_iota(jnp.int32, (1, SPAN), 1)
    count = jnp.zeros((1, SPAN), jnp.int32)
    for t in range(5):
        if t < 3:
            ids, targets, mask = long_ids[t : t + 1, :], long_targets[t : t + 1, :], long_mask[t : t + 1, :]
            keep = (lane + seq * SPAN < long_len[t]).astype(jnp.int32)
        else:
            row = (1, 0)[t - 3]
            ids, targets, mask = (member[row : row + 1, :] for member in (short_ids, short_targets, short_mask))
            keep = (lane < short_len[row]).astype(jnp.int32)
        target = pieces.at[t] if t < 4 else land.at[4]
        target[0:1, :] = ids
        target[2:3, :] = targets
        target[3:4, :] = mask * keep
        target[5:6, :] = keep
        count = count + mask * keep
    count = jnp.sum(count.astype(F32), 1, keepdims=True)
    high = jnp.floor(count * (1.0 / 256.0))

    wide_shard[:, 0:4096] = tall[:, 0:4096]
    edge = jnp.zeros((24, 128), F32)
    tile_lane = lax.broadcasted_iota(jnp.int32, (24, 128), 1)
    tall_edge = tall[:, 4096:VOCAB]
    members = [lane_at(tall_edge, i) for i in range(VOCAB - 4096)]
    members += [column_of(norms[i : i + 1, :]) for i in range(6)]
    members += [high, count - high * 256.0]
    for i, member in enumerate(members):
        edge = jnp.where(tile_lane == i, member, edge)
    wide_shard[:, 4096:4224] = edge
    wide_shard[:, 4224:PLACE_AT] = jnp.zeros((24, PLACE_AT - 4224), F32)
    wide_shard[:, PLACE_AT:] = place[...]
    shards = (wide_shard, qkv_s, out_s, in_s, down_s)

    pl.semaphore_wait(barrier, 7)
    swaps = []
    for m in (E_, Q_, I_, D_, O_):
        size, half = SHAPES[m][0], SHAPES[m][1] // 2
        swaps.append(
            pltpu.make_async_remote_copy(
                src_ref=shards[m].at[:, pl.ds(pl.multiple_of((1 - c) * half, 128), half)],
                dst_ref=merge[m].at[pl.ds(pl.multiple_of(c * size, 8), size), :],
                send_sem=swap_send.at[m],
                recv_sem=swap_recv.at[m],
                device_id=peers[SIDE],
                device_id_type=MESH,
            )
        )
        swaps[-1].start()
    token_copies = []
    for i, (to_x, to_c) in enumerate(((x, 1 - c), (1 - x, c), (1 - x, 1 - c))):
        token_copies.append(
            pltpu.make_async_remote_copy(
                src_ref=pieces.at[to_x * 2 + to_c],
                dst_ref=land.at[seq],
                send_sem=token_send.at[i],
                recv_sem=token_recv.at[i],
                device_id=device(z, y, to_x, to_c),
                device_id_type=MESH,
            )
        )
        token_copies[-1].start()
    land[seq] = pieces[seq]

    def part(piece, k, half):
        m, skip, wide_part = PIECES[piece]
        size = 2 * SHAPES[m][0]
        start = pl.multiple_of(half * (SHAPES[m][1] // 2) + skip, 128)
        return weights[m].at[pl.ds(pl.multiple_of(k * size, size), size), pl.ds(start, wide_part)]

    FIRST_WAY, SECOND_WAY, SIDE_WAY = 0, 1, 2

    def copy_of(piece, k, way):
        ways = (XWAY, YWAY) if piece in Y_FIRST else (YWAY, XWAY)
        peer = column[way - 3] if way > 2 else peers[SIDE] if way == SIDE_WAY else peers[ways[way]]
        return pltpu.make_async_remote_copy(
            src_ref=part(piece, k, c),
            dst_ref=part(piece, k, c),
            send_sem=send_sem.at[piece, k, way],
            recv_sem=(side_recv if way == SIDE_WAY else link_recv).at[piece, k],
            device_id=peer,
            device_id_type=MESH,
        )

    def block_of(number):
        piece, task = number // 32, number % 32
        last_y = piece in Y_FIRST
        if task < 5:
            return piece, me, (3 + task if task < 3 else FIRST_WAY if task == 3 else SECOND_WAY,), False
        if task < 8:
            return piece, chip((z + task - 4) % 4, y, x), (FIRST_WAY, SECOND_WAY, SIDE_WAY), True
        if task < 12:
            t = (z + task - 8) % 4
            return piece, chip(t, y, 1 - x) if last_y else chip(t, 1 - y, x), (SECOND_WAY, SIDE_WAY), True
        t, other = (z + (task - 12) // 2) % 4, (task - 12) % 2
        if last_y:
            return piece, chip(t, 1 - y, 1 - x if other else x), (SIDE_WAY,), True
        return piece, chip(t, 1 - y if other else y, 1 - x), (SIDE_WAY,), True

    def transfer(number):
        piece, k, ways, waits = block_of(number)
        if waits:
            copy_of(piece, k, FIRST_WAY).wait_recv()
        for way in ways:
            copy_of(piece, k, way).start()

    def before(step, index, base=0):
        for (name, part_index), tasks in hooks.items():
            part_index = part_index - base
            if name != step or not tasks or (step == EMBED and not 0 <= part_index < 3):
                continue
            if index is None or isinstance(index, int):
                if part_index == (index or 0):
                    for number in tasks:
                        transfer(number)
            else:

                @pl.when(index == part_index)
                def _(tasks=tasks):
                    for number in tasks:
                        transfer(number)

    def need(*wanted):
        for piece in wanted:
            for k in range(16):
                pltpu.make_async_remote_copy(
                    src_ref=part(piece, k, 1 - c),
                    dst_ref=part(piece, k, 1 - c),
                    send_sem=send_sem.at[piece, k, SIDE_WAY],
                    recv_sem=side_recv.at[piece, k],
                    device_id=peers[SIDE],
                    device_id_type=MESH,
                ).wait_recv()

    for number, m in enumerate((E_, Q_, I_, D_, O_)):
        swaps[number].wait_recv()
        size, half = SHAPES[m][0], SHAPES[m][1] // 2
        merge[m][pl.ds(pl.multiple_of(c * size, 8), size), :] = shards[m][:, pl.ds(pl.multiple_of(c * half, 128), half)]
        rows = pl.ds(pl.multiple_of(me * 2 * size, 2 * size), 2 * size)
        weights[m][rows, pl.ds(pl.multiple_of(c * half, 128), half)] = merge[m][...].astype(BF16)
        for piece in range(6):
            if PIECES[piece][0] == m:
                copy_of(piece, me, SIDE_WAY).start()
    for copy in token_copies:
        copy.wait_recv()
    side[...] = jnp.zeros(side.shape, F32)
    keys[...] = jnp.zeros(keys.shape, jnp.int32)
    zeros = jnp.zeros((1, SPAN), F32)
    for b in range(5):
        tile = land[b]
        shift = b * SPAN * (1 - alone) if b < 4 else 0
        row = b * alone if b < 4 else 0
        spot = (lane + shift + PLACE_AT).astype(F32)
        row_lane = (lane * 0 + row).astype(F32)
        ids, targets, weight = (tile[i : i + 1].astype(F32) for i in (0, 2, 3))
        stacked = jnp.concatenate((ids, spot, targets, weight, row_lane, zeros, zeros, zeros), 0)
        stacked = jnp.concatenate((stacked, jnp.zeros((120, SPAN), F32)), 0)
        cols[b * SPAN : (b + 1) * SPAN, :] = stacked.T.astype(jnp.int32)
        keys[0:1, b * SPAN : (b + 1) * SPAN] = tile[5:6]
        keys[1:2, b * SPAN : (b + 1) * SPAN] = lane * 0 + row
    set_bias(bias, cols, keys, last)
    found = [total_sum(member[...] * member[...]) for member in (tall, place, qkv_s, out_s, in_s, down_s)]
    norm_squares = jnp.sum(norms[...] * norms[...], 1, keepdims=True)
    squares[...] = lanes_of(found + [norm_squares[i : i + 1] for i in range(6)])

    turns, outs = {}, {}

    def turn_out(source, target, slot):
        if slot in turns:
            turns[slot].wait()

        def some(index):
            turned[slot, :, at(index, ROWS)] = source[at(index, ROWS), :].T

        each(tokens // ROWS, some)
        turns[slot] = pltpu.make_async_copy(turned.at[slot], target, turn_sem.at[slot])
        turns[slot].start()

    def put_out(name, source, target):
        outs[name] = pltpu.make_async_copy(source, target, out_sem.at[len(outs)])
        outs[name].start()

    for half in range(tokens // HALF):
        rows = pl.ds(half * HALF, HALF)
        def choose(index):
            column_lane = lax.broadcasted_iota(jnp.int32, (1, TILE), 1) + index * TILE
            hit = (cols[rows, 0:1] == column_lane) | (cols[rows, 1:2] == column_lane)
            pick[:, at(index, TILE)] = jnp.where(hit, 1.0, 0.0).astype(BF16)

        each(WIDE // TILE, choose)
        before(CHOOSE, half)
        if half == 0:
            need(1, 2)

        def embed(index):
            before(EMBED, index, half * 3)
            value[rows, at(index, TILE)] = dot_nt(pick[...], wide[at(index, TILE), :])

        each_unrolled(D // TILE, embed)

    gains = wide[:, 4096:4224].astype(F32).T
    gains_out[...] = gains[0:16]
    counts = jnp.sum(gains[11:13], 1, keepdims=True) / 24.0
    mask_count = counts[0:1] * 256.0 + counts[1:2]
    count_out[...] = mask_count
    inverse_count = 1.0 / mask_count
    norm_rows = [gains_out[5 + i : 6 + i, :] for i in range(6)]
    before(NORM_A, None)

    def norm_a(index):
        rows = at(index, ROWS)
        found, normed, inverse = layer_norm(value[rows, :], norm_rows[0], norm_rows[1])
        value[rows, :] = found
        low_a[rows, :] = found.astype(BF16)
        na[rows, :] = normed
        put_lane(side, rows, 12, inverse)

    each(tokens // ROWS, norm_a)
    put_out("na", na, na_out)
    before(PROJECT, 0)
    need(0)

    def project(index):
        before(PROJECT, index)
        qkv[:, at(index, TILE)] = dot_nn(low_a[...], qkv_w[:, at(index, TILE)]).astype(BF16)

    hooks.pop((PROJECT, 0))
    each_unrolled(3 * D // TILE, project)
    put_out("qkv", qkv, qkv_out)
    put_out("qkv_w", qkv_w, weight_outs[0])
    before(TURN_X, None)
    turn_out(low_a, x_t, 0)

    def attend_pair(pair):
        before(ATTEND, pair)
        for start, size in ((0, last), (last, SPAN)):
            rows = pl.ds(start, size)
            query = qkv[rows, at(pair, 128)]
            key = qkv[rows, pl.ds(pl.multiple_of(D + pair * 128, 128), 128)]
            val = qkv[rows, pl.ds(pl.multiple_of(2 * D + pair * 128, 128), 128)]
            mask = bias[...] if start == 0 else jnp.where(keys[0:1, last:tokens] > 0, 0.0, -1e30)
            mixed = []
            for first in (True, False):
                chosen = jnp.where(head_lanes(first), query, jnp.zeros_like(query))
                scores = dot_nt(chosen, key) * 0.125 + mask
                highest = jnp.max(scores, 1, keepdims=True)
                raised = jnp.exp(scores - highest)
                summed = jnp.sum(raised, 1, keepdims=True)
                shares = (raised * (1.0 / summed)).astype(BF16)
                mixed.append(dot_nn(shares, val))
                put_lane(side, rows, 2 * pair + (0 if first else 1), highest + jnp.log(summed))
            mix[rows, at(pair, 128)] = jnp.where(head_lanes(True), mixed[0], mixed[1]).astype(BF16)

    each(HEADS // 2, attend_pair)
    before(OUT, 0)
    hooks.pop((OUT, 0))
    need(5)

    def out_project(index):
        before(OUT, index)
        value[:, at(index, TILE)] = value[:, at(index, TILE)] + dot_nn(mix[...], out_w[:, at(index, TILE)])

    each_unrolled(D // TILE, out_project)
    put_out("out_w", out_w, weight_outs[1])
    turn_out(mix, mix_t, 1)
    before(NORM_B, None)

    def norm_b(index):
        rows = at(index, ROWS)
        found, normed, inverse = layer_norm(value[rows, :], norm_rows[2], norm_rows[3])
        value[rows, :] = found
        low_a[rows, :] = found.astype(BF16)
        nb[rows, :] = normed
        put_lane(side, rows, 13, inverse)

    each(tokens // ROWS, norm_b)
    put_out("nb", nb, nb_out)
    before(FEED_IN, 0)
    hooks.pop((FEED_IN, 0))
    need(3)

    def feed_in(index):
        before(FEED_IN, index)
        hidden = dot_nn(low_a[...], in_w[:, at(index, TILE)])
        active, slant = gelu_pair(hidden)
        active = active.astype(BF16)
        act[:, at(index, TILE)] = active
        slope[:, at(index, TILE)] = slant.astype(BF16)
        slot = index % 2
        copy = pltpu.make_async_copy(act_turned.at[slot], act_t.at[at(index, TILE), :], act_sem.at[slot])
        if index >= 2:
            copy.wait()
        act_turned[slot] = active.T
        copy.start()

    each_unrolled(4 * D // TILE, feed_in)
    for slot in range(2):
        pltpu.make_async_copy(act_turned.at[slot], act_t.at[0:TILE, :], act_sem.at[slot]).wait()
    put_out("slope", slope, slope_out)
    put_out("in_w", in_w, weight_outs[2])
    before(TURN_A, None)
    turn_out(low_a, a_t, 0)
    before(FEED_OUT, 0)
    hooks.pop((FEED_OUT, 0))
    need(4)

    def feed_out(index):
        before(FEED_OUT, index)
        value[:, at(index, TILE)] = value[:, at(index, TILE)] + dot_nn(act[...], down_w[:, at(index, TILE)])

    each_unrolled(D // TILE, feed_out)
    put_out("down_w", down_w, weight_outs[3])
    before(REST, None)
    outs["nb"].wait()

    def norm_c(index):
        rows = at(index, ROWS)
        found, normed, inverse = layer_norm(value[rows, :], norm_rows[4], norm_rows[5])
        low_a[rows, :] = found.astype(BF16)
        nb[rows, :] = normed
        put_lane(side, rows, 14, inverse)

    each(tokens // ROWS, norm_c)
    turn_out(low_a, y_t, 1)
    outs["na"].wait()
    loss = jnp.zeros((1, 1), F32)
    for half in range(tokens // HALF):
        rows = pl.ds(half * HALF, HALF)
        target = cols[rows, 2:3]
        weight = cols[rows, 3:4].astype(F32)

        def lanes(index):
            return lax.broadcasted_iota(jnp.int32, (1, TILE), 1) + index * TILE

        def multiply(index, highest):
            found = dot_nn(low_a[rows, :], wide[:, at(index, TILE)])
            if index == TABLE_TILES - 1:
                found = jnp.where(lanes(index) < VOCAB, found, -1e30)
            logits[:, at(index, TILE)] = found
            return jnp.maximum(highest, jnp.maximum(found[:, 0:128], found[:, 128:256]))

        highest = jnp.full((HALF, 128), -1e30, F32)
        for index in range(TABLE_TILES):
            highest = multiply(index, highest)
        highest = jnp.max(highest, 1, keepdims=True)

        def raise_to(index, carry):
            summed, picked = carry
            found = logits[:, at(index, TILE)]
            raised = jnp.exp(found - highest)
            logits[:, at(index, TILE)] = raised
            hit = jnp.where(lanes(index) == target, found, 0.0)
            return summed + raised[:, 0:128] + raised[:, 128:256], picked + hit[:, 0:128] + hit[:, 128:256]

        zero = jnp.zeros((HALF, 128), F32)
        summed, picked = zero, zero
        for index in range(TABLE_TILES):
            summed, picked = raise_to(index, (summed, picked))
        summed = jnp.sum(summed, 1, keepdims=True)
        picked = jnp.sum(picked, 1, keepdims=True)
        loss = loss + jnp.sum(weight * (highest + jnp.log(summed) - picked), 0, keepdims=True)
        scale = weight * inverse_count
        share = scale / summed
        if half > 0:
            outs["glog0"].wait()

        def differ(index):
            found = logits[:, at(index, TILE)] * share - jnp.where(lanes(index) == target, scale, 0.0)
            pick[:, at(index, TILE)] = found.astype(BF16)

        each_unrolled(TABLE_TILES, differ)
        put_out("glog%d" % half, pick.at[:, 0:TABLE_END], glog_out.at[rows, :])

        def back(index):
            na[rows, at(index, TILE)] = dot_nt(pick[:, 0:TABLE_END], wide[at(index, TILE), 0:TABLE_END])

        each_unrolled(D // TILE, back)
    loss_out[...] = loss

    def norm_c_back(index, carry):
        gain, shift = carry
        rows = at(index, ROWS)
        inverse = lane_at(side[rows, :], 14)
        found, normed = na[rows, :], nb[rows, :]
        na[rows, :] = layer_norm_back(found, normed, inverse, norm_rows[4])
        return gain + jnp.sum(found * normed, 0, keepdims=True), shift + jnp.sum(found, 0, keepdims=True)

    zero = jnp.zeros((1, D), F32)
    gain, shift = lax.fori_loop(0, tokens // ROWS, norm_c_back, (zero, zero))
    norm_out[0:1, :] = gain
    norm_out[1:2, :] = shift
    put_out("grad", na, grad_out)
    for swap in swaps:
        swap.wait_send()
    for copy in token_copies:
        copy.wait_send()
    for piece in range(6):
        copy_of(piece, me, SIDE_WAY).wait_send()
    for number in FRONT:
        if number < 1000:
            piece, k, ways, _ = block_of(number)
            for way in ways:
                copy_of(piece, k, way).wait_send()
    for name, copy in outs.items():
        if name not in ("na", "nb", "glog0"):
            copy.wait()
    for copy in turns.values():
        copy.wait()


def front(large, lengths):
    vmem, hbm = pl.BlockSpec(memory_space=pltpu.VMEM), pl.BlockSpec(memory_space=pl.ANY)
    smem = pl.BlockSpec(memory_space=pltpu.SMEM)
    shape, dma = jax.ShapeDtypeStruct, pltpu.SemaphoreType.DMA
    tokens = 5 * SPAN
    small = [shape((1, 1), F32), shape((1, 1), F32), shape((16, D), F32), shape((2, D), F32), shape((tokens, 128), F32)]
    small += [shape((tokens, 128), jnp.int32), shape((8, tokens), jnp.int32), shape((1, 128), F32)]
    out = [shape((D, tokens), BF16)] * 3 + [shape((4 * D, tokens), BF16), shape((D, tokens), BF16)]
    out += [shape((tokens, TABLE_END), BF16), shape((tokens, 4 * D), BF16), shape((tokens, 3 * D), BF16)]
    out += [shape((tokens, D), F32)] * 3
    out += [shape((32 * SHAPES[m][0], SHAPES[m][1]), BF16) for m in (Q_, O_, I_, D_)]
    return pl.pallas_call(
        front_kernel,
        out_shape=small + out,
        in_specs=[hbm] * 13 + [smem] * 2,
        out_specs=[vmem] * len(small) + [hbm] * len(out),
        scratch_shapes=[pltpu.VMEM((32 * size, wide), BF16) for size, wide in SHAPES]
        + [pltpu.VMEM((tokens, D), F32)] * 3
        + [pltpu.VMEM((tokens, D), BF16)] * 2
        + [
            pltpu.VMEM((tokens, 3 * D), BF16),
            pltpu.VMEM((tokens, 4 * D), BF16),
            pltpu.VMEM((tokens, 4 * D), BF16),
            pltpu.VMEM((HALF, TABLE_END), F32),
            pltpu.VMEM((HALF, WIDE), BF16),
            pltpu.VMEM((tokens - SPAN, tokens - SPAN), F32),
            pltpu.VMEM((2, D, tokens), BF16),
            pltpu.VMEM((2, TILE, tokens), BF16),
        ]
        + [pltpu.VMEM(member.shape, member.dtype) for member in large]
        + [pltpu.VMEM(SHAPES[E_], F32)]
        + [pltpu.VMEM((2 * size, wide // 2), F32) for size, wide in SHAPES]
        + [pltpu.VMEM((4, 8, SPAN), jnp.int32), pltpu.VMEM((5, 8, SPAN), jnp.int32)]
        + [dma((13,)), dma((5,)), dma((5,)), dma((3,)), dma((3,)), dma((6, 16, 6)), dma((6, 16)), dma((6, 16))]
        + [dma((12,)), dma((2,)), dma((2,))],
        compiler_params=pltpu.CompilerParams(
            collective_id=0, has_side_effects=True, vmem_limit_bytes=63 * 1024 * 1024
        ),
    )(*large, *lengths)


def backward_kernel(*refs):
    loaded, (cols, keys, side, gains) = refs[0:9], refs[9:13]
    norm_out, ge_t, gffn_out, gh_out, gattn_out, gqkv_out = refs[13:19]
    qkv_w, out_w, in_w, down_w, slope, qkv, na, nb, grad = refs[19:28]
    low, attn, gh, bias, turned, load_sem, out_sem = refs[28:35]
    tokens = grad.shape[0]
    last = tokens - SPAN
    held = (qkv_w, out_w, in_w, down_w, slope, qkv, na, nb, grad)
    loads = [pltpu.make_async_copy(loaded[i], held[i], load_sem.at[i]) for i in range(9)]
    order = (8, 3, 4, 2, 7, 1, 5, 0, 6)
    for i in order:
        loads[i].start()
    outs = []

    def put_out(source, target):
        copy = pltpu.make_async_copy(source, target, out_sem.at[len(outs)])
        copy.start()
        outs.append(copy)

    set_bias(bias, cols, keys, last)
    loads[8].wait()

    def round_grad(index):
        rows = at(index, ROWS)
        low[rows, :] = grad[rows, :].astype(BF16)

    each(tokens // ROWS, round_grad)
    put_out(low, gffn_out)
    loads[3].wait()
    loads[4].wait()

    def feed_out_back(index):
        found = dot_nt(low[...], down_w[at(index, TILE), :]) * slope[:, at(index, TILE)].astype(F32)
        gh[:, at(index, TILE)] = found.astype(BF16)

    each_unrolled(4 * D // TILE, feed_out_back)
    put_out(gh, gh_out)
    loads[2].wait()

    def feed_in_back(index):
        grad[:, at(index, TILE)] = grad[:, at(index, TILE)] + dot_nt(gh[...], in_w[at(index, TILE), :])

    each_unrolled(D // TILE, feed_in_back)
    loads[7].wait()
    outs[0].wait()
    zero = jnp.zeros((1, D), F32)

    def norm_b_back(index, carry):
        gain, shift = carry
        rows = at(index, ROWS)
        inverse = lane_at(side[rows, :], 13)
        found, normed = grad[rows, :], nb[rows, :]
        back = layer_norm_back(found, normed, inverse, gains[7:8, :])
        grad[rows, :] = back
        low[rows, :] = back.astype(BF16)
        return gain + jnp.sum(found * normed, 0, keepdims=True), shift + jnp.sum(found, 0, keepdims=True)

    gain, shift = lax.fori_loop(0, tokens // ROWS, norm_b_back, (zero, zero))
    norm_out[2:3, :] = gain
    norm_out[3:4, :] = shift
    put_out(low, gattn_out)
    loads[1].wait()

    def out_back(index):
        attn[:, at(index, TILE)] = dot_nt(low[...], out_w[at(index, TILE), :]).astype(BF16)

    each_unrolled(D // TILE, out_back)
    loads[5].wait()

    def attend_pair_back(pair):
        for start, size in ((0, last), (last, SPAN)):
            rows = pl.ds(start, size)
            spots = [pl.ds(pl.multiple_of(i * D + pair * 128, 128), 128) for i in range(3)]
            query, key, val = (qkv[rows, spot] for spot in spots)
            given = attn[rows, at(pair, 128)]
            mask = bias[...] if start == 0 else jnp.where(keys[0:1, last:tokens] > 0, 0.0, -1e30)
            found = []
            for first in (True, False):
                lanes = head_lanes(first)
                chosen = jnp.where(lanes, query, jnp.zeros_like(query))
                mine = jnp.where(lanes, given, jnp.zeros_like(given))
                total = lane_at(side[rows, :], 2 * pair + (0 if first else 1))
                shares = jnp.exp(dot_nt(chosen, key) * 0.125 + mask - total)
                grad_share = dot_nt(mine, val)
                middle = jnp.sum(shares * grad_share, 1, keepdims=True)
                grad_score = (shares * (grad_share - middle)).astype(BF16)
                found.append(
                    (
                        dot_nn(grad_score, key) * 0.125,
                        dot_tn(grad_score, query) * 0.125,
                        dot_tn(shares.astype(BF16), given),
                    )
                )
            for i in range(3):
                qkv[rows, spots[i]] = jnp.where(head_lanes(True), found[0][i], found[1][i]).astype(BF16)

    each(HEADS // 2, attend_pair_back)
    put_out(qkv, gqkv_out)
    loads[0].wait()

    def project_back(index):
        grad[:, at(index, TILE)] = grad[:, at(index, TILE)] + dot_nt(qkv[...], qkv_w[at(index, TILE), :])

    each_unrolled(D // TILE, project_back)
    loads[6].wait()

    def norm_a_back(index, carry):
        gain, shift = carry
        rows = at(index, ROWS)
        inverse = lane_at(side[rows, :], 12)
        found, normed = grad[rows, :], na[rows, :]
        turned[:, rows] = layer_norm_back(found, normed, inverse, gains[5:6, :]).astype(BF16).T
        return gain + jnp.sum(found * normed, 0, keepdims=True), shift + jnp.sum(found, 0, keepdims=True)

    gain, shift = lax.fori_loop(0, tokens // ROWS, norm_a_back, (zero, zero))
    norm_out[0:1, :] = gain
    norm_out[1:2, :] = shift
    put_out(turned, ge_t)
    for copy in outs[1:]:
        copy.wait()


def backward(weights, slope, qkv, na, nb, grad, cols, keys, side, gains):
    tokens = grad.shape[0]
    vmem, hbm = pl.BlockSpec(memory_space=pltpu.VMEM), pl.BlockSpec(memory_space=pl.ANY)
    shape = jax.ShapeDtypeStruct
    loaded = tuple(weights) + (slope, qkv, na, nb, grad)
    widths = (D, D, 4 * D, D, 3 * D)
    return pl.pallas_call(
        backward_kernel,
        out_shape=[shape((4, D), F32), shape((D, tokens), BF16)]
        + [shape((tokens, width), BF16) for width in (D, 4 * D, D, 3 * D)],
        in_specs=[hbm] * 9 + [vmem] * 4,
        out_specs=[vmem] + [hbm] * 5,
        scratch_shapes=[pltpu.VMEM(member.shape, member.dtype) for member in loaded]
        + [
            pltpu.VMEM((tokens, D), BF16),
            pltpu.VMEM((tokens, D), BF16),
            pltpu.VMEM((tokens, 4 * D), BF16),
            pltpu.VMEM((tokens - SPAN, tokens - SPAN), F32),
            pltpu.VMEM((D, tokens), BF16),
            pltpu.SemaphoreType.DMA((9,)),
            pltpu.SemaphoreType.DMA((5,)),
        ],
        compiler_params=pltpu.CompilerParams(vmem_limit_bytes=60 * 1024 * 1024),
    )(*loaded, cols, keys, side, gains)


LEFT = 768
PIECES = ((Q_, 0, 1152), (E_, 0, 1280), (E_, 1280, 1280), (I_, 0, 1536), (D_, 0, 384), (O_, 0, 384))
Y_FIRST = (0, 1, 4)
TASKS = (
    0, 1, 96, 9, 4, 129, 97, 2, 103, 5, 99, 7, 8, 6, 101, 128, 102, 105,
    100, 132, 133, 64, 108, 12, 104, 136, 139, 134, 65, 15, 107, 111, 109, 137, 161, 13,
    160, 3, 131, 11, 141, 142, 70, 32, 68, 112, 110, 76, 140, 16, 168, 67, 144, 72,
    169, 75, 135, 71, 33, 36, 69, 143, 166, 173, 38, 98, 39, 43, 78, 130, 167, 73,
    37, 40, 79, 44, 34, 164, 46, 66, 77, 14, 47, 165, 45, 162, 171, 41, 172, 176,
    80, 138, 174, 74, 48, 10, 106, 42, 175, 35, 81, 145, 163, 170, 113, 17, 49, 177,
)


def reduce_kernel(*refs):
    given, (cols, norm_ab, norm_c, loss, squares) = refs[0:11], refs[11:16]
    y_t, ge_t, glog, x_t, gqkv, mix_t, gattn, a_t, gh, act_t, gffn = given
    lane_olds, side_olds, moment = refs[16:22], refs[22:28], refs[28]
    outs, sums_out, totals_out = refs[29:34], refs[34], refs[35]
    own, side, first, second, column, fin = (refs[36 + 6 * i : 42 + 6 * i] for i in range(6))
    left, (glog_v, gqkv_v, gattn_v, gh_v, gffn_v), stage, tails, norm_t = refs[72:79], refs[79:84], refs[84], refs[85], refs[86]
    spread, spread_small = refs[87:90], refs[90:93]
    load_sem, ring_sem, tail_sem, side_recv, first_send, first_recv, second_send, second_recv = refs[93:101]
    z_send, z_recv, swap_send, swap_recv = refs[101:105]
    sems, small_sems = refs[105:111], refs[111:117]
    z, y, x, c = here()
    peers = all_peers()
    me = chip(z, y, x)

    barrier = pltpu.get_barrier_semaphore()
    greeted = [peers[XWAY], peers[YWAY], peers[SIDE], device(z, 1 - y, 1 - x, c)]
    greeted += [device((z + 1 + i) % 4, y, x, c) for i in range(3)]
    for peer in greeted:
        pl.semaphore_signal(barrier, inc=1, device_id=peer, device_id_type=MESH)

    def act_part(group):
        return act_t.at[pl.ds(LEFT * group, LEFT), :]

    operands = (
        ((x_t, left[1]), (gqkv, gqkv_v)),
        ((y_t, left[2]), (ge_t, left[3]), (glog, glog_v)),
        (),
        ((a_t, left[0]), (gh, gh_v)),
        ((gffn, gffn_v), (act_part(0), left[5]), (act_part(1), left[6])),
        ((mix_t, left[4]), (gattn, gattn_v)),
    )
    loads = {}
    waited = set()
    for task in TASKS:
        piece = task // 32 if task // 32 != 2 else 1
        if piece not in loads:
            loads[piece] = []
            for source, target in operands[piece]:
                number = sum(len(member) for member in loads.values())
                loads[piece].append(pltpu.make_async_copy(source, target, load_sem.at[number]))
                loads[piece][-1].start()

    def loaded(piece):
        piece = 1 if piece == 2 else piece
        if piece not in waited:
            waited.add(piece)
            for member in loads[piece]:
                member.wait()

    norm_t[...] = jnp.zeros(norm_t.shape, F32)
    norm_t[5:9, :] = norm_ab[...]
    norm_t[9:11, :] = norm_c[...]
    pl.semaphore_wait(barrier, 7)

    def size_of(piece):
        return 2 * SHAPES[PIECES[piece][0]][0]

    def slot(ref, piece, index):
        size = size_of(piece)
        return ref[piece].at[pl.ds(pl.multiple_of(index * size, size), size), :]

    def half_of(piece):
        return SHAPES[PIECES[piece][0]][1] // 2

    def chosen(start):
        lane = lax.broadcasted_iota(jnp.int32, (1, TILE), 1) + start
        hit = (cols[:, 0:1] == lane) | (cols[:, 1:2] == lane)
        return jnp.where(hit, 1.0, 0.0).astype(BF16)

    def ring_copy(piece, rows, lanes, number, index):
        place = lax.rem(number, 3)
        return pltpu.make_async_remote_copy(
            src_ref=stage.at[place],
            dst_ref=side[piece].at[rows, lanes],
            send_sem=ring_sem.at[place],
            recv_sem=side_recv.at[piece, index],
            device_id=peers[SIDE],
            device_id_type=MESH,
        )

    def tail_copy(piece, rows, lanes, number, index):
        return pltpu.make_async_remote_copy(
            src_ref=tails.at[number],
            dst_ref=side[piece].at[rows, lanes],
            send_sem=tail_sem.at[number],
            recv_sem=side_recv.at[piece, index],
            device_id=peers[SIDE],
            device_id_type=MESH,
        )

    whole = pl.ds(0, LEFT)
    ring_count, tail_count = [0], [0]

    def give(piece, rows, lanes, number, index):
        def before():
            @pl.when(number >= 3)
            def _():
                ring_copy(piece, rows, lanes, number, index).wait_send()

        def write(value):
            stage[lax.rem(number, 3)] = value.astype(BF16)

        return before, write, lambda: ring_copy(piece, rows, lanes, number, index).start()

    def keep(piece, rows, lanes):
        def write(value):
            own[piece][rows, lanes] = value.astype(BF16)

        return lambda: None, write, lambda: None

    def plain(piece, mine, source, right, group):
        wide = PIECES[piece][2]
        half = c if mine else 1 - c
        rows = pl.ds(LEFT * group, LEFT)
        base = ring_count[0]

        def step(j):
            lanes = at(j, TILE)
            before, write, after = keep(piece, rows, lanes) if mine else give(
                piece, rows, lanes, base + j, group * (wide // TILE) + j
            )
            before()
            write(dot_nn(source[...], right[:, pl.ds(pl.multiple_of(half * wide + j * TILE, 128), TILE)]))
            after()

        each(wide // TILE, step)
        if not mine:
            ring_count[0] += wide // TILE
        if wide % TILE:
            start = wide - 128
            value = dot_nn(source[...], right[:, pl.ds(pl.multiple_of(half * wide + start, 128), 128)])
            if mine:
                own[piece][rows, start:wide] = value.astype(BF16)
            else:
                number = tail_count[0]
                tail_count[0] += 1
                groups = SHAPES[PIECES[piece][0]][0] // 24
                tails[number] = value.astype(BF16)
                tail_copy(piece, rows, pl.ds(start, 128), number, groups * (wide // TILE) + group).start()

    def wide_product(piece, mine):
        half = c if mine else 1 - c
        wide = half_of(piece)
        skip = PIECES[piece][1] // TILE
        base = ring_count[0]

        def both(j):
            start = pl.multiple_of(half * wide + (skip + j) * TILE, TILE)
            return dot_nn(left[2][...], glog_v[:, pl.ds(start, TILE)]) + dot_nn(left[3][...], chosen(start))

        def target(j):
            lanes = at(j, TILE)
            return keep(piece, whole, lanes) if mine else give(piece, whole, lanes, base + j, j)

        def step(j):
            before, write, after = target(j)
            before()
            write(both(j))
            after()

        if not mine:
            ring_count[0] += 5
        if skip == 0:
            each(5, step)
            return
        each(1, step)
        before, write, after = target(1)
        before()
        norm_part = jnp.where(half == 1, norm_t[...], 0.0).T
        write(both(1) + jnp.concatenate((norm_part, jnp.zeros((LEFT, TILE - 128), F32)), 1))
        after()
        for j in range(2, 5):
            before, write, after = target(j)
            before()

            @pl.when(half == 0)
            def _():
                write(both(j))

            @pl.when(half == 1)
            def _():
                if j == 2:
                    write(jnp.zeros((LEFT, TILE), F32))
                else:
                    write(dot_nn(left[3][...], chosen(half_of(piece) + (skip + j) * TILE)))

            after()

    def products(piece, mine):
        loaded(piece)
        if piece in (1, 2):
            wide_product(piece, mine)
        elif piece == 4:
            if not mine:
                for group in range(4):
                    source = left[5 + group % 2]
                    if group >= 2:
                        loads[piece][1 + group % 2].wait()
                    plain(piece, False, source, gffn_v, group)
                    plain(piece, True, source, gffn_v, group)
                    if group < 2:
                        again = pltpu.make_async_copy(act_part(group + 2), source, load_sem.at[12 + group])
                        again.start()
                        loads[piece][1 + group] = again
        else:
            source, right = {0: (left[1], gqkv_v), 3: (left[0], gh_v), 5: (left[4], gattn_v)}[piece]
            plain(piece, mine, source, right, 0)

    def combine(piece, target, parts):
        def some(rows, lanes):
            total = parts[0][rows, lanes].astype(F32)
            for member in parts[1:]:
                total = total + member[rows, lanes].astype(F32)
            target[rows, lanes] = total.astype(target.dtype)

        wide = PIECES[piece][2]
        if piece == 4:
            each(4, lambda group: some(at(group, 48), slice(0, wide)))
            return
        if wide >= 512:
            each(wide // 512, lambda j: some(slice(0, 48), at(j, 512)))
        if wide % 512:
            some(slice(0, 48), slice(wide // 512 * 512, wide))

    def hop(piece, k, land, index, sems, way):
        return pltpu.make_async_remote_copy(
            src_ref=slot(own, piece, k),
            dst_ref=slot(land, piece, index),
            send_sem=sems[0].at[piece, index],
            recv_sem=sems[1].at[piece, index],
            device_id=peers[way],
            device_id_type=MESH,
        )

    FIRST, SECOND = (first_send, first_recv), (second_send, second_recv)

    def landed(piece, land, index, sems):
        hop(piece, me, land, index, sems, XWAY).wait_recv()

    def block(piece, a, b, far):
        return chip(far, a, b) if piece in Y_FIRST else chip(far, b, a)

    def split(piece):
        return (y, x, YWAY, XWAY) if piece in Y_FIRST else (x, y, XWAY, YWAY)

    readied = set()

    def ready(piece):
        if piece in readied:
            return
        readied.add(piece)
        wide, groups = PIECES[piece][2], SHAPES[PIECES[piece][0]][0] // 24
        for group in range(groups):
            for j in range(wide // TILE):
                ring_copy(piece, pl.ds(LEFT * group, LEFT), at(j, TILE), 0, group * (wide // TILE) + j).wait_recv()
            if wide % TILE:
                index = groups * (wide // TILE) + group
                tail_copy(piece, pl.ds(LEFT * group, LEFT), pl.ds(wide - 128, 128), 0, index).wait_recv()

    def both_cores(piece, k):
        return (slot(own, piece, k), slot(side, piece, k))

    def first_block(piece, i):
        a, b, way, _ = split(piece)
        t, v = (z + i // 2) % 4, (1 - b) if i % 2 == 0 else b
        return block(piece, 1 - a, v, t), 2 * t + v, way

    def first_send_of(piece, i):
        ready(piece)
        k, index, way = first_block(piece, i)
        combine(piece, slot(own, piece, k), both_cores(piece, k))
        hop(piece, k, first, index, FIRST, way).start()

    def second_block(piece, i):
        a, b, _, way = split(piece)
        t = (z + i) % 4
        return block(piece, a, 1 - b, t), t, way

    def second_send_of(piece, i):
        k, t, way = second_block(piece, i)
        spot = 2 * t + 1 - split(piece)[1]
        landed(piece, first, spot, FIRST)
        combine(piece, slot(own, piece, k), both_cores(piece, k) + (slot(first, piece, spot),))
        hop(piece, k, second, t, SECOND, way).start()

    def z_copy(piece, i):
        t = (z + i) % 4
        return pltpu.make_async_remote_copy(
            src_ref=slot(own, piece, chip(t, y, x)),
            dst_ref=slot(column, piece, z),
            send_sem=z_send.at[piece, t],
            recv_sem=z_recv.at[piece, z],
            device_id=device(t, y, x, c),
            device_id_type=MESH,
        )

    def z_landed(piece, i):
        t = (z + i) % 4
        pltpu.make_async_remote_copy(
            src_ref=slot(own, piece, me),
            dst_ref=slot(column, piece, t),
            send_sem=z_send.at[piece, t],
            recv_sem=z_recv.at[piece, t],
            device_id=device(t, y, x, c),
            device_id_type=MESH,
        ).wait_recv()
        return slot(column, piece, t)

    def gathered(piece, t):
        spot = 2 * t + split(piece)[1]
        landed(piece, first, spot, FIRST)
        landed(piece, second, t, SECOND)
        return both_cores(piece, chip(t, y, x)) + (slot(first, piece, spot), slot(second, piece, t))

    def z_send_of(piece, i):
        t = (z + i) % 4
        combine(piece, slot(own, piece, chip(t, y, x)), gathered(piece, t))
        z_copy(piece, i).start()

    swaps = []

    def finish(piece):
        parts = gathered(piece, z)
        parts = parts + tuple(z_landed(piece, i) for i in (1, 2, 3))
        combine(piece, fin[piece], parts)
        m, skip, wide = PIECES[piece]
        size = SHAPES[m][0]
        lanes = pl.ds(pl.multiple_of(c * half_of(piece) + skip, 128), wide)
        swaps.append(
            pltpu.make_async_remote_copy(
                src_ref=fin[piece].at[pl.ds(pl.multiple_of((1 - c) * size, 8), size), :],
                dst_ref=outs[m].at[:, lanes],
                send_sem=swap_send.at[piece],
                recv_sem=swap_recv.at[piece],
                device_id=peers[SIDE],
                device_id_type=MESH,
            )
        )
        swaps[-1].start()
        outs[m][:, lanes] = fin[piece][pl.ds(pl.multiple_of(c * size, 8), size), :]

    for task in TASKS:
        piece, number = task // 32, task % 32
        if number < 2:
            products(piece, number == 1)
        elif number < 10:
            first_send_of(piece, number - 2)
        elif number < 14:
            second_send_of(piece, number - 10)
        elif number < 17:
            z_send_of(piece, number - 13)
        else:
            finish(piece)
    for piece in range(6):
        for i in range(8):
            k, index, way = first_block(piece, i)
            hop(piece, k, first, index, FIRST, way).wait_send()
        for i in range(4):
            k, t, way = second_block(piece, i)
            hop(piece, k, second, t, SECOND, way).wait_send()
        for i in (1, 2, 3):
            z_copy(piece, i).wait_send()
    for number in range(ring_count[0] - 3, ring_count[0]):
        ring_copy(1, whole, pl.ds(0, TILE), number, 0).wait_send()
    for number in range(tail_count[0]):
        tail_copy(1, whole, pl.ds(0, 128), number, 0).wait_send()
    for swap in swaps:
        swap.wait()

    sides, lanes, _, gs = statistics(outs, lane_olds, side_olds)
    scalars = lanes_of([jnp.sum(member, 0, keepdims=True) for member in sides] + [loss[...]])
    sums = jnp.concatenate(lanes + [scalars, squares[...]], 1)
    sums = sum_everywhere(sums, *spread, sems)
    sums_out[...] = sums
    updates = updates_of(sums, gs, sides, lane_olds, moment)[0]
    totals = lanes_of(
        [total_sum(update * update) for update in updates[:6]]
        + [jnp.sum(updates[6][i : i + 1] * updates[6][i : i + 1], 1, keepdims=True) for i in range(6)]
    )
    totals_out[...] = sum_everywhere(totals, *spread_small, small_sems)


def statistics(grads, lane_olds, side_olds):
    wide_g = grads[E_][...]
    gs = (wide_g[:, :VOCAB], wide_g[:, PLACE_AT:]) + tuple(grads[m][...] for m in (Q_, O_, I_, D_))
    gs = gs + (wide_g[:, 4096:4224],)
    decay = 1.0 - STEP ** (-0.8)
    sides, lanes = [], []
    wide_square = wide_g * wide_g + SQUARE_FLOOR
    squares = [wide_square[:, :VOCAB], wide_square[:, PLACE_AT:]] + [g * g + SQUARE_FLOOR for g in gs[2:6]]
    for index in range(6):
        mean = jnp.sum(squares[index], 1, keepdims=True) / squares[index].shape[1]
        sides.append(decay * column_of(as_row(side_olds[index])) + (1.0 - decay) * mean)
    lanes = [jnp.sum(square, 0, keepdims=True) for square in [wide_square] + squares[2:]]
    return sides, lanes, squares, gs


def updates_of(sums, gs, sides, lane_olds, moment):
    decay = 1.0 - STEP ** (-0.8)
    fresh = 1.0 - decay
    parts = [sums[:, :VOCAB], sums[:, PLACE_AT:WIDE]]
    parts += [sums[:, SUM_AT[i] : SUM_AT[i + 1]] for i in range(1, 5)]
    scalars = sums[:, SUM_AT[5] : SUM_AT[5] + 128]
    updates, lane_news = [], []
    for index in range(6):
        height = gs[index].shape[0] * 32
        lane_news.append(decay * as_row(lane_olds[index]) + fresh * (parts[index] / height))
        if index < 2:
            mean = jnp.sum(lane_news[index], 1, keepdims=True) / lane_news[index].shape[1]
        else:
            mean = lane_at(scalars, index) / height
        updates.append(gs[index] * lax.rsqrt(sides[index] * lane_news[index] / mean))
    norm_g = jnp.concatenate([row_of(lane_at(gs[6], NORM_AT - 4096 + i)) for i in range(6)], 0)
    moment_new = decay * moment[...] + fresh * (norm_g * norm_g + SQUARE_FLOOR)
    updates.append(norm_g * lax.rsqrt(moment_new))
    return updates, lane_news, norm_g, moment_new


def reduce_grads(large, small):
    tokens = large[2].shape[0]
    vmem, hbm = pl.BlockSpec(memory_space=pltpu.VMEM), pl.BlockSpec(memory_space=pl.ANY)
    dma = pltpu.SemaphoreType.DMA
    scratch = []
    for count in (16, 16, 8, 4, 4):
        scratch += [pltpu.VMEM((count * 2 * SHAPES[m][0], wide), BF16) for m, _, wide in PIECES]
    scratch += [pltpu.VMEM((2 * SHAPES[m][0], wide), F32) for m, _, wide in PIECES]
    scratch += [pltpu.VMEM((LEFT, tokens), BF16)] * 7
    scratch += [pltpu.VMEM((tokens, width), BF16) for width in (TABLE_END, 3 * D, D, 4 * D, D)]
    scratch += [pltpu.VMEM((3, LEFT, TILE), BF16), pltpu.VMEM((6, LEFT, 128), BF16), pltpu.VMEM((128, D), F32)]
    scratch += [pltpu.VMEM((count, 1, SUMS), F32) for count in (2, 4, 4)]
    scratch += [pltpu.VMEM((count, 1, 128), F32) for count in (2, 4, 4)]
    scratch += [dma((14,)), dma((3,)), dma((6,)), dma((6, 10)), dma((6, 8)), dma((6, 8)), dma((6, 4)), dma((6, 4))]
    scratch += [dma((6, 4)), dma((6, 4)), dma((6,)), dma((6,))]
    scratch += ([dma] * 2 + [dma((3,))] * 4) * 2
    return pl.pallas_call(
        reduce_kernel,
        out_shape=[jax.ShapeDtypeStruct(shape, F32) for shape in SHAPES + ((1, SUMS), (1, 128))],
        in_specs=[hbm] * 11 + [vmem] * len(small),
        out_specs=[vmem] * 7,
        scratch_shapes=scratch,
        compiler_params=pltpu.CompilerParams(
            collective_id=1, has_side_effects=True, vmem_limit_bytes=63 * 1024 * 1024
        ),
    )(*large, *small)


def update_kernel(*refs):
    copies = [pltpu.make_async_copy(refs[i], refs[55 + i], refs[82].at[i]) for i in range(27)]
    for copy in copies:
        copy.start()
    for copy in copies:
        copy.wait()
    refs = refs[55:82] + refs[27:55]
    grads, sums, totals, ws, norms = refs[0:5], refs[5], refs[6], refs[7:13], refs[13]
    lane_olds, side_olds, moment = refs[14:20], refs[20:26], refs[26]
    loss_out, table_g, place_g, norm_g_out = refs[27:31]
    lane_outs, side_outs, moment_out, news, norm_new = refs[31:37], refs[37:43], refs[43], refs[44:50], refs[50]
    grad_outs = refs[51:55]
    sides, _, _, gs = statistics(grads, lane_olds, side_olds)
    updates, lane_news, norm_g, moment_new = updates_of(sums[...], gs, sides, lane_olds, moment)
    scalars = sums[:, SUM_AT[5] : SUM_AT[5] + 128]
    squares = sums[:, SUM_AT[5] + 128 :]
    loss_out[...] = lane_at(scalars, 6)
    table_g[...] = gs[0]
    place_g[...] = gs[1]
    norm_g_out[...] = norm_g
    moment_out[...] = moment_new
    for index in range(6):
        lane_outs[index][...] = lane_news[index].reshape(lane_outs[index].shape)
        side_outs[index][...] = row_of(sides[index]).reshape(side_outs[index].shape)
        if index >= 2:
            grad_outs[index - 2][...] = gs[index]
        entries = gs[index].shape[0] * gs[index].shape[1] * 32
        clip = jnp.maximum(1.0, jnp.sqrt(lane_at(totals[...], index) / entries))
        scale = learn_rate * jnp.sqrt(lane_at(squares, index) / entries) / clip
        news[index][...] = ws[index][...] - scale * updates[index]
    for i in range(6):
        clip = jnp.maximum(1.0, jnp.sqrt(lane_at(totals[...], 6 + i) / D))
        scale = learn_rate * jnp.sqrt(lane_at(squares, 6 + i) / D) / clip
        norm_new[i : i + 1, :] = norms[i : i + 1, :] - scale * updates[6][i : i + 1, :]


def update_weights(operands):
    lanes = (VOCAB, 512, 3 * D, D, 4 * D, D)
    held = (24, 24, 24, 24, 24, 96)
    shapes = [(1, 1), (24, VOCAB), (24, 512), (6, 24)]
    shapes += [(lane,) for lane in lanes] + [(size,) for size in held] + [(6, 24)]
    shapes += list(zip(held, lanes)) + [(6, 24)] + list(zip(held, lanes))[2:]
    return pl.pallas_call(
        update_kernel,
        out_shape=[jax.ShapeDtypeStruct(shape, F32) for shape in shapes],
        in_specs=[pl.BlockSpec(memory_space=pl.ANY)] * len(operands),
        out_specs=[pl.BlockSpec(memory_space=pltpu.VMEM)] * len(shapes),
        scratch_shapes=[pltpu.VMEM(member.shape, member.dtype) for member in operands]
        + [pltpu.SemaphoreType.DMA((len(operands),))],
        compiler_params=pltpu.CompilerParams(vmem_limit_bytes=63 * 1024 * 1024),
    )(*operands)


def norm_forward(value, gain, shift):
    centred = value - jnp.mean(value, -1, keepdims=True)
    inverse = lax.rsqrt(jnp.mean(centred * centred, -1, keepdims=True) + EPSILON)
    normed = centred * inverse
    return (normed * gain + shift, normed, inverse)


def norm_backward(grad_out, normed, inverse, gain):
    scaled = grad_out * gain
    back = inverse * (
        scaled
        - jnp.mean(scaled, -1, keepdims=True)
        - normed * jnp.mean(scaled * normed, -1, keepdims=True)
    )
    return (back, jnp.sum(grad_out * normed, 0), jnp.sum(grad_out, 0))


def mm(left, right, sides):
    return lax.dot_general(left, right, ((sides[:1], sides[1:]), ((), ())), preferred_element_type=F32)


def attend(qkv, allowed):
    by_head = qkv.reshape(qkv.shape[0], 3, HEADS, HEAD_DIM)
    query, key, value = by_head[:, 0], by_head[:, 1], by_head[:, 2]
    scores = jnp.einsum("qhe,khe->hqk", query, key, preferred_element_type=F32) * 0.125
    scores = jnp.where(allowed[None], scores, -1e30)
    highest = jnp.max(scores, -1, keepdims=True)
    raised = jnp.exp(scores - highest)
    summed = jnp.sum(raised, -1, keepdims=True)
    shares = (raised / summed).astype(BF16)
    mixture = jnp.einsum("hqk,khe->qhe", shares, value, preferred_element_type=F32)
    return mixture.astype(BF16).reshape(qkv.shape[0], D), highest + jnp.log(summed)


def attend_back(qkv, allowed, log_total, grad_mix):
    by_head = qkv.reshape(qkv.shape[0], 3, HEADS, HEAD_DIM)
    query, key, value = by_head[:, 0], by_head[:, 1], by_head[:, 2]
    grad_mix = grad_mix.reshape(qkv.shape[0], HEADS, HEAD_DIM)
    scores = jnp.einsum("qhe,khe->hqk", query, key, preferred_element_type=F32) * 0.125
    scores = jnp.where(allowed[None], scores, -1e30)
    shares = jnp.exp(scores - log_total)
    grad_share = jnp.einsum("qhe,khe->hqk", grad_mix, value, preferred_element_type=F32)
    grad_score = (shares * (grad_share - jnp.sum(shares * grad_share, -1, keepdims=True))).astype(BF16)
    grad_query = jnp.einsum("hqk,khe->qhe", grad_score, key, preferred_element_type=F32) * 0.125
    grad_key = jnp.einsum("hqk,qhe->khe", grad_score, query, preferred_element_type=F32) * 0.125
    grad_value = jnp.einsum("hqk,qhe->khe", shares.astype(BF16), grad_mix, preferred_element_type=F32)
    return jnp.stack((grad_query, grad_key, grad_value), 1).astype(BF16).reshape(qkv.shape)


def on_slice(token_arrays, lengths, weights, lane_olds, side_olds, moment):
    olds = lane_olds + side_olds + (moment,)
    found = front(token_arrays + weights, lengths)
    loss_part, mask_count, gains, norm_c, side, cols, keys, weight_sq = found[0:8]
    x_t, mix_t, a_t, act_t, y_t, grad_logit, slope, qkv_b, normed_a, normed_b, grad_second = found[8:19]
    norm_ab, ge_t, grad_ffn, grad_hidden, grad_attn, grad_qkv = backward(
        found[19:23], slope, qkv_b, normed_a, normed_b, grad_second, cols, keys, side, gains
    )
    reduced = reduce_grads(
        (y_t, ge_t, grad_logit, x_t, grad_qkv, mix_t, grad_attn, a_t, grad_hidden, act_t, grad_ffn),
        (cols, norm_ab, norm_c, loss_part, weight_sq) + olds,
    )
    found = update_weights(tuple(reduced) + weights + olds)
    grads = (None,) + tuple(found[24:28])
    mask_count = mask_count.reshape(())
    loss_sum, table_g, place_g, norm_g = found[0:4]
    lane_news = found[4:10]
    side_news = found[10:16]
    moment_new, norm_new = found[16], found[23]
    news = found[17:23]
    return (
        loss_sum.reshape(()),
        mask_count,
        table_g.T,
        place_g.T,
        grads[1],
        grads[2],
        grads[3],
        grads[4],
        norm_g.T,
        lane_news[0],
        side_news[0],
        lane_news[1],
        side_news[1],
        side_news[2],
        lane_news[2],
        side_news[3],
        lane_news[3],
        side_news[4],
        lane_news[4],
        side_news[5],
        lane_news[5],
        moment_new.T,
        news[0].T,
        news[1].T,
        news[2],
        news[3],
        news[4],
        news[5],
        norm_new.T,
    )


def on_device(
    whole_mesh,
    long_ids,
    long_targets,
    long_mask,
    long_lengths,
    short_ids,
    short_targets,
    short_mask,
    short_lengths,
    table,
    position,
    qkv_weight,
    out_weight,
    in_weight,
    down_weight,
    norms,
    table_rows,
    table_cols,
    position_rows,
    position_cols,
    qkv_rows,
    qkv_cols,
    out_rows,
    out_cols,
    in_rows,
    in_cols,
    down_rows,
    down_cols,
    norm_moment,
):
    if whole_mesh == (8, 4):
        return on_slice(
            (long_ids, long_targets, long_mask, short_ids, short_targets, short_mask),
            (long_lengths, short_lengths),
            (table.T, position.T, qkv_weight, out_weight, in_weight, down_weight, norms.T),
            (table_rows, position_rows, qkv_cols, out_cols, in_cols, down_cols),
            (table_cols, position_cols, qkv_rows, out_rows, in_rows, down_rows),
            norm_moment.T,
        )
    devices = lax.axis_size(("dp", "seq"))
    seq_index = lax.axis_index("seq")
    held = norms.shape[0]

    span = long_ids.shape[1]
    long_place = seq_index * span + lax.iota(jnp.int32, span)
    long_keep = (long_place[None, :] < long_lengths[:, None]).astype(jnp.int32)
    short_keep = (lax.iota(jnp.int32, SPAN)[None, :] < short_lengths[:, None]).astype(jnp.int32)
    long_pack = jnp.stack((long_ids, long_targets, long_mask * long_keep, long_keep), 1)
    short_pack = jnp.stack((short_ids, short_targets, short_mask * short_keep, short_keep), 1)
    moved = lax.all_to_all(
        jnp.concatenate((long_pack, short_pack[1:]), 0), "seq", split_axis=0, concat_axis=0, tiled=True
    )
    tokens = jnp.concatenate((moved, short_pack[:1]), 0)
    ids, targets, weight, keep = (tokens[:, i].reshape(-1) for i in range(4))
    weight = weight.astype(F32)
    count = tokens.shape[0] * span
    last = count - span
    alone = seq_index == lax.axis_size("seq") - 1
    token = lax.iota(jnp.int32, count)
    place = jnp.where(alone | (token >= last), token % span, token)
    row = jnp.where(alone | (token >= last), token // span, 0)
    allowed_long = (row[:last, None] == row[None, :last]) & (keep[None, :last] > 0)
    allowed_short = jnp.broadcast_to(keep[None, last:] > 0, (span, span))

    here_count = jnp.sum(long_pack[:, 2]) + jnp.sum(short_pack[:, 2])
    tall = table.T
    counts = jnp.broadcast_to(jnp.stack((here_count // 256, here_count % 256)).astype(F32)[None], (held, 2))
    wide_shard = jnp.concatenate(
        (tall, norms, counts, jnp.zeros((held, PLACE_AT - COUNT_AT - 2), F32), position.T), 1
    )
    shards = (wide_shard, qkv_weight, out_weight, in_weight, down_weight)
    wide_w, qkv_w, out_w, in_w, down_w = (
        lax.all_gather(shard.astype(BF16), ("dp", "seq"), axis=0, tiled=True) for shard in shards
    )
    column = lax.broadcasted_iota(jnp.int32, (1, WIDE), 1)
    chosen = ((ids[:, None] == column) | ((place[:, None] + PLACE_AT) == column)).astype(BF16)
    gains = wide_w[:, NORM_AT : NORM_AT + 6].astype(F32)
    sums = jnp.sum(wide_w[:, COUNT_AT : COUNT_AT + 2].astype(F32), 0)
    mask_count = (sums[0] * 256.0 + sums[1]) / held
    inverse_count = 1.0 / mask_count

    embedded = mm(chosen, wide_w, (1, 1))
    first, normed_a, inverse_a = norm_forward(embedded, gains[:, 0], gains[:, 1])
    first_b = first.astype(BF16)
    qkv_b = mm(first_b, qkv_w, (1, 0)).astype(BF16)
    mix_long, total_long = attend(qkv_b[:last], allowed_long)
    mix_short, total_short = attend(qkv_b[last:], allowed_short)
    mixture = jnp.concatenate((mix_long, mix_short), 0)
    second, normed_b, inverse_b = norm_forward(first + mm(mixture, out_w, (1, 0)), gains[:, 2], gains[:, 3])
    second_b = second.astype(BF16)
    hidden = mm(second_b, in_w, (1, 0))
    active, slope = gelu_pair(hidden)
    active_b = active.astype(BF16)
    third, normed_c, inverse_c = norm_forward(second + mm(active_b, down_w, (1, 0)), gains[:, 4], gains[:, 5])
    third_b = third.astype(BF16)
    logits = jnp.where(column < VOCAB, mm(third_b, wide_w, (1, 0)), -1e30)
    highest = jnp.max(logits, -1, keepdims=True)
    log_sum = highest + jnp.log(jnp.sum(jnp.exp(logits - highest), -1, keepdims=True))
    onehot = targets[:, None] == column
    picked = jnp.sum(jnp.where(onehot, logits, 0.0), -1)
    loss_part = jnp.sum(weight * (log_sum[:, 0] - picked))
    grad_logit = (
        (jnp.exp(logits - log_sum) - onehot.astype(F32)) * (weight * inverse_count)[:, None]
    ).astype(BF16)
    grad_third = mm(grad_logit, wide_w, (1, 1))
    grad_second, gain_c, shift_c = norm_backward(grad_third, normed_c, inverse_c, gains[:, 4])
    grad_ffn = grad_second.astype(BF16)
    down_grad = mm(active_b, grad_ffn, (0, 0)).astype(BF16)
    grad_hidden = (mm(grad_ffn, down_w, (1, 1)) * slope).astype(BF16)
    in_grad = mm(second_b, grad_hidden, (0, 0)).astype(BF16)
    grad_second = grad_second + mm(grad_hidden, in_w, (1, 1))
    grad_first, gain_b, shift_b = norm_backward(grad_second, normed_b, inverse_b, gains[:, 2])
    grad_attn = grad_first.astype(BF16)
    out_grad = mm(mixture, grad_attn, (0, 0)).astype(BF16)
    grad_mix = mm(grad_attn, out_w, (1, 1)).astype(BF16)
    grad_qkv = jnp.concatenate(
        (
            attend_back(qkv_b[:last], allowed_long, total_long, grad_mix[:last]),
            attend_back(qkv_b[last:], allowed_short, total_short, grad_mix[last:]),
        ),
        0,
    )
    qkv_grad = mm(first_b, grad_qkv, (0, 0)).astype(BF16)
    grad_first = grad_first + mm(grad_qkv, qkv_w, (1, 1))
    grad_embed, gain_a, shift_a = norm_backward(grad_first, normed_a, inverse_a, gains[:, 0])
    wide_grad = mm(
        jnp.concatenate((third_b, grad_embed.astype(BF16)), 0),
        jnp.concatenate((grad_logit, chosen), 0),
        (0, 0),
    )
    norm_part = jnp.stack((gain_a, shift_a, gain_b, shift_b, gain_c, shift_c), 1)
    wide_grad = lax.dynamic_update_slice(wide_grad.astype(BF16), norm_part.astype(BF16), (0, NORM_AT))
    grads = (wide_grad, qkv_grad, out_grad, in_grad, down_grad)
    wide_g, qkv_g, out_g, in_g, down_g = (
        lax.psum_scatter(grad.astype(F32), ("dp", "seq"), scatter_dimension=0, tiled=True) for grad in grads
    )
    table_g, place_g = wide_g[:, :VOCAB], wide_g[:, PLACE_AT:]
    norm_g = wide_g[:, NORM_AT : NORM_AT + 6]

    decay = 1.0 - STEP ** (-0.8)
    matrices = (
        (qkv_weight, qkv_g, qkv_rows, qkv_cols),
        (out_weight, out_g, out_rows, out_cols),
        (in_weight, in_g, in_rows, in_cols),
        (down_weight, down_g, down_rows, down_cols),
    )
    wide = (
        (tall, table_g, table_cols, table_rows),
        (position.T, place_g, position_cols, position_rows),
    )
    row_news = [
        decay * member[2] + (1.0 - decay) * jnp.mean(member[1] * member[1] + SQUARE_FLOOR, 1)
        for member in matrices + wide
    ]
    col_parts = [jnp.sum(member[1] * member[1] + SQUARE_FLOOR, 0) for member in matrices + wide]
    row_totals = jnp.stack([jnp.sum(rows_new) for rows_new in row_news])
    weight_sq = jnp.stack([jnp.sum(member[0] * member[0]) for member in matrices + wide])
    stats = lax.psum(
        col_parts + [row_totals, weight_sq, jnp.sum(norms * norms, 0), loss_part.reshape(1)], ("dp", "seq")
    )
    updates = []
    cols_out = []
    for index, member in enumerate(matrices + wide):
        full_rows = member[0].shape[0] * devices
        cols_new = decay * member[3] + (1.0 - decay) * stats[index] / full_rows
        if index < 4:
            mean = stats[6][index] / full_rows
        else:
            mean = jnp.mean(cols_new)
        updates.append(member[1] * lax.rsqrt(row_news[index][:, None] * cols_new[None, :] / mean))
        cols_out.append(cols_new)
    moment_new = decay * norm_moment + (1.0 - decay) * (norm_g * norm_g + SQUARE_FLOOR)
    norm_update = norm_g * lax.rsqrt(moment_new)
    update_sq = jnp.stack([jnp.sum(update * update) for update in updates])
    totals = lax.psum((update_sq, jnp.sum(norm_update * norm_update, 0)), ("dp", "seq"))
    news = []
    for index, member in enumerate(matrices + wide):
        entries = member[0].shape[0] * member[0].shape[1] * devices
        clip = jnp.maximum(1.0, jnp.sqrt(totals[0][index] / entries))
        news.append(
            member[0] - learn_rate * jnp.sqrt(stats[7][index] / entries) * updates[index] / clip
        )
    norm_rows = norms.shape[0] * devices
    norm_clip = jnp.maximum(1.0, jnp.sqrt(totals[1] / norm_rows))
    norm_new = norms - learn_rate * jnp.sqrt(stats[8] / norm_rows) * norm_update / norm_clip
    return (
        stats[9][0],
        mask_count,
        table_g.T,
        place_g.T,
        qkv_g,
        out_g,
        in_g,
        down_g,
        norm_g,
        cols_out[4],
        row_news[4],
        cols_out[5],
        row_news[5],
        row_news[0],
        cols_out[0],
        row_news[1],
        cols_out[1],
        row_news[2],
        cols_out[2],
        row_news[3],
        cols_out[3],
        moment_new,
        news[4].T,
        news[5].T,
        news[0],
        news[1],
        news[2],
        news[3],
        norm_new,
    )


def solution(mesh):
    split, wide = P(("dp", "seq"), None), P(None, ("dp", "seq"))
    shard, same = P(("dp", "seq")), P()
    return jax.shard_map(
        functools.partial(on_device, (mesh.shape["dp"], mesh.shape["seq"])),
        mesh=mesh,
        in_specs=(P("dp", "seq"),) * 3
        + (P("dp"),)
        + (split,) * 3
        + (shard,)
        + (wide,) * 2
        + (split,) * 5
        + (same, shard) * 2
        + (shard, same) * 4
        + (split,),
        out_specs=(same, same)
        + (wide,) * 2
        + (split,) * 5
        + (same, shard) * 2
        + (shard, same) * 4
        + (split,)
        + (wide,) * 2
        + (split,) * 5,
        check_vma=False,
    )
```

```python
import functools

import jax
import jax.numpy as jnp
from jax import lax
from jax.experimental import pallas as pl
from jax.experimental.pallas import tpu as pltpu
from jax.sharding import PartitionSpec as P

D = 768
HEADS = 12
HEAD_DIM = 64
VOCAB = 4101
STEP = 10
SPAN = 128

EPSILON = 1e-12
SQUARE_FLOOR = 1e-30
learn_rate = 0.3

MESH = pl.DeviceIdType.MESH
F32 = jnp.float32
BF16 = jnp.bfloat16

NORM_AT = VOCAB
COUNT_AT = VOCAB + 6
TABLE_END = 4352
PLACE_AT = 4608
WIDE = PLACE_AT + 512

SHAPES = ((24, WIDE), (24, 3 * D), (24, D), (24, 4 * D), (96, D))
E_, Q_, O_, I_, D_ = range(5)
CLASS_A, CLASS_B, CLASS_C = (E_, O_), (Q_, D_), (I_,)
UP, DOWN, XWAY, YWAY, SIDE = range(5)


def here():
    dp, seq = lax.axis_index("dp"), lax.axis_index("seq")
    return dp // 2, dp % 2, seq // 2, seq % 2


def device(z, y, x, c):
    return {"dp": z * 2 + y, "seq": x * 2 + c}


def chip(z, y, x):
    return z * 4 + y * 2 + x


def all_peers():
    z, y, x, c = here()
    return (
        device(z + 1, y, x, c),
        device(z - 1, y, x, c),
        device(z, y, 1 - x, c),
        device(z, 1 - y, x, c),
        device(z, y, x, 1 - c),
    )


SUM_AT = (0, WIDE, WIDE + 3 * D, WIDE + 4 * D, WIDE + 8 * D, WIDE + 9 * D)
SUMS = WIDE + 9 * D + 256


def lanes_of(members):
    lane = lax.broadcasted_iota(jnp.int32, (1, 128), 1)
    row = jnp.zeros((1, 128), F32)
    for index, member in enumerate(members):
        row = jnp.where(lane == index, member, row)
    return row


def lane_at(row, index):
    lane = lax.broadcasted_iota(jnp.int32, row.shape, 1)
    return jnp.sum(jnp.where(lane == index, row, 0.0), 1, keepdims=True)


def column_of(row):
    size = row.shape[1]
    diagonal = lax.broadcasted_iota(jnp.int32, (size, size), 0) == lax.broadcasted_iota(
        jnp.int32, (size, size), 1
    )
    return jnp.sum(jnp.where(diagonal, row, 0.0), 1, keepdims=True)


def row_of(column):
    size = column.shape[0]
    diagonal = lax.broadcasted_iota(jnp.int32, (size, size), 0) == lax.broadcasted_iota(
        jnp.int32, (size, size), 1
    )
    return jnp.sum(jnp.where(diagonal, column, 0.0), 0, keepdims=True)


def as_row(ref):
    return ref[...].reshape(1, ref.shape[0])


def total_sum(array):
    return jnp.sum(jnp.sum(array, 1, keepdims=True), 0, keepdims=True)


def sum_everywhere(value, first, second, third, sems):
    z, y, x, c = here()
    spot = y * 2 + x
    side_send, side_recv, plane_send, plane_recv, z_send, z_recv = sems

    def copy(src, dst, send, recv, peer):
        return pltpu.make_async_remote_copy(
            src_ref=src, dst_ref=dst, send_sem=send, recv_sem=recv, device_id=peer, device_id_type=MESH
        )

    first[0] = value
    swap = copy(first.at[0], first.at[1], side_send, side_recv, device(z, y, x, 1 - c))
    swap.start()
    swap.wait_recv()
    second[spot] = first[0] + first[1]
    plane = []
    for i, (to_y, to_x) in enumerate(((y, 1 - x), (1 - y, x), (1 - y, 1 - x))):
        plane.append(
            copy(second.at[spot], second.at[spot], plane_send.at[i], plane_recv.at[i], device(z, to_y, to_x, c))
        )
        plane[i].start()
    for member in plane:
        member.wait_recv()
    third[z] = (second[0] + second[1]) + (second[2] + second[3])
    column = []
    for i in range(3):
        to_z = (z + 1 + i) % 4
        column.append(copy(third.at[z], third.at[z], z_send.at[i], z_recv.at[i], device(to_z, y, x, c)))
        column[i].start()
    for member in column:
        member.wait_recv()
    for member in [swap] + plane + column:
        member.wait_send()
    return (third[0] + third[1]) + (third[2] + third[3])


def gelu_pair(hidden):
    normal_cdf = 0.5 * (1.0 + lax.erf(hidden * 0.7071067811865476))
    return (
        hidden * normal_cdf,
        normal_cdf + hidden * jnp.exp(-0.5 * hidden * hidden) * 0.3989422804014327,
    )


def dot_nn(left, right):
    return jnp.dot(left, right, preferred_element_type=F32)


def dot_nt(left, right):
    return lax.dot_general(left, right, (((1,), (1,)), ((), ())), preferred_element_type=F32)


def dot_tn(left, right):
    return lax.dot_general(left, right, (((0,), (0,)), ((), ())), preferred_element_type=F32)


def at(index, size):
    if isinstance(index, int):
        return pl.ds(index * size, size)
    return pl.ds(pl.multiple_of(index * size, size), size)


def each(count, body):
    def step(index, carry):
        body(index)
        return carry

    lax.fori_loop(0, count, step, 0)


def each_unrolled(count, body):
    for index in range(count):
        body(index)


ROWS = 128
TILE = 256
HALF = 320
TABLE_TILES = TABLE_END // TILE


def head_lanes(first):
    lane = lax.broadcasted_iota(jnp.int32, (1, 128), 1)
    return (lane < HEAD_DIM) if first else (lane >= HEAD_DIM)


def layer_norm(value, gain, shift):
    centred = value - jnp.sum(value, 1, keepdims=True) / D
    inverse = lax.rsqrt(jnp.sum(centred * centred, 1, keepdims=True) / D + EPSILON)
    normed = centred * inverse
    return normed * gain + shift, normed, inverse


def layer_norm_back(grad, normed, inverse, gain):
    scaled = grad * gain
    return inverse * (
        scaled - jnp.sum(scaled, 1, keepdims=True) / D - normed * (jnp.sum(scaled * normed, 1, keepdims=True) / D)
    )


def put_lane(ref, rows, index, value):
    lane = lax.broadcasted_iota(jnp.int32, (1, 128), 1)
    ref[rows, :] = jnp.where(lane == index, value, ref[rows, :])


def set_bias(bias, cols, keys, last):
    same = cols[0:last, 4:5] == keys[1:2, 0:last]
    bias[...] = jnp.where(same & (keys[0:1, 0:last] > 0), 0.0, -1e30)


CHOOSE, EMBED, NORM_A, PROJECT, TURN_X, ATTEND, OUT, NORM_B, FEED_IN, TURN_A, FEED_OUT, REST = range(12)
FRONT = (
    67, 35, 36, 66, 32, 64, 100, 131, 1000, 69, 39, 1, 108, 161, 68, 33, 164, 73, 34, 4,
    99, 65, 71, 43, 50, 40, 75, 38, 3, 130, 162, 163, 160, 37, 6, 79, 172, 2, 0, 70,
    46, 96, 8, 76, 98, 166, 165, 44, 41, 169, 83, 42, 80, 74, 97, 175, 72, 47, 5, 129,
    78, 13, 170, 48, 10, 7, 168, 1001, 45, 132, 16, 104, 51, 82, 81, 49, 77, 174, 12, 1016,
    1017, 1018, 128, 18, 9, 11, 102, 1019, 1020, 1021, 103, 17, 1032, 177, 15, 14, 19, 173, 101, 167,
    109, 176, 135, 136, 1048, 1049, 1050, 1051, 1052, 1053, 1054, 1055, 133, 1056, 1064, 1080, 107, 1081, 171, 1082,
    106, 114, 1083, 105, 112, 1084, 178, 137, 134, 146, 179, 115, 142, 1085, 113, 141, 140, 1096, 1097, 1098,
    110, 111, 139, 1112, 1128, 1129, 1130, 138, 1131, 1132, 1133, 1134, 1135, 1136, 147, 144, 143, 145, 1137, 1138,
    1139, 1160, 1161, 1162, 1176,
)


def front_hooks():
    hooks, before = {}, []
    for task in FRONT:
        if task < 1000:
            before.append(task)
        else:
            hooks[((task - 1000) // 16, (task - 1000) % 16)] = before
            before = []
    return hooks


def front_kernel(*refs):
    raw, (long_len, short_len) = refs[0:13], refs[13:15]
    count_out, gains_out, side, cols, keys, squares = refs[15:21]
    x_t, mix_out, a_out, act_out, y_out, slope_out, qkv_out, na_out = refs[21:29]
    nb_outs, nc_outs, weight_outs = refs[29:31], refs[31:33], refs[33:38]
    wide, qkv_w, out_w, in_w, down_w = weights = refs[38:43]
    value, na, low_a, low_y, mix, qkv, act, slope, pick, pick_two, bias, turned = refs[43:55]
    nb, nc = refs[55:57], refs[57:59]
    held, wide_shard, merge, pieces, land = refs[59:72], refs[72], refs[73:78], refs[78], refs[79]
    raw_sem, swap_send, swap_recv, token_send, token_recv, send_sem, link_recv, side_recv = refs[80:88]
    out_sem, turn_sem = refs[88:90]
    z, y, x, c = here()
    peers = all_peers()
    me = chip(z, y, x)
    seq = x * 2 + c
    alone = seq // 3
    tokens = value.shape[0]
    last = tokens - SPAN
    hooks = front_hooks()

    barrier = pltpu.get_barrier_semaphore()
    cross = device(z, y, 1 - x, 1 - c)
    column = [device((z + 1 + i) % 4, y, x, c) for i in range(3)]
    for peer in [peers[XWAY], peers[YWAY], peers[SIDE], cross] + column:
        pl.semaphore_signal(barrier, inc=1, device_id=peer, device_id_type=MESH)
    raws = [pltpu.make_async_copy(raw[i], held[i], raw_sem.at[i]) for i in range(13)]
    for member in raws:
        member.start()
    for member in raws:
        member.wait()
    long_ids, long_targets, long_mask, short_ids, short_targets, short_mask, tall, place, qkv_s, out_s, in_s, down_s, norms = held

    pieces[...] = jnp.zeros(pieces.shape, jnp.int32)
    land[4] = jnp.zeros((8, SPAN), jnp.int32)
    lane = lax.broadcasted_iota(jnp.int32, (1, SPAN), 1)
    count = jnp.zeros((1, SPAN), jnp.int32)
    for t in range(5):
        if t < 3:
            ids, targets, mask = long_ids[t : t + 1, :], long_targets[t : t + 1, :], long_mask[t : t + 1, :]
            keep = (lane + seq * SPAN < long_len[t]).astype(jnp.int32)
        else:
            row = (1, 0)[t - 3]
            ids, targets, mask = (member[row : row + 1, :] for member in (short_ids, short_targets, short_mask))
            keep = (lane < short_len[row]).astype(jnp.int32)
        target = pieces.at[t] if t < 4 else land.at[4]
        target[0:1, :] = ids
        target[2:3, :] = targets
        target[3:4, :] = mask * keep
        target[5:6, :] = keep
        count = count + mask * keep
    count = jnp.sum(count.astype(F32), 1, keepdims=True)
    high = jnp.floor(count * (1.0 / 256.0))

    wide_shard[:, 0:4096] = tall[:, 0:4096]
    edge = jnp.zeros((24, 128), F32)
    tile_lane = lax.broadcasted_iota(jnp.int32, (24, 128), 1)
    tall_edge = tall[:, 4096:VOCAB]
    members = [lane_at(tall_edge, i) for i in range(VOCAB - 4096)]
    members += [column_of(norms[i : i + 1, :]) for i in range(6)]
    members += [high, count - high * 256.0]
    for i, member in enumerate(members):
        edge = jnp.where(tile_lane == i, member, edge)
    wide_shard[:, 4096:4224] = edge
    wide_shard[:, 4224:PLACE_AT] = jnp.zeros((24, PLACE_AT - 4224), F32)
    wide_shard[:, PLACE_AT:] = place[...]
    shards = (wide_shard, qkv_s, out_s, in_s, down_s)

    pl.semaphore_wait(barrier, 7)
    swaps = []
    for m in (E_, Q_, I_, D_, O_):
        size, half = SHAPES[m][0], SHAPES[m][1] // 2
        swaps.append(
            pltpu.make_async_remote_copy(
                src_ref=shards[m].at[:, pl.ds(pl.multiple_of((1 - c) * half, 128), half)],
                dst_ref=merge[m].at[pl.ds(pl.multiple_of(c * size, 8), size), :],
                send_sem=swap_send.at[m],
                recv_sem=swap_recv.at[m],
                device_id=peers[SIDE],
                device_id_type=MESH,
            )
        )
        swaps[-1].start()
    token_copies = []
    for i, (to_x, to_c) in enumerate(((x, 1 - c), (1 - x, c), (1 - x, 1 - c))):
        token_copies.append(
            pltpu.make_async_remote_copy(
                src_ref=pieces.at[to_x * 2 + to_c],
                dst_ref=land.at[seq],
                send_sem=token_send.at[i],
                recv_sem=token_recv.at[i],
                device_id=device(z, y, to_x, to_c),
                device_id_type=MESH,
            )
        )
        token_copies[-1].start()
    land[seq] = pieces[seq]

    def part(piece, k, half):
        m, skip, wide_part = PIECES[piece]
        size = 2 * SHAPES[m][0]
        start = pl.multiple_of(half * (SHAPES[m][1] // 2) + skip, 128)
        return weights[m].at[pl.ds(pl.multiple_of(k * size, size), size), pl.ds(start, wide_part)]

    FIRST_WAY, SECOND_WAY, SIDE_WAY = 0, 1, 2

    def copy_of(piece, k, way):
        ways = (XWAY, YWAY) if piece in Y_FIRST else (YWAY, XWAY)
        peer = column[way - 3] if way > 2 else peers[SIDE] if way == SIDE_WAY else peers[ways[way]]
        return pltpu.make_async_remote_copy(
            src_ref=part(piece, k, c),
            dst_ref=part(piece, k, c),
            send_sem=send_sem.at[piece, k, way],
            recv_sem=(side_recv if way == SIDE_WAY else link_recv).at[piece, k],
            device_id=peer,
            device_id_type=MESH,
        )

    def block_of(number):
        piece, task = number // 32, number % 32
        last_y = piece in Y_FIRST
        if task < 5:
            return piece, me, (3 + task if task < 3 else FIRST_WAY if task == 3 else SECOND_WAY,), False
        if task < 8:
            return piece, chip((z + task - 4) % 4, y, x), (FIRST_WAY, SECOND_WAY, SIDE_WAY), True
        if task < 12:
            t = (z + task - 8) % 4
            return piece, chip(t, y, 1 - x) if last_y else chip(t, 1 - y, x), (SECOND_WAY, SIDE_WAY), True
        t, other = (z + (task - 12) // 2) % 4, (task - 12) % 2
        if last_y:
            return piece, chip(t, 1 - y, 1 - x if other else x), (SIDE_WAY,), True
        return piece, chip(t, 1 - y if other else y, 1 - x), (SIDE_WAY,), True

    def transfer(number):
        piece, k, ways, waits = block_of(number)
        if waits:
            copy_of(piece, k, FIRST_WAY).wait_recv()
        for way in ways:
            copy_of(piece, k, way).start()

    def before(step, index, base=0):
        for (name, part_index), tasks in hooks.items():
            part_index = part_index - base
            if name != step or not tasks or (step == EMBED and not 0 <= part_index < 3):
                continue
            if index is None or isinstance(index, int):
                if part_index == (index or 0):
                    for number in tasks:
                        transfer(number)
            else:

                @pl.when(index == part_index)
                def _(tasks=tasks):
                    for number in tasks:
                        transfer(number)

    def need(*wanted):
        for piece in wanted:
            for k in range(16):
                pltpu.make_async_remote_copy(
                    src_ref=part(piece, k, 1 - c),
                    dst_ref=part(piece, k, 1 - c),
                    send_sem=send_sem.at[piece, k, SIDE_WAY],
                    recv_sem=side_recv.at[piece, k],
                    device_id=peers[SIDE],
                    device_id_type=MESH,
                ).wait_recv()

    for number, m in enumerate((E_, Q_, I_, D_, O_)):
        swaps[number].wait_recv()
        size, half = SHAPES[m][0], SHAPES[m][1] // 2
        merge[m][pl.ds(pl.multiple_of(c * size, 8), size), :] = shards[m][:, pl.ds(pl.multiple_of(c * half, 128), half)]
        rows = pl.ds(pl.multiple_of(me * 2 * size, 2 * size), 2 * size)
        weights[m][rows, pl.ds(pl.multiple_of(c * half, 128), half)] = merge[m][...].astype(BF16)
        for piece in range(6):
            if PIECES[piece][0] == m:
                copy_of(piece, me, SIDE_WAY).start()
    for copy in token_copies:
        copy.wait_recv()
    side[...] = jnp.zeros(side.shape, F32)
    keys[...] = jnp.zeros(keys.shape, jnp.int32)
    zeros = jnp.zeros((1, SPAN), F32)
    for b in range(5):
        tile = land[b]
        shift = b * SPAN * (1 - alone) if b < 4 else 0
        row = b * alone if b < 4 else 4
        spot = (lane + shift + PLACE_AT).astype(F32)
        row_lane = (lane * 0 + row).astype(F32)
        ids, targets, weight = (tile[i : i + 1].astype(F32) for i in (0, 2, 3))
        stacked = jnp.concatenate((ids, spot, targets, weight, row_lane, zeros, zeros, zeros), 0)
        stacked = jnp.concatenate((stacked, jnp.zeros((120, SPAN), F32)), 0)
        cols[b * SPAN : (b + 1) * SPAN, :] = stacked.T.astype(jnp.int32)
        keys[0:1, b * SPAN : (b + 1) * SPAN] = tile[5:6]
        keys[1:2, b * SPAN : (b + 1) * SPAN] = lane * 0 + row
        keys[2:4, b * SPAN : (b + 1) * SPAN] = tile[2:4]
    set_bias(bias, cols, keys, last)
    found = [total_sum(member[...] * member[...]) for member in (tall, place, qkv_s, out_s, in_s, down_s)]
    norm_squares = jnp.sum(norms[...] * norms[...], 1, keepdims=True)
    squares[...] = lanes_of(found + [norm_squares[i : i + 1] for i in range(6)])

    turns, outs = {}, {}

    def turn_out(source, target, slot):
        if slot in turns:
            turns[slot].wait()

        def some(index):
            turned[slot, :, at(index, ROWS)] = source[at(index, ROWS), :].T

        each(tokens // ROWS, some)
        turns[slot] = pltpu.make_async_copy(turned.at[slot], target, turn_sem.at[slot])
        turns[slot].start()

    def put_out(name, source, target):
        outs[name] = pltpu.make_async_copy(source, target, out_sem.at[len(outs)])
        outs[name].start()

    picks = (pick, pick_two)
    halves = [pl.ds(half * HALF, HALF) for half in range(2)]
    for half in range(2):

        def choose(index):
            column_lane = lax.broadcasted_iota(jnp.int32, (1, TILE), 1) + index * TILE
            hit = (cols[halves[half], 0:1] == column_lane) | (cols[halves[half], 1:2] == column_lane)
            picks[half][:, at(index, TILE)] = jnp.where(hit, 1.0, 0.0).astype(BF16)

        before(CHOOSE, half)
        each(WIDE // TILE, choose)

    before(EMBED, 0)
    hooks.pop((EMBED, 0))
    need(1, 2)
    put_out("wide", wide, weight_outs[4])
    for half in range(2):

        def embed(index):
            before(EMBED, index, half * 3)
            value[halves[half], at(index, TILE)] = dot_nt(picks[half][...], wide[at(index, TILE), :])

        each_unrolled(D // TILE, embed)

    gains = wide[:, 4096:4224].astype(F32).T
    gains_out[...] = gains[0:16]
    counts = jnp.sum(gains[11:13], 1, keepdims=True) / 24.0
    mask_count = counts[0:1] * 256.0 + counts[1:2]
    count_out[...] = mask_count
    norm_rows = [gains_out[5 + i : 6 + i, :] for i in range(6)]
    before(NORM_A, None)

    def norm_a(index):
        rows = at(index, ROWS)
        found, normed, inverse = layer_norm(value[rows, :], norm_rows[0], norm_rows[1])
        value[rows, :] = found
        low_a[rows, :] = found.astype(BF16)
        na[rows, :] = normed
        put_lane(side, rows, 12, inverse)

    each(tokens // ROWS, norm_a)
    put_out("na", na, na_out)
    before(PROJECT, 0)
    need(0)

    def project(index):
        before(PROJECT, index)
        qkv[:, at(index, TILE)] = dot_nn(low_a[...], qkv_w[:, at(index, TILE)]).astype(BF16)

    hooks.pop((PROJECT, 0))
    each_unrolled(3 * D // TILE, project)
    put_out("qkv", qkv, qkv_out)
    put_out("qkv_w", qkv_w, weight_outs[0])
    before(TURN_X, None)
    turn_out(low_a, x_t, 0)

    def attend_pair(pair):
        before(ATTEND, pair)
        for start, size in ((0, last), (last, SPAN)):
            rows = pl.ds(start, size)
            query = qkv[rows, at(pair, 128)]
            key = qkv[rows, pl.ds(pl.multiple_of(D + pair * 128, 128), 128)]
            val = qkv[rows, pl.ds(pl.multiple_of(2 * D + pair * 128, 128), 128)]
            mask = bias[...] if start == 0 else jnp.where(keys[0:1, last:tokens] > 0, 0.0, -1e30)
            mixed = []
            for first in (True, False):
                chosen = jnp.where(head_lanes(first), query, jnp.zeros_like(query))
                scores = dot_nt(chosen, key) * 0.125 + mask
                highest = jnp.max(scores, 1, keepdims=True)
                raised = jnp.exp(scores - highest)
                summed = jnp.sum(raised, 1, keepdims=True)
                shares = (raised * (1.0 / summed)).astype(BF16)
                mixed.append(dot_nn(shares, val))
                put_lane(side, rows, 2 * pair + (0 if first else 1), highest + jnp.log(summed))
            mix[rows, at(pair, 128)] = jnp.where(head_lanes(True), mixed[0], mixed[1]).astype(BF16)

    each(HEADS // 2, attend_pair)
    before(OUT, 0)
    hooks.pop((OUT, 0))
    need(5)

    def out_project(index):
        before(OUT, index)
        value[:, at(index, TILE)] = value[:, at(index, TILE)] + dot_nn(mix[...], out_w[:, at(index, TILE)])

    each_unrolled(D // TILE, out_project)
    put_out("out_w", out_w, weight_outs[1])
    put_out("mix", mix, mix_out)
    before(NORM_B, None)

    def norm_b(index):
        rows = at(index, ROWS)
        found, normed, inverse = layer_norm(value[rows, :], norm_rows[2], norm_rows[3])
        value[rows, :] = found
        low_y[rows, :] = found.astype(BF16)
        nb[0][rows, :], nb[1][rows, :] = split_two(normed)
        put_lane(side, rows, 13, inverse)

    each(tokens // ROWS, norm_b)
    put_out("a", low_y, a_out)
    put_out("nb0", nb[0], nb_outs[0])
    put_out("nb1", nb[1], nb_outs[1])
    before(FEED_IN, 0)
    hooks.pop((FEED_IN, 0))
    need(3)

    def feed_in(index):
        before(FEED_IN, index)
        hidden = dot_nn(low_y[...], in_w[:, at(index, TILE)])
        active, slant = gelu_pair(hidden)
        active = active.astype(BF16)
        act[:, at(index, TILE)] = active
        slope[:, at(index, TILE)] = slant.astype(BF16)

    each_unrolled(4 * D // TILE, feed_in)
    put_out("act", act, act_out)
    put_out("slope", slope, slope_out)
    put_out("in_w", in_w, weight_outs[2])
    before(TURN_A, None)
    before(FEED_OUT, 0)
    hooks.pop((FEED_OUT, 0))
    need(4)

    def feed_out(index):
        before(FEED_OUT, index)
        value[:, at(index, TILE)] = value[:, at(index, TILE)] + dot_nn(act[...], down_w[:, at(index, TILE)])

    each_unrolled(D // TILE, feed_out)
    put_out("down_w", down_w, weight_outs[3])
    before(REST, None)
    turns[0].wait()

    def norm_c(index):
        rows = at(index, ROWS)
        found, normed, inverse = layer_norm(value[rows, :], norm_rows[4], norm_rows[5])
        low_a[rows, :] = found.astype(BF16)
        nc[0][rows, :], nc[1][rows, :] = split_two(normed)
        put_lane(side, rows, 14, inverse)

    each(tokens // ROWS, norm_c)
    put_out("y", low_a, y_out)
    put_out("nc0", nc[0], nc_outs[0])
    put_out("nc1", nc[1], nc_outs[1])
    for swap in swaps:
        swap.wait_send()
    for copy in token_copies:
        copy.wait_send()
    for piece in range(6):
        copy_of(piece, me, SIDE_WAY).wait_send()
    for number in FRONT:
        if number < 1000:
            piece, k, ways, _ = block_of(number)
            for way in ways:
                copy_of(piece, k, way).wait_send()
    for copy in outs.values():
        copy.wait()


def front(large, lengths):
    vmem, hbm = pl.BlockSpec(memory_space=pltpu.VMEM), pl.BlockSpec(memory_space=pl.ANY)
    smem = pl.BlockSpec(memory_space=pltpu.SMEM)
    shape, dma = jax.ShapeDtypeStruct, pltpu.SemaphoreType.DMA
    tokens = 5 * SPAN
    small = [shape((1, 1), F32), shape((16, D), F32), shape((tokens, 128), F32)]
    small += [shape((tokens, 128), jnp.int32), shape((8, tokens), jnp.int32), shape((1, 128), F32)]
    out = [shape((D, tokens), BF16)] + [shape((tokens, width), BF16) for width in (D, D, 4 * D, D, 4 * D, 3 * D)]
    out += [shape((tokens, D), F32)] + [shape((tokens, D), BF16)] * 4
    out += [shape((32 * SHAPES[m][0], SHAPES[m][1]), BF16) for m in (Q_, O_, I_, D_, E_)]
    return pl.pallas_call(
        front_kernel,
        out_shape=small + out,
        in_specs=[hbm] * 13 + [smem] * 2,
        out_specs=[vmem] * len(small) + [hbm] * len(out),
        scratch_shapes=[pltpu.VMEM((32 * size, wide), BF16) for size, wide in SHAPES]
        + [pltpu.VMEM((tokens, D), F32)] * 2
        + [pltpu.VMEM((tokens, D), BF16)] * 3
        + [
            pltpu.VMEM((tokens, 3 * D), BF16),
            pltpu.VMEM((tokens, 4 * D), BF16),
            pltpu.VMEM((tokens, 4 * D), BF16),
            pltpu.VMEM((HALF, WIDE), BF16),
            pltpu.VMEM((HALF, WIDE), BF16),
            pltpu.VMEM((tokens - SPAN, tokens - SPAN), F32),
            pltpu.VMEM((1, D, tokens), BF16),
        ]
        + [pltpu.VMEM((tokens, D), BF16)] * 4
        + [pltpu.VMEM(member.shape, member.dtype) for member in large]
        + [pltpu.VMEM(SHAPES[E_], F32)]
        + [pltpu.VMEM((2 * size, wide // 2), F32) for size, wide in SHAPES]
        + [pltpu.VMEM((4, 8, SPAN), jnp.int32), pltpu.VMEM((5, 8, SPAN), jnp.int32)]
        + [dma((13,)), dma((5,)), dma((5,)), dma((3,)), dma((3,)), dma((6, 16, 6)), dma((6, 16)), dma((6, 16))]
        + [dma((18,)), dma((1,))],
        compiler_params=pltpu.CompilerParams(
            collective_id=0, has_side_effects=True, vmem_limit_bytes=63 * 1024 * 1024
        ),
    )(*large, *lengths)


PACK = 256


def split_two(value):
    high = value.astype(BF16)
    return high, (value - high.astype(F32)).astype(BF16)


def middle_kernel(*refs):
    (wide_h, qkv_wh, out_wh, in_wh, down_h, y_h, act_h, a_h, mix_h, slope_h, qkv_h, na_h) = refs[0:12]
    nb_h, nc_h = refs[12:14], refs[14:16]
    cols, keys, side, gains, count = refs[16:21]
    loss_out, norm_out = refs[21:23]
    glog_out, y_t, a_t, mix_t, act_t, ge_t, gffn_out, gh_out, gattn_out, gqkv_out = refs[23:33]
    wide, qkv_w, out_w, in_w, plain, qkv, na = refs[33:40]
    nb, nc = refs[40:42], refs[42:44]
    slope_ring, act_ring, down_ring = refs[44:47]
    logits, glog, gh, gffn, gattn, gatt, packed, grad, turned, act_turned = refs[47:57]
    back_kv, gqkv, whole_grad, pick, pick_t, bias, side_pack, dq, ge = refs[57:66]
    load_sem, ring_sem, out_sem = refs[66:69]
    tokens = cols.shape[0]
    names = ("wide", "y", "nc0", "nc1", "in_w", "nb0", "nb1", "out_w", "qkv", "qkv_w", "na")
    sources = (wide_h, y_h, nc_h[0], nc_h[1], in_wh, nb_h[0], nb_h[1], out_wh, qkv_h, qkv_wh, na_h)
    targets = (wide, plain, nc[0], nc[1], in_w, nb[0], nb[1], out_w, qkv, qkv_w, na)
    loads = {}
    for i, name in enumerate(names):
        if name != "y":
            loads[name] = pltpu.make_async_copy(sources[i], targets[i], load_sem.at[i])
            loads[name].start()

    weight_row = keys[3:4, :].astype(F32)
    weight_col = cols[:, 3:4].astype(F32)
    earlier = lax.broadcasted_iota(jnp.int32, (tokens, tokens), 0) < lax.broadcasted_iota(jnp.int32, (tokens, tokens), 1)
    later = lax.broadcasted_iota(jnp.int32, (tokens, tokens), 0) > lax.broadcasted_iota(jnp.int32, (tokens, tokens), 1)
    rank_row = dot_nn(
        jnp.broadcast_to(weight_row, (16, tokens)).astype(BF16), jnp.where(earlier, 1.0, 0.0).astype(BF16)
    )[0:1]
    rank_col = dot_nn(
        jnp.where(later, 1.0, 0.0).astype(BF16), jnp.broadcast_to(weight_col, (tokens, 128)).astype(BF16)
    )[:, 0:1]
    rank_row = jnp.where(weight_row > 0, rank_row, -1.0)
    rank_col = jnp.where(weight_col > 0, rank_col, -1.0)
    blocks = (jnp.sum(weight_row).astype(jnp.int32) + (PACK - 1)) // PACK
    blocks = jnp.maximum(blocks, 1)
    inverse_count = 1.0 / count[...]
    norm_rows = [gains[5 + i : 6 + i, :] for i in range(6)]
    loss_out[...] = jnp.zeros((1, 1), F32)
    norm_out[...] = jnp.zeros(norm_out.shape, F32)
    back_kv[...] = jnp.zeros(back_kv.shape, F32)
    whole_grad[...] = jnp.zeros(whole_grad.shape, F32)
    gqkv[:, 0:D] = jnp.zeros((tokens, D), BF16)
    side_first = side[...].astype(BF16)
    rest = side[...] - side_first.astype(F32)
    side_second = rest.astype(BF16)
    side_third = (rest - side_second.astype(F32)).astype(BF16)
    waited = set()

    def load_plain(source):
        return pltpu.make_async_copy(source, plain, load_sem.at[1])

    def ring(kind, source, target):
        def copy(j):
            piece = source.at[at(j, TILE), :] if kind == 2 else source.at[:, at(j, TILE)]
            return pltpu.make_async_copy(piece, target.at[j % 2], ring_sem.at[kind * 2 + j % 2])

        return copy

    rings = [ring(0, slope_h, slope_ring), ring(1, act_h, act_ring), ring(2, down_h, down_ring)]
    outs = [
        (glog, glog_out, 0),
        (turned.at[0], y_t, 1),
        (turned.at[1], a_t, 1),
        (turned.at[2], mix_t, 1),
        (act_turned, act_t, 1),
        (gffn, gffn_out, 0),
        (gh, gh_out, 0),
        (gattn, gattn_out, 0),
    ]

    def out_copy(i, block):
        source, target, axis = outs[i]
        place = at(block, PACK)
        return pltpu.make_async_copy(
            source, target.at[place, :] if axis == 0 else target.at[:, place], out_sem.at[i]
        )

    def wait_load(name):
        loads[name].wait()

    load_plain(y_h).start()
    for name in names:
        if name in ("wide", "nc0", "nc1"):
            wait_load(name)

    def block_step(block, carry):
        slot_col = lax.broadcasted_iota(jnp.int32, (PACK, 1), 0).astype(F32) + (block * PACK).astype(F32)
        slot_row = lax.broadcasted_iota(jnp.int32, (1, PACK), 1).astype(F32) + (block * PACK).astype(F32)
        hit = jnp.where(rank_row == slot_col, 1.0, 0.0)
        pick[...] = hit.astype(BF16)
        pick_t[...] = jnp.where(rank_col == slot_row, 1.0, 0.0).astype(BF16)
        target = jnp.sum(hit * keys[2:3, :].astype(F32), 1, keepdims=True)
        row_of_token = jnp.sum(hit * keys[1:2, :].astype(F32), 1, keepdims=True)
        weight = jnp.sum(hit, 1, keepdims=True)
        bias[...] = jnp.where(
            (row_of_token == keys[1:2, :].astype(F32)) & (keys[0:1, :] > 0), 0.0, -1e30
        )
        side_pack[...] = (
            dot_nn(pick[...], side_first) + dot_nn(pick[...], side_second) + dot_nn(pick[...], side_third)
        )
        for kind in range(3):
            for j in range(2):
                rings[kind](j).start()
        load_plain(y_h).wait()
        packed[...] = dot_nn(pick[...], plain[...]).astype(BF16)
        load_plain(a_h).start()
        turned[0] = packed[...].T
        out_copy(1, block).start()

        def lanes(index):
            return (lax.broadcasted_iota(jnp.int32, (1, TILE), 1) + index * TILE).astype(F32)

        highest = jnp.full((PACK, 128), -1e30, F32)
        for index in range(TABLE_TILES):
            found = dot_nn(packed[...], wide[:, at(index, TILE)])
            if index == TABLE_TILES - 1:
                found = jnp.where(lanes(index) < VOCAB, found, -1e30)
            logits[:, at(index, TILE)] = found
            highest = jnp.maximum(highest, jnp.maximum(found[:, 0:128], found[:, 128:256]))
        highest = jnp.max(highest, 1, keepdims=True)
        summed, picked = jnp.zeros((PACK, 128), F32), jnp.zeros((PACK, 128), F32)
        for index in range(TABLE_TILES):
            found = logits[:, at(index, TILE)]
            raised = jnp.exp(found - highest)
            logits[:, at(index, TILE)] = raised
            own = jnp.where(lanes(index) == target, found, 0.0)
            summed = summed + raised[:, 0:128] + raised[:, 128:256]
            picked = picked + own[:, 0:128] + own[:, 128:256]
        summed = jnp.sum(summed, 1, keepdims=True)
        picked = jnp.sum(picked, 1, keepdims=True)
        loss_out[...] = loss_out[...] + jnp.sum(weight * (highest + jnp.log(summed) - picked), 0, keepdims=True)
        scale = weight * inverse_count
        share = scale / summed
        for index in range(TABLE_TILES):
            found = logits[:, at(index, TILE)] * share - jnp.where(lanes(index) == target, scale, 0.0)
            glog[:, at(index, TILE)] = found.astype(BF16)
        out_copy(0, block).start()
        for index in range(D // TILE):
            grad[:, at(index, TILE)] = dot_nt(glog[...], wide[at(index, TILE), 0:TABLE_END])
        normed = dot_nn(pick[...], nc[0][...]) + dot_nn(pick[...], nc[1][...])
        found = grad[...]
        back = layer_norm_back(found, normed, lane_at(side_pack[...], 14), norm_rows[4])
        norm_out[4:5, :] = norm_out[4:5, :] + jnp.sum(found * normed, 0, keepdims=True)
        norm_out[5:6, :] = norm_out[5:6, :] + jnp.sum(found, 0, keepdims=True)
        grad[...] = back
        gffn[...] = back.astype(BF16)
        out_copy(5, block).start()

        load_plain(a_h).wait()
        turned[1] = dot_nn(pick[...], plain[...]).astype(BF16).T
        out_copy(2, block).start()
        load_plain(mix_h).start()
        for index in range(4 * D // TILE):
            for kind in range(3):
                rings[kind](index).wait()
            slant = dot_nn(pick[...], slope_ring[index % 2])
            found = dot_nt(gffn[...], down_ring[index % 2]) * slant
            gh[:, at(index, TILE)] = found.astype(BF16)
            act_turned[at(index, TILE), :] = dot_nn(pick[...], act_ring[index % 2]).astype(BF16).T
            if index + 2 < 4 * D // TILE:
                for kind in range(3):
                    rings[kind](index + 2).start()
        out_copy(6, block).start()
        out_copy(4, block).start()
        load_plain(mix_h).wait()
        turned[2] = dot_nn(pick[...], plain[...]).astype(BF16).T
        out_copy(3, block).start()
        load_plain(y_h).start()

        @pl.when(block == 0)
        def _():
            for name in names[4:8]:
                wait_load(name)

        for index in range(D // TILE):
            grad[:, at(index, TILE)] = grad[:, at(index, TILE)] + dot_nt(gh[...], in_w[at(index, TILE), :])
        normed = dot_nn(pick[...], nb[0][...]) + dot_nn(pick[...], nb[1][...])
        found = grad[...]
        back = layer_norm_back(found, normed, lane_at(side_pack[...], 13), norm_rows[2])
        norm_out[2:3, :] = norm_out[2:3, :] + jnp.sum(found * normed, 0, keepdims=True)
        norm_out[3:4, :] = norm_out[3:4, :] + jnp.sum(found, 0, keepdims=True)
        gattn[...] = back.astype(BF16)
        out_copy(7, block).start()
        high, low = split_two(back)
        whole_grad[...] = whole_grad[...] + dot_nn(pick_t[...], high) + dot_nn(pick_t[...], low)
        for index in range(D // TILE):
            gatt[:, at(index, TILE)] = dot_nt(gattn[...], out_w[at(index, TILE), :]).astype(BF16)

        @pl.when(block == 0)
        def _():
            wait_load("qkv")

        def attend_pair_back(pair):
            spots = [pl.ds(pl.multiple_of(i * D + pair * 128, 128), 128) for i in range(3)]
            query = dot_nn(pick[...], qkv[:, spots[0]]).astype(BF16)
            key, val = qkv[:, spots[1]], qkv[:, spots[2]]
            given = gatt[:, at(pair, 128)]
            found = []
            for first in (True, False):
                lanes_here = head_lanes(first)
                chosen = jnp.where(lanes_here, query, jnp.zeros_like(query))
                mine = jnp.where(lanes_here, given, jnp.zeros_like(given))
                total = lane_at(side_pack[...], 2 * pair + (0 if first else 1))
                shares = jnp.exp(dot_nt(chosen, key) * 0.125 + bias[...] - total)
                grad_share = dot_nt(mine, val)
                middle = jnp.sum(shares * grad_share, 1, keepdims=True)
                grad_score = (shares * (grad_share - middle)).astype(BF16)
                found.append(
                    (
                        dot_nn(grad_score, key) * 0.125,
                        dot_tn(grad_score, query) * 0.125,
                        dot_tn(shares.astype(BF16), given),
                    )
                )
            lanes_here = head_lanes(True)
            dq[:, at(pair, 128)] = jnp.where(lanes_here, found[0][0], found[1][0]).astype(BF16)
            for i in (1, 2):
                spot = pl.ds(pl.multiple_of((i - 1) * D + pair * 128, 128), 128)
                back_kv[:, spot] = back_kv[:, spot] + jnp.where(lanes_here, found[0][i], found[1][i])

        each(HEADS // 2, attend_pair_back)
        gqkv[:, 0:D] = (gqkv[:, 0:D].astype(F32) + dot_nn(pick_t[...], dq[...])).astype(BF16)
        for i in range(len(outs)):
            out_copy(i, block).wait()
        return carry

    lax.fori_loop(0, blocks, block_step, 0)
    load_plain(y_h).wait()
    gqkv[:, D:] = back_kv[...].astype(BF16)
    copy_qkv = pltpu.make_async_copy(gqkv, gqkv_out, out_sem.at[8])
    copy_qkv.start()
    for ref in (glog, gffn, gh, gattn):
        ref[...] = jnp.zeros(ref.shape, BF16)
    for block in range(1, 3):

        @pl.when(blocks <= block)
        def _():
            for i in range(len(outs)):
                out_copy(i, block).start()

    for name in names[9:]:
        wait_load(name)
    for index in range(D // TILE):
        whole_grad[:, at(index, TILE)] = whole_grad[:, at(index, TILE)] + dot_nt(gqkv[...], qkv_w[at(index, TILE), :])
    zero = jnp.zeros((1, D), F32)

    def norm_a_back(index, carry):
        gain, shift = carry
        rows = at(index, ROWS)
        inverse = lane_at(side[rows, :], 12)
        found, normed = whole_grad[rows, :], na[rows, :]
        ge[:, rows] = layer_norm_back(found, normed, inverse, norm_rows[0]).astype(BF16).T
        return gain + jnp.sum(found * normed, 0, keepdims=True), shift + jnp.sum(found, 0, keepdims=True)

    gain, shift = lax.fori_loop(0, tokens // ROWS, norm_a_back, (zero, zero))
    norm_out[0:1, :] = gain
    norm_out[1:2, :] = shift
    copy_ge = pltpu.make_async_copy(ge, ge_t, out_sem.at[9])
    copy_ge.start()
    for block in range(1, 3):

        @pl.when(blocks <= block)
        def _():
            for i in range(len(outs)):
                out_copy(i, block).wait()

    copy_qkv.wait()
    copy_ge.wait()


def middle(large, small):
    tokens = 5 * SPAN
    slots = 3 * PACK
    vmem, hbm = pl.BlockSpec(memory_space=pltpu.VMEM), pl.BlockSpec(memory_space=pl.ANY)
    shape, dma = jax.ShapeDtypeStruct, pltpu.SemaphoreType.DMA
    out = [shape((slots, TABLE_END), BF16)] + [shape((D, slots), BF16)] * 3 + [shape((4 * D, slots), BF16)]
    out += [shape((D, tokens), BF16), shape((slots, D), BF16), shape((slots, 4 * D), BF16), shape((slots, D), BF16)]
    out += [shape((tokens, 3 * D), BF16)]

    def rows(count, width, kind=BF16):
        return pltpu.VMEM((count, width), kind)

    scratch = [rows(D, WIDE), rows(D, 3 * D), rows(D, D), rows(D, 4 * D), rows(tokens, D), rows(tokens, 3 * D)]
    scratch += [rows(tokens, D, F32)] + [rows(tokens, D)] * 4
    scratch += [pltpu.VMEM((2, tokens, TILE), BF16)] * 2 + [pltpu.VMEM((2, TILE, D), BF16)]
    scratch += [rows(PACK, TABLE_END, F32), rows(PACK, TABLE_END), rows(PACK, 4 * D)] + [rows(PACK, D)] * 4
    scratch += [rows(PACK, D, F32), pltpu.VMEM((3, D, PACK), BF16), rows(4 * D, PACK)]
    scratch += [rows(tokens, 2 * D, F32), rows(tokens, 3 * D), rows(tokens, D, F32), rows(PACK, tokens)]
    scratch += [rows(tokens, PACK), rows(PACK, tokens, F32), rows(PACK, 128, F32), rows(PACK, D), rows(D, tokens)]
    scratch += [dma((11,)), dma((6,)), dma((10,))]
    return pl.pallas_call(
        middle_kernel,
        out_shape=[shape((1, 1), F32), shape((6, D), F32)] + out,
        in_specs=[hbm] * 16 + [vmem] * 5,
        out_specs=[vmem] * 2 + [hbm] * len(out),
        scratch_shapes=scratch,
        compiler_params=pltpu.CompilerParams(vmem_limit_bytes=63 * 1024 * 1024),
    )(*large, *small)


LEFT = 768
PIECES = ((Q_, 0, 1152), (E_, 0, 1280), (E_, 1280, 1280), (I_, 0, 1536), (D_, 0, 384), (O_, 0, 384))
Y_FIRST = (0, 1, 4)
TASKS = (
    0, 1, 96, 9, 4, 129, 97, 2, 103, 5, 99, 7, 8, 6, 101, 128, 102, 105,
    100, 132, 133, 64, 108, 12, 104, 136, 139, 134, 65, 15, 107, 111, 109, 137, 161, 13,
    160, 3, 131, 11, 141, 142, 70, 32, 68, 112, 110, 76, 140, 16, 168, 67, 144, 72,
    169, 75, 135, 71, 33, 36, 69, 143, 166, 173, 38, 98, 39, 43, 78, 130, 167, 73,
    37, 40, 79, 44, 34, 164, 46, 66, 77, 14, 47, 165, 45, 162, 171, 41, 172, 176,
    80, 138, 174, 74, 48, 10, 106, 42, 175, 35, 81, 145, 163, 170, 113, 17, 49, 177,
)


def reduce_kernel(*refs):
    given, (cols, norm_sums, loss, squares) = refs[0:11], refs[11:15]
    y_t, ge_t, glog, x_t, gqkv, mix_t, gattn, a_t, gh, act_t, gffn = given
    lane_olds, side_olds, moment = refs[15:21], refs[21:27], refs[27]
    outs, sums_out, totals_out = refs[28:33], refs[33], refs[34]
    own, side, first, second, column, fin = (refs[35 + 6 * i : 41 + 6 * i] for i in range(6))
    left, (glog_v, gqkv_v, gattn_v, gh_v, gffn_v), stage, tails, norm_t = refs[71:78], refs[78:83], refs[83], refs[84], refs[85]
    spread, spread_small = refs[86:89], refs[89:92]
    load_sem, ring_sem, tail_sem, side_recv, first_send, first_recv, second_send, second_recv = refs[92:100]
    z_send, z_recv, swap_send, swap_recv = refs[100:104]
    sems, small_sems = refs[104:110], refs[110:116]
    z, y, x, c = here()
    peers = all_peers()
    me = chip(z, y, x)

    barrier = pltpu.get_barrier_semaphore()
    greeted = [peers[XWAY], peers[YWAY], peers[SIDE], device(z, 1 - y, 1 - x, c)]
    greeted += [device((z + 1 + i) % 4, y, x, c) for i in range(3)]
    for peer in greeted:
        pl.semaphore_signal(barrier, inc=1, device_id=peer, device_id_type=MESH)

    tokens = cols.shape[0]

    def act_part(group):
        return act_t.at[pl.ds(LEFT * group, LEFT), 0:tokens]

    operands = (
        ((x_t, left[1]), (gqkv, gqkv_v)),
        ((y_t.at[:, 0:tokens], left[2]), (ge_t, left[3]), (glog.at[0:tokens, :], glog_v)),
        (),
        ((a_t.at[:, 0:tokens], left[0]), (gh.at[0:tokens, :], gh_v)),
        ((gffn.at[0:tokens, :], gffn_v), (act_part(0), left[5]), (act_part(1), left[6])),
        ((mix_t.at[:, 0:tokens], left[4]), (gattn.at[0:tokens, :], gattn_v)),
    )
    loads = {}
    waited = set()
    for task in TASKS:
        piece = task // 32 if task // 32 != 2 else 1
        if piece not in loads:
            loads[piece] = []
            for source, target in operands[piece]:
                number = sum(len(member) for member in loads.values())
                loads[piece].append(pltpu.make_async_copy(source, target, load_sem.at[number]))
                loads[piece][-1].start()

    def loaded(piece):
        piece = 1 if piece == 2 else piece
        if piece not in waited:
            waited.add(piece)
            for member in loads[piece]:
                member.wait()

    norm_t[...] = jnp.zeros(norm_t.shape, F32)
    norm_t[5:11, :] = norm_sums[...]
    pl.semaphore_wait(barrier, 7)

    def size_of(piece):
        return 2 * SHAPES[PIECES[piece][0]][0]

    def slot(ref, piece, index):
        size = size_of(piece)
        return ref[piece].at[pl.ds(pl.multiple_of(index * size, size), size), :]

    def half_of(piece):
        return SHAPES[PIECES[piece][0]][1] // 2

    def chosen(start):
        lane = lax.broadcasted_iota(jnp.int32, (1, TILE), 1) + start
        hit = (cols[:, 0:1] == lane) | (cols[:, 1:2] == lane)
        return jnp.where(hit, 1.0, 0.0).astype(BF16)

    def ring_copy(piece, rows, lanes, number, index):
        place = lax.rem(number, 3)
        return pltpu.make_async_remote_copy(
            src_ref=stage.at[place],
            dst_ref=side[piece].at[rows, lanes],
            send_sem=ring_sem.at[place],
            recv_sem=side_recv.at[piece, index],
            device_id=peers[SIDE],
            device_id_type=MESH,
        )

    def tail_copy(piece, rows, lanes, number, index):
        return pltpu.make_async_remote_copy(
            src_ref=tails.at[number],
            dst_ref=side[piece].at[rows, lanes],
            send_sem=tail_sem.at[number],
            recv_sem=side_recv.at[piece, index],
            device_id=peers[SIDE],
            device_id_type=MESH,
        )

    whole = pl.ds(0, LEFT)
    ring_count, tail_count = [0], [0]

    def give(piece, rows, lanes, number, index):
        def before():
            @pl.when(number >= 3)
            def _():
                ring_copy(piece, rows, lanes, number, index).wait_send()

        def write(value):
            stage[lax.rem(number, 3)] = value.astype(BF16)

        return before, write, lambda: ring_copy(piece, rows, lanes, number, index).start()

    def keep(piece, rows, lanes):
        def write(value):
            own[piece][rows, lanes] = value.astype(BF16)

        return lambda: None, write, lambda: None

    def plain(piece, mine, source, right, group):
        wide = PIECES[piece][2]
        half = c if mine else 1 - c
        rows = pl.ds(LEFT * group, LEFT)
        base = ring_count[0]

        def step(j):
            lanes = at(j, TILE)
            before, write, after = keep(piece, rows, lanes) if mine else give(
                piece, rows, lanes, base + j, group * (wide // TILE) + j
            )
            before()
            write(dot_nn(source[...], right[:, pl.ds(pl.multiple_of(half * wide + j * TILE, 128), TILE)]))
            after()

        each(wide // TILE, step)
        if not mine:
            ring_count[0] += wide // TILE
        if wide % TILE:
            start = wide - 128
            value = dot_nn(source[...], right[:, pl.ds(pl.multiple_of(half * wide + start, 128), 128)])
            if mine:
                own[piece][rows, start:wide] = value.astype(BF16)
            else:
                number = tail_count[0]
                tail_count[0] += 1
                groups = SHAPES[PIECES[piece][0]][0] // 24
                tails[number] = value.astype(BF16)
                tail_copy(piece, rows, pl.ds(start, 128), number, groups * (wide // TILE) + group).start()

    def wide_product(piece, mine):
        half = c if mine else 1 - c
        wide = half_of(piece)
        skip = PIECES[piece][1] // TILE
        base = ring_count[0]

        def both(j):
            start = pl.multiple_of(half * wide + (skip + j) * TILE, TILE)
            return dot_nn(left[2][...], glog_v[:, pl.ds(start, TILE)]) + dot_nn(left[3][...], chosen(start))

        def target(j):
            lanes = at(j, TILE)
            return keep(piece, whole, lanes) if mine else give(piece, whole, lanes, base + j, j)

        def step(j):
            before, write, after = target(j)
            before()
            write(both(j))
            after()

        if not mine:
            ring_count[0] += 5
        if skip == 0:
            each(5, step)
            return
        each(1, step)
        before, write, after = target(1)
        before()
        norm_part = jnp.where(half == 1, norm_t[...], 0.0).T
        write(both(1) + jnp.concatenate((norm_part, jnp.zeros((LEFT, TILE - 128), F32)), 1))
        after()
        for j in range(2, 5):
            before, write, after = target(j)
            before()

            @pl.when(half == 0)
            def _():
                write(both(j))

            @pl.when(half == 1)
            def _():
                if j == 2:
                    write(jnp.zeros((LEFT, TILE), F32))
                else:
                    write(dot_nn(left[3][...], chosen(half_of(piece) + (skip + j) * TILE)))

            after()

    def products(piece, mine):
        loaded(piece)
        if piece in (1, 2):
            wide_product(piece, mine)
        elif piece == 4:
            if not mine:
                for group in range(4):
                    source = left[5 + group % 2]
                    if group >= 2:
                        loads[piece][1 + group % 2].wait()
                    plain(piece, False, source, gffn_v, group)
                    plain(piece, True, source, gffn_v, group)
                    if group < 2:
                        again = pltpu.make_async_copy(act_part(group + 2), source, load_sem.at[12 + group])
                        again.start()
                        loads[piece][1 + group] = again
        else:
            source, right = {0: (left[1], gqkv_v), 3: (left[0], gh_v), 5: (left[4], gattn_v)}[piece]
            plain(piece, mine, source, right, 0)

    def combine(piece, target, parts):
        def some(rows, lanes):
            total = parts[0][rows, lanes].astype(F32)
            for member in parts[1:]:
                total = total + member[rows, lanes].astype(F32)
            target[rows, lanes] = total.astype(target.dtype)

        wide = PIECES[piece][2]
        if piece == 4:
            each(4, lambda group: some(at(group, 48), slice(0, wide)))
            return
        if wide >= 512:
            each(wide // 512, lambda j: some(slice(0, 48), at(j, 512)))
        if wide % 512:
            some(slice(0, 48), slice(wide // 512 * 512, wide))

    def hop(piece, k, land, index, sems, way):
        return pltpu.make_async_remote_copy(
            src_ref=slot(own, piece, k),
            dst_ref=slot(land, piece, index),
            send_sem=sems[0].at[piece, index],
            recv_sem=sems[1].at[piece, index],
            device_id=peers[way],
            device_id_type=MESH,
        )

    FIRST, SECOND = (first_send, first_recv), (second_send, second_recv)

    def landed(piece, land, index, sems):
        hop(piece, me, land, index, sems, XWAY).wait_recv()

    def block(piece, a, b, far):
        return chip(far, a, b) if piece in Y_FIRST else chip(far, b, a)

    def split(piece):
        return (y, x, YWAY, XWAY) if piece in Y_FIRST else (x, y, XWAY, YWAY)

    readied = set()

    def ready(piece):
        if piece in readied:
            return
        readied.add(piece)
        wide, groups = PIECES[piece][2], SHAPES[PIECES[piece][0]][0] // 24
        for group in range(groups):
            for j in range(wide // TILE):
                ring_copy(piece, pl.ds(LEFT * group, LEFT), at(j, TILE), 0, group * (wide // TILE) + j).wait_recv()
            if wide % TILE:
                index = groups * (wide // TILE) + group
                tail_copy(piece, pl.ds(LEFT * group, LEFT), pl.ds(wide - 128, 128), 0, index).wait_recv()

    def both_cores(piece, k):
        return (slot(own, piece, k), slot(side, piece, k))

    def first_block(piece, i):
        a, b, way, _ = split(piece)
        t, v = (z + i // 2) % 4, (1 - b) if i % 2 == 0 else b
        return block(piece, 1 - a, v, t), 2 * t + v, way

    def first_send_of(piece, i):
        ready(piece)
        k, index, way = first_block(piece, i)
        combine(piece, slot(own, piece, k), both_cores(piece, k))
        hop(piece, k, first, index, FIRST, way).start()

    def second_block(piece, i):
        a, b, _, way = split(piece)
        t = (z + i) % 4
        return block(piece, a, 1 - b, t), t, way

    def second_send_of(piece, i):
        k, t, way = second_block(piece, i)
        spot = 2 * t + 1 - split(piece)[1]
        landed(piece, first, spot, FIRST)
        combine(piece, slot(own, piece, k), both_cores(piece, k) + (slot(first, piece, spot),))
        hop(piece, k, second, t, SECOND, way).start()

    def z_copy(piece, i):
        t = (z + i) % 4
        return pltpu.make_async_remote_copy(
            src_ref=slot(own, piece, chip(t, y, x)),
            dst_ref=slot(column, piece, z),
            send_sem=z_send.at[piece, t],
            recv_sem=z_recv.at[piece, z],
            device_id=device(t, y, x, c),
            device_id_type=MESH,
        )

    def z_landed(piece, i):
        t = (z + i) % 4
        pltpu.make_async_remote_copy(
            src_ref=slot(own, piece, me),
            dst_ref=slot(column, piece, t),
            send_sem=z_send.at[piece, t],
            recv_sem=z_recv.at[piece, t],
            device_id=device(t, y, x, c),
            device_id_type=MESH,
        ).wait_recv()
        return slot(column, piece, t)

    def gathered(piece, t):
        spot = 2 * t + split(piece)[1]
        landed(piece, first, spot, FIRST)
        landed(piece, second, t, SECOND)
        return both_cores(piece, chip(t, y, x)) + (slot(first, piece, spot), slot(second, piece, t))

    def z_send_of(piece, i):
        t = (z + i) % 4
        combine(piece, slot(own, piece, chip(t, y, x)), gathered(piece, t))
        z_copy(piece, i).start()

    swaps = []

    def finish(piece):
        parts = gathered(piece, z)
        parts = parts + tuple(z_landed(piece, i) for i in (1, 2, 3))
        combine(piece, fin[piece], parts)
        m, skip, wide = PIECES[piece]
        size = SHAPES[m][0]
        lanes = pl.ds(pl.multiple_of(c * half_of(piece) + skip, 128), wide)
        swaps.append(
            pltpu.make_async_remote_copy(
                src_ref=fin[piece].at[pl.ds(pl.multiple_of((1 - c) * size, 8), size), :],
                dst_ref=outs[m].at[:, lanes],
                send_sem=swap_send.at[piece],
                recv_sem=swap_recv.at[piece],
                device_id=peers[SIDE],
                device_id_type=MESH,
            )
        )
        swaps[-1].start()
        outs[m][:, lanes] = fin[piece][pl.ds(pl.multiple_of(c * size, 8), size), :]

    for task in TASKS:
        piece, number = task // 32, task % 32
        if number < 2:
            products(piece, number == 1)
        elif number < 10:
            first_send_of(piece, number - 2)
        elif number < 14:
            second_send_of(piece, number - 10)
        elif number < 17:
            z_send_of(piece, number - 13)
        else:
            finish(piece)
    for piece in range(6):
        for i in range(8):
            k, index, way = first_block(piece, i)
            hop(piece, k, first, index, FIRST, way).wait_send()
        for i in range(4):
            k, t, way = second_block(piece, i)
            hop(piece, k, second, t, SECOND, way).wait_send()
        for i in (1, 2, 3):
            z_copy(piece, i).wait_send()
    for number in range(ring_count[0] - 3, ring_count[0]):
        ring_copy(1, whole, pl.ds(0, TILE), number, 0).wait_send()
    for number in range(tail_count[0]):
        tail_copy(1, whole, pl.ds(0, 128), number, 0).wait_send()
    for swap in swaps:
        swap.wait()

    sides, lanes, _, gs = statistics(outs, lane_olds, side_olds)
    scalars = lanes_of([jnp.sum(member, 0, keepdims=True) for member in sides] + [loss[...]])
    sums = jnp.concatenate(lanes + [scalars, squares[...]], 1)
    sums = sum_everywhere(sums, *spread, sems)
    sums_out[...] = sums
    updates = updates_of(sums, gs, sides, lane_olds, moment)[0]
    totals = lanes_of(
        [total_sum(update * update) for update in updates[:6]]
        + [jnp.sum(updates[6][i : i + 1] * updates[6][i : i + 1], 1, keepdims=True) for i in range(6)]
    )
    totals_out[...] = sum_everywhere(totals, *spread_small, small_sems)


def statistics(grads, lane_olds, side_olds):
    wide_g = grads[E_][...]
    gs = (wide_g[:, :VOCAB], wide_g[:, PLACE_AT:]) + tuple(grads[m][...] for m in (Q_, O_, I_, D_))
    gs = gs + (wide_g[:, 4096:4224],)
    decay = 1.0 - STEP ** (-0.8)
    sides, lanes = [], []
    wide_square = wide_g * wide_g + SQUARE_FLOOR
    squares = [wide_square[:, :VOCAB], wide_square[:, PLACE_AT:]] + [g * g + SQUARE_FLOOR for g in gs[2:6]]
    for index in range(6):
        mean = jnp.sum(squares[index], 1, keepdims=True) / squares[index].shape[1]
        sides.append(decay * column_of(as_row(side_olds[index])) + (1.0 - decay) * mean)
    lanes = [jnp.sum(square, 0, keepdims=True) for square in [wide_square] + squares[2:]]
    return sides, lanes, squares, gs


def updates_of(sums, gs, sides, lane_olds, moment):
    decay = 1.0 - STEP ** (-0.8)
    fresh = 1.0 - decay
    parts = [sums[:, :VOCAB], sums[:, PLACE_AT:WIDE]]
    parts += [sums[:, SUM_AT[i] : SUM_AT[i + 1]] for i in range(1, 5)]
    scalars = sums[:, SUM_AT[5] : SUM_AT[5] + 128]
    updates, lane_news = [], []
    for index in range(6):
        height = gs[index].shape[0] * 32
        lane_news.append(decay * as_row(lane_olds[index]) + fresh * (parts[index] / height))
        if index < 2:
            mean = jnp.sum(lane_news[index], 1, keepdims=True) / lane_news[index].shape[1]
        else:
            mean = lane_at(scalars, index) / height
        updates.append(gs[index] * lax.rsqrt(sides[index] * lane_news[index] / mean))
    norm_g = jnp.concatenate([row_of(lane_at(gs[6], NORM_AT - 4096 + i)) for i in range(6)], 0)
    moment_new = decay * moment[...] + fresh * (norm_g * norm_g + SQUARE_FLOOR)
    updates.append(norm_g * lax.rsqrt(moment_new))
    return updates, lane_news, norm_g, moment_new


def reduce_grads(large, small):
    tokens = 5 * SPAN
    vmem, hbm = pl.BlockSpec(memory_space=pltpu.VMEM), pl.BlockSpec(memory_space=pl.ANY)
    dma = pltpu.SemaphoreType.DMA
    scratch = []
    for count in (16, 16, 8, 4, 4):
        scratch += [pltpu.VMEM((count * 2 * SHAPES[m][0], wide), BF16) for m, _, wide in PIECES]
    scratch += [pltpu.VMEM((2 * SHAPES[m][0], wide), F32) for m, _, wide in PIECES]
    scratch += [pltpu.VMEM((LEFT, tokens), BF16)] * 7
    scratch += [pltpu.VMEM((tokens, width), BF16) for width in (TABLE_END, 3 * D, D, 4 * D, D)]
    scratch += [pltpu.VMEM((3, LEFT, TILE), BF16), pltpu.VMEM((6, LEFT, 128), BF16), pltpu.VMEM((128, D), F32)]
    scratch += [pltpu.VMEM((count, 1, SUMS), F32) for count in (2, 4, 4)]
    scratch += [pltpu.VMEM((count, 1, 128), F32) for count in (2, 4, 4)]
    scratch += [dma((14,)), dma((3,)), dma((6,)), dma((6, 10)), dma((6, 8)), dma((6, 8)), dma((6, 4)), dma((6, 4))]
    scratch += [dma((6, 4)), dma((6, 4)), dma((6,)), dma((6,))]
    scratch += ([dma] * 2 + [dma((3,))] * 4) * 2
    return pl.pallas_call(
        reduce_kernel,
        out_shape=[jax.ShapeDtypeStruct(shape, F32) for shape in SHAPES + ((1, SUMS), (1, 128))],
        in_specs=[hbm] * 11 + [vmem] * len(small),
        out_specs=[vmem] * 7,
        scratch_shapes=scratch,
        compiler_params=pltpu.CompilerParams(
            collective_id=1, has_side_effects=True, vmem_limit_bytes=63 * 1024 * 1024
        ),
    )(*large, *small)


def update_kernel(*refs):
    copies = [pltpu.make_async_copy(refs[i], refs[55 + i], refs[82].at[i]) for i in range(27)]
    for copy in copies:
        copy.start()
    for copy in copies:
        copy.wait()
    refs = refs[55:82] + refs[27:55]
    grads, sums, totals, ws, norms = refs[0:5], refs[5], refs[6], refs[7:13], refs[13]
    lane_olds, side_olds, moment = refs[14:20], refs[20:26], refs[26]
    loss_out, table_g, place_g, norm_g_out = refs[27:31]
    lane_outs, side_outs, moment_out, news, norm_new = refs[31:37], refs[37:43], refs[43], refs[44:50], refs[50]
    grad_outs = refs[51:55]
    sides, _, _, gs = statistics(grads, lane_olds, side_olds)
    updates, lane_news, norm_g, moment_new = updates_of(sums[...], gs, sides, lane_olds, moment)
    scalars = sums[:, SUM_AT[5] : SUM_AT[5] + 128]
    squares = sums[:, SUM_AT[5] + 128 :]
    loss_out[...] = lane_at(scalars, 6)
    table_g[...] = gs[0]
    place_g[...] = gs[1]
    norm_g_out[...] = norm_g
    moment_out[...] = moment_new
    for index in range(6):
        lane_outs[index][...] = lane_news[index].reshape(lane_outs[index].shape)
        side_outs[index][...] = row_of(sides[index]).reshape(side_outs[index].shape)
        if index >= 2:
            grad_outs[index - 2][...] = gs[index]
        entries = gs[index].shape[0] * gs[index].shape[1] * 32
        clip = jnp.maximum(1.0, jnp.sqrt(lane_at(totals[...], index) / entries))
        scale = learn_rate * jnp.sqrt(lane_at(squares, index) / entries) / clip
        news[index][...] = ws[index][...] - scale * updates[index]
    for i in range(6):
        clip = jnp.maximum(1.0, jnp.sqrt(lane_at(totals[...], 6 + i) / D))
        scale = learn_rate * jnp.sqrt(lane_at(squares, 6 + i) / D) / clip
        norm_new[i : i + 1, :] = norms[i : i + 1, :] - scale * updates[6][i : i + 1, :]


def update_weights(operands):
    lanes = (VOCAB, 512, 3 * D, D, 4 * D, D)
    held = (24, 24, 24, 24, 24, 96)
    shapes = [(1, 1), (24, VOCAB), (24, 512), (6, 24)]
    shapes += [(lane,) for lane in lanes] + [(size,) for size in held] + [(6, 24)]
    shapes += list(zip(held, lanes)) + [(6, 24)] + list(zip(held, lanes))[2:]
    return pl.pallas_call(
        update_kernel,
        out_shape=[jax.ShapeDtypeStruct(shape, F32) for shape in shapes],
        in_specs=[pl.BlockSpec(memory_space=pl.ANY)] * len(operands),
        out_specs=[pl.BlockSpec(memory_space=pltpu.VMEM)] * len(shapes),
        scratch_shapes=[pltpu.VMEM(member.shape, member.dtype) for member in operands]
        + [pltpu.SemaphoreType.DMA((len(operands),))],
        compiler_params=pltpu.CompilerParams(vmem_limit_bytes=63 * 1024 * 1024),
    )(*operands)


def norm_forward(value, gain, shift):
    centred = value - jnp.mean(value, -1, keepdims=True)
    inverse = lax.rsqrt(jnp.mean(centred * centred, -1, keepdims=True) + EPSILON)
    normed = centred * inverse
    return (normed * gain + shift, normed, inverse)


def norm_backward(grad_out, normed, inverse, gain):
    scaled = grad_out * gain
    back = inverse * (
        scaled
        - jnp.mean(scaled, -1, keepdims=True)
        - normed * jnp.mean(scaled * normed, -1, keepdims=True)
    )
    return (back, jnp.sum(grad_out * normed, 0), jnp.sum(grad_out, 0))


def mm(left, right, sides):
    return lax.dot_general(left, right, ((sides[:1], sides[1:]), ((), ())), preferred_element_type=F32)


def attend(qkv, allowed):
    by_head = qkv.reshape(qkv.shape[0], 3, HEADS, HEAD_DIM)
    query, key, value = by_head[:, 0], by_head[:, 1], by_head[:, 2]
    scores = jnp.einsum("qhe,khe->hqk", query, key, preferred_element_type=F32) * 0.125
    scores = jnp.where(allowed[None], scores, -1e30)
    highest = jnp.max(scores, -1, keepdims=True)
    raised = jnp.exp(scores - highest)
    summed = jnp.sum(raised, -1, keepdims=True)
    shares = (raised / summed).astype(BF16)
    mixture = jnp.einsum("hqk,khe->qhe", shares, value, preferred_element_type=F32)
    return mixture.astype(BF16).reshape(qkv.shape[0], D), highest + jnp.log(summed)


def attend_back(qkv, allowed, log_total, grad_mix):
    by_head = qkv.reshape(qkv.shape[0], 3, HEADS, HEAD_DIM)
    query, key, value = by_head[:, 0], by_head[:, 1], by_head[:, 2]
    grad_mix = grad_mix.reshape(qkv.shape[0], HEADS, HEAD_DIM)
    scores = jnp.einsum("qhe,khe->hqk", query, key, preferred_element_type=F32) * 0.125
    scores = jnp.where(allowed[None], scores, -1e30)
    shares = jnp.exp(scores - log_total)
    grad_share = jnp.einsum("qhe,khe->hqk", grad_mix, value, preferred_element_type=F32)
    grad_score = (shares * (grad_share - jnp.sum(shares * grad_share, -1, keepdims=True))).astype(BF16)
    grad_query = jnp.einsum("hqk,khe->qhe", grad_score, key, preferred_element_type=F32) * 0.125
    grad_key = jnp.einsum("hqk,qhe->khe", grad_score, query, preferred_element_type=F32) * 0.125
    grad_value = jnp.einsum("hqk,qhe->khe", shares.astype(BF16), grad_mix, preferred_element_type=F32)
    return jnp.stack((grad_query, grad_key, grad_value), 1).astype(BF16).reshape(qkv.shape)


def on_slice(token_arrays, lengths, weights, lane_olds, side_olds, moment):
    olds = lane_olds + side_olds + (moment,)
    found = front(token_arrays + weights, lengths)
    mask_count, gains, side, cols, keys, weight_sq = found[0:6]
    x_t, mix, a, act, y, slope, qkv_b, normed_a = found[6:14]
    normed_bc, (qkv_w, out_w, in_w, down_w, wide_w) = found[14:18], found[18:23]
    found = middle(
        (wide_w, qkv_w, out_w, in_w, down_w, y, act, a, mix, slope, qkv_b, normed_a) + tuple(normed_bc),
        (cols, keys, side, gains, mask_count),
    )
    loss_part, norm_sums = found[0:2]
    grad_logit, y_t, a_t, mix_t, act_t, ge_t, grad_ffn, grad_hidden, grad_attn, grad_qkv = found[2:]
    reduced = reduce_grads(
        (y_t, ge_t, grad_logit, x_t, grad_qkv, mix_t, grad_attn, a_t, grad_hidden, act_t, grad_ffn),
        (cols, norm_sums, loss_part, weight_sq) + olds,
    )
    found = update_weights(tuple(reduced) + weights + olds)
    grads = (None,) + tuple(found[24:28])
    mask_count = mask_count.reshape(())
    loss_sum, table_g, place_g, norm_g = found[0:4]
    lane_news = found[4:10]
    side_news = found[10:16]
    moment_new, norm_new = found[16], found[23]
    news = found[17:23]
    return (
        loss_sum.reshape(()),
        mask_count,
        table_g.T,
        place_g.T,
        grads[1],
        grads[2],
        grads[3],
        grads[4],
        norm_g.T,
        lane_news[0],
        side_news[0],
        lane_news[1],
        side_news[1],
        side_news[2],
        lane_news[2],
        side_news[3],
        lane_news[3],
        side_news[4],
        lane_news[4],
        side_news[5],
        lane_news[5],
        moment_new.T,
        news[0].T,
        news[1].T,
        news[2],
        news[3],
        news[4],
        news[5],
        norm_new.T,
    )


def on_device(
    whole_mesh,
    long_ids,
    long_targets,
    long_mask,
    long_lengths,
    short_ids,
    short_targets,
    short_mask,
    short_lengths,
    table,
    position,
    qkv_weight,
    out_weight,
    in_weight,
    down_weight,
    norms,
    table_rows,
    table_cols,
    position_rows,
    position_cols,
    qkv_rows,
    qkv_cols,
    out_rows,
    out_cols,
    in_rows,
    in_cols,
    down_rows,
    down_cols,
    norm_moment,
):
    if whole_mesh == (8, 4):
        return on_slice(
            (long_ids, long_targets, long_mask, short_ids, short_targets, short_mask),
            (long_lengths, short_lengths),
            (table.T, position.T, qkv_weight, out_weight, in_weight, down_weight, norms.T),
            (table_rows, position_rows, qkv_cols, out_cols, in_cols, down_cols),
            (table_cols, position_cols, qkv_rows, out_rows, in_rows, down_rows),
            norm_moment.T,
        )
    devices = lax.axis_size(("dp", "seq"))
    seq_index = lax.axis_index("seq")
    held = norms.shape[0]

    span = long_ids.shape[1]
    long_place = seq_index * span + lax.iota(jnp.int32, span)
    long_keep = (long_place[None, :] < long_lengths[:, None]).astype(jnp.int32)
    short_keep = (lax.iota(jnp.int32, SPAN)[None, :] < short_lengths[:, None]).astype(jnp.int32)
    long_pack = jnp.stack((long_ids, long_targets, long_mask * long_keep, long_keep), 1)
    short_pack = jnp.stack((short_ids, short_targets, short_mask * short_keep, short_keep), 1)
    moved = lax.all_to_all(
        jnp.concatenate((long_pack, short_pack[1:]), 0), "seq", split_axis=0, concat_axis=0, tiled=True
    )
    tokens = jnp.concatenate((moved, short_pack[:1]), 0)
    ids, targets, weight, keep = (tokens[:, i].reshape(-1) for i in range(4))
    weight = weight.astype(F32)
    count = tokens.shape[0] * span
    last = count - span
    alone = seq_index == lax.axis_size("seq") - 1
    token = lax.iota(jnp.int32, count)
    place = jnp.where(alone | (token >= last), token % span, token)
    row = jnp.where(alone | (token >= last), token // span, 0)
    allowed_long = (row[:last, None] == row[None, :last]) & (keep[None, :last] > 0)
    allowed_short = jnp.broadcast_to(keep[None, last:] > 0, (span, span))

    here_count = jnp.sum(long_pack[:, 2]) + jnp.sum(short_pack[:, 2])
    tall = table.T
    counts = jnp.broadcast_to(jnp.stack((here_count // 256, here_count % 256)).astype(F32)[None], (held, 2))
    wide_shard = jnp.concatenate(
        (tall, norms, counts, jnp.zeros((held, PLACE_AT - COUNT_AT - 2), F32), position.T), 1
    )
    shards = (wide_shard, qkv_weight, out_weight, in_weight, down_weight)
    wide_w, qkv_w, out_w, in_w, down_w = (
        lax.all_gather(shard.astype(BF16), ("dp", "seq"), axis=0, tiled=True) for shard in shards
    )
    column = lax.broadcasted_iota(jnp.int32, (1, WIDE), 1)
    chosen = ((ids[:, None] == column) | ((place[:, None] + PLACE_AT) == column)).astype(BF16)
    gains = wide_w[:, NORM_AT : NORM_AT + 6].astype(F32)
    sums = jnp.sum(wide_w[:, COUNT_AT : COUNT_AT + 2].astype(F32), 0)
    mask_count = (sums[0] * 256.0 + sums[1]) / held
    inverse_count = 1.0 / mask_count

    embedded = mm(chosen, wide_w, (1, 1))
    first, normed_a, inverse_a = norm_forward(embedded, gains[:, 0], gains[:, 1])
    first_b = first.astype(BF16)
    qkv_b = mm(first_b, qkv_w, (1, 0)).astype(BF16)
    mix_long, total_long = attend(qkv_b[:last], allowed_long)
    mix_short, total_short = attend(qkv_b[last:], allowed_short)
    mixture = jnp.concatenate((mix_long, mix_short), 0)
    second, normed_b, inverse_b = norm_forward(first + mm(mixture, out_w, (1, 0)), gains[:, 2], gains[:, 3])
    second_b = second.astype(BF16)
    hidden = mm(second_b, in_w, (1, 0))
    active, slope = gelu_pair(hidden)
    active_b = active.astype(BF16)
    third, normed_c, inverse_c = norm_forward(second + mm(active_b, down_w, (1, 0)), gains[:, 4], gains[:, 5])
    third_b = third.astype(BF16)
    logits = jnp.where(column < VOCAB, mm(third_b, wide_w, (1, 0)), -1e30)
    highest = jnp.max(logits, -1, keepdims=True)
    log_sum = highest + jnp.log(jnp.sum(jnp.exp(logits - highest), -1, keepdims=True))
    onehot = targets[:, None] == column
    picked = jnp.sum(jnp.where(onehot, logits, 0.0), -1)
    loss_part = jnp.sum(weight * (log_sum[:, 0] - picked))
    grad_logit = (
        (jnp.exp(logits - log_sum) - onehot.astype(F32)) * (weight * inverse_count)[:, None]
    ).astype(BF16)
    grad_third = mm(grad_logit, wide_w, (1, 1))
    grad_second, gain_c, shift_c = norm_backward(grad_third, normed_c, inverse_c, gains[:, 4])
    grad_ffn = grad_second.astype(BF16)
    down_grad = mm(active_b, grad_ffn, (0, 0)).astype(BF16)
    grad_hidden = (mm(grad_ffn, down_w, (1, 1)) * slope).astype(BF16)
    in_grad = mm(second_b, grad_hidden, (0, 0)).astype(BF16)
    grad_second = grad_second + mm(grad_hidden, in_w, (1, 1))
    grad_first, gain_b, shift_b = norm_backward(grad_second, normed_b, inverse_b, gains[:, 2])
    grad_attn = grad_first.astype(BF16)
    out_grad = mm(mixture, grad_attn, (0, 0)).astype(BF16)
    grad_mix = mm(grad_attn, out_w, (1, 1)).astype(BF16)
    grad_qkv = jnp.concatenate(
        (
            attend_back(qkv_b[:last], allowed_long, total_long, grad_mix[:last]),
            attend_back(qkv_b[last:], allowed_short, total_short, grad_mix[last:]),
        ),
        0,
    )
    qkv_grad = mm(first_b, grad_qkv, (0, 0)).astype(BF16)
    grad_first = grad_first + mm(grad_qkv, qkv_w, (1, 1))
    grad_embed, gain_a, shift_a = norm_backward(grad_first, normed_a, inverse_a, gains[:, 0])
    wide_grad = mm(
        jnp.concatenate((third_b, grad_embed.astype(BF16)), 0),
        jnp.concatenate((grad_logit, chosen), 0),
        (0, 0),
    )
    norm_part = jnp.stack((gain_a, shift_a, gain_b, shift_b, gain_c, shift_c), 1)
    wide_grad = lax.dynamic_update_slice(wide_grad.astype(BF16), norm_part.astype(BF16), (0, NORM_AT))
    grads = (wide_grad, qkv_grad, out_grad, in_grad, down_grad)
    wide_g, qkv_g, out_g, in_g, down_g = (
        lax.psum_scatter(grad.astype(F32), ("dp", "seq"), scatter_dimension=0, tiled=True) for grad in grads
    )
    table_g, place_g = wide_g[:, :VOCAB], wide_g[:, PLACE_AT:]
    norm_g = wide_g[:, NORM_AT : NORM_AT + 6]

    decay = 1.0 - STEP ** (-0.8)
    matrices = (
        (qkv_weight, qkv_g, qkv_rows, qkv_cols),
        (out_weight, out_g, out_rows, out_cols),
        (in_weight, in_g, in_rows, in_cols),
        (down_weight, down_g, down_rows, down_cols),
    )
    wide = (
        (tall, table_g, table_cols, table_rows),
        (position.T, place_g, position_cols, position_rows),
    )
    row_news = [
        decay * member[2] + (1.0 - decay) * jnp.mean(member[1] * member[1] + SQUARE_FLOOR, 1)
        for member in matrices + wide
    ]
    col_parts = [jnp.sum(member[1] * member[1] + SQUARE_FLOOR, 0) for member in matrices + wide]
    row_totals = jnp.stack([jnp.sum(rows_new) for rows_new in row_news])
    weight_sq = jnp.stack([jnp.sum(member[0] * member[0]) for member in matrices + wide])
    stats = lax.psum(
        col_parts + [row_totals, weight_sq, jnp.sum(norms * norms, 0), loss_part.reshape(1)], ("dp", "seq")
    )
    updates = []
    cols_out = []
    for index, member in enumerate(matrices + wide):
        full_rows = member[0].shape[0] * devices
        cols_new = decay * member[3] + (1.0 - decay) * stats[index] / full_rows
        if index < 4:
            mean = stats[6][index] / full_rows
        else:
            mean = jnp.mean(cols_new)
        updates.append(member[1] * lax.rsqrt(row_news[index][:, None] * cols_new[None, :] / mean))
        cols_out.append(cols_new)
    moment_new = decay * norm_moment + (1.0 - decay) * (norm_g * norm_g + SQUARE_FLOOR)
    norm_update = norm_g * lax.rsqrt(moment_new)
    update_sq = jnp.stack([jnp.sum(update * update) for update in updates])
    totals = lax.psum((update_sq, jnp.sum(norm_update * norm_update, 0)), ("dp", "seq"))
    news = []
    for index, member in enumerate(matrices + wide):
        entries = member[0].shape[0] * member[0].shape[1] * devices
        clip = jnp.maximum(1.0, jnp.sqrt(totals[0][index] / entries))
        news.append(
            member[0] - learn_rate * jnp.sqrt(stats[7][index] / entries) * updates[index] / clip
        )
    norm_rows = norms.shape[0] * devices
    norm_clip = jnp.maximum(1.0, jnp.sqrt(totals[1] / norm_rows))
    norm_new = norms - learn_rate * jnp.sqrt(stats[8] / norm_rows) * norm_update / norm_clip
    return (
        stats[9][0],
        mask_count,
        table_g.T,
        place_g.T,
        qkv_g,
        out_g,
        in_g,
        down_g,
        norm_g,
        cols_out[4],
        row_news[4],
        cols_out[5],
        row_news[5],
        row_news[0],
        cols_out[0],
        row_news[1],
        cols_out[1],
        row_news[2],
        cols_out[2],
        row_news[3],
        cols_out[3],
        moment_new,
        news[4].T,
        news[5].T,
        news[0],
        news[1],
        news[2],
        news[3],
        norm_new,
    )


def solution(mesh):
    split, wide = P(("dp", "seq"), None), P(None, ("dp", "seq"))
    shard, same = P(("dp", "seq")), P()
    return jax.shard_map(
        functools.partial(on_device, (mesh.shape["dp"], mesh.shape["seq"])),
        mesh=mesh,
        in_specs=(P("dp", "seq"),) * 3
        + (P("dp"),)
        + (split,) * 3
        + (shard,)
        + (wide,) * 2
        + (split,) * 5
        + (same, shard) * 2
        + (shard, same) * 4
        + (split,),
        out_specs=(same, same)
        + (wide,) * 2
        + (split,) * 5
        + (same, shard) * 2
        + (shard, same) * 4
        + (split,)
        + (wide,) * 2
        + (split,) * 5,
        check_vma=False,
    )
```

```python
import functools

import jax
import jax.numpy as jnp
from jax import lax
from jax.experimental import pallas as pl
from jax.experimental.pallas import tpu as pltpu
from jax.sharding import PartitionSpec as P

D = 768
HEADS = 12
HEAD_DIM = 64
VOCAB = 4101
STEP = 10
SPAN = 128

EPSILON = 1e-12
SQUARE_FLOOR = 1e-30
learn_rate = 0.3

MESH = pl.DeviceIdType.MESH
F32 = jnp.float32
BF16 = jnp.bfloat16

NORM_AT = VOCAB
COUNT_AT = VOCAB + 6
TABLE_END = 4352
PLACE_AT = 4608
WIDE = PLACE_AT + 512

SHAPES = ((24, WIDE), (24, 3 * D), (24, D), (24, 4 * D), (96, D))
E_, Q_, O_, I_, D_ = range(5)
CLASS_A, CLASS_B, CLASS_C = (E_, O_), (Q_, D_), (I_,)
UP, DOWN, XWAY, YWAY, SIDE = range(5)


def here():
    dp, seq = lax.axis_index("dp"), lax.axis_index("seq")
    return dp // 2, dp % 2, seq // 2, seq % 2


def device(z, y, x, c):
    return {"dp": z * 2 + y, "seq": x * 2 + c}


def chip(z, y, x):
    return z * 4 + y * 2 + x


def all_peers():
    z, y, x, c = here()
    return (
        device(z + 1, y, x, c),
        device(z - 1, y, x, c),
        device(z, y, 1 - x, c),
        device(z, 1 - y, x, c),
        device(z, y, x, 1 - c),
    )


SUM_AT = (0, WIDE, WIDE + 3 * D, WIDE + 4 * D, WIDE + 8 * D, WIDE + 9 * D)
SUMS = WIDE + 9 * D + 256


def lanes_of(members):
    lane = lax.broadcasted_iota(jnp.int32, (1, 128), 1)
    row = jnp.zeros((1, 128), F32)
    for index, member in enumerate(members):
        row = jnp.where(lane == index, member, row)
    return row


def lane_at(row, index):
    lane = lax.broadcasted_iota(jnp.int32, row.shape, 1)
    return jnp.sum(jnp.where(lane == index, row, 0.0), 1, keepdims=True)


def column_of(row):
    size = row.shape[1]
    diagonal = lax.broadcasted_iota(jnp.int32, (size, size), 0) == lax.broadcasted_iota(
        jnp.int32, (size, size), 1
    )
    return jnp.sum(jnp.where(diagonal, row, 0.0), 1, keepdims=True)


def row_of(column):
    size = column.shape[0]
    diagonal = lax.broadcasted_iota(jnp.int32, (size, size), 0) == lax.broadcasted_iota(
        jnp.int32, (size, size), 1
    )
    return jnp.sum(jnp.where(diagonal, column, 0.0), 0, keepdims=True)


def as_row(ref):
    return ref[...].reshape(1, ref.shape[0])


def total_sum(array):
    return jnp.sum(jnp.sum(array, 1, keepdims=True), 0, keepdims=True)


def sum_everywhere(value, first, second, third, sems):
    z, y, x, c = here()
    spot = y * 2 + x
    side_send, side_recv, plane_send, plane_recv, z_send, z_recv = sems

    def copy(src, dst, send, recv, peer):
        return pltpu.make_async_remote_copy(
            src_ref=src, dst_ref=dst, send_sem=send, recv_sem=recv, device_id=peer, device_id_type=MESH
        )

    first[0] = value
    swap = copy(first.at[0], first.at[1], side_send, side_recv, device(z, y, x, 1 - c))
    swap.start()
    swap.wait_recv()
    second[spot] = first[0] + first[1]
    plane = []
    for i, (to_y, to_x) in enumerate(((y, 1 - x), (1 - y, x), (1 - y, 1 - x))):
        plane.append(
            copy(second.at[spot], second.at[spot], plane_send.at[i], plane_recv.at[i], device(z, to_y, to_x, c))
        )
        plane[i].start()
    for member in plane:
        member.wait_recv()
    third[z] = (second[0] + second[1]) + (second[2] + second[3])
    column = []
    for i in range(3):
        to_z = (z + 1 + i) % 4
        column.append(copy(third.at[z], third.at[z], z_send.at[i], z_recv.at[i], device(to_z, y, x, c)))
        column[i].start()
    for member in column:
        member.wait_recv()
    for member in [swap] + plane + column:
        member.wait_send()
    return (third[0] + third[1]) + (third[2] + third[3])


def gelu_pair(hidden):
    normal_cdf = 0.5 * (1.0 + lax.erf(hidden * 0.7071067811865476))
    return (
        hidden * normal_cdf,
        normal_cdf + hidden * jnp.exp(-0.5 * hidden * hidden) * 0.3989422804014327,
    )


def dot_nn(left, right):
    return jnp.dot(left, right, preferred_element_type=F32)


def dot_nt(left, right):
    return lax.dot_general(left, right, (((1,), (1,)), ((), ())), preferred_element_type=F32)


def dot_tn(left, right):
    return lax.dot_general(left, right, (((0,), (0,)), ((), ())), preferred_element_type=F32)


def at(index, size):
    if isinstance(index, int):
        return pl.ds(index * size, size)
    return pl.ds(pl.multiple_of(index * size, size), size)


def each(count, body):
    def step(index, carry):
        body(index)
        return carry

    lax.fori_loop(0, count, step, 0)


def each_unrolled(count, body):
    for index in range(count):
        body(index)


ROWS = 128
TILE = 256
HALF = 320
TABLE_TILES = TABLE_END // TILE


def head_lanes(first):
    lane = lax.broadcasted_iota(jnp.int32, (1, 128), 1)
    return (lane < HEAD_DIM) if first else (lane >= HEAD_DIM)


def layer_norm(value, gain, shift):
    centred = value - jnp.sum(value, 1, keepdims=True) / D
    inverse = lax.rsqrt(jnp.sum(centred * centred, 1, keepdims=True) / D + EPSILON)
    normed = centred * inverse
    return normed * gain + shift, normed, inverse


def layer_norm_back(grad, normed, inverse, gain):
    scaled = grad * gain
    return inverse * (
        scaled - jnp.sum(scaled, 1, keepdims=True) / D - normed * (jnp.sum(scaled * normed, 1, keepdims=True) / D)
    )


def put_lane(ref, rows, index, value):
    lane = lax.broadcasted_iota(jnp.int32, (1, 128), 1)
    ref[rows, :] = jnp.where(lane == index, value, ref[rows, :])


def set_bias(bias, cols, keys, last):
    same = cols[0:last, 4:5] == keys[1:2, 0:last]
    bias[...] = jnp.where(same & (keys[0:1, 0:last] > 0), 0.0, -1e30)


CHOOSE, EMBED, NORM_A, PROJECT, TURN_X, ATTEND, OUT, NORM_B, FEED_IN, TURN_A, FEED_OUT, REST = range(12)
FRONT = (
    67, 35, 36, 66, 32, 64, 100, 131, 1000, 69, 39, 1, 108, 161, 68, 33, 164, 73, 34, 4,
    99, 65, 71, 43, 50, 40, 75, 38, 3, 130, 162, 163, 160, 37, 6, 79, 172, 2, 0, 70,
    46, 96, 8, 76, 98, 166, 165, 44, 41, 169, 83, 42, 80, 74, 97, 175, 72, 47, 5, 129,
    78, 13, 170, 48, 10, 7, 168, 1001, 45, 132, 16, 104, 51, 82, 81, 49, 77, 174, 12, 1016,
    1017, 1018, 128, 18, 9, 11, 102, 1019, 1020, 1021, 103, 17, 1032, 177, 15, 14, 19, 173, 101, 167,
    109, 176, 135, 136, 1048, 1049, 1050, 1051, 1052, 1053, 1054, 1055, 133, 1056, 1064, 1080, 107, 1081, 171, 1082,
    106, 114, 1083, 105, 112, 1084, 178, 137, 134, 146, 179, 115, 142, 1085, 113, 141, 140, 1096, 1097, 1098,
    110, 111, 139, 1112, 1128, 1129, 1130, 138, 1131, 1132, 1133, 1134, 1135, 1136, 147, 144, 143, 145, 1137, 1138,
    1139, 1160, 1161, 1162, 1176,
)


def front_hooks():
    hooks, before = {}, []
    for task in FRONT:
        if task < 1000:
            before.append(task)
        else:
            hooks[((task - 1000) // 16, (task - 1000) % 16)] = before
            before = []
    return hooks


def front_kernel(*refs):
    raw, (long_len, short_len) = refs[0:13], refs[13:15]
    count_out, gains_out, side, cols, keys, squares = refs[15:21]
    x_t, mix_out, a_out, act_out, y_out, slope_out, qkv_out, na_out = refs[21:29]
    nb_outs, nc_outs, weight_outs = refs[29:31], refs[31:33], refs[33:38]
    wide, qkv_w, out_w, in_w, down_w = weights = refs[38:43]
    value, na, low_a, low_y, mix, qkv, act, slope, pick, pick_two, bias, turned = refs[43:55]
    nb, nc = refs[55:57], refs[57:59]
    held, wide_shard, merge, pieces, land = refs[59:72], refs[72], refs[73:78], refs[78], refs[79]
    raw_sem, swap_send, swap_recv, token_send, token_recv, send_sem, link_recv, side_recv = refs[80:88]
    out_sem, turn_sem = refs[88:90]
    z, y, x, c = here()
    peers = all_peers()
    me = chip(z, y, x)
    seq = x * 2 + c
    alone = seq // 3
    tokens = value.shape[0]
    last = tokens - SPAN
    hooks = front_hooks()

    barrier = pltpu.get_barrier_semaphore()
    cross = device(z, y, 1 - x, 1 - c)
    column = [device((z + 1 + i) % 4, y, x, c) for i in range(3)]
    for peer in [peers[XWAY], peers[YWAY], peers[SIDE], cross] + column:
        pl.semaphore_signal(barrier, inc=1, device_id=peer, device_id_type=MESH)
    raws = [pltpu.make_async_copy(raw[i], held[i], raw_sem.at[i]) for i in range(13)]
    for member in raws:
        member.start()
    for member in raws:
        member.wait()
    long_ids, long_targets, long_mask, short_ids, short_targets, short_mask, tall, place, qkv_s, out_s, in_s, down_s, norms = held

    pieces[...] = jnp.zeros(pieces.shape, jnp.int32)
    land[4] = jnp.zeros((8, SPAN), jnp.int32)
    lane = lax.broadcasted_iota(jnp.int32, (1, SPAN), 1)
    count = jnp.zeros((1, SPAN), jnp.int32)
    for t in range(5):
        if t < 3:
            ids, targets, mask = long_ids[t : t + 1, :], long_targets[t : t + 1, :], long_mask[t : t + 1, :]
            keep = (lane + seq * SPAN < long_len[t]).astype(jnp.int32)
        else:
            row = (1, 0)[t - 3]
            ids, targets, mask = (member[row : row + 1, :] for member in (short_ids, short_targets, short_mask))
            keep = (lane < short_len[row]).astype(jnp.int32)
        target = pieces.at[t] if t < 4 else land.at[4]
        target[0:1, :] = ids
        target[2:3, :] = targets
        target[3:4, :] = mask * keep
        target[5:6, :] = keep
        count = count + mask * keep
    count = jnp.sum(count.astype(F32), 1, keepdims=True)
    high = jnp.floor(count * (1.0 / 256.0))

    wide_shard[:, 0:4096] = tall[:, 0:4096]
    edge = jnp.zeros((24, 128), F32)
    tile_lane = lax.broadcasted_iota(jnp.int32, (24, 128), 1)
    tall_edge = tall[:, 4096:VOCAB]
    members = [lane_at(tall_edge, i) for i in range(VOCAB - 4096)]
    members += [column_of(norms[i : i + 1, :]) for i in range(6)]
    members += [high, count - high * 256.0]
    for i, member in enumerate(members):
        edge = jnp.where(tile_lane == i, member, edge)
    wide_shard[:, 4096:4224] = edge
    wide_shard[:, 4224:PLACE_AT] = jnp.zeros((24, PLACE_AT - 4224), F32)
    wide_shard[:, PLACE_AT:] = place[...]
    shards = (wide_shard, qkv_s, out_s, in_s, down_s)

    pl.semaphore_wait(barrier, 7)
    swaps = []
    for m in (E_, Q_, I_, D_, O_):
        size, half = SHAPES[m][0], SHAPES[m][1] // 2
        swaps.append(
            pltpu.make_async_remote_copy(
                src_ref=shards[m].at[:, pl.ds(pl.multiple_of((1 - c) * half, 128), half)],
                dst_ref=merge[m].at[pl.ds(pl.multiple_of(c * size, 8), size), :],
                send_sem=swap_send.at[m],
                recv_sem=swap_recv.at[m],
                device_id=peers[SIDE],
                device_id_type=MESH,
            )
        )
        swaps[-1].start()
    token_copies = []
    for i, (to_x, to_c) in enumerate(((x, 1 - c), (1 - x, c), (1 - x, 1 - c))):
        token_copies.append(
            pltpu.make_async_remote_copy(
                src_ref=pieces.at[to_x * 2 + to_c],
                dst_ref=land.at[seq],
                send_sem=token_send.at[i],
                recv_sem=token_recv.at[i],
                device_id=device(z, y, to_x, to_c),
                device_id_type=MESH,
            )
        )
        token_copies[-1].start()
    land[seq] = pieces[seq]

    def part(piece, k, half):
        m, skip, wide_part = PIECES[piece]
        size = 2 * SHAPES[m][0]
        start = pl.multiple_of(half * (SHAPES[m][1] // 2) + skip, 128)
        return weights[m].at[pl.ds(pl.multiple_of(k * size, size), size), pl.ds(start, wide_part)]

    FIRST_WAY, SECOND_WAY, SIDE_WAY = 0, 1, 2

    def copy_of(piece, k, way):
        ways = (XWAY, YWAY) if piece in Y_FIRST else (YWAY, XWAY)
        peer = column[way - 3] if way > 2 else peers[SIDE] if way == SIDE_WAY else peers[ways[way]]
        return pltpu.make_async_remote_copy(
            src_ref=part(piece, k, c),
            dst_ref=part(piece, k, c),
            send_sem=send_sem.at[piece, k, way],
            recv_sem=(side_recv if way == SIDE_WAY else link_recv).at[piece, k],
            device_id=peer,
            device_id_type=MESH,
        )

    def block_of(number):
        piece, task = number // 32, number % 32
        last_y = piece in Y_FIRST
        if task < 5:
            return piece, me, (3 + task if task < 3 else FIRST_WAY if task == 3 else SECOND_WAY,), False
        if task < 8:
            return piece, chip((z + task - 4) % 4, y, x), (FIRST_WAY, SECOND_WAY, SIDE_WAY), True
        if task < 12:
            t = (z + task - 8) % 4
            return piece, chip(t, y, 1 - x) if last_y else chip(t, 1 - y, x), (SECOND_WAY, SIDE_WAY), True
        t, other = (z + (task - 12) // 2) % 4, (task - 12) % 2
        if last_y:
            return piece, chip(t, 1 - y, 1 - x if other else x), (SIDE_WAY,), True
        return piece, chip(t, 1 - y if other else y, 1 - x), (SIDE_WAY,), True

    def transfer(number):
        piece, k, ways, waits = block_of(number)
        if waits:
            copy_of(piece, k, FIRST_WAY).wait_recv()
        for way in ways:
            copy_of(piece, k, way).start()

    def before(step, index, base=0):
        for (name, part_index), tasks in hooks.items():
            part_index = part_index - base
            if name != step or not tasks or (step == EMBED and not 0 <= part_index < 3):
                continue
            if index is None or isinstance(index, int):
                if part_index == (index or 0):
                    for number in tasks:
                        transfer(number)
            else:

                @pl.when(index == part_index)
                def _(tasks=tasks):
                    for number in tasks:
                        transfer(number)

    def need(*wanted):
        for piece in wanted:
            for k in range(16):
                pltpu.make_async_remote_copy(
                    src_ref=part(piece, k, 1 - c),
                    dst_ref=part(piece, k, 1 - c),
                    send_sem=send_sem.at[piece, k, SIDE_WAY],
                    recv_sem=side_recv.at[piece, k],
                    device_id=peers[SIDE],
                    device_id_type=MESH,
                ).wait_recv()

    for number, m in enumerate((E_, Q_, I_, D_, O_)):
        swaps[number].wait_recv()
        size, half = SHAPES[m][0], SHAPES[m][1] // 2
        merge[m][pl.ds(pl.multiple_of(c * size, 8), size), :] = shards[m][:, pl.ds(pl.multiple_of(c * half, 128), half)]
        rows = pl.ds(pl.multiple_of(me * 2 * size, 2 * size), 2 * size)
        weights[m][rows, pl.ds(pl.multiple_of(c * half, 128), half)] = merge[m][...].astype(BF16)
        for piece in range(6):
            if PIECES[piece][0] == m:
                copy_of(piece, me, SIDE_WAY).start()
    for copy in token_copies:
        copy.wait_recv()
    side[...] = jnp.zeros(side.shape, F32)
    keys[...] = jnp.zeros(keys.shape, jnp.int32)
    zeros = jnp.zeros((1, SPAN), F32)
    for b in range(5):
        tile = land[b]
        shift = b * SPAN * (1 - alone) if b < 4 else 0
        row = b * alone if b < 4 else 4
        spot = (lane + shift + PLACE_AT).astype(F32)
        row_lane = (lane * 0 + row).astype(F32)
        ids, targets, weight = (tile[i : i + 1].astype(F32) for i in (0, 2, 3))
        stacked = jnp.concatenate((ids, spot, targets, weight, row_lane, tile[5:6].astype(F32), zeros, zeros), 0)
        stacked = jnp.concatenate((stacked, jnp.zeros((120, SPAN), F32)), 0)
        cols[b * SPAN : (b + 1) * SPAN, :] = stacked.T.astype(jnp.int32)
        keys[0:1, b * SPAN : (b + 1) * SPAN] = tile[5:6]
        keys[1:2, b * SPAN : (b + 1) * SPAN] = lane * 0 + row
        keys[2:4, b * SPAN : (b + 1) * SPAN] = tile[2:4]
    set_bias(bias, cols, keys, last)
    found = [total_sum(member[...] * member[...]) for member in (tall, place, qkv_s, out_s, in_s, down_s)]
    norm_squares = jnp.sum(norms[...] * norms[...], 1, keepdims=True)
    squares[...] = lanes_of(found + [norm_squares[i : i + 1] for i in range(6)])

    turns, outs = {}, {}

    def turn_out(source, target, slot):
        if slot in turns:
            turns[slot].wait()

        def some(index):
            turned[slot, :, at(index, ROWS)] = source[at(index, ROWS), :].T

        each(tokens // ROWS, some)
        turns[slot] = pltpu.make_async_copy(turned.at[slot], target, turn_sem.at[slot])
        turns[slot].start()

    def put_out(name, source, target):
        outs[name] = pltpu.make_async_copy(source, target, out_sem.at[len(outs)])
        outs[name].start()

    picks = (pick, pick_two)
    halves = [pl.ds(half * HALF, HALF) for half in range(2)]
    for half in range(2):

        def choose(index):
            column_lane = lax.broadcasted_iota(jnp.int32, (1, TILE), 1) + index * TILE
            hit = (cols[halves[half], 0:1] == column_lane) | (cols[halves[half], 1:2] == column_lane)
            picks[half][:, at(index, TILE)] = jnp.where(hit, 1.0, 0.0).astype(BF16)

        before(CHOOSE, half)
        each(WIDE // TILE, choose)

    before(EMBED, 0)
    hooks.pop((EMBED, 0))
    need(1, 2)
    put_out("wide", wide, weight_outs[4])
    for half in range(2):

        def embed(index):
            before(EMBED, index, half * 3)
            value[halves[half], at(index, TILE)] = dot_nt(picks[half][...], wide[at(index, TILE), :])

        each_unrolled(D // TILE, embed)

    gains = wide[:, 4096:4224].astype(F32).T
    gains_out[...] = gains[0:16]
    counts = jnp.sum(gains[11:13], 1, keepdims=True) / 24.0
    mask_count = counts[0:1] * 256.0 + counts[1:2]
    count_out[...] = mask_count
    norm_rows = [gains_out[5 + i : 6 + i, :] for i in range(6)]
    before(NORM_A, None)

    def norm_a(index):
        rows = at(index, ROWS)
        found, normed, inverse = layer_norm(value[rows, :], norm_rows[0], norm_rows[1])
        value[rows, :] = found
        low_a[rows, :] = found.astype(BF16)
        na[rows, :] = normed
        put_lane(side, rows, 12, inverse)

    each(tokens // ROWS, norm_a)
    put_out("na", na, na_out)
    before(PROJECT, 0)
    need(0)

    def project(index):
        before(PROJECT, index)
        qkv[:, at(index, TILE)] = dot_nn(low_a[...], qkv_w[:, at(index, TILE)]).astype(BF16)

    hooks.pop((PROJECT, 0))
    each_unrolled(3 * D // TILE, project)
    put_out("qkv", qkv, qkv_out)
    put_out("qkv_w", qkv_w, weight_outs[0])
    before(TURN_X, None)
    turn_out(low_a, x_t, 0)

    def attend_pair(pair):
        before(ATTEND, pair)
        for start, size in ((0, last), (last, SPAN)):
            rows = pl.ds(start, size)
            query = qkv[rows, at(pair, 128)]
            key = qkv[rows, pl.ds(pl.multiple_of(D + pair * 128, 128), 128)]
            val = qkv[rows, pl.ds(pl.multiple_of(2 * D + pair * 128, 128), 128)]
            mask = bias[...] if start == 0 else jnp.where(keys[0:1, last:tokens] > 0, 0.0, -1e30)
            mixed = []
            for first in (True, False):
                chosen = jnp.where(head_lanes(first), query, jnp.zeros_like(query))
                scores = dot_nt(chosen, key) * 0.125 + mask
                highest = jnp.max(scores, 1, keepdims=True)
                raised = jnp.exp(scores - highest)
                summed = jnp.sum(raised, 1, keepdims=True)
                shares = (raised * (1.0 / summed)).astype(BF16)
                mixed.append(dot_nn(shares, val))
                put_lane(side, rows, 2 * pair + (0 if first else 1), highest + jnp.log(summed))
            mix[rows, at(pair, 128)] = jnp.where(head_lanes(True), mixed[0], mixed[1]).astype(BF16)

    each(HEADS // 2, attend_pair)
    before(OUT, 0)
    hooks.pop((OUT, 0))
    need(5)

    def out_project(index):
        before(OUT, index)
        value[:, at(index, TILE)] = value[:, at(index, TILE)] + dot_nn(mix[...], out_w[:, at(index, TILE)])

    each_unrolled(D // TILE, out_project)
    put_out("out_w", out_w, weight_outs[1])
    put_out("mix", mix, mix_out)
    before(NORM_B, None)

    def norm_b(index):
        rows = at(index, ROWS)
        found, normed, inverse = layer_norm(value[rows, :], norm_rows[2], norm_rows[3])
        value[rows, :] = found
        low_y[rows, :] = found.astype(BF16)
        nb[0][rows, :], nb[1][rows, :] = split_two(normed)
        put_lane(side, rows, 13, inverse)

    each(tokens // ROWS, norm_b)
    put_out("a", low_y, a_out)
    put_out("nb0", nb[0], nb_outs[0])
    put_out("nb1", nb[1], nb_outs[1])
    before(FEED_IN, 0)
    hooks.pop((FEED_IN, 0))
    need(3)

    def feed_in(index):
        before(FEED_IN, index)
        hidden = dot_nn(low_y[...], in_w[:, at(index, TILE)])
        active, slant = gelu_pair(hidden)
        active = active.astype(BF16)
        act[:, at(index, TILE)] = active
        slope[:, at(index, TILE)] = slant.astype(BF16)

    each_unrolled(4 * D // TILE, feed_in)
    put_out("act", act, act_out)
    put_out("slope", slope, slope_out)
    put_out("in_w", in_w, weight_outs[2])
    before(TURN_A, None)
    before(FEED_OUT, 0)
    hooks.pop((FEED_OUT, 0))
    need(4)

    def feed_out(index):
        before(FEED_OUT, index)
        value[:, at(index, TILE)] = value[:, at(index, TILE)] + dot_nn(act[...], down_w[:, at(index, TILE)])

    each_unrolled(D // TILE, feed_out)
    put_out("down_w", down_w, weight_outs[3])
    before(REST, None)
    turns[0].wait()

    def norm_c(index):
        rows = at(index, ROWS)
        found, normed, inverse = layer_norm(value[rows, :], norm_rows[4], norm_rows[5])
        low_a[rows, :] = found.astype(BF16)
        nc[0][rows, :], nc[1][rows, :] = split_two(normed)
        put_lane(side, rows, 14, inverse)

    each(tokens // ROWS, norm_c)
    put_out("y", low_a, y_out)
    put_out("nc0", nc[0], nc_outs[0])
    put_out("nc1", nc[1], nc_outs[1])
    for swap in swaps:
        swap.wait_send()
    for copy in token_copies:
        copy.wait_send()
    for piece in range(6):
        copy_of(piece, me, SIDE_WAY).wait_send()
    for number in FRONT:
        if number < 1000:
            piece, k, ways, _ = block_of(number)
            for way in ways:
                copy_of(piece, k, way).wait_send()
    for copy in outs.values():
        copy.wait()


def front(large, lengths):
    vmem, hbm = pl.BlockSpec(memory_space=pltpu.VMEM), pl.BlockSpec(memory_space=pl.ANY)
    smem = pl.BlockSpec(memory_space=pltpu.SMEM)
    shape, dma = jax.ShapeDtypeStruct, pltpu.SemaphoreType.DMA
    tokens = 5 * SPAN
    small = [shape((1, 1), F32), shape((16, D), F32), shape((tokens, 128), F32)]
    small += [shape((tokens, 128), jnp.int32), shape((8, tokens), jnp.int32), shape((1, 128), F32)]
    out = [shape((D, tokens), BF16)] + [shape((tokens, width), BF16) for width in (D, D, 4 * D, D, 4 * D, 3 * D)]
    out += [shape((tokens, D), F32)] + [shape((tokens, D), BF16)] * 4
    out += [shape((32 * SHAPES[m][0], SHAPES[m][1]), BF16) for m in (Q_, O_, I_, D_, E_)]
    return pl.pallas_call(
        front_kernel,
        out_shape=small + out,
        in_specs=[hbm] * 13 + [smem] * 2,
        out_specs=[vmem] * len(small) + [hbm] * len(out),
        scratch_shapes=[pltpu.VMEM((32 * size, wide), BF16) for size, wide in SHAPES]
        + [pltpu.VMEM((tokens, D), F32)] * 2
        + [pltpu.VMEM((tokens, D), BF16)] * 3
        + [
            pltpu.VMEM((tokens, 3 * D), BF16),
            pltpu.VMEM((tokens, 4 * D), BF16),
            pltpu.VMEM((tokens, 4 * D), BF16),
            pltpu.VMEM((HALF, WIDE), BF16),
            pltpu.VMEM((HALF, WIDE), BF16),
            pltpu.VMEM((tokens - SPAN, tokens - SPAN), F32),
            pltpu.VMEM((1, D, tokens), BF16),
        ]
        + [pltpu.VMEM((tokens, D), BF16)] * 4
        + [pltpu.VMEM(member.shape, member.dtype) for member in large]
        + [pltpu.VMEM(SHAPES[E_], F32)]
        + [pltpu.VMEM((2 * size, wide // 2), F32) for size, wide in SHAPES]
        + [pltpu.VMEM((4, 8, SPAN), jnp.int32), pltpu.VMEM((5, 8, SPAN), jnp.int32)]
        + [dma((13,)), dma((5,)), dma((5,)), dma((3,)), dma((3,)), dma((6, 16, 6)), dma((6, 16)), dma((6, 16))]
        + [dma((18,)), dma((1,))],
        compiler_params=pltpu.CompilerParams(
            collective_id=0, has_side_effects=True, vmem_limit_bytes=63 * 1024 * 1024
        ),
    )(*large, *lengths)


PACK = 256


def split_two(value):
    high = value.astype(BF16)
    return high, (value - high.astype(F32)).astype(BF16)


def middle_kernel(*refs):
    (wide_h, qkv_wh, out_wh, in_wh, down_h, y_h, act_h, a_h, mix_h, slope_h, qkv_h, na_h) = refs[0:12]
    nb_h, nc_h = refs[12:14], refs[14:16]
    cols, keys, side, gains, count = refs[16:21]
    loss_out, norm_out = refs[21:23]
    glog_out, y_t, a_t, mix_t, act_t, ge_t, gffn_out, gh_out, gattn_out, gqkv_out = refs[23:33]
    wide, qkv_w, out_w, in_w, plain, qkv, na = refs[33:40]
    nb, nc = refs[40:42], refs[42:44]
    slope_ring, act_ring, down_ring = refs[44:47]
    logits, glog, gh, gffn, gattn, gatt, packed, grad, turned, act_turned = refs[47:57]
    back_kv, gqkv, whole_grad, pick, pick_t, bias, side_pack, side_turned, dq, ge = refs[57:67]
    load_sem, ring_sem, out_sem = refs[67:70]
    tokens = cols.shape[0]
    names = ("wide", "y", "nc0", "nc1", "in_w", "nb0", "nb1", "out_w", "qkv", "qkv_w", "na")
    sources = (wide_h, y_h, nc_h[0], nc_h[1], in_wh, nb_h[0], nb_h[1], out_wh, qkv_h, qkv_wh, na_h)
    targets = (wide, plain, nc[0], nc[1], in_w, nb[0], nb[1], out_w, qkv, qkv_w, na)
    loads = {name: pltpu.make_async_copy(sources[i], targets[i], load_sem.at[i]) for i, name in enumerate(names)}
    for name in ("y", "wide"):
        loads[name].start()

    weight_row = keys[3:4, :].astype(F32)
    weight_col = cols[:, 3:4].astype(F32)
    earlier = lax.broadcasted_iota(jnp.int32, (tokens, tokens), 0) < lax.broadcasted_iota(jnp.int32, (tokens, tokens), 1)
    later = lax.broadcasted_iota(jnp.int32, (tokens, tokens), 0) > lax.broadcasted_iota(jnp.int32, (tokens, tokens), 1)
    rank_row = dot_nn(
        jnp.broadcast_to(weight_row, (16, tokens)).astype(BF16), jnp.where(earlier, 1.0, 0.0).astype(BF16)
    )[0:1]
    rank_col = dot_nn(
        jnp.where(later, 1.0, 0.0).astype(BF16), jnp.broadcast_to(weight_col, (tokens, 128)).astype(BF16)
    )[:, 0:1]
    rank_row = jnp.where(weight_row > 0, rank_row, -1.0)
    rank_col = jnp.where(weight_col > 0, rank_col, -1.0)
    blocks = (jnp.sum(weight_row).astype(jnp.int32) + (PACK - 1)) // PACK
    blocks = jnp.maximum(blocks, 1)
    inverse_count = 1.0 / count[...]
    norm_rows = [gains[5 + i : 6 + i, :] for i in range(6)]
    loss_out[...] = jnp.zeros((1, 1), F32)
    norm_out[...] = jnp.zeros(norm_out.shape, F32)
    back_kv[...] = jnp.zeros(back_kv.shape, F32)
    whole_grad[...] = jnp.zeros(whole_grad.shape, F32)
    gqkv[:, 0:D] = jnp.zeros((tokens, D), BF16)
    side_first = side[...].astype(BF16)
    rest = side[...] - side_first.astype(F32)
    side_second = rest.astype(BF16)
    side_third = (rest - side_second.astype(F32)).astype(BF16)
    waited = set()

    def load_plain(source):
        return pltpu.make_async_copy(source, plain, load_sem.at[1])

    def ring(kind, source, target):
        def copy(j):
            piece = source.at[at(j, TILE), :] if kind == 2 else source.at[:, at(j, TILE)]
            return pltpu.make_async_copy(piece, target.at[j % 2], ring_sem.at[kind * 2 + j % 2])

        return copy

    rings = [ring(0, slope_h, slope_ring), ring(1, act_h, act_ring), ring(2, down_h, down_ring)]
    outs = [
        (glog, glog_out, 0),
        (turned.at[0], y_t, 1),
        (turned.at[1], a_t, 1),
        (turned.at[2], mix_t, 1),
        (act_turned, act_t, 1),
        (gffn, gffn_out, 0),
        (gh, gh_out, 0),
        (gattn, gattn_out, 0),
    ]

    def out_copy(i, block):
        source, target, axis = outs[i]
        place = at(block, PACK)
        return pltpu.make_async_copy(
            source, target.at[place, :] if axis == 0 else target.at[:, place], out_sem.at[i]
        )

    def wait_load(name):
        loads[name].wait()

    wait_load("wide")
    for name in names[2:]:
        loads[name].start()

    def block_step(block, carry):
        slot_col = lax.broadcasted_iota(jnp.int32, (PACK, 1), 0).astype(F32) + (block * PACK).astype(F32)
        slot_row = lax.broadcasted_iota(jnp.int32, (1, PACK), 1).astype(F32) + (block * PACK).astype(F32)
        hit = jnp.where(rank_row == slot_col, 1.0, 0.0)
        pick[...] = hit.astype(BF16)
        hit_t = jnp.where(rank_col == slot_row, 1.0, 0.0)
        pick_t[...] = hit_t.astype(BF16)
        target = jnp.sum(hit * keys[2:3, :].astype(F32), 1, keepdims=True)
        weight = jnp.sum(hit, 1, keepdims=True)
        row_col = cols[:, 4:5].astype(F32)
        row_of_token = jnp.sum(hit_t * row_col, 0, keepdims=True)
        bias[...] = jnp.where((row_of_token == row_col) & (cols[:, 5:6] > 0), 0.0, -1e30)
        side_pack[...] = (
            dot_nn(pick[...], side_first) + dot_nn(pick[...], side_second) + dot_nn(pick[...], side_third)
        )
        side_turned[...] = side_pack[...].T
        for kind in range(3):
            for j in range(2):
                rings[kind](j).start()
        load_plain(y_h).wait()
        packed[...] = dot_nn(pick[...], plain[...]).astype(BF16)
        load_plain(a_h).start()
        turned[0] = packed[...].T
        out_copy(1, block).start()

        def lanes(index):
            return (lax.broadcasted_iota(jnp.int32, (1, TILE), 1) + index * TILE).astype(F32)

        highest = jnp.full((PACK, 128), -1e30, F32)
        for index in range(TABLE_TILES):
            found = dot_nn(packed[...], wide[:, at(index, TILE)])
            if index == TABLE_TILES - 1:
                found = jnp.where(lanes(index) < VOCAB, found, -1e30)
            logits[:, at(index, TILE)] = found
            highest = jnp.maximum(highest, jnp.maximum(found[:, 0:128], found[:, 128:256]))
        highest = jnp.max(highest, 1, keepdims=True)
        summed, picked = jnp.zeros((PACK, 128), F32), jnp.zeros((PACK, 128), F32)
        for index in range(TABLE_TILES):
            found = logits[:, at(index, TILE)]
            raised = jnp.exp(found - highest)
            logits[:, at(index, TILE)] = raised
            own = jnp.where(lanes(index) == target, found, 0.0)
            summed = summed + raised[:, 0:128] + raised[:, 128:256]
            picked = picked + own[:, 0:128] + own[:, 128:256]
        summed = jnp.sum(summed, 1, keepdims=True)
        picked = jnp.sum(picked, 1, keepdims=True)
        loss_out[...] = loss_out[...] + jnp.sum(weight * (highest + jnp.log(summed) - picked), 0, keepdims=True)
        scale = weight * inverse_count
        share = scale / summed
        for index in range(TABLE_TILES):
            found = logits[:, at(index, TILE)] * share - jnp.where(lanes(index) == target, scale, 0.0)
            glog[:, at(index, TILE)] = found.astype(BF16)
        out_copy(0, block).start()
        for index in range(D // TILE):
            grad[:, at(index, TILE)] = dot_nt(glog[...], wide[at(index, TILE), 0:TABLE_END])

        @pl.when(block == 0)
        def _():
            for name in names[2:4]:
                wait_load(name)

        normed = dot_nn(pick[...], nc[0][...]) + dot_nn(pick[...], nc[1][...])
        found = grad[...]
        back = layer_norm_back(found, normed, lane_at(side_pack[...], 14), norm_rows[4])
        norm_out[4:5, :] = norm_out[4:5, :] + jnp.sum(found * normed, 0, keepdims=True)
        norm_out[5:6, :] = norm_out[5:6, :] + jnp.sum(found, 0, keepdims=True)
        grad[...] = back
        gffn[...] = back.astype(BF16)
        out_copy(5, block).start()

        load_plain(a_h).wait()
        turned[1] = dot_nn(pick[...], plain[...]).astype(BF16).T
        out_copy(2, block).start()
        load_plain(mix_h).start()
        for index in range(4 * D // TILE):
            for kind in range(3):
                rings[kind](index).wait()
            slant = dot_nn(pick[...], slope_ring[index % 2])
            found = dot_nt(gffn[...], down_ring[index % 2]) * slant
            gh[:, at(index, TILE)] = found.astype(BF16)
            act_turned[at(index, TILE), :] = dot_nn(pick[...], act_ring[index % 2]).astype(BF16).T
            if index + 2 < 4 * D // TILE:
                for kind in range(3):
                    rings[kind](index + 2).start()
        out_copy(6, block).start()
        out_copy(4, block).start()
        load_plain(mix_h).wait()
        turned[2] = dot_nn(pick[...], plain[...]).astype(BF16).T
        out_copy(3, block).start()
        load_plain(y_h).start()

        @pl.when(block == 0)
        def _():
            for name in names[4:8]:
                wait_load(name)

        for index in range(D // TILE):
            grad[:, at(index, TILE)] = grad[:, at(index, TILE)] + dot_nt(gh[...], in_w[at(index, TILE), :])
        normed = dot_nn(pick[...], nb[0][...]) + dot_nn(pick[...], nb[1][...])
        found = grad[...]
        back = layer_norm_back(found, normed, lane_at(side_pack[...], 13), norm_rows[2])
        norm_out[2:3, :] = norm_out[2:3, :] + jnp.sum(found * normed, 0, keepdims=True)
        norm_out[3:4, :] = norm_out[3:4, :] + jnp.sum(found, 0, keepdims=True)
        gattn[...] = back.astype(BF16)
        out_copy(7, block).start()
        high, low = split_two(back)
        whole_grad[...] = whole_grad[...] + dot_nn(pick_t[...], high) + dot_nn(pick_t[...], low)
        for index in range(D // TILE):
            gatt[:, at(index, TILE)] = dot_nt(gattn[...], out_w[at(index, TILE), :]).astype(BF16)

        @pl.when(block == 0)
        def _():
            wait_load("qkv")

        def attend_pair_back(pair):
            spots = [pl.ds(pl.multiple_of(i * D + pair * 128, 128), 128) for i in range(3)]
            query = dot_nn(pick[...], qkv[:, spots[0]]).astype(BF16)
            key, val = qkv[:, spots[1]], qkv[:, spots[2]]
            given = gatt[:, at(pair, 128)]
            key_t = key.T
            found = []
            for first in (True, False):
                lanes_here = head_lanes(first)
                chosen = jnp.where(lanes_here, query, jnp.zeros_like(query))
                mine = jnp.where(lanes_here, given, jnp.zeros_like(given))
                total = side_turned[pl.ds(2 * pair + (0 if first else 1), 1), :]
                shares = jnp.exp(dot_nt(key, chosen) * 0.125 + bias[...] - total)
                grad_share = dot_nt(val, mine)
                middle = jnp.sum(shares * grad_share, 0, keepdims=True)
                grad_score = (shares * (grad_share - middle)).astype(BF16)
                found.append(
                    (
                        dot_nn(key_t, grad_score) * 0.125,
                        dot_nn(grad_score, query) * 0.125,
                        dot_nn(shares.astype(BF16), given),
                    )
                )
            lanes_here = head_lanes(True)
            both = jnp.concatenate((found[0][0][0:HEAD_DIM], found[1][0][HEAD_DIM:]), 0)
            dq[at(pair, 128), :] = both.astype(BF16)
            for i in (1, 2):
                spot = pl.ds(pl.multiple_of((i - 1) * D + pair * 128, 128), 128)
                back_kv[:, spot] = back_kv[:, spot] + jnp.where(lanes_here, found[0][i], found[1][i])

        each(HEADS // 2, attend_pair_back)
        gqkv[:, 0:D] = (gqkv[:, 0:D].astype(F32) + dot_nt(pick_t[...], dq[...])).astype(BF16)
        for i in range(len(outs)):
            out_copy(i, block).wait()
        return carry

    lax.fori_loop(0, blocks, block_step, 0)
    load_plain(y_h).wait()
    gqkv[:, D:] = back_kv[...].astype(BF16)
    copy_qkv = pltpu.make_async_copy(gqkv, gqkv_out, out_sem.at[8])
    copy_qkv.start()
    for ref in (glog, gffn, gh, gattn):
        ref[...] = jnp.zeros(ref.shape, BF16)
    for block in range(1, 3):

        @pl.when(blocks <= block)
        def _():
            for i in range(len(outs)):
                out_copy(i, block).start()

    for name in names[9:]:
        wait_load(name)
    for index in range(D // TILE):
        whole_grad[:, at(index, TILE)] = whole_grad[:, at(index, TILE)] + dot_nt(gqkv[...], qkv_w[at(index, TILE), :])
    zero = jnp.zeros((1, D), F32)

    def norm_a_back(index, carry):
        gain, shift = carry
        rows = at(index, ROWS)
        inverse = lane_at(side[rows, :], 12)
        found, normed = whole_grad[rows, :], na[rows, :]
        ge[:, rows] = layer_norm_back(found, normed, inverse, norm_rows[0]).astype(BF16).T
        return gain + jnp.sum(found * normed, 0, keepdims=True), shift + jnp.sum(found, 0, keepdims=True)

    gain, shift = lax.fori_loop(0, tokens // ROWS, norm_a_back, (zero, zero))
    norm_out[0:1, :] = gain
    norm_out[1:2, :] = shift
    copy_ge = pltpu.make_async_copy(ge, ge_t, out_sem.at[9])
    copy_ge.start()
    for block in range(1, 3):

        @pl.when(blocks <= block)
        def _():
            for i in range(len(outs)):
                out_copy(i, block).wait()

    copy_qkv.wait()
    copy_ge.wait()


def middle(large, small):
    tokens = 5 * SPAN
    slots = 3 * PACK
    vmem, hbm = pl.BlockSpec(memory_space=pltpu.VMEM), pl.BlockSpec(memory_space=pl.ANY)
    shape, dma = jax.ShapeDtypeStruct, pltpu.SemaphoreType.DMA
    out = [shape((slots, TABLE_END), BF16)] + [shape((D, slots), BF16)] * 3 + [shape((4 * D, slots), BF16)]
    out += [shape((D, tokens), BF16), shape((slots, D), BF16), shape((slots, 4 * D), BF16), shape((slots, D), BF16)]
    out += [shape((tokens, 3 * D), BF16)]

    def rows(count, width, kind=BF16):
        return pltpu.VMEM((count, width), kind)

    scratch = [rows(D, WIDE), rows(D, 3 * D), rows(D, D), rows(D, 4 * D), rows(tokens, D), rows(tokens, 3 * D)]
    scratch += [rows(tokens, D, F32)] + [rows(tokens, D)] * 4
    scratch += [pltpu.VMEM((2, tokens, TILE), BF16)] * 2 + [pltpu.VMEM((2, TILE, D), BF16)]
    scratch += [rows(PACK, TABLE_END, F32), rows(PACK, TABLE_END), rows(PACK, 4 * D)] + [rows(PACK, D)] * 4
    scratch += [rows(PACK, D, F32), pltpu.VMEM((3, D, PACK), BF16), rows(4 * D, PACK)]
    scratch += [rows(tokens, 2 * D, F32), rows(tokens, 3 * D), rows(tokens, D, F32), rows(PACK, tokens)]
    scratch += [rows(tokens, PACK), rows(tokens, PACK, F32), rows(PACK, 128, F32), rows(128, PACK, F32)]
    scratch += [rows(D, PACK), rows(D, tokens)]
    scratch += [dma((11,)), dma((6,)), dma((10,))]
    return pl.pallas_call(
        middle_kernel,
        out_shape=[shape((1, 1), F32), shape((6, D), F32)] + out,
        in_specs=[hbm] * 16 + [vmem] * 5,
        out_specs=[vmem] * 2 + [hbm] * len(out),
        scratch_shapes=scratch,
        compiler_params=pltpu.CompilerParams(vmem_limit_bytes=63 * 1024 * 1024),
    )(*large, *small)


LEFT = 768
PIECES = ((Q_, 0, 1152), (E_, 0, 1280), (E_, 1280, 1280), (I_, 0, 1536), (D_, 0, 384), (O_, 0, 384))
Y_FIRST = (0, 1, 4)
TASKS = (
    0, 1, 96, 9, 4, 129, 97, 2, 103, 5, 99, 7, 8, 6, 101, 128, 102, 105,
    100, 132, 133, 64, 108, 12, 104, 136, 139, 134, 65, 15, 107, 111, 109, 137, 161, 13,
    160, 3, 131, 11, 141, 142, 70, 32, 68, 112, 110, 76, 140, 16, 168, 67, 144, 72,
    169, 75, 135, 71, 33, 36, 69, 143, 166, 173, 38, 98, 39, 43, 78, 130, 167, 73,
    37, 40, 79, 44, 34, 164, 46, 66, 77, 14, 47, 165, 45, 162, 171, 41, 172, 176,
    80, 138, 174, 74, 48, 10, 106, 42, 175, 35, 81, 145, 163, 170, 113, 17, 49, 177,
)


def reduce_kernel(*refs):
    given, (cols, norm_sums, loss, squares) = refs[0:11], refs[11:15]
    y_t, ge_t, glog, x_t, gqkv, mix_t, gattn, a_t, gh, act_t, gffn = given
    lane_olds, side_olds, moment = refs[15:21], refs[21:27], refs[27]
    outs, sums_out, totals_out = refs[28:33], refs[33], refs[34]
    own, side, first, second, column, fin = (refs[35 + 6 * i : 41 + 6 * i] for i in range(6))
    left, (glog_v, gqkv_v, gattn_v, gh_v, gffn_v), stage, tails, norm_t = refs[71:78], refs[78:83], refs[83], refs[84], refs[85]
    spread, spread_small = refs[86:89], refs[89:92]
    load_sem, ring_sem, tail_sem, side_recv, first_send, first_recv, second_send, second_recv = refs[92:100]
    z_send, z_recv, swap_send, swap_recv = refs[100:104]
    sems, small_sems = refs[104:110], refs[110:116]
    z, y, x, c = here()
    peers = all_peers()
    me = chip(z, y, x)

    barrier = pltpu.get_barrier_semaphore()
    greeted = [peers[XWAY], peers[YWAY], peers[SIDE], device(z, 1 - y, 1 - x, c)]
    greeted += [device((z + 1 + i) % 4, y, x, c) for i in range(3)]
    for peer in greeted:
        pl.semaphore_signal(barrier, inc=1, device_id=peer, device_id_type=MESH)

    tokens = cols.shape[0]

    def act_part(group):
        return act_t.at[pl.ds(LEFT * group, LEFT), 0:tokens]

    operands = (
        ((x_t, left[1]), (gqkv, gqkv_v)),
        ((y_t.at[:, 0:tokens], left[2]), (ge_t, left[3]), (glog.at[0:tokens, :], glog_v)),
        (),
        ((a_t.at[:, 0:tokens], left[0]), (gh.at[0:tokens, :], gh_v)),
        ((gffn.at[0:tokens, :], gffn_v), (act_part(0), left[5]), (act_part(1), left[6])),
        ((mix_t.at[:, 0:tokens], left[4]), (gattn.at[0:tokens, :], gattn_v)),
    )
    loads = {}
    waited = set()
    for task in TASKS:
        piece = task // 32 if task // 32 != 2 else 1
        if piece not in loads:
            loads[piece] = []
            for source, target in operands[piece]:
                number = sum(len(member) for member in loads.values())
                loads[piece].append(pltpu.make_async_copy(source, target, load_sem.at[number]))
                loads[piece][-1].start()

    def loaded(piece):
        piece = 1 if piece == 2 else piece
        if piece not in waited:
            waited.add(piece)
            for member in loads[piece]:
                member.wait()

    norm_t[...] = jnp.zeros(norm_t.shape, F32)
    norm_t[5:11, :] = norm_sums[...]
    pl.semaphore_wait(barrier, 7)

    def size_of(piece):
        return 2 * SHAPES[PIECES[piece][0]][0]

    def slot(ref, piece, index):
        size = size_of(piece)
        return ref[piece].at[pl.ds(pl.multiple_of(index * size, size), size), :]

    def half_of(piece):
        return SHAPES[PIECES[piece][0]][1] // 2

    def chosen(start):
        lane = lax.broadcasted_iota(jnp.int32, (1, TILE), 1) + start
        hit = (cols[:, 0:1] == lane) | (cols[:, 1:2] == lane)
        return jnp.where(hit, 1.0, 0.0).astype(BF16)

    def ring_copy(piece, rows, lanes, number, index):
        place = lax.rem(number, 3)
        return pltpu.make_async_remote_copy(
            src_ref=stage.at[place],
            dst_ref=side[piece].at[rows, lanes],
            send_sem=ring_sem.at[place],
            recv_sem=side_recv.at[piece, index],
            device_id=peers[SIDE],
            device_id_type=MESH,
        )

    def tail_copy(piece, rows, lanes, number, index):
        return pltpu.make_async_remote_copy(
            src_ref=tails.at[number],
            dst_ref=side[piece].at[rows, lanes],
            send_sem=tail_sem.at[number],
            recv_sem=side_recv.at[piece, index],
            device_id=peers[SIDE],
            device_id_type=MESH,
        )

    whole = pl.ds(0, LEFT)
    ring_count, tail_count = [0], [0]

    def give(piece, rows, lanes, number, index):
        def before():
            @pl.when(number >= 3)
            def _():
                ring_copy(piece, rows, lanes, number, index).wait_send()

        def write(value):
            stage[lax.rem(number, 3)] = value.astype(BF16)

        return before, write, lambda: ring_copy(piece, rows, lanes, number, index).start()

    def keep(piece, rows, lanes):
        def write(value):
            own[piece][rows, lanes] = value.astype(BF16)

        return lambda: None, write, lambda: None

    def plain(piece, mine, source, right, group):
        wide = PIECES[piece][2]
        half = c if mine else 1 - c
        rows = pl.ds(LEFT * group, LEFT)
        base = ring_count[0]

        def step(j):
            lanes = at(j, TILE)
            before, write, after = keep(piece, rows, lanes) if mine else give(
                piece, rows, lanes, base + j, group * (wide // TILE) + j
            )
            before()
            write(dot_nn(source[...], right[:, pl.ds(pl.multiple_of(half * wide + j * TILE, 128), TILE)]))
            after()

        each(wide // TILE, step)
        if not mine:
            ring_count[0] += wide // TILE
        if wide % TILE:
            start = wide - 128
            value = dot_nn(source[...], right[:, pl.ds(pl.multiple_of(half * wide + start, 128), 128)])
            if mine:
                own[piece][rows, start:wide] = value.astype(BF16)
            else:
                number = tail_count[0]
                tail_count[0] += 1
                groups = SHAPES[PIECES[piece][0]][0] // 24
                tails[number] = value.astype(BF16)
                tail_copy(piece, rows, pl.ds(start, 128), number, groups * (wide // TILE) + group).start()

    def wide_product(piece, mine):
        half = c if mine else 1 - c
        wide = half_of(piece)
        skip = PIECES[piece][1] // TILE
        base = ring_count[0]

        def both(j):
            start = pl.multiple_of(half * wide + (skip + j) * TILE, TILE)
            return dot_nn(left[2][...], glog_v[:, pl.ds(start, TILE)]) + dot_nn(left[3][...], chosen(start))

        def target(j):
            lanes = at(j, TILE)
            return keep(piece, whole, lanes) if mine else give(piece, whole, lanes, base + j, j)

        def step(j):
            before, write, after = target(j)
            before()
            write(both(j))
            after()

        if not mine:
            ring_count[0] += 5
        if skip == 0:
            each(5, step)
            return
        each(1, step)
        before, write, after = target(1)
        before()
        norm_part = jnp.where(half == 1, norm_t[...], 0.0).T
        write(both(1) + jnp.concatenate((norm_part, jnp.zeros((LEFT, TILE - 128), F32)), 1))
        after()
        for j in range(2, 5):
            before, write, after = target(j)
            before()

            @pl.when(half == 0)
            def _():
                write(both(j))

            @pl.when(half == 1)
            def _():
                if j == 2:
                    write(jnp.zeros((LEFT, TILE), F32))
                else:
                    write(dot_nn(left[3][...], chosen(half_of(piece) + (skip + j) * TILE)))

            after()

    def products(piece, mine):
        loaded(piece)
        if piece in (1, 2):
            wide_product(piece, mine)
        elif piece == 4:
            if not mine:
                for group in range(4):
                    source = left[5 + group % 2]
                    if group >= 2:
                        loads[piece][1 + group % 2].wait()
                    plain(piece, False, source, gffn_v, group)
                    plain(piece, True, source, gffn_v, group)
                    if group < 2:
                        again = pltpu.make_async_copy(act_part(group + 2), source, load_sem.at[12 + group])
                        again.start()
                        loads[piece][1 + group] = again
        else:
            source, right = {0: (left[1], gqkv_v), 3: (left[0], gh_v), 5: (left[4], gattn_v)}[piece]
            plain(piece, mine, source, right, 0)

    def combine(piece, target, parts):
        def some(rows, lanes):
            total = parts[0][rows, lanes].astype(F32)
            for member in parts[1:]:
                total = total + member[rows, lanes].astype(F32)
            target[rows, lanes] = total.astype(target.dtype)

        wide = PIECES[piece][2]
        if piece == 4:
            each(4, lambda group: some(at(group, 48), slice(0, wide)))
            return
        if wide >= 512:
            each(wide // 512, lambda j: some(slice(0, 48), at(j, 512)))
        if wide % 512:
            some(slice(0, 48), slice(wide // 512 * 512, wide))

    def hop(piece, k, land, index, sems, way):
        return pltpu.make_async_remote_copy(
            src_ref=slot(own, piece, k),
            dst_ref=slot(land, piece, index),
            send_sem=sems[0].at[piece, index],
            recv_sem=sems[1].at[piece, index],
            device_id=peers[way],
            device_id_type=MESH,
        )

    FIRST, SECOND = (first_send, first_recv), (second_send, second_recv)

    def landed(piece, land, index, sems):
        hop(piece, me, land, index, sems, XWAY).wait_recv()

    def block(piece, a, b, far):
        return chip(far, a, b) if piece in Y_FIRST else chip(far, b, a)

    def split(piece):
        return (y, x, YWAY, XWAY) if piece in Y_FIRST else (x, y, XWAY, YWAY)

    readied = set()

    def ready(piece):
        if piece in readied:
            return
        readied.add(piece)
        wide, groups = PIECES[piece][2], SHAPES[PIECES[piece][0]][0] // 24
        for group in range(groups):
            for j in range(wide // TILE):
                ring_copy(piece, pl.ds(LEFT * group, LEFT), at(j, TILE), 0, group * (wide // TILE) + j).wait_recv()
            if wide % TILE:
                index = groups * (wide // TILE) + group
                tail_copy(piece, pl.ds(LEFT * group, LEFT), pl.ds(wide - 128, 128), 0, index).wait_recv()

    def both_cores(piece, k):
        return (slot(own, piece, k), slot(side, piece, k))

    def first_block(piece, i):
        a, b, way, _ = split(piece)
        t, v = (z + i // 2) % 4, (1 - b) if i % 2 == 0 else b
        return block(piece, 1 - a, v, t), 2 * t + v, way

    def first_send_of(piece, i):
        ready(piece)
        k, index, way = first_block(piece, i)
        combine(piece, slot(own, piece, k), both_cores(piece, k))
        hop(piece, k, first, index, FIRST, way).start()

    def second_block(piece, i):
        a, b, _, way = split(piece)
        t = (z + i) % 4
        return block(piece, a, 1 - b, t), t, way

    def second_send_of(piece, i):
        k, t, way = second_block(piece, i)
        spot = 2 * t + 1 - split(piece)[1]
        landed(piece, first, spot, FIRST)
        combine(piece, slot(own, piece, k), both_cores(piece, k) + (slot(first, piece, spot),))
        hop(piece, k, second, t, SECOND, way).start()

    def z_copy(piece, i):
        t = (z + i) % 4
        return pltpu.make_async_remote_copy(
            src_ref=slot(own, piece, chip(t, y, x)),
            dst_ref=slot(column, piece, z),
            send_sem=z_send.at[piece, t],
            recv_sem=z_recv.at[piece, z],
            device_id=device(t, y, x, c),
            device_id_type=MESH,
        )

    def z_landed(piece, i):
        t = (z + i) % 4
        pltpu.make_async_remote_copy(
            src_ref=slot(own, piece, me),
            dst_ref=slot(column, piece, t),
            send_sem=z_send.at[piece, t],
            recv_sem=z_recv.at[piece, t],
            device_id=device(t, y, x, c),
            device_id_type=MESH,
        ).wait_recv()
        return slot(column, piece, t)

    def gathered(piece, t):
        spot = 2 * t + split(piece)[1]
        landed(piece, first, spot, FIRST)
        landed(piece, second, t, SECOND)
        return both_cores(piece, chip(t, y, x)) + (slot(first, piece, spot), slot(second, piece, t))

    def z_send_of(piece, i):
        t = (z + i) % 4
        combine(piece, slot(own, piece, chip(t, y, x)), gathered(piece, t))
        z_copy(piece, i).start()

    swaps = []

    def finish(piece):
        parts = gathered(piece, z)
        parts = parts + tuple(z_landed(piece, i) for i in (1, 2, 3))
        combine(piece, fin[piece], parts)
        m, skip, wide = PIECES[piece]
        size = SHAPES[m][0]
        lanes = pl.ds(pl.multiple_of(c * half_of(piece) + skip, 128), wide)
        swaps.append(
            pltpu.make_async_remote_copy(
                src_ref=fin[piece].at[pl.ds(pl.multiple_of((1 - c) * size, 8), size), :],
                dst_ref=outs[m].at[:, lanes],
                send_sem=swap_send.at[piece],
                recv_sem=swap_recv.at[piece],
                device_id=peers[SIDE],
                device_id_type=MESH,
            )
        )
        swaps[-1].start()
        outs[m][:, lanes] = fin[piece][pl.ds(pl.multiple_of(c * size, 8), size), :]

    for task in TASKS:
        piece, number = task // 32, task % 32
        if number < 2:
            products(piece, number == 1)
        elif number < 10:
            first_send_of(piece, number - 2)
        elif number < 14:
            second_send_of(piece, number - 10)
        elif number < 17:
            z_send_of(piece, number - 13)
        else:
            finish(piece)
    for piece in range(6):
        for i in range(8):
            k, index, way = first_block(piece, i)
            hop(piece, k, first, index, FIRST, way).wait_send()
        for i in range(4):
            k, t, way = second_block(piece, i)
            hop(piece, k, second, t, SECOND, way).wait_send()
        for i in (1, 2, 3):
            z_copy(piece, i).wait_send()
    for number in range(ring_count[0] - 3, ring_count[0]):
        ring_copy(1, whole, pl.ds(0, TILE), number, 0).wait_send()
    for number in range(tail_count[0]):
        tail_copy(1, whole, pl.ds(0, 128), number, 0).wait_send()
    for swap in swaps:
        swap.wait()

    sides, lanes, _, gs = statistics(outs, lane_olds, side_olds)
    scalars = lanes_of([jnp.sum(member, 0, keepdims=True) for member in sides] + [loss[...]])
    sums = jnp.concatenate(lanes + [scalars, squares[...]], 1)
    sums = sum_everywhere(sums, *spread, sems)
    sums_out[...] = sums
    updates = updates_of(sums, gs, sides, lane_olds, moment)[0]
    totals = lanes_of(
        [total_sum(update * update) for update in updates[:6]]
        + [jnp.sum(updates[6][i : i + 1] * updates[6][i : i + 1], 1, keepdims=True) for i in range(6)]
    )
    totals_out[...] = sum_everywhere(totals, *spread_small, small_sems)


def statistics(grads, lane_olds, side_olds):
    wide_g = grads[E_][...]
    gs = (wide_g[:, :VOCAB], wide_g[:, PLACE_AT:]) + tuple(grads[m][...] for m in (Q_, O_, I_, D_))
    gs = gs + (wide_g[:, 4096:4224],)
    decay = 1.0 - STEP ** (-0.8)
    sides, lanes = [], []
    wide_square = wide_g * wide_g + SQUARE_FLOOR
    squares = [wide_square[:, :VOCAB], wide_square[:, PLACE_AT:]] + [g * g + SQUARE_FLOOR for g in gs[2:6]]
    for index in range(6):
        mean = jnp.sum(squares[index], 1, keepdims=True) / squares[index].shape[1]
        sides.append(decay * column_of(as_row(side_olds[index])) + (1.0 - decay) * mean)
    lanes = [jnp.sum(square, 0, keepdims=True) for square in [wide_square] + squares[2:]]
    return sides, lanes, squares, gs


def updates_of(sums, gs, sides, lane_olds, moment):
    decay = 1.0 - STEP ** (-0.8)
    fresh = 1.0 - decay
    parts = [sums[:, :VOCAB], sums[:, PLACE_AT:WIDE]]
    parts += [sums[:, SUM_AT[i] : SUM_AT[i + 1]] for i in range(1, 5)]
    scalars = sums[:, SUM_AT[5] : SUM_AT[5] + 128]
    updates, lane_news = [], []
    for index in range(6):
        height = gs[index].shape[0] * 32
        lane_news.append(decay * as_row(lane_olds[index]) + fresh * (parts[index] / height))
        if index < 2:
            mean = jnp.sum(lane_news[index], 1, keepdims=True) / lane_news[index].shape[1]
        else:
            mean = lane_at(scalars, index) / height
        updates.append(gs[index] * lax.rsqrt(sides[index] * lane_news[index] / mean))
    norm_g = jnp.concatenate([row_of(lane_at(gs[6], NORM_AT - 4096 + i)) for i in range(6)], 0)
    moment_new = decay * moment[...] + fresh * (norm_g * norm_g + SQUARE_FLOOR)
    updates.append(norm_g * lax.rsqrt(moment_new))
    return updates, lane_news, norm_g, moment_new


def reduce_grads(large, small):
    tokens = 5 * SPAN
    vmem, hbm = pl.BlockSpec(memory_space=pltpu.VMEM), pl.BlockSpec(memory_space=pl.ANY)
    dma = pltpu.SemaphoreType.DMA
    scratch = []
    for count in (16, 16, 8, 4, 4):
        scratch += [pltpu.VMEM((count * 2 * SHAPES[m][0], wide), BF16) for m, _, wide in PIECES]
    scratch += [pltpu.VMEM((2 * SHAPES[m][0], wide), F32) for m, _, wide in PIECES]
    scratch += [pltpu.VMEM((LEFT, tokens), BF16)] * 7
    scratch += [pltpu.VMEM((tokens, width), BF16) for width in (TABLE_END, 3 * D, D, 4 * D, D)]
    scratch += [pltpu.VMEM((3, LEFT, TILE), BF16), pltpu.VMEM((6, LEFT, 128), BF16), pltpu.VMEM((128, D), F32)]
    scratch += [pltpu.VMEM((count, 1, SUMS), F32) for count in (2, 4, 4)]
    scratch += [pltpu.VMEM((count, 1, 128), F32) for count in (2, 4, 4)]
    scratch += [dma((14,)), dma((3,)), dma((6,)), dma((6, 10)), dma((6, 8)), dma((6, 8)), dma((6, 4)), dma((6, 4))]
    scratch += [dma((6, 4)), dma((6, 4)), dma((6,)), dma((6,))]
    scratch += ([dma] * 2 + [dma((3,))] * 4) * 2
    return pl.pallas_call(
        reduce_kernel,
        out_shape=[jax.ShapeDtypeStruct(shape, F32) for shape in SHAPES + ((1, SUMS), (1, 128))],
        in_specs=[hbm] * 11 + [vmem] * len(small),
        out_specs=[vmem] * 7,
        scratch_shapes=scratch,
        compiler_params=pltpu.CompilerParams(
            collective_id=1, has_side_effects=True, vmem_limit_bytes=63 * 1024 * 1024
        ),
    )(*large, *small)


def update_kernel(*refs):
    copies = [pltpu.make_async_copy(refs[i], refs[55 + i], refs[82].at[i]) for i in range(27)]
    for copy in copies:
        copy.start()
    for copy in copies:
        copy.wait()
    refs = refs[55:82] + refs[27:55]
    grads, sums, totals, ws, norms = refs[0:5], refs[5], refs[6], refs[7:13], refs[13]
    lane_olds, side_olds, moment = refs[14:20], refs[20:26], refs[26]
    loss_out, table_g, place_g, norm_g_out = refs[27:31]
    lane_outs, side_outs, moment_out, news, norm_new = refs[31:37], refs[37:43], refs[43], refs[44:50], refs[50]
    grad_outs = refs[51:55]
    sides, _, _, gs = statistics(grads, lane_olds, side_olds)
    updates, lane_news, norm_g, moment_new = updates_of(sums[...], gs, sides, lane_olds, moment)
    scalars = sums[:, SUM_AT[5] : SUM_AT[5] + 128]
    squares = sums[:, SUM_AT[5] + 128 :]
    loss_out[...] = lane_at(scalars, 6)
    table_g[...] = gs[0]
    place_g[...] = gs[1]
    norm_g_out[...] = norm_g
    moment_out[...] = moment_new
    for index in range(6):
        lane_outs[index][...] = lane_news[index].reshape(lane_outs[index].shape)
        side_outs[index][...] = row_of(sides[index]).reshape(side_outs[index].shape)
        if index >= 2:
            grad_outs[index - 2][...] = gs[index]
        entries = gs[index].shape[0] * gs[index].shape[1] * 32
        clip = jnp.maximum(1.0, jnp.sqrt(lane_at(totals[...], index) / entries))
        scale = learn_rate * jnp.sqrt(lane_at(squares, index) / entries) / clip
        news[index][...] = ws[index][...] - scale * updates[index]
    for i in range(6):
        clip = jnp.maximum(1.0, jnp.sqrt(lane_at(totals[...], 6 + i) / D))
        scale = learn_rate * jnp.sqrt(lane_at(squares, 6 + i) / D) / clip
        norm_new[i : i + 1, :] = norms[i : i + 1, :] - scale * updates[6][i : i + 1, :]


def update_weights(operands):
    lanes = (VOCAB, 512, 3 * D, D, 4 * D, D)
    held = (24, 24, 24, 24, 24, 96)
    shapes = [(1, 1), (24, VOCAB), (24, 512), (6, 24)]
    shapes += [(lane,) for lane in lanes] + [(size,) for size in held] + [(6, 24)]
    shapes += list(zip(held, lanes)) + [(6, 24)] + list(zip(held, lanes))[2:]
    return pl.pallas_call(
        update_kernel,
        out_shape=[jax.ShapeDtypeStruct(shape, F32) for shape in shapes],
        in_specs=[pl.BlockSpec(memory_space=pl.ANY)] * len(operands),
        out_specs=[pl.BlockSpec(memory_space=pltpu.VMEM)] * len(shapes),
        scratch_shapes=[pltpu.VMEM(member.shape, member.dtype) for member in operands]
        + [pltpu.SemaphoreType.DMA((len(operands),))],
        compiler_params=pltpu.CompilerParams(vmem_limit_bytes=63 * 1024 * 1024),
    )(*operands)


def norm_forward(value, gain, shift):
    centred = value - jnp.mean(value, -1, keepdims=True)
    inverse = lax.rsqrt(jnp.mean(centred * centred, -1, keepdims=True) + EPSILON)
    normed = centred * inverse
    return (normed * gain + shift, normed, inverse)


def norm_backward(grad_out, normed, inverse, gain):
    scaled = grad_out * gain
    back = inverse * (
        scaled
        - jnp.mean(scaled, -1, keepdims=True)
        - normed * jnp.mean(scaled * normed, -1, keepdims=True)
    )
    return (back, jnp.sum(grad_out * normed, 0), jnp.sum(grad_out, 0))


def mm(left, right, sides):
    return lax.dot_general(left, right, ((sides[:1], sides[1:]), ((), ())), preferred_element_type=F32)


def attend(qkv, allowed):
    by_head = qkv.reshape(qkv.shape[0], 3, HEADS, HEAD_DIM)
    query, key, value = by_head[:, 0], by_head[:, 1], by_head[:, 2]
    scores = jnp.einsum("qhe,khe->hqk", query, key, preferred_element_type=F32) * 0.125
    scores = jnp.where(allowed[None], scores, -1e30)
    highest = jnp.max(scores, -1, keepdims=True)
    raised = jnp.exp(scores - highest)
    summed = jnp.sum(raised, -1, keepdims=True)
    shares = (raised / summed).astype(BF16)
    mixture = jnp.einsum("hqk,khe->qhe", shares, value, preferred_element_type=F32)
    return mixture.astype(BF16).reshape(qkv.shape[0], D), highest + jnp.log(summed)


def attend_back(qkv, allowed, log_total, grad_mix):
    by_head = qkv.reshape(qkv.shape[0], 3, HEADS, HEAD_DIM)
    query, key, value = by_head[:, 0], by_head[:, 1], by_head[:, 2]
    grad_mix = grad_mix.reshape(qkv.shape[0], HEADS, HEAD_DIM)
    scores = jnp.einsum("qhe,khe->hqk", query, key, preferred_element_type=F32) * 0.125
    scores = jnp.where(allowed[None], scores, -1e30)
    shares = jnp.exp(scores - log_total)
    grad_share = jnp.einsum("qhe,khe->hqk", grad_mix, value, preferred_element_type=F32)
    grad_score = (shares * (grad_share - jnp.sum(shares * grad_share, -1, keepdims=True))).astype(BF16)
    grad_query = jnp.einsum("hqk,khe->qhe", grad_score, key, preferred_element_type=F32) * 0.125
    grad_key = jnp.einsum("hqk,qhe->khe", grad_score, query, preferred_element_type=F32) * 0.125
    grad_value = jnp.einsum("hqk,qhe->khe", shares.astype(BF16), grad_mix, preferred_element_type=F32)
    return jnp.stack((grad_query, grad_key, grad_value), 1).astype(BF16).reshape(qkv.shape)


def on_slice(token_arrays, lengths, weights, lane_olds, side_olds, moment):
    olds = lane_olds + side_olds + (moment,)
    found = front(token_arrays + weights, lengths)
    mask_count, gains, side, cols, keys, weight_sq = found[0:6]
    x_t, mix, a, act, y, slope, qkv_b, normed_a = found[6:14]
    normed_bc, (qkv_w, out_w, in_w, down_w, wide_w) = found[14:18], found[18:23]
    found = middle(
        (wide_w, qkv_w, out_w, in_w, down_w, y, act, a, mix, slope, qkv_b, normed_a) + tuple(normed_bc),
        (cols, keys, side, gains, mask_count),
    )
    loss_part, norm_sums = found[0:2]
    grad_logit, y_t, a_t, mix_t, act_t, ge_t, grad_ffn, grad_hidden, grad_attn, grad_qkv = found[2:]
    reduced = reduce_grads(
        (y_t, ge_t, grad_logit, x_t, grad_qkv, mix_t, grad_attn, a_t, grad_hidden, act_t, grad_ffn),
        (cols, norm_sums, loss_part, weight_sq) + olds,
    )
    found = update_weights(tuple(reduced) + weights + olds)
    grads = (None,) + tuple(found[24:28])
    mask_count = mask_count.reshape(())
    loss_sum, table_g, place_g, norm_g = found[0:4]
    lane_news = found[4:10]
    side_news = found[10:16]
    moment_new, norm_new = found[16], found[23]
    news = found[17:23]
    return (
        loss_sum.reshape(()),
        mask_count,
        table_g.T,
        place_g.T,
        grads[1],
        grads[2],
        grads[3],
        grads[4],
        norm_g.T,
        lane_news[0],
        side_news[0],
        lane_news[1],
        side_news[1],
        side_news[2],
        lane_news[2],
        side_news[3],
        lane_news[3],
        side_news[4],
        lane_news[4],
        side_news[5],
        lane_news[5],
        moment_new.T,
        news[0].T,
        news[1].T,
        news[2],
        news[3],
        news[4],
        news[5],
        norm_new.T,
    )


def on_device(
    whole_mesh,
    long_ids,
    long_targets,
    long_mask,
    long_lengths,
    short_ids,
    short_targets,
    short_mask,
    short_lengths,
    table,
    position,
    qkv_weight,
    out_weight,
    in_weight,
    down_weight,
    norms,
    table_rows,
    table_cols,
    position_rows,
    position_cols,
    qkv_rows,
    qkv_cols,
    out_rows,
    out_cols,
    in_rows,
    in_cols,
    down_rows,
    down_cols,
    norm_moment,
):
    if whole_mesh == (8, 4):
        return on_slice(
            (long_ids, long_targets, long_mask, short_ids, short_targets, short_mask),
            (long_lengths, short_lengths),
            (table.T, position.T, qkv_weight, out_weight, in_weight, down_weight, norms.T),
            (table_rows, position_rows, qkv_cols, out_cols, in_cols, down_cols),
            (table_cols, position_cols, qkv_rows, out_rows, in_rows, down_rows),
            norm_moment.T,
        )
    devices = lax.axis_size(("dp", "seq"))
    seq_index = lax.axis_index("seq")
    held = norms.shape[0]

    span = long_ids.shape[1]
    long_place = seq_index * span + lax.iota(jnp.int32, span)
    long_keep = (long_place[None, :] < long_lengths[:, None]).astype(jnp.int32)
    short_keep = (lax.iota(jnp.int32, SPAN)[None, :] < short_lengths[:, None]).astype(jnp.int32)
    long_pack = jnp.stack((long_ids, long_targets, long_mask * long_keep, long_keep), 1)
    short_pack = jnp.stack((short_ids, short_targets, short_mask * short_keep, short_keep), 1)
    moved = lax.all_to_all(
        jnp.concatenate((long_pack, short_pack[1:]), 0), "seq", split_axis=0, concat_axis=0, tiled=True
    )
    tokens = jnp.concatenate((moved, short_pack[:1]), 0)
    ids, targets, weight, keep = (tokens[:, i].reshape(-1) for i in range(4))
    weight = weight.astype(F32)
    count = tokens.shape[0] * span
    last = count - span
    alone = seq_index == lax.axis_size("seq") - 1
    token = lax.iota(jnp.int32, count)
    place = jnp.where(alone | (token >= last), token % span, token)
    row = jnp.where(alone | (token >= last), token // span, 0)
    allowed_long = (row[:last, None] == row[None, :last]) & (keep[None, :last] > 0)
    allowed_short = jnp.broadcast_to(keep[None, last:] > 0, (span, span))

    here_count = jnp.sum(long_pack[:, 2]) + jnp.sum(short_pack[:, 2])
    tall = table.T
    counts = jnp.broadcast_to(jnp.stack((here_count // 256, here_count % 256)).astype(F32)[None], (held, 2))
    wide_shard = jnp.concatenate(
        (tall, norms, counts, jnp.zeros((held, PLACE_AT - COUNT_AT - 2), F32), position.T), 1
    )
    shards = (wide_shard, qkv_weight, out_weight, in_weight, down_weight)
    wide_w, qkv_w, out_w, in_w, down_w = (
        lax.all_gather(shard.astype(BF16), ("dp", "seq"), axis=0, tiled=True) for shard in shards
    )
    column = lax.broadcasted_iota(jnp.int32, (1, WIDE), 1)
    chosen = ((ids[:, None] == column) | ((place[:, None] + PLACE_AT) == column)).astype(BF16)
    gains = wide_w[:, NORM_AT : NORM_AT + 6].astype(F32)
    sums = jnp.sum(wide_w[:, COUNT_AT : COUNT_AT + 2].astype(F32), 0)
    mask_count = (sums[0] * 256.0 + sums[1]) / held
    inverse_count = 1.0 / mask_count

    embedded = mm(chosen, wide_w, (1, 1))
    first, normed_a, inverse_a = norm_forward(embedded, gains[:, 0], gains[:, 1])
    first_b = first.astype(BF16)
    qkv_b = mm(first_b, qkv_w, (1, 0)).astype(BF16)
    mix_long, total_long = attend(qkv_b[:last], allowed_long)
    mix_short, total_short = attend(qkv_b[last:], allowed_short)
    mixture = jnp.concatenate((mix_long, mix_short), 0)
    second, normed_b, inverse_b = norm_forward(first + mm(mixture, out_w, (1, 0)), gains[:, 2], gains[:, 3])
    second_b = second.astype(BF16)
    hidden = mm(second_b, in_w, (1, 0))
    active, slope = gelu_pair(hidden)
    active_b = active.astype(BF16)
    third, normed_c, inverse_c = norm_forward(second + mm(active_b, down_w, (1, 0)), gains[:, 4], gains[:, 5])
    third_b = third.astype(BF16)
    logits = jnp.where(column < VOCAB, mm(third_b, wide_w, (1, 0)), -1e30)
    highest = jnp.max(logits, -1, keepdims=True)
    log_sum = highest + jnp.log(jnp.sum(jnp.exp(logits - highest), -1, keepdims=True))
    onehot = targets[:, None] == column
    picked = jnp.sum(jnp.where(onehot, logits, 0.0), -1)
    loss_part = jnp.sum(weight * (log_sum[:, 0] - picked))
    grad_logit = (
        (jnp.exp(logits - log_sum) - onehot.astype(F32)) * (weight * inverse_count)[:, None]
    ).astype(BF16)
    grad_third = mm(grad_logit, wide_w, (1, 1))
    grad_second, gain_c, shift_c = norm_backward(grad_third, normed_c, inverse_c, gains[:, 4])
    grad_ffn = grad_second.astype(BF16)
    down_grad = mm(active_b, grad_ffn, (0, 0)).astype(BF16)
    grad_hidden = (mm(grad_ffn, down_w, (1, 1)) * slope).astype(BF16)
    in_grad = mm(second_b, grad_hidden, (0, 0)).astype(BF16)
    grad_second = grad_second + mm(grad_hidden, in_w, (1, 1))
    grad_first, gain_b, shift_b = norm_backward(grad_second, normed_b, inverse_b, gains[:, 2])
    grad_attn = grad_first.astype(BF16)
    out_grad = mm(mixture, grad_attn, (0, 0)).astype(BF16)
    grad_mix = mm(grad_attn, out_w, (1, 1)).astype(BF16)
    grad_qkv = jnp.concatenate(
        (
            attend_back(qkv_b[:last], allowed_long, total_long, grad_mix[:last]),
            attend_back(qkv_b[last:], allowed_short, total_short, grad_mix[last:]),
        ),
        0,
    )
    qkv_grad = mm(first_b, grad_qkv, (0, 0)).astype(BF16)
    grad_first = grad_first + mm(grad_qkv, qkv_w, (1, 1))
    grad_embed, gain_a, shift_a = norm_backward(grad_first, normed_a, inverse_a, gains[:, 0])
    wide_grad = mm(
        jnp.concatenate((third_b, grad_embed.astype(BF16)), 0),
        jnp.concatenate((grad_logit, chosen), 0),
        (0, 0),
    )
    norm_part = jnp.stack((gain_a, shift_a, gain_b, shift_b, gain_c, shift_c), 1)
    wide_grad = lax.dynamic_update_slice(wide_grad.astype(BF16), norm_part.astype(BF16), (0, NORM_AT))
    grads = (wide_grad, qkv_grad, out_grad, in_grad, down_grad)
    wide_g, qkv_g, out_g, in_g, down_g = (
        lax.psum_scatter(grad.astype(F32), ("dp", "seq"), scatter_dimension=0, tiled=True) for grad in grads
    )
    table_g, place_g = wide_g[:, :VOCAB], wide_g[:, PLACE_AT:]
    norm_g = wide_g[:, NORM_AT : NORM_AT + 6]

    decay = 1.0 - STEP ** (-0.8)
    matrices = (
        (qkv_weight, qkv_g, qkv_rows, qkv_cols),
        (out_weight, out_g, out_rows, out_cols),
        (in_weight, in_g, in_rows, in_cols),
        (down_weight, down_g, down_rows, down_cols),
    )
    wide = (
        (tall, table_g, table_cols, table_rows),
        (position.T, place_g, position_cols, position_rows),
    )
    row_news = [
        decay * member[2] + (1.0 - decay) * jnp.mean(member[1] * member[1] + SQUARE_FLOOR, 1)
        for member in matrices + wide
    ]
    col_parts = [jnp.sum(member[1] * member[1] + SQUARE_FLOOR, 0) for member in matrices + wide]
    row_totals = jnp.stack([jnp.sum(rows_new) for rows_new in row_news])
    weight_sq = jnp.stack([jnp.sum(member[0] * member[0]) for member in matrices + wide])
    stats = lax.psum(
        col_parts + [row_totals, weight_sq, jnp.sum(norms * norms, 0), loss_part.reshape(1)], ("dp", "seq")
    )
    updates = []
    cols_out = []
    for index, member in enumerate(matrices + wide):
        full_rows = member[0].shape[0] * devices
        cols_new = decay * member[3] + (1.0 - decay) * stats[index] / full_rows
        if index < 4:
            mean = stats[6][index] / full_rows
        else:
            mean = jnp.mean(cols_new)
        updates.append(member[1] * lax.rsqrt(row_news[index][:, None] * cols_new[None, :] / mean))
        cols_out.append(cols_new)
    moment_new = decay * norm_moment + (1.0 - decay) * (norm_g * norm_g + SQUARE_FLOOR)
    norm_update = norm_g * lax.rsqrt(moment_new)
    update_sq = jnp.stack([jnp.sum(update * update) for update in updates])
    totals = lax.psum((update_sq, jnp.sum(norm_update * norm_update, 0)), ("dp", "seq"))
    news = []
    for index, member in enumerate(matrices + wide):
        entries = member[0].shape[0] * member[0].shape[1] * devices
        clip = jnp.maximum(1.0, jnp.sqrt(totals[0][index] / entries))
        news.append(
            member[0] - learn_rate * jnp.sqrt(stats[7][index] / entries) * updates[index] / clip
        )
    norm_rows = norms.shape[0] * devices
    norm_clip = jnp.maximum(1.0, jnp.sqrt(totals[1] / norm_rows))
    norm_new = norms - learn_rate * jnp.sqrt(stats[8] / norm_rows) * norm_update / norm_clip
    return (
        stats[9][0],
        mask_count,
        table_g.T,
        place_g.T,
        qkv_g,
        out_g,
        in_g,
        down_g,
        norm_g,
        cols_out[4],
        row_news[4],
        cols_out[5],
        row_news[5],
        row_news[0],
        cols_out[0],
        row_news[1],
        cols_out[1],
        row_news[2],
        cols_out[2],
        row_news[3],
        cols_out[3],
        moment_new,
        news[4].T,
        news[5].T,
        news[0],
        news[1],
        news[2],
        news[3],
        norm_new,
    )


def solution(mesh):
    split, wide = P(("dp", "seq"), None), P(None, ("dp", "seq"))
    shard, same = P(("dp", "seq")), P()
    return jax.shard_map(
        functools.partial(on_device, (mesh.shape["dp"], mesh.shape["seq"])),
        mesh=mesh,
        in_specs=(P("dp", "seq"),) * 3
        + (P("dp"),)
        + (split,) * 3
        + (shard,)
        + (wide,) * 2
        + (split,) * 5
        + (same, shard) * 2
        + (shard, same) * 4
        + (split,),
        out_specs=(same, same)
        + (wide,) * 2
        + (split,) * 5
        + (same, shard) * 2
        + (shard, same) * 4
        + (split,)
        + (wide,) * 2
        + (split,) * 5,
        check_vma=False,
    )
```

```python
import functools

import jax
import jax.numpy as jnp
from jax import lax
from jax.experimental import pallas as pl
from jax.experimental.pallas import tpu as pltpu
from jax.sharding import PartitionSpec as P

D = 768
HEADS = 12
HEAD_DIM = 64
VOCAB = 4101
STEP = 10
SPAN = 128

EPSILON = 1e-12
SQUARE_FLOOR = 1e-30
learn_rate = 0.3

MESH = pl.DeviceIdType.MESH
F32 = jnp.float32
BF16 = jnp.bfloat16

NORM_AT = VOCAB
COUNT_AT = VOCAB + 6
TABLE_END = 4352
PLACE_AT = 4608
WIDE = PLACE_AT + 512

SHAPES = ((24, WIDE), (24, 3 * D), (24, D), (24, 4 * D), (96, D))
E_, Q_, O_, I_, D_ = range(5)
CLASS_A, CLASS_B, CLASS_C = (E_, O_), (Q_, D_), (I_,)
UP, DOWN, XWAY, YWAY, SIDE = range(5)


def here():
    dp, seq = lax.axis_index("dp"), lax.axis_index("seq")
    return dp // 2, dp % 2, seq // 2, seq % 2


def device(z, y, x, c):
    return {"dp": z * 2 + y, "seq": x * 2 + c}


def chip(z, y, x):
    return z * 4 + y * 2 + x


def all_peers():
    z, y, x, c = here()
    return (
        device(z + 1, y, x, c),
        device(z - 1, y, x, c),
        device(z, y, 1 - x, c),
        device(z, 1 - y, x, c),
        device(z, y, x, 1 - c),
    )


SUM_AT = (0, WIDE, WIDE + 3 * D, WIDE + 4 * D, WIDE + 8 * D, WIDE + 9 * D)
SUMS = WIDE + 9 * D + 256
HALF_AT = tuple(start // 2 for start in SUM_AT)
HALF_SUMS = HALF_AT[5]


def lanes_of(members):
    lane = lax.broadcasted_iota(jnp.int32, (1, 128), 1)
    row = jnp.zeros((1, 128), F32)
    for index, member in enumerate(members):
        row = jnp.where(lane == index, member, row)
    return row


def lane_at(row, index):
    lane = lax.broadcasted_iota(jnp.int32, row.shape, 1)
    return jnp.sum(jnp.where(lane == index, row, 0.0), 1, keepdims=True)


def column_of(row):
    size = row.shape[1]
    diagonal = lax.broadcasted_iota(jnp.int32, (size, size), 0) == lax.broadcasted_iota(
        jnp.int32, (size, size), 1
    )
    return jnp.sum(jnp.where(diagonal, row, 0.0), 1, keepdims=True)


def row_of(column):
    size = column.shape[0]
    diagonal = lax.broadcasted_iota(jnp.int32, (size, size), 0) == lax.broadcasted_iota(
        jnp.int32, (size, size), 1
    )
    return jnp.sum(jnp.where(diagonal, column, 0.0), 0, keepdims=True)


def as_row(ref):
    return ref[...].reshape(1, ref.shape[0])


def total_sum(array):
    return jnp.sum(jnp.sum(array, 1, keepdims=True), 0, keepdims=True)


def gelu_pair(hidden):
    normal_cdf = 0.5 * (1.0 + lax.erf(hidden * 0.7071067811865476))
    return (
        hidden * normal_cdf,
        normal_cdf + hidden * jnp.exp(-0.5 * hidden * hidden) * 0.3989422804014327,
    )


def dot_nn(left, right):
    return jnp.dot(left, right, preferred_element_type=F32)


def dot_nt(left, right):
    return lax.dot_general(left, right, (((1,), (1,)), ((), ())), preferred_element_type=F32)


def dot_tn(left, right):
    return lax.dot_general(left, right, (((0,), (0,)), ((), ())), preferred_element_type=F32)


def at(index, size):
    if isinstance(index, int):
        return pl.ds(index * size, size)
    return pl.ds(pl.multiple_of(index * size, size), size)


def each(count, body):
    def step(index, carry):
        body(index)
        return carry

    lax.fori_loop(0, count, step, 0)


def each_unrolled(count, body):
    for index in range(count):
        body(index)


ROWS = 128
TILE = 256
HALF = 320
TABLE_TILES = TABLE_END // TILE


def head_lanes(first):
    lane = lax.broadcasted_iota(jnp.int32, (1, 128), 1)
    return (lane < HEAD_DIM) if first else (lane >= HEAD_DIM)


def layer_norm(value, gain, shift):
    centred = value - jnp.sum(value, 1, keepdims=True) / D
    inverse = lax.rsqrt(jnp.sum(centred * centred, 1, keepdims=True) / D + EPSILON)
    normed = centred * inverse
    return normed * gain + shift, normed, inverse


def layer_norm_back(grad, normed, inverse, gain):
    scaled = grad * gain
    return inverse * (
        scaled - jnp.sum(scaled, 1, keepdims=True) / D - normed * (jnp.sum(scaled * normed, 1, keepdims=True) / D)
    )


def put_lane(ref, rows, index, value):
    lane = lax.broadcasted_iota(jnp.int32, (1, 128), 1)
    ref[rows, :] = jnp.where(lane == index, value, ref[rows, :])


def set_bias(bias, cols, keys, last):
    same = cols[0:last, 4:5] == keys[1:2, 0:last]
    bias[...] = jnp.where(same & (keys[0:1, 0:last] > 0), 0.0, -1e30)


CHOOSE, EMBED, NORM_A, PROJECT, TURN_X, ATTEND, OUT, NORM_B, FEED_IN, TURN_A, FEED_OUT, REST = range(12)
FRONT = (
    100, 65, 1000, 4, 33, 3, 64, 1001, 160, 2, 35, 68, 163, 66, 132, 67, 72, 40, 99, 164,
    0, 32, 34, 8, 38, 12, 168, 74, 42, 162, 36, 69, 5, 7, 44, 37, 70, 108, 1, 13,
    173, 39, 167, 161, 165, 172, 71, 98, 41, 73, 75, 14, 11, 43, 50, 82, 76, 171, 47, 18,
    79, 77, 80, 81, 97, 6, 178, 51, 49, 174, 45, 48, 9, 96, 10, 131, 169, 46, 78, 128,
    166, 83, 19, 101, 1016, 1017, 1018, 176, 1019, 102, 16, 1020, 1021, 130, 15, 129, 17, 1032, 140, 133,
    170, 179, 104, 138, 105, 175, 103, 1048, 1049, 1050, 1051, 1052, 1053, 1054, 1055, 1056, 1064, 1080, 1081, 1082,
    136, 1083, 110, 107, 134, 1084, 114, 112, 111, 135, 106, 177, 1085, 109, 115, 139, 146, 1096, 1097, 142,
    1098, 113, 1112, 143, 141, 144, 137, 1128, 1129, 1130, 1131, 1132, 1133, 1134, 1135, 1136, 145, 1137, 147, 1138,
    1139, 1160, 1161, 1162, 1176,
)


def front_hooks():
    hooks, before = {}, []
    for task in FRONT:
        if task < 1000:
            before.append(task)
        else:
            hooks[((task - 1000) // 16, (task - 1000) % 16)] = before
            before = []
    return hooks


def front_kernel(*refs):
    raw, (long_len, short_len) = refs[0:13], refs[13:15]
    count_out, gains_out, side, cols, keys, squares = refs[15:21]
    x_t, mix_out, a_out, act_out, y_out, slope_out, qkv_out, na_out = refs[21:29]
    nb_outs, nc_outs, weight_outs = refs[29:31], refs[31:33], refs[33:38]
    wide, qkv_w, out_w, in_w, down_w = weights = refs[38:43]
    value, na, low_a, low_y, mix, qkv, act, slope, pick, pick_two, bias, turned = refs[43:55]
    nb, nc = refs[55:57], (mix, low_y)
    held, wide_shard, merge, pieces, land = refs[57:70], refs[70], refs[71:76], refs[76], refs[77]
    raw_sem, swap_send, swap_recv, token_send, token_recv, send_sem, link_recv, side_recv = refs[78:86]
    out_sem, turn_sem = refs[86:88]
    z, y, x, c = here()
    peers = all_peers()
    me = chip(z, y, x)
    seq = x * 2 + c
    alone = seq // 3
    tokens = value.shape[0]
    last = tokens - SPAN
    hooks = front_hooks()

    barrier = pltpu.get_barrier_semaphore()
    cross = device(z, y, 1 - x, 1 - c)
    column = [device((z + 1 + i) % 4, y, x, c) for i in range(3)]
    for peer in [peers[XWAY], peers[YWAY], peers[SIDE], cross] + column:
        pl.semaphore_signal(barrier, inc=1, device_id=peer, device_id_type=MESH)
    raws = [pltpu.make_async_copy(raw[i], held[i], raw_sem.at[i]) for i in range(13)]
    for member in raws:
        member.start()
    for member in raws:
        member.wait()
    long_ids, long_targets, long_mask, short_ids, short_targets, short_mask, tall, place, qkv_s, out_s, in_s, down_s, norms = held

    pieces[...] = jnp.zeros(pieces.shape, jnp.int32)
    land[4] = jnp.zeros((8, SPAN), jnp.int32)
    lane = lax.broadcasted_iota(jnp.int32, (1, SPAN), 1)
    count = jnp.zeros((1, SPAN), jnp.int32)
    for t in range(5):
        if t < 3:
            ids, targets, mask = long_ids[t : t + 1, :], long_targets[t : t + 1, :], long_mask[t : t + 1, :]
            keep = (lane + seq * SPAN < long_len[t]).astype(jnp.int32)
        else:
            row = (1, 0)[t - 3]
            ids, targets, mask = (member[row : row + 1, :] for member in (short_ids, short_targets, short_mask))
            keep = (lane < short_len[row]).astype(jnp.int32)
        target = pieces.at[t] if t < 4 else land.at[4]
        target[0:1, :] = ids
        target[2:3, :] = targets
        target[3:4, :] = mask * keep
        target[5:6, :] = keep
        count = count + mask * keep
    count = jnp.sum(count.astype(F32), 1, keepdims=True)
    high = jnp.floor(count * (1.0 / 256.0))

    wide_shard[:, 0:4096] = tall[:, 0:4096]
    edge = jnp.zeros((24, 128), F32)
    tile_lane = lax.broadcasted_iota(jnp.int32, (24, 128), 1)
    tall_edge = tall[:, 4096:VOCAB]
    members = [lane_at(tall_edge, i) for i in range(VOCAB - 4096)]
    members += [column_of(norms[i : i + 1, :]) for i in range(6)]
    members += [high, count - high * 256.0]
    for i, member in enumerate(members):
        edge = jnp.where(tile_lane == i, member, edge)
    wide_shard[:, 4096:4224] = edge
    wide_shard[:, 4224:PLACE_AT] = jnp.zeros((24, PLACE_AT - 4224), F32)
    wide_shard[:, PLACE_AT:] = place[...]
    shards = (wide_shard, qkv_s, out_s, in_s, down_s)

    pl.semaphore_wait(barrier, 7)
    swaps = []
    for m in (E_, Q_, I_, D_, O_):
        size, half = SHAPES[m][0], SHAPES[m][1] // 2
        swaps.append(
            pltpu.make_async_remote_copy(
                src_ref=shards[m].at[:, pl.ds(pl.multiple_of((1 - c) * half, 128), half)],
                dst_ref=merge[m].at[pl.ds(pl.multiple_of(c * size, 8), size), :],
                send_sem=swap_send.at[m],
                recv_sem=swap_recv.at[m],
                device_id=peers[SIDE],
                device_id_type=MESH,
            )
        )
        swaps[-1].start()
    token_copies = []
    for i, (to_x, to_c) in enumerate(((x, 1 - c), (1 - x, c), (1 - x, 1 - c))):
        token_copies.append(
            pltpu.make_async_remote_copy(
                src_ref=pieces.at[to_x * 2 + to_c],
                dst_ref=land.at[seq],
                send_sem=token_send.at[i],
                recv_sem=token_recv.at[i],
                device_id=device(z, y, to_x, to_c),
                device_id_type=MESH,
            )
        )
        token_copies[-1].start()
    land[seq] = pieces[seq]

    def part(piece, k, half):
        m, skip, wide_part = PIECES[piece]
        size = 2 * SHAPES[m][0]
        start = pl.multiple_of(half * (SHAPES[m][1] // 2) + skip, 128)
        return weights[m].at[pl.ds(pl.multiple_of(k * size, size), size), pl.ds(start, wide_part)]

    FIRST_WAY, SECOND_WAY, SIDE_WAY = 0, 1, 2

    def copy_of(piece, k, way):
        ways = (XWAY, YWAY) if GATHER_WAY[piece] % 2 == 0 else (YWAY, XWAY)
        peer = column[way - 3] if way > 2 else peers[SIDE] if way == SIDE_WAY else peers[ways[way]]
        return pltpu.make_async_remote_copy(
            src_ref=part(piece, k, c),
            dst_ref=part(piece, k, c),
            send_sem=send_sem.at[piece, k, way],
            recv_sem=(side_recv if way == SIDE_WAY else link_recv).at[piece, k],
            device_id=peer,
            device_id_type=MESH,
        )

    def block_of(number):
        piece, task = number // 32, number % 32
        way = GATHER_WAY[piece]

        def of(last, earlier, t):
            to_y, to_x = (last, earlier) if way % 2 == 0 else (earlier, last)
            return chip(t, 1 - y if to_y else y, 1 - x if to_x else x)

        if task < 5:
            return piece, me, (3 + task if task < 3 else FIRST_WAY if task == 3 else SECOND_WAY,), False
        if task >= 12:
            return piece, of(1, (task - 12) % 2, (z + (task - 12) // 2) % 4), (SIDE_WAY,), True
        if way < 2:
            if task < 8:
                return piece, of(0, 0, (z + task - 4) % 4), (FIRST_WAY, SECOND_WAY, SIDE_WAY), True
            return piece, of(0, 1, (z + task - 8) % 4), (SECOND_WAY, SIDE_WAY), True
        if task == 5:
            return piece, of(0, 1, z), (3, 4, 5, SECOND_WAY, SIDE_WAY), True
        return piece, of(0, (task - 6) % 2, (z + 1 + (task - 6) // 2) % 4), (SECOND_WAY, SIDE_WAY), True

    def transfer(number):
        piece, k, ways, waits = block_of(number)
        if waits:
            copy_of(piece, k, FIRST_WAY).wait_recv()
        for way in ways:
            copy_of(piece, k, way).start()

    def before(step, index, base=0):
        for (name, part_index), tasks in hooks.items():
            part_index = part_index - base
            if name != step or not tasks or (step == EMBED and not 0 <= part_index < 3):
                continue
            if index is None or isinstance(index, int):
                if part_index == (index or 0):
                    for number in tasks:
                        transfer(number)
            else:

                @pl.when(index == part_index)
                def _(tasks=tasks):
                    for number in tasks:
                        transfer(number)

    def need(*wanted):
        for piece in wanted:
            for k in range(16):
                pltpu.make_async_remote_copy(
                    src_ref=part(piece, k, 1 - c),
                    dst_ref=part(piece, k, 1 - c),
                    send_sem=send_sem.at[piece, k, SIDE_WAY],
                    recv_sem=side_recv.at[piece, k],
                    device_id=peers[SIDE],
                    device_id_type=MESH,
                ).wait_recv()

    for number, m in enumerate((E_, Q_, I_, D_, O_)):
        swaps[number].wait_recv()
        size, half = SHAPES[m][0], SHAPES[m][1] // 2
        merge[m][pl.ds(pl.multiple_of(c * size, 8), size), :] = shards[m][:, pl.ds(pl.multiple_of(c * half, 128), half)]
        rows = pl.ds(pl.multiple_of(me * 2 * size, 2 * size), 2 * size)
        weights[m][rows, pl.ds(pl.multiple_of(c * half, 128), half)] = merge[m][...].astype(BF16)
        for piece in range(6):
            if PIECES[piece][0] == m:
                copy_of(piece, me, SIDE_WAY).start()
    for copy in token_copies:
        copy.wait_recv()
    side[...] = jnp.zeros(side.shape, F32)
    keys[...] = jnp.zeros(keys.shape, jnp.int32)
    zeros = jnp.zeros((1, SPAN), F32)
    for b in range(5):
        tile = land[b]
        shift = b * SPAN * (1 - alone) if b < 4 else 0
        row = b * alone if b < 4 else 4
        spot = (lane + shift + PLACE_AT).astype(F32)
        row_lane = (lane * 0 + row).astype(F32)
        ids, targets, weight = (tile[i : i + 1].astype(F32) for i in (0, 2, 3))
        stacked = jnp.concatenate((ids, spot, targets, weight, row_lane, tile[5:6].astype(F32), zeros, zeros), 0)
        stacked = jnp.concatenate((stacked, jnp.zeros((120, SPAN), F32)), 0)
        cols[b * SPAN : (b + 1) * SPAN, :] = stacked.T.astype(jnp.int32)
        keys[0:1, b * SPAN : (b + 1) * SPAN] = tile[5:6]
        keys[1:2, b * SPAN : (b + 1) * SPAN] = lane * 0 + row
        keys[2:4, b * SPAN : (b + 1) * SPAN] = tile[2:4]
    set_bias(bias, cols, keys, last)
    found = [total_sum(member[...] * member[...]) for member in (tall, place, qkv_s, out_s, in_s, down_s)]
    norm_squares = jnp.sum(norms[...] * norms[...], 1, keepdims=True)
    squares[...] = lanes_of(found + [norm_squares[i : i + 1] for i in range(6)])

    turns, outs, out_count = {}, {}, [0]

    def turn_out(source, target, slot):
        if slot in turns:
            turns[slot].wait()

        def some(index):
            turned[slot, :, at(index, ROWS)] = source[at(index, ROWS), :].T

        each_unrolled(tokens // ROWS, some)
        turns[slot] = pltpu.make_async_copy(turned.at[slot], target, turn_sem.at[slot])
        turns[slot].start()

    def put_out(name, source, target):
        outs[name] = pltpu.make_async_copy(source, target, out_sem.at[out_count[0]])
        out_count[0] += 1
        outs[name].start()

    picks = (pick, pick_two)
    halves = [pl.ds(half * HALF, HALF) for half in range(2)]
    for half in range(2):

        def choose(index):
            column_lane = lax.broadcasted_iota(jnp.int32, (1, TILE), 1) + index * TILE
            hit = (cols[halves[half], 0:1] == column_lane) | (cols[halves[half], 1:2] == column_lane)
            picks[half][:, at(index, TILE)] = jnp.where(hit, 1.0, 0.0).astype(BF16)

        before(CHOOSE, half)
        each_unrolled(WIDE // TILE, choose)

    before(EMBED, 0)
    hooks.pop((EMBED, 0))
    need(1, 2)
    put_out("wide", wide, weight_outs[4])
    for half in range(2):

        def embed(index):
            before(EMBED, index, half * 3)
            value[halves[half], at(index, TILE)] = dot_nt(picks[half][...], wide[at(index, TILE), :])

        each_unrolled(D // TILE, embed)

    gains = wide[:, 4096:4224].astype(F32).T
    gains_out[...] = gains[0:16]
    counts = jnp.sum(gains[11:13], 1, keepdims=True) / 24.0
    mask_count = counts[0:1] * 256.0 + counts[1:2]
    count_out[...] = mask_count
    norm_rows = [gains_out[5 + i : 6 + i, :] for i in range(6)]
    before(NORM_A, None)

    def norm_a(index):
        rows = at(index, ROWS)
        found, normed, inverse = layer_norm(value[rows, :], norm_rows[0], norm_rows[1])
        value[rows, :] = found
        low_a[rows, :] = found.astype(BF16)
        na[rows, :] = normed
        put_lane(side, rows, 12, inverse)

    each_unrolled(tokens // ROWS, norm_a)
    put_out("na", na, na_out)
    before(PROJECT, 0)
    need(0)

    def project(index):
        before(PROJECT, index)
        qkv[:, at(index, TILE)] = dot_nn(low_a[...], qkv_w[:, at(index, TILE)]).astype(BF16)

    hooks.pop((PROJECT, 0))
    each_unrolled(3 * D // TILE, project)
    put_out("qkv", qkv, qkv_out)
    put_out("qkv_w", qkv_w, weight_outs[0])
    before(TURN_X, None)
    turn_out(low_a, x_t, 0)

    def attend_pair(pair):
        before(ATTEND, pair)
        for start, size in ((0, last), (last, SPAN)):
            rows = pl.ds(start, size)
            query = qkv[rows, at(pair, 128)]
            key = qkv[rows, pl.ds(D + pair * 128, 128)]
            val = qkv[rows, pl.ds(2 * D + pair * 128, 128)]
            mask = bias[...] if start == 0 else jnp.where(keys[0:1, last:tokens] > 0, 0.0, -1e30)
            mixed = []
            for first in (True, False):
                chosen = jnp.where(head_lanes(first), query, jnp.zeros_like(query))
                scores = dot_nt(chosen, key) * 0.125 + mask
                highest = jnp.max(scores, 1, keepdims=True)
                raised = jnp.exp(scores - highest)
                summed = jnp.sum(raised, 1, keepdims=True)
                shares = (raised * (1.0 / summed)).astype(BF16)
                mixed.append(dot_nn(shares, val))
                put_lane(side, rows, 2 * pair + (0 if first else 1), highest + jnp.log(summed))
            mix[rows, at(pair, 128)] = jnp.where(head_lanes(True), mixed[0], mixed[1]).astype(BF16)

    each_unrolled(HEADS // 2, attend_pair)
    before(OUT, 0)
    hooks.pop((OUT, 0))
    need(5)

    def out_project(index):
        before(OUT, index)
        value[:, at(index, TILE)] = value[:, at(index, TILE)] + dot_nn(mix[...], out_w[:, at(index, TILE)])

    each_unrolled(D // TILE, out_project)
    put_out("out_w", out_w, weight_outs[1])
    put_out("mix", mix, mix_out)
    before(NORM_B, None)

    def norm_b(index):
        rows = at(index, ROWS)
        found, normed, inverse = layer_norm(value[rows, :], norm_rows[2], norm_rows[3])
        value[rows, :] = found
        low_y[rows, :] = found.astype(BF16)
        nb[0][rows, :], nb[1][rows, :] = split_two(normed)
        put_lane(side, rows, 13, inverse)

    each_unrolled(tokens // ROWS, norm_b)
    put_out("a", low_y, a_out)
    put_out("nb0", nb[0], nb_outs[0])
    put_out("nb1", nb[1], nb_outs[1])
    before(FEED_IN, 0)
    hooks.pop((FEED_IN, 0))
    need(3)

    def feed_in(index):
        before(FEED_IN, index)
        hidden = dot_nn(low_y[...], in_w[:, at(index, TILE)])
        active, slant = gelu_pair(hidden)
        active = active.astype(BF16)
        act[:, at(index, TILE)] = active
        slope[:, at(index, TILE)] = slant.astype(BF16)

    each_unrolled(4 * D // TILE, feed_in)
    put_out("act", act, act_out)
    put_out("slope", slope, slope_out)
    put_out("in_w", in_w, weight_outs[2])
    before(TURN_A, None)
    before(FEED_OUT, 0)
    hooks.pop((FEED_OUT, 0))
    need(4)

    def feed_out(index):
        before(FEED_OUT, index)
        value[:, at(index, TILE)] = value[:, at(index, TILE)] + dot_nn(act[...], down_w[:, at(index, TILE)])

    each_unrolled(D // TILE, feed_out)
    put_out("down_w", down_w, weight_outs[3])
    before(REST, None)
    turns[0].wait()
    outs.pop("mix").wait()
    outs.pop("a").wait()

    def norm_c(index):
        rows = at(index, ROWS)
        found, normed, inverse = layer_norm(value[rows, :], norm_rows[4], norm_rows[5])
        low_a[rows, :] = found.astype(BF16)
        nc[0][rows, :], nc[1][rows, :] = split_two(normed)
        put_lane(side, rows, 14, inverse)

    each_unrolled(tokens // ROWS, norm_c)
    put_out("y", low_a, y_out)
    put_out("nc0", nc[0], nc_outs[0])
    put_out("nc1", nc[1], nc_outs[1])
    for swap in swaps:
        swap.wait_send()
    for copy in token_copies:
        copy.wait_send()
    for piece in range(6):
        copy_of(piece, me, SIDE_WAY).wait_send()
    for number in FRONT:
        if number < 1000:
            piece, k, ways, _ = block_of(number)
            for way in ways:
                copy_of(piece, k, way).wait_send()
    for copy in outs.values():
        copy.wait()


def front(large, lengths):
    vmem, hbm = pl.BlockSpec(memory_space=pltpu.VMEM), pl.BlockSpec(memory_space=pl.ANY)
    smem = pl.BlockSpec(memory_space=pltpu.SMEM)
    shape, dma = jax.ShapeDtypeStruct, pltpu.SemaphoreType.DMA
    tokens = 5 * SPAN
    small = [shape((1, 1), F32), shape((16, D), F32), shape((tokens, 128), F32)]
    small += [shape((tokens, 128), jnp.int32), shape((8, tokens), jnp.int32), shape((1, 128), F32)]
    out = [shape((D, tokens), BF16)] + [shape((tokens, width), BF16) for width in (D, D, 4 * D, D, 4 * D, 3 * D)]
    out += [shape((tokens, D), F32)] + [shape((tokens, D), BF16)] * 4
    out += [shape((32 * SHAPES[m][0], SHAPES[m][1]), BF16) for m in (Q_, O_, I_, D_, E_)]
    return pl.pallas_call(
        front_kernel,
        out_shape=small + out,
        in_specs=[hbm] * 13 + [smem] * 2,
        out_specs=[vmem] * len(small) + [hbm] * len(out),
        scratch_shapes=[pltpu.VMEM((32 * size, wide), BF16) for size, wide in SHAPES]
        + [pltpu.VMEM((tokens, D), F32)] * 2
        + [pltpu.VMEM((tokens, D), BF16)] * 3
        + [
            pltpu.VMEM((tokens, 3 * D), BF16),
            pltpu.VMEM((tokens, 4 * D), BF16),
            pltpu.VMEM((tokens, 4 * D), BF16),
            pltpu.VMEM((HALF, WIDE), BF16),
            pltpu.VMEM((HALF, WIDE), BF16),
            pltpu.VMEM((tokens - SPAN, tokens - SPAN), F32),
            pltpu.VMEM((1, D, tokens), BF16),
        ]
        + [pltpu.VMEM((tokens, D), BF16)] * 2
        + [pltpu.VMEM(member.shape, member.dtype) for member in large]
        + [pltpu.VMEM(SHAPES[E_], F32)]
        + [pltpu.VMEM((2 * size, wide // 2), F32) for size, wide in SHAPES]
        + [pltpu.VMEM((4, 8, SPAN), jnp.int32), pltpu.VMEM((5, 8, SPAN), jnp.int32)]
        + [dma((13,)), dma((5,)), dma((5,)), dma((3,)), dma((3,)), dma((6, 16, 6)), dma((6, 16)), dma((6, 16))]
        + [dma((18,)), dma((1,))],
        compiler_params=pltpu.CompilerParams(
            collective_id=0, has_side_effects=True, vmem_limit_bytes=63 * 1024 * 1024
        ),
    )(*large, *lengths)


PACK = 256


def split_two(value):
    high = value.astype(BF16)
    return high, (value - high.astype(F32)).astype(BF16)


def middle_kernel(*refs):
    (wide_h, qkv_wh, out_wh, in_wh, down_h, y_h, act_h, a_h, mix_h, slope_h, qkv_h, na_h) = refs[0:12]
    nb_h, nc_h = refs[12:14], refs[14:16]
    cols, keys, side, gains, count = refs[16:21]
    loss_out, norm_out = refs[21:23]
    glog_out, y_t, a_t, mix_t, act_t, ge_t, gffn_out, gh_out, gattn_out, gqkv_out = refs[23:33]
    wide, qkv_w, out_w, in_w, plain, qkv = refs[33:39]
    nb = refs[39:41]
    slope_ring, act_ring, down_ring = refs[41:44]
    logits, glog, gh, gffn, gattn, packed, grad, turned, act_turned = refs[44:53]
    back_kv, gqkv, whole_grad, pick, pick_t, bias, side_pack, side_turned, dq, ge = refs[53:63]
    load_sem, ring_sem, out_sem = refs[63:66]
    nc = (gqkv.at[:, D : 2 * D], gqkv.at[:, 2 * D : 3 * D])
    gatt = packed
    tokens = cols.shape[0]
    names = ("wide", "y", "nc0", "nc1", "in_w", "nb0", "nb1", "out_w", "qkv", "qkv_w")
    sources = (wide_h, y_h, nc_h[0], nc_h[1], in_wh, nb_h[0], nb_h[1], out_wh, qkv_h, qkv_wh)
    targets = (wide, plain, nc[0], nc[1], in_w, nb[0], nb[1], out_w, qkv, qkv_w)

    def na_copy(i):
        return pltpu.make_async_copy(
            na_h.at[:, at(i, TILE)], logits.at[pl.ds(i * tokens, tokens), :], load_sem.at[10 + i]
        )

    def tile_of(index):
        return pl.ds(index * PACK, PACK)

    loads = {name: pltpu.make_async_copy(sources[i], targets[i], load_sem.at[i]) for i, name in enumerate(names)}
    for name in ("y", "wide"):
        loads[name].start()

    weight_row = keys[3:4, :].astype(F32)
    weight_col = cols[:, 3:4].astype(F32)
    earlier = lax.broadcasted_iota(jnp.int32, (tokens, tokens), 0) < lax.broadcasted_iota(jnp.int32, (tokens, tokens), 1)
    later = lax.broadcasted_iota(jnp.int32, (tokens, tokens), 0) > lax.broadcasted_iota(jnp.int32, (tokens, tokens), 1)
    rank_row = dot_nn(
        jnp.broadcast_to(weight_row, (16, tokens)).astype(BF16), jnp.where(earlier, 1.0, 0.0).astype(BF16)
    )[0:1]
    rank_col = dot_nn(
        jnp.where(later, 1.0, 0.0).astype(BF16), jnp.broadcast_to(weight_col, (tokens, 128)).astype(BF16)
    )[:, 0:1]
    rank_row = jnp.where(weight_row > 0, rank_row, -1.0)
    rank_col = jnp.where(weight_col > 0, rank_col, -1.0)
    blocks = (jnp.sum(weight_row).astype(jnp.int32) + (PACK - 1)) // PACK
    blocks = jnp.maximum(blocks, 1)
    inverse_count = 1.0 / count[...]
    norm_rows = [gains[5 + i : 6 + i, :] for i in range(6)]
    loss_out[...] = jnp.zeros((1, 1), F32)
    norm_out[...] = jnp.zeros(norm_out.shape, F32)
    back_kv[...] = jnp.zeros(back_kv.shape, F32)
    whole_grad[...] = jnp.zeros(whole_grad.shape, F32)
    gqkv[:, 0:D] = jnp.zeros((tokens, D), BF16)
    side_first = side[...].astype(BF16)
    rest = side[...] - side_first.astype(F32)
    side_second = rest.astype(BF16)
    side_third = (rest - side_second.astype(F32)).astype(BF16)
    waited = set()

    def load_plain(source):
        return pltpu.make_async_copy(source, plain, load_sem.at[1])

    def ring(kind, source, target):
        def copy(j):
            piece = source.at[at(j, TILE), :] if kind == 2 else source.at[:, at(j, TILE)]
            return pltpu.make_async_copy(piece, target.at[j % 2], ring_sem.at[kind * 2 + j % 2])

        return copy

    rings = [ring(0, slope_h, slope_ring), ring(1, act_h, act_ring), ring(2, down_h, down_ring)]
    outs = [
        (glog, glog_out, 0),
        (turned.at[0], y_t, 1),
        (turned.at[1], a_t, 1),
        (turned.at[2], mix_t, 1),
        (act_turned, act_t, 1),
        (gffn, gffn_out, 0),
        (gh, gh_out, 0),
        (gattn, gattn_out, 0),
    ]

    def out_copy(i, block):
        source, target, axis = outs[i]
        place = at(block, PACK)
        return pltpu.make_async_copy(
            source, target.at[place, :] if axis == 0 else target.at[:, place], out_sem.at[i]
        )

    def wait_load(name):
        loads[name].wait()

    wait_load("wide")
    for name in names[2:]:
        loads[name].start()

    def block_step(block, carry):
        slot_col = lax.broadcasted_iota(jnp.int32, (PACK, 1), 0).astype(F32) + (block * PACK).astype(F32)
        slot_row = lax.broadcasted_iota(jnp.int32, (1, PACK), 1).astype(F32) + (block * PACK).astype(F32)
        hit = jnp.where(rank_row == slot_col, 1.0, 0.0)
        pick[...] = hit.astype(BF16)
        hit_t = jnp.where(rank_col == slot_row, 1.0, 0.0)
        pick_t[...] = hit_t.astype(BF16)
        target = jnp.sum(hit * keys[2:3, :].astype(F32), 1, keepdims=True)
        weight = jnp.sum(hit, 1, keepdims=True)
        row_col = cols[:, 4:5].astype(F32)
        row_of_token = jnp.sum(hit_t * row_col, 0, keepdims=True)
        bias[...] = jnp.where((row_of_token == row_col) & (cols[:, 5:6] > 0), 0.0, -1e30)
        side_pack[...] = (
            dot_nn(pick[...], side_first) + dot_nn(pick[...], side_second) + dot_nn(pick[...], side_third)
        )
        side_turned[...] = side_pack[...].T
        for kind in range(3):
            for j in range(2):
                rings[kind](j).start()
        load_plain(y_h).wait()
        packed[...] = dot_nn(pick[...], plain[...]).astype(BF16)
        load_plain(a_h).start()
        turned[0] = packed[...].T
        out_copy(1, block).start()

        def lanes(index):
            return (lax.broadcasted_iota(jnp.int32, (1, TILE), 1) + index * TILE).astype(F32)

        highest = jnp.full((PACK, 128), -1e30, F32)
        for index in range(TABLE_TILES):
            found = dot_nn(packed[...], wide[:, at(index, TILE)])
            if index == TABLE_TILES - 1:
                found = jnp.where(lanes(index) < VOCAB, found, -1e30)
            logits[tile_of(index), :] = found
            highest = jnp.maximum(highest, jnp.maximum(found[:, 0:128], found[:, 128:256]))
        highest = jnp.max(highest, 1, keepdims=True)
        summed, picked = jnp.zeros((PACK, 128), F32), jnp.zeros((PACK, 128), F32)
        for index in range(TABLE_TILES):
            found = logits[tile_of(index), :]
            raised = jnp.exp(found - highest)
            logits[tile_of(index), :] = raised
            own = jnp.where(lanes(index) == target, found, 0.0)
            summed = summed + raised[:, 0:128] + raised[:, 128:256]
            picked = picked + own[:, 0:128] + own[:, 128:256]
        summed = jnp.sum(summed, 1, keepdims=True)
        picked = jnp.sum(picked, 1, keepdims=True)
        loss_out[...] = loss_out[...] + jnp.sum(weight * (highest + jnp.log(summed) - picked), 0, keepdims=True)
        scale = weight * inverse_count
        share = scale / summed
        for index in range(TABLE_TILES):
            found = logits[tile_of(index), :] * share - jnp.where(lanes(index) == target, scale, 0.0)
            glog[:, at(index, TILE)] = found.astype(BF16)
        out_copy(0, block).start()
        for index in range(D // TILE):
            grad[:, at(index, TILE)] = dot_nt(glog[...], wide[at(index, TILE), 0:TABLE_END])

        @pl.when(block == 0)
        def _():
            for name in names[2:4]:
                wait_load(name)

        normed = dot_nn(pick[...], nc[0][...]) + dot_nn(pick[...], nc[1][...])
        found = grad[...]
        back = layer_norm_back(found, normed, lane_at(side_pack[...], 14), norm_rows[4])
        norm_out[4:5, :] = norm_out[4:5, :] + jnp.sum(found * normed, 0, keepdims=True)
        norm_out[5:6, :] = norm_out[5:6, :] + jnp.sum(found, 0, keepdims=True)
        grad[...] = back
        gffn[...] = back.astype(BF16)
        out_copy(5, block).start()

        load_plain(a_h).wait()
        turned[1] = dot_nn(pick[...], plain[...]).astype(BF16).T
        out_copy(2, block).start()
        load_plain(mix_h).start()
        for index in range(4 * D // TILE):
            for kind in range(3):
                rings[kind](index).wait()
            slant = dot_nn(pick[...], slope_ring[index % 2])
            found = dot_nt(gffn[...], down_ring[index % 2]) * slant
            gh[:, at(index, TILE)] = found.astype(BF16)
            act_turned[at(index, TILE), :] = dot_nn(pick[...], act_ring[index % 2]).astype(BF16).T
            if index + 2 < 4 * D // TILE:
                for kind in range(3):
                    rings[kind](index + 2).start()
        out_copy(6, block).start()
        out_copy(4, block).start()
        load_plain(mix_h).wait()
        turned[2] = dot_nn(pick[...], plain[...]).astype(BF16).T
        out_copy(3, block).start()
        load_plain(y_h).start()

        @pl.when(block == 0)
        def _():
            for name in names[4:8]:
                wait_load(name)

        for index in range(D // TILE):
            grad[:, at(index, TILE)] = grad[:, at(index, TILE)] + dot_nt(gh[...], in_w[at(index, TILE), :])
        normed = dot_nn(pick[...], nb[0][...]) + dot_nn(pick[...], nb[1][...])
        found = grad[...]
        back = layer_norm_back(found, normed, lane_at(side_pack[...], 13), norm_rows[2])
        norm_out[2:3, :] = norm_out[2:3, :] + jnp.sum(found * normed, 0, keepdims=True)
        norm_out[3:4, :] = norm_out[3:4, :] + jnp.sum(found, 0, keepdims=True)
        gattn[...] = back.astype(BF16)
        out_copy(7, block).start()
        high, low = split_two(back)
        whole_grad[...] = whole_grad[...] + dot_nn(pick_t[...], high) + dot_nn(pick_t[...], low)
        for index in range(D // TILE):
            gatt[:, at(index, TILE)] = dot_nt(gattn[...], out_w[at(index, TILE), :]).astype(BF16)

        @pl.when(block == 0)
        def _():
            wait_load("qkv")

        def attend_pair_back(pair):
            spots = [pl.ds(i * D + pair * 128, 128) for i in range(3)]
            query = dot_nn(pick[...], qkv[:, spots[0]]).astype(BF16)
            key, val = qkv[:, spots[1]], qkv[:, spots[2]]
            given = gatt[:, at(pair, 128)]
            key_t = key.T
            found = []
            for first in (True, False):
                lanes_here = head_lanes(first)
                chosen = jnp.where(lanes_here, query, jnp.zeros_like(query))
                mine = jnp.where(lanes_here, given, jnp.zeros_like(given))
                total = side_turned[pl.ds(2 * pair + (0 if first else 1), 1), :]
                shares = jnp.exp(dot_nt(key, chosen) * 0.125 + bias[...] - total)
                grad_share = dot_nt(val, mine)
                middle = jnp.sum(shares * grad_share, 0, keepdims=True)
                grad_score = (shares * (grad_share - middle)).astype(BF16)
                found.append(
                    (
                        dot_nn(key_t, grad_score) * 0.125,
                        dot_nn(grad_score, query) * 0.125,
                        dot_nn(shares.astype(BF16), given),
                    )
                )
            lanes_here = head_lanes(True)
            both = jnp.concatenate((found[0][0][0:HEAD_DIM], found[1][0][HEAD_DIM:]), 0)
            dq[at(pair, 128), :] = both.astype(BF16)
            for i in (1, 2):
                spot = pl.ds((i - 1) * D + pair * 128, 128)
                back_kv[:, spot] = back_kv[:, spot] + jnp.where(lanes_here, found[0][i], found[1][i])

        each_unrolled(HEADS // 2, attend_pair_back)
        gqkv[:, 0:D] = (gqkv[:, 0:D].astype(F32) + dot_nt(pick_t[...], dq[...])).astype(BF16)
        for i in range(len(outs)):
            out_copy(i, block).wait()
        return carry

    lax.fori_loop(0, blocks, block_step, 0)
    load_plain(y_h).wait()
    for i in range(D // TILE):
        na_copy(i).start()
    gqkv[:, D:] = back_kv[...].astype(BF16)
    copy_qkv = pltpu.make_async_copy(gqkv, gqkv_out, out_sem.at[8])
    copy_qkv.start()
    for ref in (glog, gffn, gh, gattn):
        ref[...] = jnp.zeros(ref.shape, BF16)
    for block in range(1, 3):

        @pl.when(blocks <= block)
        def _():
            for i in range(len(outs)):
                out_copy(i, block).start()

    wait_load("qkv_w")
    for index in range(D // TILE):
        whole_grad[:, at(index, TILE)] = whole_grad[:, at(index, TILE)] + dot_nt(gqkv[...], qkv_w[at(index, TILE), :])
    for i in range(D // TILE):
        na_copy(i).wait()
    zero = jnp.zeros((1, D), F32)

    def norm_a_back(index, carry):
        gain, shift = carry
        rows = at(index, ROWS)
        inverse = lane_at(side[rows, :], 12)
        found = whole_grad[rows, :]
        normed = jnp.concatenate(
            [logits[pl.ds(i * tokens + index * ROWS, ROWS), :] for i in range(D // TILE)], 1
        )
        ge[:, rows] = layer_norm_back(found, normed, inverse, norm_rows[0]).astype(BF16).T
        return gain + jnp.sum(found * normed, 0, keepdims=True), shift + jnp.sum(found, 0, keepdims=True)

    gain, shift = zero, zero
    for index in range(tokens // ROWS):
        gain, shift = norm_a_back(index, (gain, shift))
    norm_out[0:1, :] = gain
    norm_out[1:2, :] = shift
    copy_ge = pltpu.make_async_copy(ge, ge_t, out_sem.at[9])
    copy_ge.start()
    for block in range(1, 3):

        @pl.when(blocks <= block)
        def _():
            for i in range(len(outs)):
                out_copy(i, block).wait()

    copy_qkv.wait()
    copy_ge.wait()


def middle(large, small):
    tokens = 5 * SPAN
    slots = 3 * PACK
    vmem, hbm = pl.BlockSpec(memory_space=pltpu.VMEM), pl.BlockSpec(memory_space=pl.ANY)
    shape, dma = jax.ShapeDtypeStruct, pltpu.SemaphoreType.DMA
    out = [shape((slots, TABLE_END), BF16)] + [shape((D, slots), BF16)] * 3 + [shape((4 * D, slots), BF16)]
    out += [shape((D, tokens), BF16), shape((slots, D), BF16), shape((slots, 4 * D), BF16), shape((slots, D), BF16)]
    out += [shape((tokens, 3 * D), BF16)]

    def rows(count, width, kind=BF16):
        return pltpu.VMEM((count, width), kind)

    scratch = [rows(D, WIDE), rows(D, 3 * D), rows(D, D), rows(D, 4 * D), rows(tokens, D), rows(tokens, 3 * D)]
    scratch += [rows(tokens, D)] * 2
    scratch += [pltpu.VMEM((2, tokens, TILE), BF16)] * 2 + [pltpu.VMEM((2, TILE, D), BF16)]
    scratch += [rows(PACK * TABLE_TILES, TILE, F32), rows(PACK, TABLE_END), rows(PACK, 4 * D)] + [rows(PACK, D)] * 3
    scratch += [rows(PACK, D, F32), pltpu.VMEM((3, D, PACK), BF16), rows(4 * D, PACK)]
    scratch += [rows(tokens, 2 * D, F32), rows(tokens, 3 * D), rows(tokens, D, F32), rows(PACK, tokens)]
    scratch += [rows(tokens, PACK), rows(tokens, PACK, F32), rows(PACK, 128, F32), rows(128, PACK, F32)]
    scratch += [rows(D, PACK), rows(D, tokens)]
    scratch += [dma((13,)), dma((6,)), dma((10,))]
    return pl.pallas_call(
        middle_kernel,
        out_shape=[shape((1, 1), F32), shape((6, D), F32)] + out,
        in_specs=[hbm] * 16 + [vmem] * 5,
        out_specs=[vmem] * 2 + [hbm] * len(out),
        scratch_shapes=scratch,
        compiler_params=pltpu.CompilerParams(vmem_limit_bytes=63 * 1024 * 1024),
    )(*large, *small)


LEFT = 768
PIECES = ((Q_, 0, 1152), (E_, 0, 1280), (E_, 1280, 1280), (I_, 0, 1536), (D_, 0, 384), (O_, 0, 384))
SUM_WAY = (3, 1, 1, 2, 0, 0)
GATHER_WAY = (0, 1, 2, 0, 3, 1)
TASKS = (
    129, 0, 1, 96, 7, 5, 6, 4, 97, 13, 102, 103, 11, 128, 101, 12, 9, 8,
    132, 3, 104, 105, 2, 100, 108, 64, 14, 65, 71, 15, 111, 70, 134, 160, 106, 72,
    136, 161, 68, 10, 140, 135, 107, 73, 130, 110, 109, 33, 168, 166, 76, 137, 141, 143,
    139, 69, 173, 133, 77, 32, 169, 172, 144, 38, 164, 66, 40, 75, 39, 138, 176, 131,
    44, 36, 41, 142, 98, 167, 79, 34, 37, 80, 45, 165, 145, 47, 43, 74, 162, 67,
    48, 16, 171, 78, 35, 42, 46, 174, 99, 112, 81, 170, 163, 175, 17, 49, 113, 177,
)


def reduce_kernel(*refs):
    given, (cols, norm_sums, loss, squares) = refs[0:11], refs[11:15]
    y_t, ge_t, glog, x_t, gqkv, mix_t, gattn, a_t, gh, act_t, gffn = given
    lane_olds, side_olds, moment = refs[15:21], refs[21:27], refs[27]
    outs, sums_out, totals_out = refs[28:33], refs[33], refs[34]
    own, side, first, second, column, fin = (refs[35 + 6 * i : 41 + 6 * i] for i in range(6))
    left, (glog_v, gqkv_v, gattn_v, gh_v, gffn_v), stage, tails, norm_t = refs[71:78], refs[78:83], refs[83], refs[84], refs[85]
    lane_plane, lane_z, lane_halves = refs[86:89]
    scalar_sums, total_sums = refs[89:91], refs[91:93]
    load_sem, ring_sem, tail_sem, side_recv, first_send, first_recv, second_send, second_recv = refs[93:101]
    z_send, z_recv, swap_send, swap_recv = refs[101:105]
    lane_send, lane_recv, scalar_send, scalar_recv, total_send, total_recv = refs[105:111]
    z, y, x, c = here()
    peers = all_peers()
    me = chip(z, y, x)

    barrier = pltpu.get_barrier_semaphore()
    spot = y * 2 + x
    column_peers = [device((z + 1 + i) % 4, y, x, c) for i in range(3)]
    plane = [(y, 1 - x), (1 - y, x), (1 - y, 1 - x)]
    plane_peers = [device(z, to_y, to_x, c) for to_y, to_x in plane]
    greeted = column_peers + plane_peers + [device(z, to_y, to_x, 1 - c) for to_y, to_x in [(y, x)] + plane]
    for peer in greeted:
        pl.semaphore_signal(barrier, inc=1, device_id=peer, device_id_type=MESH)

    tokens = cols.shape[0]

    def act_part(group):
        return act_t.at[pl.ds(LEFT * group, LEFT), 0:tokens]

    operands = (
        ((x_t, left[1]), (gqkv, gqkv_v)),
        ((y_t.at[:, 0:tokens], left[2]), (ge_t, left[3]), (glog.at[0:tokens, :], glog_v)),
        (),
        ((a_t.at[:, 0:tokens], left[0]), (gh.at[0:tokens, :], gh_v)),
        ((gffn.at[0:tokens, :], gffn_v), (act_part(0), left[5]), (act_part(1), left[6])),
        ((mix_t.at[:, 0:tokens], left[4]), (gattn.at[0:tokens, :], gattn_v)),
    )
    loads = {}
    waited = set()
    for task in TASKS:
        piece = task // 32 if task // 32 != 2 else 1
        if piece not in loads:
            loads[piece] = []
            for source, target in operands[piece]:
                number = sum(len(member) for member in loads.values())
                loads[piece].append(pltpu.make_async_copy(source, target, load_sem.at[number]))
                loads[piece][-1].start()

    def loaded(piece):
        piece = 1 if piece == 2 else piece
        if piece not in waited:
            waited.add(piece)
            for member in loads[piece]:
                member.wait()

    norm_t[...] = jnp.zeros(norm_t.shape, F32)
    norm_t[5:11, :] = norm_sums[...]
    pl.semaphore_wait(barrier, 10)

    def size_of(piece):
        return 2 * SHAPES[PIECES[piece][0]][0]

    def slot(ref, piece, index):
        size = size_of(piece)
        return ref[piece].at[pl.ds(pl.multiple_of(index * size, size), size), :]

    def half_of(piece):
        return SHAPES[PIECES[piece][0]][1] // 2

    def chosen(start):
        lane = lax.broadcasted_iota(jnp.int32, (1, TILE), 1) + start
        hit = (cols[:, 0:1] == lane) | (cols[:, 1:2] == lane)
        return jnp.where(hit, 1.0, 0.0).astype(BF16)

    def ring_copy(piece, rows, lanes, number, index):
        place = number % 3
        return pltpu.make_async_remote_copy(
            src_ref=stage.at[place],
            dst_ref=side[piece].at[rows, lanes],
            send_sem=ring_sem.at[place],
            recv_sem=side_recv.at[piece, index],
            device_id=peers[SIDE],
            device_id_type=MESH,
        )

    def tail_copy(piece, rows, lanes, number, index):
        return pltpu.make_async_remote_copy(
            src_ref=tails.at[number],
            dst_ref=side[piece].at[rows, lanes],
            send_sem=tail_sem.at[number],
            recv_sem=side_recv.at[piece, index],
            device_id=peers[SIDE],
            device_id_type=MESH,
        )

    whole = pl.ds(0, LEFT)
    ring_count, tail_count = [0], [0]

    def give(piece, rows, lanes, number, index):
        def before():
            if number >= 3:
                ring_copy(piece, rows, lanes, number, index).wait_send()

        def write(value):
            stage[number % 3] = value.astype(BF16)

        return before, write, lambda: ring_copy(piece, rows, lanes, number, index).start()

    def keep(piece, rows, lanes):
        def write(value):
            own[piece][rows, lanes] = value.astype(BF16)

        return lambda: None, write, lambda: None

    def plain(piece, mine, source, right, group):
        wide = PIECES[piece][2]
        half = c if mine else 1 - c
        rows = pl.ds(LEFT * group, LEFT)
        base = ring_count[0]

        def step(j):
            lanes = at(j, TILE)
            before, write, after = keep(piece, rows, lanes) if mine else give(
                piece, rows, lanes, base + j, group * (wide // TILE) + j
            )
            before()
            write(dot_nn(source[...], right[:, pl.ds(pl.multiple_of(half * wide + j * TILE, 128), TILE)]))
            after()

        each_unrolled(wide // TILE, step)
        if not mine:
            ring_count[0] += wide // TILE
        if wide % TILE:
            start = wide - 128
            value = dot_nn(source[...], right[:, pl.ds(pl.multiple_of(half * wide + start, 128), 128)])
            if mine:
                own[piece][rows, start:wide] = value.astype(BF16)
            else:
                number = tail_count[0]
                tail_count[0] += 1
                groups = SHAPES[PIECES[piece][0]][0] // 24
                tails[number] = value.astype(BF16)
                tail_copy(piece, rows, pl.ds(start, 128), number, groups * (wide // TILE) + group).start()

    def wide_product(piece, mine):
        half = c if mine else 1 - c
        wide = half_of(piece)
        skip = PIECES[piece][1] // TILE
        base = ring_count[0]

        def both(j):
            start = pl.multiple_of(half * wide + (skip + j) * TILE, TILE)
            return dot_nn(left[2][...], glog_v[:, pl.ds(start, TILE)]) + dot_nn(left[3][...], chosen(start))

        def target(j):
            lanes = at(j, TILE)
            return keep(piece, whole, lanes) if mine else give(piece, whole, lanes, base + j, j)

        def step(j):
            before, write, after = target(j)
            before()
            write(both(j))
            after()

        if not mine:
            ring_count[0] += 5
        if skip == 0:
            each_unrolled(5, step)
            return
        each_unrolled(1, step)
        before, write, after = target(1)
        before()
        norm_part = jnp.where(half == 1, norm_t[...], 0.0).T
        write(both(1) + jnp.concatenate((norm_part, jnp.zeros((LEFT, TILE - 128), F32)), 1))
        after()
        for j in range(2, 5):
            before, write, after = target(j)
            before()

            @pl.when(half == 0)
            def _():
                write(both(j))

            @pl.when(half == 1)
            def _():
                if j == 2:
                    write(jnp.zeros((LEFT, TILE), F32))
                else:
                    write(dot_nn(left[3][...], chosen(half_of(piece) + (skip + j) * TILE)))

            after()

    def products(piece, mine):
        loaded(piece)
        if piece in (1, 2):
            wide_product(piece, mine)
        elif piece == 4:
            if not mine:
                for group in range(4):
                    source = left[5 + group % 2]
                    if group >= 2:
                        loads[piece][1 + group % 2].wait()
                    plain(piece, False, source, gffn_v, group)
                    plain(piece, True, source, gffn_v, group)
                    if group < 2:
                        again = pltpu.make_async_copy(act_part(group + 2), source, load_sem.at[12 + group])
                        again.start()
                        loads[piece][1 + group] = again
        else:
            source, right = {0: (left[1], gqkv_v), 3: (left[0], gh_v), 5: (left[4], gattn_v)}[piece]
            plain(piece, mine, source, right, 0)

    def combine(piece, target, parts):
        def some(rows, lanes):
            total = parts[0][rows, lanes].astype(F32)
            for member in parts[1:]:
                total = total + member[rows, lanes].astype(F32)
            target[rows, lanes] = total.astype(target.dtype)

        wide = PIECES[piece][2]
        if piece == 4:
            each(4, lambda group: some(at(group, 48), slice(0, wide)))
            return
        if wide >= 512:
            each(wide // 512, lambda j: some(slice(0, 48), at(j, 512)))
        if wide % 512:
            some(slice(0, 48), slice(wide // 512 * 512, wide))

    def hop(piece, k, land, index, sems, way):
        return pltpu.make_async_remote_copy(
            src_ref=slot(own, piece, k),
            dst_ref=slot(land, piece, index),
            send_sem=sems[0].at[piece, index],
            recv_sem=sems[1].at[piece, index],
            device_id=peers[way],
            device_id_type=MESH,
        )

    FIRST, SECOND = (first_send, first_recv), (second_send, second_recv)

    def landed(piece, land, index, sems):
        hop(piece, me, land, index, sems, XWAY).wait_recv()

    def block(piece, a, b, far):
        return chip(far, a, b) if SUM_WAY[piece] % 2 == 0 else chip(far, b, a)

    def split(piece):
        return (y, x, YWAY, XWAY) if SUM_WAY[piece] % 2 == 0 else (x, y, XWAY, YWAY)

    readied = set()

    def ready(piece):
        if piece in readied:
            return
        readied.add(piece)
        wide, groups = PIECES[piece][2], SHAPES[PIECES[piece][0]][0] // 24
        for group in range(groups):
            for j in range(wide // TILE):
                ring_copy(piece, pl.ds(LEFT * group, LEFT), at(j, TILE), 0, group * (wide // TILE) + j).wait_recv()
            if wide % TILE:
                index = groups * (wide // TILE) + group
                tail_copy(piece, pl.ds(LEFT * group, LEFT), pl.ds(wide - 128, 128), 0, index).wait_recv()

    def both_cores(piece, k):
        return (slot(own, piece, k), slot(side, piece, k))

    def first_block(piece, i):
        a, b, way, _ = split(piece)
        t, v = (z + i // 2) % 4, (1 - b) if i % 2 == 0 else b
        return block(piece, 1 - a, v, t), 2 * t + v, way

    def first_send_of(piece, i):
        ready(piece)
        k, index, way = first_block(piece, i)
        combine(piece, slot(own, piece, k), both_cores(piece, k))
        hop(piece, k, first, index, FIRST, way).start()

    def second_block(piece, i):
        a, b, _, way = split(piece)
        if SUM_WAY[piece] > 1:
            return block(piece, a, 1 - b, z), 0, way
        t = (z + i) % 4
        return block(piece, a, 1 - b, t), t, way

    def z_slots(piece, v):
        for i in range(3):
            t = (z + 1 + i) % 4
            index = t if v is None else 2 * t + v
            pltpu.make_async_remote_copy(
                src_ref=slot(own, piece, me),
                dst_ref=slot(column, piece, index),
                send_sem=z_send.at[piece, index],
                recv_sem=z_recv.at[piece, index],
                device_id=column_peers[i],
                device_id_type=MESH,
            ).wait_recv()
        return tuple(
            slot(column, piece, (z + 1 + i) % 4 if v is None else 2 * ((z + 1 + i) % 4) + v) for i in range(3)
        )

    def first_slot(piece, v, t):
        landed(piece, first, 2 * t + v, FIRST)
        return (slot(first, piece, 2 * t + v),)

    def second_slot(piece, index):
        landed(piece, second, index, SECOND)
        return (slot(second, piece, index),)

    def second_send_of(piece, i):
        k, index, way = second_block(piece, i)
        other = 1 - split(piece)[1]
        if SUM_WAY[piece] > 1:
            parts = first_slot(piece, other, z) + z_slots(piece, other)
        else:
            parts = first_slot(piece, other, index)
        combine(piece, slot(own, piece, k), both_cores(piece, k) + parts)
        hop(piece, k, second, index, SECOND, way).start()

    def z_block(piece, i):
        a, b, _, _ = split(piece)
        if SUM_WAY[piece] > 1:
            t, v = (z + 1 + i // 2) % 4, (1 - b) if i % 2 == 0 else b
            return block(piece, a, v, t), t, v, 2 * z + v, 2 * t + v, column_peers[i // 2]
        t = (z + 1 + i) % 4
        return chip(t, y, x), t, None, z, t, column_peers[i]

    def z_copy(piece, i):
        k, _, _, there, number, peer = z_block(piece, i)
        return pltpu.make_async_remote_copy(
            src_ref=slot(own, piece, k),
            dst_ref=slot(column, piece, there),
            send_sem=z_send.at[piece, number],
            recv_sem=z_recv.at[piece, there],
            device_id=peer,
            device_id_type=MESH,
        )

    def z_send_of(piece, i):
        k, t, v, _, _, _ = z_block(piece, i)
        if v is None:
            parts = first_slot(piece, split(piece)[1], t) + second_slot(piece, t)
        else:
            parts = first_slot(piece, v, t)
        combine(piece, slot(own, piece, k), both_cores(piece, k) + parts)
        z_copy(piece, i).start()

    swaps = []

    def finish(piece):
        mine = split(piece)[1]
        parts = both_cores(piece, me) + first_slot(piece, mine, z)
        if SUM_WAY[piece] > 1:
            parts = parts + z_slots(piece, mine) + second_slot(piece, 0)
        else:
            parts = parts + second_slot(piece, z) + z_slots(piece, None)
        combine(piece, fin[piece], parts)
        m, skip, wide = PIECES[piece]
        size = SHAPES[m][0]
        lanes = pl.ds(pl.multiple_of(c * half_of(piece) + skip, 128), wide)
        swaps.append(
            pltpu.make_async_remote_copy(
                src_ref=fin[piece].at[pl.ds(pl.multiple_of((1 - c) * size, 8), size), :],
                dst_ref=outs[m].at[:, lanes],
                send_sem=swap_send.at[piece],
                recv_sem=swap_recv.at[piece],
                device_id=peers[SIDE],
                device_id_type=MESH,
            )
        )
        swaps[-1].start()
        squared = fin[piece][...] * fin[piece][...] + SQUARE_FLOOR
        lane_plane[spot, :, HALF_AT[m] + skip : HALF_AT[m] + skip + wide] = jnp.sum(squared, 0, keepdims=True)
        outs[m][:, lanes] = fin[piece][pl.ds(pl.multiple_of(c * size, 8), size), :]

    for task in TASKS:
        piece, number = task // 32, task % 32
        if number < 2:
            products(piece, number == 1)
        elif number < 10:
            first_send_of(piece, number - 2)
        elif number == 17:
            finish(piece)
        elif SUM_WAY[piece] > 1:
            if number < 16:
                z_send_of(piece, number - 10)
            else:
                second_send_of(piece, 0)
        elif number < 14:
            second_send_of(piece, number - 10)
        else:
            z_send_of(piece, number - 14)

    def spread(source, target, send, recv, peer):
        copy = pltpu.make_async_remote_copy(
            src_ref=source, dst_ref=target, send_sem=send, recv_sem=recv, device_id=peer, device_id_type=MESH
        )
        copy.start()
        return copy

    def arrive(copies):
        for copy in copies:
            copy.wait_recv()
        return copies

    plane_copies = [
        spread(lane_plane.at[spot], lane_plane.at[spot], lane_send.at[i], lane_recv.at[i], plane_peers[i])
        for i in range(3)
    ]
    for swap in swaps:
        swap.wait()
    sides, gs = statistics(outs, side_olds)

    def spread_eight(buffers, value, send, recv):
        buffers[0][2 * spot + c] = value
        mine = buffers[0].at[2 * spot + c]
        return [spread(mine, mine, send.at[i], recv.at[i], greeted[3 + i]) for i in range(7)]

    def spread_four(buffers, send, recv):
        total = [buffers[0][2 * i] + buffers[0][2 * i + 1] for i in range(4)]
        buffers[1][z] = (total[0] + total[1]) + (total[2] + total[3])
        mine = buffers[1].at[z]
        return [spread(mine, mine, send.at[7 + i], recv.at[7 + i], column_peers[i]) for i in range(3)]

    def four(buffer):
        return (buffer[0] + buffer[1]) + (buffer[2] + buffer[3])

    scalars = lanes_of([jnp.sum(member, 0, keepdims=True) for member in sides] + [loss[...]])
    scalars = jnp.concatenate((scalars, squares[...]), 1)
    sent = spread_eight(scalar_sums, scalars, scalar_send, scalar_recv)
    sent += arrive(plane_copies)
    lane_z[z] = four(lane_plane)
    z_copies = [
        spread(lane_z.at[z], lane_z.at[z], lane_send.at[3 + i], lane_recv.at[3 + i], column_peers[i]) for i in range(3)
    ]
    arrive(sent[0:7])
    last_copies = spread_four(scalar_sums, scalar_send, scalar_recv)
    sent += arrive(z_copies)
    lane_halves[c] = four(lane_z)
    halves_copy = spread(lane_halves.at[c], lane_halves.at[c], lane_send.at[6], lane_recv.at[6], peers[SIDE])
    sent += arrive(last_copies)
    sent += arrive([halves_copy])
    pair = (lane_halves[0], lane_halves[1])
    lanes = [half[:, HALF_AT[m] : HALF_AT[m] + SHAPES[m][1] // 2] for m in range(5) for half in pair]
    sums = jnp.concatenate(lanes + [four(scalar_sums[1])], 1)
    sums_out[...] = sums
    updates = updates_of(sums, gs, sides, lane_olds, moment)[0]
    totals = lanes_of(
        [total_sum(update * update) for update in updates[:6]]
        + [jnp.sum(updates[6][i : i + 1] * updates[6][i : i + 1], 1, keepdims=True) for i in range(6)]
    )
    sent += arrive(spread_eight(total_sums, totals, total_send, total_recv))
    sent += arrive(spread_four(total_sums, total_send, total_recv))
    totals_out[...] = four(total_sums[1])
    for copy in sent:
        copy.wait_send()
    for piece in range(6):
        for i in range(8):
            k, index, way = first_block(piece, i)
            hop(piece, k, first, index, FIRST, way).wait_send()
        for i in range(1 if SUM_WAY[piece] > 1 else 4):
            k, index, way = second_block(piece, i)
            hop(piece, k, second, index, SECOND, way).wait_send()
        for i in range(6 if SUM_WAY[piece] > 1 else 3):
            z_copy(piece, i).wait_send()
    for number in range(ring_count[0] - 3, ring_count[0]):
        ring_copy(1, whole, pl.ds(0, TILE), number, 0).wait_send()
    for number in range(tail_count[0]):
        tail_copy(1, whole, pl.ds(0, 128), number, 0).wait_send()


def statistics(grads, side_olds):
    wide_g = grads[E_][...]
    gs = (wide_g[:, :VOCAB], wide_g[:, PLACE_AT:]) + tuple(grads[m][...] for m in (Q_, O_, I_, D_))
    decay = 1.0 - STEP ** (-0.8)
    sides = []
    for index in range(6):
        mean = jnp.sum(gs[index] * gs[index] + SQUARE_FLOOR, 1, keepdims=True) / gs[index].shape[1]
        sides.append(decay * column_of(as_row(side_olds[index])) + (1.0 - decay) * mean)
    return sides, gs + (wide_g[:, 4096:4224],)


def updates_of(sums, gs, sides, lane_olds, moment):
    decay = 1.0 - STEP ** (-0.8)
    fresh = 1.0 - decay
    parts = [sums[:, :VOCAB], sums[:, PLACE_AT:WIDE]]
    parts += [sums[:, SUM_AT[i] : SUM_AT[i + 1]] for i in range(1, 5)]
    scalars = sums[:, SUM_AT[5] : SUM_AT[5] + 128]
    updates, lane_news = [], []
    for index in range(6):
        height = gs[index].shape[0] * 32
        lane_news.append(decay * as_row(lane_olds[index]) + fresh * (parts[index] / height))
        if index < 2:
            mean = jnp.sum(lane_news[index], 1, keepdims=True) / lane_news[index].shape[1]
        else:
            mean = lane_at(scalars, index) / height
        updates.append(gs[index] * lax.rsqrt(sides[index] * lane_news[index] / mean))
    norm_g = jnp.concatenate([row_of(lane_at(gs[6], NORM_AT - 4096 + i)) for i in range(6)], 0)
    moment_new = decay * moment[...] + fresh * (norm_g * norm_g + SQUARE_FLOOR)
    updates.append(norm_g * lax.rsqrt(moment_new))
    return updates, lane_news, norm_g, moment_new


def reduce_grads(large, small):
    tokens = 5 * SPAN
    vmem, hbm = pl.BlockSpec(memory_space=pltpu.VMEM), pl.BlockSpec(memory_space=pl.ANY)
    dma = pltpu.SemaphoreType.DMA
    scratch = []
    for counts in ((16, 16), (16, 16), (8, 8), (4, 1), (4, 8)):
        for (m, _, wide), way in zip(PIECES, SUM_WAY):
            scratch.append(pltpu.VMEM((counts[way // 2] * 2 * SHAPES[m][0], wide), BF16))
    scratch += [pltpu.VMEM((2 * SHAPES[m][0], wide), F32) for m, _, wide in PIECES]
    scratch += [pltpu.VMEM((LEFT, tokens), BF16)] * 7
    scratch += [pltpu.VMEM((tokens, width), BF16) for width in (TABLE_END, 3 * D, D, 4 * D, D)]
    scratch += [pltpu.VMEM((3, LEFT, TILE), BF16), pltpu.VMEM((6, LEFT, 128), BF16), pltpu.VMEM((128, D), F32)]
    scratch += [pltpu.VMEM((count, 1, HALF_SUMS), F32) for count in (4, 4, 2)]
    scratch += [pltpu.VMEM((count, 1, width), F32) for width in (256, 128) for count in (8, 4)]
    scratch += [dma((14,)), dma((3,)), dma((6,)), dma((6, 10)), dma((6, 8)), dma((6, 8)), dma((6, 4)), dma((6, 4))]
    scratch += [dma((6, 8)), dma((6, 8)), dma((6,)), dma((6,))]
    scratch += [dma((7,))] * 2 + [dma((10,))] * 4
    return pl.pallas_call(
        reduce_kernel,
        out_shape=[jax.ShapeDtypeStruct(shape, F32) for shape in SHAPES + ((1, SUMS), (1, 128))],
        in_specs=[hbm] * 11 + [vmem] * len(small),
        out_specs=[vmem] * 7,
        scratch_shapes=scratch,
        compiler_params=pltpu.CompilerParams(
            collective_id=1, has_side_effects=True, vmem_limit_bytes=63 * 1024 * 1024
        ),
    )(*large, *small)


def update_kernel(*refs):
    copies = [pltpu.make_async_copy(refs[i], refs[55 + i], refs[82].at[i]) for i in range(27)]
    for copy in copies:
        copy.start()
    for copy in copies:
        copy.wait()
    refs = refs[55:82] + refs[27:55]
    grads, sums, totals, ws, norms = refs[0:5], refs[5], refs[6], refs[7:13], refs[13]
    lane_olds, side_olds, moment = refs[14:20], refs[20:26], refs[26]
    loss_out, table_g, place_g, norm_g_out = refs[27:31]
    lane_outs, side_outs, moment_out, news, norm_new = refs[31:37], refs[37:43], refs[43], refs[44:50], refs[50]
    grad_outs = refs[51:55]
    sides, gs = statistics(grads, side_olds)
    updates, lane_news, norm_g, moment_new = updates_of(sums[...], gs, sides, lane_olds, moment)
    scalars = sums[:, SUM_AT[5] : SUM_AT[5] + 128]
    squares = sums[:, SUM_AT[5] + 128 :]
    loss_out[...] = lane_at(scalars, 6)
    table_g[...] = gs[0]
    place_g[...] = gs[1]
    norm_g_out[...] = norm_g
    moment_out[...] = moment_new
    for index in range(6):
        lane_outs[index][...] = lane_news[index].reshape(lane_outs[index].shape)
        side_outs[index][...] = row_of(sides[index]).reshape(side_outs[index].shape)
        if index >= 2:
            grad_outs[index - 2][...] = gs[index]
        entries = gs[index].shape[0] * gs[index].shape[1] * 32
        clip = jnp.maximum(1.0, jnp.sqrt(lane_at(totals[...], index) / entries))
        scale = learn_rate * jnp.sqrt(lane_at(squares, index) / entries) / clip
        news[index][...] = ws[index][...] - scale * updates[index]
    for i in range(6):
        clip = jnp.maximum(1.0, jnp.sqrt(lane_at(totals[...], 6 + i) / D))
        scale = learn_rate * jnp.sqrt(lane_at(squares, 6 + i) / D) / clip
        norm_new[i : i + 1, :] = norms[i : i + 1, :] - scale * updates[6][i : i + 1, :]


def update_weights(operands):
    lanes = (VOCAB, 512, 3 * D, D, 4 * D, D)
    held = (24, 24, 24, 24, 24, 96)
    shapes = [(1, 1), (24, VOCAB), (24, 512), (6, 24)]
    shapes += [(lane,) for lane in lanes] + [(size,) for size in held] + [(6, 24)]
    shapes += list(zip(held, lanes)) + [(6, 24)] + list(zip(held, lanes))[2:]
    return pl.pallas_call(
        update_kernel,
        out_shape=[jax.ShapeDtypeStruct(shape, F32) for shape in shapes],
        in_specs=[pl.BlockSpec(memory_space=pl.ANY)] * len(operands),
        out_specs=[pl.BlockSpec(memory_space=pltpu.VMEM)] * len(shapes),
        scratch_shapes=[pltpu.VMEM(member.shape, member.dtype) for member in operands]
        + [pltpu.SemaphoreType.DMA((len(operands),))],
        compiler_params=pltpu.CompilerParams(vmem_limit_bytes=63 * 1024 * 1024),
    )(*operands)


def norm_forward(value, gain, shift):
    centred = value - jnp.mean(value, -1, keepdims=True)
    inverse = lax.rsqrt(jnp.mean(centred * centred, -1, keepdims=True) + EPSILON)
    normed = centred * inverse
    return (normed * gain + shift, normed, inverse)


def norm_backward(grad_out, normed, inverse, gain):
    scaled = grad_out * gain
    back = inverse * (
        scaled
        - jnp.mean(scaled, -1, keepdims=True)
        - normed * jnp.mean(scaled * normed, -1, keepdims=True)
    )
    return (back, jnp.sum(grad_out * normed, 0), jnp.sum(grad_out, 0))


def mm(left, right, sides):
    return lax.dot_general(left, right, ((sides[:1], sides[1:]), ((), ())), preferred_element_type=F32)


def attend(qkv, allowed):
    by_head = qkv.reshape(qkv.shape[0], 3, HEADS, HEAD_DIM)
    query, key, value = by_head[:, 0], by_head[:, 1], by_head[:, 2]
    scores = jnp.einsum("qhe,khe->hqk", query, key, preferred_element_type=F32) * 0.125
    scores = jnp.where(allowed[None], scores, -1e30)
    highest = jnp.max(scores, -1, keepdims=True)
    raised = jnp.exp(scores - highest)
    summed = jnp.sum(raised, -1, keepdims=True)
    shares = (raised / summed).astype(BF16)
    mixture = jnp.einsum("hqk,khe->qhe", shares, value, preferred_element_type=F32)
    return mixture.astype(BF16).reshape(qkv.shape[0], D), highest + jnp.log(summed)


def attend_back(qkv, allowed, log_total, grad_mix):
    by_head = qkv.reshape(qkv.shape[0], 3, HEADS, HEAD_DIM)
    query, key, value = by_head[:, 0], by_head[:, 1], by_head[:, 2]
    grad_mix = grad_mix.reshape(qkv.shape[0], HEADS, HEAD_DIM)
    scores = jnp.einsum("qhe,khe->hqk", query, key, preferred_element_type=F32) * 0.125
    scores = jnp.where(allowed[None], scores, -1e30)
    shares = jnp.exp(scores - log_total)
    grad_share = jnp.einsum("qhe,khe->hqk", grad_mix, value, preferred_element_type=F32)
    grad_score = (shares * (grad_share - jnp.sum(shares * grad_share, -1, keepdims=True))).astype(BF16)
    grad_query = jnp.einsum("hqk,khe->qhe", grad_score, key, preferred_element_type=F32) * 0.125
    grad_key = jnp.einsum("hqk,qhe->khe", grad_score, query, preferred_element_type=F32) * 0.125
    grad_value = jnp.einsum("hqk,qhe->khe", shares.astype(BF16), grad_mix, preferred_element_type=F32)
    return jnp.stack((grad_query, grad_key, grad_value), 1).astype(BF16).reshape(qkv.shape)


def on_slice(token_arrays, lengths, weights, lane_olds, side_olds, moment):
    olds = lane_olds + side_olds + (moment,)
    found = front(token_arrays + weights, lengths)
    mask_count, gains, side, cols, keys, weight_sq = found[0:6]
    x_t, mix, a, act, y, slope, qkv_b, normed_a = found[6:14]
    normed_bc, (qkv_w, out_w, in_w, down_w, wide_w) = found[14:18], found[18:23]
    found = middle(
        (wide_w, qkv_w, out_w, in_w, down_w, y, act, a, mix, slope, qkv_b, normed_a) + tuple(normed_bc),
        (cols, keys, side, gains, mask_count),
    )
    loss_part, norm_sums = found[0:2]
    grad_logit, y_t, a_t, mix_t, act_t, ge_t, grad_ffn, grad_hidden, grad_attn, grad_qkv = found[2:]
    reduced = reduce_grads(
        (y_t, ge_t, grad_logit, x_t, grad_qkv, mix_t, grad_attn, a_t, grad_hidden, act_t, grad_ffn),
        (cols, norm_sums, loss_part, weight_sq) + olds,
    )
    found = update_weights(tuple(reduced) + weights + olds)
    grads = (None,) + tuple(found[24:28])
    mask_count = mask_count.reshape(())
    loss_sum, table_g, place_g, norm_g = found[0:4]
    lane_news = found[4:10]
    side_news = found[10:16]
    moment_new, norm_new = found[16], found[23]
    news = found[17:23]
    return (
        loss_sum.reshape(()),
        mask_count,
        table_g.T,
        place_g.T,
        grads[1],
        grads[2],
        grads[3],
        grads[4],
        norm_g.T,
        lane_news[0],
        side_news[0],
        lane_news[1],
        side_news[1],
        side_news[2],
        lane_news[2],
        side_news[3],
        lane_news[3],
        side_news[4],
        lane_news[4],
        side_news[5],
        lane_news[5],
        moment_new.T,
        news[0].T,
        news[1].T,
        news[2],
        news[3],
        news[4],
        news[5],
        norm_new.T,
    )


def on_device(
    whole_mesh,
    long_ids,
    long_targets,
    long_mask,
    long_lengths,
    short_ids,
    short_targets,
    short_mask,
    short_lengths,
    table,
    position,
    qkv_weight,
    out_weight,
    in_weight,
    down_weight,
    norms,
    table_rows,
    table_cols,
    position_rows,
    position_cols,
    qkv_rows,
    qkv_cols,
    out_rows,
    out_cols,
    in_rows,
    in_cols,
    down_rows,
    down_cols,
    norm_moment,
):
    if whole_mesh == (8, 4):
        return on_slice(
            (long_ids, long_targets, long_mask, short_ids, short_targets, short_mask),
            (long_lengths, short_lengths),
            (table.T, position.T, qkv_weight, out_weight, in_weight, down_weight, norms.T),
            (table_rows, position_rows, qkv_cols, out_cols, in_cols, down_cols),
            (table_cols, position_cols, qkv_rows, out_rows, in_rows, down_rows),
            norm_moment.T,
        )
    devices = lax.axis_size(("dp", "seq"))
    seq_index = lax.axis_index("seq")
    held = norms.shape[0]

    span = long_ids.shape[1]
    long_place = seq_index * span + lax.iota(jnp.int32, span)
    long_keep = (long_place[None, :] < long_lengths[:, None]).astype(jnp.int32)
    short_keep = (lax.iota(jnp.int32, SPAN)[None, :] < short_lengths[:, None]).astype(jnp.int32)
    long_pack = jnp.stack((long_ids, long_targets, long_mask * long_keep, long_keep), 1)
    short_pack = jnp.stack((short_ids, short_targets, short_mask * short_keep, short_keep), 1)
    moved = lax.all_to_all(
        jnp.concatenate((long_pack, short_pack[1:]), 0), "seq", split_axis=0, concat_axis=0, tiled=True
    )
    tokens = jnp.concatenate((moved, short_pack[:1]), 0)
    ids, targets, weight, keep = (tokens[:, i].reshape(-1) for i in range(4))
    weight = weight.astype(F32)
    count = tokens.shape[0] * span
    last = count - span
    alone = seq_index == lax.axis_size("seq") - 1
    token = lax.iota(jnp.int32, count)
    place = jnp.where(alone | (token >= last), token % span, token)
    row = jnp.where(alone | (token >= last), token // span, 0)
    allowed_long = (row[:last, None] == row[None, :last]) & (keep[None, :last] > 0)
    allowed_short = jnp.broadcast_to(keep[None, last:] > 0, (span, span))

    here_count = jnp.sum(long_pack[:, 2]) + jnp.sum(short_pack[:, 2])
    tall = table.T
    counts = jnp.broadcast_to(jnp.stack((here_count // 256, here_count % 256)).astype(F32)[None], (held, 2))
    wide_shard = jnp.concatenate(
        (tall, norms, counts, jnp.zeros((held, PLACE_AT - COUNT_AT - 2), F32), position.T), 1
    )
    shards = (wide_shard, qkv_weight, out_weight, in_weight, down_weight)
    wide_w, qkv_w, out_w, in_w, down_w = (
        lax.all_gather(shard.astype(BF16), ("dp", "seq"), axis=0, tiled=True) for shard in shards
    )
    column = lax.broadcasted_iota(jnp.int32, (1, WIDE), 1)
    chosen = ((ids[:, None] == column) | ((place[:, None] + PLACE_AT) == column)).astype(BF16)
    gains = wide_w[:, NORM_AT : NORM_AT + 6].astype(F32)
    sums = jnp.sum(wide_w[:, COUNT_AT : COUNT_AT + 2].astype(F32), 0)
    mask_count = (sums[0] * 256.0 + sums[1]) / held
    inverse_count = 1.0 / mask_count

    embedded = mm(chosen, wide_w, (1, 1))
    first, normed_a, inverse_a = norm_forward(embedded, gains[:, 0], gains[:, 1])
    first_b = first.astype(BF16)
    qkv_b = mm(first_b, qkv_w, (1, 0)).astype(BF16)
    mix_long, total_long = attend(qkv_b[:last], allowed_long)
    mix_short, total_short = attend(qkv_b[last:], allowed_short)
    mixture = jnp.concatenate((mix_long, mix_short), 0)
    second, normed_b, inverse_b = norm_forward(first + mm(mixture, out_w, (1, 0)), gains[:, 2], gains[:, 3])
    second_b = second.astype(BF16)
    hidden = mm(second_b, in_w, (1, 0))
    active, slope = gelu_pair(hidden)
    active_b = active.astype(BF16)
    third, normed_c, inverse_c = norm_forward(second + mm(active_b, down_w, (1, 0)), gains[:, 4], gains[:, 5])
    third_b = third.astype(BF16)
    logits = jnp.where(column < VOCAB, mm(third_b, wide_w, (1, 0)), -1e30)
    highest = jnp.max(logits, -1, keepdims=True)
    log_sum = highest + jnp.log(jnp.sum(jnp.exp(logits - highest), -1, keepdims=True))
    onehot = targets[:, None] == column
    picked = jnp.sum(jnp.where(onehot, logits, 0.0), -1)
    loss_part = jnp.sum(weight * (log_sum[:, 0] - picked))
    grad_logit = (
        (jnp.exp(logits - log_sum) - onehot.astype(F32)) * (weight * inverse_count)[:, None]
    ).astype(BF16)
    grad_third = mm(grad_logit, wide_w, (1, 1))
    grad_second, gain_c, shift_c = norm_backward(grad_third, normed_c, inverse_c, gains[:, 4])
    grad_ffn = grad_second.astype(BF16)
    down_grad = mm(active_b, grad_ffn, (0, 0)).astype(BF16)
    grad_hidden = (mm(grad_ffn, down_w, (1, 1)) * slope).astype(BF16)
    in_grad = mm(second_b, grad_hidden, (0, 0)).astype(BF16)
    grad_second = grad_second + mm(grad_hidden, in_w, (1, 1))
    grad_first, gain_b, shift_b = norm_backward(grad_second, normed_b, inverse_b, gains[:, 2])
    grad_attn = grad_first.astype(BF16)
    out_grad = mm(mixture, grad_attn, (0, 0)).astype(BF16)
    grad_mix = mm(grad_attn, out_w, (1, 1)).astype(BF16)
    grad_qkv = jnp.concatenate(
        (
            attend_back(qkv_b[:last], allowed_long, total_long, grad_mix[:last]),
            attend_back(qkv_b[last:], allowed_short, total_short, grad_mix[last:]),
        ),
        0,
    )
    qkv_grad = mm(first_b, grad_qkv, (0, 0)).astype(BF16)
    grad_first = grad_first + mm(grad_qkv, qkv_w, (1, 1))
    grad_embed, gain_a, shift_a = norm_backward(grad_first, normed_a, inverse_a, gains[:, 0])
    wide_grad = mm(
        jnp.concatenate((third_b, grad_embed.astype(BF16)), 0),
        jnp.concatenate((grad_logit, chosen), 0),
        (0, 0),
    )
    norm_part = jnp.stack((gain_a, shift_a, gain_b, shift_b, gain_c, shift_c), 1)
    wide_grad = lax.dynamic_update_slice(wide_grad.astype(BF16), norm_part.astype(BF16), (0, NORM_AT))
    grads = (wide_grad, qkv_grad, out_grad, in_grad, down_grad)
    wide_g, qkv_g, out_g, in_g, down_g = (
        lax.psum_scatter(grad.astype(F32), ("dp", "seq"), scatter_dimension=0, tiled=True) for grad in grads
    )
    table_g, place_g = wide_g[:, :VOCAB], wide_g[:, PLACE_AT:]
    norm_g = wide_g[:, NORM_AT : NORM_AT + 6]

    decay = 1.0 - STEP ** (-0.8)
    matrices = (
        (qkv_weight, qkv_g, qkv_rows, qkv_cols),
        (out_weight, out_g, out_rows, out_cols),
        (in_weight, in_g, in_rows, in_cols),
        (down_weight, down_g, down_rows, down_cols),
    )
    wide = (
        (tall, table_g, table_cols, table_rows),
        (position.T, place_g, position_cols, position_rows),
    )
    row_news = [
        decay * member[2] + (1.0 - decay) * jnp.mean(member[1] * member[1] + SQUARE_FLOOR, 1)
        for member in matrices + wide
    ]
    col_parts = [jnp.sum(member[1] * member[1] + SQUARE_FLOOR, 0) for member in matrices + wide]
    row_totals = jnp.stack([jnp.sum(rows_new) for rows_new in row_news])
    weight_sq = jnp.stack([jnp.sum(member[0] * member[0]) for member in matrices + wide])
    stats = lax.psum(
        col_parts + [row_totals, weight_sq, jnp.sum(norms * norms, 0), loss_part.reshape(1)], ("dp", "seq")
    )
    updates = []
    cols_out = []
    for index, member in enumerate(matrices + wide):
        full_rows = member[0].shape[0] * devices
        cols_new = decay * member[3] + (1.0 - decay) * stats[index] / full_rows
        if index < 4:
            mean = stats[6][index] / full_rows
        else:
            mean = jnp.mean(cols_new)
        updates.append(member[1] * lax.rsqrt(row_news[index][:, None] * cols_new[None, :] / mean))
        cols_out.append(cols_new)
    moment_new = decay * norm_moment + (1.0 - decay) * (norm_g * norm_g + SQUARE_FLOOR)
    norm_update = norm_g * lax.rsqrt(moment_new)
    update_sq = jnp.stack([jnp.sum(update * update) for update in updates])
    totals = lax.psum((update_sq, jnp.sum(norm_update * norm_update, 0)), ("dp", "seq"))
    news = []
    for index, member in enumerate(matrices + wide):
        entries = member[0].shape[0] * member[0].shape[1] * devices
        clip = jnp.maximum(1.0, jnp.sqrt(totals[0][index] / entries))
        news.append(
            member[0] - learn_rate * jnp.sqrt(stats[7][index] / entries) * updates[index] / clip
        )
    norm_rows = norms.shape[0] * devices
    norm_clip = jnp.maximum(1.0, jnp.sqrt(totals[1] / norm_rows))
    norm_new = norms - learn_rate * jnp.sqrt(stats[8] / norm_rows) * norm_update / norm_clip
    return (
        stats[9][0],
        mask_count,
        table_g.T,
        place_g.T,
        qkv_g,
        out_g,
        in_g,
        down_g,
        norm_g,
        cols_out[4],
        row_news[4],
        cols_out[5],
        row_news[5],
        row_news[0],
        cols_out[0],
        row_news[1],
        cols_out[1],
        row_news[2],
        cols_out[2],
        row_news[3],
        cols_out[3],
        moment_new,
        news[4].T,
        news[5].T,
        news[0],
        news[1],
        news[2],
        news[3],
        norm_new,
    )


def solution(mesh):
    split, wide = P(("dp", "seq"), None), P(None, ("dp", "seq"))
    shard, same = P(("dp", "seq")), P()
    return jax.shard_map(
        functools.partial(on_device, (mesh.shape["dp"], mesh.shape["seq"])),
        mesh=mesh,
        in_specs=(P("dp", "seq"),) * 3
        + (P("dp"),)
        + (split,) * 3
        + (shard,)
        + (wide,) * 2
        + (split,) * 5
        + (same, shard) * 2
        + (shard, same) * 4
        + (split,),
        out_specs=(same, same)
        + (wide,) * 2
        + (split,) * 5
        + (same, shard) * 2
        + (shard, same) * 4
        + (split,)
        + (wide,) * 2
        + (split,) * 5,
        check_vma=False,
    )
```

```python
import functools

import jax
import jax.numpy as jnp
from jax import lax
from jax.experimental import pallas as pl
from jax.experimental.pallas import tpu as pltpu
from jax.sharding import PartitionSpec as P

D = 768
HEADS = 12
HEAD_DIM = 64
VOCAB = 4101
STEP = 10
SPAN = 128

EPSILON = 1e-12
SQUARE_FLOOR = 1e-30
learn_rate = 0.3

MESH = pl.DeviceIdType.MESH
F32 = jnp.float32
BF16 = jnp.bfloat16

NORM_AT = VOCAB
COUNT_AT = VOCAB + 6
TABLE_END = 4352
PLACE_AT = 4352
WIDE = PLACE_AT + 512

SHAPES = ((24, WIDE), (24, 3 * D), (24, D), (24, 4 * D), (96, D))
E_, Q_, O_, I_, D_ = range(5)
CLASS_A, CLASS_B, CLASS_C = (E_, O_), (Q_, D_), (I_,)
UP, DOWN, XWAY, YWAY, SIDE = range(5)


def here():
    dp, seq = lax.axis_index("dp"), lax.axis_index("seq")
    return dp // 2, dp % 2, seq // 2, seq % 2


def device(z, y, x, c):
    return {"dp": z * 2 + y, "seq": x * 2 + c}


def chip(z, y, x):
    return z * 4 + y * 2 + x


def near_first(z, s):
    inner = (z * (3 - z)) // 2
    found = s + inner * (1, 1, -2, 0)[s]
    return found + (z // 2) * (3 - 2 * found)


def all_peers():
    z, y, x, c = here()
    return (
        device(z + 1, y, x, c),
        device(z - 1, y, x, c),
        device(z, y, 1 - x, c),
        device(z, 1 - y, x, c),
        device(z, y, x, 1 - c),
    )


SUM_AT = (0, WIDE, WIDE + 3 * D, WIDE + 4 * D, WIDE + 8 * D, WIDE + 9 * D)
SUMS = WIDE + 9 * D + 256
HALF_AT = tuple(start // 2 for start in SUM_AT)
HALF_SUMS = HALF_AT[5]


def lanes_of(members):
    lane = lax.broadcasted_iota(jnp.int32, (1, 128), 1)
    row = jnp.zeros((1, 128), F32)
    for index, member in enumerate(members):
        row = jnp.where(lane == index, member, row)
    return row


def lane_at(row, index):
    lane = lax.broadcasted_iota(jnp.int32, row.shape, 1)
    return jnp.sum(jnp.where(lane == index, row, 0.0), 1, keepdims=True)


def column_of(row):
    size = row.shape[1]
    diagonal = lax.broadcasted_iota(jnp.int32, (size, size), 0) == lax.broadcasted_iota(
        jnp.int32, (size, size), 1
    )
    return jnp.sum(jnp.where(diagonal, row, 0.0), 1, keepdims=True)


def row_of(column):
    size = column.shape[0]
    diagonal = lax.broadcasted_iota(jnp.int32, (size, size), 0) == lax.broadcasted_iota(
        jnp.int32, (size, size), 1
    )
    return jnp.sum(jnp.where(diagonal, column, 0.0), 0, keepdims=True)


def as_row(ref):
    return ref[...].reshape(1, ref.shape[0])


def total_sum(array):
    return jnp.sum(jnp.sum(array, 1, keepdims=True), 0, keepdims=True)


def gelu_pair(hidden):
    normal_cdf = 0.5 * (1.0 + lax.erf(hidden * 0.7071067811865476))
    return (
        hidden * normal_cdf,
        normal_cdf + hidden * jnp.exp(-0.5 * hidden * hidden) * 0.3989422804014327,
    )


def dot_nn(left, right):
    return jnp.dot(left, right, preferred_element_type=F32)


def dot_nt(left, right):
    return lax.dot_general(left, right, (((1,), (1,)), ((), ())), preferred_element_type=F32)


def dot_tn(left, right):
    return lax.dot_general(left, right, (((0,), (0,)), ((), ())), preferred_element_type=F32)


def at(index, size):
    if isinstance(index, int):
        return pl.ds(index * size, size)
    return pl.ds(pl.multiple_of(index * size, size), size)


def each(count, body):
    def step(index, carry):
        body(index)
        return carry

    lax.fori_loop(0, count, step, 0)


def each_unrolled(count, body):
    for index in range(count):
        body(index)


ROWS = 128
TILE = 256
HALF = 320
TABLE_TILES = TABLE_END // TILE


def head_lanes(first):
    lane = lax.broadcasted_iota(jnp.int32, (1, 128), 1)
    return (lane < HEAD_DIM) if first else (lane >= HEAD_DIM)


def layer_norm(value, gain, shift):
    centred = value - jnp.sum(value, 1, keepdims=True) / D
    inverse = lax.rsqrt(jnp.sum(centred * centred, 1, keepdims=True) / D + EPSILON)
    normed = centred * inverse
    return normed * gain + shift, normed, inverse


def layer_norm_back(grad, normed, inverse, gain):
    scaled = grad * gain
    return inverse * (
        scaled - jnp.sum(scaled, 1, keepdims=True) / D - normed * (jnp.sum(scaled * normed, 1, keepdims=True) / D)
    )


def put_lane(ref, rows, index, value):
    lane = lax.broadcasted_iota(jnp.int32, (1, 128), 1)
    ref[rows, :] = jnp.where(lane == index, value, ref[rows, :])


def set_bias(bias, cols, keys, last):
    same = cols[0:last, 4:5] == keys[1:2, 0:last]
    bias[...] = jnp.where(same & (keys[0:1, 0:last] > 0), 0.0, -1e30)


CHOOSE, EMBED, NORM_A, PROJECT, TURN_X, ATTEND, OUT, NORM_B, FEED_IN, TURN_A, FEED_OUT, REST = range(12)
FRONT = (
    100, 64, 65, 99, 161, 4, 0, 3, 69, 67, 160, 36, 102, 1, 35, 8, 101, 70, 165, 32,
    5, 33, 80, 68, 37, 71, 166, 6, 7, 40, 74, 75, 105, 38, 103, 12, 96, 163, 39, 176,
    72, 44, 106, 128, 97, 76, 170, 110, 45, 41, 13, 1000, 82, 18, 81, 83, 78, 73, 129, 50,
    16, 9, 42, 43, 109, 114, 47, 10, 77, 167, 11, 48, 168, 49, 132, 46, 14, 1001, 169, 177,
    164, 79, 51, 171, 131, 133, 104, 174, 107, 134, 1016, 15, 1017, 1018, 108, 140, 1019, 17, 1020, 1021,
    19, 1032, 178, 111, 1048, 1049, 1050, 135, 1051, 1052, 1053, 1054, 1055, 1056, 179, 1064, 144, 1080, 136, 142,
    1081, 113, 1082, 173, 1083, 137, 112, 172, 1084, 138, 175, 1085, 115, 1096, 1097, 1098, 146, 141, 1112, 139,
    1128, 1129, 1130, 1131, 145, 143, 1132, 1133, 1134, 1135, 1136, 147, 1137, 1138, 1139, 1160, 1161, 1162, 1176,
)


def front_hooks():
    hooks, before = {}, []
    for task in FRONT:
        if task < 1000:
            before.append(task)
        else:
            hooks[((task - 1000) // 16, (task - 1000) % 16)] = before
            before = []
    return hooks


def front_kernel(*refs):
    raw, (long_len, short_len) = refs[0:13], refs[13:15]
    count_out, gains_out, side, cols, keys, squares = refs[15:21]
    x_t, mix_out, a_out, act_out, y_out, slope_out, qkv_out, na_out = refs[21:29]
    nb_outs, nc_outs, weight_outs = refs[29:31], refs[31:33], refs[33:38]
    wide, qkv_w, out_w, in_w, down_w = weights = refs[38:43]
    value, na, low_a, low_y, mix, qkv, act, slope, pick, pick_two, bias, turned = refs[43:55]
    nb, nc = refs[55:57], (mix, low_y)
    held, wide_shard, merge, pieces, land = refs[57:70], refs[70], refs[71:76], refs[76], refs[77]
    raw_sem, swap_send, swap_recv, token_send, token_recv, send_sem, link_recv, side_recv = refs[78:86]
    out_sem, turn_sem = refs[86:88]
    z, y, x, c = here()
    peers = all_peers()
    me = chip(z, y, x)
    seq = x * 2 + c
    alone = seq // 3
    tokens = value.shape[0]
    last = tokens - SPAN
    hooks = front_hooks()

    barrier = pltpu.get_barrier_semaphore()
    cross = device(z, y, 1 - x, 1 - c)
    column = [device((z + 1 + i) % 4, y, x, c) for i in range(3)]
    for peer in [peers[XWAY], peers[YWAY], peers[SIDE], cross] + column:
        pl.semaphore_signal(barrier, inc=1, device_id=peer, device_id_type=MESH)
    raws = [pltpu.make_async_copy(raw[i], held[i], raw_sem.at[i]) for i in range(13)]
    for member in raws:
        member.start()
    for member in raws:
        member.wait()
    long_ids, long_targets, long_mask, short_ids, short_targets, short_mask, tall, place, qkv_s, out_s, in_s, down_s, norms = held

    pieces[...] = jnp.zeros(pieces.shape, jnp.int32)
    land[4] = jnp.zeros((8, SPAN), jnp.int32)
    lane = lax.broadcasted_iota(jnp.int32, (1, SPAN), 1)
    count = jnp.zeros((1, SPAN), jnp.int32)
    for t in range(5):
        if t < 3:
            ids, targets, mask = long_ids[t : t + 1, :], long_targets[t : t + 1, :], long_mask[t : t + 1, :]
            keep = (lane + seq * SPAN < long_len[t]).astype(jnp.int32)
        else:
            row = (1, 0)[t - 3]
            ids, targets, mask = (member[row : row + 1, :] for member in (short_ids, short_targets, short_mask))
            keep = (lane < short_len[row]).astype(jnp.int32)
        target = pieces.at[t] if t < 4 else land.at[4]
        target[0:1, :] = ids
        target[2:3, :] = targets
        target[3:4, :] = mask * keep
        target[5:6, :] = keep
        count = count + mask * keep
    count = jnp.sum(count.astype(F32), 1, keepdims=True)
    high = jnp.floor(count * (1.0 / 256.0))

    wide_shard[:, 0:4096] = tall[:, 0:4096]
    edge = jnp.zeros((24, 128), F32)
    tile_lane = lax.broadcasted_iota(jnp.int32, (24, 128), 1)
    tall_edge = tall[:, 4096:VOCAB]
    members = [lane_at(tall_edge, i) for i in range(VOCAB - 4096)]
    members += [column_of(norms[i : i + 1, :]) for i in range(6)]
    members += [high, count - high * 256.0]
    for i, member in enumerate(members):
        edge = jnp.where(tile_lane == i, member, edge)
    wide_shard[:, 4096:4224] = edge
    wide_shard[:, 4224:PLACE_AT] = jnp.zeros((24, PLACE_AT - 4224), F32)
    wide_shard[:, PLACE_AT:] = place[...]
    shards = (wide_shard, qkv_s, out_s, in_s, down_s)

    pl.semaphore_wait(barrier, 7)
    swaps = []
    for m in (E_, Q_, I_, D_, O_):
        size, half = SHAPES[m][0], SHAPES[m][1] // 2
        swaps.append(
            pltpu.make_async_remote_copy(
                src_ref=shards[m].at[:, pl.ds(pl.multiple_of((1 - c) * half, 128), half)],
                dst_ref=merge[m].at[pl.ds(pl.multiple_of(c * size, 8), size), :],
                send_sem=swap_send.at[m],
                recv_sem=swap_recv.at[m],
                device_id=peers[SIDE],
                device_id_type=MESH,
            )
        )
        swaps[-1].start()
    token_copies = []
    for i, (to_x, to_c) in enumerate(((x, 1 - c), (1 - x, c), (1 - x, 1 - c))):
        token_copies.append(
            pltpu.make_async_remote_copy(
                src_ref=pieces.at[to_x * 2 + to_c],
                dst_ref=land.at[seq],
                send_sem=token_send.at[i],
                recv_sem=token_recv.at[i],
                device_id=device(z, y, to_x, to_c),
                device_id_type=MESH,
            )
        )
        token_copies[-1].start()
    land[seq] = pieces[seq]

    def part(piece, k, half):
        m, skip, wide_part = PIECES[piece]
        size = 2 * SHAPES[m][0]
        start = pl.multiple_of(half * (SHAPES[m][1] // 2) + skip, 128)
        return weights[m].at[pl.ds(pl.multiple_of(k * size, size), size), pl.ds(start, wide_part)]

    FIRST_WAY, SECOND_WAY, SIDE_WAY, UP_WAY, DOWN_WAY = range(5)

    def copy_of(piece, k, way):
        ways = (XWAY, YWAY) if GATHER_WAY[piece] == 0 else (YWAY, XWAY)
        return pltpu.make_async_remote_copy(
            src_ref=part(piece, k, c),
            dst_ref=part(piece, k, c),
            send_sem=send_sem.at[piece, k, way],
            recv_sem=(side_recv if way == SIDE_WAY else link_recv).at[piece, k],
            device_id=peers[(ways + (SIDE, UP, DOWN))[way]],
            device_id_type=MESH,
        )

    def block_of(number):
        piece, task = number // 32, number % 32
        way = GATHER_WAY[piece]
        up, down = (UP_WAY, z < 3), (DOWN_WAY, z > 0)
        first, second, across = (FIRST_WAY, None), (SECOND_WAY, None), (SIDE_WAY, None)

        def of(last, earlier, t):
            to_y, to_x = (last, earlier) if way == 0 else (earlier, last)
            return chip(t, 1 - y if to_y else y, 1 - x if to_x else x)

        def onward(t):
            return (UP_WAY, (t < z) & (z < 3)), (DOWN_WAY, (t > z) & (z > 0))

        if task < 5:
            return piece, me, (up, down, None, first, second)[task : task + 1], False
        if way < 2:
            if task < 8:
                t = near_first(z, task - 4)
                return piece, of(0, 0, t), onward(t) + (first, second, across), True
            if task < 12:
                return piece, of(0, 1, near_first(z, task - 8)), (second, across), True
            return piece, of(1, (task - 12) % 2, near_first(z, (task - 12) // 2)), (across,), True
        if task == 5:
            return piece, of(0, 1, z), (second, up, down, across), True
        if task < 8:
            return piece, of(1, task - 6, z), (up, down, across), True
        t, place_of = near_first(z, 1 + (task - 8) // 4), (task - 8) % 4
        return piece, of(place_of // 2, place_of % 2, t), onward(t) + (across,), True

    def for_each_way(number, act):
        piece, k, ways, _ = block_of(number)
        for way, only in ways:
            if only is None:
                act(copy_of(piece, k, way))
            else:

                @pl.when(only)
                def _(way=way):
                    act(copy_of(piece, k, way))

    def transfer(number):
        piece, k, _, waits = block_of(number)
        if waits:
            copy_of(piece, k, FIRST_WAY).wait_recv()
        for_each_way(number, lambda copy: copy.start())

    def before(step, index, base=0):
        for (name, part_index), tasks in hooks.items():
            part_index = part_index - base
            if name != step or not tasks or (step == EMBED and not 0 <= part_index < 3):
                continue
            if index is None or isinstance(index, int):
                if part_index == (index or 0):
                    for number in tasks:
                        transfer(number)
            else:

                @pl.when(index == part_index)
                def _(tasks=tasks):
                    for number in tasks:
                        transfer(number)

    def need(*wanted):
        for piece in wanted:
            for k in range(16):
                pltpu.make_async_remote_copy(
                    src_ref=part(piece, k, 1 - c),
                    dst_ref=part(piece, k, 1 - c),
                    send_sem=send_sem.at[piece, k, SIDE_WAY],
                    recv_sem=side_recv.at[piece, k],
                    device_id=peers[SIDE],
                    device_id_type=MESH,
                ).wait_recv()

    for number, m in enumerate((E_, Q_, I_, D_, O_)):
        swaps[number].wait_recv()
        size, half = SHAPES[m][0], SHAPES[m][1] // 2
        merge[m][pl.ds(pl.multiple_of(c * size, 8), size), :] = shards[m][:, pl.ds(pl.multiple_of(c * half, 128), half)]
        rows = pl.ds(pl.multiple_of(me * 2 * size, 2 * size), 2 * size)
        weights[m][rows, pl.ds(pl.multiple_of(c * half, 128), half)] = merge[m][...].astype(BF16)
        for piece in range(6):
            if PIECES[piece][0] == m:
                copy_of(piece, me, SIDE_WAY).start()
    for copy in token_copies:
        copy.wait_recv()
    side[...] = jnp.zeros(side.shape, F32)
    keys[...] = jnp.zeros(keys.shape, jnp.int32)
    zeros = jnp.zeros((1, SPAN), F32)
    for b in range(5):
        tile = land[b]
        shift = b * SPAN * (1 - alone) if b < 4 else 0
        row = b * alone if b < 4 else 4
        spot = (lane + shift + PLACE_AT).astype(F32)
        row_lane = (lane * 0 + row).astype(F32)
        ids, targets, weight = (tile[i : i + 1].astype(F32) for i in (0, 2, 3))
        stacked = jnp.concatenate((ids, spot, targets, weight, row_lane, tile[5:6].astype(F32), zeros, zeros), 0)
        stacked = jnp.concatenate((stacked, jnp.zeros((120, SPAN), F32)), 0)
        cols[b * SPAN : (b + 1) * SPAN, :] = stacked.T.astype(jnp.int32)
        keys[0:1, b * SPAN : (b + 1) * SPAN] = tile[5:6]
        keys[1:2, b * SPAN : (b + 1) * SPAN] = lane * 0 + row
        keys[2:4, b * SPAN : (b + 1) * SPAN] = tile[2:4]
    set_bias(bias, cols, keys, last)
    found = [total_sum(member[...] * member[...]) for member in (tall, place, qkv_s, out_s, in_s, down_s)]
    norm_squares = jnp.sum(norms[...] * norms[...], 1, keepdims=True)
    squares[...] = lanes_of(found + [norm_squares[i : i + 1] for i in range(6)])

    turns, outs, out_count = {}, {}, [0]

    def turn_out(source, target, slot):
        if slot in turns:
            turns[slot].wait()

        def some(index):
            turned[slot, :, at(index, ROWS)] = source[at(index, ROWS), :].T

        each_unrolled(tokens // ROWS, some)
        turns[slot] = pltpu.make_async_copy(turned.at[slot], target, turn_sem.at[slot])
        turns[slot].start()

    def put_out(name, source, target):
        outs[name] = pltpu.make_async_copy(source, target, out_sem.at[out_count[0]])
        out_count[0] += 1
        outs[name].start()

    picks = (pick, pick_two)
    halves = [pl.ds(half * HALF, HALF) for half in range(2)]
    for half in range(2):

        def choose(index):
            column_lane = lax.broadcasted_iota(jnp.int32, (1, TILE), 1) + index * TILE
            hit = (cols[halves[half], 0:1] == column_lane) | (cols[halves[half], 1:2] == column_lane)
            picks[half][:, at(index, TILE)] = jnp.where(hit, 1.0, 0.0).astype(BF16)

        before(CHOOSE, half)
        each_unrolled(WIDE // TILE, choose)

    before(EMBED, 0)
    hooks.pop((EMBED, 0))
    need(1, 2)
    put_out("wide", wide, weight_outs[4])
    for half in range(2):

        def embed(index):
            before(EMBED, index, half * 3)
            value[halves[half], at(index, TILE)] = dot_nt(picks[half][...], wide[at(index, TILE), :])

        each_unrolled(D // TILE, embed)

    gains = wide[:, 4096:4224].astype(F32).T
    gains_out[...] = gains[0:16]
    counts = jnp.sum(gains[11:13], 1, keepdims=True) / 24.0
    mask_count = counts[0:1] * 256.0 + counts[1:2]
    count_out[...] = mask_count
    norm_rows = [gains_out[5 + i : 6 + i, :] for i in range(6)]
    before(NORM_A, None)

    def norm_a(index):
        rows = at(index, ROWS)
        found, normed, inverse = layer_norm(value[rows, :], norm_rows[0], norm_rows[1])
        value[rows, :] = found
        low_a[rows, :] = found.astype(BF16)
        na[rows, :] = normed
        put_lane(side, rows, 12, inverse)

    each_unrolled(tokens // ROWS, norm_a)
    put_out("na", na, na_out)
    before(PROJECT, 0)
    need(0)

    def project(index):
        before(PROJECT, index)
        qkv[:, at(index, TILE)] = dot_nn(low_a[...], qkv_w[:, at(index, TILE)]).astype(BF16)

    hooks.pop((PROJECT, 0))
    each_unrolled(3 * D // TILE, project)
    put_out("qkv", qkv, qkv_out)
    put_out("qkv_w", qkv_w, weight_outs[0])
    before(TURN_X, None)
    turn_out(low_a, x_t, 0)

    def attend_pair(pair):
        before(ATTEND, pair)
        for start, size in ((0, last), (last, SPAN)):
            rows = pl.ds(start, size)
            query = qkv[rows, at(pair, 128)]
            key = qkv[rows, pl.ds(D + pair * 128, 128)]
            val = qkv[rows, pl.ds(2 * D + pair * 128, 128)]
            mask = bias[...] if start == 0 else jnp.where(keys[0:1, last:tokens] > 0, 0.0, -1e30)
            mixed = []
            for first in (True, False):
                chosen = jnp.where(head_lanes(first), query, jnp.zeros_like(query))
                scores = dot_nt(chosen, key) * 0.125 + mask
                highest = jnp.max(scores, 1, keepdims=True)
                raised = jnp.exp(scores - highest)
                summed = jnp.sum(raised, 1, keepdims=True)
                shares = (raised * (1.0 / summed)).astype(BF16)
                mixed.append(dot_nn(shares, val))
                put_lane(side, rows, 2 * pair + (0 if first else 1), highest + jnp.log(summed))
            mix[rows, at(pair, 128)] = jnp.where(head_lanes(True), mixed[0], mixed[1]).astype(BF16)

    each_unrolled(HEADS // 2, attend_pair)
    before(OUT, 0)
    hooks.pop((OUT, 0))
    need(5)

    def out_project(index):
        before(OUT, index)
        value[:, at(index, TILE)] = value[:, at(index, TILE)] + dot_nn(mix[...], out_w[:, at(index, TILE)])

    each_unrolled(D // TILE, out_project)
    put_out("out_w", out_w, weight_outs[1])
    put_out("mix", mix, mix_out)
    before(NORM_B, None)

    def norm_b(index):
        rows = at(index, ROWS)
        found, normed, inverse = layer_norm(value[rows, :], norm_rows[2], norm_rows[3])
        value[rows, :] = found
        low_y[rows, :] = found.astype(BF16)
        nb[0][rows, :], nb[1][rows, :] = split_two(normed)
        put_lane(side, rows, 13, inverse)

    each_unrolled(tokens // ROWS, norm_b)
    put_out("a", low_y, a_out)
    put_out("nb0", nb[0], nb_outs[0])
    put_out("nb1", nb[1], nb_outs[1])
    before(FEED_IN, 0)
    hooks.pop((FEED_IN, 0))
    need(3)

    def feed_in(index):
        before(FEED_IN, index)
        hidden = dot_nn(low_y[...], in_w[:, at(index, TILE)])
        active, slant = gelu_pair(hidden)
        active = active.astype(BF16)
        act[:, at(index, TILE)] = active
        slope[:, at(index, TILE)] = slant.astype(BF16)

    each_unrolled(4 * D // TILE, feed_in)
    put_out("act", act, act_out)
    put_out("slope", slope, slope_out)
    put_out("in_w", in_w, weight_outs[2])
    before(TURN_A, None)
    before(FEED_OUT, 0)
    hooks.pop((FEED_OUT, 0))
    need(4)

    def feed_out(index):
        before(FEED_OUT, index)
        value[:, at(index, TILE)] = value[:, at(index, TILE)] + dot_nn(act[...], down_w[:, at(index, TILE)])

    each_unrolled(D // TILE, feed_out)
    put_out("down_w", down_w, weight_outs[3])
    before(REST, None)
    turns[0].wait()
    outs.pop("mix").wait()
    outs.pop("a").wait()

    def norm_c(index):
        rows = at(index, ROWS)
        found, normed, inverse = layer_norm(value[rows, :], norm_rows[4], norm_rows[5])
        low_a[rows, :] = found.astype(BF16)
        nc[0][rows, :], nc[1][rows, :] = split_two(normed)
        put_lane(side, rows, 14, inverse)

    each_unrolled(tokens // ROWS, norm_c)
    put_out("y", low_a, y_out)
    put_out("nc0", nc[0], nc_outs[0])
    put_out("nc1", nc[1], nc_outs[1])
    for swap in swaps:
        swap.wait_send()
    for copy in token_copies:
        copy.wait_send()
    for piece in range(6):
        copy_of(piece, me, SIDE_WAY).wait_send()
    for number in FRONT:
        if number < 1000:
            for_each_way(number, lambda copy: copy.wait_send())
    for copy in outs.values():
        copy.wait()


def front(large, lengths):
    vmem, hbm = pl.BlockSpec(memory_space=pltpu.VMEM), pl.BlockSpec(memory_space=pl.ANY)
    smem = pl.BlockSpec(memory_space=pltpu.SMEM)
    shape, dma = jax.ShapeDtypeStruct, pltpu.SemaphoreType.DMA
    tokens = 5 * SPAN
    small = [shape((1, 1), F32), shape((16, D), F32), shape((tokens, 128), F32)]
    small += [shape((tokens, 128), jnp.int32), shape((8, tokens), jnp.int32), shape((1, 128), F32)]
    out = [shape((D, tokens), BF16)] + [shape((tokens, width), BF16) for width in (D, D, 4 * D, D, 4 * D, 3 * D)]
    out += [shape((tokens, D), F32)] + [shape((tokens, D), BF16)] * 4
    out += [shape((32 * SHAPES[m][0], SHAPES[m][1]), BF16) for m in (Q_, O_, I_, D_, E_)]
    return pl.pallas_call(
        front_kernel,
        out_shape=small + out,
        in_specs=[hbm] * 13 + [smem] * 2,
        out_specs=[vmem] * len(small) + [hbm] * len(out),
        scratch_shapes=[pltpu.VMEM((32 * size, wide), BF16) for size, wide in SHAPES]
        + [pltpu.VMEM((tokens, D), F32)] * 2
        + [pltpu.VMEM((tokens, D), BF16)] * 3
        + [
            pltpu.VMEM((tokens, 3 * D), BF16),
            pltpu.VMEM((tokens, 4 * D), BF16),
            pltpu.VMEM((tokens, 4 * D), BF16),
            pltpu.VMEM((HALF, WIDE), BF16),
            pltpu.VMEM((HALF, WIDE), BF16),
            pltpu.VMEM((tokens - SPAN, tokens - SPAN), F32),
            pltpu.VMEM((1, D, tokens), BF16),
        ]
        + [pltpu.VMEM((tokens, D), BF16)] * 2
        + [pltpu.VMEM(member.shape, member.dtype) for member in large]
        + [pltpu.VMEM(SHAPES[E_], F32)]
        + [pltpu.VMEM((2 * size, wide // 2), F32) for size, wide in SHAPES]
        + [pltpu.VMEM((4, 8, SPAN), jnp.int32), pltpu.VMEM((5, 8, SPAN), jnp.int32)]
        + [dma((13,)), dma((5,)), dma((5,)), dma((3,)), dma((3,)), dma((6, 16, 5)), dma((6, 16)), dma((6, 16))]
        + [dma((18,)), dma((1,))],
        compiler_params=pltpu.CompilerParams(
            collective_id=0, has_side_effects=True, vmem_limit_bytes=63 * 1024 * 1024
        ),
    )(*large, *lengths)


PACK = 256


def split_two(value):
    high = value.astype(BF16)
    return high, (value - high.astype(F32)).astype(BF16)


def middle_kernel(*refs):
    (wide_h, qkv_wh, out_wh, in_wh, down_h, y_h, act_h, a_h, mix_h, slope_h, qkv_h, na_h) = refs[0:12]
    nb_h, nc_h = refs[12:14], refs[14:16]
    cols, keys, side, gains, count = refs[16:21]
    loss_out, norm_out = refs[21:23]
    glog_out, y_t, a_t, mix_t, act_t, ge_t, gffn_out, gh_out, gattn_out, gqkv_out = refs[23:33]
    wide, qkv_w, out_w, in_w, plain, qkv = refs[33:39]
    nb = refs[39:41]
    slope_ring, act_ring, down_ring = refs[41:44]
    logits, glog, gh, gffn, gattn, packed, grad, turned, act_turned = refs[44:53]
    back_kv, gqkv, whole_grad, pick, pick_t, bias, side_pack, side_turned, dq, ge = refs[53:63]
    load_sem, ring_sem, out_sem = refs[63:66]
    nc = (gqkv.at[:, D : 2 * D], gqkv.at[:, 2 * D : 3 * D])
    gatt = packed
    tokens = cols.shape[0]
    names = ("wide", "y", "nc0", "nc1", "in_w", "nb0", "nb1", "out_w", "qkv", "qkv_w")
    sources = (wide_h, y_h, nc_h[0], nc_h[1], in_wh, nb_h[0], nb_h[1], out_wh, qkv_h, qkv_wh)
    targets = (wide, plain, nc[0], nc[1], in_w, nb[0], nb[1], out_w, qkv, qkv_w)

    def na_copy(i):
        return pltpu.make_async_copy(
            na_h.at[:, at(i, TILE)], logits.at[pl.ds(i * tokens, tokens), :], load_sem.at[10 + i]
        )

    def tile_of(index):
        return pl.ds(index * PACK, PACK)

    loads = {name: pltpu.make_async_copy(sources[i], targets[i], load_sem.at[i]) for i, name in enumerate(names)}
    for name in ("y", "wide"):
        loads[name].start()

    weight_row = keys[3:4, :].astype(F32)
    weight_col = cols[:, 3:4].astype(F32)
    earlier = lax.broadcasted_iota(jnp.int32, (tokens, tokens), 0) < lax.broadcasted_iota(jnp.int32, (tokens, tokens), 1)
    later = lax.broadcasted_iota(jnp.int32, (tokens, tokens), 0) > lax.broadcasted_iota(jnp.int32, (tokens, tokens), 1)
    rank_row = dot_nn(
        jnp.broadcast_to(weight_row, (16, tokens)).astype(BF16), jnp.where(earlier, 1.0, 0.0).astype(BF16)
    )[0:1]
    rank_col = dot_nn(
        jnp.where(later, 1.0, 0.0).astype(BF16), jnp.broadcast_to(weight_col, (tokens, 128)).astype(BF16)
    )[:, 0:1]
    rank_row = jnp.where(weight_row > 0, rank_row, -1.0)
    rank_col = jnp.where(weight_col > 0, rank_col, -1.0)
    blocks = (jnp.sum(weight_row).astype(jnp.int32) + (PACK - 1)) // PACK
    blocks = jnp.maximum(blocks, 1)
    inverse_count = 1.0 / count[...]
    norm_rows = [gains[5 + i : 6 + i, :] for i in range(6)]
    loss_out[...] = jnp.zeros((1, 1), F32)
    norm_out[...] = jnp.zeros(norm_out.shape, F32)
    back_kv[...] = jnp.zeros(back_kv.shape, F32)
    whole_grad[...] = jnp.zeros(whole_grad.shape, F32)
    gqkv[:, 0:D] = jnp.zeros((tokens, D), BF16)
    side_first = side[...].astype(BF16)
    rest = side[...] - side_first.astype(F32)
    side_second = rest.astype(BF16)
    side_third = (rest - side_second.astype(F32)).astype(BF16)
    waited = set()

    def load_plain(source):
        return pltpu.make_async_copy(source, plain, load_sem.at[1])

    def ring(kind, source, target):
        def copy(j):
            piece = source.at[at(j, TILE), :] if kind == 2 else source.at[:, at(j, TILE)]
            return pltpu.make_async_copy(piece, target.at[j % 2], ring_sem.at[kind * 2 + j % 2])

        return copy

    rings = [ring(0, slope_h, slope_ring), ring(1, act_h, act_ring), ring(2, down_h, down_ring)]
    outs = [
        (glog, glog_out, 0),
        (turned.at[0], y_t, 1),
        (turned.at[1], a_t, 1),
        (turned.at[2], mix_t, 1),
        (act_turned, act_t, 1),
        (gffn, gffn_out, 0),
        (gh, gh_out, 0),
        (gattn, gattn_out, 0),
    ]

    def out_copy(i, block):
        source, target, axis = outs[i]
        place = at(block, PACK)
        return pltpu.make_async_copy(
            source, target.at[place, :] if axis == 0 else target.at[:, place], out_sem.at[i]
        )

    def wait_load(name):
        loads[name].wait()

    wait_load("wide")
    for name in names[2:]:
        loads[name].start()

    def block_step(block, carry):
        slot_col = lax.broadcasted_iota(jnp.int32, (PACK, 1), 0).astype(F32) + (block * PACK).astype(F32)
        slot_row = lax.broadcasted_iota(jnp.int32, (1, PACK), 1).astype(F32) + (block * PACK).astype(F32)
        hit = jnp.where(rank_row == slot_col, 1.0, 0.0)
        pick[...] = hit.astype(BF16)
        hit_t = jnp.where(rank_col == slot_row, 1.0, 0.0)
        pick_t[...] = hit_t.astype(BF16)
        target = jnp.sum(hit * keys[2:3, :].astype(F32), 1, keepdims=True)
        weight = jnp.sum(hit, 1, keepdims=True)
        row_col = cols[:, 4:5].astype(F32)
        row_of_token = jnp.sum(hit_t * row_col, 0, keepdims=True)
        bias[...] = jnp.where((row_of_token == row_col) & (cols[:, 5:6] > 0), 0.0, -1e30)
        side_pack[...] = (
            dot_nn(pick[...], side_first) + dot_nn(pick[...], side_second) + dot_nn(pick[...], side_third)
        )
        side_turned[...] = side_pack[...].T
        for kind in range(3):
            for j in range(2):
                rings[kind](j).start()
        load_plain(y_h).wait()
        packed[...] = dot_nn(pick[...], plain[...]).astype(BF16)
        load_plain(a_h).start()
        turned[0] = packed[...].T
        out_copy(1, block).start()

        def lanes(index):
            return (lax.broadcasted_iota(jnp.int32, (1, TILE), 1) + index * TILE).astype(F32)

        highest = jnp.full((PACK, 128), -1e30, F32)
        for index in range(TABLE_TILES):
            found = dot_nn(packed[...], wide[:, at(index, TILE)])
            if index == TABLE_TILES - 1:
                found = jnp.where(lanes(index) < VOCAB, found, -1e30)
            logits[tile_of(index), :] = found
            highest = jnp.maximum(highest, jnp.maximum(found[:, 0:128], found[:, 128:256]))
        highest = jnp.max(highest, 1, keepdims=True)
        summed, picked = jnp.zeros((PACK, 128), F32), jnp.zeros((PACK, 128), F32)
        for index in range(TABLE_TILES):
            found = logits[tile_of(index), :]
            raised = jnp.exp(found - highest)
            logits[tile_of(index), :] = raised
            own = jnp.where(lanes(index) == target, found, 0.0)
            summed = summed + raised[:, 0:128] + raised[:, 128:256]
            picked = picked + own[:, 0:128] + own[:, 128:256]
        summed = jnp.sum(summed, 1, keepdims=True)
        picked = jnp.sum(picked, 1, keepdims=True)
        loss_out[...] = loss_out[...] + jnp.sum(weight * (highest + jnp.log(summed) - picked), 0, keepdims=True)
        scale = weight * inverse_count
        share = scale / summed
        for index in range(TABLE_TILES):
            found = logits[tile_of(index), :] * share - jnp.where(lanes(index) == target, scale, 0.0)
            glog[:, at(index, TILE)] = found.astype(BF16)
        out_copy(0, block).start()
        for index in range(D // TILE):
            grad[:, at(index, TILE)] = dot_nt(glog[...], wide[at(index, TILE), 0:TABLE_END])

        @pl.when(block == 0)
        def _():
            for name in names[2:4]:
                wait_load(name)

        normed = dot_nn(pick[...], nc[0][...]) + dot_nn(pick[...], nc[1][...])
        found = grad[...]
        back = layer_norm_back(found, normed, lane_at(side_pack[...], 14), norm_rows[4])
        norm_out[4:5, :] = norm_out[4:5, :] + jnp.sum(found * normed, 0, keepdims=True)
        norm_out[5:6, :] = norm_out[5:6, :] + jnp.sum(found, 0, keepdims=True)
        grad[...] = back
        gffn[...] = back.astype(BF16)
        out_copy(5, block).start()

        load_plain(a_h).wait()
        turned[1] = dot_nn(pick[...], plain[...]).astype(BF16).T
        out_copy(2, block).start()
        load_plain(mix_h).start()
        for index in range(4 * D // TILE):
            for kind in range(3):
                rings[kind](index).wait()
            slant = dot_nn(pick[...], slope_ring[index % 2])
            found = dot_nt(gffn[...], down_ring[index % 2]) * slant
            gh[:, at(index, TILE)] = found.astype(BF16)
            act_turned[at(index, TILE), :] = dot_nn(pick[...], act_ring[index % 2]).astype(BF16).T
            if index + 2 < 4 * D // TILE:
                for kind in range(3):
                    rings[kind](index + 2).start()
        out_copy(6, block).start()
        out_copy(4, block).start()
        load_plain(mix_h).wait()
        turned[2] = dot_nn(pick[...], plain[...]).astype(BF16).T
        out_copy(3, block).start()
        load_plain(y_h).start()

        @pl.when(block == 0)
        def _():
            for name in names[4:8]:
                wait_load(name)

        for index in range(D // TILE):
            grad[:, at(index, TILE)] = grad[:, at(index, TILE)] + dot_nt(gh[...], in_w[at(index, TILE), :])
        normed = dot_nn(pick[...], nb[0][...]) + dot_nn(pick[...], nb[1][...])
        found = grad[...]
        back = layer_norm_back(found, normed, lane_at(side_pack[...], 13), norm_rows[2])
        norm_out[2:3, :] = norm_out[2:3, :] + jnp.sum(found * normed, 0, keepdims=True)
        norm_out[3:4, :] = norm_out[3:4, :] + jnp.sum(found, 0, keepdims=True)
        gattn[...] = back.astype(BF16)
        out_copy(7, block).start()
        high, low = split_two(back)
        whole_grad[...] = whole_grad[...] + dot_nn(pick_t[...], high) + dot_nn(pick_t[...], low)
        for index in range(D // TILE):
            gatt[:, at(index, TILE)] = dot_nt(gattn[...], out_w[at(index, TILE), :]).astype(BF16)

        @pl.when(block == 0)
        def _():
            wait_load("qkv")

        def attend_pair_back(pair):
            spots = [pl.ds(i * D + pair * 128, 128) for i in range(3)]
            query = dot_nn(pick[...], qkv[:, spots[0]]).astype(BF16)
            key, val = qkv[:, spots[1]], qkv[:, spots[2]]
            given = gatt[:, at(pair, 128)]
            key_t = key.T
            found = []
            for first in (True, False):
                lanes_here = head_lanes(first)
                chosen = jnp.where(lanes_here, query, jnp.zeros_like(query))
                mine = jnp.where(lanes_here, given, jnp.zeros_like(given))
                total = side_turned[pl.ds(2 * pair + (0 if first else 1), 1), :]
                shares = jnp.exp(dot_nt(key, chosen) * 0.125 + bias[...] - total)
                grad_share = dot_nt(val, mine)
                middle = jnp.sum(shares * grad_share, 0, keepdims=True)
                grad_score = (shares * (grad_share - middle)).astype(BF16)
                found.append(
                    (
                        dot_nn(key_t, grad_score) * 0.125,
                        dot_nn(grad_score, query) * 0.125,
                        dot_nn(shares.astype(BF16), given),
                    )
                )
            lanes_here = head_lanes(True)
            both = jnp.concatenate((found[0][0][0:HEAD_DIM], found[1][0][HEAD_DIM:]), 0)
            dq[at(pair, 128), :] = both.astype(BF16)
            for i in (1, 2):
                spot = pl.ds((i - 1) * D + pair * 128, 128)
                back_kv[:, spot] = back_kv[:, spot] + jnp.where(lanes_here, found[0][i], found[1][i])

        each_unrolled(HEADS // 2, attend_pair_back)
        gqkv[:, 0:D] = (gqkv[:, 0:D].astype(F32) + dot_nt(pick_t[...], dq[...])).astype(BF16)
        for i in range(len(outs)):
            out_copy(i, block).wait()
        return carry

    lax.fori_loop(0, blocks, block_step, 0)
    load_plain(y_h).wait()
    for i in range(D // TILE):
        na_copy(i).start()
    gqkv[:, D:] = back_kv[...].astype(BF16)
    copy_qkv = pltpu.make_async_copy(gqkv, gqkv_out, out_sem.at[8])
    copy_qkv.start()
    for ref in (glog, gffn, gh, gattn):
        ref[...] = jnp.zeros(ref.shape, BF16)
    for block in range(1, 3):

        @pl.when(blocks <= block)
        def _():
            for i in range(len(outs)):
                out_copy(i, block).start()

    wait_load("qkv_w")
    for index in range(D // TILE):
        whole_grad[:, at(index, TILE)] = whole_grad[:, at(index, TILE)] + dot_nt(gqkv[...], qkv_w[at(index, TILE), :])
    for i in range(D // TILE):
        na_copy(i).wait()
    zero = jnp.zeros((1, D), F32)

    def norm_a_back(index, carry):
        gain, shift = carry
        rows = at(index, ROWS)
        inverse = lane_at(side[rows, :], 12)
        found = whole_grad[rows, :]
        normed = jnp.concatenate(
            [logits[pl.ds(i * tokens + index * ROWS, ROWS), :] for i in range(D // TILE)], 1
        )
        ge[:, rows] = layer_norm_back(found, normed, inverse, norm_rows[0]).astype(BF16).T
        return gain + jnp.sum(found * normed, 0, keepdims=True), shift + jnp.sum(found, 0, keepdims=True)

    gain, shift = zero, zero
    for index in range(tokens // ROWS):
        gain, shift = norm_a_back(index, (gain, shift))
    norm_out[0:1, :] = gain
    norm_out[1:2, :] = shift
    copy_ge = pltpu.make_async_copy(ge, ge_t, out_sem.at[9])
    copy_ge.start()
    for block in range(1, 3):

        @pl.when(blocks <= block)
        def _():
            for i in range(len(outs)):
                out_copy(i, block).wait()

    copy_qkv.wait()
    copy_ge.wait()


def middle(large, small):
    tokens = 5 * SPAN
    slots = 3 * PACK
    vmem, hbm = pl.BlockSpec(memory_space=pltpu.VMEM), pl.BlockSpec(memory_space=pl.ANY)
    shape, dma = jax.ShapeDtypeStruct, pltpu.SemaphoreType.DMA
    out = [shape((slots, TABLE_END), BF16)] + [shape((D, slots), BF16)] * 3 + [shape((4 * D, slots), BF16)]
    out += [shape((D, tokens), BF16), shape((slots, D), BF16), shape((slots, 4 * D), BF16), shape((slots, D), BF16)]
    out += [shape((tokens, 3 * D), BF16)]

    def rows(count, width, kind=BF16):
        return pltpu.VMEM((count, width), kind)

    scratch = [rows(D, WIDE), rows(D, 3 * D), rows(D, D), rows(D, 4 * D), rows(tokens, D), rows(tokens, 3 * D)]
    scratch += [rows(tokens, D)] * 2
    scratch += [pltpu.VMEM((2, tokens, TILE), BF16)] * 2 + [pltpu.VMEM((2, TILE, D), BF16)]
    scratch += [rows(PACK * TABLE_TILES, TILE, F32), rows(PACK, TABLE_END), rows(PACK, 4 * D)] + [rows(PACK, D)] * 3
    scratch += [rows(PACK, D, F32), pltpu.VMEM((3, D, PACK), BF16), rows(4 * D, PACK)]
    scratch += [rows(tokens, 2 * D, F32), rows(tokens, 3 * D), rows(tokens, D, F32), rows(PACK, tokens)]
    scratch += [rows(tokens, PACK), rows(tokens, PACK, F32), rows(PACK, 128, F32), rows(128, PACK, F32)]
    scratch += [rows(D, PACK), rows(D, tokens)]
    scratch += [dma((13,)), dma((6,)), dma((10,))]
    return pl.pallas_call(
        middle_kernel,
        out_shape=[shape((1, 1), F32), shape((6, D), F32)] + out,
        in_specs=[hbm] * 16 + [vmem] * 5,
        out_specs=[vmem] * 2 + [hbm] * len(out),
        scratch_shapes=scratch,
        compiler_params=pltpu.CompilerParams(vmem_limit_bytes=63 * 1024 * 1024),
    )(*large, *small)


LEFT = 768
PIECES = ((Q_, 0, 1152), (E_, 0, 1280), (E_, 1280, 1152), (I_, 0, 1536), (D_, 0, 384), (O_, 0, 384))
SUM_WAY = (3, 1, 1, 2, 0, 0)
GATHER_WAY = (0, 1, 0, 2, 1, 0)
TASKS = (
    129, 0, 1, 96, 7, 5, 6, 4, 97, 13, 102, 103, 11, 128, 101, 12, 9, 8,
    132, 3, 104, 105, 2, 100, 108, 64, 14, 65, 71, 15, 111, 70, 134, 160, 106, 72,
    136, 161, 68, 10, 140, 135, 107, 73, 130, 110, 109, 33, 168, 166, 76, 137, 141, 143,
    139, 69, 173, 133, 77, 32, 169, 172, 144, 38, 164, 66, 40, 75, 39, 138, 176, 131,
    44, 36, 41, 142, 98, 167, 79, 34, 37, 80, 45, 165, 145, 47, 43, 74, 162, 67,
    48, 16, 171, 78, 35, 42, 46, 174, 99, 112, 81, 170, 163, 175, 17, 49, 113, 177,
)


def reduce_kernel(*refs):
    given, (cols, norm_sums, loss, squares) = refs[0:11], refs[11:15]
    y_t, ge_t, glog, x_t, gqkv, mix_t, gattn, a_t, gh, act_t, gffn = given
    lane_olds, side_olds, moment = refs[15:21], refs[21:27], refs[27]
    outs, sums_out, totals_out = refs[28:33], refs[33], refs[34]
    own, side, first, second, column, fin = (refs[35 + 6 * i : 41 + 6 * i] for i in range(6))
    left, (glog_v, gqkv_v, gattn_v, gh_v, gffn_v), stage, tails, norm_t = refs[71:78], refs[78:83], refs[83], refs[84], refs[85]
    lane_plane, lane_z, lane_halves = refs[86:89]
    scalar_sums, total_sums = refs[89:91], refs[91:93]
    load_sem, ring_sem, tail_sem, side_recv, first_send, first_recv, second_send, second_recv = refs[93:101]
    z_send, z_recv, swap_send, swap_recv = refs[101:105]
    lane_send, lane_recv, scalar_send, scalar_recv, total_send, total_recv = refs[105:111]
    z, y, x, c = here()
    peers = all_peers()
    me = chip(z, y, x)

    barrier = pltpu.get_barrier_semaphore()
    spot = y * 2 + x
    column_peers = [device((z + 1 + i) % 4, y, x, c) for i in range(3)]
    plane = [(y, 1 - x), (1 - y, x), (1 - y, 1 - x)]
    plane_peers = [device(z, to_y, to_x, c) for to_y, to_x in plane]
    greeted = column_peers + plane_peers + [device(z, to_y, to_x, 1 - c) for to_y, to_x in [(y, x)] + plane]
    for peer in greeted:
        pl.semaphore_signal(barrier, inc=1, device_id=peer, device_id_type=MESH)

    tokens = cols.shape[0]

    def act_part(group):
        return act_t.at[pl.ds(LEFT * group, LEFT), 0:tokens]

    operands = (
        ((x_t, left[1]), (gqkv, gqkv_v)),
        ((y_t.at[:, 0:tokens], left[2]), (ge_t, left[3]), (glog.at[0:tokens, :], glog_v)),
        (),
        ((a_t.at[:, 0:tokens], left[0]), (gh.at[0:tokens, :], gh_v)),
        ((gffn.at[0:tokens, :], gffn_v), (act_part(0), left[5]), (act_part(1), left[6])),
        ((mix_t.at[:, 0:tokens], left[4]), (gattn.at[0:tokens, :], gattn_v)),
    )
    loads = {}
    waited = set()
    for task in TASKS:
        piece = task // 32 if task // 32 != 2 else 1
        if piece not in loads:
            loads[piece] = []
            for source, target in operands[piece]:
                number = sum(len(member) for member in loads.values())
                loads[piece].append(pltpu.make_async_copy(source, target, load_sem.at[number]))
                loads[piece][-1].start()

    def loaded(piece):
        piece = 1 if piece == 2 else piece
        if piece not in waited:
            waited.add(piece)
            for member in loads[piece]:
                member.wait()

    norm_t[...] = jnp.zeros(norm_t.shape, F32)
    norm_t[5:11, :] = norm_sums[...]
    pl.semaphore_wait(barrier, 10)

    def size_of(piece):
        return 2 * SHAPES[PIECES[piece][0]][0]

    def slot(ref, piece, index):
        size = size_of(piece)
        return ref[piece].at[pl.ds(pl.multiple_of(index * size, size), size), :]

    def half_of(piece):
        return SHAPES[PIECES[piece][0]][1] // 2

    def chosen(start):
        lane = lax.broadcasted_iota(jnp.int32, (1, TILE), 1) + start
        hit = (cols[:, 0:1] == lane) | (cols[:, 1:2] == lane)
        return jnp.where(hit, 1.0, 0.0).astype(BF16)

    def ring_copy(piece, rows, lanes, number, index):
        place = lax.rem(number, 3)
        return pltpu.make_async_remote_copy(
            src_ref=stage.at[place],
            dst_ref=side[piece].at[rows, lanes],
            send_sem=ring_sem.at[place],
            recv_sem=side_recv.at[piece, index],
            device_id=peers[SIDE],
            device_id_type=MESH,
        )

    def tail_copy(piece, rows, lanes, number, index):
        return pltpu.make_async_remote_copy(
            src_ref=tails.at[number],
            dst_ref=side[piece].at[rows, lanes],
            send_sem=tail_sem.at[number],
            recv_sem=side_recv.at[piece, index],
            device_id=peers[SIDE],
            device_id_type=MESH,
        )

    whole = pl.ds(0, LEFT)
    ring_count, tail_count = [0], [0]

    def give(piece, rows, lanes, number, index):
        def before():
            @pl.when(number >= 3)
            def _():
                ring_copy(piece, rows, lanes, number, index).wait_send()

        def write(value):
            stage[lax.rem(number, 3)] = value.astype(BF16)

        return before, write, lambda: ring_copy(piece, rows, lanes, number, index).start()

    def keep(piece, rows, lanes):
        def write(value):
            own[piece][rows, lanes] = value.astype(BF16)

        return lambda: None, write, lambda: None

    def plain(piece, mine, source, right, group):
        wide = PIECES[piece][2]
        half = c if mine else 1 - c
        rows = pl.ds(LEFT * group, LEFT)
        base = ring_count[0]

        def step(j):
            lanes = at(j, TILE)
            before, write, after = keep(piece, rows, lanes) if mine else give(
                piece, rows, lanes, base + j, group * (wide // TILE) + j
            )
            before()
            write(dot_nn(source[...], right[:, pl.ds(pl.multiple_of(half * wide + j * TILE, 128), TILE)]))
            after()

        each(wide // TILE, step)
        if not mine:
            ring_count[0] += wide // TILE
        if wide % TILE:
            start = wide - 128
            value = dot_nn(source[...], right[:, pl.ds(pl.multiple_of(half * wide + start, 128), 128)])
            if mine:
                own[piece][rows, start:wide] = value.astype(BF16)
            else:
                number = tail_count[0]
                tail_count[0] += 1
                groups = SHAPES[PIECES[piece][0]][0] // 24
                tails[number] = value.astype(BF16)
                tail_copy(piece, rows, pl.ds(start, 128), number, groups * (wide // TILE) + group).start()

    def wide_product(piece, mine):
        half = c if mine else 1 - c
        wide, skip, width = half_of(piece), PIECES[piece][1], PIECES[piece][2]
        base = ring_count[0]

        def start_of(j):
            return pl.multiple_of(half * wide + skip + j * TILE, 128)

        def both(j, size=TILE):
            return dot_nn(left[2][...], glog_v[:, pl.ds(start_of(j), size)]) + dot_nn(
                left[3][...], chosen(start_of(j))[:, 0:size]
            )

        def target(j):
            lanes = at(j, TILE)
            return keep(piece, whole, lanes) if mine else give(piece, whole, lanes, base + j, j)

        def step(j):
            before, write, after = target(j)
            before()
            write(both(j))
            after()

        if not mine:
            ring_count[0] += width // TILE
        if skip == 0:
            each(width // TILE, step)
            return
        each(1, step)
        before, write, after = target(1)
        before()
        norm_part = jnp.where(half == 1, norm_t[...], 0.0).T
        write(both(1) + jnp.concatenate((jnp.zeros((LEFT, TILE - 128), F32), norm_part), 1))
        after()

        def by_half(j, size, write):
            @pl.when(half == 0)
            def _():
                write(both(j, size))

            @pl.when(half == 1)
            def _():
                write(dot_nn(left[3][...], chosen(start_of(j))[:, 0:size]))

        for j in (2, 3):
            before, write, after = target(j)
            before()
            by_half(j, TILE, write)
            after()

        def write_tail(value):
            if mine:
                own[piece][whole, width - 128 : width] = value.astype(BF16)
            else:
                tails[tail_count[0]] = value.astype(BF16)

        by_half(4, 128, write_tail)
        if not mine:
            tail_copy(piece, whole, pl.ds(width - 128, 128), tail_count[0], width // TILE).start()
            tail_count[0] += 1

    def products(piece, mine):
        loaded(piece)
        if piece in (1, 2):
            wide_product(piece, mine)
        elif piece == 4:
            if not mine:
                for group in range(4):
                    source = left[5 + group % 2]
                    if group >= 2:
                        loads[piece][1 + group % 2].wait()
                    plain(piece, False, source, gffn_v, group)
                    plain(piece, True, source, gffn_v, group)
                    if group < 2:
                        again = pltpu.make_async_copy(act_part(group + 2), source, load_sem.at[12 + group])
                        again.start()
                        loads[piece][1 + group] = again
        else:
            source, right = {0: (left[1], gqkv_v), 3: (left[0], gh_v), 5: (left[4], gattn_v)}[piece]
            plain(piece, mine, source, right, 0)

    def combine(piece, target, parts):
        def some(rows, lanes):
            total = parts[0][rows, lanes].astype(F32)
            for member in parts[1:]:
                total = total + member[rows, lanes].astype(F32)
            target[rows, lanes] = total.astype(target.dtype)

        wide = PIECES[piece][2]
        if piece == 4:
            each(4, lambda group: some(at(group, 48), slice(0, wide)))
            return
        if wide >= 512:
            each(wide // 512, lambda j: some(slice(0, 48), at(j, 512)))
        if wide % 512:
            some(slice(0, 48), slice(wide // 512 * 512, wide))

    def hop(piece, k, land, index, sems, way):
        return pltpu.make_async_remote_copy(
            src_ref=slot(own, piece, k),
            dst_ref=slot(land, piece, index),
            send_sem=sems[0].at[piece, index],
            recv_sem=sems[1].at[piece, index],
            device_id=peers[way],
            device_id_type=MESH,
        )

    FIRST, SECOND = (first_send, first_recv), (second_send, second_recv)

    def landed(piece, land, index, sems):
        hop(piece, me, land, index, sems, XWAY).wait_recv()

    def block(piece, a, b, far):
        return chip(far, a, b) if SUM_WAY[piece] % 2 == 0 else chip(far, b, a)

    def split(piece):
        return (y, x, YWAY, XWAY) if SUM_WAY[piece] % 2 == 0 else (x, y, XWAY, YWAY)

    readied = set()

    def ready(piece):
        if piece in readied:
            return
        readied.add(piece)
        wide, groups = PIECES[piece][2], SHAPES[PIECES[piece][0]][0] // 24
        for group in range(groups):
            for j in range(wide // TILE):
                ring_copy(piece, pl.ds(LEFT * group, LEFT), at(j, TILE), 0, group * (wide // TILE) + j).wait_recv()
            if wide % TILE:
                index = groups * (wide // TILE) + group
                tail_copy(piece, pl.ds(LEFT * group, LEFT), pl.ds(wide - 128, 128), 0, index).wait_recv()

    def both_cores(piece, k):
        return (slot(own, piece, k), slot(side, piece, k))

    def first_block(piece, i):
        a, b, way, _ = split(piece)
        t, v = (z + i // 2) % 4, (1 - b) if i % 2 == 0 else b
        return block(piece, 1 - a, v, t), 2 * t + v, way

    def first_send_of(piece, i):
        ready(piece)
        k, index, way = first_block(piece, i)
        combine(piece, slot(own, piece, k), both_cores(piece, k))
        hop(piece, k, first, index, FIRST, way).start()

    def second_block(piece, i):
        a, b, _, way = split(piece)
        if SUM_WAY[piece] > 1:
            return block(piece, a, 1 - b, z), 0, way
        t = (z + i) % 4
        return block(piece, a, 1 - b, t), t, way

    def z_slots(piece, v):
        for i in range(3):
            t = (z + 1 + i) % 4
            index = t if v is None else 2 * t + v
            pltpu.make_async_remote_copy(
                src_ref=slot(own, piece, me),
                dst_ref=slot(column, piece, index),
                send_sem=z_send.at[piece, index],
                recv_sem=z_recv.at[piece, index],
                device_id=column_peers[i],
                device_id_type=MESH,
            ).wait_recv()
        return tuple(
            slot(column, piece, (z + 1 + i) % 4 if v is None else 2 * ((z + 1 + i) % 4) + v) for i in range(3)
        )

    def first_slot(piece, v, t):
        landed(piece, first, 2 * t + v, FIRST)
        return (slot(first, piece, 2 * t + v),)

    def second_slot(piece, index):
        landed(piece, second, index, SECOND)
        return (slot(second, piece, index),)

    def second_send_of(piece, i):
        k, index, way = second_block(piece, i)
        other = 1 - split(piece)[1]
        if SUM_WAY[piece] > 1:
            parts = first_slot(piece, other, z) + z_slots(piece, other)
        else:
            parts = first_slot(piece, other, index)
        combine(piece, slot(own, piece, k), both_cores(piece, k) + parts)
        hop(piece, k, second, index, SECOND, way).start()

    def z_block(piece, i):
        a, b, _, _ = split(piece)
        if SUM_WAY[piece] > 1:
            t, v = (z + 1 + i // 2) % 4, (1 - b) if i % 2 == 0 else b
            return block(piece, a, v, t), t, v, 2 * z + v, 2 * t + v, column_peers[i // 2]
        t = (z + 1 + i) % 4
        return chip(t, y, x), t, None, z, t, column_peers[i]

    def z_copy(piece, i):
        k, _, _, there, number, peer = z_block(piece, i)
        return pltpu.make_async_remote_copy(
            src_ref=slot(own, piece, k),
            dst_ref=slot(column, piece, there),
            send_sem=z_send.at[piece, number],
            recv_sem=z_recv.at[piece, there],
            device_id=peer,
            device_id_type=MESH,
        )

    def z_send_of(piece, i):
        k, t, v, _, _, _ = z_block(piece, i)
        if v is None:
            parts = first_slot(piece, split(piece)[1], t) + second_slot(piece, t)
        else:
            parts = first_slot(piece, v, t)
        combine(piece, slot(own, piece, k), both_cores(piece, k) + parts)
        z_copy(piece, i).start()

    swaps = []

    def finish(piece):
        mine = split(piece)[1]
        parts = both_cores(piece, me) + first_slot(piece, mine, z)
        if SUM_WAY[piece] > 1:
            parts = parts + z_slots(piece, mine) + second_slot(piece, 0)
        else:
            parts = parts + second_slot(piece, z) + z_slots(piece, None)
        combine(piece, fin[piece], parts)
        m, skip, wide = PIECES[piece]
        size = SHAPES[m][0]
        lanes = pl.ds(pl.multiple_of(c * half_of(piece) + skip, 128), wide)
        swaps.append(
            pltpu.make_async_remote_copy(
                src_ref=fin[piece].at[pl.ds(pl.multiple_of((1 - c) * size, 8), size), :],
                dst_ref=outs[m].at[:, lanes],
                send_sem=swap_send.at[piece],
                recv_sem=swap_recv.at[piece],
                device_id=peers[SIDE],
                device_id_type=MESH,
            )
        )
        swaps[-1].start()
        squared = fin[piece][...] * fin[piece][...] + SQUARE_FLOOR
        lane_plane[spot, :, HALF_AT[m] + skip : HALF_AT[m] + skip + wide] = jnp.sum(squared, 0, keepdims=True)
        outs[m][:, lanes] = fin[piece][pl.ds(pl.multiple_of(c * size, 8), size), :]

    for task in TASKS:
        piece, number = task // 32, task % 32
        if number < 2:
            products(piece, number == 1)
        elif number < 10:
            first_send_of(piece, number - 2)
        elif number == 17:
            finish(piece)
        elif SUM_WAY[piece] > 1:
            if number < 16:
                z_send_of(piece, number - 10)
            else:
                second_send_of(piece, 0)
        elif number < 14:
            second_send_of(piece, number - 10)
        else:
            z_send_of(piece, number - 14)

    def spread(source, target, send, recv, peer):
        copy = pltpu.make_async_remote_copy(
            src_ref=source, dst_ref=target, send_sem=send, recv_sem=recv, device_id=peer, device_id_type=MESH
        )
        copy.start()
        return copy

    def arrive(copies):
        for copy in copies:
            copy.wait_recv()
        return copies

    plane_copies = [
        spread(lane_plane.at[spot], lane_plane.at[spot], lane_send.at[i], lane_recv.at[i], plane_peers[i])
        for i in range(3)
    ]
    for swap in swaps:
        swap.wait()
    sides, gs = statistics(outs, side_olds)

    def spread_eight(buffers, value, send, recv):
        buffers[0][2 * spot + c] = value
        mine = buffers[0].at[2 * spot + c]
        return [spread(mine, mine, send.at[i], recv.at[i], greeted[3 + i]) for i in range(7)]

    def spread_four(buffers, send, recv):
        total = [buffers[0][2 * i] + buffers[0][2 * i + 1] for i in range(4)]
        buffers[1][z] = (total[0] + total[1]) + (total[2] + total[3])
        mine = buffers[1].at[z]
        return [spread(mine, mine, send.at[7 + i], recv.at[7 + i], column_peers[i]) for i in range(3)]

    def four(buffer):
        return (buffer[0] + buffer[1]) + (buffer[2] + buffer[3])

    scalars = lanes_of([jnp.sum(member, 0, keepdims=True) for member in sides] + [loss[...]])
    scalars = jnp.concatenate((scalars, squares[...]), 1)
    sent = spread_eight(scalar_sums, scalars, scalar_send, scalar_recv)
    sent += arrive(plane_copies)
    lane_z[z] = four(lane_plane)
    z_copies = [
        spread(lane_z.at[z], lane_z.at[z], lane_send.at[3 + i], lane_recv.at[3 + i], column_peers[i]) for i in range(3)
    ]
    arrive(sent[0:7])
    last_copies = spread_four(scalar_sums, scalar_send, scalar_recv)
    sent += arrive(z_copies)
    lane_halves[c] = four(lane_z)
    halves_copy = spread(lane_halves.at[c], lane_halves.at[c], lane_send.at[6], lane_recv.at[6], peers[SIDE])
    sent += arrive(last_copies)
    sent += arrive([halves_copy])
    pair = (lane_halves[0], lane_halves[1])
    lanes = [half[:, HALF_AT[m] : HALF_AT[m] + SHAPES[m][1] // 2] for m in range(5) for half in pair]
    sums = jnp.concatenate(lanes + [four(scalar_sums[1])], 1)
    sums_out[...] = sums
    updates = updates_of(sums, gs, sides, lane_olds, moment)[0]
    totals = lanes_of(
        [total_sum(update * update) for update in updates[:6]]
        + [jnp.sum(updates[6][i : i + 1] * updates[6][i : i + 1], 1, keepdims=True) for i in range(6)]
    )
    sent += arrive(spread_eight(total_sums, totals, total_send, total_recv))
    sent += arrive(spread_four(total_sums, total_send, total_recv))
    totals_out[...] = four(total_sums[1])
    for copy in sent:
        copy.wait_send()
    for piece in range(6):
        for i in range(8):
            k, index, way = first_block(piece, i)
            hop(piece, k, first, index, FIRST, way).wait_send()
        for i in range(1 if SUM_WAY[piece] > 1 else 4):
            k, index, way = second_block(piece, i)
            hop(piece, k, second, index, SECOND, way).wait_send()
        for i in range(6 if SUM_WAY[piece] > 1 else 3):
            z_copy(piece, i).wait_send()
    for number in range(ring_count[0] - 3, ring_count[0]):
        ring_copy(1, whole, pl.ds(0, TILE), number, 0).wait_send()
    for number in range(tail_count[0]):
        tail_copy(1, whole, pl.ds(0, 128), number, 0).wait_send()


def statistics(grads, side_olds):
    wide_g = grads[E_][...]
    gs = (wide_g[:, :VOCAB], wide_g[:, PLACE_AT:]) + tuple(grads[m][...] for m in (Q_, O_, I_, D_))
    decay = 1.0 - STEP ** (-0.8)
    sides = []
    for index in range(6):
        mean = jnp.sum(gs[index] * gs[index] + SQUARE_FLOOR, 1, keepdims=True) / gs[index].shape[1]
        sides.append(decay * column_of(as_row(side_olds[index])) + (1.0 - decay) * mean)
    return sides, gs + (wide_g[:, 4096:4224],)


def updates_of(sums, gs, sides, lane_olds, moment):
    decay = 1.0 - STEP ** (-0.8)
    fresh = 1.0 - decay
    parts = [sums[:, :VOCAB], sums[:, PLACE_AT:WIDE]]
    parts += [sums[:, SUM_AT[i] : SUM_AT[i + 1]] for i in range(1, 5)]
    scalars = sums[:, SUM_AT[5] : SUM_AT[5] + 128]
    updates, lane_news = [], []
    for index in range(6):
        height = gs[index].shape[0] * 32
        lane_news.append(decay * as_row(lane_olds[index]) + fresh * (parts[index] / height))
        if index < 2:
            mean = jnp.sum(lane_news[index], 1, keepdims=True) / lane_news[index].shape[1]
        else:
            mean = lane_at(scalars, index) / height
        updates.append(gs[index] * lax.rsqrt(sides[index] * lane_news[index] / mean))
    norm_g = jnp.concatenate([row_of(lane_at(gs[6], NORM_AT - 4096 + i)) for i in range(6)], 0)
    moment_new = decay * moment[...] + fresh * (norm_g * norm_g + SQUARE_FLOOR)
    updates.append(norm_g * lax.rsqrt(moment_new))
    return updates, lane_news, norm_g, moment_new


def reduce_grads(large, small):
    tokens = 5 * SPAN
    vmem, hbm = pl.BlockSpec(memory_space=pltpu.VMEM), pl.BlockSpec(memory_space=pl.ANY)
    dma = pltpu.SemaphoreType.DMA
    scratch = []
    for counts in ((16, 16), (16, 16), (8, 8), (4, 1), (4, 8)):
        for (m, _, wide), way in zip(PIECES, SUM_WAY):
            scratch.append(pltpu.VMEM((counts[way // 2] * 2 * SHAPES[m][0], wide), BF16))
    scratch += [pltpu.VMEM((2 * SHAPES[m][0], wide), F32) for m, _, wide in PIECES]
    scratch += [pltpu.VMEM((LEFT, tokens), BF16)] * 7
    scratch += [pltpu.VMEM((tokens, width), BF16) for width in (TABLE_END, 3 * D, D, 4 * D, D)]
    scratch += [pltpu.VMEM((3, LEFT, TILE), BF16), pltpu.VMEM((7, LEFT, 128), BF16), pltpu.VMEM((128, D), F32)]
    scratch += [pltpu.VMEM((count, 1, HALF_SUMS), F32) for count in (4, 4, 2)]
    scratch += [pltpu.VMEM((count, 1, width), F32) for width in (256, 128) for count in (8, 4)]
    scratch += [dma((14,)), dma((3,)), dma((7,)), dma((6, 10)), dma((6, 8)), dma((6, 8)), dma((6, 4)), dma((6, 4))]
    scratch += [dma((6, 8)), dma((6, 8)), dma((6,)), dma((6,))]
    scratch += [dma((7,))] * 2 + [dma((10,))] * 4
    return pl.pallas_call(
        reduce_kernel,
        out_shape=[jax.ShapeDtypeStruct(shape, F32) for shape in SHAPES + ((1, SUMS), (1, 128))],
        in_specs=[hbm] * 11 + [vmem] * len(small),
        out_specs=[vmem] * 7,
        scratch_shapes=scratch,
        compiler_params=pltpu.CompilerParams(
            collective_id=1, has_side_effects=True, vmem_limit_bytes=63 * 1024 * 1024
        ),
    )(*large, *small)


def update_kernel(*refs):
    copies = [pltpu.make_async_copy(refs[i], refs[55 + i], refs[82].at[i]) for i in range(27)]
    for copy in copies:
        copy.start()
    for copy in copies:
        copy.wait()
    refs = refs[55:82] + refs[27:55]
    grads, sums, totals, ws, norms = refs[0:5], refs[5], refs[6], refs[7:13], refs[13]
    lane_olds, side_olds, moment = refs[14:20], refs[20:26], refs[26]
    loss_out, table_g, place_g, norm_g_out = refs[27:31]
    lane_outs, side_outs, moment_out, news, norm_new = refs[31:37], refs[37:43], refs[43], refs[44:50], refs[50]
    grad_outs = refs[51:55]
    sides, gs = statistics(grads, side_olds)
    updates, lane_news, norm_g, moment_new = updates_of(sums[...], gs, sides, lane_olds, moment)
    scalars = sums[:, SUM_AT[5] : SUM_AT[5] + 128]
    squares = sums[:, SUM_AT[5] + 128 :]
    loss_out[...] = lane_at(scalars, 6)
    table_g[...] = gs[0]
    place_g[...] = gs[1]
    norm_g_out[...] = norm_g
    moment_out[...] = moment_new
    for index in range(6):
        lane_outs[index][...] = lane_news[index].reshape(lane_outs[index].shape)
        side_outs[index][...] = row_of(sides[index]).reshape(side_outs[index].shape)
        if index >= 2:
            grad_outs[index - 2][...] = gs[index]
        entries = gs[index].shape[0] * gs[index].shape[1] * 32
        clip = jnp.maximum(1.0, jnp.sqrt(lane_at(totals[...], index) / entries))
        scale = learn_rate * jnp.sqrt(lane_at(squares, index) / entries) / clip
        news[index][...] = ws[index][...] - scale * updates[index]
    for i in range(6):
        clip = jnp.maximum(1.0, jnp.sqrt(lane_at(totals[...], 6 + i) / D))
        scale = learn_rate * jnp.sqrt(lane_at(squares, 6 + i) / D) / clip
        norm_new[i : i + 1, :] = norms[i : i + 1, :] - scale * updates[6][i : i + 1, :]


def update_weights(operands):
    lanes = (VOCAB, 512, 3 * D, D, 4 * D, D)
    held = (24, 24, 24, 24, 24, 96)
    shapes = [(1, 1), (24, VOCAB), (24, 512), (6, 24)]
    shapes += [(lane,) for lane in lanes] + [(size,) for size in held] + [(6, 24)]
    shapes += list(zip(held, lanes)) + [(6, 24)] + list(zip(held, lanes))[2:]
    return pl.pallas_call(
        update_kernel,
        out_shape=[jax.ShapeDtypeStruct(shape, F32) for shape in shapes],
        in_specs=[pl.BlockSpec(memory_space=pl.ANY)] * len(operands),
        out_specs=[pl.BlockSpec(memory_space=pltpu.VMEM)] * len(shapes),
        scratch_shapes=[pltpu.VMEM(member.shape, member.dtype) for member in operands]
        + [pltpu.SemaphoreType.DMA((len(operands),))],
        compiler_params=pltpu.CompilerParams(vmem_limit_bytes=63 * 1024 * 1024),
    )(*operands)


def norm_forward(value, gain, shift):
    centred = value - jnp.mean(value, -1, keepdims=True)
    inverse = lax.rsqrt(jnp.mean(centred * centred, -1, keepdims=True) + EPSILON)
    normed = centred * inverse
    return (normed * gain + shift, normed, inverse)


def norm_backward(grad_out, normed, inverse, gain):
    scaled = grad_out * gain
    back = inverse * (
        scaled
        - jnp.mean(scaled, -1, keepdims=True)
        - normed * jnp.mean(scaled * normed, -1, keepdims=True)
    )
    return (back, jnp.sum(grad_out * normed, 0), jnp.sum(grad_out, 0))


def mm(left, right, sides):
    return lax.dot_general(left, right, ((sides[:1], sides[1:]), ((), ())), preferred_element_type=F32)


def attend(qkv, allowed):
    by_head = qkv.reshape(qkv.shape[0], 3, HEADS, HEAD_DIM)
    query, key, value = by_head[:, 0], by_head[:, 1], by_head[:, 2]
    scores = jnp.einsum("qhe,khe->hqk", query, key, preferred_element_type=F32) * 0.125
    scores = jnp.where(allowed[None], scores, -1e30)
    highest = jnp.max(scores, -1, keepdims=True)
    raised = jnp.exp(scores - highest)
    summed = jnp.sum(raised, -1, keepdims=True)
    shares = (raised / summed).astype(BF16)
    mixture = jnp.einsum("hqk,khe->qhe", shares, value, preferred_element_type=F32)
    return mixture.astype(BF16).reshape(qkv.shape[0], D), highest + jnp.log(summed)


def attend_back(qkv, allowed, log_total, grad_mix):
    by_head = qkv.reshape(qkv.shape[0], 3, HEADS, HEAD_DIM)
    query, key, value = by_head[:, 0], by_head[:, 1], by_head[:, 2]
    grad_mix = grad_mix.reshape(qkv.shape[0], HEADS, HEAD_DIM)
    scores = jnp.einsum("qhe,khe->hqk", query, key, preferred_element_type=F32) * 0.125
    scores = jnp.where(allowed[None], scores, -1e30)
    shares = jnp.exp(scores - log_total)
    grad_share = jnp.einsum("qhe,khe->hqk", grad_mix, value, preferred_element_type=F32)
    grad_score = (shares * (grad_share - jnp.sum(shares * grad_share, -1, keepdims=True))).astype(BF16)
    grad_query = jnp.einsum("hqk,khe->qhe", grad_score, key, preferred_element_type=F32) * 0.125
    grad_key = jnp.einsum("hqk,qhe->khe", grad_score, query, preferred_element_type=F32) * 0.125
    grad_value = jnp.einsum("hqk,qhe->khe", shares.astype(BF16), grad_mix, preferred_element_type=F32)
    return jnp.stack((grad_query, grad_key, grad_value), 1).astype(BF16).reshape(qkv.shape)


def on_slice(token_arrays, lengths, weights, lane_olds, side_olds, moment):
    olds = lane_olds + side_olds + (moment,)
    found = front(token_arrays + weights, lengths)
    mask_count, gains, side, cols, keys, weight_sq = found[0:6]
    x_t, mix, a, act, y, slope, qkv_b, normed_a = found[6:14]
    normed_bc, (qkv_w, out_w, in_w, down_w, wide_w) = found[14:18], found[18:23]
    found = middle(
        (wide_w, qkv_w, out_w, in_w, down_w, y, act, a, mix, slope, qkv_b, normed_a) + tuple(normed_bc),
        (cols, keys, side, gains, mask_count),
    )
    loss_part, norm_sums = found[0:2]
    grad_logit, y_t, a_t, mix_t, act_t, ge_t, grad_ffn, grad_hidden, grad_attn, grad_qkv = found[2:]
    reduced = reduce_grads(
        (y_t, ge_t, grad_logit, x_t, grad_qkv, mix_t, grad_attn, a_t, grad_hidden, act_t, grad_ffn),
        (cols, norm_sums, loss_part, weight_sq) + olds,
    )
    found = update_weights(tuple(reduced) + weights + olds)
    grads = (None,) + tuple(found[24:28])
    mask_count = mask_count.reshape(())
    loss_sum, table_g, place_g, norm_g = found[0:4]
    lane_news = found[4:10]
    side_news = found[10:16]
    moment_new, norm_new = found[16], found[23]
    news = found[17:23]
    return (
        loss_sum.reshape(()),
        mask_count,
        table_g.T,
        place_g.T,
        grads[1],
        grads[2],
        grads[3],
        grads[4],
        norm_g.T,
        lane_news[0],
        side_news[0],
        lane_news[1],
        side_news[1],
        side_news[2],
        lane_news[2],
        side_news[3],
        lane_news[3],
        side_news[4],
        lane_news[4],
        side_news[5],
        lane_news[5],
        moment_new.T,
        news[0].T,
        news[1].T,
        news[2],
        news[3],
        news[4],
        news[5],
        norm_new.T,
    )


def on_device(
    whole_mesh,
    long_ids,
    long_targets,
    long_mask,
    long_lengths,
    short_ids,
    short_targets,
    short_mask,
    short_lengths,
    table,
    position,
    qkv_weight,
    out_weight,
    in_weight,
    down_weight,
    norms,
    table_rows,
    table_cols,
    position_rows,
    position_cols,
    qkv_rows,
    qkv_cols,
    out_rows,
    out_cols,
    in_rows,
    in_cols,
    down_rows,
    down_cols,
    norm_moment,
):
    if whole_mesh == (8, 4):
        return on_slice(
            (long_ids, long_targets, long_mask, short_ids, short_targets, short_mask),
            (long_lengths, short_lengths),
            (table.T, position.T, qkv_weight, out_weight, in_weight, down_weight, norms.T),
            (table_rows, position_rows, qkv_cols, out_cols, in_cols, down_cols),
            (table_cols, position_cols, qkv_rows, out_rows, in_rows, down_rows),
            norm_moment.T,
        )
    devices = lax.axis_size(("dp", "seq"))
    seq_index = lax.axis_index("seq")
    held = norms.shape[0]

    span = long_ids.shape[1]
    long_place = seq_index * span + lax.iota(jnp.int32, span)
    long_keep = (long_place[None, :] < long_lengths[:, None]).astype(jnp.int32)
    short_keep = (lax.iota(jnp.int32, SPAN)[None, :] < short_lengths[:, None]).astype(jnp.int32)
    long_pack = jnp.stack((long_ids, long_targets, long_mask * long_keep, long_keep), 1)
    short_pack = jnp.stack((short_ids, short_targets, short_mask * short_keep, short_keep), 1)
    moved = lax.all_to_all(
        jnp.concatenate((long_pack, short_pack[1:]), 0), "seq", split_axis=0, concat_axis=0, tiled=True
    )
    tokens = jnp.concatenate((moved, short_pack[:1]), 0)
    ids, targets, weight, keep = (tokens[:, i].reshape(-1) for i in range(4))
    weight = weight.astype(F32)
    count = tokens.shape[0] * span
    last = count - span
    alone = seq_index == lax.axis_size("seq") - 1
    token = lax.iota(jnp.int32, count)
    place = jnp.where(alone | (token >= last), token % span, token)
    row = jnp.where(alone | (token >= last), token // span, 0)
    allowed_long = (row[:last, None] == row[None, :last]) & (keep[None, :last] > 0)
    allowed_short = jnp.broadcast_to(keep[None, last:] > 0, (span, span))

    here_count = jnp.sum(long_pack[:, 2]) + jnp.sum(short_pack[:, 2])
    tall = table.T
    counts = jnp.broadcast_to(jnp.stack((here_count // 256, here_count % 256)).astype(F32)[None], (held, 2))
    wide_shard = jnp.concatenate(
        (tall, norms, counts, jnp.zeros((held, PLACE_AT - COUNT_AT - 2), F32), position.T), 1
    )
    shards = (wide_shard, qkv_weight, out_weight, in_weight, down_weight)
    wide_w, qkv_w, out_w, in_w, down_w = (
        lax.all_gather(shard.astype(BF16), ("dp", "seq"), axis=0, tiled=True) for shard in shards
    )
    column = lax.broadcasted_iota(jnp.int32, (1, WIDE), 1)
    chosen = ((ids[:, None] == column) | ((place[:, None] + PLACE_AT) == column)).astype(BF16)
    gains = wide_w[:, NORM_AT : NORM_AT + 6].astype(F32)
    sums = jnp.sum(wide_w[:, COUNT_AT : COUNT_AT + 2].astype(F32), 0)
    mask_count = (sums[0] * 256.0 + sums[1]) / held
    inverse_count = 1.0 / mask_count

    embedded = mm(chosen, wide_w, (1, 1))
    first, normed_a, inverse_a = norm_forward(embedded, gains[:, 0], gains[:, 1])
    first_b = first.astype(BF16)
    qkv_b = mm(first_b, qkv_w, (1, 0)).astype(BF16)
    mix_long, total_long = attend(qkv_b[:last], allowed_long)
    mix_short, total_short = attend(qkv_b[last:], allowed_short)
    mixture = jnp.concatenate((mix_long, mix_short), 0)
    second, normed_b, inverse_b = norm_forward(first + mm(mixture, out_w, (1, 0)), gains[:, 2], gains[:, 3])
    second_b = second.astype(BF16)
    hidden = mm(second_b, in_w, (1, 0))
    active, slope = gelu_pair(hidden)
    active_b = active.astype(BF16)
    third, normed_c, inverse_c = norm_forward(second + mm(active_b, down_w, (1, 0)), gains[:, 4], gains[:, 5])
    third_b = third.astype(BF16)
    logits = jnp.where(column < VOCAB, mm(third_b, wide_w, (1, 0)), -1e30)
    highest = jnp.max(logits, -1, keepdims=True)
    log_sum = highest + jnp.log(jnp.sum(jnp.exp(logits - highest), -1, keepdims=True))
    onehot = targets[:, None] == column
    picked = jnp.sum(jnp.where(onehot, logits, 0.0), -1)
    loss_part = jnp.sum(weight * (log_sum[:, 0] - picked))
    grad_logit = (
        (jnp.exp(logits - log_sum) - onehot.astype(F32)) * (weight * inverse_count)[:, None]
    ).astype(BF16)
    grad_third = mm(grad_logit, wide_w, (1, 1))
    grad_second, gain_c, shift_c = norm_backward(grad_third, normed_c, inverse_c, gains[:, 4])
    grad_ffn = grad_second.astype(BF16)
    down_grad = mm(active_b, grad_ffn, (0, 0)).astype(BF16)
    grad_hidden = (mm(grad_ffn, down_w, (1, 1)) * slope).astype(BF16)
    in_grad = mm(second_b, grad_hidden, (0, 0)).astype(BF16)
    grad_second = grad_second + mm(grad_hidden, in_w, (1, 1))
    grad_first, gain_b, shift_b = norm_backward(grad_second, normed_b, inverse_b, gains[:, 2])
    grad_attn = grad_first.astype(BF16)
    out_grad = mm(mixture, grad_attn, (0, 0)).astype(BF16)
    grad_mix = mm(grad_attn, out_w, (1, 1)).astype(BF16)
    grad_qkv = jnp.concatenate(
        (
            attend_back(qkv_b[:last], allowed_long, total_long, grad_mix[:last]),
            attend_back(qkv_b[last:], allowed_short, total_short, grad_mix[last:]),
        ),
        0,
    )
    qkv_grad = mm(first_b, grad_qkv, (0, 0)).astype(BF16)
    grad_first = grad_first + mm(grad_qkv, qkv_w, (1, 1))
    grad_embed, gain_a, shift_a = norm_backward(grad_first, normed_a, inverse_a, gains[:, 0])
    wide_grad = mm(
        jnp.concatenate((third_b, grad_embed.astype(BF16)), 0),
        jnp.concatenate((grad_logit, chosen), 0),
        (0, 0),
    )
    norm_part = jnp.stack((gain_a, shift_a, gain_b, shift_b, gain_c, shift_c), 1)
    wide_grad = lax.dynamic_update_slice(wide_grad.astype(BF16), norm_part.astype(BF16), (0, NORM_AT))
    grads = (wide_grad, qkv_grad, out_grad, in_grad, down_grad)
    wide_g, qkv_g, out_g, in_g, down_g = (
        lax.psum_scatter(grad.astype(F32), ("dp", "seq"), scatter_dimension=0, tiled=True) for grad in grads
    )
    table_g, place_g = wide_g[:, :VOCAB], wide_g[:, PLACE_AT:]
    norm_g = wide_g[:, NORM_AT : NORM_AT + 6]

    decay = 1.0 - STEP ** (-0.8)
    matrices = (
        (qkv_weight, qkv_g, qkv_rows, qkv_cols),
        (out_weight, out_g, out_rows, out_cols),
        (in_weight, in_g, in_rows, in_cols),
        (down_weight, down_g, down_rows, down_cols),
    )
    wide = (
        (tall, table_g, table_cols, table_rows),
        (position.T, place_g, position_cols, position_rows),
    )
    row_news = [
        decay * member[2] + (1.0 - decay) * jnp.mean(member[1] * member[1] + SQUARE_FLOOR, 1)
        for member in matrices + wide
    ]
    col_parts = [jnp.sum(member[1] * member[1] + SQUARE_FLOOR, 0) for member in matrices + wide]
    row_totals = jnp.stack([jnp.sum(rows_new) for rows_new in row_news])
    weight_sq = jnp.stack([jnp.sum(member[0] * member[0]) for member in matrices + wide])
    stats = lax.psum(
        col_parts + [row_totals, weight_sq, jnp.sum(norms * norms, 0), loss_part.reshape(1)], ("dp", "seq")
    )
    updates = []
    cols_out = []
    for index, member in enumerate(matrices + wide):
        full_rows = member[0].shape[0] * devices
        cols_new = decay * member[3] + (1.0 - decay) * stats[index] / full_rows
        if index < 4:
            mean = stats[6][index] / full_rows
        else:
            mean = jnp.mean(cols_new)
        updates.append(member[1] * lax.rsqrt(row_news[index][:, None] * cols_new[None, :] / mean))
        cols_out.append(cols_new)
    moment_new = decay * norm_moment + (1.0 - decay) * (norm_g * norm_g + SQUARE_FLOOR)
    norm_update = norm_g * lax.rsqrt(moment_new)
    update_sq = jnp.stack([jnp.sum(update * update) for update in updates])
    totals = lax.psum((update_sq, jnp.sum(norm_update * norm_update, 0)), ("dp", "seq"))
    news = []
    for index, member in enumerate(matrices + wide):
        entries = member[0].shape[0] * member[0].shape[1] * devices
        clip = jnp.maximum(1.0, jnp.sqrt(totals[0][index] / entries))
        news.append(
            member[0] - learn_rate * jnp.sqrt(stats[7][index] / entries) * updates[index] / clip
        )
    norm_rows = norms.shape[0] * devices
    norm_clip = jnp.maximum(1.0, jnp.sqrt(totals[1] / norm_rows))
    norm_new = norms - learn_rate * jnp.sqrt(stats[8] / norm_rows) * norm_update / norm_clip
    return (
        stats[9][0],
        mask_count,
        table_g.T,
        place_g.T,
        qkv_g,
        out_g,
        in_g,
        down_g,
        norm_g,
        cols_out[4],
        row_news[4],
        cols_out[5],
        row_news[5],
        row_news[0],
        cols_out[0],
        row_news[1],
        cols_out[1],
        row_news[2],
        cols_out[2],
        row_news[3],
        cols_out[3],
        moment_new,
        news[4].T,
        news[5].T,
        news[0],
        news[1],
        news[2],
        news[3],
        norm_new,
    )


def solution(mesh):
    split, wide = P(("dp", "seq"), None), P(None, ("dp", "seq"))
    shard, same = P(("dp", "seq")), P()
    return jax.shard_map(
        functools.partial(on_device, (mesh.shape["dp"], mesh.shape["seq"])),
        mesh=mesh,
        in_specs=(P("dp", "seq"),) * 3
        + (P("dp"),)
        + (split,) * 3
        + (shard,)
        + (wide,) * 2
        + (split,) * 5
        + (same, shard) * 2
        + (shard, same) * 4
        + (split,),
        out_specs=(same, same)
        + (wide,) * 2
        + (split,) * 5
        + (same, shard) * 2
        + (shard, same) * 4
        + (split,)
        + (wide,) * 2
        + (split,) * 5,
        check_vma=False,
    )
```

```python
import functools

import jax
import jax.numpy as jnp
from jax import lax
from jax.experimental import pallas as pl
from jax.experimental.pallas import tpu as pltpu
from jax.sharding import PartitionSpec as P

D = 768
HEADS = 12
HEAD_DIM = 64
VOCAB = 4101
STEP = 10
SPAN = 128

EPSILON = 1e-12
SQUARE_FLOOR = 1e-30
learn_rate = 0.3

MESH = pl.DeviceIdType.MESH
F32 = jnp.float32
BF16 = jnp.bfloat16

NORM_AT = VOCAB
COUNT_AT = VOCAB + 6
TABLE_END = 4352
PLACE_AT = 4352
WIDE = PLACE_AT + 512

SHAPES = ((24, WIDE), (24, 3 * D), (24, D), (24, 4 * D), (96, D))
E_, Q_, O_, I_, D_ = range(5)
CLASS_A, CLASS_B, CLASS_C = (E_, O_), (Q_, D_), (I_,)
UP, DOWN, XWAY, YWAY, SIDE = range(5)


def here():
    dp, seq = lax.axis_index("dp"), lax.axis_index("seq")
    return dp // 2, dp % 2, seq // 2, seq % 2


def device(z, y, x, c):
    return {"dp": z * 2 + y, "seq": x * 2 + c}


def chip(z, y, x):
    return z * 4 + y * 2 + x


def near_first(z, s):
    inner = (z * (3 - z)) // 2
    found = s + inner * (1, 1, -2, 0)[s]
    return found + (z // 2) * (3 - 2 * found)


def all_peers():
    z, y, x, c = here()
    return (
        device(z + 1, y, x, c),
        device(z - 1, y, x, c),
        device(z, y, 1 - x, c),
        device(z, 1 - y, x, c),
        device(z, y, x, 1 - c),
    )


SUM_AT = (0, WIDE, WIDE + 3 * D, WIDE + 4 * D, WIDE + 8 * D, WIDE + 9 * D)
SUMS = WIDE + 9 * D + 256
HALF_AT = tuple(start // 2 for start in SUM_AT)
HALF_SUMS = HALF_AT[5]


def lanes_of(members):
    lane = lax.broadcasted_iota(jnp.int32, (1, 128), 1)
    row = jnp.zeros((1, 128), F32)
    for index, member in enumerate(members):
        row = jnp.where(lane == index, member, row)
    return row


def lane_at(row, index):
    lane = lax.broadcasted_iota(jnp.int32, row.shape, 1)
    return jnp.sum(jnp.where(lane == index, row, 0.0), 1, keepdims=True)


def column_of(row):
    size = row.shape[1]
    diagonal = lax.broadcasted_iota(jnp.int32, (size, size), 0) == lax.broadcasted_iota(
        jnp.int32, (size, size), 1
    )
    return jnp.sum(jnp.where(diagonal, row, 0.0), 1, keepdims=True)


def row_of(column):
    size = column.shape[0]
    diagonal = lax.broadcasted_iota(jnp.int32, (size, size), 0) == lax.broadcasted_iota(
        jnp.int32, (size, size), 1
    )
    return jnp.sum(jnp.where(diagonal, column, 0.0), 0, keepdims=True)


def as_row(ref):
    return ref[...].reshape(1, ref.shape[0])


def total_sum(array):
    return jnp.sum(jnp.sum(array, 1, keepdims=True), 0, keepdims=True)


def gelu_pair(hidden):
    normal_cdf = 0.5 * (1.0 + lax.erf(hidden * 0.7071067811865476))
    return (
        hidden * normal_cdf,
        normal_cdf + hidden * jnp.exp(-0.5 * hidden * hidden) * 0.3989422804014327,
    )


def dot_nn(left, right):
    return jnp.dot(left, right, preferred_element_type=F32)


def dot_nt(left, right):
    return lax.dot_general(left, right, (((1,), (1,)), ((), ())), preferred_element_type=F32)


def dot_tn(left, right):
    return lax.dot_general(left, right, (((0,), (0,)), ((), ())), preferred_element_type=F32)


def at(index, size):
    if isinstance(index, int):
        return pl.ds(index * size, size)
    return pl.ds(pl.multiple_of(index * size, size), size)


def each(count, body):
    def step(index, carry):
        body(index)
        return carry

    lax.fori_loop(0, count, step, 0)


def each_unrolled(count, body):
    for index in range(count):
        body(index)


ROWS = 128
TILE = 256
HALF = 320
TABLE_TILES = TABLE_END // TILE


def head_lanes(first):
    lane = lax.broadcasted_iota(jnp.int32, (1, 128), 1)
    return (lane < HEAD_DIM) if first else (lane >= HEAD_DIM)


def layer_norm(value, gain, shift):
    centred = value - jnp.sum(value, 1, keepdims=True) / D
    inverse = lax.rsqrt(jnp.sum(centred * centred, 1, keepdims=True) / D + EPSILON)
    normed = centred * inverse
    return normed * gain + shift, normed, inverse


def layer_norm_back(grad, normed, inverse, gain):
    scaled = grad * gain
    return inverse * (
        scaled - jnp.sum(scaled, 1, keepdims=True) / D - normed * (jnp.sum(scaled * normed, 1, keepdims=True) / D)
    )


def put_lane(ref, rows, index, value):
    lane = lax.broadcasted_iota(jnp.int32, (1, 128), 1)
    ref[rows, :] = jnp.where(lane == index, value, ref[rows, :])


def set_bias(bias, cols, keys, last):
    same = cols[0:last, 4:5] == keys[1:2, 0:last]
    bias[...] = jnp.where(same & (keys[0:1, 0:last] > 0), 0.0, -1e30)


CHOOSE, EMBED, NORM_A, PROJECT, TURN_X, ATTEND, OUT, NORM_B, FEED_IN, TURN_A, FEED_OUT, REST = range(12)
FRONT = (
    35, 99, 33, 67, 65, 32, 4, 64, 3, 36, 1, 160, 69, 101, 40, 37, 1000, 163, 100, 0,
    129, 70, 1001, 68, 164, 128, 103, 72, 46, 44, 73, 161, 97, 96, 38, 5, 45, 74, 39, 77,
    102, 6, 172, 71, 7, 105, 82, 8, 41, 11, 10, 107, 12, 42, 14, 43, 79, 75, 9, 47,
    166, 168, 165, 104, 80, 78, 133, 81, 76, 18, 49, 111, 51, 48, 170, 50, 134, 167, 83, 132,
    108, 106, 13, 16, 1016, 17, 1017, 1018, 15, 1019, 1020, 135, 110, 19, 1021, 1032, 144, 176, 169, 142,
    1048, 1049, 171, 115, 1050, 1051, 173, 137, 1052, 131, 1053, 1054, 1055, 109, 1056, 1064, 174, 1080, 177, 140,
    1081, 138, 112, 178, 1082, 1083, 139, 114, 1084, 175, 179, 1085, 145, 143, 1096, 113, 146, 1097, 1098, 136,
    1112, 1128, 1129, 147, 1130, 1131, 1132, 1133, 1134, 1135, 141, 1136, 1137, 1138, 1139, 1160, 1161, 1162, 1176,
)


def front_hooks():
    hooks, before = {}, []
    for task in FRONT:
        if task < 1000:
            before.append(task)
        else:
            hooks[((task - 1000) // 16, (task - 1000) % 16)] = before
            before = []
    return hooks


def front_kernel(*refs):
    raw, (long_len, short_len) = refs[0:13], refs[13:15]
    count_out, gains_out, side, cols, keys, squares = refs[15:21]
    x_t, mix_out, a_out, act_out, y_out, slope_out, qkv_out, na_out = refs[21:29]
    nb_outs, nc_outs, weight_outs = refs[29:31], refs[31:33], refs[33:38]
    wide, qkv_w, out_w, in_w, down_w = weights = refs[38:43]
    value, na, low_a, low_y, mix, qkv, act, slope, pick, pick_two, bias, turned = refs[43:55]
    nb, nc = refs[55:57], (mix, low_y)
    held, wide_shard, merge, pieces, land = refs[57:70], refs[70], refs[71:76], refs[76], refs[77]
    raw_sem, swap_send, swap_recv, token_send, token_recv, send_sem, link_recv, side_recv = refs[78:86]
    out_sem, turn_sem = refs[86:88]
    z, y, x, c = here()
    peers = all_peers()
    me = chip(z, y, x)
    seq = x * 2 + c
    alone = seq // 3
    tokens = value.shape[0]
    last = tokens - SPAN
    hooks = front_hooks()

    barrier = pltpu.get_barrier_semaphore()
    cross = device(z, y, 1 - x, 1 - c)
    column = [device((z + 1 + i) % 4, y, x, c) for i in range(3)]
    for peer in [peers[XWAY], peers[YWAY], peers[SIDE], cross] + column:
        pl.semaphore_signal(barrier, inc=1, device_id=peer, device_id_type=MESH)
    raws = [pltpu.make_async_copy(raw[i], held[i], raw_sem.at[i]) for i in range(13)]
    for member in raws:
        member.start()
    for member in raws:
        member.wait()
    long_ids, long_targets, long_mask, short_ids, short_targets, short_mask, tall, place, qkv_s, out_s, in_s, down_s, norms = held

    pieces[...] = jnp.zeros(pieces.shape, jnp.int32)
    land[4] = jnp.zeros((8, SPAN), jnp.int32)
    lane = lax.broadcasted_iota(jnp.int32, (1, SPAN), 1)
    count = jnp.zeros((1, SPAN), jnp.int32)
    for t in range(5):
        if t < 3:
            ids, targets, mask = long_ids[t : t + 1, :], long_targets[t : t + 1, :], long_mask[t : t + 1, :]
            keep = (lane + seq * SPAN < long_len[t]).astype(jnp.int32)
        else:
            row = (1, 0)[t - 3]
            ids, targets, mask = (member[row : row + 1, :] for member in (short_ids, short_targets, short_mask))
            keep = (lane < short_len[row]).astype(jnp.int32)
        target = pieces.at[t] if t < 4 else land.at[4]
        target[0:1, :] = ids
        target[2:3, :] = targets
        target[3:4, :] = mask * keep
        target[5:6, :] = keep
        count = count + mask * keep
    count = jnp.sum(count.astype(F32), 1, keepdims=True)
    high = jnp.floor(count * (1.0 / 256.0))

    wide_shard[:, 0:4096] = tall[:, 0:4096]
    edge = jnp.zeros((24, 128), F32)
    tile_lane = lax.broadcasted_iota(jnp.int32, (24, 128), 1)
    tall_edge = tall[:, 4096:VOCAB]
    members = [lane_at(tall_edge, i) for i in range(VOCAB - 4096)]
    members += [column_of(norms[i : i + 1, :]) for i in range(6)]
    members += [high, count - high * 256.0]
    for i, member in enumerate(members):
        edge = jnp.where(tile_lane == i, member, edge)
    wide_shard[:, 4096:4224] = edge
    wide_shard[:, 4224:PLACE_AT] = jnp.zeros((24, PLACE_AT - 4224), F32)
    wide_shard[:, PLACE_AT:] = place[...]
    shards = (wide_shard, qkv_s, out_s, in_s, down_s)
    for m, (size, whole) in enumerate(SHAPES):
        half = whole // 2
        merge[m][pl.ds(pl.multiple_of(c * size, 8), size), :] = shards[m][:, pl.ds(pl.multiple_of(c * half, 128), half)]

    pl.semaphore_wait(barrier, 7)
    swaps = []
    for m in (E_, Q_, I_, D_, O_):
        size, half = SHAPES[m][0], SHAPES[m][1] // 2
        swaps.append(
            pltpu.make_async_remote_copy(
                src_ref=shards[m].at[:, pl.ds(pl.multiple_of((1 - c) * half, 128), half)],
                dst_ref=merge[m].at[pl.ds(pl.multiple_of(c * size, 8), size), :],
                send_sem=swap_send.at[m],
                recv_sem=swap_recv.at[m],
                device_id=peers[SIDE],
                device_id_type=MESH,
            )
        )
        swaps[-1].start()
    token_copies = []
    for i, (to_x, to_c) in enumerate(((x, 1 - c), (1 - x, c), (1 - x, 1 - c))):
        token_copies.append(
            pltpu.make_async_remote_copy(
                src_ref=pieces.at[to_x * 2 + to_c],
                dst_ref=land.at[seq],
                send_sem=token_send.at[i],
                recv_sem=token_recv.at[i],
                device_id=device(z, y, to_x, to_c),
                device_id_type=MESH,
            )
        )
        token_copies[-1].start()
    land[seq] = pieces[seq]

    def part(piece, k, half):
        m, skip, wide_part = PIECES[piece]
        size = 2 * SHAPES[m][0]
        start = pl.multiple_of(half * (SHAPES[m][1] // 2) + skip, 128)
        return weights[m].at[pl.ds(pl.multiple_of(k * size, size), size), pl.ds(start, wide_part)]

    FIRST_WAY, SECOND_WAY, SIDE_WAY, UP_WAY, DOWN_WAY = range(5)

    def copy_of(piece, k, way):
        ways = (XWAY, YWAY) if GATHER_WAY[piece] == 0 else (YWAY, XWAY)
        return pltpu.make_async_remote_copy(
            src_ref=part(piece, k, c),
            dst_ref=part(piece, k, c),
            send_sem=send_sem.at[piece, k, way],
            recv_sem=(side_recv if way == SIDE_WAY else link_recv).at[piece, k],
            device_id=peers[(ways + (SIDE, UP, DOWN))[way]],
            device_id_type=MESH,
        )

    def block_of(number):
        piece, task = number // 32, number % 32
        way = GATHER_WAY[piece]
        up, down = (UP_WAY, z < 3), (DOWN_WAY, z > 0)
        first, second, across = (FIRST_WAY, None), (SECOND_WAY, None), (SIDE_WAY, None)

        def of(last, earlier, t):
            to_y, to_x = (last, earlier) if way == 0 else (earlier, last)
            return chip(t, 1 - y if to_y else y, 1 - x if to_x else x)

        def onward(t):
            return (UP_WAY, (t < z) & (z < 3)), (DOWN_WAY, (t > z) & (z > 0))

        if task < 5:
            return piece, me, (up, down, None, first, second)[task : task + 1], False
        if way < 2:
            if task < 8:
                t = near_first(z, task - 4)
                return piece, of(0, 0, t), onward(t) + (first, second, across), True
            if task < 12:
                return piece, of(0, 1, near_first(z, task - 8)), (second, across), True
            return piece, of(1, (task - 12) % 2, near_first(z, (task - 12) // 2)), (across,), True
        if task == 5:
            return piece, of(0, 1, z), (second, up, down, across), True
        if task < 8:
            return piece, of(1, task - 6, z), (up, down, across), True
        t, place_of = near_first(z, 1 + (task - 8) // 4), (task - 8) % 4
        return piece, of(place_of // 2, place_of % 2, t), onward(t) + (across,), True

    def for_each_way(number, act):
        piece, k, ways, _ = block_of(number)
        for way, only in ways:
            if only is None:
                act(copy_of(piece, k, way))
            else:

                @pl.when(only)
                def _(way=way):
                    act(copy_of(piece, k, way))

    def transfer(number):
        piece, k, _, waits = block_of(number)
        if waits:
            copy_of(piece, k, FIRST_WAY).wait_recv()
        for_each_way(number, lambda copy: copy.start())

    def before(step, index, base=0):
        for (name, part_index), tasks in hooks.items():
            part_index = part_index - base
            if name != step or not tasks or (step == EMBED and not 0 <= part_index < 3):
                continue
            if index is None or isinstance(index, int):
                if part_index == (index or 0):
                    for number in tasks:
                        transfer(number)
            else:

                @pl.when(index == part_index)
                def _(tasks=tasks):
                    for number in tasks:
                        transfer(number)

    def need(*wanted):
        for piece in wanted:
            for k in range(16):
                pltpu.make_async_remote_copy(
                    src_ref=part(piece, k, 1 - c),
                    dst_ref=part(piece, k, 1 - c),
                    send_sem=send_sem.at[piece, k, SIDE_WAY],
                    recv_sem=side_recv.at[piece, k],
                    device_id=peers[SIDE],
                    device_id_type=MESH,
                ).wait_recv()

    for number, m in enumerate((E_, Q_, I_, D_, O_)):
        swaps[number].wait_recv()
        size, half = SHAPES[m][0], SHAPES[m][1] // 2
        rows = pl.ds(pl.multiple_of(me * 2 * size, 2 * size), 2 * size)
        weights[m][rows, pl.ds(pl.multiple_of(c * half, 128), half)] = merge[m][...].astype(BF16)
        for piece in range(6):
            if PIECES[piece][0] == m:
                copy_of(piece, me, SIDE_WAY).start()
    opening = hooks[(CHOOSE, 0)]
    while opening and opening[0] % 32 < 5:
        transfer(opening.pop(0))
    for copy in token_copies:
        copy.wait_recv()
    side[...] = jnp.zeros(side.shape, F32)
    keys[...] = jnp.zeros(keys.shape, jnp.int32)
    zeros = jnp.zeros((1, SPAN), F32)
    for b in range(5):
        tile = land[b]
        shift = b * SPAN * (1 - alone) if b < 4 else 0
        row = b * alone if b < 4 else 4
        spot = (lane + shift + PLACE_AT).astype(F32)
        row_lane = (lane * 0 + row).astype(F32)
        ids, targets, weight = (tile[i : i + 1].astype(F32) for i in (0, 2, 3))
        stacked = jnp.concatenate((ids, spot, targets, weight, row_lane, tile[5:6].astype(F32), zeros, zeros), 0)
        stacked = jnp.concatenate((stacked, jnp.zeros((120, SPAN), F32)), 0)
        cols[b * SPAN : (b + 1) * SPAN, :] = stacked.T.astype(jnp.int32)
        keys[0:1, b * SPAN : (b + 1) * SPAN] = tile[5:6]
        keys[1:2, b * SPAN : (b + 1) * SPAN] = lane * 0 + row
        keys[2:4, b * SPAN : (b + 1) * SPAN] = tile[2:4]
    set_bias(bias, cols, keys, last)
    found = [total_sum(member[...] * member[...]) for member in (tall, place, qkv_s, out_s, in_s, down_s)]
    norm_squares = jnp.sum(norms[...] * norms[...], 1, keepdims=True)
    squares[...] = lanes_of(found + [norm_squares[i : i + 1] for i in range(6)])

    turns, outs, out_count = {}, {}, [0]

    def turn_out(source, target, slot):
        if slot in turns:
            turns[slot].wait()

        def some(index):
            turned[slot, :, at(index, ROWS)] = source[at(index, ROWS), :].T

        each_unrolled(tokens // ROWS, some)
        turns[slot] = pltpu.make_async_copy(turned.at[slot], target, turn_sem.at[slot])
        turns[slot].start()

    def put_out(name, source, target):
        outs[name] = pltpu.make_async_copy(source, target, out_sem.at[out_count[0]])
        out_count[0] += 1
        outs[name].start()

    picks = (pick, pick_two)
    halves = [pl.ds(half * HALF, HALF) for half in range(2)]
    for half in range(2):

        def choose(index):
            column_lane = lax.broadcasted_iota(jnp.int32, (1, TILE), 1) + index * TILE
            hit = (cols[halves[half], 0:1] == column_lane) | (cols[halves[half], 1:2] == column_lane)
            picks[half][:, at(index, TILE)] = jnp.where(hit, 1.0, 0.0).astype(BF16)

        before(CHOOSE, half)
        each_unrolled(WIDE // TILE, choose)

    before(EMBED, 0)
    hooks.pop((EMBED, 0))
    need(1, 2)
    put_out("wide", wide, weight_outs[4])
    for half in range(2):

        def embed(index):
            before(EMBED, index, half * 3)
            value[halves[half], at(index, TILE)] = dot_nt(picks[half][...], wide[at(index, TILE), :])

        each_unrolled(D // TILE, embed)

    gains = wide[:, 4096:4224].astype(F32).T
    gains_out[...] = gains[0:16]
    counts = jnp.sum(gains[11:13], 1, keepdims=True) / 24.0
    mask_count = counts[0:1] * 256.0 + counts[1:2]
    count_out[...] = mask_count
    norm_rows = [gains_out[5 + i : 6 + i, :] for i in range(6)]
    before(NORM_A, None)

    def norm_a(index):
        rows = at(index, ROWS)
        found, normed, inverse = layer_norm(value[rows, :], norm_rows[0], norm_rows[1])
        value[rows, :] = found
        low_a[rows, :] = found.astype(BF16)
        na[rows, :] = normed
        put_lane(side, rows, 12, inverse)

    each_unrolled(tokens // ROWS, norm_a)
    put_out("na", na, na_out)
    before(PROJECT, 0)
    need(0)

    def project(index):
        before(PROJECT, index)
        qkv[:, at(index, TILE)] = dot_nn(low_a[...], qkv_w[:, at(index, TILE)]).astype(BF16)

    hooks.pop((PROJECT, 0))
    each_unrolled(3 * D // TILE, project)
    put_out("qkv", qkv, qkv_out)
    put_out("qkv_w", qkv_w, weight_outs[0])
    before(TURN_X, None)
    turn_out(low_a, x_t, 0)

    def attend_pair(pair):
        before(ATTEND, pair)
        for start, size in ((0, last), (last, SPAN)):
            rows = pl.ds(start, size)
            query = qkv[rows, at(pair, 128)]
            key = qkv[rows, pl.ds(D + pair * 128, 128)]
            val = qkv[rows, pl.ds(2 * D + pair * 128, 128)]
            mask = bias[...] if start == 0 else jnp.where(keys[0:1, last:tokens] > 0, 0.0, -1e30)
            mixed = []
            for first in (True, False):
                chosen = jnp.where(head_lanes(first), query, jnp.zeros_like(query))
                scores = dot_nt(chosen, key) * 0.125 + mask
                highest = jnp.max(scores, 1, keepdims=True)
                raised = jnp.exp(scores - highest)
                summed = jnp.sum(raised, 1, keepdims=True)
                shares = (raised * (1.0 / summed)).astype(BF16)
                mixed.append(dot_nn(shares, val))
                put_lane(side, rows, 2 * pair + (0 if first else 1), highest + jnp.log(summed))
            mix[rows, at(pair, 128)] = jnp.where(head_lanes(True), mixed[0], mixed[1]).astype(BF16)

    each_unrolled(HEADS // 2, attend_pair)
    before(OUT, 0)
    hooks.pop((OUT, 0))
    need(5)

    def out_project(index):
        before(OUT, index)
        value[:, at(index, TILE)] = value[:, at(index, TILE)] + dot_nn(mix[...], out_w[:, at(index, TILE)])

    each_unrolled(D // TILE, out_project)
    put_out("out_w", out_w, weight_outs[1])
    put_out("mix", mix, mix_out)
    before(NORM_B, None)

    def norm_b(index):
        rows = at(index, ROWS)
        found, normed, inverse = layer_norm(value[rows, :], norm_rows[2], norm_rows[3])
        value[rows, :] = found
        low_y[rows, :] = found.astype(BF16)
        nb[0][rows, :], nb[1][rows, :] = split_two(normed)
        put_lane(side, rows, 13, inverse)

    each_unrolled(tokens // ROWS, norm_b)
    put_out("a", low_y, a_out)
    put_out("nb0", nb[0], nb_outs[0])
    put_out("nb1", nb[1], nb_outs[1])
    before(FEED_IN, 0)
    hooks.pop((FEED_IN, 0))
    need(3)

    def feed_in(index):
        before(FEED_IN, index)
        hidden = dot_nn(low_y[...], in_w[:, at(index, TILE)])
        active, slant = gelu_pair(hidden)
        active = active.astype(BF16)
        act[:, at(index, TILE)] = active
        slope[:, at(index, TILE)] = slant.astype(BF16)

    each_unrolled(4 * D // TILE, feed_in)
    put_out("act", act, act_out)
    put_out("slope", slope, slope_out)
    put_out("in_w", in_w, weight_outs[2])
    before(TURN_A, None)
    before(FEED_OUT, 0)
    hooks.pop((FEED_OUT, 0))
    need(4)

    def feed_out(index):
        before(FEED_OUT, index)
        value[:, at(index, TILE)] = value[:, at(index, TILE)] + dot_nn(act[...], down_w[:, at(index, TILE)])

    each_unrolled(D // TILE, feed_out)
    put_out("down_w", down_w, weight_outs[3])
    before(REST, None)
    turns[0].wait()
    outs.pop("mix").wait()
    outs.pop("a").wait()

    def norm_c(index):
        rows = at(index, ROWS)
        found, normed, inverse = layer_norm(value[rows, :], norm_rows[4], norm_rows[5])
        low_a[rows, :] = found.astype(BF16)
        nc[0][rows, :], nc[1][rows, :] = split_two(normed)
        put_lane(side, rows, 14, inverse)

    each_unrolled(tokens // ROWS, norm_c)
    put_out("y", low_a, y_out)
    put_out("nc0", nc[0], nc_outs[0])
    put_out("nc1", nc[1], nc_outs[1])
    for swap in swaps:
        swap.wait_send()
    for copy in token_copies:
        copy.wait_send()
    for piece in range(6):
        copy_of(piece, me, SIDE_WAY).wait_send()
    for number in FRONT:
        if number < 1000:
            for_each_way(number, lambda copy: copy.wait_send())
    for copy in outs.values():
        copy.wait()


def front(large, lengths):
    vmem, hbm = pl.BlockSpec(memory_space=pltpu.VMEM), pl.BlockSpec(memory_space=pl.ANY)
    smem = pl.BlockSpec(memory_space=pltpu.SMEM)
    shape, dma = jax.ShapeDtypeStruct, pltpu.SemaphoreType.DMA
    tokens = 5 * SPAN
    small = [shape((1, 1), F32), shape((16, D), F32), shape((tokens, 128), F32)]
    small += [shape((tokens, 128), jnp.int32), shape((8, tokens), jnp.int32), shape((1, 128), F32)]
    out = [shape((D, tokens), BF16)] + [shape((tokens, width), BF16) for width in (D, D, 4 * D, D, 4 * D, 3 * D)]
    out += [shape((tokens, D), F32)] + [shape((tokens, D), BF16)] * 4
    out += [shape((32 * SHAPES[m][0], SHAPES[m][1]), BF16) for m in (Q_, O_, I_, D_, E_)]
    return pl.pallas_call(
        front_kernel,
        out_shape=small + out,
        in_specs=[hbm] * 13 + [smem] * 2,
        out_specs=[vmem] * len(small) + [hbm] * len(out),
        scratch_shapes=[pltpu.VMEM((32 * size, wide), BF16) for size, wide in SHAPES]
        + [pltpu.VMEM((tokens, D), F32)] * 2
        + [pltpu.VMEM((tokens, D), BF16)] * 3
        + [
            pltpu.VMEM((tokens, 3 * D), BF16),
            pltpu.VMEM((tokens, 4 * D), BF16),
            pltpu.VMEM((tokens, 4 * D), BF16),
            pltpu.VMEM((HALF, WIDE), BF16),
            pltpu.VMEM((HALF, WIDE), BF16),
            pltpu.VMEM((tokens - SPAN, tokens - SPAN), F32),
            pltpu.VMEM((1, D, tokens), BF16),
        ]
        + [pltpu.VMEM((tokens, D), BF16)] * 2
        + [pltpu.VMEM(member.shape, member.dtype) for member in large]
        + [pltpu.VMEM(SHAPES[E_], F32)]
        + [pltpu.VMEM((2 * size, wide // 2), F32) for size, wide in SHAPES]
        + [pltpu.VMEM((4, 8, SPAN), jnp.int32), pltpu.VMEM((5, 8, SPAN), jnp.int32)]
        + [dma((13,)), dma((5,)), dma((5,)), dma((3,)), dma((3,)), dma((6, 16, 5)), dma((6, 16)), dma((6, 16))]
        + [dma((18,)), dma((1,))],
        compiler_params=pltpu.CompilerParams(
            collective_id=0, has_side_effects=True, vmem_limit_bytes=63 * 1024 * 1024
        ),
    )(*large, *lengths)


PACK = 256


def split_two(value):
    high = value.astype(BF16)
    return high, (value - high.astype(F32)).astype(BF16)


def middle_kernel(*refs):
    (wide_h, qkv_wh, out_wh, in_wh, down_h, y_h, act_h, a_h, mix_h, slope_h, qkv_h, na_h) = refs[0:12]
    nb_h, nc_h = refs[12:14], refs[14:16]
    cols, keys, side, gains, count = refs[16:21]
    loss_out, norm_out = refs[21:23]
    glog_out, y_t, a_t, mix_t, act_t, ge_t, gffn_out, gh_out, gattn_out, gqkv_out = refs[23:33]
    wide, qkv_w, out_w, in_w, plain, qkv = refs[33:39]
    nb = refs[39:41]
    slope_ring, act_ring, down_ring = refs[41:44]
    logits, glog, gh, gffn, gattn, packed, grad, turned, act_turned = refs[44:53]
    back_kv, gqkv, whole_grad, pick, pick_t, bias, side_pack, side_turned, dq, ge = refs[53:63]
    load_sem, ring_sem, out_sem = refs[63:66]
    nc = (gqkv.at[:, D : 2 * D], gqkv.at[:, 2 * D : 3 * D])
    gatt = packed
    tokens = cols.shape[0]
    names = ("wide", "y", "nc0", "nc1", "in_w", "nb0", "nb1", "out_w", "qkv", "qkv_w")
    sources = (wide_h, y_h, nc_h[0], nc_h[1], in_wh, nb_h[0], nb_h[1], out_wh, qkv_h, qkv_wh)
    targets = (wide, plain, nc[0], nc[1], in_w, nb[0], nb[1], out_w, qkv, qkv_w)

    def na_copy(i):
        return pltpu.make_async_copy(
            na_h.at[:, at(i, TILE)], logits.at[pl.ds(i * tokens, tokens), :], load_sem.at[10 + i]
        )

    def tile_of(index):
        return pl.ds(index * PACK, PACK)

    loads = {name: pltpu.make_async_copy(sources[i], targets[i], load_sem.at[i]) for i, name in enumerate(names)}
    for name in ("y", "wide"):
        loads[name].start()

    weight_row = keys[3:4, :].astype(F32)
    weight_col = cols[:, 3:4].astype(F32)
    earlier = lax.broadcasted_iota(jnp.int32, (tokens, tokens), 0) < lax.broadcasted_iota(jnp.int32, (tokens, tokens), 1)
    later = lax.broadcasted_iota(jnp.int32, (tokens, tokens), 0) > lax.broadcasted_iota(jnp.int32, (tokens, tokens), 1)
    rank_row = dot_nn(
        jnp.broadcast_to(weight_row, (16, tokens)).astype(BF16), jnp.where(earlier, 1.0, 0.0).astype(BF16)
    )[0:1]
    rank_col = dot_nn(
        jnp.where(later, 1.0, 0.0).astype(BF16), jnp.broadcast_to(weight_col, (tokens, 128)).astype(BF16)
    )[:, 0:1]
    rank_row = jnp.where(weight_row > 0, rank_row, -1.0)
    rank_col = jnp.where(weight_col > 0, rank_col, -1.0)
    blocks = (jnp.sum(weight_row).astype(jnp.int32) + (PACK - 1)) // PACK
    blocks = jnp.maximum(blocks, 1)
    inverse_count = 1.0 / count[...]
    norm_rows = [gains[5 + i : 6 + i, :] for i in range(6)]
    loss_out[...] = jnp.zeros((1, 1), F32)
    norm_out[...] = jnp.zeros(norm_out.shape, F32)
    back_kv[...] = jnp.zeros(back_kv.shape, F32)
    whole_grad[...] = jnp.zeros(whole_grad.shape, F32)
    gqkv[:, 0:D] = jnp.zeros((tokens, D), BF16)
    side_first = side[...].astype(BF16)
    rest = side[...] - side_first.astype(F32)
    side_second = rest.astype(BF16)
    side_third = (rest - side_second.astype(F32)).astype(BF16)
    waited = set()

    def load_plain(source):
        return pltpu.make_async_copy(source, plain, load_sem.at[1])

    def ring(kind, source, target):
        def copy(j):
            piece = source.at[at(j, TILE), :] if kind == 2 else source.at[:, at(j, TILE)]
            return pltpu.make_async_copy(piece, target.at[j % 2], ring_sem.at[kind * 2 + j % 2])

        return copy

    rings = [ring(0, slope_h, slope_ring), ring(1, act_h, act_ring), ring(2, down_h, down_ring)]
    outs = [
        (glog, glog_out, 0),
        (turned.at[0], y_t, 1),
        (turned.at[1], a_t, 1),
        (turned.at[2], mix_t, 1),
        (act_turned, act_t, 1),
        (gffn, gffn_out, 0),
        (gh, gh_out, 0),
        (gattn, gattn_out, 0),
    ]

    def out_copy(i, block):
        source, target, axis = outs[i]
        place = at(block, PACK)
        return pltpu.make_async_copy(
            source, target.at[place, :] if axis == 0 else target.at[:, place], out_sem.at[i]
        )

    def wait_load(name):
        loads[name].wait()

    wait_load("wide")
    for name in names[2:]:
        loads[name].start()

    def block_step(block, carry):
        slot_col = lax.broadcasted_iota(jnp.int32, (PACK, 1), 0).astype(F32) + (block * PACK).astype(F32)
        slot_row = lax.broadcasted_iota(jnp.int32, (1, PACK), 1).astype(F32) + (block * PACK).astype(F32)
        hit = jnp.where(rank_row == slot_col, 1.0, 0.0)
        pick[...] = hit.astype(BF16)
        hit_t = jnp.where(rank_col == slot_row, 1.0, 0.0)
        pick_t[...] = hit_t.astype(BF16)
        target = jnp.sum(hit * keys[2:3, :].astype(F32), 1, keepdims=True)
        weight = jnp.sum(hit, 1, keepdims=True)
        row_col = cols[:, 4:5].astype(F32)
        row_of_token = jnp.sum(hit_t * row_col, 0, keepdims=True)
        bias[...] = jnp.where((row_of_token == row_col) & (cols[:, 5:6] > 0), 0.0, -1e30)
        side_pack[...] = (
            dot_nn(pick[...], side_first) + dot_nn(pick[...], side_second) + dot_nn(pick[...], side_third)
        )
        side_turned[...] = side_pack[...].T
        for kind in range(3):
            for j in range(2):
                rings[kind](j).start()
        load_plain(y_h).wait()
        packed[...] = dot_nn(pick[...], plain[...]).astype(BF16)
        load_plain(a_h).start()
        turned[0] = packed[...].T
        out_copy(1, block).start()

        def lanes(index):
            return (lax.broadcasted_iota(jnp.int32, (1, TILE), 1) + index * TILE).astype(F32)

        highest = jnp.full((PACK, 128), -1e30, F32)
        for index in range(TABLE_TILES):
            found = dot_nn(packed[...], wide[:, at(index, TILE)])
            if index == TABLE_TILES - 1:
                found = jnp.where(lanes(index) < VOCAB, found, -1e30)
            logits[tile_of(index), :] = found
            highest = jnp.maximum(highest, jnp.maximum(found[:, 0:128], found[:, 128:256]))
        highest = jnp.max(highest, 1, keepdims=True)
        summed, picked = jnp.zeros((PACK, 128), F32), jnp.zeros((PACK, 128), F32)
        for index in range(TABLE_TILES):
            found = logits[tile_of(index), :]
            raised = jnp.exp(found - highest)
            logits[tile_of(index), :] = raised
            own = jnp.where(lanes(index) == target, found, 0.0)
            summed = summed + raised[:, 0:128] + raised[:, 128:256]
            picked = picked + own[:, 0:128] + own[:, 128:256]
        summed = jnp.sum(summed, 1, keepdims=True)
        picked = jnp.sum(picked, 1, keepdims=True)
        loss_out[...] = loss_out[...] + jnp.sum(weight * (highest + jnp.log(summed) - picked), 0, keepdims=True)
        scale = weight * inverse_count
        share = scale / summed
        for index in range(TABLE_TILES):
            found = logits[tile_of(index), :] * share - jnp.where(lanes(index) == target, scale, 0.0)
            glog[:, at(index, TILE)] = found.astype(BF16)
        out_copy(0, block).start()
        for index in range(D // TILE):
            grad[:, at(index, TILE)] = dot_nt(glog[...], wide[at(index, TILE), 0:TABLE_END])

        @pl.when(block == 0)
        def _():
            for name in names[2:4]:
                wait_load(name)

        normed = dot_nn(pick[...], nc[0][...]) + dot_nn(pick[...], nc[1][...])
        found = grad[...]
        back = layer_norm_back(found, normed, lane_at(side_pack[...], 14), norm_rows[4])
        norm_out[4:5, :] = norm_out[4:5, :] + jnp.sum(found * normed, 0, keepdims=True)
        norm_out[5:6, :] = norm_out[5:6, :] + jnp.sum(found, 0, keepdims=True)
        grad[...] = back
        gffn[...] = back.astype(BF16)
        out_copy(5, block).start()

        load_plain(a_h).wait()
        turned[1] = dot_nn(pick[...], plain[...]).astype(BF16).T
        out_copy(2, block).start()
        load_plain(mix_h).start()
        for index in range(4 * D // TILE):
            for kind in range(3):
                rings[kind](index).wait()
            slant = dot_nn(pick[...], slope_ring[index % 2])
            found = dot_nt(gffn[...], down_ring[index % 2]) * slant
            gh[:, at(index, TILE)] = found.astype(BF16)
            act_turned[at(index, TILE), :] = dot_nn(pick[...], act_ring[index % 2]).astype(BF16).T
            if index + 2 < 4 * D // TILE:
                for kind in range(3):
                    rings[kind](index + 2).start()
        out_copy(6, block).start()
        out_copy(4, block).start()
        load_plain(mix_h).wait()
        turned[2] = dot_nn(pick[...], plain[...]).astype(BF16).T
        out_copy(3, block).start()
        load_plain(y_h).start()

        @pl.when(block == 0)
        def _():
            for name in names[4:8]:
                wait_load(name)

        for index in range(D // TILE):
            grad[:, at(index, TILE)] = grad[:, at(index, TILE)] + dot_nt(gh[...], in_w[at(index, TILE), :])
        normed = dot_nn(pick[...], nb[0][...]) + dot_nn(pick[...], nb[1][...])
        found = grad[...]
        back = layer_norm_back(found, normed, lane_at(side_pack[...], 13), norm_rows[2])
        norm_out[2:3, :] = norm_out[2:3, :] + jnp.sum(found * normed, 0, keepdims=True)
        norm_out[3:4, :] = norm_out[3:4, :] + jnp.sum(found, 0, keepdims=True)
        gattn[...] = back.astype(BF16)
        out_copy(7, block).start()
        high, low = split_two(back)
        whole_grad[...] = whole_grad[...] + dot_nn(pick_t[...], high) + dot_nn(pick_t[...], low)
        for index in range(D // TILE):
            gatt[:, at(index, TILE)] = dot_nt(gattn[...], out_w[at(index, TILE), :]).astype(BF16)

        @pl.when(block == 0)
        def _():
            wait_load("qkv")

        def attend_pair_back(pair):
            spots = [pl.ds(i * D + pair * 128, 128) for i in range(3)]
            query = dot_nn(pick[...], qkv[:, spots[0]]).astype(BF16)
            key, val = qkv[:, spots[1]], qkv[:, spots[2]]
            given = gatt[:, at(pair, 128)]
            key_t = key.T
            found = []
            for first in (True, False):
                lanes_here = head_lanes(first)
                chosen = jnp.where(lanes_here, query, jnp.zeros_like(query))
                mine = jnp.where(lanes_here, given, jnp.zeros_like(given))
                total = side_turned[pl.ds(2 * pair + (0 if first else 1), 1), :]
                shares = jnp.exp(dot_nt(key, chosen) * 0.125 + bias[...] - total)
                grad_share = dot_nt(val, mine)
                middle = jnp.sum(shares * grad_share, 0, keepdims=True)
                grad_score = (shares * (grad_share - middle)).astype(BF16)
                found.append(
                    (
                        dot_nn(key_t, grad_score) * 0.125,
                        dot_nn(grad_score, query) * 0.125,
                        dot_nn(shares.astype(BF16), given),
                    )
                )
            lanes_here = head_lanes(True)
            both = jnp.concatenate((found[0][0][0:HEAD_DIM], found[1][0][HEAD_DIM:]), 0)
            dq[at(pair, 128), :] = both.astype(BF16)
            for i in (1, 2):
                spot = pl.ds((i - 1) * D + pair * 128, 128)
                back_kv[:, spot] = back_kv[:, spot] + jnp.where(lanes_here, found[0][i], found[1][i])

        each_unrolled(HEADS // 2, attend_pair_back)
        gqkv[:, 0:D] = (gqkv[:, 0:D].astype(F32) + dot_nt(pick_t[...], dq[...])).astype(BF16)
        for i in range(len(outs)):
            out_copy(i, block).wait()
        return carry

    lax.fori_loop(0, blocks, block_step, 0)
    load_plain(y_h).wait()
    for i in range(D // TILE):
        na_copy(i).start()
    gqkv[:, D:] = back_kv[...].astype(BF16)
    copy_qkv = pltpu.make_async_copy(gqkv, gqkv_out, out_sem.at[8])
    copy_qkv.start()
    for ref in (glog, gffn, gh, gattn):
        ref[...] = jnp.zeros(ref.shape, BF16)
    for block in range(1, 3):

        @pl.when(blocks <= block)
        def _():
            for i in range(len(outs)):
                out_copy(i, block).start()

    wait_load("qkv_w")
    for index in range(D // TILE):
        whole_grad[:, at(index, TILE)] = whole_grad[:, at(index, TILE)] + dot_nt(gqkv[...], qkv_w[at(index, TILE), :])
    for i in range(D // TILE):
        na_copy(i).wait()
    zero = jnp.zeros((1, D), F32)

    def norm_a_back(index, carry):
        gain, shift = carry
        rows = at(index, ROWS)
        inverse = lane_at(side[rows, :], 12)
        found = whole_grad[rows, :]
        normed = jnp.concatenate(
            [logits[pl.ds(i * tokens + index * ROWS, ROWS), :] for i in range(D // TILE)], 1
        )
        ge[:, rows] = layer_norm_back(found, normed, inverse, norm_rows[0]).astype(BF16).T
        return gain + jnp.sum(found * normed, 0, keepdims=True), shift + jnp.sum(found, 0, keepdims=True)

    gain, shift = zero, zero
    for index in range(tokens // ROWS):
        gain, shift = norm_a_back(index, (gain, shift))
    norm_out[0:1, :] = gain
    norm_out[1:2, :] = shift
    copy_ge = pltpu.make_async_copy(ge, ge_t, out_sem.at[9])
    copy_ge.start()
    for block in range(1, 3):

        @pl.when(blocks <= block)
        def _():
            for i in range(len(outs)):
                out_copy(i, block).wait()

    copy_qkv.wait()
    copy_ge.wait()


def middle(large, small):
    tokens = 5 * SPAN
    slots = 3 * PACK
    vmem, hbm = pl.BlockSpec(memory_space=pltpu.VMEM), pl.BlockSpec(memory_space=pl.ANY)
    shape, dma = jax.ShapeDtypeStruct, pltpu.SemaphoreType.DMA
    out = [shape((slots, TABLE_END), BF16)] + [shape((D, slots), BF16)] * 3 + [shape((4 * D, slots), BF16)]
    out += [shape((D, tokens), BF16), shape((slots, D), BF16), shape((slots, 4 * D), BF16), shape((slots, D), BF16)]
    out += [shape((tokens, 3 * D), BF16)]

    def rows(count, width, kind=BF16):
        return pltpu.VMEM((count, width), kind)

    scratch = [rows(D, WIDE), rows(D, 3 * D), rows(D, D), rows(D, 4 * D), rows(tokens, D), rows(tokens, 3 * D)]
    scratch += [rows(tokens, D)] * 2
    scratch += [pltpu.VMEM((2, tokens, TILE), BF16)] * 2 + [pltpu.VMEM((2, TILE, D), BF16)]
    scratch += [rows(PACK * TABLE_TILES, TILE, F32), rows(PACK, TABLE_END), rows(PACK, 4 * D)] + [rows(PACK, D)] * 3
    scratch += [rows(PACK, D, F32), pltpu.VMEM((3, D, PACK), BF16), rows(4 * D, PACK)]
    scratch += [rows(tokens, 2 * D, F32), rows(tokens, 3 * D), rows(tokens, D, F32), rows(PACK, tokens)]
    scratch += [rows(tokens, PACK), rows(tokens, PACK, F32), rows(PACK, 128, F32), rows(128, PACK, F32)]
    scratch += [rows(D, PACK), rows(D, tokens)]
    scratch += [dma((13,)), dma((6,)), dma((10,))]
    return pl.pallas_call(
        middle_kernel,
        out_shape=[shape((1, 1), F32), shape((6, D), F32)] + out,
        in_specs=[hbm] * 16 + [vmem] * 5,
        out_specs=[vmem] * 2 + [hbm] * len(out),
        scratch_shapes=scratch,
        compiler_params=pltpu.CompilerParams(vmem_limit_bytes=63 * 1024 * 1024),
    )(*large, *small)


LEFT = 768
PIECES = ((Q_, 0, 1152), (E_, 0, 1280), (E_, 1280, 1152), (I_, 0, 1536), (D_, 0, 384), (O_, 0, 384))
SUM_WAY = (3, 1, 1, 2, 0, 0)
GATHER_WAY = (0, 1, 0, 2, 1, 0)
TASKS = (
    129, 0, 1, 96, 7, 5, 6, 4, 97, 13, 102, 103, 11, 128, 101, 12, 9, 8,
    132, 3, 104, 105, 2, 100, 108, 64, 14, 65, 71, 15, 111, 70, 134, 160, 106, 72,
    136, 161, 68, 10, 140, 135, 107, 73, 130, 110, 109, 33, 168, 166, 76, 137, 141, 143,
    139, 69, 173, 133, 77, 32, 169, 172, 144, 38, 164, 66, 40, 75, 39, 138, 176, 131,
    44, 36, 41, 142, 98, 167, 79, 34, 37, 80, 45, 165, 145, 47, 43, 74, 162, 67,
    48, 16, 171, 78, 35, 42, 46, 174, 99, 112, 81, 170, 163, 175, 17, 49, 113, 177,
)


def reduce_kernel(*refs):
    given, (cols, norm_sums, loss, squares) = refs[0:11], refs[11:15]
    y_t, ge_t, glog, x_t, gqkv, mix_t, gattn, a_t, gh, act_t, gffn = given
    lane_olds, side_olds, moment = refs[15:21], refs[21:27], refs[27]
    outs, sums_out, totals_out = refs[28:33], refs[33], refs[34]
    own, side, first, second, column, fin = (refs[35 + 6 * i : 41 + 6 * i] for i in range(6))
    left, (glog_v, gqkv_v, gattn_v, gh_v, gffn_v), stage, tails, norm_t = refs[71:78], refs[78:83], refs[83], refs[84], refs[85]
    lane_plane, lane_z, lane_halves = refs[86:89]
    scalar_sums, total_sums = refs[89:91], refs[91:93]
    load_sem, ring_sem, tail_sem, side_recv, first_send, first_recv, second_send, second_recv = refs[93:101]
    z_send, z_recv, swap_send, swap_recv = refs[101:105]
    lane_send, lane_recv, scalar_send, scalar_recv, total_send, total_recv = refs[105:111]
    z, y, x, c = here()
    peers = all_peers()
    me = chip(z, y, x)

    barrier = pltpu.get_barrier_semaphore()
    spot = y * 2 + x
    column_peers = [device((z + 1 + i) % 4, y, x, c) for i in range(3)]
    plane = [(y, 1 - x), (1 - y, x), (1 - y, 1 - x)]
    plane_peers = [device(z, to_y, to_x, c) for to_y, to_x in plane]
    greeted = column_peers + plane_peers + [device(z, to_y, to_x, 1 - c) for to_y, to_x in [(y, x)] + plane]
    for peer in greeted:
        pl.semaphore_signal(barrier, inc=1, device_id=peer, device_id_type=MESH)

    tokens = cols.shape[0]

    def act_part(group):
        return act_t.at[pl.ds(LEFT * group, LEFT), 0:tokens]

    operands = (
        ((x_t, left[1]), (gqkv, gqkv_v)),
        ((y_t.at[:, 0:tokens], left[2]), (ge_t, left[3]), (glog.at[0:tokens, :], glog_v)),
        (),
        ((a_t.at[:, 0:tokens], left[0]), (gh.at[0:tokens, :], gh_v)),
        ((gffn.at[0:tokens, :], gffn_v), (act_part(0), left[5]), (act_part(1), left[6])),
        ((mix_t.at[:, 0:tokens], left[4]), (gattn.at[0:tokens, :], gattn_v)),
    )
    loads = {}
    waited = set()
    for task in TASKS:
        piece = task // 32 if task // 32 != 2 else 1
        if piece not in loads:
            loads[piece] = []
            for source, target in operands[piece]:
                number = sum(len(member) for member in loads.values())
                loads[piece].append(pltpu.make_async_copy(source, target, load_sem.at[number]))
                loads[piece][-1].start()

    def loaded(piece):
        piece = 1 if piece == 2 else piece
        if piece not in waited:
            waited.add(piece)
            for member in loads[piece]:
                member.wait()

    norm_t[...] = jnp.zeros(norm_t.shape, F32)
    norm_t[5:11, :] = norm_sums[...]
    pl.semaphore_wait(barrier, 10)

    def size_of(piece):
        return 2 * SHAPES[PIECES[piece][0]][0]

    def slot(ref, piece, index):
        size = size_of(piece)
        return ref[piece].at[pl.ds(pl.multiple_of(index * size, size), size), :]

    def half_of(piece):
        return SHAPES[PIECES[piece][0]][1] // 2

    def chosen(start):
        lane = lax.broadcasted_iota(jnp.int32, (1, TILE), 1) + start
        hit = (cols[:, 0:1] == lane) | (cols[:, 1:2] == lane)
        return jnp.where(hit, 1.0, 0.0).astype(BF16)

    def ring_copy(piece, rows, lanes, number, index):
        place = lax.rem(number, 3)
        return pltpu.make_async_remote_copy(
            src_ref=stage.at[place],
            dst_ref=side[piece].at[rows, lanes],
            send_sem=ring_sem.at[place],
            recv_sem=side_recv.at[piece, index],
            device_id=peers[SIDE],
            device_id_type=MESH,
        )

    def tail_copy(piece, rows, lanes, number, index):
        return pltpu.make_async_remote_copy(
            src_ref=tails.at[number],
            dst_ref=side[piece].at[rows, lanes],
            send_sem=tail_sem.at[number],
            recv_sem=side_recv.at[piece, index],
            device_id=peers[SIDE],
            device_id_type=MESH,
        )

    whole = pl.ds(0, LEFT)
    ring_count, tail_count = [0], [0]

    def give(piece, rows, lanes, number, index):
        def before():
            @pl.when(number >= 3)
            def _():
                ring_copy(piece, rows, lanes, number, index).wait_send()

        def write(value):
            stage[lax.rem(number, 3)] = value.astype(BF16)

        return before, write, lambda: ring_copy(piece, rows, lanes, number, index).start()

    def keep(piece, rows, lanes):
        def write(value):
            own[piece][rows, lanes] = value.astype(BF16)

        return lambda: None, write, lambda: None

    def plain(piece, mine, source, right, group):
        wide = PIECES[piece][2]
        half = c if mine else 1 - c
        rows = pl.ds(LEFT * group, LEFT)
        base = ring_count[0]

        def step(j):
            lanes = at(j, TILE)
            before, write, after = keep(piece, rows, lanes) if mine else give(
                piece, rows, lanes, base + j, group * (wide // TILE) + j
            )
            before()
            write(dot_nn(source[...], right[:, pl.ds(pl.multiple_of(half * wide + j * TILE, 128), TILE)]))
            after()

        each(wide // TILE, step)
        if not mine:
            ring_count[0] += wide // TILE
        if wide % TILE:
            start = wide - 128
            value = dot_nn(source[...], right[:, pl.ds(pl.multiple_of(half * wide + start, 128), 128)])
            if mine:
                own[piece][rows, start:wide] = value.astype(BF16)
            else:
                number = tail_count[0]
                tail_count[0] += 1
                groups = SHAPES[PIECES[piece][0]][0] // 24
                tails[number] = value.astype(BF16)
                tail_copy(piece, rows, pl.ds(start, 128), number, groups * (wide // TILE) + group).start()

    def wide_product(piece, mine):
        half = c if mine else 1 - c
        wide, skip, width = half_of(piece), PIECES[piece][1], PIECES[piece][2]
        base = ring_count[0]

        def start_of(j):
            return pl.multiple_of(half * wide + skip + j * TILE, 128)

        def both(j, size=TILE):
            return dot_nn(left[2][...], glog_v[:, pl.ds(start_of(j), size)]) + dot_nn(
                left[3][...], chosen(start_of(j))[:, 0:size]
            )

        def target(j):
            lanes = at(j, TILE)
            return keep(piece, whole, lanes) if mine else give(piece, whole, lanes, base + j, j)

        def step(j):
            before, write, after = target(j)
            before()
            write(both(j))
            after()

        if not mine:
            ring_count[0] += width // TILE
        if skip == 0:
            each(width // TILE, step)
            return
        each(1, step)
        before, write, after = target(1)
        before()
        norm_part = jnp.where(half == 1, norm_t[...], 0.0).T
        write(both(1) + jnp.concatenate((jnp.zeros((LEFT, TILE - 128), F32), norm_part), 1))
        after()

        def by_half(j, size, write):
            @pl.when(half == 0)
            def _():
                write(both(j, size))

            @pl.when(half == 1)
            def _():
                write(dot_nn(left[3][...], chosen(start_of(j))[:, 0:size]))

        for j in (2, 3):
            before, write, after = target(j)
            before()
            by_half(j, TILE, write)
            after()

        def write_tail(value):
            if mine:
                own[piece][whole, width - 128 : width] = value.astype(BF16)
            else:
                tails[tail_count[0]] = value.astype(BF16)

        by_half(4, 128, write_tail)
        if not mine:
            tail_copy(piece, whole, pl.ds(width - 128, 128), tail_count[0], width // TILE).start()
            tail_count[0] += 1

    def products(piece, mine):
        loaded(piece)
        if piece in (1, 2):
            wide_product(piece, mine)
        elif piece == 4:
            if not mine:
                for group in range(4):
                    source = left[5 + group % 2]
                    if group >= 2:
                        loads[piece][1 + group % 2].wait()
                    plain(piece, False, source, gffn_v, group)
                    plain(piece, True, source, gffn_v, group)
                    if group < 2:
                        again = pltpu.make_async_copy(act_part(group + 2), source, load_sem.at[12 + group])
                        again.start()
                        loads[piece][1 + group] = again
        else:
            source, right = {0: (left[1], gqkv_v), 3: (left[0], gh_v), 5: (left[4], gattn_v)}[piece]
            plain(piece, mine, source, right, 0)

    def combine(piece, target, parts):
        def some(rows, lanes):
            total = parts[0][rows, lanes].astype(F32)
            for member in parts[1:]:
                total = total + member[rows, lanes].astype(F32)
            target[rows, lanes] = total.astype(target.dtype)

        wide = PIECES[piece][2]
        if piece == 4:
            each(4, lambda group: some(at(group, 48), slice(0, wide)))
            return
        if wide >= 512:
            each(wide // 512, lambda j: some(slice(0, 48), at(j, 512)))
        if wide % 512:
            some(slice(0, 48), slice(wide // 512 * 512, wide))

    def hop(piece, k, land, index, sems, way):
        return pltpu.make_async_remote_copy(
            src_ref=slot(own, piece, k),
            dst_ref=slot(land, piece, index),
            send_sem=sems[0].at[piece, index],
            recv_sem=sems[1].at[piece, index],
            device_id=peers[way],
            device_id_type=MESH,
        )

    FIRST, SECOND = (first_send, first_recv), (second_send, second_recv)

    def landed(piece, land, index, sems):
        hop(piece, me, land, index, sems, XWAY).wait_recv()

    def block(piece, a, b, far):
        return chip(far, a, b) if SUM_WAY[piece] % 2 == 0 else chip(far, b, a)

    def split(piece):
        return (y, x, YWAY, XWAY) if SUM_WAY[piece] % 2 == 0 else (x, y, XWAY, YWAY)

    readied = set()

    def ready(piece):
        if piece in readied:
            return
        readied.add(piece)
        wide, groups = PIECES[piece][2], SHAPES[PIECES[piece][0]][0] // 24
        for group in range(groups):
            for j in range(wide // TILE):
                ring_copy(piece, pl.ds(LEFT * group, LEFT), at(j, TILE), 0, group * (wide // TILE) + j).wait_recv()
            if wide % TILE:
                index = groups * (wide // TILE) + group
                tail_copy(piece, pl.ds(LEFT * group, LEFT), pl.ds(wide - 128, 128), 0, index).wait_recv()

    def both_cores(piece, k):
        return (slot(own, piece, k), slot(side, piece, k))

    def first_block(piece, i):
        a, b, way, _ = split(piece)
        t, v = (z + i // 2) % 4, (1 - b) if i % 2 == 0 else b
        return block(piece, 1 - a, v, t), 2 * t + v, way

    def first_send_of(piece, i):
        ready(piece)
        k, index, way = first_block(piece, i)
        combine(piece, slot(own, piece, k), both_cores(piece, k))
        hop(piece, k, first, index, FIRST, way).start()

    def second_block(piece, i):
        a, b, _, way = split(piece)
        if SUM_WAY[piece] > 1:
            return block(piece, a, 1 - b, z), 0, way
        t = (z + i) % 4
        return block(piece, a, 1 - b, t), t, way

    def z_slots(piece, v):
        for i in range(3):
            t = (z + 1 + i) % 4
            index = t if v is None else 2 * t + v
            pltpu.make_async_remote_copy(
                src_ref=slot(own, piece, me),
                dst_ref=slot(column, piece, index),
                send_sem=z_send.at[piece, index],
                recv_sem=z_recv.at[piece, index],
                device_id=column_peers[i],
                device_id_type=MESH,
            ).wait_recv()
        return tuple(
            slot(column, piece, (z + 1 + i) % 4 if v is None else 2 * ((z + 1 + i) % 4) + v) for i in range(3)
        )

    def first_slot(piece, v, t):
        landed(piece, first, 2 * t + v, FIRST)
        return (slot(first, piece, 2 * t + v),)

    def second_slot(piece, index):
        landed(piece, second, index, SECOND)
        return (slot(second, piece, index),)

    def second_send_of(piece, i):
        k, index, way = second_block(piece, i)
        other = 1 - split(piece)[1]
        if SUM_WAY[piece] > 1:
            parts = first_slot(piece, other, z) + z_slots(piece, other)
        else:
            parts = first_slot(piece, other, index)
        combine(piece, slot(own, piece, k), both_cores(piece, k) + parts)
        hop(piece, k, second, index, SECOND, way).start()

    def z_block(piece, i):
        a, b, _, _ = split(piece)
        if SUM_WAY[piece] > 1:
            t, v = (z + 1 + i // 2) % 4, (1 - b) if i % 2 == 0 else b
            return block(piece, a, v, t), t, v, 2 * z + v, 2 * t + v, column_peers[i // 2]
        t = (z + 1 + i) % 4
        return chip(t, y, x), t, None, z, t, column_peers[i]

    def z_copy(piece, i):
        k, _, _, there, number, peer = z_block(piece, i)
        return pltpu.make_async_remote_copy(
            src_ref=slot(own, piece, k),
            dst_ref=slot(column, piece, there),
            send_sem=z_send.at[piece, number],
            recv_sem=z_recv.at[piece, there],
            device_id=peer,
            device_id_type=MESH,
        )

    def z_send_of(piece, i):
        k, t, v, _, _, _ = z_block(piece, i)
        if v is None:
            parts = first_slot(piece, split(piece)[1], t) + second_slot(piece, t)
        else:
            parts = first_slot(piece, v, t)
        combine(piece, slot(own, piece, k), both_cores(piece, k) + parts)
        z_copy(piece, i).start()

    swaps = []

    def finish(piece):
        mine = split(piece)[1]
        parts = both_cores(piece, me) + first_slot(piece, mine, z)
        if SUM_WAY[piece] > 1:
            parts = parts + z_slots(piece, mine) + second_slot(piece, 0)
        else:
            parts = parts + second_slot(piece, z) + z_slots(piece, None)
        combine(piece, fin[piece], parts)
        m, skip, wide = PIECES[piece]
        size = SHAPES[m][0]
        lanes = pl.ds(pl.multiple_of(c * half_of(piece) + skip, 128), wide)
        swaps.append(
            pltpu.make_async_remote_copy(
                src_ref=fin[piece].at[pl.ds(pl.multiple_of((1 - c) * size, 8), size), :],
                dst_ref=outs[m].at[:, lanes],
                send_sem=swap_send.at[piece],
                recv_sem=swap_recv.at[piece],
                device_id=peers[SIDE],
                device_id_type=MESH,
            )
        )
        swaps[-1].start()
        squared = fin[piece][...] * fin[piece][...] + SQUARE_FLOOR
        lane_plane[spot, :, HALF_AT[m] + skip : HALF_AT[m] + skip + wide] = jnp.sum(squared, 0, keepdims=True)
        outs[m][:, lanes] = fin[piece][pl.ds(pl.multiple_of(c * size, 8), size), :]

    for task in TASKS:
        piece, number = task // 32, task % 32
        if number < 2:
            products(piece, number == 1)
        elif number < 10:
            first_send_of(piece, number - 2)
        elif number == 17:
            finish(piece)
        elif SUM_WAY[piece] > 1:
            if number < 16:
                z_send_of(piece, number - 10)
            else:
                second_send_of(piece, 0)
        elif number < 14:
            second_send_of(piece, number - 10)
        else:
            z_send_of(piece, number - 14)

    def spread(source, target, send, recv, peer):
        copy = pltpu.make_async_remote_copy(
            src_ref=source, dst_ref=target, send_sem=send, recv_sem=recv, device_id=peer, device_id_type=MESH
        )
        copy.start()
        return copy

    def arrive(copies):
        for copy in copies:
            copy.wait_recv()
        return copies

    plane_copies = [
        spread(lane_plane.at[spot], lane_plane.at[spot], lane_send.at[i], lane_recv.at[i], plane_peers[i])
        for i in range(3)
    ]
    for swap in swaps:
        swap.wait()
    sides, gs = statistics(outs, side_olds)

    def spread_eight(buffers, value, send, recv):
        buffers[0][2 * spot + c] = value
        mine = buffers[0].at[2 * spot + c]
        return [spread(mine, mine, send.at[i], recv.at[i], greeted[3 + i]) for i in range(7)]

    def spread_four(buffers, send, recv):
        total = [buffers[0][2 * i] + buffers[0][2 * i + 1] for i in range(4)]
        buffers[1][z] = (total[0] + total[1]) + (total[2] + total[3])
        mine = buffers[1].at[z]
        return [spread(mine, mine, send.at[7 + i], recv.at[7 + i], column_peers[i]) for i in range(3)]

    def four(buffer):
        return (buffer[0] + buffer[1]) + (buffer[2] + buffer[3])

    scalars = lanes_of([jnp.sum(member, 0, keepdims=True) for member in sides] + [loss[...]])
    scalars = jnp.concatenate((scalars, squares[...]), 1)
    sent = spread_eight(scalar_sums, scalars, scalar_send, scalar_recv)
    sent += arrive(plane_copies)
    lane_z[z] = four(lane_plane)
    z_copies = [
        spread(lane_z.at[z], lane_z.at[z], lane_send.at[3 + i], lane_recv.at[3 + i], column_peers[i]) for i in range(3)
    ]
    arrive(sent[0:7])
    last_copies = spread_four(scalar_sums, scalar_send, scalar_recv)
    sent += arrive(z_copies)
    lane_halves[c] = four(lane_z)
    halves_copy = spread(lane_halves.at[c], lane_halves.at[c], lane_send.at[6], lane_recv.at[6], peers[SIDE])
    sent += arrive(last_copies)
    sent += arrive([halves_copy])
    pair = (lane_halves[0], lane_halves[1])
    lanes = [half[:, HALF_AT[m] : HALF_AT[m] + SHAPES[m][1] // 2] for m in range(5) for half in pair]
    sums = jnp.concatenate(lanes + [four(scalar_sums[1])], 1)
    sums_out[...] = sums
    updates = updates_of(sums, gs, sides, lane_olds, moment)[0]
    totals = lanes_of(
        [total_sum(update * update) for update in updates[:6]]
        + [jnp.sum(updates[6][i : i + 1] * updates[6][i : i + 1], 1, keepdims=True) for i in range(6)]
    )
    sent += arrive(spread_eight(total_sums, totals, total_send, total_recv))
    sent += arrive(spread_four(total_sums, total_send, total_recv))
    totals_out[...] = four(total_sums[1])
    for copy in sent:
        copy.wait_send()
    for piece in range(6):
        for i in range(8):
            k, index, way = first_block(piece, i)
            hop(piece, k, first, index, FIRST, way).wait_send()
        for i in range(1 if SUM_WAY[piece] > 1 else 4):
            k, index, way = second_block(piece, i)
            hop(piece, k, second, index, SECOND, way).wait_send()
        for i in range(6 if SUM_WAY[piece] > 1 else 3):
            z_copy(piece, i).wait_send()
    for number in range(ring_count[0] - 3, ring_count[0]):
        ring_copy(1, whole, pl.ds(0, TILE), number, 0).wait_send()
    for number in range(tail_count[0]):
        tail_copy(1, whole, pl.ds(0, 128), number, 0).wait_send()


def statistics(grads, side_olds):
    wide_g = grads[E_][...]
    gs = (wide_g[:, :VOCAB], wide_g[:, PLACE_AT:]) + tuple(grads[m][...] for m in (Q_, O_, I_, D_))
    decay = 1.0 - STEP ** (-0.8)
    sides = []
    for index in range(6):
        mean = jnp.sum(gs[index] * gs[index] + SQUARE_FLOOR, 1, keepdims=True) / gs[index].shape[1]
        sides.append(decay * column_of(as_row(side_olds[index])) + (1.0 - decay) * mean)
    return sides, gs + (wide_g[:, 4096:4224],)


def updates_of(sums, gs, sides, lane_olds, moment):
    decay = 1.0 - STEP ** (-0.8)
    fresh = 1.0 - decay
    parts = [sums[:, :VOCAB], sums[:, PLACE_AT:WIDE]]
    parts += [sums[:, SUM_AT[i] : SUM_AT[i + 1]] for i in range(1, 5)]
    scalars = sums[:, SUM_AT[5] : SUM_AT[5] + 128]
    updates, lane_news = [], []
    for index in range(6):
        height = gs[index].shape[0] * 32
        lane_news.append(decay * as_row(lane_olds[index]) + fresh * (parts[index] / height))
        if index < 2:
            mean = jnp.sum(lane_news[index], 1, keepdims=True) / lane_news[index].shape[1]
        else:
            mean = lane_at(scalars, index) / height
        updates.append(gs[index] * lax.rsqrt(sides[index] * lane_news[index] / mean))
    norm_g = jnp.concatenate([row_of(lane_at(gs[6], NORM_AT - 4096 + i)) for i in range(6)], 0)
    moment_new = decay * moment[...] + fresh * (norm_g * norm_g + SQUARE_FLOOR)
    updates.append(norm_g * lax.rsqrt(moment_new))
    return updates, lane_news, norm_g, moment_new


def reduce_grads(large, small):
    tokens = 5 * SPAN
    vmem, hbm = pl.BlockSpec(memory_space=pltpu.VMEM), pl.BlockSpec(memory_space=pl.ANY)
    dma = pltpu.SemaphoreType.DMA
    scratch = []
    for counts in ((16, 16), (16, 16), (8, 8), (4, 1), (4, 8)):
        for (m, _, wide), way in zip(PIECES, SUM_WAY):
            scratch.append(pltpu.VMEM((counts[way // 2] * 2 * SHAPES[m][0], wide), BF16))
    scratch += [pltpu.VMEM((2 * SHAPES[m][0], wide), F32) for m, _, wide in PIECES]
    scratch += [pltpu.VMEM((LEFT, tokens), BF16)] * 7
    scratch += [pltpu.VMEM((tokens, width), BF16) for width in (TABLE_END, 3 * D, D, 4 * D, D)]
    scratch += [pltpu.VMEM((3, LEFT, TILE), BF16), pltpu.VMEM((7, LEFT, 128), BF16), pltpu.VMEM((128, D), F32)]
    scratch += [pltpu.VMEM((count, 1, HALF_SUMS), F32) for count in (4, 4, 2)]
    scratch += [pltpu.VMEM((count, 1, width), F32) for width in (256, 128) for count in (8, 4)]
    scratch += [dma((14,)), dma((3,)), dma((7,)), dma((6, 10)), dma((6, 8)), dma((6, 8)), dma((6, 4)), dma((6, 4))]
    scratch += [dma((6, 8)), dma((6, 8)), dma((6,)), dma((6,))]
    scratch += [dma((7,))] * 2 + [dma((10,))] * 4
    return pl.pallas_call(
        reduce_kernel,
        out_shape=[jax.ShapeDtypeStruct(shape, F32) for shape in SHAPES + ((1, SUMS), (1, 128))],
        in_specs=[hbm] * 11 + [vmem] * len(small),
        out_specs=[vmem] * 7,
        scratch_shapes=scratch,
        compiler_params=pltpu.CompilerParams(
            collective_id=1, has_side_effects=True, vmem_limit_bytes=63 * 1024 * 1024
        ),
    )(*large, *small)


def update_kernel(*refs):
    copies = [pltpu.make_async_copy(refs[i], refs[55 + i], refs[82].at[i]) for i in range(27)]
    for copy in copies:
        copy.start()
    for copy in copies:
        copy.wait()
    refs = refs[55:82] + refs[27:55]
    grads, sums, totals, ws, norms = refs[0:5], refs[5], refs[6], refs[7:13], refs[13]
    lane_olds, side_olds, moment = refs[14:20], refs[20:26], refs[26]
    loss_out, table_g, place_g, norm_g_out = refs[27:31]
    lane_outs, side_outs, moment_out, news, norm_new = refs[31:37], refs[37:43], refs[43], refs[44:50], refs[50]
    grad_outs = refs[51:55]
    sides, gs = statistics(grads, side_olds)
    updates, lane_news, norm_g, moment_new = updates_of(sums[...], gs, sides, lane_olds, moment)
    scalars = sums[:, SUM_AT[5] : SUM_AT[5] + 128]
    squares = sums[:, SUM_AT[5] + 128 :]
    loss_out[...] = lane_at(scalars, 6)
    table_g[...] = gs[0]
    place_g[...] = gs[1]
    norm_g_out[...] = norm_g
    moment_out[...] = moment_new
    for index in range(6):
        lane_outs[index][...] = lane_news[index].reshape(lane_outs[index].shape)
        side_outs[index][...] = row_of(sides[index]).reshape(side_outs[index].shape)
        if index >= 2:
            grad_outs[index - 2][...] = gs[index]
        entries = gs[index].shape[0] * gs[index].shape[1] * 32
        clip = jnp.maximum(1.0, jnp.sqrt(lane_at(totals[...], index) / entries))
        scale = learn_rate * jnp.sqrt(lane_at(squares, index) / entries) / clip
        news[index][...] = ws[index][...] - scale * updates[index]
    for i in range(6):
        clip = jnp.maximum(1.0, jnp.sqrt(lane_at(totals[...], 6 + i) / D))
        scale = learn_rate * jnp.sqrt(lane_at(squares, 6 + i) / D) / clip
        norm_new[i : i + 1, :] = norms[i : i + 1, :] - scale * updates[6][i : i + 1, :]


def update_weights(operands):
    lanes = (VOCAB, 512, 3 * D, D, 4 * D, D)
    held = (24, 24, 24, 24, 24, 96)
    shapes = [(1, 1), (24, VOCAB), (24, 512), (6, 24)]
    shapes += [(lane,) for lane in lanes] + [(size,) for size in held] + [(6, 24)]
    shapes += list(zip(held, lanes)) + [(6, 24)] + list(zip(held, lanes))[2:]
    return pl.pallas_call(
        update_kernel,
        out_shape=[jax.ShapeDtypeStruct(shape, F32) for shape in shapes],
        in_specs=[pl.BlockSpec(memory_space=pl.ANY)] * len(operands),
        out_specs=[pl.BlockSpec(memory_space=pltpu.VMEM)] * len(shapes),
        scratch_shapes=[pltpu.VMEM(member.shape, member.dtype) for member in operands]
        + [pltpu.SemaphoreType.DMA((len(operands),))],
        compiler_params=pltpu.CompilerParams(vmem_limit_bytes=63 * 1024 * 1024),
    )(*operands)


def norm_forward(value, gain, shift):
    centred = value - jnp.mean(value, -1, keepdims=True)
    inverse = lax.rsqrt(jnp.mean(centred * centred, -1, keepdims=True) + EPSILON)
    normed = centred * inverse
    return (normed * gain + shift, normed, inverse)


def norm_backward(grad_out, normed, inverse, gain):
    scaled = grad_out * gain
    back = inverse * (
        scaled
        - jnp.mean(scaled, -1, keepdims=True)
        - normed * jnp.mean(scaled * normed, -1, keepdims=True)
    )
    return (back, jnp.sum(grad_out * normed, 0), jnp.sum(grad_out, 0))


def mm(left, right, sides):
    return lax.dot_general(left, right, ((sides[:1], sides[1:]), ((), ())), preferred_element_type=F32)


def attend(qkv, allowed):
    by_head = qkv.reshape(qkv.shape[0], 3, HEADS, HEAD_DIM)
    query, key, value = by_head[:, 0], by_head[:, 1], by_head[:, 2]
    scores = jnp.einsum("qhe,khe->hqk", query, key, preferred_element_type=F32) * 0.125
    scores = jnp.where(allowed[None], scores, -1e30)
    highest = jnp.max(scores, -1, keepdims=True)
    raised = jnp.exp(scores - highest)
    summed = jnp.sum(raised, -1, keepdims=True)
    shares = (raised / summed).astype(BF16)
    mixture = jnp.einsum("hqk,khe->qhe", shares, value, preferred_element_type=F32)
    return mixture.astype(BF16).reshape(qkv.shape[0], D), highest + jnp.log(summed)


def attend_back(qkv, allowed, log_total, grad_mix):
    by_head = qkv.reshape(qkv.shape[0], 3, HEADS, HEAD_DIM)
    query, key, value = by_head[:, 0], by_head[:, 1], by_head[:, 2]
    grad_mix = grad_mix.reshape(qkv.shape[0], HEADS, HEAD_DIM)
    scores = jnp.einsum("qhe,khe->hqk", query, key, preferred_element_type=F32) * 0.125
    scores = jnp.where(allowed[None], scores, -1e30)
    shares = jnp.exp(scores - log_total)
    grad_share = jnp.einsum("qhe,khe->hqk", grad_mix, value, preferred_element_type=F32)
    grad_score = (shares * (grad_share - jnp.sum(shares * grad_share, -1, keepdims=True))).astype(BF16)
    grad_query = jnp.einsum("hqk,khe->qhe", grad_score, key, preferred_element_type=F32) * 0.125
    grad_key = jnp.einsum("hqk,qhe->khe", grad_score, query, preferred_element_type=F32) * 0.125
    grad_value = jnp.einsum("hqk,qhe->khe", shares.astype(BF16), grad_mix, preferred_element_type=F32)
    return jnp.stack((grad_query, grad_key, grad_value), 1).astype(BF16).reshape(qkv.shape)


def on_slice(token_arrays, lengths, weights, lane_olds, side_olds, moment):
    olds = lane_olds + side_olds + (moment,)
    found = front(token_arrays + weights, lengths)
    mask_count, gains, side, cols, keys, weight_sq = found[0:6]
    x_t, mix, a, act, y, slope, qkv_b, normed_a = found[6:14]
    normed_bc, (qkv_w, out_w, in_w, down_w, wide_w) = found[14:18], found[18:23]
    found = middle(
        (wide_w, qkv_w, out_w, in_w, down_w, y, act, a, mix, slope, qkv_b, normed_a) + tuple(normed_bc),
        (cols, keys, side, gains, mask_count),
    )
    loss_part, norm_sums = found[0:2]
    grad_logit, y_t, a_t, mix_t, act_t, ge_t, grad_ffn, grad_hidden, grad_attn, grad_qkv = found[2:]
    reduced = reduce_grads(
        (y_t, ge_t, grad_logit, x_t, grad_qkv, mix_t, grad_attn, a_t, grad_hidden, act_t, grad_ffn),
        (cols, norm_sums, loss_part, weight_sq) + olds,
    )
    found = update_weights(tuple(reduced) + weights + olds)
    grads = (None,) + tuple(found[24:28])
    mask_count = mask_count.reshape(())
    loss_sum, table_g, place_g, norm_g = found[0:4]
    lane_news = found[4:10]
    side_news = found[10:16]
    moment_new, norm_new = found[16], found[23]
    news = found[17:23]
    return (
        loss_sum.reshape(()),
        mask_count,
        table_g.T,
        place_g.T,
        grads[1],
        grads[2],
        grads[3],
        grads[4],
        norm_g.T,
        lane_news[0],
        side_news[0],
        lane_news[1],
        side_news[1],
        side_news[2],
        lane_news[2],
        side_news[3],
        lane_news[3],
        side_news[4],
        lane_news[4],
        side_news[5],
        lane_news[5],
        moment_new.T,
        news[0].T,
        news[1].T,
        news[2],
        news[3],
        news[4],
        news[5],
        norm_new.T,
    )


def on_device(
    whole_mesh,
    long_ids,
    long_targets,
    long_mask,
    long_lengths,
    short_ids,
    short_targets,
    short_mask,
    short_lengths,
    table,
    position,
    qkv_weight,
    out_weight,
    in_weight,
    down_weight,
    norms,
    table_rows,
    table_cols,
    position_rows,
    position_cols,
    qkv_rows,
    qkv_cols,
    out_rows,
    out_cols,
    in_rows,
    in_cols,
    down_rows,
    down_cols,
    norm_moment,
):
    if whole_mesh == (8, 4):
        return on_slice(
            (long_ids, long_targets, long_mask, short_ids, short_targets, short_mask),
            (long_lengths, short_lengths),
            (table.T, position.T, qkv_weight, out_weight, in_weight, down_weight, norms.T),
            (table_rows, position_rows, qkv_cols, out_cols, in_cols, down_cols),
            (table_cols, position_cols, qkv_rows, out_rows, in_rows, down_rows),
            norm_moment.T,
        )
    devices = lax.axis_size(("dp", "seq"))
    seq_index = lax.axis_index("seq")
    held = norms.shape[0]

    span = long_ids.shape[1]
    long_place = seq_index * span + lax.iota(jnp.int32, span)
    long_keep = (long_place[None, :] < long_lengths[:, None]).astype(jnp.int32)
    short_keep = (lax.iota(jnp.int32, SPAN)[None, :] < short_lengths[:, None]).astype(jnp.int32)
    long_pack = jnp.stack((long_ids, long_targets, long_mask * long_keep, long_keep), 1)
    short_pack = jnp.stack((short_ids, short_targets, short_mask * short_keep, short_keep), 1)
    moved = lax.all_to_all(
        jnp.concatenate((long_pack, short_pack[1:]), 0), "seq", split_axis=0, concat_axis=0, tiled=True
    )
    tokens = jnp.concatenate((moved, short_pack[:1]), 0)
    ids, targets, weight, keep = (tokens[:, i].reshape(-1) for i in range(4))
    weight = weight.astype(F32)
    count = tokens.shape[0] * span
    last = count - span
    alone = seq_index == lax.axis_size("seq") - 1
    token = lax.iota(jnp.int32, count)
    place = jnp.where(alone | (token >= last), token % span, token)
    row = jnp.where(alone | (token >= last), token // span, 0)
    allowed_long = (row[:last, None] == row[None, :last]) & (keep[None, :last] > 0)
    allowed_short = jnp.broadcast_to(keep[None, last:] > 0, (span, span))

    here_count = jnp.sum(long_pack[:, 2]) + jnp.sum(short_pack[:, 2])
    tall = table.T
    counts = jnp.broadcast_to(jnp.stack((here_count // 256, here_count % 256)).astype(F32)[None], (held, 2))
    wide_shard = jnp.concatenate(
        (tall, norms, counts, jnp.zeros((held, PLACE_AT - COUNT_AT - 2), F32), position.T), 1
    )
    shards = (wide_shard, qkv_weight, out_weight, in_weight, down_weight)
    wide_w, qkv_w, out_w, in_w, down_w = (
        lax.all_gather(shard.astype(BF16), ("dp", "seq"), axis=0, tiled=True) for shard in shards
    )
    column = lax.broadcasted_iota(jnp.int32, (1, WIDE), 1)
    chosen = ((ids[:, None] == column) | ((place[:, None] + PLACE_AT) == column)).astype(BF16)
    gains = wide_w[:, NORM_AT : NORM_AT + 6].astype(F32)
    sums = jnp.sum(wide_w[:, COUNT_AT : COUNT_AT + 2].astype(F32), 0)
    mask_count = (sums[0] * 256.0 + sums[1]) / held
    inverse_count = 1.0 / mask_count

    embedded = mm(chosen, wide_w, (1, 1))
    first, normed_a, inverse_a = norm_forward(embedded, gains[:, 0], gains[:, 1])
    first_b = first.astype(BF16)
    qkv_b = mm(first_b, qkv_w, (1, 0)).astype(BF16)
    mix_long, total_long = attend(qkv_b[:last], allowed_long)
    mix_short, total_short = attend(qkv_b[last:], allowed_short)
    mixture = jnp.concatenate((mix_long, mix_short), 0)
    second, normed_b, inverse_b = norm_forward(first + mm(mixture, out_w, (1, 0)), gains[:, 2], gains[:, 3])
    second_b = second.astype(BF16)
    hidden = mm(second_b, in_w, (1, 0))
    active, slope = gelu_pair(hidden)
    active_b = active.astype(BF16)
    third, normed_c, inverse_c = norm_forward(second + mm(active_b, down_w, (1, 0)), gains[:, 4], gains[:, 5])
    third_b = third.astype(BF16)
    logits = jnp.where(column < VOCAB, mm(third_b, wide_w, (1, 0)), -1e30)
    highest = jnp.max(logits, -1, keepdims=True)
    log_sum = highest + jnp.log(jnp.sum(jnp.exp(logits - highest), -1, keepdims=True))
    onehot = targets[:, None] == column
    picked = jnp.sum(jnp.where(onehot, logits, 0.0), -1)
    loss_part = jnp.sum(weight * (log_sum[:, 0] - picked))
    grad_logit = (
        (jnp.exp(logits - log_sum) - onehot.astype(F32)) * (weight * inverse_count)[:, None]
    ).astype(BF16)
    grad_third = mm(grad_logit, wide_w, (1, 1))
    grad_second, gain_c, shift_c = norm_backward(grad_third, normed_c, inverse_c, gains[:, 4])
    grad_ffn = grad_second.astype(BF16)
    down_grad = mm(active_b, grad_ffn, (0, 0)).astype(BF16)
    grad_hidden = (mm(grad_ffn, down_w, (1, 1)) * slope).astype(BF16)
    in_grad = mm(second_b, grad_hidden, (0, 0)).astype(BF16)
    grad_second = grad_second + mm(grad_hidden, in_w, (1, 1))
    grad_first, gain_b, shift_b = norm_backward(grad_second, normed_b, inverse_b, gains[:, 2])
    grad_attn = grad_first.astype(BF16)
    out_grad = mm(mixture, grad_attn, (0, 0)).astype(BF16)
    grad_mix = mm(grad_attn, out_w, (1, 1)).astype(BF16)
    grad_qkv = jnp.concatenate(
        (
            attend_back(qkv_b[:last], allowed_long, total_long, grad_mix[:last]),
            attend_back(qkv_b[last:], allowed_short, total_short, grad_mix[last:]),
        ),
        0,
    )
    qkv_grad = mm(first_b, grad_qkv, (0, 0)).astype(BF16)
    grad_first = grad_first + mm(grad_qkv, qkv_w, (1, 1))
    grad_embed, gain_a, shift_a = norm_backward(grad_first, normed_a, inverse_a, gains[:, 0])
    wide_grad = mm(
        jnp.concatenate((third_b, grad_embed.astype(BF16)), 0),
        jnp.concatenate((grad_logit, chosen), 0),
        (0, 0),
    )
    norm_part = jnp.stack((gain_a, shift_a, gain_b, shift_b, gain_c, shift_c), 1)
    wide_grad = lax.dynamic_update_slice(wide_grad.astype(BF16), norm_part.astype(BF16), (0, NORM_AT))
    grads = (wide_grad, qkv_grad, out_grad, in_grad, down_grad)
    wide_g, qkv_g, out_g, in_g, down_g = (
        lax.psum_scatter(grad.astype(F32), ("dp", "seq"), scatter_dimension=0, tiled=True) for grad in grads
    )
    table_g, place_g = wide_g[:, :VOCAB], wide_g[:, PLACE_AT:]
    norm_g = wide_g[:, NORM_AT : NORM_AT + 6]

    decay = 1.0 - STEP ** (-0.8)
    matrices = (
        (qkv_weight, qkv_g, qkv_rows, qkv_cols),
        (out_weight, out_g, out_rows, out_cols),
        (in_weight, in_g, in_rows, in_cols),
        (down_weight, down_g, down_rows, down_cols),
    )
    wide = (
        (tall, table_g, table_cols, table_rows),
        (position.T, place_g, position_cols, position_rows),
    )
    row_news = [
        decay * member[2] + (1.0 - decay) * jnp.mean(member[1] * member[1] + SQUARE_FLOOR, 1)
        for member in matrices + wide
    ]
    col_parts = [jnp.sum(member[1] * member[1] + SQUARE_FLOOR, 0) for member in matrices + wide]
    row_totals = jnp.stack([jnp.sum(rows_new) for rows_new in row_news])
    weight_sq = jnp.stack([jnp.sum(member[0] * member[0]) for member in matrices + wide])
    stats = lax.psum(
        col_parts + [row_totals, weight_sq, jnp.sum(norms * norms, 0), loss_part.reshape(1)], ("dp", "seq")
    )
    updates = []
    cols_out = []
    for index, member in enumerate(matrices + wide):
        full_rows = member[0].shape[0] * devices
        cols_new = decay * member[3] + (1.0 - decay) * stats[index] / full_rows
        if index < 4:
            mean = stats[6][index] / full_rows
        else:
            mean = jnp.mean(cols_new)
        updates.append(member[1] * lax.rsqrt(row_news[index][:, None] * cols_new[None, :] / mean))
        cols_out.append(cols_new)
    moment_new = decay * norm_moment + (1.0 - decay) * (norm_g * norm_g + SQUARE_FLOOR)
    norm_update = norm_g * lax.rsqrt(moment_new)
    update_sq = jnp.stack([jnp.sum(update * update) for update in updates])
    totals = lax.psum((update_sq, jnp.sum(norm_update * norm_update, 0)), ("dp", "seq"))
    news = []
    for index, member in enumerate(matrices + wide):
        entries = member[0].shape[0] * member[0].shape[1] * devices
        clip = jnp.maximum(1.0, jnp.sqrt(totals[0][index] / entries))
        news.append(
            member[0] - learn_rate * jnp.sqrt(stats[7][index] / entries) * updates[index] / clip
        )
    norm_rows = norms.shape[0] * devices
    norm_clip = jnp.maximum(1.0, jnp.sqrt(totals[1] / norm_rows))
    norm_new = norms - learn_rate * jnp.sqrt(stats[8] / norm_rows) * norm_update / norm_clip
    return (
        stats[9][0],
        mask_count,
        table_g.T,
        place_g.T,
        qkv_g,
        out_g,
        in_g,
        down_g,
        norm_g,
        cols_out[4],
        row_news[4],
        cols_out[5],
        row_news[5],
        row_news[0],
        cols_out[0],
        row_news[1],
        cols_out[1],
        row_news[2],
        cols_out[2],
        row_news[3],
        cols_out[3],
        moment_new,
        news[4].T,
        news[5].T,
        news[0],
        news[1],
        news[2],
        news[3],
        norm_new,
    )


def solution(mesh):
    split, wide = P(("dp", "seq"), None), P(None, ("dp", "seq"))
    shard, same = P(("dp", "seq")), P()
    return jax.shard_map(
        functools.partial(on_device, (mesh.shape["dp"], mesh.shape["seq"])),
        mesh=mesh,
        in_specs=(P("dp", "seq"),) * 3
        + (P("dp"),)
        + (split,) * 3
        + (shard,)
        + (wide,) * 2
        + (split,) * 5
        + (same, shard) * 2
        + (shard, same) * 4
        + (split,),
        out_specs=(same, same)
        + (wide,) * 2
        + (split,) * 5
        + (same, shard) * 2
        + (shard, same) * 4
        + (split,)
        + (wide,) * 2
        + (split,) * 5,
        check_vma=False,
    )
```

```python
import functools

import jax
import jax.numpy as jnp
from jax import lax
from jax.experimental import pallas as pl
from jax.experimental.pallas import tpu as pltpu
from jax.sharding import PartitionSpec as P

D = 768
HEADS = 12
HEAD_DIM = 64
VOCAB = 4101
STEP = 10
SPAN = 128

EPSILON = 1e-12
SQUARE_FLOOR = 1e-30
learn_rate = 0.3

MESH = pl.DeviceIdType.MESH
F32 = jnp.float32
BF16 = jnp.bfloat16

NORM_AT = VOCAB
COUNT_AT = VOCAB + 6
TABLE_END = 4352
PLACE_AT = 4352
WIDE = PLACE_AT + 512

SHAPES = ((24, WIDE), (24, 3 * D), (24, D), (24, 4 * D), (96, D))
E_, Q_, O_, I_, D_ = range(5)
CLASS_A, CLASS_B, CLASS_C = (E_, O_), (Q_, D_), (I_,)
UP, DOWN, XWAY, YWAY, SIDE = range(5)


def here():
    dp, seq = lax.axis_index("dp"), lax.axis_index("seq")
    return dp // 2, dp % 2, seq // 2, seq % 2


def device(z, y, x, c):
    return {"dp": z * 2 + y, "seq": x * 2 + c}


def chip(z, y, x):
    return z * 4 + y * 2 + x


def near_first(z, s):
    inner = (z * (3 - z)) // 2
    found = s + inner * (1, 1, -2, 0)[s]
    return found + (z // 2) * (3 - 2 * found)


def all_peers():
    z, y, x, c = here()
    return (
        device(z + 1, y, x, c),
        device(z - 1, y, x, c),
        device(z, y, 1 - x, c),
        device(z, 1 - y, x, c),
        device(z, y, x, 1 - c),
    )


SUM_AT = (0, WIDE, WIDE + 3 * D, WIDE + 4 * D, WIDE + 8 * D, WIDE + 9 * D)
SUMS = WIDE + 9 * D + 256
HALF_AT = tuple(start // 2 for start in SUM_AT)
HALF_SUMS = HALF_AT[5]


def lanes_of(members):
    lane = lax.broadcasted_iota(jnp.int32, (1, 128), 1)
    row = jnp.zeros((1, 128), F32)
    for index, member in enumerate(members):
        row = jnp.where(lane == index, member, row)
    return row


def lane_at(row, index):
    lane = lax.broadcasted_iota(jnp.int32, row.shape, 1)
    return jnp.sum(jnp.where(lane == index, row, 0.0), 1, keepdims=True)


def column_of(row):
    size = row.shape[1]
    diagonal = lax.broadcasted_iota(jnp.int32, (size, size), 0) == lax.broadcasted_iota(
        jnp.int32, (size, size), 1
    )
    return jnp.sum(jnp.where(diagonal, row, 0.0), 1, keepdims=True)


def row_of(column):
    size = column.shape[0]
    diagonal = lax.broadcasted_iota(jnp.int32, (size, size), 0) == lax.broadcasted_iota(
        jnp.int32, (size, size), 1
    )
    return jnp.sum(jnp.where(diagonal, column, 0.0), 0, keepdims=True)


def as_row(ref):
    return ref[...].reshape(1, ref.shape[0])


def total_sum(array):
    return jnp.sum(jnp.sum(array, 1, keepdims=True), 0, keepdims=True)


def gelu_pair(hidden):
    normal_cdf = 0.5 * (1.0 + lax.erf(hidden * 0.7071067811865476))
    return (
        hidden * normal_cdf,
        normal_cdf + hidden * jnp.exp(-0.5 * hidden * hidden) * 0.3989422804014327,
    )


def dot_nn(left, right):
    return jnp.dot(left, right, preferred_element_type=F32)


def dot_nt(left, right):
    return lax.dot_general(left, right, (((1,), (1,)), ((), ())), preferred_element_type=F32)


def dot_tn(left, right):
    return lax.dot_general(left, right, (((0,), (0,)), ((), ())), preferred_element_type=F32)


def at(index, size):
    if isinstance(index, int):
        return pl.ds(index * size, size)
    return pl.ds(pl.multiple_of(index * size, size), size)


def each(count, body):
    def step(index, carry):
        body(index)
        return carry

    lax.fori_loop(0, count, step, 0)


def each_unrolled(count, body):
    for index in range(count):
        body(index)


ROWS = 128
TILE = 256
HALF = 320
TABLE_TILES = TABLE_END // TILE


def head_lanes(first):
    lane = lax.broadcasted_iota(jnp.int32, (1, 128), 1)
    return (lane < HEAD_DIM) if first else (lane >= HEAD_DIM)


def layer_norm(value, gain, shift):
    centred = value - jnp.sum(value, 1, keepdims=True) / D
    inverse = lax.rsqrt(jnp.sum(centred * centred, 1, keepdims=True) / D + EPSILON)
    normed = centred * inverse
    return normed * gain + shift, normed, inverse


def layer_norm_back(grad, normed, inverse, gain):
    scaled = grad * gain
    return inverse * (
        scaled - jnp.sum(scaled, 1, keepdims=True) / D - normed * (jnp.sum(scaled * normed, 1, keepdims=True) / D)
    )


def put_lane(ref, rows, index, value):
    lane = lax.broadcasted_iota(jnp.int32, (1, 128), 1)
    ref[rows, :] = jnp.where(lane == index, value, ref[rows, :])


def set_bias(bias, cols, keys, last):
    same = cols[0:last, 4:5] == keys[1:2, 0:last]
    bias[...] = jnp.where(same & (keys[0:1, 0:last] > 0), 0.0, -1e30)


CHOOSE, EMBED, NORM_A, PROJECT, TURN_X, ATTEND, OUT, NORM_B, FEED_IN, TURN_A, FEED_OUT, REST = range(12)
FRONT = (
    35, 99, 33, 67, 65, 32, 4, 64, 3, 36, 1, 160, 69, 101, 40, 37, 1000, 163, 100, 0,
    129, 70, 1001, 68, 164, 128, 103, 72, 46, 44, 73, 161, 97, 96, 38, 5, 45, 74, 39, 77,
    102, 6, 172, 71, 7, 105, 82, 8, 41, 11, 10, 107, 12, 42, 14, 43, 79, 75, 9, 47,
    166, 168, 165, 104, 80, 78, 133, 81, 76, 18, 49, 111, 51, 48, 170, 50, 134, 167, 83, 132,
    108, 106, 13, 16, 1016, 17, 1017, 1018, 15, 1019, 1020, 135, 110, 19, 1021, 1032, 144, 176, 169, 142,
    1048, 1049, 171, 115, 1050, 1051, 173, 137, 1052, 131, 1053, 1054, 1055, 109, 1056, 1064, 174, 1080, 177, 140,
    1081, 138, 112, 178, 1082, 1083, 139, 114, 1084, 175, 179, 1085, 145, 143, 1096, 113, 146, 1097, 1098, 136,
    1112, 1128, 1129, 147, 1130, 1131, 1132, 1133, 1134, 1135, 141, 1136, 1137, 1138, 1139, 1160, 1161, 1162, 1176,
)


def front_hooks():
    hooks, before = {}, []
    for task in FRONT:
        if task < 1000:
            before.append(task)
        else:
            hooks[((task - 1000) // 16, (task - 1000) % 16)] = before
            before = []
    return hooks


def front_kernel(*refs):
    raw, (long_len, short_len) = refs[0:13], refs[13:15]
    count_out, gains_out, side, cols, keys, squares = refs[15:21]
    x_t, mix_out, a_out, act_out, y_out, slope_out, qkv_out, na_out = refs[21:29]
    nb_outs, nc_outs, weight_outs = refs[29:31], refs[31:33], refs[33:38]
    wide, qkv_w, out_w, in_w, down_w = weights = refs[38:43]
    value, na, low_a, low_y, mix, qkv, act, slope, pick, pick_two, bias, turned = refs[43:55]
    nb, nc = refs[55:57], (mix, low_y)
    held, wide_shard, merge, pieces, land = refs[57:70], refs[70], refs[71:76], refs[76], refs[77]
    raw_sem, swap_send, swap_recv, token_send, token_recv, send_sem, link_recv, side_recv = refs[78:86]
    out_sem, turn_sem = refs[86:88]
    z, y, x, c = here()
    peers = all_peers()
    me = chip(z, y, x)
    seq = x * 2 + c
    alone = seq // 3
    tokens = value.shape[0]
    last = tokens - SPAN
    hooks = front_hooks()

    barrier = pltpu.get_barrier_semaphore()
    cross = device(z, y, 1 - x, 1 - c)
    column = [device((z + 1 + i) % 4, y, x, c) for i in range(3)]
    for peer in [peers[XWAY], peers[YWAY], peers[SIDE], cross] + column:
        pl.semaphore_signal(barrier, inc=1, device_id=peer, device_id_type=MESH)
    raws = [pltpu.make_async_copy(raw[i], held[i], raw_sem.at[i]) for i in range(13)]
    for member in raws:
        member.start()
    for member in raws:
        member.wait()
    long_ids, long_targets, long_mask, short_ids, short_targets, short_mask, tall, place, qkv_s, out_s, in_s, down_s, norms = held

    pieces[...] = jnp.zeros(pieces.shape, jnp.int32)
    land[4] = jnp.zeros((8, SPAN), jnp.int32)
    lane = lax.broadcasted_iota(jnp.int32, (1, SPAN), 1)
    count = jnp.zeros((1, SPAN), jnp.int32)
    for t in range(5):
        if t < 3:
            ids, targets, mask = long_ids[t : t + 1, :], long_targets[t : t + 1, :], long_mask[t : t + 1, :]
            keep = (lane + seq * SPAN < long_len[t]).astype(jnp.int32)
        else:
            row = (1, 0)[t - 3]
            ids, targets, mask = (member[row : row + 1, :] for member in (short_ids, short_targets, short_mask))
            keep = (lane < short_len[row]).astype(jnp.int32)
        target = pieces.at[t] if t < 4 else land.at[4]
        target[0:1, :] = ids
        target[2:3, :] = targets
        target[3:4, :] = mask * keep
        target[5:6, :] = keep
        count = count + mask * keep
    count = jnp.sum(count.astype(F32), 1, keepdims=True)
    high = jnp.floor(count * (1.0 / 256.0))

    wide_shard[:, 0:4096] = tall[:, 0:4096]
    edge = jnp.zeros((24, 128), F32)
    tile_lane = lax.broadcasted_iota(jnp.int32, (24, 128), 1)
    tall_edge = tall[:, 4096:VOCAB]
    members = [lane_at(tall_edge, i) for i in range(VOCAB - 4096)]
    members += [column_of(norms[i : i + 1, :]) for i in range(6)]
    members += [high, count - high * 256.0]
    for i, member in enumerate(members):
        edge = jnp.where(tile_lane == i, member, edge)
    wide_shard[:, 4096:4224] = edge
    wide_shard[:, 4224:PLACE_AT] = jnp.zeros((24, PLACE_AT - 4224), F32)
    wide_shard[:, PLACE_AT:] = place[...]
    shards = (wide_shard, qkv_s, out_s, in_s, down_s)
    for m, (size, whole) in enumerate(SHAPES):
        half = whole // 2
        merge[m][pl.ds(pl.multiple_of(c * size, 8), size), :] = shards[m][:, pl.ds(pl.multiple_of(c * half, 128), half)]

    pl.semaphore_wait(barrier, 7)
    swaps = []
    for m in (E_, Q_, I_, D_, O_):
        size, half = SHAPES[m][0], SHAPES[m][1] // 2
        swaps.append(
            pltpu.make_async_remote_copy(
                src_ref=shards[m].at[:, pl.ds(pl.multiple_of((1 - c) * half, 128), half)],
                dst_ref=merge[m].at[pl.ds(pl.multiple_of(c * size, 8), size), :],
                send_sem=swap_send.at[m],
                recv_sem=swap_recv.at[m],
                device_id=peers[SIDE],
                device_id_type=MESH,
            )
        )
        swaps[-1].start()
    token_copies = []
    for i, (to_x, to_c) in enumerate(((x, 1 - c), (1 - x, c), (1 - x, 1 - c))):
        token_copies.append(
            pltpu.make_async_remote_copy(
                src_ref=pieces.at[to_x * 2 + to_c],
                dst_ref=land.at[seq],
                send_sem=token_send.at[i],
                recv_sem=token_recv.at[i],
                device_id=device(z, y, to_x, to_c),
                device_id_type=MESH,
            )
        )
        token_copies[-1].start()
    land[seq] = pieces[seq]

    def part(piece, k, half):
        m, skip, wide_part = PIECES[piece]
        size = 2 * SHAPES[m][0]
        start = pl.multiple_of(half * (SHAPES[m][1] // 2) + skip, 128)
        return weights[m].at[pl.ds(pl.multiple_of(k * size, size), size), pl.ds(start, wide_part)]

    FIRST_WAY, SECOND_WAY, SIDE_WAY, UP_WAY, DOWN_WAY = range(5)

    def copy_of(piece, k, way):
        ways = (XWAY, YWAY) if GATHER_WAY[piece] == 0 else (YWAY, XWAY)
        return pltpu.make_async_remote_copy(
            src_ref=part(piece, k, c),
            dst_ref=part(piece, k, c),
            send_sem=send_sem.at[piece, k, way],
            recv_sem=(side_recv if way == SIDE_WAY else link_recv).at[piece, k],
            device_id=peers[(ways + (SIDE, UP, DOWN))[way]],
            device_id_type=MESH,
        )

    def block_of(number):
        piece, task = number // 32, number % 32
        way = GATHER_WAY[piece]
        up, down = (UP_WAY, z < 3), (DOWN_WAY, z > 0)
        first, second, across = (FIRST_WAY, None), (SECOND_WAY, None), (SIDE_WAY, None)

        def of(last, earlier, t):
            to_y, to_x = (last, earlier) if way == 0 else (earlier, last)
            return chip(t, 1 - y if to_y else y, 1 - x if to_x else x)

        def onward(t):
            return (UP_WAY, (t < z) & (z < 3)), (DOWN_WAY, (t > z) & (z > 0))

        if task < 5:
            return piece, me, (up, down, None, first, second)[task : task + 1], False
        if way < 2:
            if task < 8:
                t = near_first(z, task - 4)
                return piece, of(0, 0, t), onward(t) + (first, second, across), True
            if task < 12:
                return piece, of(0, 1, near_first(z, task - 8)), (second, across), True
            return piece, of(1, (task - 12) % 2, near_first(z, (task - 12) // 2)), (across,), True
        if task == 5:
            return piece, of(0, 1, z), (second, up, down, across), True
        if task < 8:
            return piece, of(1, task - 6, z), (up, down, across), True
        t, place_of = near_first(z, 1 + (task - 8) // 4), (task - 8) % 4
        return piece, of(place_of // 2, place_of % 2, t), onward(t) + (across,), True

    def for_each_way(number, act):
        piece, k, ways, _ = block_of(number)
        for way, only in ways:
            if only is None:
                act(copy_of(piece, k, way))
            else:

                @pl.when(only)
                def _(way=way):
                    act(copy_of(piece, k, way))

    def transfer(number):
        piece, k, _, waits = block_of(number)
        if waits:
            copy_of(piece, k, FIRST_WAY).wait_recv()
        for_each_way(number, lambda copy: copy.start())

    def before(step, index, base=0):
        for (name, part_index), tasks in hooks.items():
            part_index = part_index - base
            if name != step or not tasks or (step == EMBED and not 0 <= part_index < 3):
                continue
            if index is None or isinstance(index, int):
                if part_index == (index or 0):
                    for number in tasks:
                        transfer(number)
            else:

                @pl.when(index == part_index)
                def _(tasks=tasks):
                    for number in tasks:
                        transfer(number)

    def need(*wanted):
        for piece in wanted:
            for k in range(16):
                pltpu.make_async_remote_copy(
                    src_ref=part(piece, k, 1 - c),
                    dst_ref=part(piece, k, 1 - c),
                    send_sem=send_sem.at[piece, k, SIDE_WAY],
                    recv_sem=side_recv.at[piece, k],
                    device_id=peers[SIDE],
                    device_id_type=MESH,
                ).wait_recv()

    for number, m in enumerate((E_, Q_, I_, D_, O_)):
        swaps[number].wait_recv()
        size, half = SHAPES[m][0], SHAPES[m][1] // 2
        rows = pl.ds(pl.multiple_of(me * 2 * size, 2 * size), 2 * size)
        weights[m][rows, pl.ds(pl.multiple_of(c * half, 128), half)] = merge[m][...].astype(BF16)
        for piece in range(6):
            if PIECES[piece][0] == m:
                copy_of(piece, me, SIDE_WAY).start()
    opening = hooks[(CHOOSE, 0)]
    while opening and opening[0] % 32 < 5:
        transfer(opening.pop(0))
    for copy in token_copies:
        copy.wait_recv()
    side[...] = jnp.zeros(side.shape, F32)
    keys[...] = jnp.zeros(keys.shape, jnp.int32)
    zeros = jnp.zeros((1, SPAN), F32)
    for b in range(5):
        tile = land[b]
        shift = b * SPAN * (1 - alone) if b < 4 else 0
        row = b * alone if b < 4 else 4
        spot = (lane + shift + PLACE_AT).astype(F32)
        row_lane = (lane * 0 + row).astype(F32)
        ids, targets, weight = (tile[i : i + 1].astype(F32) for i in (0, 2, 3))
        stacked = jnp.concatenate((ids, spot, targets, weight, row_lane, tile[5:6].astype(F32), zeros, zeros), 0)
        stacked = jnp.concatenate((stacked, jnp.zeros((120, SPAN), F32)), 0)
        cols[b * SPAN : (b + 1) * SPAN, :] = stacked.T.astype(jnp.int32)
        keys[0:1, b * SPAN : (b + 1) * SPAN] = tile[5:6]
        keys[1:2, b * SPAN : (b + 1) * SPAN] = lane * 0 + row
        keys[2:4, b * SPAN : (b + 1) * SPAN] = tile[2:4]
    set_bias(bias, cols, keys, last)
    found = [total_sum(member[...] * member[...]) for member in (tall, place, qkv_s, out_s, in_s, down_s)]
    norm_squares = jnp.sum(norms[...] * norms[...], 1, keepdims=True)
    squares[...] = lanes_of(found + [norm_squares[i : i + 1] for i in range(6)])

    turns, outs, out_count = {}, {}, [0]

    def turn_out(source, target, slot):
        if slot in turns:
            turns[slot].wait()

        def some(index):
            turned[slot, :, at(index, ROWS)] = source[at(index, ROWS), :].T

        each_unrolled(tokens // ROWS, some)
        turns[slot] = pltpu.make_async_copy(turned.at[slot], target, turn_sem.at[slot])
        turns[slot].start()

    def put_out(name, source, target):
        outs[name] = pltpu.make_async_copy(source, target, out_sem.at[out_count[0]])
        out_count[0] += 1
        outs[name].start()

    picks = (pick, pick_two)
    halves = [pl.ds(half * HALF, HALF) for half in range(2)]
    for half in range(2):

        def choose(index):
            column_lane = lax.broadcasted_iota(jnp.int32, (1, TILE), 1) + index * TILE
            hit = (cols[halves[half], 0:1] == column_lane) | (cols[halves[half], 1:2] == column_lane)
            picks[half][:, at(index, TILE)] = jnp.where(hit, 1.0, 0.0).astype(BF16)

        before(CHOOSE, half)
        each_unrolled(WIDE // TILE, choose)

    before(EMBED, 0)
    hooks.pop((EMBED, 0))
    need(1, 2)
    put_out("wide", wide, weight_outs[4])
    for half in range(2):

        def embed(index):
            before(EMBED, index, half * 3)
            value[halves[half], at(index, TILE)] = dot_nt(picks[half][...], wide[at(index, TILE), :])

        each_unrolled(D // TILE, embed)

    gains = wide[:, 4096:4224].astype(F32).T
    gains_out[...] = gains[0:16]
    counts = jnp.sum(gains[11:13], 1, keepdims=True) / 24.0
    mask_count = counts[0:1] * 256.0 + counts[1:2]
    count_out[...] = mask_count
    norm_rows = [gains_out[5 + i : 6 + i, :] for i in range(6)]
    before(NORM_A, None)

    def norm_a(index):
        rows = at(index, ROWS)
        found, normed, inverse = layer_norm(value[rows, :], norm_rows[0], norm_rows[1])
        value[rows, :] = found
        low_a[rows, :] = found.astype(BF16)
        na[rows, :] = normed
        put_lane(side, rows, 12, inverse)

    each_unrolled(tokens // ROWS, norm_a)
    put_out("na", na, na_out)
    before(PROJECT, 0)
    need(0)

    def project(index):
        before(PROJECT, index)
        qkv[:, at(index, TILE)] = dot_nn(low_a[...], qkv_w[:, at(index, TILE)]).astype(BF16)

    hooks.pop((PROJECT, 0))
    each_unrolled(3 * D // TILE, project)
    put_out("qkv", qkv, qkv_out)
    put_out("qkv_w", qkv_w, weight_outs[0])
    before(TURN_X, None)
    turn_out(low_a, x_t, 0)

    def attend_pair(pair):
        before(ATTEND, pair)
        for start, size in ((0, last), (last, SPAN)):
            rows = pl.ds(start, size)
            query = qkv[rows, at(pair, 128)]
            key = qkv[rows, pl.ds(D + pair * 128, 128)]
            val = qkv[rows, pl.ds(2 * D + pair * 128, 128)]
            mask = bias[...] if start == 0 else jnp.where(keys[0:1, last:tokens] > 0, 0.0, -1e30)
            mixed = []
            for first in (True, False):
                chosen = jnp.where(head_lanes(first), query, jnp.zeros_like(query))
                scores = dot_nt(chosen, key) * 0.125 + mask
                highest = jnp.max(scores, 1, keepdims=True)
                raised = jnp.exp(scores - highest)
                summed = jnp.sum(raised, 1, keepdims=True)
                shares = (raised * (1.0 / summed)).astype(BF16)
                mixed.append(dot_nn(shares, val))
                put_lane(side, rows, 2 * pair + (0 if first else 1), highest + jnp.log(summed))
            mix[rows, at(pair, 128)] = jnp.where(head_lanes(True), mixed[0], mixed[1]).astype(BF16)

    each_unrolled(HEADS // 2, attend_pair)
    before(OUT, 0)
    hooks.pop((OUT, 0))
    need(5)

    def out_project(index):
        before(OUT, index)
        value[:, at(index, TILE)] = value[:, at(index, TILE)] + dot_nn(mix[...], out_w[:, at(index, TILE)])

    each_unrolled(D // TILE, out_project)
    put_out("out_w", out_w, weight_outs[1])
    put_out("mix", mix, mix_out)
    before(NORM_B, None)

    def norm_b(index):
        rows = at(index, ROWS)
        found, normed, inverse = layer_norm(value[rows, :], norm_rows[2], norm_rows[3])
        value[rows, :] = found
        low_y[rows, :] = found.astype(BF16)
        nb[0][rows, :], nb[1][rows, :] = split_two(normed)
        put_lane(side, rows, 13, inverse)

    each_unrolled(tokens // ROWS, norm_b)
    put_out("a", low_y, a_out)
    put_out("nb0", nb[0], nb_outs[0])
    put_out("nb1", nb[1], nb_outs[1])
    before(FEED_IN, 0)
    hooks.pop((FEED_IN, 0))
    need(3)

    def feed_in(index):
        before(FEED_IN, index)
        hidden = dot_nn(low_y[...], in_w[:, at(index, TILE)])
        active, slant = gelu_pair(hidden)
        active = active.astype(BF16)
        act[:, at(index, TILE)] = active
        slope[:, at(index, TILE)] = slant.astype(BF16)

    each_unrolled(4 * D // TILE, feed_in)
    put_out("act", act, act_out)
    put_out("slope", slope, slope_out)
    put_out("in_w", in_w, weight_outs[2])
    before(TURN_A, None)
    before(FEED_OUT, 0)
    hooks.pop((FEED_OUT, 0))
    need(4)

    def feed_out(index):
        before(FEED_OUT, index)
        value[:, at(index, TILE)] = value[:, at(index, TILE)] + dot_nn(act[...], down_w[:, at(index, TILE)])

    each_unrolled(D // TILE, feed_out)
    put_out("down_w", down_w, weight_outs[3])
    before(REST, None)
    turns[0].wait()
    outs.pop("mix").wait()
    outs.pop("a").wait()

    def norm_c(index):
        rows = at(index, ROWS)
        found, normed, inverse = layer_norm(value[rows, :], norm_rows[4], norm_rows[5])
        low_a[rows, :] = found.astype(BF16)
        nc[0][rows, :], nc[1][rows, :] = split_two(normed)
        put_lane(side, rows, 14, inverse)

    each_unrolled(tokens // ROWS, norm_c)
    put_out("y", low_a, y_out)
    put_out("nc0", nc[0], nc_outs[0])
    put_out("nc1", nc[1], nc_outs[1])
    for swap in swaps:
        swap.wait_send()
    for copy in token_copies:
        copy.wait_send()
    for piece in range(6):
        copy_of(piece, me, SIDE_WAY).wait_send()
    for number in FRONT:
        if number < 1000:
            for_each_way(number, lambda copy: copy.wait_send())
    for copy in outs.values():
        copy.wait()


def front(large, lengths):
    vmem, hbm = pl.BlockSpec(memory_space=pltpu.VMEM), pl.BlockSpec(memory_space=pl.ANY)
    smem = pl.BlockSpec(memory_space=pltpu.SMEM)
    shape, dma = jax.ShapeDtypeStruct, pltpu.SemaphoreType.DMA
    tokens = 5 * SPAN
    small = [shape((1, 1), F32), shape((16, D), F32), shape((tokens, 128), F32)]
    small += [shape((tokens, 128), jnp.int32), shape((8, tokens), jnp.int32), shape((1, 128), F32)]
    out = [shape((D, tokens), BF16)] + [shape((tokens, width), BF16) for width in (D, D, 4 * D, D, 4 * D, 3 * D)]
    out += [shape((tokens, D), F32)] + [shape((tokens, D), BF16)] * 4
    out += [shape((32 * SHAPES[m][0], SHAPES[m][1]), BF16) for m in (Q_, O_, I_, D_, E_)]
    return pl.pallas_call(
        front_kernel,
        out_shape=small + out,
        in_specs=[hbm] * 13 + [smem] * 2,
        out_specs=[vmem] * len(small) + [hbm] * len(out),
        scratch_shapes=[pltpu.VMEM((32 * size, wide), BF16) for size, wide in SHAPES]
        + [pltpu.VMEM((tokens, D), F32)] * 2
        + [pltpu.VMEM((tokens, D), BF16)] * 3
        + [
            pltpu.VMEM((tokens, 3 * D), BF16),
            pltpu.VMEM((tokens, 4 * D), BF16),
            pltpu.VMEM((tokens, 4 * D), BF16),
            pltpu.VMEM((HALF, WIDE), BF16),
            pltpu.VMEM((HALF, WIDE), BF16),
            pltpu.VMEM((tokens - SPAN, tokens - SPAN), F32),
            pltpu.VMEM((1, D, tokens), BF16),
        ]
        + [pltpu.VMEM((tokens, D), BF16)] * 2
        + [pltpu.VMEM(member.shape, member.dtype) for member in large]
        + [pltpu.VMEM(SHAPES[E_], F32)]
        + [pltpu.VMEM((2 * size, wide // 2), F32) for size, wide in SHAPES]
        + [pltpu.VMEM((4, 8, SPAN), jnp.int32), pltpu.VMEM((5, 8, SPAN), jnp.int32)]
        + [dma((13,)), dma((5,)), dma((5,)), dma((3,)), dma((3,)), dma((6, 16, 5)), dma((6, 16)), dma((6, 16))]
        + [dma((18,)), dma((1,))],
        compiler_params=pltpu.CompilerParams(
            collective_id=0, has_side_effects=True, vmem_limit_bytes=63 * 1024 * 1024
        ),
    )(*large, *lengths)


PACK = 256


def split_two(value):
    high = value.astype(BF16)
    return high, (value - high.astype(F32)).astype(BF16)


def middle_kernel(*refs):
    (wide_h, qkv_wh, out_wh, in_wh, down_h, y_h, act_h, a_h, mix_h, slope_h, qkv_h, na_h) = refs[0:12]
    nb_h, nc_h = refs[12:14], refs[14:16]
    cols, keys, side, gains, count = refs[16:21]
    loss_out, norm_out = refs[21:23]
    glog_out, y_t, a_t, mix_t, act_t, ge_t, gffn_out, gh_out, gattn_out, gqkv_out = refs[23:33]
    wide, qkv_w, out_w, in_w, plain, qkv = refs[33:39]
    nb = refs[39:41]
    slope_ring, act_ring, down_ring = refs[41:44]
    logits, glog, gh, gffn, gattn, packed, grad, turned, act_turned = refs[44:53]
    back_kv, gqkv, whole_grad, pick, pick_t, bias, side_pack, side_turned, dq, ge = refs[53:63]
    load_sem, ring_sem, out_sem = refs[63:66]
    nc = (gqkv.at[:, D : 2 * D], gqkv.at[:, 2 * D : 3 * D])
    gatt = packed
    tokens = cols.shape[0]
    names = ("wide", "y", "nc0", "nc1", "in_w", "nb0", "nb1", "out_w", "qkv", "qkv_w")
    sources = (wide_h, y_h, nc_h[0], nc_h[1], in_wh, nb_h[0], nb_h[1], out_wh, qkv_h, qkv_wh)
    targets = (wide, plain, nc[0], nc[1], in_w, nb[0], nb[1], out_w, qkv, qkv_w)

    def na_copy(i):
        return pltpu.make_async_copy(
            na_h.at[:, at(i, TILE)], logits.at[pl.ds(i * tokens, tokens), :], load_sem.at[10 + i]
        )

    def tile_of(index):
        return pl.ds(index * PACK, PACK)

    loads = {name: pltpu.make_async_copy(sources[i], targets[i], load_sem.at[i]) for i, name in enumerate(names)}
    for name in ("y", "wide"):
        loads[name].start()

    weight_row = keys[3:4, :].astype(F32)
    weight_col = cols[:, 3:4].astype(F32)
    earlier = lax.broadcasted_iota(jnp.int32, (tokens, tokens), 0) < lax.broadcasted_iota(jnp.int32, (tokens, tokens), 1)
    later = lax.broadcasted_iota(jnp.int32, (tokens, tokens), 0) > lax.broadcasted_iota(jnp.int32, (tokens, tokens), 1)
    rank_row = dot_nn(
        jnp.broadcast_to(weight_row, (16, tokens)).astype(BF16), jnp.where(earlier, 1.0, 0.0).astype(BF16)
    )[0:1]
    rank_col = dot_nn(
        jnp.where(later, 1.0, 0.0).astype(BF16), jnp.broadcast_to(weight_col, (tokens, 128)).astype(BF16)
    )[:, 0:1]
    rank_row = jnp.where(weight_row > 0, rank_row, -1.0)
    rank_col = jnp.where(weight_col > 0, rank_col, -1.0)
    blocks = (jnp.sum(weight_row).astype(jnp.int32) + (PACK - 1)) // PACK
    blocks = jnp.maximum(blocks, 1)
    inverse_count = 1.0 / count[...]
    norm_rows = [gains[5 + i : 6 + i, :] for i in range(6)]
    loss_out[...] = jnp.zeros((1, 1), F32)
    norm_out[...] = jnp.zeros(norm_out.shape, F32)
    back_kv[...] = jnp.zeros(back_kv.shape, F32)
    whole_grad[...] = jnp.zeros(whole_grad.shape, F32)
    gqkv[:, 0:D] = jnp.zeros((tokens, D), BF16)
    side_first = side[...].astype(BF16)
    rest = side[...] - side_first.astype(F32)
    side_second = rest.astype(BF16)
    side_third = (rest - side_second.astype(F32)).astype(BF16)
    waited = set()

    def load_plain(source):
        return pltpu.make_async_copy(source, plain, load_sem.at[1])

    def ring(kind, source, target):
        def copy(j):
            piece = source.at[at(j, TILE), :] if kind == 2 else source.at[:, at(j, TILE)]
            return pltpu.make_async_copy(piece, target.at[j % 2], ring_sem.at[kind * 2 + j % 2])

        return copy

    rings = [ring(0, slope_h, slope_ring), ring(1, act_h, act_ring), ring(2, down_h, down_ring)]
    outs = [
        (glog, glog_out, 0),
        (turned.at[0], y_t, 1),
        (turned.at[1], a_t, 1),
        (turned.at[2], mix_t, 1),
        (act_turned, act_t, 1),
        (gffn, gffn_out, 0),
        (gh, gh_out, 0),
        (gattn, gattn_out, 0),
    ]

    def out_copy(i, block):
        source, target, axis = outs[i]
        place = at(block, PACK)
        return pltpu.make_async_copy(
            source, target.at[place, :] if axis == 0 else target.at[:, place], out_sem.at[i]
        )

    def wait_load(name):
        loads[name].wait()

    wait_load("wide")
    for name in names[2:]:
        loads[name].start()

    def block_step(block, carry):
        slot_col = lax.broadcasted_iota(jnp.int32, (PACK, 1), 0).astype(F32) + (block * PACK).astype(F32)
        slot_row = lax.broadcasted_iota(jnp.int32, (1, PACK), 1).astype(F32) + (block * PACK).astype(F32)
        hit = jnp.where(rank_row == slot_col, 1.0, 0.0)
        pick[...] = hit.astype(BF16)
        hit_t = jnp.where(rank_col == slot_row, 1.0, 0.0)
        pick_t[...] = hit_t.astype(BF16)
        target = jnp.sum(hit * keys[2:3, :].astype(F32), 1, keepdims=True)
        weight = jnp.sum(hit, 1, keepdims=True)
        row_col = cols[:, 4:5].astype(F32)
        row_of_token = jnp.sum(hit_t * row_col, 0, keepdims=True)
        bias[...] = jnp.where((row_of_token == row_col) & (cols[:, 5:6] > 0), 0.0, -1e30)
        side_pack[...] = (
            dot_nn(pick[...], side_first) + dot_nn(pick[...], side_second) + dot_nn(pick[...], side_third)
        )
        side_turned[...] = side_pack[...].T
        for kind in range(3):
            for j in range(2):
                rings[kind](j).start()
        load_plain(y_h).wait()
        packed[...] = dot_nn(pick[...], plain[...]).astype(BF16)
        load_plain(a_h).start()
        turned[0] = packed[...].T
        out_copy(1, block).start()

        def lanes(index):
            return (lax.broadcasted_iota(jnp.int32, (1, TILE), 1) + index * TILE).astype(F32)

        highest = jnp.full((PACK, 128), -1e30, F32)
        for index in range(TABLE_TILES):
            found = dot_nn(packed[...], wide[:, at(index, TILE)])
            if index == TABLE_TILES - 1:
                found = jnp.where(lanes(index) < VOCAB, found, -1e30)
            logits[tile_of(index), :] = found
            highest = jnp.maximum(highest, jnp.maximum(found[:, 0:128], found[:, 128:256]))
        highest = jnp.max(highest, 1, keepdims=True)
        summed, picked = jnp.zeros((PACK, 128), F32), jnp.zeros((PACK, 128), F32)
        for index in range(TABLE_TILES):
            found = logits[tile_of(index), :]
            raised = jnp.exp(found - highest)
            logits[tile_of(index), :] = raised
            own = jnp.where(lanes(index) == target, found, 0.0)
            summed = summed + raised[:, 0:128] + raised[:, 128:256]
            picked = picked + own[:, 0:128] + own[:, 128:256]
        summed = jnp.sum(summed, 1, keepdims=True)
        picked = jnp.sum(picked, 1, keepdims=True)
        loss_out[...] = loss_out[...] + jnp.sum(weight * (highest + jnp.log(summed) - picked), 0, keepdims=True)
        scale = weight * inverse_count
        share = scale / summed
        for index in range(TABLE_TILES):
            found = logits[tile_of(index), :] * share - jnp.where(lanes(index) == target, scale, 0.0)
            glog[:, at(index, TILE)] = found.astype(BF16)
        out_copy(0, block).start()
        for index in range(D // TILE):
            grad[:, at(index, TILE)] = dot_nt(glog[...], wide[at(index, TILE), 0:TABLE_END])

        @pl.when(block == 0)
        def _():
            for name in names[2:4]:
                wait_load(name)

        normed = dot_nn(pick[...], nc[0][...]) + dot_nn(pick[...], nc[1][...])
        found = grad[...]
        back = layer_norm_back(found, normed, lane_at(side_pack[...], 14), norm_rows[4])
        norm_out[4:5, :] = norm_out[4:5, :] + jnp.sum(found * normed, 0, keepdims=True)
        norm_out[5:6, :] = norm_out[5:6, :] + jnp.sum(found, 0, keepdims=True)
        grad[...] = back
        gffn[...] = back.astype(BF16)
        out_copy(5, block).start()

        load_plain(a_h).wait()
        turned[1] = dot_nn(pick[...], plain[...]).astype(BF16).T
        out_copy(2, block).start()
        load_plain(mix_h).start()
        for index in range(4 * D // TILE):
            for kind in range(3):
                rings[kind](index).wait()
            slant = dot_nn(pick[...], slope_ring[index % 2])
            found = dot_nt(gffn[...], down_ring[index % 2]) * slant
            gh[:, at(index, TILE)] = found.astype(BF16)
            act_turned[at(index, TILE), :] = dot_nn(pick[...], act_ring[index % 2]).astype(BF16).T
            if index + 2 < 4 * D // TILE:
                for kind in range(3):
                    rings[kind](index + 2).start()
        out_copy(6, block).start()
        out_copy(4, block).start()
        load_plain(mix_h).wait()
        turned[2] = dot_nn(pick[...], plain[...]).astype(BF16).T
        out_copy(3, block).start()
        load_plain(y_h).start()

        @pl.when(block == 0)
        def _():
            for name in names[4:8]:
                wait_load(name)

        for index in range(D // TILE):
            grad[:, at(index, TILE)] = grad[:, at(index, TILE)] + dot_nt(gh[...], in_w[at(index, TILE), :])
        normed = dot_nn(pick[...], nb[0][...]) + dot_nn(pick[...], nb[1][...])
        found = grad[...]
        back = layer_norm_back(found, normed, lane_at(side_pack[...], 13), norm_rows[2])
        norm_out[2:3, :] = norm_out[2:3, :] + jnp.sum(found * normed, 0, keepdims=True)
        norm_out[3:4, :] = norm_out[3:4, :] + jnp.sum(found, 0, keepdims=True)
        gattn[...] = back.astype(BF16)
        out_copy(7, block).start()
        high, low = split_two(back)
        whole_grad[...] = whole_grad[...] + dot_nn(pick_t[...], high) + dot_nn(pick_t[...], low)
        for index in range(D // TILE):
            gatt[:, at(index, TILE)] = dot_nt(gattn[...], out_w[at(index, TILE), :]).astype(BF16)

        @pl.when(block == 0)
        def _():
            wait_load("qkv")

        def attend_pair_back(pair):
            spots = [pl.ds(i * D + pair * 128, 128) for i in range(3)]
            query = dot_nn(pick[...], qkv[:, spots[0]]).astype(BF16)
            key, val = qkv[:, spots[1]], qkv[:, spots[2]]
            given = gatt[:, at(pair, 128)]
            key_t = key.T
            found = []
            for first in (True, False):
                lanes_here = head_lanes(first)
                chosen = jnp.where(lanes_here, query, jnp.zeros_like(query))
                mine = jnp.where(lanes_here, given, jnp.zeros_like(given))
                total = side_turned[pl.ds(2 * pair + (0 if first else 1), 1), :]
                shares = jnp.exp(dot_nt(key, chosen) * 0.125 + bias[...] - total)
                grad_share = dot_nt(val, mine)
                middle = jnp.sum(shares * grad_share, 0, keepdims=True)
                grad_score = (shares * (grad_share - middle)).astype(BF16)
                found.append(
                    (
                        dot_nn(key_t, grad_score) * 0.125,
                        dot_nn(grad_score, query) * 0.125,
                        dot_nn(shares.astype(BF16), given),
                    )
                )
            lanes_here = head_lanes(True)
            both = jnp.concatenate((found[0][0][0:HEAD_DIM], found[1][0][HEAD_DIM:]), 0)
            dq[at(pair, 128), :] = both.astype(BF16)
            for i in (1, 2):
                spot = pl.ds((i - 1) * D + pair * 128, 128)
                back_kv[:, spot] = back_kv[:, spot] + jnp.where(lanes_here, found[0][i], found[1][i])

        each_unrolled(HEADS // 2, attend_pair_back)
        gqkv[:, 0:D] = (gqkv[:, 0:D].astype(F32) + dot_nt(pick_t[...], dq[...])).astype(BF16)
        for i in range(len(outs)):
            out_copy(i, block).wait()
        return carry

    lax.fori_loop(0, blocks, block_step, 0)
    load_plain(y_h).wait()
    for i in range(D // TILE):
        na_copy(i).start()
    gqkv[:, D:] = back_kv[...].astype(BF16)
    copy_qkv = pltpu.make_async_copy(gqkv, gqkv_out, out_sem.at[8])
    copy_qkv.start()
    for ref in (glog, gffn, gh, gattn):
        ref[...] = jnp.zeros(ref.shape, BF16)
    for block in range(1, 3):

        @pl.when(blocks <= block)
        def _():
            for i in range(len(outs)):
                out_copy(i, block).start()

    wait_load("qkv_w")
    for index in range(D // TILE):
        whole_grad[:, at(index, TILE)] = whole_grad[:, at(index, TILE)] + dot_nt(gqkv[...], qkv_w[at(index, TILE), :])
    for i in range(D // TILE):
        na_copy(i).wait()
    zero = jnp.zeros((1, D), F32)

    def norm_a_back(index, carry):
        gain, shift = carry
        rows = at(index, ROWS)
        inverse = lane_at(side[rows, :], 12)
        found = whole_grad[rows, :]
        normed = jnp.concatenate(
            [logits[pl.ds(i * tokens + index * ROWS, ROWS), :] for i in range(D // TILE)], 1
        )
        ge[:, rows] = layer_norm_back(found, normed, inverse, norm_rows[0]).astype(BF16).T
        return gain + jnp.sum(found * normed, 0, keepdims=True), shift + jnp.sum(found, 0, keepdims=True)

    gain, shift = zero, zero
    for index in range(tokens // ROWS):
        gain, shift = norm_a_back(index, (gain, shift))
    norm_out[0:1, :] = gain
    norm_out[1:2, :] = shift
    copy_ge = pltpu.make_async_copy(ge, ge_t, out_sem.at[9])
    copy_ge.start()
    for block in range(1, 3):

        @pl.when(blocks <= block)
        def _():
            for i in range(len(outs)):
                out_copy(i, block).wait()

    copy_qkv.wait()
    copy_ge.wait()


def middle(large, small):
    tokens = 5 * SPAN
    slots = 3 * PACK
    vmem, hbm = pl.BlockSpec(memory_space=pltpu.VMEM), pl.BlockSpec(memory_space=pl.ANY)
    shape, dma = jax.ShapeDtypeStruct, pltpu.SemaphoreType.DMA
    out = [shape((slots, TABLE_END), BF16)] + [shape((D, slots), BF16)] * 3 + [shape((4 * D, slots), BF16)]
    out += [shape((D, tokens), BF16), shape((slots, D), BF16), shape((slots, 4 * D), BF16), shape((slots, D), BF16)]
    out += [shape((tokens, 3 * D), BF16)]

    def rows(count, width, kind=BF16):
        return pltpu.VMEM((count, width), kind)

    scratch = [rows(D, WIDE), rows(D, 3 * D), rows(D, D), rows(D, 4 * D), rows(tokens, D), rows(tokens, 3 * D)]
    scratch += [rows(tokens, D)] * 2
    scratch += [pltpu.VMEM((2, tokens, TILE), BF16)] * 2 + [pltpu.VMEM((2, TILE, D), BF16)]
    scratch += [rows(PACK * TABLE_TILES, TILE, F32), rows(PACK, TABLE_END), rows(PACK, 4 * D)] + [rows(PACK, D)] * 3
    scratch += [rows(PACK, D, F32), pltpu.VMEM((3, D, PACK), BF16), rows(4 * D, PACK)]
    scratch += [rows(tokens, 2 * D, F32), rows(tokens, 3 * D), rows(tokens, D, F32), rows(PACK, tokens)]
    scratch += [rows(tokens, PACK), rows(tokens, PACK, F32), rows(PACK, 128, F32), rows(128, PACK, F32)]
    scratch += [rows(D, PACK), rows(D, tokens)]
    scratch += [dma((13,)), dma((6,)), dma((10,))]
    return pl.pallas_call(
        middle_kernel,
        out_shape=[shape((1, 1), F32), shape((6, D), F32)] + out,
        in_specs=[hbm] * 16 + [vmem] * 5,
        out_specs=[vmem] * 2 + [hbm] * len(out),
        scratch_shapes=scratch,
        compiler_params=pltpu.CompilerParams(vmem_limit_bytes=63 * 1024 * 1024),
    )(*large, *small)


LEFT = 768
PIECES = ((Q_, 0, 1152), (E_, 0, 1280), (E_, 1280, 1152), (I_, 0, 1536), (D_, 0, 384), (O_, 0, 384))
SUM_WAY = (0, 1, 0, 3, 1, 0)
GATHER_WAY = (0, 1, 0, 2, 1, 0)
TASKS = (
    160, 128, 161, 129, 96, 1, 168, 136, 164, 165, 0, 130, 97, 162, 169, 141, 99, 137,
    166, 133, 4, 6, 2, 8, 7, 98, 138, 9, 173, 132, 103, 32, 142, 174, 3, 134,
    102, 135, 131, 64, 12, 140, 10, 100, 65, 101, 72, 104, 33, 34, 167, 105, 70, 109,
    40, 71, 13, 73, 11, 143, 41, 139, 14, 77, 172, 108, 45, 171, 107, 68, 38, 111,
    144, 69, 36, 175, 76, 37, 46, 5, 44, 66, 78, 176, 15, 39, 75, 112, 43, 42,
    16, 110, 35, 79, 47, 17, 106, 163, 48, 145, 170, 74, 67, 80, 49, 113, 177, 81,
)


def reduce_kernel(*refs):
    given, (cols, norm_sums, loss, squares) = refs[0:11], refs[11:15]
    y_t, ge_t, glog, x_t, gqkv, mix_t, gattn, a_t, gh, act_t, gffn = given
    lane_olds, side_olds, moment = refs[15:21], refs[21:27], refs[27]
    outs, sums_out, totals_out = refs[28:33], refs[33], refs[34]
    own, side, first, second, column, fin = (refs[35 + 6 * i : 41 + 6 * i] for i in range(6))
    left, (glog_v, gqkv_v, gattn_v, gh_v, gffn_v), stage, tails, norm_t = refs[71:78], refs[78:83], refs[83], refs[84], refs[85]
    lane_plane, lane_z, lane_halves = refs[86:89]
    scalar_sums, total_sums = refs[89:91], refs[91:93]
    load_sem, ring_sem, tail_sem, side_recv, first_send, first_recv, second_send, second_recv = refs[93:101]
    z_send, z_recv, swap_send, swap_recv = refs[101:105]
    lane_send, lane_recv, scalar_send, scalar_recv, total_send, total_recv = refs[105:111]
    z, y, x, c = here()
    peers = all_peers()
    me = chip(z, y, x)

    barrier = pltpu.get_barrier_semaphore()
    spot = y * 2 + x
    column_peers = [device((z + 1 + i) % 4, y, x, c) for i in range(3)]
    plane = [(y, 1 - x), (1 - y, x), (1 - y, 1 - x)]
    plane_peers = [device(z, to_y, to_x, c) for to_y, to_x in plane]
    greeted = column_peers + plane_peers + [device(z, to_y, to_x, 1 - c) for to_y, to_x in [(y, x)] + plane]
    for peer in greeted:
        pl.semaphore_signal(barrier, inc=1, device_id=peer, device_id_type=MESH)

    tokens = cols.shape[0]

    def act_part(group):
        return act_t.at[pl.ds(LEFT * group, LEFT), 0:tokens]

    operands = (
        ((x_t, left[1]), (gqkv, gqkv_v)),
        ((y_t.at[:, 0:tokens], left[2]), (ge_t, left[3]), (glog.at[0:tokens, :], glog_v)),
        (),
        ((a_t.at[:, 0:tokens], left[0]), (gh.at[0:tokens, :], gh_v)),
        ((gffn.at[0:tokens, :], gffn_v), (act_part(0), left[5]), (act_part(1), left[6])),
        ((mix_t.at[:, 0:tokens], left[4]), (gattn.at[0:tokens, :], gattn_v)),
    )
    loads = {}
    waited = set()
    for task in TASKS:
        piece = task // 32 if task // 32 != 2 else 1
        if piece not in loads:
            loads[piece] = []
            for source, target in operands[piece]:
                number = sum(len(member) for member in loads.values())
                loads[piece].append(pltpu.make_async_copy(source, target, load_sem.at[number]))
                loads[piece][-1].start()

    def loaded(piece):
        piece = 1 if piece == 2 else piece
        if piece not in waited:
            waited.add(piece)
            for member in loads[piece]:
                member.wait()

    norm_t[...] = jnp.zeros(norm_t.shape, F32)
    norm_t[5:11, :] = norm_sums[...]
    pl.semaphore_wait(barrier, 10)

    def size_of(piece):
        return 2 * SHAPES[PIECES[piece][0]][0]

    def slot(ref, piece, index):
        size = size_of(piece)
        return ref[piece].at[pl.ds(pl.multiple_of(index * size, size), size), :]

    def half_of(piece):
        return SHAPES[PIECES[piece][0]][1] // 2

    def chosen(start):
        lane = lax.broadcasted_iota(jnp.int32, (1, TILE), 1) + start
        hit = (cols[:, 0:1] == lane) | (cols[:, 1:2] == lane)
        return jnp.where(hit, 1.0, 0.0).astype(BF16)

    def ring_copy(piece, rows, lanes, number, index):
        place = lax.rem(number, 3)
        return pltpu.make_async_remote_copy(
            src_ref=stage.at[place],
            dst_ref=side[piece].at[rows, lanes],
            send_sem=ring_sem.at[place],
            recv_sem=side_recv.at[piece, index],
            device_id=peers[SIDE],
            device_id_type=MESH,
        )

    def tail_copy(piece, rows, lanes, number, index):
        return pltpu.make_async_remote_copy(
            src_ref=tails.at[number],
            dst_ref=side[piece].at[rows, lanes],
            send_sem=tail_sem.at[number],
            recv_sem=side_recv.at[piece, index],
            device_id=peers[SIDE],
            device_id_type=MESH,
        )

    whole = pl.ds(0, LEFT)
    ring_count, tail_count = [0], [0]

    def give(piece, rows, lanes, number, index):
        def before():
            @pl.when(number >= 3)
            def _():
                ring_copy(piece, rows, lanes, number, index).wait_send()

        def write(value):
            stage[lax.rem(number, 3)] = value.astype(BF16)

        return before, write, lambda: ring_copy(piece, rows, lanes, number, index).start()

    def keep(piece, rows, lanes):
        def write(value):
            own[piece][rows, lanes] = value.astype(BF16)

        return lambda: None, write, lambda: None

    def plain(piece, mine, source, right, group):
        wide = PIECES[piece][2]
        half = c if mine else 1 - c
        rows = pl.ds(LEFT * group, LEFT)
        base = ring_count[0]

        def step(j):
            lanes = at(j, TILE)
            before, write, after = keep(piece, rows, lanes) if mine else give(
                piece, rows, lanes, base + j, group * (wide // TILE) + j
            )
            before()
            write(dot_nn(source[...], right[:, pl.ds(pl.multiple_of(half * wide + j * TILE, 128), TILE)]))
            after()

        each(wide // TILE, step)
        if not mine:
            ring_count[0] += wide // TILE
        if wide % TILE:
            start = wide - 128
            value = dot_nn(source[...], right[:, pl.ds(pl.multiple_of(half * wide + start, 128), 128)])
            if mine:
                own[piece][rows, start:wide] = value.astype(BF16)
            else:
                number = tail_count[0]
                tail_count[0] += 1
                groups = SHAPES[PIECES[piece][0]][0] // 24
                tails[number] = value.astype(BF16)
                tail_copy(piece, rows, pl.ds(start, 128), number, groups * (wide // TILE) + group).start()

    def wide_product(piece, mine):
        half = c if mine else 1 - c
        wide, skip, width = half_of(piece), PIECES[piece][1], PIECES[piece][2]
        base = ring_count[0]

        def start_of(j):
            return pl.multiple_of(half * wide + skip + j * TILE, 128)

        def both(j, size=TILE):
            return dot_nn(left[2][...], glog_v[:, pl.ds(start_of(j), size)]) + dot_nn(
                left[3][...], chosen(start_of(j))[:, 0:size]
            )

        def target(j):
            lanes = at(j, TILE)
            return keep(piece, whole, lanes) if mine else give(piece, whole, lanes, base + j, j)

        def step(j):
            before, write, after = target(j)
            before()
            write(both(j))
            after()

        if not mine:
            ring_count[0] += width // TILE
        if skip == 0:
            each(width // TILE, step)
            return
        each(1, step)
        before, write, after = target(1)
        before()
        norm_part = jnp.where(half == 1, norm_t[...], 0.0).T
        write(both(1) + jnp.concatenate((jnp.zeros((LEFT, TILE - 128), F32), norm_part), 1))
        after()

        def by_half(j, size, write):
            @pl.when(half == 0)
            def _():
                write(both(j, size))

            @pl.when(half == 1)
            def _():
                write(dot_nn(left[3][...], chosen(start_of(j))[:, 0:size]))

        for j in (2, 3):
            before, write, after = target(j)
            before()
            by_half(j, TILE, write)
            after()

        def write_tail(value):
            if mine:
                own[piece][whole, width - 128 : width] = value.astype(BF16)
            else:
                tails[tail_count[0]] = value.astype(BF16)

        by_half(4, 128, write_tail)
        if not mine:
            tail_copy(piece, whole, pl.ds(width - 128, 128), tail_count[0], width // TILE).start()
            tail_count[0] += 1

    def products(piece, mine):
        loaded(piece)
        if piece in (1, 2):
            wide_product(piece, mine)
        elif piece == 4:
            if not mine:
                for group in range(4):
                    source = left[5 + group % 2]
                    if group >= 2:
                        loads[piece][1 + group % 2].wait()
                    plain(piece, False, source, gffn_v, group)
                    plain(piece, True, source, gffn_v, group)
                    if group < 2:
                        again = pltpu.make_async_copy(act_part(group + 2), source, load_sem.at[12 + group])
                        again.start()
                        loads[piece][1 + group] = again
        else:
            source, right = {0: (left[1], gqkv_v), 3: (left[0], gh_v), 5: (left[4], gattn_v)}[piece]
            plain(piece, mine, source, right, 0)

    def combine(piece, target, parts):
        def some(rows, lanes):
            total = parts[0][rows, lanes].astype(F32)
            for member in parts[1:]:
                total = total + member[rows, lanes].astype(F32)
            target[rows, lanes] = total.astype(target.dtype)

        wide = PIECES[piece][2]
        if piece == 4:
            each(4, lambda group: some(at(group, 48), slice(0, wide)))
            return
        if wide >= 512:
            each(wide // 512, lambda j: some(slice(0, 48), at(j, 512)))
        if wide % 512:
            some(slice(0, 48), slice(wide // 512 * 512, wide))

    def hop(piece, k, land, index, sems, way):
        return pltpu.make_async_remote_copy(
            src_ref=slot(own, piece, k),
            dst_ref=slot(land, piece, index),
            send_sem=sems[0].at[piece, index],
            recv_sem=sems[1].at[piece, index],
            device_id=peers[way],
            device_id_type=MESH,
        )

    FIRST, SECOND = (first_send, first_recv), (second_send, second_recv)

    def landed(piece, land, index, sems):
        hop(piece, me, land, index, sems, XWAY).wait_recv()

    def block(piece, a, b, far):
        return chip(far, a, b) if SUM_WAY[piece] in (0, 3) else chip(far, b, a)

    def split(piece):
        return (y, x, YWAY, XWAY) if SUM_WAY[piece] in (0, 3) else (x, y, XWAY, YWAY)

    readied = set()

    def ready(piece):
        if piece in readied:
            return
        readied.add(piece)
        wide, groups = PIECES[piece][2], SHAPES[PIECES[piece][0]][0] // 24
        for group in range(groups):
            for j in range(wide // TILE):
                ring_copy(piece, pl.ds(LEFT * group, LEFT), at(j, TILE), 0, group * (wide // TILE) + j).wait_recv()
            if wide % TILE:
                index = groups * (wide // TILE) + group
                tail_copy(piece, pl.ds(LEFT * group, LEFT), pl.ds(wide - 128, 128), 0, index).wait_recv()

    def both_cores(piece, k):
        return (slot(own, piece, k), slot(side, piece, k))

    def rest_of(piece):
        return SUM_WAY[piece] > 1

    def first_block(piece, i):
        a, b, way, _ = split(piece)
        if rest_of(piece):
            return block(piece, 1 - a, (1 - b) if i else b, z), i, way
        t, v = near_first(z, i // 2), (1 - b) if i % 2 == 0 else b
        return block(piece, 1 - a, v, t), 2 * t + v, way

    def second_block(piece, i):
        a, b, _, way = split(piece)
        if rest_of(piece):
            return block(piece, a, 1 - b, z), 0, way
        t = near_first(z, i)
        return block(piece, a, 1 - b, t), t, way

    def z_block(piece, i):
        a, b, _, _ = split(piece)
        if rest_of(piece):
            t, q = near_first(z, 3 - i // 4), i % 4
            k = block(piece, (1 - a) if q // 2 else a, (1 - b) if q % 2 else b, t)
        else:
            t, q = near_first(z, 3 - i), 0
            k = block(piece, a, b, t)
        return k, t, q, (z - t + 3) // 4

    def plane_count(piece):
        return 4 if rest_of(piece) else 1

    def z_copy(piece, i):
        k, t, q, down = z_block(piece, i)
        n = plane_count(piece)
        there = (t - z - 1 + 6 * down) * n + q
        return pltpu.make_async_remote_copy(
            src_ref=slot(own, piece, k),
            dst_ref=slot(column, piece, there),
            send_sem=z_send.at[piece, t * n + q],
            recv_sem=z_recv.at[piece, there],
            device_id=device(z + 1 - 2 * down, y, x, c),
            device_id_type=MESH,
        )

    def z_landed(piece, index):
        pltpu.make_async_remote_copy(
            src_ref=slot(own, piece, me),
            dst_ref=slot(column, piece, index),
            send_sem=z_send.at[piece, 0],
            recv_sem=z_recv.at[piece, index],
            device_id=peers[XWAY],
            device_id_type=MESH,
        ).wait_recv()
        return slot(column, piece, index)

    def first_slot(piece, index):
        landed(piece, first, index, FIRST)
        return (slot(first, piece, index),)

    def second_slot(piece, index):
        landed(piece, second, index, SECOND)
        return (slot(second, piece, index),)

    def with_ends(piece, target, parts, q):
        low, high = q, 4 * plane_count(piece) + q

        @pl.when(z == 0)
        def _():
            combine(piece, target, parts + (z_landed(piece, high),))

        @pl.when(z == 3)
        def _():
            combine(piece, target, parts + (z_landed(piece, low),))

        @pl.when((z > 0) & (z < 3))
        def _():
            combine(piece, target, parts + (z_landed(piece, low), z_landed(piece, high)))

    def first_send_of(piece, i):
        ready(piece)
        k, index, way = first_block(piece, i)
        if rest_of(piece):
            with_ends(piece, slot(own, piece, k), both_cores(piece, k), 2 + i)
        else:
            combine(piece, slot(own, piece, k), both_cores(piece, k))
        hop(piece, k, first, index, FIRST, way).start()

    def second_send_of(piece, i):
        k, index, way = second_block(piece, i)
        if rest_of(piece):
            with_ends(piece, slot(own, piece, k), both_cores(piece, k) + first_slot(piece, 1), 1)
        else:
            parts = first_slot(piece, 2 * index + 1 - split(piece)[1])
            combine(piece, slot(own, piece, k), both_cores(piece, k) + parts)
        hop(piece, k, second, index, SECOND, way).start()

    def z_send_of(piece, i):
        ready(piece)
        k, t, q, down = z_block(piece, i)
        parts = both_cores(piece, k)
        if not rest_of(piece):
            parts = parts + first_slot(piece, 2 * t + split(piece)[1]) + second_slot(piece, t)

        @pl.when((z == 0) | (z == 3))
        def _():
            combine(piece, slot(own, piece, k), parts)

        @pl.when((z > 0) & (z < 3))
        def _():
            came = z_landed(piece, (t - z + 4 * down) * plane_count(piece) + q)
            combine(piece, slot(own, piece, k), parts + (came,))

        z_copy(piece, i).start()

    swaps = []

    def finish(piece):
        if rest_of(piece):
            parts = first_slot(piece, 0) + second_slot(piece, 0)
        else:
            parts = first_slot(piece, 2 * z + split(piece)[1]) + second_slot(piece, z)
        with_ends(piece, fin[piece], both_cores(piece, me) + parts, 0)
        m, skip, wide = PIECES[piece]
        size = SHAPES[m][0]
        lanes = pl.ds(pl.multiple_of(c * half_of(piece) + skip, 128), wide)
        swaps.append(
            pltpu.make_async_remote_copy(
                src_ref=fin[piece].at[pl.ds(pl.multiple_of((1 - c) * size, 8), size), :],
                dst_ref=outs[m].at[:, lanes],
                send_sem=swap_send.at[piece],
                recv_sem=swap_recv.at[piece],
                device_id=peers[SIDE],
                device_id_type=MESH,
            )
        )
        swaps[-1].start()
        squared = fin[piece][...] * fin[piece][...] + SQUARE_FLOOR
        lane_plane[spot, :, HALF_AT[m] + skip : HALF_AT[m] + skip + wide] = jnp.sum(squared, 0, keepdims=True)
        outs[m][:, lanes] = fin[piece][pl.ds(pl.multiple_of(c * size, 8), size), :]

    for task in TASKS:
        piece, number = task // 32, task % 32
        if number < 2:
            products(piece, number == 1)
        elif number == 17:
            finish(piece)
        elif rest_of(piece):
            if number < 14:
                z_send_of(piece, number - 2)
            elif number < 16:
                first_send_of(piece, number - 14)
            else:
                second_send_of(piece, 0)
        elif number < 10:
            first_send_of(piece, number - 2)
        elif number < 14:
            second_send_of(piece, number - 10)
        else:
            z_send_of(piece, number - 14)

    def spread(source, target, send, recv, peer):
        copy = pltpu.make_async_remote_copy(
            src_ref=source, dst_ref=target, send_sem=send, recv_sem=recv, device_id=peer, device_id_type=MESH
        )
        copy.start()
        return copy

    def arrive(copies):
        for copy in copies:
            copy.wait_recv()
        return copies

    plane_copies = [
        spread(lane_plane.at[spot], lane_plane.at[spot], lane_send.at[i], lane_recv.at[i], plane_peers[i])
        for i in range(3)
    ]
    for swap in swaps:
        swap.wait()
    sides, gs = statistics(outs, side_olds)

    def spread_eight(buffers, value, send, recv):
        buffers[0][2 * spot + c] = value
        mine = buffers[0].at[2 * spot + c]
        return [spread(mine, mine, send.at[i], recv.at[i], greeted[3 + i]) for i in range(7)]

    def spread_four(buffers, send, recv):
        total = [buffers[0][2 * i] + buffers[0][2 * i + 1] for i in range(4)]
        buffers[1][z] = (total[0] + total[1]) + (total[2] + total[3])
        mine = buffers[1].at[z]
        return [spread(mine, mine, send.at[7 + i], recv.at[7 + i], column_peers[i]) for i in range(3)]

    def four(buffer):
        return (buffer[0] + buffer[1]) + (buffer[2] + buffer[3])

    scalars = lanes_of([jnp.sum(member, 0, keepdims=True) for member in sides] + [loss[...]])
    scalars = jnp.concatenate((scalars, squares[...]), 1)
    sent = spread_eight(scalar_sums, scalars, scalar_send, scalar_recv)
    sent += arrive(plane_copies)
    lane_z[z] = four(lane_plane)
    z_copies = [
        spread(lane_z.at[z], lane_z.at[z], lane_send.at[3 + i], lane_recv.at[3 + i], column_peers[i]) for i in range(3)
    ]
    arrive(sent[0:7])
    last_copies = spread_four(scalar_sums, scalar_send, scalar_recv)
    sent += arrive(z_copies)
    lane_halves[c] = four(lane_z)
    halves_copy = spread(lane_halves.at[c], lane_halves.at[c], lane_send.at[6], lane_recv.at[6], peers[SIDE])
    sent += arrive(last_copies)
    sent += arrive([halves_copy])
    pair = (lane_halves[0], lane_halves[1])
    lanes = [half[:, HALF_AT[m] : HALF_AT[m] + SHAPES[m][1] // 2] for m in range(5) for half in pair]
    sums = jnp.concatenate(lanes + [four(scalar_sums[1])], 1)
    sums_out[...] = sums
    updates = updates_of(sums, gs, sides, lane_olds, moment)[0]
    totals = lanes_of(
        [total_sum(update * update) for update in updates[:6]]
        + [jnp.sum(updates[6][i : i + 1] * updates[6][i : i + 1], 1, keepdims=True) for i in range(6)]
    )
    sent += arrive(spread_eight(total_sums, totals, total_send, total_recv))
    sent += arrive(spread_four(total_sums, total_send, total_recv))
    totals_out[...] = four(total_sums[1])
    for copy in sent:
        copy.wait_send()
    for piece in range(6):
        for i in range(2 if rest_of(piece) else 8):
            k, index, way = first_block(piece, i)
            hop(piece, k, first, index, FIRST, way).wait_send()
        for i in range(1 if rest_of(piece) else 4):
            k, index, way = second_block(piece, i)
            hop(piece, k, second, index, SECOND, way).wait_send()
        for i in range(12 if rest_of(piece) else 3):
            z_copy(piece, i).wait_send()
    for number in range(ring_count[0] - 3, ring_count[0]):
        ring_copy(1, whole, pl.ds(0, TILE), number, 0).wait_send()
    for number in range(tail_count[0]):
        tail_copy(1, whole, pl.ds(0, 128), number, 0).wait_send()


def statistics(grads, side_olds):
    wide_g = grads[E_][...]
    gs = (wide_g[:, :VOCAB], wide_g[:, PLACE_AT:]) + tuple(grads[m][...] for m in (Q_, O_, I_, D_))
    decay = 1.0 - STEP ** (-0.8)
    sides = []
    for index in range(6):
        mean = jnp.sum(gs[index] * gs[index] + SQUARE_FLOOR, 1, keepdims=True) / gs[index].shape[1]
        sides.append(decay * column_of(as_row(side_olds[index])) + (1.0 - decay) * mean)
    return sides, gs + (wide_g[:, 4096:4224],)


def updates_of(sums, gs, sides, lane_olds, moment):
    decay = 1.0 - STEP ** (-0.8)
    fresh = 1.0 - decay
    parts = [sums[:, :VOCAB], sums[:, PLACE_AT:WIDE]]
    parts += [sums[:, SUM_AT[i] : SUM_AT[i + 1]] for i in range(1, 5)]
    scalars = sums[:, SUM_AT[5] : SUM_AT[5] + 128]
    updates, lane_news = [], []
    for index in range(6):
        height = gs[index].shape[0] * 32
        lane_news.append(decay * as_row(lane_olds[index]) + fresh * (parts[index] / height))
        if index < 2:
            mean = jnp.sum(lane_news[index], 1, keepdims=True) / lane_news[index].shape[1]
        else:
            mean = lane_at(scalars, index) / height
        updates.append(gs[index] * lax.rsqrt(sides[index] * lane_news[index] / mean))
    norm_g = jnp.concatenate([row_of(lane_at(gs[6], NORM_AT - 4096 + i)) for i in range(6)], 0)
    moment_new = decay * moment[...] + fresh * (norm_g * norm_g + SQUARE_FLOOR)
    updates.append(norm_g * lax.rsqrt(moment_new))
    return updates, lane_news, norm_g, moment_new


def reduce_grads(large, small):
    tokens = 5 * SPAN
    vmem, hbm = pl.BlockSpec(memory_space=pltpu.VMEM), pl.BlockSpec(memory_space=pl.ANY)
    dma = pltpu.SemaphoreType.DMA
    scratch = []
    for counts in ((16, 16), (16, 16), (8, 2), (4, 1), (5, 20)):
        for (m, _, wide), way in zip(PIECES, SUM_WAY):
            scratch.append(pltpu.VMEM((counts[way // 2] * 2 * SHAPES[m][0], wide), BF16))
    scratch += [pltpu.VMEM((2 * SHAPES[m][0], wide), F32) for m, _, wide in PIECES]
    scratch += [pltpu.VMEM((LEFT, tokens), BF16)] * 7
    scratch += [pltpu.VMEM((tokens, width), BF16) for width in (TABLE_END, 3 * D, D, 4 * D, D)]
    scratch += [pltpu.VMEM((3, LEFT, TILE), BF16), pltpu.VMEM((7, LEFT, 128), BF16), pltpu.VMEM((128, D), F32)]
    scratch += [pltpu.VMEM((count, 1, HALF_SUMS), F32) for count in (4, 4, 2)]
    scratch += [pltpu.VMEM((count, 1, width), F32) for width in (256, 128) for count in (8, 4)]
    scratch += [dma((14,)), dma((3,)), dma((7,)), dma((6, 10)), dma((6, 8)), dma((6, 8)), dma((6, 4)), dma((6, 4))]
    scratch += [dma((6, 16)), dma((6, 20)), dma((6,)), dma((6,))]
    scratch += [dma((7,))] * 2 + [dma((10,))] * 4
    return pl.pallas_call(
        reduce_kernel,
        out_shape=[jax.ShapeDtypeStruct(shape, F32) for shape in SHAPES + ((1, SUMS), (1, 128))],
        in_specs=[hbm] * 11 + [vmem] * len(small),
        out_specs=[vmem] * 7,
        scratch_shapes=scratch,
        compiler_params=pltpu.CompilerParams(
            collective_id=1, has_side_effects=True, vmem_limit_bytes=63 * 1024 * 1024
        ),
    )(*large, *small)


def update_kernel(*refs):
    copies = [pltpu.make_async_copy(refs[i], refs[55 + i], refs[82].at[i]) for i in range(27)]
    for copy in copies:
        copy.start()
    for copy in copies:
        copy.wait()
    refs = refs[55:82] + refs[27:55]
    grads, sums, totals, ws, norms = refs[0:5], refs[5], refs[6], refs[7:13], refs[13]
    lane_olds, side_olds, moment = refs[14:20], refs[20:26], refs[26]
    loss_out, table_g, place_g, norm_g_out = refs[27:31]
    lane_outs, side_outs, moment_out, news, norm_new = refs[31:37], refs[37:43], refs[43], refs[44:50], refs[50]
    grad_outs = refs[51:55]
    sides, gs = statistics(grads, side_olds)
    updates, lane_news, norm_g, moment_new = updates_of(sums[...], gs, sides, lane_olds, moment)
    scalars = sums[:, SUM_AT[5] : SUM_AT[5] + 128]
    squares = sums[:, SUM_AT[5] + 128 :]
    loss_out[...] = lane_at(scalars, 6)
    table_g[...] = gs[0]
    place_g[...] = gs[1]
    norm_g_out[...] = norm_g
    moment_out[...] = moment_new
    for index in range(6):
        lane_outs[index][...] = lane_news[index].reshape(lane_outs[index].shape)
        side_outs[index][...] = row_of(sides[index]).reshape(side_outs[index].shape)
        if index >= 2:
            grad_outs[index - 2][...] = gs[index]
        entries = gs[index].shape[0] * gs[index].shape[1] * 32
        clip = jnp.maximum(1.0, jnp.sqrt(lane_at(totals[...], index) / entries))
        scale = learn_rate * jnp.sqrt(lane_at(squares, index) / entries) / clip
        news[index][...] = ws[index][...] - scale * updates[index]
    for i in range(6):
        clip = jnp.maximum(1.0, jnp.sqrt(lane_at(totals[...], 6 + i) / D))
        scale = learn_rate * jnp.sqrt(lane_at(squares, 6 + i) / D) / clip
        norm_new[i : i + 1, :] = norms[i : i + 1, :] - scale * updates[6][i : i + 1, :]


def update_weights(operands):
    lanes = (VOCAB, 512, 3 * D, D, 4 * D, D)
    held = (24, 24, 24, 24, 24, 96)
    shapes = [(1, 1), (24, VOCAB), (24, 512), (6, 24)]
    shapes += [(lane,) for lane in lanes] + [(size,) for size in held] + [(6, 24)]
    shapes += list(zip(held, lanes)) + [(6, 24)] + list(zip(held, lanes))[2:]
    return pl.pallas_call(
        update_kernel,
        out_shape=[jax.ShapeDtypeStruct(shape, F32) for shape in shapes],
        in_specs=[pl.BlockSpec(memory_space=pl.ANY)] * len(operands),
        out_specs=[pl.BlockSpec(memory_space=pltpu.VMEM)] * len(shapes),
        scratch_shapes=[pltpu.VMEM(member.shape, member.dtype) for member in operands]
        + [pltpu.SemaphoreType.DMA((len(operands),))],
        compiler_params=pltpu.CompilerParams(vmem_limit_bytes=63 * 1024 * 1024),
    )(*operands)


def norm_forward(value, gain, shift):
    centred = value - jnp.mean(value, -1, keepdims=True)
    inverse = lax.rsqrt(jnp.mean(centred * centred, -1, keepdims=True) + EPSILON)
    normed = centred * inverse
    return (normed * gain + shift, normed, inverse)


def norm_backward(grad_out, normed, inverse, gain):
    scaled = grad_out * gain
    back = inverse * (
        scaled
        - jnp.mean(scaled, -1, keepdims=True)
        - normed * jnp.mean(scaled * normed, -1, keepdims=True)
    )
    return (back, jnp.sum(grad_out * normed, 0), jnp.sum(grad_out, 0))


def mm(left, right, sides):
    return lax.dot_general(left, right, ((sides[:1], sides[1:]), ((), ())), preferred_element_type=F32)


def attend(qkv, allowed):
    by_head = qkv.reshape(qkv.shape[0], 3, HEADS, HEAD_DIM)
    query, key, value = by_head[:, 0], by_head[:, 1], by_head[:, 2]
    scores = jnp.einsum("qhe,khe->hqk", query, key, preferred_element_type=F32) * 0.125
    scores = jnp.where(allowed[None], scores, -1e30)
    highest = jnp.max(scores, -1, keepdims=True)
    raised = jnp.exp(scores - highest)
    summed = jnp.sum(raised, -1, keepdims=True)
    shares = (raised / summed).astype(BF16)
    mixture = jnp.einsum("hqk,khe->qhe", shares, value, preferred_element_type=F32)
    return mixture.astype(BF16).reshape(qkv.shape[0], D), highest + jnp.log(summed)


def attend_back(qkv, allowed, log_total, grad_mix):
    by_head = qkv.reshape(qkv.shape[0], 3, HEADS, HEAD_DIM)
    query, key, value = by_head[:, 0], by_head[:, 1], by_head[:, 2]
    grad_mix = grad_mix.reshape(qkv.shape[0], HEADS, HEAD_DIM)
    scores = jnp.einsum("qhe,khe->hqk", query, key, preferred_element_type=F32) * 0.125
    scores = jnp.where(allowed[None], scores, -1e30)
    shares = jnp.exp(scores - log_total)
    grad_share = jnp.einsum("qhe,khe->hqk", grad_mix, value, preferred_element_type=F32)
    grad_score = (shares * (grad_share - jnp.sum(shares * grad_share, -1, keepdims=True))).astype(BF16)
    grad_query = jnp.einsum("hqk,khe->qhe", grad_score, key, preferred_element_type=F32) * 0.125
    grad_key = jnp.einsum("hqk,qhe->khe", grad_score, query, preferred_element_type=F32) * 0.125
    grad_value = jnp.einsum("hqk,qhe->khe", shares.astype(BF16), grad_mix, preferred_element_type=F32)
    return jnp.stack((grad_query, grad_key, grad_value), 1).astype(BF16).reshape(qkv.shape)


def on_slice(token_arrays, lengths, weights, lane_olds, side_olds, moment):
    olds = lane_olds + side_olds + (moment,)
    found = front(token_arrays + weights, lengths)
    mask_count, gains, side, cols, keys, weight_sq = found[0:6]
    x_t, mix, a, act, y, slope, qkv_b, normed_a = found[6:14]
    normed_bc, (qkv_w, out_w, in_w, down_w, wide_w) = found[14:18], found[18:23]
    found = middle(
        (wide_w, qkv_w, out_w, in_w, down_w, y, act, a, mix, slope, qkv_b, normed_a) + tuple(normed_bc),
        (cols, keys, side, gains, mask_count),
    )
    loss_part, norm_sums = found[0:2]
    grad_logit, y_t, a_t, mix_t, act_t, ge_t, grad_ffn, grad_hidden, grad_attn, grad_qkv = found[2:]
    reduced = reduce_grads(
        (y_t, ge_t, grad_logit, x_t, grad_qkv, mix_t, grad_attn, a_t, grad_hidden, act_t, grad_ffn),
        (cols, norm_sums, loss_part, weight_sq) + olds,
    )
    found = update_weights(tuple(reduced) + weights + olds)
    grads = (None,) + tuple(found[24:28])
    mask_count = mask_count.reshape(())
    loss_sum, table_g, place_g, norm_g = found[0:4]
    lane_news = found[4:10]
    side_news = found[10:16]
    moment_new, norm_new = found[16], found[23]
    news = found[17:23]
    return (
        loss_sum.reshape(()),
        mask_count,
        table_g.T,
        place_g.T,
        grads[1],
        grads[2],
        grads[3],
        grads[4],
        norm_g.T,
        lane_news[0],
        side_news[0],
        lane_news[1],
        side_news[1],
        side_news[2],
        lane_news[2],
        side_news[3],
        lane_news[3],
        side_news[4],
        lane_news[4],
        side_news[5],
        lane_news[5],
        moment_new.T,
        news[0].T,
        news[1].T,
        news[2],
        news[3],
        news[4],
        news[5],
        norm_new.T,
    )


def on_device(
    whole_mesh,
    long_ids,
    long_targets,
    long_mask,
    long_lengths,
    short_ids,
    short_targets,
    short_mask,
    short_lengths,
    table,
    position,
    qkv_weight,
    out_weight,
    in_weight,
    down_weight,
    norms,
    table_rows,
    table_cols,
    position_rows,
    position_cols,
    qkv_rows,
    qkv_cols,
    out_rows,
    out_cols,
    in_rows,
    in_cols,
    down_rows,
    down_cols,
    norm_moment,
):
    if whole_mesh == (8, 4):
        return on_slice(
            (long_ids, long_targets, long_mask, short_ids, short_targets, short_mask),
            (long_lengths, short_lengths),
            (table.T, position.T, qkv_weight, out_weight, in_weight, down_weight, norms.T),
            (table_rows, position_rows, qkv_cols, out_cols, in_cols, down_cols),
            (table_cols, position_cols, qkv_rows, out_rows, in_rows, down_rows),
            norm_moment.T,
        )
    devices = lax.axis_size(("dp", "seq"))
    seq_index = lax.axis_index("seq")
    held = norms.shape[0]

    span = long_ids.shape[1]
    long_place = seq_index * span + lax.iota(jnp.int32, span)
    long_keep = (long_place[None, :] < long_lengths[:, None]).astype(jnp.int32)
    short_keep = (lax.iota(jnp.int32, SPAN)[None, :] < short_lengths[:, None]).astype(jnp.int32)
    long_pack = jnp.stack((long_ids, long_targets, long_mask * long_keep, long_keep), 1)
    short_pack = jnp.stack((short_ids, short_targets, short_mask * short_keep, short_keep), 1)
    moved = lax.all_to_all(
        jnp.concatenate((long_pack, short_pack[1:]), 0), "seq", split_axis=0, concat_axis=0, tiled=True
    )
    tokens = jnp.concatenate((moved, short_pack[:1]), 0)
    ids, targets, weight, keep = (tokens[:, i].reshape(-1) for i in range(4))
    weight = weight.astype(F32)
    count = tokens.shape[0] * span
    last = count - span
    alone = seq_index == lax.axis_size("seq") - 1
    token = lax.iota(jnp.int32, count)
    place = jnp.where(alone | (token >= last), token % span, token)
    row = jnp.where(alone | (token >= last), token // span, 0)
    allowed_long = (row[:last, None] == row[None, :last]) & (keep[None, :last] > 0)
    allowed_short = jnp.broadcast_to(keep[None, last:] > 0, (span, span))

    here_count = jnp.sum(long_pack[:, 2]) + jnp.sum(short_pack[:, 2])
    tall = table.T
    counts = jnp.broadcast_to(jnp.stack((here_count // 256, here_count % 256)).astype(F32)[None], (held, 2))
    wide_shard = jnp.concatenate(
        (tall, norms, counts, jnp.zeros((held, PLACE_AT - COUNT_AT - 2), F32), position.T), 1
    )
    shards = (wide_shard, qkv_weight, out_weight, in_weight, down_weight)
    wide_w, qkv_w, out_w, in_w, down_w = (
        lax.all_gather(shard.astype(BF16), ("dp", "seq"), axis=0, tiled=True) for shard in shards
    )
    column = lax.broadcasted_iota(jnp.int32, (1, WIDE), 1)
    chosen = ((ids[:, None] == column) | ((place[:, None] + PLACE_AT) == column)).astype(BF16)
    gains = wide_w[:, NORM_AT : NORM_AT + 6].astype(F32)
    sums = jnp.sum(wide_w[:, COUNT_AT : COUNT_AT + 2].astype(F32), 0)
    mask_count = (sums[0] * 256.0 + sums[1]) / held
    inverse_count = 1.0 / mask_count

    embedded = mm(chosen, wide_w, (1, 1))
    first, normed_a, inverse_a = norm_forward(embedded, gains[:, 0], gains[:, 1])
    first_b = first.astype(BF16)
    qkv_b = mm(first_b, qkv_w, (1, 0)).astype(BF16)
    mix_long, total_long = attend(qkv_b[:last], allowed_long)
    mix_short, total_short = attend(qkv_b[last:], allowed_short)
    mixture = jnp.concatenate((mix_long, mix_short), 0)
    second, normed_b, inverse_b = norm_forward(first + mm(mixture, out_w, (1, 0)), gains[:, 2], gains[:, 3])
    second_b = second.astype(BF16)
    hidden = mm(second_b, in_w, (1, 0))
    active, slope = gelu_pair(hidden)
    active_b = active.astype(BF16)
    third, normed_c, inverse_c = norm_forward(second + mm(active_b, down_w, (1, 0)), gains[:, 4], gains[:, 5])
    third_b = third.astype(BF16)
    logits = jnp.where(column < VOCAB, mm(third_b, wide_w, (1, 0)), -1e30)
    highest = jnp.max(logits, -1, keepdims=True)
    log_sum = highest + jnp.log(jnp.sum(jnp.exp(logits - highest), -1, keepdims=True))
    onehot = targets[:, None] == column
    picked = jnp.sum(jnp.where(onehot, logits, 0.0), -1)
    loss_part = jnp.sum(weight * (log_sum[:, 0] - picked))
    grad_logit = (
        (jnp.exp(logits - log_sum) - onehot.astype(F32)) * (weight * inverse_count)[:, None]
    ).astype(BF16)
    grad_third = mm(grad_logit, wide_w, (1, 1))
    grad_second, gain_c, shift_c = norm_backward(grad_third, normed_c, inverse_c, gains[:, 4])
    grad_ffn = grad_second.astype(BF16)
    down_grad = mm(active_b, grad_ffn, (0, 0)).astype(BF16)
    grad_hidden = (mm(grad_ffn, down_w, (1, 1)) * slope).astype(BF16)
    in_grad = mm(second_b, grad_hidden, (0, 0)).astype(BF16)
    grad_second = grad_second + mm(grad_hidden, in_w, (1, 1))
    grad_first, gain_b, shift_b = norm_backward(grad_second, normed_b, inverse_b, gains[:, 2])
    grad_attn = grad_first.astype(BF16)
    out_grad = mm(mixture, grad_attn, (0, 0)).astype(BF16)
    grad_mix = mm(grad_attn, out_w, (1, 1)).astype(BF16)
    grad_qkv = jnp.concatenate(
        (
            attend_back(qkv_b[:last], allowed_long, total_long, grad_mix[:last]),
            attend_back(qkv_b[last:], allowed_short, total_short, grad_mix[last:]),
        ),
        0,
    )
    qkv_grad = mm(first_b, grad_qkv, (0, 0)).astype(BF16)
    grad_first = grad_first + mm(grad_qkv, qkv_w, (1, 1))
    grad_embed, gain_a, shift_a = norm_backward(grad_first, normed_a, inverse_a, gains[:, 0])
    wide_grad = mm(
        jnp.concatenate((third_b, grad_embed.astype(BF16)), 0),
        jnp.concatenate((grad_logit, chosen), 0),
        (0, 0),
    )
    norm_part = jnp.stack((gain_a, shift_a, gain_b, shift_b, gain_c, shift_c), 1)
    wide_grad = lax.dynamic_update_slice(wide_grad.astype(BF16), norm_part.astype(BF16), (0, NORM_AT))
    grads = (wide_grad, qkv_grad, out_grad, in_grad, down_grad)
    wide_g, qkv_g, out_g, in_g, down_g = (
        lax.psum_scatter(grad.astype(F32), ("dp", "seq"), scatter_dimension=0, tiled=True) for grad in grads
    )
    table_g, place_g = wide_g[:, :VOCAB], wide_g[:, PLACE_AT:]
    norm_g = wide_g[:, NORM_AT : NORM_AT + 6]

    decay = 1.0 - STEP ** (-0.8)
    matrices = (
        (qkv_weight, qkv_g, qkv_rows, qkv_cols),
        (out_weight, out_g, out_rows, out_cols),
        (in_weight, in_g, in_rows, in_cols),
        (down_weight, down_g, down_rows, down_cols),
    )
    wide = (
        (tall, table_g, table_cols, table_rows),
        (position.T, place_g, position_cols, position_rows),
    )
    row_news = [
        decay * member[2] + (1.0 - decay) * jnp.mean(member[1] * member[1] + SQUARE_FLOOR, 1)
        for member in matrices + wide
    ]
    col_parts = [jnp.sum(member[1] * member[1] + SQUARE_FLOOR, 0) for member in matrices + wide]
    row_totals = jnp.stack([jnp.sum(rows_new) for rows_new in row_news])
    weight_sq = jnp.stack([jnp.sum(member[0] * member[0]) for member in matrices + wide])
    stats = lax.psum(
        col_parts + [row_totals, weight_sq, jnp.sum(norms * norms, 0), loss_part.reshape(1)], ("dp", "seq")
    )
    updates = []
    cols_out = []
    for index, member in enumerate(matrices + wide):
        full_rows = member[0].shape[0] * devices
        cols_new = decay * member[3] + (1.0 - decay) * stats[index] / full_rows
        if index < 4:
            mean = stats[6][index] / full_rows
        else:
            mean = jnp.mean(cols_new)
        updates.append(member[1] * lax.rsqrt(row_news[index][:, None] * cols_new[None, :] / mean))
        cols_out.append(cols_new)
    moment_new = decay * norm_moment + (1.0 - decay) * (norm_g * norm_g + SQUARE_FLOOR)
    norm_update = norm_g * lax.rsqrt(moment_new)
    update_sq = jnp.stack([jnp.sum(update * update) for update in updates])
    totals = lax.psum((update_sq, jnp.sum(norm_update * norm_update, 0)), ("dp", "seq"))
    news = []
    for index, member in enumerate(matrices + wide):
        entries = member[0].shape[0] * member[0].shape[1] * devices
        clip = jnp.maximum(1.0, jnp.sqrt(totals[0][index] / entries))
        news.append(
            member[0] - learn_rate * jnp.sqrt(stats[7][index] / entries) * updates[index] / clip
        )
    norm_rows = norms.shape[0] * devices
    norm_clip = jnp.maximum(1.0, jnp.sqrt(totals[1] / norm_rows))
    norm_new = norms - learn_rate * jnp.sqrt(stats[8] / norm_rows) * norm_update / norm_clip
    return (
        stats[9][0],
        mask_count,
        table_g.T,
        place_g.T,
        qkv_g,
        out_g,
        in_g,
        down_g,
        norm_g,
        cols_out[4],
        row_news[4],
        cols_out[5],
        row_news[5],
        row_news[0],
        cols_out[0],
        row_news[1],
        cols_out[1],
        row_news[2],
        cols_out[2],
        row_news[3],
        cols_out[3],
        moment_new,
        news[4].T,
        news[5].T,
        news[0],
        news[1],
        news[2],
        news[3],
        norm_new,
    )


def solution(mesh):
    split, wide = P(("dp", "seq"), None), P(None, ("dp", "seq"))
    shard, same = P(("dp", "seq")), P()
    return jax.shard_map(
        functools.partial(on_device, (mesh.shape["dp"], mesh.shape["seq"])),
        mesh=mesh,
        in_specs=(P("dp", "seq"),) * 3
        + (P("dp"),)
        + (split,) * 3
        + (shard,)
        + (wide,) * 2
        + (split,) * 5
        + (same, shard) * 2
        + (shard, same) * 4
        + (split,),
        out_specs=(same, same)
        + (wide,) * 2
        + (split,) * 5
        + (same, shard) * 2
        + (shard, same) * 4
        + (split,)
        + (wide,) * 2
        + (split,) * 5,
        check_vma=False,
    )
```

```python
import functools

import jax
import jax.numpy as jnp
from jax import lax
from jax.experimental import pallas as pl
from jax.experimental.pallas import tpu as pltpu
from jax.sharding import PartitionSpec as P

D = 768
HEADS = 12
HEAD_DIM = 64
VOCAB = 4101
STEP = 10
SPAN = 128

EPSILON = 1e-12
SQUARE_FLOOR = 1e-30
learn_rate = 0.3

MESH = pl.DeviceIdType.MESH
F32 = jnp.float32
BF16 = jnp.bfloat16

NORM_AT = VOCAB
COUNT_AT = VOCAB + 6
TABLE_END = 4352
PLACE_AT = 4352
WIDE = PLACE_AT + 512

SHAPES = ((24, WIDE), (24, 3 * D), (24, D), (24, 4 * D), (96, D))
E_, Q_, O_, I_, D_ = range(5)
CLASS_A, CLASS_B, CLASS_C = (E_, O_), (Q_, D_), (I_,)
UP, DOWN, XWAY, YWAY, SIDE = range(5)


def here():
    dp, seq = lax.axis_index("dp"), lax.axis_index("seq")
    return dp // 2, dp % 2, seq // 2, seq % 2


def device(z, y, x, c):
    return {"dp": z * 2 + y, "seq": x * 2 + c}


def chip(z, y, x):
    return z * 4 + y * 2 + x


def near_first(z, s):
    inner = (z * (3 - z)) // 2
    found = s + inner * (1, 1, -2, 0)[s]
    return found + (z // 2) * (3 - 2 * found)


def all_peers():
    z, y, x, c = here()
    return (
        device(z + 1, y, x, c),
        device(z - 1, y, x, c),
        device(z, y, 1 - x, c),
        device(z, 1 - y, x, c),
        device(z, y, x, 1 - c),
    )


SUM_AT = (0, WIDE, WIDE + 3 * D, WIDE + 4 * D, WIDE + 8 * D, WIDE + 9 * D)
SUMS = WIDE + 9 * D + 256
HALF_AT = tuple(start // 2 for start in SUM_AT)
HALF_SUMS = HALF_AT[5]


def lanes_of(members):
    lane = lax.broadcasted_iota(jnp.int32, (1, 128), 1)
    row = jnp.zeros((1, 128), F32)
    for index, member in enumerate(members):
        row = jnp.where(lane == index, member, row)
    return row


def lane_at(row, index):
    lane = lax.broadcasted_iota(jnp.int32, row.shape, 1)
    return jnp.sum(jnp.where(lane == index, row, 0.0), 1, keepdims=True)


def column_of(row):
    size = row.shape[1]
    diagonal = lax.broadcasted_iota(jnp.int32, (size, size), 0) == lax.broadcasted_iota(
        jnp.int32, (size, size), 1
    )
    return jnp.sum(jnp.where(diagonal, row, 0.0), 1, keepdims=True)


def row_of(column):
    size = column.shape[0]
    diagonal = lax.broadcasted_iota(jnp.int32, (size, size), 0) == lax.broadcasted_iota(
        jnp.int32, (size, size), 1
    )
    return jnp.sum(jnp.where(diagonal, column, 0.0), 0, keepdims=True)


def as_row(ref):
    return ref[...].reshape(1, ref.shape[0])


def total_sum(array):
    return jnp.sum(jnp.sum(array, 1, keepdims=True), 0, keepdims=True)


def gelu_pair(hidden):
    normal_cdf = 0.5 * (1.0 + lax.erf(hidden * 0.7071067811865476))
    return (
        hidden * normal_cdf,
        normal_cdf + hidden * jnp.exp(-0.5 * hidden * hidden) * 0.3989422804014327,
    )


def dot_nn(left, right):
    return jnp.dot(left, right, preferred_element_type=F32)


def dot_nt(left, right):
    return lax.dot_general(left, right, (((1,), (1,)), ((), ())), preferred_element_type=F32)


def dot_tn(left, right):
    return lax.dot_general(left, right, (((0,), (0,)), ((), ())), preferred_element_type=F32)


def at(index, size):
    if isinstance(index, int):
        return pl.ds(index * size, size)
    return pl.ds(pl.multiple_of(index * size, size), size)


def each(count, body):
    def step(index, carry):
        body(index)
        return carry

    lax.fori_loop(0, count, step, 0)


def each_unrolled(count, body):
    for index in range(count):
        body(index)


ROWS = 128
TILE = 256
HALF = 320
TABLE_TILES = TABLE_END // TILE


def head_lanes(first):
    lane = lax.broadcasted_iota(jnp.int32, (1, 128), 1)
    return (lane < HEAD_DIM) if first else (lane >= HEAD_DIM)


def layer_norm(value, gain, shift):
    centred = value - jnp.sum(value, 1, keepdims=True) / D
    inverse = lax.rsqrt(jnp.sum(centred * centred, 1, keepdims=True) / D + EPSILON)
    normed = centred * inverse
    return normed * gain + shift, normed, inverse


def layer_norm_back(grad, normed, inverse, gain):
    scaled = grad * gain
    return inverse * (
        scaled - jnp.sum(scaled, 1, keepdims=True) / D - normed * (jnp.sum(scaled * normed, 1, keepdims=True) / D)
    )


def put_lane(ref, rows, index, value):
    lane = lax.broadcasted_iota(jnp.int32, (1, 128), 1)
    ref[rows, :] = jnp.where(lane == index, value, ref[rows, :])


def set_bias(bias, cols, keys, last):
    same = cols[0:last, 4:5] == keys[1:2, 0:last]
    bias[...] = jnp.where(same & (keys[0:1, 0:last] > 0), 0.0, -1e30)


CHOOSE, EMBED, NORM_A, PROJECT, TURN_X, ATTEND, OUT, NORM_B, FEED_IN, TURN_A, FEED_OUT, REST = range(12)
FRONT = (
    35, 99, 33, 67, 65, 32, 4, 64, 3, 36, 1, 160, 69, 101, 40, 37, 1000, 163, 100, 0,
    129, 70, 1001, 68, 164, 128, 103, 72, 46, 44, 73, 161, 97, 96, 38, 5, 45, 74, 39, 77,
    102, 6, 172, 71, 7, 105, 82, 8, 41, 11, 10, 107, 12, 42, 14, 43, 79, 75, 9, 47,
    166, 168, 165, 104, 80, 78, 133, 81, 76, 18, 49, 111, 51, 48, 170, 50, 134, 167, 83, 132,
    108, 106, 13, 16, 1016, 17, 1017, 1018, 15, 1019, 1020, 135, 110, 19, 1021, 1032, 144, 176, 169, 142,
    1048, 1049, 171, 115, 1050, 1051, 173, 137, 1052, 131, 1053, 1054, 1055, 109, 1056, 1064, 174, 1080, 177, 140,
    1081, 138, 112, 178, 1082, 1083, 139, 114, 1084, 175, 179, 1085, 145, 143, 1096, 113, 146, 1097, 1098, 136,
    1112, 1128, 1129, 147, 1130, 1131, 1132, 1133, 1134, 1135, 141, 1136, 1137, 1138, 1139, 1160, 1161, 1162, 1176,
)


def front_hooks():
    hooks, before = {}, []
    for task in FRONT:
        if task < 1000:
            before.append(task)
        else:
            hooks[((task - 1000) // 16, (task - 1000) % 16)] = before
            before = []
    return hooks


def front_kernel(*refs):
    raw, (long_len, short_len) = refs[0:13], refs[13:15]
    count_out, gains_out, side, cols, keys, squares = refs[15:21]
    x_t, mix_out, a_out, act_out, y_out, slope_out, qkv_out, na_out = refs[21:29]
    nb_outs, nc_outs, weight_outs = refs[29:31], refs[31:33], refs[33:38]
    wide, qkv_w, out_w, in_w, down_w = weights = refs[38:43]
    value, na, low_a, low_y, mix, qkv, act, slope, pick, pick_two, bias, turned = refs[43:55]
    nb, nc = refs[55:57], (mix, low_y)
    held, wide_shard, merge, pieces, land = refs[57:70], refs[70], refs[71:76], refs[76], refs[77]
    raw_sem, swap_send, swap_recv, token_send, token_recv, send_sem, link_recv, side_recv = refs[78:86]
    out_sem, turn_sem = refs[86:88]
    z, y, x, c = here()
    peers = all_peers()
    me = chip(z, y, x)
    seq = x * 2 + c
    alone = seq // 3
    tokens = value.shape[0]
    last = tokens - SPAN
    hooks = front_hooks()

    barrier = pltpu.get_barrier_semaphore()
    cross = device(z, y, 1 - x, 1 - c)
    column = [device((z + 1 + i) % 4, y, x, c) for i in range(3)]
    for peer in [peers[XWAY], peers[YWAY], peers[SIDE], cross] + column:
        pl.semaphore_signal(barrier, inc=1, device_id=peer, device_id_type=MESH)
    raws = [pltpu.make_async_copy(raw[i], held[i], raw_sem.at[i]) for i in range(13)]
    for member in raws:
        member.start()
    for member in raws:
        member.wait()
    long_ids, long_targets, long_mask, short_ids, short_targets, short_mask, tall, place, qkv_s, out_s, in_s, down_s, norms = held

    pieces[...] = jnp.zeros(pieces.shape, jnp.int32)
    land[4] = jnp.zeros((8, SPAN), jnp.int32)
    lane = lax.broadcasted_iota(jnp.int32, (1, SPAN), 1)
    count = jnp.zeros((1, SPAN), jnp.int32)
    for t in range(5):
        if t < 3:
            ids, targets, mask = long_ids[t : t + 1, :], long_targets[t : t + 1, :], long_mask[t : t + 1, :]
            keep = (lane + seq * SPAN < long_len[t]).astype(jnp.int32)
        else:
            row = (1, 0)[t - 3]
            ids, targets, mask = (member[row : row + 1, :] for member in (short_ids, short_targets, short_mask))
            keep = (lane < short_len[row]).astype(jnp.int32)
        target = pieces.at[t] if t < 4 else land.at[4]
        target[0:1, :] = ids
        target[2:3, :] = targets
        target[3:4, :] = mask * keep
        target[5:6, :] = keep
        count = count + mask * keep
    count = jnp.sum(count.astype(F32), 1, keepdims=True)
    high = jnp.floor(count * (1.0 / 256.0))

    wide_shard[:, 0:4096] = tall[:, 0:4096]
    edge = jnp.zeros((24, 128), F32)
    tile_lane = lax.broadcasted_iota(jnp.int32, (24, 128), 1)
    tall_edge = tall[:, 4096:VOCAB]
    members = [lane_at(tall_edge, i) for i in range(VOCAB - 4096)]
    members += [column_of(norms[i : i + 1, :]) for i in range(6)]
    members += [high, count - high * 256.0]
    for i, member in enumerate(members):
        edge = jnp.where(tile_lane == i, member, edge)
    wide_shard[:, 4096:4224] = edge
    wide_shard[:, 4224:PLACE_AT] = jnp.zeros((24, PLACE_AT - 4224), F32)
    wide_shard[:, PLACE_AT:] = place[...]
    shards = (wide_shard, qkv_s, out_s, in_s, down_s)
    for m, (size, whole) in enumerate(SHAPES):
        half = whole // 2
        merge[m][pl.ds(pl.multiple_of(c * size, 8), size), :] = shards[m][:, pl.ds(pl.multiple_of(c * half, 128), half)]

    pl.semaphore_wait(barrier, 7)
    swaps = []
    for m in (E_, Q_, I_, D_, O_):
        size, half = SHAPES[m][0], SHAPES[m][1] // 2
        swaps.append(
            pltpu.make_async_remote_copy(
                src_ref=shards[m].at[:, pl.ds(pl.multiple_of((1 - c) * half, 128), half)],
                dst_ref=merge[m].at[pl.ds(pl.multiple_of(c * size, 8), size), :],
                send_sem=swap_send.at[m],
                recv_sem=swap_recv.at[m],
                device_id=peers[SIDE],
                device_id_type=MESH,
            )
        )
        swaps[-1].start()
    token_copies = []
    for i, (to_x, to_c) in enumerate(((x, 1 - c), (1 - x, c), (1 - x, 1 - c))):
        token_copies.append(
            pltpu.make_async_remote_copy(
                src_ref=pieces.at[to_x * 2 + to_c],
                dst_ref=land.at[seq],
                send_sem=token_send.at[i],
                recv_sem=token_recv.at[i],
                device_id=device(z, y, to_x, to_c),
                device_id_type=MESH,
            )
        )
        token_copies[-1].start()
    land[seq] = pieces[seq]

    def part(piece, k, half):
        m, skip, wide_part = PIECES[piece]
        size = 2 * SHAPES[m][0]
        start = pl.multiple_of(half * (SHAPES[m][1] // 2) + skip, 128)
        return weights[m].at[pl.ds(pl.multiple_of(k * size, size), size), pl.ds(start, wide_part)]

    FIRST_WAY, SECOND_WAY, SIDE_WAY, UP_WAY, DOWN_WAY = range(5)

    def copy_of(piece, k, way):
        ways = (XWAY, YWAY) if GATHER_WAY[piece] == 0 else (YWAY, XWAY)
        return pltpu.make_async_remote_copy(
            src_ref=part(piece, k, c),
            dst_ref=part(piece, k, c),
            send_sem=send_sem.at[piece, k, way],
            recv_sem=(side_recv if way == SIDE_WAY else link_recv).at[piece, k],
            device_id=peers[(ways + (SIDE, UP, DOWN))[way]],
            device_id_type=MESH,
        )

    def block_of(number):
        piece, task = number // 32, number % 32
        way = GATHER_WAY[piece]
        up, down = (UP_WAY, z < 3), (DOWN_WAY, z > 0)
        first, second, across = (FIRST_WAY, None), (SECOND_WAY, None), (SIDE_WAY, None)

        def of(last, earlier, t):
            to_y, to_x = (last, earlier) if way == 0 else (earlier, last)
            return chip(t, 1 - y if to_y else y, 1 - x if to_x else x)

        def onward(t):
            return (UP_WAY, (t < z) & (z < 3)), (DOWN_WAY, (t > z) & (z > 0))

        if task < 5:
            return piece, me, (up, down, None, first, second)[task : task + 1], False
        if way < 2:
            if task < 8:
                t = near_first(z, task - 4)
                return piece, of(0, 0, t), onward(t) + (first, second, across), True
            if task < 12:
                return piece, of(0, 1, near_first(z, task - 8)), (second, across), True
            return piece, of(1, (task - 12) % 2, near_first(z, (task - 12) // 2)), (across,), True
        if task == 5:
            return piece, of(0, 1, z), (second, up, down, across), True
        if task < 8:
            return piece, of(1, task - 6, z), (up, down, across), True
        t, place_of = near_first(z, 1 + (task - 8) // 4), (task - 8) % 4
        return piece, of(place_of // 2, place_of % 2, t), onward(t) + (across,), True

    def for_each_way(number, act):
        piece, k, ways, _ = block_of(number)
        for way, only in ways:
            if only is None:
                act(copy_of(piece, k, way))
            else:

                @pl.when(only)
                def _(way=way):
                    act(copy_of(piece, k, way))

    def transfer(number):
        piece, k, _, waits = block_of(number)
        if waits:
            copy_of(piece, k, FIRST_WAY).wait_recv()
        for_each_way(number, lambda copy: copy.start())

    def before(step, index, base=0):
        for (name, part_index), tasks in hooks.items():
            part_index = part_index - base
            if name != step or not tasks or (step == EMBED and not 0 <= part_index < 3):
                continue
            if index is None or isinstance(index, int):
                if part_index == (index or 0):
                    for number in tasks:
                        transfer(number)
            else:

                @pl.when(index == part_index)
                def _(tasks=tasks):
                    for number in tasks:
                        transfer(number)

    def need(*wanted):
        for piece in wanted:
            for k in range(16):
                pltpu.make_async_remote_copy(
                    src_ref=part(piece, k, 1 - c),
                    dst_ref=part(piece, k, 1 - c),
                    send_sem=send_sem.at[piece, k, SIDE_WAY],
                    recv_sem=side_recv.at[piece, k],
                    device_id=peers[SIDE],
                    device_id_type=MESH,
                ).wait_recv()

    for number, m in enumerate((E_, Q_, I_, D_, O_)):
        swaps[number].wait_recv()
        size, half = SHAPES[m][0], SHAPES[m][1] // 2
        rows = pl.ds(pl.multiple_of(me * 2 * size, 2 * size), 2 * size)
        weights[m][rows, pl.ds(pl.multiple_of(c * half, 128), half)] = merge[m][...].astype(BF16)
        for piece in range(6):
            if PIECES[piece][0] == m:
                copy_of(piece, me, SIDE_WAY).start()
    opening = hooks[(CHOOSE, 0)]
    while opening and opening[0] % 32 < 5:
        transfer(opening.pop(0))
    for copy in token_copies:
        copy.wait_recv()
    side[...] = jnp.zeros(side.shape, F32)
    keys[...] = jnp.zeros(keys.shape, jnp.int32)
    zeros = jnp.zeros((1, SPAN), F32)
    for b in range(5):
        tile = land[b]
        shift = b * SPAN * (1 - alone) if b < 4 else 0
        row = b * alone if b < 4 else 4
        spot = (lane + shift + PLACE_AT).astype(F32)
        row_lane = (lane * 0 + row).astype(F32)
        ids, targets, weight = (tile[i : i + 1].astype(F32) for i in (0, 2, 3))
        stacked = jnp.concatenate((ids, spot, targets, weight, row_lane, tile[5:6].astype(F32), zeros, zeros), 0)
        stacked = jnp.concatenate((stacked, jnp.zeros((120, SPAN), F32)), 0)
        cols[b * SPAN : (b + 1) * SPAN, :] = stacked.T.astype(jnp.int32)
        keys[0:1, b * SPAN : (b + 1) * SPAN] = tile[5:6]
        keys[1:2, b * SPAN : (b + 1) * SPAN] = lane * 0 + row
        keys[2:4, b * SPAN : (b + 1) * SPAN] = tile[2:4]
    set_bias(bias, cols, keys, last)
    found = [total_sum(member[...] * member[...]) for member in (tall, place, qkv_s, out_s, in_s, down_s)]
    norm_squares = jnp.sum(norms[...] * norms[...], 1, keepdims=True)
    squares[...] = lanes_of(found + [norm_squares[i : i + 1] for i in range(6)])

    turns, outs, out_count = {}, {}, [0]

    def turn_out(source, target, slot):
        if slot in turns:
            turns[slot].wait()

        def some(index):
            turned[slot, :, at(index, ROWS)] = source[at(index, ROWS), :].T

        each_unrolled(tokens // ROWS, some)
        turns[slot] = pltpu.make_async_copy(turned.at[slot], target, turn_sem.at[slot])
        turns[slot].start()

    def put_out(name, source, target):
        outs[name] = pltpu.make_async_copy(source, target, out_sem.at[out_count[0]])
        out_count[0] += 1
        outs[name].start()

    picks = (pick, pick_two)
    halves = [pl.ds(half * HALF, HALF) for half in range(2)]
    for half in range(2):

        def choose(index):
            column_lane = lax.broadcasted_iota(jnp.int32, (1, TILE), 1) + index * TILE
            hit = (cols[halves[half], 0:1] == column_lane) | (cols[halves[half], 1:2] == column_lane)
            picks[half][:, at(index, TILE)] = jnp.where(hit, 1.0, 0.0).astype(BF16)

        before(CHOOSE, half)
        each_unrolled(WIDE // TILE, choose)

    before(EMBED, 0)
    hooks.pop((EMBED, 0))
    need(1, 2)
    put_out("wide", wide, weight_outs[4])
    for half in range(2):

        def embed(index):
            before(EMBED, index, half * 3)
            value[halves[half], at(index, TILE)] = dot_nt(picks[half][...], wide[at(index, TILE), :])

        each_unrolled(D // TILE, embed)

    gains = wide[:, 4096:4224].astype(F32).T
    gains_out[...] = gains[0:16]
    counts = jnp.sum(gains[11:13], 1, keepdims=True) / 24.0
    mask_count = counts[0:1] * 256.0 + counts[1:2]
    count_out[...] = mask_count
    norm_rows = [gains_out[5 + i : 6 + i, :] for i in range(6)]
    before(NORM_A, None)

    def norm_a(index):
        rows = at(index, ROWS)
        found, normed, inverse = layer_norm(value[rows, :], norm_rows[0], norm_rows[1])
        value[rows, :] = found
        low_a[rows, :] = found.astype(BF16)
        na[rows, :] = normed
        put_lane(side, rows, 12, inverse)

    each_unrolled(tokens // ROWS, norm_a)
    put_out("na", na, na_out)
    before(PROJECT, 0)
    need(0)

    def project(index):
        before(PROJECT, index)
        qkv[:, at(index, TILE)] = dot_nn(low_a[...], qkv_w[:, at(index, TILE)]).astype(BF16)

    hooks.pop((PROJECT, 0))
    each_unrolled(3 * D // TILE, project)
    put_out("qkv", qkv, qkv_out)
    put_out("qkv_w", qkv_w, weight_outs[0])
    before(TURN_X, None)
    turn_out(low_a, x_t, 0)

    def attend_pair(pair):
        before(ATTEND, pair)
        for start, size in ((0, last), (last, SPAN)):
            rows = pl.ds(start, size)
            query = qkv[rows, at(pair, 128)]
            key = qkv[rows, pl.ds(D + pair * 128, 128)]
            val = qkv[rows, pl.ds(2 * D + pair * 128, 128)]
            mask = bias[...] if start == 0 else jnp.where(keys[0:1, last:tokens] > 0, 0.0, -1e30)
            mixed = []
            for first in (True, False):
                chosen = jnp.where(head_lanes(first), query, jnp.zeros_like(query))
                scores = dot_nt(chosen, key) * 0.125 + mask
                highest = jnp.max(scores, 1, keepdims=True)
                raised = jnp.exp(scores - highest)
                summed = jnp.sum(raised, 1, keepdims=True)
                shares = (raised * (1.0 / summed)).astype(BF16)
                mixed.append(dot_nn(shares, val))
                put_lane(side, rows, 2 * pair + (0 if first else 1), highest + jnp.log(summed))
            mix[rows, at(pair, 128)] = jnp.where(head_lanes(True), mixed[0], mixed[1]).astype(BF16)

    each_unrolled(HEADS // 2, attend_pair)
    before(OUT, 0)
    hooks.pop((OUT, 0))
    need(5)

    def out_project(index):
        before(OUT, index)
        value[:, at(index, TILE)] = value[:, at(index, TILE)] + dot_nn(mix[...], out_w[:, at(index, TILE)])

    each_unrolled(D // TILE, out_project)
    put_out("out_w", out_w, weight_outs[1])
    put_out("mix", mix, mix_out)
    before(NORM_B, None)

    def norm_b(index):
        rows = at(index, ROWS)
        found, normed, inverse = layer_norm(value[rows, :], norm_rows[2], norm_rows[3])
        value[rows, :] = found
        low_y[rows, :] = found.astype(BF16)
        nb[0][rows, :], nb[1][rows, :] = split_two(normed)
        put_lane(side, rows, 13, inverse)

    each_unrolled(tokens // ROWS, norm_b)
    put_out("a", low_y, a_out)
    put_out("nb0", nb[0], nb_outs[0])
    put_out("nb1", nb[1], nb_outs[1])
    before(FEED_IN, 0)
    hooks.pop((FEED_IN, 0))
    need(3)

    def feed_in(index):
        before(FEED_IN, index)
        hidden = dot_nn(low_y[...], in_w[:, at(index, TILE)])
        active, slant = gelu_pair(hidden)
        active = active.astype(BF16)
        act[:, at(index, TILE)] = active
        slope[:, at(index, TILE)] = slant.astype(BF16)

    each_unrolled(4 * D // TILE, feed_in)
    put_out("act", act, act_out)
    put_out("slope", slope, slope_out)
    put_out("in_w", in_w, weight_outs[2])
    before(TURN_A, None)
    before(FEED_OUT, 0)
    hooks.pop((FEED_OUT, 0))
    need(4)

    def feed_out(index):
        before(FEED_OUT, index)
        value[:, at(index, TILE)] = value[:, at(index, TILE)] + dot_nn(act[...], down_w[:, at(index, TILE)])

    each_unrolled(D // TILE, feed_out)
    put_out("down_w", down_w, weight_outs[3])
    before(REST, None)
    turns[0].wait()
    outs.pop("mix").wait()
    outs.pop("a").wait()

    def norm_c(index):
        rows = at(index, ROWS)
        found, normed, inverse = layer_norm(value[rows, :], norm_rows[4], norm_rows[5])
        low_a[rows, :] = found.astype(BF16)
        nc[0][rows, :], nc[1][rows, :] = split_two(normed)
        put_lane(side, rows, 14, inverse)

    each_unrolled(tokens // ROWS, norm_c)
    put_out("y", low_a, y_out)
    put_out("nc0", nc[0], nc_outs[0])
    put_out("nc1", nc[1], nc_outs[1])
    for swap in swaps:
        swap.wait_send()
    for copy in token_copies:
        copy.wait_send()
    for piece in range(6):
        copy_of(piece, me, SIDE_WAY).wait_send()
    for number in FRONT:
        if number < 1000:
            for_each_way(number, lambda copy: copy.wait_send())
    for copy in outs.values():
        copy.wait()


def front(large, lengths):
    vmem, hbm = pl.BlockSpec(memory_space=pltpu.VMEM), pl.BlockSpec(memory_space=pl.ANY)
    smem = pl.BlockSpec(memory_space=pltpu.SMEM)
    shape, dma = jax.ShapeDtypeStruct, pltpu.SemaphoreType.DMA
    tokens = 5 * SPAN
    small = [shape((1, 1), F32), shape((16, D), F32), shape((tokens, 128), F32)]
    small += [shape((tokens, 128), jnp.int32), shape((8, tokens), jnp.int32), shape((1, 128), F32)]
    out = [shape((D, tokens), BF16)] + [shape((tokens, width), BF16) for width in (D, D, 4 * D, D, 4 * D, 3 * D)]
    out += [shape((tokens, D), F32)] + [shape((tokens, D), BF16)] * 4
    out += [shape((32 * SHAPES[m][0], SHAPES[m][1]), BF16) for m in (Q_, O_, I_, D_, E_)]
    return pl.pallas_call(
        front_kernel,
        out_shape=small + out,
        in_specs=[hbm] * 13 + [smem] * 2,
        out_specs=[vmem] * len(small) + [hbm] * len(out),
        scratch_shapes=[pltpu.VMEM((32 * size, wide), BF16) for size, wide in SHAPES]
        + [pltpu.VMEM((tokens, D), F32)] * 2
        + [pltpu.VMEM((tokens, D), BF16)] * 3
        + [
            pltpu.VMEM((tokens, 3 * D), BF16),
            pltpu.VMEM((tokens, 4 * D), BF16),
            pltpu.VMEM((tokens, 4 * D), BF16),
            pltpu.VMEM((HALF, WIDE), BF16),
            pltpu.VMEM((HALF, WIDE), BF16),
            pltpu.VMEM((tokens - SPAN, tokens - SPAN), F32),
            pltpu.VMEM((1, D, tokens), BF16),
        ]
        + [pltpu.VMEM((tokens, D), BF16)] * 2
        + [pltpu.VMEM(member.shape, member.dtype) for member in large]
        + [pltpu.VMEM(SHAPES[E_], F32)]
        + [pltpu.VMEM((2 * size, wide // 2), F32) for size, wide in SHAPES]
        + [pltpu.VMEM((4, 8, SPAN), jnp.int32), pltpu.VMEM((5, 8, SPAN), jnp.int32)]
        + [dma((13,)), dma((5,)), dma((5,)), dma((3,)), dma((3,)), dma((6, 16, 5)), dma((6, 16)), dma((6, 16))]
        + [dma((18,)), dma((1,))],
        compiler_params=pltpu.CompilerParams(
            collective_id=0, has_side_effects=True, vmem_limit_bytes=63 * 1024 * 1024
        ),
    )(*large, *lengths)


PACK = 256


def split_two(value):
    high = value.astype(BF16)
    return high, (value - high.astype(F32)).astype(BF16)


def middle_kernel(*refs):
    (wide_h, qkv_wh, out_wh, in_wh, down_h, y_h, act_h, a_h, mix_h, slope_h, qkv_h, na_h) = refs[0:12]
    nb_h, nc_h = refs[12:14], refs[14:16]
    cols, keys, side, gains, count = refs[16:21]
    loss_out, norm_out = refs[21:23]
    glog_out, y_t, a_t, mix_t, act_t, ge_t, gffn_out, gh_out, gattn_out, gqkv_out = refs[23:33]
    wide, qkv_w, out_w, in_w, plain, qkv = refs[33:39]
    nb = refs[39:41]
    slope_ring, act_ring, down_ring = refs[41:44]
    logits, glog, gh, gffn, gattn, packed, grad, turned, act_turned = refs[44:53]
    back_kv, gqkv, whole_grad, pick, pick_t, bias, side_pack, side_turned, dq, ge = refs[53:63]
    load_sem, ring_sem, out_sem = refs[63:66]
    nc = (gqkv.at[:, D : 2 * D], gqkv.at[:, 2 * D : 3 * D])
    gatt = packed
    tokens = cols.shape[0]
    names = ("wide", "y", "nc0", "nc1", "in_w", "nb0", "nb1", "out_w", "qkv", "qkv_w")
    sources = (wide_h, y_h, nc_h[0], nc_h[1], in_wh, nb_h[0], nb_h[1], out_wh, qkv_h, qkv_wh)
    targets = (wide, plain, nc[0], nc[1], in_w, nb[0], nb[1], out_w, qkv, qkv_w)

    def na_copy(i):
        return pltpu.make_async_copy(
            na_h.at[:, at(i, TILE)], logits.at[pl.ds(i * tokens, tokens), :], load_sem.at[10 + i]
        )

    def tile_of(index):
        return pl.ds(index * PACK, PACK)

    loads = {name: pltpu.make_async_copy(sources[i], targets[i], load_sem.at[i]) for i, name in enumerate(names)}
    for name in ("y", "wide"):
        loads[name].start()

    weight_row = keys[3:4, :].astype(F32)
    weight_col = cols[:, 3:4].astype(F32)
    earlier = lax.broadcasted_iota(jnp.int32, (tokens, tokens), 0) < lax.broadcasted_iota(jnp.int32, (tokens, tokens), 1)
    later = lax.broadcasted_iota(jnp.int32, (tokens, tokens), 0) > lax.broadcasted_iota(jnp.int32, (tokens, tokens), 1)
    rank_row = dot_nn(
        jnp.broadcast_to(weight_row, (16, tokens)).astype(BF16), jnp.where(earlier, 1.0, 0.0).astype(BF16)
    )[0:1]
    rank_col = dot_nn(
        jnp.where(later, 1.0, 0.0).astype(BF16), jnp.broadcast_to(weight_col, (tokens, 128)).astype(BF16)
    )[:, 0:1]
    rank_row = jnp.where(weight_row > 0, rank_row, -1.0)
    rank_col = jnp.where(weight_col > 0, rank_col, -1.0)
    blocks = (jnp.sum(weight_row).astype(jnp.int32) + (PACK - 1)) // PACK
    blocks = jnp.maximum(blocks, 1)
    inverse_count = 1.0 / count[...]
    norm_rows = [gains[5 + i : 6 + i, :] for i in range(6)]
    loss_out[...] = jnp.zeros((1, 1), F32)
    norm_out[...] = jnp.zeros(norm_out.shape, F32)
    back_kv[...] = jnp.zeros(back_kv.shape, F32)
    whole_grad[...] = jnp.zeros(whole_grad.shape, F32)
    gqkv[:, 0:D] = jnp.zeros((tokens, D), BF16)
    side_first = side[...].astype(BF16)
    rest = side[...] - side_first.astype(F32)
    side_second = rest.astype(BF16)
    side_third = (rest - side_second.astype(F32)).astype(BF16)
    waited = set()

    def load_plain(source):
        return pltpu.make_async_copy(source, plain, load_sem.at[1])

    def ring(kind, source, target):
        def copy(j):
            piece = source.at[at(j, TILE), :] if kind == 2 else source.at[:, at(j, TILE)]
            return pltpu.make_async_copy(piece, target.at[j % 2], ring_sem.at[kind * 2 + j % 2])

        return copy

    rings = [ring(0, slope_h, slope_ring), ring(1, act_h, act_ring), ring(2, down_h, down_ring)]
    outs = [
        (glog, glog_out, 0),
        (turned.at[0], y_t, 1),
        (turned.at[1], a_t, 1),
        (turned.at[2], mix_t, 1),
        (act_turned, act_t, 1),
        (gffn, gffn_out, 0),
        (gh, gh_out, 0),
        (gattn, gattn_out, 0),
    ]

    def out_copy(i, block):
        source, target, axis = outs[i]
        place = at(block, PACK)
        return pltpu.make_async_copy(
            source, target.at[place, :] if axis == 0 else target.at[:, place], out_sem.at[i]
        )

    def wait_load(name):
        loads[name].wait()

    wait_load("wide")
    for name in names[2:]:
        loads[name].start()

    def block_step(block, carry):
        slot_col = lax.broadcasted_iota(jnp.int32, (PACK, 1), 0).astype(F32) + (block * PACK).astype(F32)
        slot_row = lax.broadcasted_iota(jnp.int32, (1, PACK), 1).astype(F32) + (block * PACK).astype(F32)
        hit = jnp.where(rank_row == slot_col, 1.0, 0.0)
        pick[...] = hit.astype(BF16)
        hit_t = jnp.where(rank_col == slot_row, 1.0, 0.0)
        pick_t[...] = hit_t.astype(BF16)
        target = jnp.sum(hit * keys[2:3, :].astype(F32), 1, keepdims=True)
        weight = jnp.sum(hit, 1, keepdims=True)
        row_col = cols[:, 4:5].astype(F32)
        row_of_token = jnp.sum(hit_t * row_col, 0, keepdims=True)
        bias[...] = jnp.where((row_of_token == row_col) & (cols[:, 5:6] > 0), 0.0, -1e30)
        side_pack[...] = (
            dot_nn(pick[...], side_first) + dot_nn(pick[...], side_second) + dot_nn(pick[...], side_third)
        )
        side_turned[...] = side_pack[...].T
        for kind in range(3):
            for j in range(2):
                rings[kind](j).start()
        load_plain(y_h).wait()
        packed[...] = dot_nn(pick[...], plain[...]).astype(BF16)
        load_plain(a_h).start()
        turned[0] = packed[...].T
        out_copy(1, block).start()

        def lanes(index):
            return (lax.broadcasted_iota(jnp.int32, (1, TILE), 1) + index * TILE).astype(F32)

        highest = jnp.full((PACK, 128), -1e30, F32)
        for index in range(TABLE_TILES):
            found = dot_nn(packed[...], wide[:, at(index, TILE)])
            if index == TABLE_TILES - 1:
                found = jnp.where(lanes(index) < VOCAB, found, -1e30)
            logits[tile_of(index), :] = found
            highest = jnp.maximum(highest, jnp.maximum(found[:, 0:128], found[:, 128:256]))
        highest = jnp.max(highest, 1, keepdims=True)
        summed, picked = jnp.zeros((PACK, 128), F32), jnp.zeros((PACK, 128), F32)
        for index in range(TABLE_TILES):
            found = logits[tile_of(index), :]
            raised = jnp.exp(found - highest)
            logits[tile_of(index), :] = raised
            own = jnp.where(lanes(index) == target, found, 0.0)
            summed = summed + raised[:, 0:128] + raised[:, 128:256]
            picked = picked + own[:, 0:128] + own[:, 128:256]
        summed = jnp.sum(summed, 1, keepdims=True)
        picked = jnp.sum(picked, 1, keepdims=True)
        loss_out[...] = loss_out[...] + jnp.sum(weight * (highest + jnp.log(summed) - picked), 0, keepdims=True)
        scale = weight * inverse_count
        share = scale / summed
        for index in range(TABLE_TILES):
            found = logits[tile_of(index), :] * share - jnp.where(lanes(index) == target, scale, 0.0)
            glog[:, at(index, TILE)] = found.astype(BF16)
        out_copy(0, block).start()
        for index in range(D // TILE):
            grad[:, at(index, TILE)] = dot_nt(glog[...], wide[at(index, TILE), 0:TABLE_END])

        @pl.when(block == 0)
        def _():
            for name in names[2:4]:
                wait_load(name)

        normed = dot_nn(pick[...], nc[0][...]) + dot_nn(pick[...], nc[1][...])
        found = grad[...]
        back = layer_norm_back(found, normed, lane_at(side_pack[...], 14), norm_rows[4])
        norm_out[4:5, :] = norm_out[4:5, :] + jnp.sum(found * normed, 0, keepdims=True)
        norm_out[5:6, :] = norm_out[5:6, :] + jnp.sum(found, 0, keepdims=True)
        grad[...] = back
        gffn[...] = back.astype(BF16)
        out_copy(5, block).start()

        load_plain(a_h).wait()
        turned[1] = dot_nn(pick[...], plain[...]).astype(BF16).T
        out_copy(2, block).start()
        load_plain(mix_h).start()
        for index in range(4 * D // TILE):
            for kind in range(3):
                rings[kind](index).wait()
            slant = dot_nn(pick[...], slope_ring[index % 2])
            found = dot_nt(gffn[...], down_ring[index % 2]) * slant
            gh[:, at(index, TILE)] = found.astype(BF16)
            act_turned[at(index, TILE), :] = dot_nn(pick[...], act_ring[index % 2]).astype(BF16).T
            if index + 2 < 4 * D // TILE:
                for kind in range(3):
                    rings[kind](index + 2).start()
        out_copy(6, block).start()
        out_copy(4, block).start()
        load_plain(mix_h).wait()
        turned[2] = dot_nn(pick[...], plain[...]).astype(BF16).T
        out_copy(3, block).start()
        load_plain(y_h).start()

        @pl.when(block == 0)
        def _():
            for name in names[4:8]:
                wait_load(name)

        for index in range(D // TILE):
            grad[:, at(index, TILE)] = grad[:, at(index, TILE)] + dot_nt(gh[...], in_w[at(index, TILE), :])
        normed = dot_nn(pick[...], nb[0][...]) + dot_nn(pick[...], nb[1][...])
        found = grad[...]
        back = layer_norm_back(found, normed, lane_at(side_pack[...], 13), norm_rows[2])
        norm_out[2:3, :] = norm_out[2:3, :] + jnp.sum(found * normed, 0, keepdims=True)
        norm_out[3:4, :] = norm_out[3:4, :] + jnp.sum(found, 0, keepdims=True)
        gattn[...] = back.astype(BF16)
        out_copy(7, block).start()
        high, low = split_two(back)
        whole_grad[...] = whole_grad[...] + dot_nn(pick_t[...], high) + dot_nn(pick_t[...], low)
        for index in range(D // TILE):
            gatt[:, at(index, TILE)] = dot_nt(gattn[...], out_w[at(index, TILE), :]).astype(BF16)

        @pl.when(block == 0)
        def _():
            wait_load("qkv")

        def attend_pair_back(pair):
            spots = [pl.ds(i * D + pair * 128, 128) for i in range(3)]
            query = dot_nn(pick[...], qkv[:, spots[0]]).astype(BF16)
            key, val = qkv[:, spots[1]], qkv[:, spots[2]]
            given = gatt[:, at(pair, 128)]
            key_t = key.T
            found = []
            for first in (True, False):
                lanes_here = head_lanes(first)
                chosen = jnp.where(lanes_here, query, jnp.zeros_like(query))
                mine = jnp.where(lanes_here, given, jnp.zeros_like(given))
                total = side_turned[pl.ds(2 * pair + (0 if first else 1), 1), :]
                shares = jnp.exp(dot_nt(key, chosen) * 0.125 + bias[...] - total)
                grad_share = dot_nt(val, mine)
                middle = jnp.sum(shares * grad_share, 0, keepdims=True)
                grad_score = (shares * (grad_share - middle)).astype(BF16)
                found.append(
                    (
                        dot_nn(key_t, grad_score) * 0.125,
                        dot_nn(grad_score, query) * 0.125,
                        dot_nn(shares.astype(BF16), given),
                    )
                )
            lanes_here = head_lanes(True)
            both = jnp.concatenate((found[0][0][0:HEAD_DIM], found[1][0][HEAD_DIM:]), 0)
            dq[at(pair, 128), :] = both.astype(BF16)
            for i in (1, 2):
                spot = pl.ds((i - 1) * D + pair * 128, 128)
                back_kv[:, spot] = back_kv[:, spot] + jnp.where(lanes_here, found[0][i], found[1][i])

        each_unrolled(HEADS // 2, attend_pair_back)
        gqkv[:, 0:D] = (gqkv[:, 0:D].astype(F32) + dot_nt(pick_t[...], dq[...])).astype(BF16)
        for i in range(len(outs)):
            out_copy(i, block).wait()
        return carry

    lax.fori_loop(0, blocks, block_step, 0)
    load_plain(y_h).wait()
    for i in range(D // TILE):
        na_copy(i).start()
    gqkv[:, D:] = back_kv[...].astype(BF16)
    copy_qkv = pltpu.make_async_copy(gqkv, gqkv_out, out_sem.at[8])
    copy_qkv.start()
    for ref in (glog, gffn, gh, gattn):
        ref[...] = jnp.zeros(ref.shape, BF16)
    for block in range(1, 3):

        @pl.when(blocks <= block)
        def _():
            for i in range(len(outs)):
                out_copy(i, block).start()

    wait_load("qkv_w")
    for index in range(D // TILE):
        whole_grad[:, at(index, TILE)] = whole_grad[:, at(index, TILE)] + dot_nt(gqkv[...], qkv_w[at(index, TILE), :])
    for i in range(D // TILE):
        na_copy(i).wait()
    zero = jnp.zeros((1, D), F32)

    def norm_a_back(index, carry):
        gain, shift = carry
        rows = at(index, ROWS)
        inverse = lane_at(side[rows, :], 12)
        found = whole_grad[rows, :]
        normed = jnp.concatenate(
            [logits[pl.ds(i * tokens + index * ROWS, ROWS), :] for i in range(D // TILE)], 1
        )
        ge[:, rows] = layer_norm_back(found, normed, inverse, norm_rows[0]).astype(BF16).T
        return gain + jnp.sum(found * normed, 0, keepdims=True), shift + jnp.sum(found, 0, keepdims=True)

    gain, shift = zero, zero
    for index in range(tokens // ROWS):
        gain, shift = norm_a_back(index, (gain, shift))
    norm_out[0:1, :] = gain
    norm_out[1:2, :] = shift
    copy_ge = pltpu.make_async_copy(ge, ge_t, out_sem.at[9])
    copy_ge.start()
    for block in range(1, 3):

        @pl.when(blocks <= block)
        def _():
            for i in range(len(outs)):
                out_copy(i, block).wait()

    copy_qkv.wait()
    copy_ge.wait()


def middle(large, small):
    tokens = 5 * SPAN
    slots = 3 * PACK
    vmem, hbm = pl.BlockSpec(memory_space=pltpu.VMEM), pl.BlockSpec(memory_space=pl.ANY)
    shape, dma = jax.ShapeDtypeStruct, pltpu.SemaphoreType.DMA
    out = [shape((slots, TABLE_END), BF16)] + [shape((D, slots), BF16)] * 3 + [shape((4 * D, slots), BF16)]
    out += [shape((D, tokens), BF16), shape((slots, D), BF16), shape((slots, 4 * D), BF16), shape((slots, D), BF16)]
    out += [shape((tokens, 3 * D), BF16)]

    def rows(count, width, kind=BF16):
        return pltpu.VMEM((count, width), kind)

    scratch = [rows(D, WIDE), rows(D, 3 * D), rows(D, D), rows(D, 4 * D), rows(tokens, D), rows(tokens, 3 * D)]
    scratch += [rows(tokens, D)] * 2
    scratch += [pltpu.VMEM((2, tokens, TILE), BF16)] * 2 + [pltpu.VMEM((2, TILE, D), BF16)]
    scratch += [rows(PACK * TABLE_TILES, TILE, F32), rows(PACK, TABLE_END), rows(PACK, 4 * D)] + [rows(PACK, D)] * 3
    scratch += [rows(PACK, D, F32), pltpu.VMEM((3, D, PACK), BF16), rows(4 * D, PACK)]
    scratch += [rows(tokens, 2 * D, F32), rows(tokens, 3 * D), rows(tokens, D, F32), rows(PACK, tokens)]
    scratch += [rows(tokens, PACK), rows(tokens, PACK, F32), rows(PACK, 128, F32), rows(128, PACK, F32)]
    scratch += [rows(D, PACK), rows(D, tokens)]
    scratch += [dma((13,)), dma((6,)), dma((10,))]
    return pl.pallas_call(
        middle_kernel,
        out_shape=[shape((1, 1), F32), shape((6, D), F32)] + out,
        in_specs=[hbm] * 16 + [vmem] * 5,
        out_specs=[vmem] * 2 + [hbm] * len(out),
        scratch_shapes=scratch,
        compiler_params=pltpu.CompilerParams(vmem_limit_bytes=63 * 1024 * 1024),
    )(*large, *small)


LEFT = 768
PIECES = ((Q_, 0, 1152), (E_, 0, 1280), (E_, 1280, 1152), (I_, 0, 1536), (D_, 0, 384), (O_, 0, 384))
SUM_WAY = (0, 1, 0, 3, 1, 0)
GATHER_WAY = (0, 1, 0, 2, 1, 0)
TASKS = (
    160, 128, 161, 129, 96, 1, 168, 136, 164, 165, 0, 130, 97, 162, 169, 141, 99, 137,
    166, 133, 4, 6, 2, 8, 7, 98, 138, 9, 173, 132, 103, 32, 142, 174, 3, 134,
    102, 135, 131, 64, 12, 140, 10, 100, 65, 101, 72, 104, 33, 34, 167, 105, 70, 109,
    40, 71, 13, 73, 11, 143, 41, 139, 14, 77, 172, 108, 45, 171, 107, 68, 38, 111,
    144, 69, 36, 175, 76, 37, 46, 5, 44, 66, 78, 176, 15, 39, 75, 112, 43, 42,
    16, 110, 35, 79, 47, 17, 106, 163, 48, 145, 170, 74, 67, 80, 49, 113, 177, 81,
)


def reduce_kernel(*refs):
    given, (cols, norm_sums, loss, squares) = refs[0:11], refs[11:15]
    y_t, ge_t, glog, x_t, gqkv, mix_t, gattn, a_t, gh, act_t, gffn = given
    lane_olds, side_olds, moment = refs[15:21], refs[21:27], refs[27]
    outs, sums_out, totals_out = refs[28:33], refs[33], refs[34]
    own, side, first, second, column, fin = (refs[35 + 6 * i : 41 + 6 * i] for i in range(6))
    left, (glog_v, gqkv_v, gattn_v, gh_v, gffn_v), stage, tails, norm_t = refs[71:78], refs[78:83], refs[83], refs[84], refs[85]
    lane_plane, lane_z, lane_halves = refs[86:89]
    scalar_sums, total_sums = refs[89:91], refs[91:93]
    load_sem, ring_sem, tail_sem, side_recv, first_send, first_recv, second_send, second_recv = refs[93:101]
    z_send, z_recv, swap_send, swap_recv = refs[101:105]
    lane_send, lane_recv, scalar_send, scalar_recv, total_send, total_recv = refs[105:111]
    z, y, x, c = here()
    peers = all_peers()
    me = chip(z, y, x)

    barrier = pltpu.get_barrier_semaphore()
    spot = y * 2 + x
    column_peers = [device((z + 1 + i) % 4, y, x, c) for i in range(3)]
    plane = [(y, 1 - x), (1 - y, x), (1 - y, 1 - x)]
    plane_peers = [device(z, to_y, to_x, c) for to_y, to_x in plane]
    greeted = column_peers + plane_peers + [device(z, to_y, to_x, 1 - c) for to_y, to_x in [(y, x)] + plane]
    for peer in greeted:
        pl.semaphore_signal(barrier, inc=1, device_id=peer, device_id_type=MESH)

    tokens = cols.shape[0]

    def act_part(group):
        return act_t.at[pl.ds(LEFT * group, LEFT), 0:tokens]

    operands = (
        ((x_t, left[1]), (gqkv, gqkv_v)),
        ((y_t.at[:, 0:tokens], left[2]), (ge_t, left[3]), (glog.at[0:tokens, :], glog_v)),
        (),
        ((a_t.at[:, 0:tokens], left[0]), (gh.at[0:tokens, :], gh_v)),
        ((gffn.at[0:tokens, :], gffn_v), (act_part(0), left[5]), (act_part(1), left[6])),
        ((mix_t.at[:, 0:tokens], left[4]), (gattn.at[0:tokens, :], gattn_v)),
    )
    loads = {}
    waited = set()
    for task in TASKS:
        piece = task // 32 if task // 32 != 2 else 1
        if piece not in loads:
            loads[piece] = []
            for source, target in operands[piece]:
                number = sum(len(member) for member in loads.values())
                loads[piece].append(pltpu.make_async_copy(source, target, load_sem.at[number]))
                loads[piece][-1].start()

    def loaded(piece):
        piece = 1 if piece == 2 else piece
        if piece not in waited:
            waited.add(piece)
            for member in loads[piece]:
                member.wait()

    norm_t[...] = jnp.zeros(norm_t.shape, F32)
    norm_t[5:11, :] = norm_sums[...]
    pl.semaphore_wait(barrier, 10)

    def size_of(piece):
        return 2 * SHAPES[PIECES[piece][0]][0]

    def slot(ref, piece, index):
        size = size_of(piece)
        return ref[piece].at[pl.ds(pl.multiple_of(index * size, size), size), :]

    def half_of(piece):
        return SHAPES[PIECES[piece][0]][1] // 2

    def chosen(start):
        lane = lax.broadcasted_iota(jnp.int32, (1, TILE), 1) + start
        hit = (cols[:, 0:1] == lane) | (cols[:, 1:2] == lane)
        return jnp.where(hit, 1.0, 0.0).astype(BF16)

    def ring_copy(piece, rows, lanes, number, index):
        place = number % 3
        return pltpu.make_async_remote_copy(
            src_ref=stage.at[place],
            dst_ref=side[piece].at[rows, lanes],
            send_sem=ring_sem.at[place],
            recv_sem=side_recv.at[piece, index],
            device_id=peers[SIDE],
            device_id_type=MESH,
        )

    def tail_copy(piece, rows, lanes, number, index):
        return pltpu.make_async_remote_copy(
            src_ref=tails.at[number],
            dst_ref=side[piece].at[rows, lanes],
            send_sem=tail_sem.at[number],
            recv_sem=side_recv.at[piece, index],
            device_id=peers[SIDE],
            device_id_type=MESH,
        )

    whole = pl.ds(0, LEFT)
    ring_count, tail_count = [0], [0]

    def give(piece, rows, lanes, number, index):
        def before():
            if number >= 3:
                ring_copy(piece, rows, lanes, number, index).wait_send()

        def write(value):
            stage[number % 3] = value.astype(BF16)

        return before, write, lambda: ring_copy(piece, rows, lanes, number, index).start()

    def keep(piece, rows, lanes):
        def write(value):
            own[piece][rows, lanes] = value.astype(BF16)

        return lambda: None, write, lambda: None

    def plain(piece, mine, source, right, group):
        wide = PIECES[piece][2]
        half = c if mine else 1 - c
        rows = pl.ds(LEFT * group, LEFT)
        base = ring_count[0]

        def step(j):
            lanes = at(j, TILE)
            before, write, after = keep(piece, rows, lanes) if mine else give(
                piece, rows, lanes, base + j, group * (wide // TILE) + j
            )
            before()
            write(dot_nn(source[...], right[:, pl.ds(pl.multiple_of(half * wide + j * TILE, 128), TILE)]))
            after()

        each_unrolled(wide // TILE, step)
        if not mine:
            ring_count[0] += wide // TILE
        if wide % TILE:
            start = wide - 128
            value = dot_nn(source[...], right[:, pl.ds(pl.multiple_of(half * wide + start, 128), 128)])
            if mine:
                own[piece][rows, start:wide] = value.astype(BF16)
            else:
                number = tail_count[0]
                tail_count[0] += 1
                groups = SHAPES[PIECES[piece][0]][0] // 24
                tails[number] = value.astype(BF16)
                tail_copy(piece, rows, pl.ds(start, 128), number, groups * (wide // TILE) + group).start()

    def wide_product(piece, mine):
        half = c if mine else 1 - c
        wide, skip, width = half_of(piece), PIECES[piece][1], PIECES[piece][2]
        base = ring_count[0]

        def start_of(j):
            return pl.multiple_of(half * wide + skip + j * TILE, 128)

        def both(j, size=TILE):
            return dot_nn(left[2][...], glog_v[:, pl.ds(start_of(j), size)]) + dot_nn(
                left[3][...], chosen(start_of(j))[:, 0:size]
            )

        def target(j):
            lanes = at(j, TILE)
            return keep(piece, whole, lanes) if mine else give(piece, whole, lanes, base + j, j)

        def step(j):
            before, write, after = target(j)
            before()
            write(both(j))
            after()

        if not mine:
            ring_count[0] += width // TILE
        if skip == 0:
            each_unrolled(width // TILE, step)
            return
        each_unrolled(1, step)
        before, write, after = target(1)
        before()
        norm_part = jnp.where(half == 1, norm_t[...], 0.0).T
        write(both(1) + jnp.concatenate((jnp.zeros((LEFT, TILE - 128), F32), norm_part), 1))
        after()

        def by_half(j, size, write):
            @pl.when(half == 0)
            def _():
                write(both(j, size))

            @pl.when(half == 1)
            def _():
                write(dot_nn(left[3][...], chosen(start_of(j))[:, 0:size]))

        for j in (2, 3):
            before, write, after = target(j)
            before()
            by_half(j, TILE, write)
            after()

        def write_tail(value):
            if mine:
                own[piece][whole, width - 128 : width] = value.astype(BF16)
            else:
                tails[tail_count[0]] = value.astype(BF16)

        by_half(4, 128, write_tail)
        if not mine:
            tail_copy(piece, whole, pl.ds(width - 128, 128), tail_count[0], width // TILE).start()
            tail_count[0] += 1

    def products(piece, mine):
        loaded(piece)
        if piece in (1, 2):
            wide_product(piece, mine)
        elif piece == 4:
            if not mine:
                for group in range(4):
                    source = left[5 + group % 2]
                    if group >= 2:
                        loads[piece][1 + group % 2].wait()
                    plain(piece, False, source, gffn_v, group)
                    plain(piece, True, source, gffn_v, group)
                    if group < 2:
                        again = pltpu.make_async_copy(act_part(group + 2), source, load_sem.at[12 + group])
                        again.start()
                        loads[piece][1 + group] = again
        else:
            source, right = {0: (left[1], gqkv_v), 3: (left[0], gh_v), 5: (left[4], gattn_v)}[piece]
            plain(piece, mine, source, right, 0)

    def combine(piece, target, parts):
        def some(rows, lanes):
            total = parts[0][rows, lanes].astype(F32)
            for member in parts[1:]:
                total = total + member[rows, lanes].astype(F32)
            target[rows, lanes] = total.astype(target.dtype)

        wide = PIECES[piece][2]
        if piece == 4:
            each(4, lambda group: some(at(group, 48), slice(0, wide)))
            return
        if wide >= 512:
            each_unrolled(wide // 512, lambda j: some(slice(0, 48), at(j, 512)))
        if wide % 512:
            some(slice(0, 48), slice(wide // 512 * 512, wide))

    def hop(piece, k, land, index, sems, way):
        return pltpu.make_async_remote_copy(
            src_ref=slot(own, piece, k),
            dst_ref=slot(land, piece, index),
            send_sem=sems[0].at[piece, index],
            recv_sem=sems[1].at[piece, index],
            device_id=peers[way],
            device_id_type=MESH,
        )

    FIRST, SECOND = (first_send, first_recv), (second_send, second_recv)

    def landed(piece, land, index, sems):
        hop(piece, me, land, index, sems, XWAY).wait_recv()

    def block(piece, a, b, far):
        return chip(far, a, b) if SUM_WAY[piece] in (0, 3) else chip(far, b, a)

    def split(piece):
        return (y, x, YWAY, XWAY) if SUM_WAY[piece] in (0, 3) else (x, y, XWAY, YWAY)

    readied = set()

    def ready(piece):
        if piece in readied:
            return
        readied.add(piece)
        wide, groups = PIECES[piece][2], SHAPES[PIECES[piece][0]][0] // 24
        for group in range(groups):
            for j in range(wide // TILE):
                ring_copy(piece, pl.ds(LEFT * group, LEFT), at(j, TILE), 0, group * (wide // TILE) + j).wait_recv()
            if wide % TILE:
                index = groups * (wide // TILE) + group
                tail_copy(piece, pl.ds(LEFT * group, LEFT), pl.ds(wide - 128, 128), 0, index).wait_recv()

    def both_cores(piece, k):
        return (slot(own, piece, k), slot(side, piece, k))

    def rest_of(piece):
        return SUM_WAY[piece] > 1

    def first_block(piece, i):
        a, b, way, _ = split(piece)
        if rest_of(piece):
            return block(piece, 1 - a, (1 - b) if i else b, z), i, way
        t, v = near_first(z, i // 2), (1 - b) if i % 2 == 0 else b
        return block(piece, 1 - a, v, t), 2 * t + v, way

    def second_block(piece, i):
        a, b, _, way = split(piece)
        if rest_of(piece):
            return block(piece, a, 1 - b, z), 0, way
        t = near_first(z, i)
        return block(piece, a, 1 - b, t), t, way

    def z_block(piece, i):
        a, b, _, _ = split(piece)
        if rest_of(piece):
            t, q = near_first(z, 3 - i // 4), i % 4
            k = block(piece, (1 - a) if q // 2 else a, (1 - b) if q % 2 else b, t)
        else:
            t, q = near_first(z, 3 - i), 0
            k = block(piece, a, b, t)
        return k, t, q, (z - t + 3) // 4

    def plane_count(piece):
        return 4 if rest_of(piece) else 1

    def z_copy(piece, i):
        k, t, q, down = z_block(piece, i)
        n = plane_count(piece)
        there = (t - z - 1 + 6 * down) * n + q
        return pltpu.make_async_remote_copy(
            src_ref=slot(own, piece, k),
            dst_ref=slot(column, piece, there),
            send_sem=z_send.at[piece, t * n + q],
            recv_sem=z_recv.at[piece, there],
            device_id=device(z + 1 - 2 * down, y, x, c),
            device_id_type=MESH,
        )

    def z_landed(piece, index):
        pltpu.make_async_remote_copy(
            src_ref=slot(own, piece, me),
            dst_ref=slot(column, piece, index),
            send_sem=z_send.at[piece, 0],
            recv_sem=z_recv.at[piece, index],
            device_id=peers[XWAY],
            device_id_type=MESH,
        ).wait_recv()
        return slot(column, piece, index)

    def first_slot(piece, index):
        landed(piece, first, index, FIRST)
        return (slot(first, piece, index),)

    def second_slot(piece, index):
        landed(piece, second, index, SECOND)
        return (slot(second, piece, index),)

    def with_ends(piece, target, parts, q):
        low, high = q, 4 * plane_count(piece) + q

        @pl.when(z == 0)
        def _():
            combine(piece, target, parts + (z_landed(piece, high),))

        @pl.when(z == 3)
        def _():
            combine(piece, target, parts + (z_landed(piece, low),))

        @pl.when((z > 0) & (z < 3))
        def _():
            combine(piece, target, parts + (z_landed(piece, low), z_landed(piece, high)))

    def first_send_of(piece, i):
        ready(piece)
        k, index, way = first_block(piece, i)
        if rest_of(piece):
            with_ends(piece, slot(own, piece, k), both_cores(piece, k), 2 + i)
        else:
            combine(piece, slot(own, piece, k), both_cores(piece, k))
        hop(piece, k, first, index, FIRST, way).start()

    def second_send_of(piece, i):
        k, index, way = second_block(piece, i)
        if rest_of(piece):
            with_ends(piece, slot(own, piece, k), both_cores(piece, k) + first_slot(piece, 1), 1)
        else:
            parts = first_slot(piece, 2 * index + 1 - split(piece)[1])
            combine(piece, slot(own, piece, k), both_cores(piece, k) + parts)
        hop(piece, k, second, index, SECOND, way).start()

    def z_send_of(piece, i):
        ready(piece)
        k, t, q, down = z_block(piece, i)
        parts = both_cores(piece, k)
        if not rest_of(piece):
            parts = parts + first_slot(piece, 2 * t + split(piece)[1]) + second_slot(piece, t)

        @pl.when((z == 0) | (z == 3))
        def _():
            combine(piece, slot(own, piece, k), parts)

        @pl.when((z > 0) & (z < 3))
        def _():
            came = z_landed(piece, (t - z + 4 * down) * plane_count(piece) + q)
            combine(piece, slot(own, piece, k), parts + (came,))

        z_copy(piece, i).start()

    swaps = []

    def finish(piece):
        if rest_of(piece):
            parts = first_slot(piece, 0) + second_slot(piece, 0)
        else:
            parts = first_slot(piece, 2 * z + split(piece)[1]) + second_slot(piece, z)
        with_ends(piece, fin[piece], both_cores(piece, me) + parts, 0)
        m, skip, wide = PIECES[piece]
        size = SHAPES[m][0]
        lanes = pl.ds(pl.multiple_of(c * half_of(piece) + skip, 128), wide)
        swaps.append(
            pltpu.make_async_remote_copy(
                src_ref=fin[piece].at[pl.ds(pl.multiple_of((1 - c) * size, 8), size), :],
                dst_ref=outs[m].at[:, lanes],
                send_sem=swap_send.at[piece],
                recv_sem=swap_recv.at[piece],
                device_id=peers[SIDE],
                device_id_type=MESH,
            )
        )
        swaps[-1].start()
        squared = fin[piece][...] * fin[piece][...] + SQUARE_FLOOR
        lane_plane[spot, :, HALF_AT[m] + skip : HALF_AT[m] + skip + wide] = jnp.sum(squared, 0, keepdims=True)
        outs[m][:, lanes] = fin[piece][pl.ds(pl.multiple_of(c * size, 8), size), :]

    for task in TASKS:
        piece, number = task // 32, task % 32
        if number < 2:
            products(piece, number == 1)
        elif number == 17:
            finish(piece)
        elif rest_of(piece):
            if number < 14:
                z_send_of(piece, number - 2)
            elif number < 16:
                first_send_of(piece, number - 14)
            else:
                second_send_of(piece, 0)
        elif number < 10:
            first_send_of(piece, number - 2)
        elif number < 14:
            second_send_of(piece, number - 10)
        else:
            z_send_of(piece, number - 14)

    def spread(source, target, send, recv, peer):
        copy = pltpu.make_async_remote_copy(
            src_ref=source, dst_ref=target, send_sem=send, recv_sem=recv, device_id=peer, device_id_type=MESH
        )
        copy.start()
        return copy

    def arrive(copies):
        for copy in copies:
            copy.wait_recv()
        return copies

    plane_copies = [
        spread(lane_plane.at[spot], lane_plane.at[spot], lane_send.at[i], lane_recv.at[i], plane_peers[i])
        for i in range(3)
    ]
    for swap in swaps:
        swap.wait()
    sides, gs = statistics(outs, side_olds)

    def spread_eight(buffers, value, send, recv):
        buffers[0][2 * spot + c] = value
        mine = buffers[0].at[2 * spot + c]
        return [spread(mine, mine, send.at[i], recv.at[i], greeted[3 + i]) for i in range(7)]

    def spread_four(buffers, send, recv):
        total = [buffers[0][2 * i] + buffers[0][2 * i + 1] for i in range(4)]
        buffers[1][z] = (total[0] + total[1]) + (total[2] + total[3])
        mine = buffers[1].at[z]
        return [spread(mine, mine, send.at[7 + i], recv.at[7 + i], column_peers[i]) for i in range(3)]

    def four(buffer):
        return (buffer[0] + buffer[1]) + (buffer[2] + buffer[3])

    scalars = lanes_of([jnp.sum(member, 0, keepdims=True) for member in sides] + [loss[...]])
    scalars = jnp.concatenate((scalars, squares[...]), 1)
    sent = spread_eight(scalar_sums, scalars, scalar_send, scalar_recv)
    sent += arrive(plane_copies)
    lane_z[z] = four(lane_plane)
    z_copies = [
        spread(lane_z.at[z], lane_z.at[z], lane_send.at[3 + i], lane_recv.at[3 + i], column_peers[i]) for i in range(3)
    ]
    arrive(sent[0:7])
    last_copies = spread_four(scalar_sums, scalar_send, scalar_recv)
    sent += arrive(z_copies)
    lane_halves[c] = four(lane_z)
    halves_copy = spread(lane_halves.at[c], lane_halves.at[c], lane_send.at[6], lane_recv.at[6], peers[SIDE])
    sent += arrive(last_copies)
    sent += arrive([halves_copy])
    pair = (lane_halves[0], lane_halves[1])
    lanes = [half[:, HALF_AT[m] : HALF_AT[m] + SHAPES[m][1] // 2] for m in range(5) for half in pair]
    sums = jnp.concatenate(lanes + [four(scalar_sums[1])], 1)
    sums_out[...] = sums
    updates = updates_of(sums, gs, sides, lane_olds, moment)[0]
    totals = lanes_of(
        [total_sum(update * update) for update in updates[:6]]
        + [jnp.sum(updates[6][i : i + 1] * updates[6][i : i + 1], 1, keepdims=True) for i in range(6)]
    )
    sent += arrive(spread_eight(total_sums, totals, total_send, total_recv))
    sent += arrive(spread_four(total_sums, total_send, total_recv))
    totals_out[...] = four(total_sums[1])
    for copy in sent:
        copy.wait_send()
    for piece in range(6):
        for i in range(2 if rest_of(piece) else 8):
            k, index, way = first_block(piece, i)
            hop(piece, k, first, index, FIRST, way).wait_send()
        for i in range(1 if rest_of(piece) else 4):
            k, index, way = second_block(piece, i)
            hop(piece, k, second, index, SECOND, way).wait_send()
        for i in range(12 if rest_of(piece) else 3):
            z_copy(piece, i).wait_send()
    for number in range(ring_count[0] - 3, ring_count[0]):
        ring_copy(1, whole, pl.ds(0, TILE), number, 0).wait_send()
    for number in range(tail_count[0]):
        tail_copy(1, whole, pl.ds(0, 128), number, 0).wait_send()


def statistics(grads, side_olds):
    wide_g = grads[E_][...]
    gs = (wide_g[:, :VOCAB], wide_g[:, PLACE_AT:]) + tuple(grads[m][...] for m in (Q_, O_, I_, D_))
    decay = 1.0 - STEP ** (-0.8)
    sides = []
    for index in range(6):
        mean = jnp.sum(gs[index] * gs[index] + SQUARE_FLOOR, 1, keepdims=True) / gs[index].shape[1]
        sides.append(decay * column_of(as_row(side_olds[index])) + (1.0 - decay) * mean)
    return sides, gs + (wide_g[:, 4096:4224],)


def updates_of(sums, gs, sides, lane_olds, moment):
    decay = 1.0 - STEP ** (-0.8)
    fresh = 1.0 - decay
    parts = [sums[:, :VOCAB], sums[:, PLACE_AT:WIDE]]
    parts += [sums[:, SUM_AT[i] : SUM_AT[i + 1]] for i in range(1, 5)]
    scalars = sums[:, SUM_AT[5] : SUM_AT[5] + 128]
    updates, lane_news = [], []
    for index in range(6):
        height = gs[index].shape[0] * 32
        lane_news.append(decay * as_row(lane_olds[index]) + fresh * (parts[index] / height))
        if index < 2:
            mean = jnp.sum(lane_news[index], 1, keepdims=True) / lane_news[index].shape[1]
        else:
            mean = lane_at(scalars, index) / height
        updates.append(gs[index] * lax.rsqrt(sides[index] * lane_news[index] / mean))
    norm_g = jnp.concatenate([row_of(lane_at(gs[6], NORM_AT - 4096 + i)) for i in range(6)], 0)
    moment_new = decay * moment[...] + fresh * (norm_g * norm_g + SQUARE_FLOOR)
    updates.append(norm_g * lax.rsqrt(moment_new))
    return updates, lane_news, norm_g, moment_new


def reduce_grads(large, small):
    tokens = 5 * SPAN
    vmem, hbm = pl.BlockSpec(memory_space=pltpu.VMEM), pl.BlockSpec(memory_space=pl.ANY)
    dma = pltpu.SemaphoreType.DMA
    scratch = []
    for counts in ((16, 16), (16, 16), (8, 2), (4, 1), (5, 20)):
        for (m, _, wide), way in zip(PIECES, SUM_WAY):
            scratch.append(pltpu.VMEM((counts[way // 2] * 2 * SHAPES[m][0], wide), BF16))
    scratch += [pltpu.VMEM((2 * SHAPES[m][0], wide), F32) for m, _, wide in PIECES]
    scratch += [pltpu.VMEM((LEFT, tokens), BF16)] * 7
    scratch += [pltpu.VMEM((tokens, width), BF16) for width in (TABLE_END, 3 * D, D, 4 * D, D)]
    scratch += [pltpu.VMEM((3, LEFT, TILE), BF16), pltpu.VMEM((7, LEFT, 128), BF16), pltpu.VMEM((128, D), F32)]
    scratch += [pltpu.VMEM((count, 1, HALF_SUMS), F32) for count in (4, 4, 2)]
    scratch += [pltpu.VMEM((count, 1, width), F32) for width in (256, 128) for count in (8, 4)]
    scratch += [dma((14,)), dma((3,)), dma((7,)), dma((6, 10)), dma((6, 8)), dma((6, 8)), dma((6, 4)), dma((6, 4))]
    scratch += [dma((6, 16)), dma((6, 20)), dma((6,)), dma((6,))]
    scratch += [dma((7,))] * 2 + [dma((10,))] * 4
    return pl.pallas_call(
        reduce_kernel,
        out_shape=[jax.ShapeDtypeStruct(shape, F32) for shape in SHAPES + ((1, SUMS), (1, 128))],
        in_specs=[hbm] * 11 + [vmem] * len(small),
        out_specs=[vmem] * 7,
        scratch_shapes=scratch,
        compiler_params=pltpu.CompilerParams(
            collective_id=1, has_side_effects=True, vmem_limit_bytes=63 * 1024 * 1024
        ),
    )(*large, *small)


def update_kernel(*refs):
    copies = [pltpu.make_async_copy(refs[i], refs[55 + i], refs[82].at[i]) for i in range(27)]
    for copy in copies:
        copy.start()
    for copy in copies:
        copy.wait()
    refs = refs[55:82] + refs[27:55]
    grads, sums, totals, ws, norms = refs[0:5], refs[5], refs[6], refs[7:13], refs[13]
    lane_olds, side_olds, moment = refs[14:20], refs[20:26], refs[26]
    loss_out, table_g, place_g, norm_g_out = refs[27:31]
    lane_outs, side_outs, moment_out, news, norm_new = refs[31:37], refs[37:43], refs[43], refs[44:50], refs[50]
    grad_outs = refs[51:55]
    sides, gs = statistics(grads, side_olds)
    updates, lane_news, norm_g, moment_new = updates_of(sums[...], gs, sides, lane_olds, moment)
    scalars = sums[:, SUM_AT[5] : SUM_AT[5] + 128]
    squares = sums[:, SUM_AT[5] + 128 :]
    loss_out[...] = lane_at(scalars, 6)
    table_g[...] = gs[0]
    place_g[...] = gs[1]
    norm_g_out[...] = norm_g
    moment_out[...] = moment_new
    for index in range(6):
        lane_outs[index][...] = lane_news[index].reshape(lane_outs[index].shape)
        side_outs[index][...] = row_of(sides[index]).reshape(side_outs[index].shape)
        if index >= 2:
            grad_outs[index - 2][...] = gs[index]
        entries = gs[index].shape[0] * gs[index].shape[1] * 32
        clip = jnp.maximum(1.0, jnp.sqrt(lane_at(totals[...], index) / entries))
        scale = learn_rate * jnp.sqrt(lane_at(squares, index) / entries) / clip
        news[index][...] = ws[index][...] - scale * updates[index]
    for i in range(6):
        clip = jnp.maximum(1.0, jnp.sqrt(lane_at(totals[...], 6 + i) / D))
        scale = learn_rate * jnp.sqrt(lane_at(squares, 6 + i) / D) / clip
        norm_new[i : i + 1, :] = norms[i : i + 1, :] - scale * updates[6][i : i + 1, :]


def update_weights(operands):
    lanes = (VOCAB, 512, 3 * D, D, 4 * D, D)
    held = (24, 24, 24, 24, 24, 96)
    shapes = [(1, 1), (24, VOCAB), (24, 512), (6, 24)]
    shapes += [(lane,) for lane in lanes] + [(size,) for size in held] + [(6, 24)]
    shapes += list(zip(held, lanes)) + [(6, 24)] + list(zip(held, lanes))[2:]
    return pl.pallas_call(
        update_kernel,
        out_shape=[jax.ShapeDtypeStruct(shape, F32) for shape in shapes],
        in_specs=[pl.BlockSpec(memory_space=pl.ANY)] * len(operands),
        out_specs=[pl.BlockSpec(memory_space=pltpu.VMEM)] * len(shapes),
        scratch_shapes=[pltpu.VMEM(member.shape, member.dtype) for member in operands]
        + [pltpu.SemaphoreType.DMA((len(operands),))],
        compiler_params=pltpu.CompilerParams(vmem_limit_bytes=63 * 1024 * 1024),
    )(*operands)


def norm_forward(value, gain, shift):
    centred = value - jnp.mean(value, -1, keepdims=True)
    inverse = lax.rsqrt(jnp.mean(centred * centred, -1, keepdims=True) + EPSILON)
    normed = centred * inverse
    return (normed * gain + shift, normed, inverse)


def norm_backward(grad_out, normed, inverse, gain):
    scaled = grad_out * gain
    back = inverse * (
        scaled
        - jnp.mean(scaled, -1, keepdims=True)
        - normed * jnp.mean(scaled * normed, -1, keepdims=True)
    )
    return (back, jnp.sum(grad_out * normed, 0), jnp.sum(grad_out, 0))


def mm(left, right, sides):
    return lax.dot_general(left, right, ((sides[:1], sides[1:]), ((), ())), preferred_element_type=F32)


def attend(qkv, allowed):
    by_head = qkv.reshape(qkv.shape[0], 3, HEADS, HEAD_DIM)
    query, key, value = by_head[:, 0], by_head[:, 1], by_head[:, 2]
    scores = jnp.einsum("qhe,khe->hqk", query, key, preferred_element_type=F32) * 0.125
    scores = jnp.where(allowed[None], scores, -1e30)
    highest = jnp.max(scores, -1, keepdims=True)
    raised = jnp.exp(scores - highest)
    summed = jnp.sum(raised, -1, keepdims=True)
    shares = (raised / summed).astype(BF16)
    mixture = jnp.einsum("hqk,khe->qhe", shares, value, preferred_element_type=F32)
    return mixture.astype(BF16).reshape(qkv.shape[0], D), highest + jnp.log(summed)


def attend_back(qkv, allowed, log_total, grad_mix):
    by_head = qkv.reshape(qkv.shape[0], 3, HEADS, HEAD_DIM)
    query, key, value = by_head[:, 0], by_head[:, 1], by_head[:, 2]
    grad_mix = grad_mix.reshape(qkv.shape[0], HEADS, HEAD_DIM)
    scores = jnp.einsum("qhe,khe->hqk", query, key, preferred_element_type=F32) * 0.125
    scores = jnp.where(allowed[None], scores, -1e30)
    shares = jnp.exp(scores - log_total)
    grad_share = jnp.einsum("qhe,khe->hqk", grad_mix, value, preferred_element_type=F32)
    grad_score = (shares * (grad_share - jnp.sum(shares * grad_share, -1, keepdims=True))).astype(BF16)
    grad_query = jnp.einsum("hqk,khe->qhe", grad_score, key, preferred_element_type=F32) * 0.125
    grad_key = jnp.einsum("hqk,qhe->khe", grad_score, query, preferred_element_type=F32) * 0.125
    grad_value = jnp.einsum("hqk,qhe->khe", shares.astype(BF16), grad_mix, preferred_element_type=F32)
    return jnp.stack((grad_query, grad_key, grad_value), 1).astype(BF16).reshape(qkv.shape)


def on_slice(token_arrays, lengths, weights, lane_olds, side_olds, moment):
    olds = lane_olds + side_olds + (moment,)
    found = front(token_arrays + weights, lengths)
    mask_count, gains, side, cols, keys, weight_sq = found[0:6]
    x_t, mix, a, act, y, slope, qkv_b, normed_a = found[6:14]
    normed_bc, (qkv_w, out_w, in_w, down_w, wide_w) = found[14:18], found[18:23]
    found = middle(
        (wide_w, qkv_w, out_w, in_w, down_w, y, act, a, mix, slope, qkv_b, normed_a) + tuple(normed_bc),
        (cols, keys, side, gains, mask_count),
    )
    loss_part, norm_sums = found[0:2]
    grad_logit, y_t, a_t, mix_t, act_t, ge_t, grad_ffn, grad_hidden, grad_attn, grad_qkv = found[2:]
    reduced = reduce_grads(
        (y_t, ge_t, grad_logit, x_t, grad_qkv, mix_t, grad_attn, a_t, grad_hidden, act_t, grad_ffn),
        (cols, norm_sums, loss_part, weight_sq) + olds,
    )
    found = update_weights(tuple(reduced) + weights + olds)
    grads = (None,) + tuple(found[24:28])
    mask_count = mask_count.reshape(())
    loss_sum, table_g, place_g, norm_g = found[0:4]
    lane_news = found[4:10]
    side_news = found[10:16]
    moment_new, norm_new = found[16], found[23]
    news = found[17:23]
    return (
        loss_sum.reshape(()),
        mask_count,
        table_g.T,
        place_g.T,
        grads[1],
        grads[2],
        grads[3],
        grads[4],
        norm_g.T,
        lane_news[0],
        side_news[0],
        lane_news[1],
        side_news[1],
        side_news[2],
        lane_news[2],
        side_news[3],
        lane_news[3],
        side_news[4],
        lane_news[4],
        side_news[5],
        lane_news[5],
        moment_new.T,
        news[0].T,
        news[1].T,
        news[2],
        news[3],
        news[4],
        news[5],
        norm_new.T,
    )


def on_device(
    whole_mesh,
    long_ids,
    long_targets,
    long_mask,
    long_lengths,
    short_ids,
    short_targets,
    short_mask,
    short_lengths,
    table,
    position,
    qkv_weight,
    out_weight,
    in_weight,
    down_weight,
    norms,
    table_rows,
    table_cols,
    position_rows,
    position_cols,
    qkv_rows,
    qkv_cols,
    out_rows,
    out_cols,
    in_rows,
    in_cols,
    down_rows,
    down_cols,
    norm_moment,
):
    if whole_mesh == (8, 4):
        return on_slice(
            (long_ids, long_targets, long_mask, short_ids, short_targets, short_mask),
            (long_lengths, short_lengths),
            (table.T, position.T, qkv_weight, out_weight, in_weight, down_weight, norms.T),
            (table_rows, position_rows, qkv_cols, out_cols, in_cols, down_cols),
            (table_cols, position_cols, qkv_rows, out_rows, in_rows, down_rows),
            norm_moment.T,
        )
    devices = lax.axis_size(("dp", "seq"))
    seq_index = lax.axis_index("seq")
    held = norms.shape[0]

    span = long_ids.shape[1]
    long_place = seq_index * span + lax.iota(jnp.int32, span)
    long_keep = (long_place[None, :] < long_lengths[:, None]).astype(jnp.int32)
    short_keep = (lax.iota(jnp.int32, SPAN)[None, :] < short_lengths[:, None]).astype(jnp.int32)
    long_pack = jnp.stack((long_ids, long_targets, long_mask * long_keep, long_keep), 1)
    short_pack = jnp.stack((short_ids, short_targets, short_mask * short_keep, short_keep), 1)
    moved = lax.all_to_all(
        jnp.concatenate((long_pack, short_pack[1:]), 0), "seq", split_axis=0, concat_axis=0, tiled=True
    )
    tokens = jnp.concatenate((moved, short_pack[:1]), 0)
    ids, targets, weight, keep = (tokens[:, i].reshape(-1) for i in range(4))
    weight = weight.astype(F32)
    count = tokens.shape[0] * span
    last = count - span
    alone = seq_index == lax.axis_size("seq") - 1
    token = lax.iota(jnp.int32, count)
    place = jnp.where(alone | (token >= last), token % span, token)
    row = jnp.where(alone | (token >= last), token // span, 0)
    allowed_long = (row[:last, None] == row[None, :last]) & (keep[None, :last] > 0)
    allowed_short = jnp.broadcast_to(keep[None, last:] > 0, (span, span))

    here_count = jnp.sum(long_pack[:, 2]) + jnp.sum(short_pack[:, 2])
    tall = table.T
    counts = jnp.broadcast_to(jnp.stack((here_count // 256, here_count % 256)).astype(F32)[None], (held, 2))
    wide_shard = jnp.concatenate(
        (tall, norms, counts, jnp.zeros((held, PLACE_AT - COUNT_AT - 2), F32), position.T), 1
    )
    shards = (wide_shard, qkv_weight, out_weight, in_weight, down_weight)
    wide_w, qkv_w, out_w, in_w, down_w = (
        lax.all_gather(shard.astype(BF16), ("dp", "seq"), axis=0, tiled=True) for shard in shards
    )
    column = lax.broadcasted_iota(jnp.int32, (1, WIDE), 1)
    chosen = ((ids[:, None] == column) | ((place[:, None] + PLACE_AT) == column)).astype(BF16)
    gains = wide_w[:, NORM_AT : NORM_AT + 6].astype(F32)
    sums = jnp.sum(wide_w[:, COUNT_AT : COUNT_AT + 2].astype(F32), 0)
    mask_count = (sums[0] * 256.0 + sums[1]) / held
    inverse_count = 1.0 / mask_count

    embedded = mm(chosen, wide_w, (1, 1))
    first, normed_a, inverse_a = norm_forward(embedded, gains[:, 0], gains[:, 1])
    first_b = first.astype(BF16)
    qkv_b = mm(first_b, qkv_w, (1, 0)).astype(BF16)
    mix_long, total_long = attend(qkv_b[:last], allowed_long)
    mix_short, total_short = attend(qkv_b[last:], allowed_short)
    mixture = jnp.concatenate((mix_long, mix_short), 0)
    second, normed_b, inverse_b = norm_forward(first + mm(mixture, out_w, (1, 0)), gains[:, 2], gains[:, 3])
    second_b = second.astype(BF16)
    hidden = mm(second_b, in_w, (1, 0))
    active, slope = gelu_pair(hidden)
    active_b = active.astype(BF16)
    third, normed_c, inverse_c = norm_forward(second + mm(active_b, down_w, (1, 0)), gains[:, 4], gains[:, 5])
    third_b = third.astype(BF16)
    logits = jnp.where(column < VOCAB, mm(third_b, wide_w, (1, 0)), -1e30)
    highest = jnp.max(logits, -1, keepdims=True)
    log_sum = highest + jnp.log(jnp.sum(jnp.exp(logits - highest), -1, keepdims=True))
    onehot = targets[:, None] == column
    picked = jnp.sum(jnp.where(onehot, logits, 0.0), -1)
    loss_part = jnp.sum(weight * (log_sum[:, 0] - picked))
    grad_logit = (
        (jnp.exp(logits - log_sum) - onehot.astype(F32)) * (weight * inverse_count)[:, None]
    ).astype(BF16)
    grad_third = mm(grad_logit, wide_w, (1, 1))
    grad_second, gain_c, shift_c = norm_backward(grad_third, normed_c, inverse_c, gains[:, 4])
    grad_ffn = grad_second.astype(BF16)
    down_grad = mm(active_b, grad_ffn, (0, 0)).astype(BF16)
    grad_hidden = (mm(grad_ffn, down_w, (1, 1)) * slope).astype(BF16)
    in_grad = mm(second_b, grad_hidden, (0, 0)).astype(BF16)
    grad_second = grad_second + mm(grad_hidden, in_w, (1, 1))
    grad_first, gain_b, shift_b = norm_backward(grad_second, normed_b, inverse_b, gains[:, 2])
    grad_attn = grad_first.astype(BF16)
    out_grad = mm(mixture, grad_attn, (0, 0)).astype(BF16)
    grad_mix = mm(grad_attn, out_w, (1, 1)).astype(BF16)
    grad_qkv = jnp.concatenate(
        (
            attend_back(qkv_b[:last], allowed_long, total_long, grad_mix[:last]),
            attend_back(qkv_b[last:], allowed_short, total_short, grad_mix[last:]),
        ),
        0,
    )
    qkv_grad = mm(first_b, grad_qkv, (0, 0)).astype(BF16)
    grad_first = grad_first + mm(grad_qkv, qkv_w, (1, 1))
    grad_embed, gain_a, shift_a = norm_backward(grad_first, normed_a, inverse_a, gains[:, 0])
    wide_grad = mm(
        jnp.concatenate((third_b, grad_embed.astype(BF16)), 0),
        jnp.concatenate((grad_logit, chosen), 0),
        (0, 0),
    )
    norm_part = jnp.stack((gain_a, shift_a, gain_b, shift_b, gain_c, shift_c), 1)
    wide_grad = lax.dynamic_update_slice(wide_grad.astype(BF16), norm_part.astype(BF16), (0, NORM_AT))
    grads = (wide_grad, qkv_grad, out_grad, in_grad, down_grad)
    wide_g, qkv_g, out_g, in_g, down_g = (
        lax.psum_scatter(grad.astype(F32), ("dp", "seq"), scatter_dimension=0, tiled=True) for grad in grads
    )
    table_g, place_g = wide_g[:, :VOCAB], wide_g[:, PLACE_AT:]
    norm_g = wide_g[:, NORM_AT : NORM_AT + 6]

    decay = 1.0 - STEP ** (-0.8)
    matrices = (
        (qkv_weight, qkv_g, qkv_rows, qkv_cols),
        (out_weight, out_g, out_rows, out_cols),
        (in_weight, in_g, in_rows, in_cols),
        (down_weight, down_g, down_rows, down_cols),
    )
    wide = (
        (tall, table_g, table_cols, table_rows),
        (position.T, place_g, position_cols, position_rows),
    )
    row_news = [
        decay * member[2] + (1.0 - decay) * jnp.mean(member[1] * member[1] + SQUARE_FLOOR, 1)
        for member in matrices + wide
    ]
    col_parts = [jnp.sum(member[1] * member[1] + SQUARE_FLOOR, 0) for member in matrices + wide]
    row_totals = jnp.stack([jnp.sum(rows_new) for rows_new in row_news])
    weight_sq = jnp.stack([jnp.sum(member[0] * member[0]) for member in matrices + wide])
    stats = lax.psum(
        col_parts + [row_totals, weight_sq, jnp.sum(norms * norms, 0), loss_part.reshape(1)], ("dp", "seq")
    )
    updates = []
    cols_out = []
    for index, member in enumerate(matrices + wide):
        full_rows = member[0].shape[0] * devices
        cols_new = decay * member[3] + (1.0 - decay) * stats[index] / full_rows
        if index < 4:
            mean = stats[6][index] / full_rows
        else:
            mean = jnp.mean(cols_new)
        updates.append(member[1] * lax.rsqrt(row_news[index][:, None] * cols_new[None, :] / mean))
        cols_out.append(cols_new)
    moment_new = decay * norm_moment + (1.0 - decay) * (norm_g * norm_g + SQUARE_FLOOR)
    norm_update = norm_g * lax.rsqrt(moment_new)
    update_sq = jnp.stack([jnp.sum(update * update) for update in updates])
    totals = lax.psum((update_sq, jnp.sum(norm_update * norm_update, 0)), ("dp", "seq"))
    news = []
    for index, member in enumerate(matrices + wide):
        entries = member[0].shape[0] * member[0].shape[1] * devices
        clip = jnp.maximum(1.0, jnp.sqrt(totals[0][index] / entries))
        news.append(
            member[0] - learn_rate * jnp.sqrt(stats[7][index] / entries) * updates[index] / clip
        )
    norm_rows = norms.shape[0] * devices
    norm_clip = jnp.maximum(1.0, jnp.sqrt(totals[1] / norm_rows))
    norm_new = norms - learn_rate * jnp.sqrt(stats[8] / norm_rows) * norm_update / norm_clip
    return (
        stats[9][0],
        mask_count,
        table_g.T,
        place_g.T,
        qkv_g,
        out_g,
        in_g,
        down_g,
        norm_g,
        cols_out[4],
        row_news[4],
        cols_out[5],
        row_news[5],
        row_news[0],
        cols_out[0],
        row_news[1],
        cols_out[1],
        row_news[2],
        cols_out[2],
        row_news[3],
        cols_out[3],
        moment_new,
        news[4].T,
        news[5].T,
        news[0],
        news[1],
        news[2],
        news[3],
        norm_new,
    )


def solution(mesh):
    split, wide = P(("dp", "seq"), None), P(None, ("dp", "seq"))
    shard, same = P(("dp", "seq")), P()
    return jax.shard_map(
        functools.partial(on_device, (mesh.shape["dp"], mesh.shape["seq"])),
        mesh=mesh,
        in_specs=(P("dp", "seq"),) * 3
        + (P("dp"),)
        + (split,) * 3
        + (shard,)
        + (wide,) * 2
        + (split,) * 5
        + (same, shard) * 2
        + (shard, same) * 4
        + (split,),
        out_specs=(same, same)
        + (wide,) * 2
        + (split,) * 5
        + (same, shard) * 2
        + (shard, same) * 4
        + (split,)
        + (wide,) * 2
        + (split,) * 5,
        check_vma=False,
    )
```
